32 devices in a mesh: dp: 4 (over z), blk: 8 (over y, x, core).
Axes of the slice: x: 2, y: 2, z: 4, core: 2. Of those that a mesh axis runs over, the one named last changes fastest.
Arguments:
- tokens: bfloat16 [4, 2048, 960], P('dp', 'blk'), may hold values from -6 to 6
- depths: int32 [4, 2048], P('dp', 'blk'), may hold values from 1 to 2
- segments: int32 [4, 2048], P('dp', 'blk'), may hold values from 0 to 3, as said below
- norm_attn: bfloat16 [960], replicated, may hold values from 0.5 to 1.5
- norm_ffn: bfloat16 [960], replicated, may hold values from 0.5 to 1.5
- w_query: bfloat16 [960, 960], replicated, may hold values from -0.1875 to 0.1875
- key_weight: bfloat16 [960, 320], replicated, may hold values from -0.1875 to 0.1875
- value_weight: bfloat16 [960, 320], replicated, may hold values from -0.1875 to 0.1875
- w_out: bfloat16 [960, 960], replicated, may hold values from -0.75 to 0.75
- w_gate: bfloat16 [960, 2560], replicated, may hold values from -0.1875 to 0.1875
- w_up: bfloat16 [960, 2560], replicated, may hold values from -0.1875 to 0.1875
- w_down: bfloat16 [2560, 960], replicated, may hold values from -0.125 to 0.125
- w_router: bfloat16 [960, 2], replicated, may hold values from -0.1875 to 0.1875
- cotangent: bfloat16 [4, 2048, 960], P('dp', 'blk'), may hold values from -6 to 6
Outputs:
- hidden_out: float32 [4, 2048, 960], P('dp', 'blk')
- grad_tokens: float32 [4, 2048, 960], P('dp', 'blk')
- grad_norm_attn: float32 [960], P('blk')
- grad_norm_ffn: float32 [960], P('blk')
- grad_query: float32 [960, 960], P('blk')
- grad_key: float32 [960, 320], P('blk')
- grad_value: float32 [960, 320], P('blk')
- grad_out: float32 [960, 960], P('blk')
- grad_gate: float32 [960, 2560], P('blk')
- grad_up: float32 [960, 2560], P('blk')
- grad_down: float32 [2560, 960], P('blk')
- grad_router: float32 [960, 2], P('blk')
The draws below stay inside these ranges and needn't reach their ends.
Inputs may be any that keep to these rules, and one draw needn't show every extreme that they name: `segments`: in each row the numbers start at 0 and never fall; a number may be skipped. One row is a single document, all 0; every other row ends at 3, with boundaries of its own.
All inputs are finite; a program needn't handle non-finite values.
Results may differ from the reference program's by a relative error of at most 0.025.
Values may be sent and summed in bfloat16 or wider, within the bound.
A program may use at most 320 MiB of HBM per device.

```python
import math
import jax
import jax.numpy as jnp
from jax import lax

MODEL_DIMENSION = 960
QUERY_HEADS = 15
KEY_VALUE_HEADS = 5
HEAD_DIMENSION = 64
FF = 2560
RECUR = 2
PACKED_LENGTH = 2048
ROWS = 4


def draw_segments(key, part):
    key = jax.random.fold_in(key, 11)
    single_key, cut_key = jax.random.split(key)
    single_row = jax.random.randint(single_key, (), 0, ROWS)
    cuts = jax.random.randint(cut_key, (ROWS, 3), 1, PACKED_LENGTH)
    cuts = jnp.sort(cuts, axis=-1)
    row_numbers = jnp.arange(ROWS, dtype=jnp.int32)
    cuts = jnp.where((row_numbers == single_row)[:, None], PACKED_LENGTH, cuts)
    places = jnp.arange(PACKED_LENGTH, dtype=jnp.int32)
    counted = jnp.sum((cuts[:, None, :] <= places[None, :, None]).astype(jnp.int32), axis=-1)
    return counted.astype(jnp.int32)


def touch_ends(array, key, low, largest):
    shape = array.shape
    index_at = [jax.random.randint(jax.random.fold_in(key, axis), (), 0, shape[axis]) for axis in range(len(shape))]
    array = array.at[tuple(index_at)].set(low)
    longest = shape.index(max(shape))
    index_at[longest] = (index_at[longest] + 1) % shape[longest]
    return array.at[tuple(index_at)].set(largest)


def block_scale(rng, extent, cuts, smallest, high):
    gain, own = 1.0, jax.random.fold_in(rng, 6)
    for axis_at, shards_of in cuts:
        steps = jnp.exp(jax.random.uniform(jax.random.fold_in(own, axis_at), (shards_of,), jnp.float32, smallest / len(cuts), high / len(cuts)))
        gain = gain * jnp.repeat(steps, extent[axis_at] // shards_of).reshape([-1 if axis == axis_at else 1 for axis in range(len(extent))])
    return gain


def scatter_about(own_key, extent, spread, most, pieces=(), kind=jnp.bfloat16):
    values = jax.random.normal(own_key, extent, jnp.float32) * spread
    if len(pieces) > 0:
        values = block_scale(own_key, extent, pieces, -0.22, 0.18) * values
    return jnp.clip(values, min=-most, max=most).astype(kind)


def setup_inputs(seed: int = 0) -> dict:
    arg_keys = jax.random.split(jax.random.key(seed), 15)
    return {
        "tokens": scatter_about(arg_keys[0], (ROWS, PACKED_LENGTH, MODEL_DIMENSION), 1.0, 6.0, ((0, 4), (1, 8))),
        "depths": touch_ends(jax.random.randint(arg_keys[1], (ROWS, PACKED_LENGTH), 1, RECUR + 1), jax.random.fold_in(arg_keys[1], 1), 1, RECUR).astype(jnp.int32),
        "segments": draw_segments(jax.random.fold_in(arg_keys[14], 71), 0),
        "norm_attn": jnp.clip(1.0 + 0.1 * jax.random.normal(arg_keys[3], (MODEL_DIMENSION,), jnp.float32), 0.5, 1.5).astype(jnp.bfloat16),
        "norm_ffn": jnp.clip(1.0 + 0.1 * jax.random.normal(arg_keys[4], (MODEL_DIMENSION,), jnp.float32), 0.5, 1.5).astype(jnp.bfloat16),
        "w_query": scatter_about(arg_keys[5], (MODEL_DIMENSION, QUERY_HEADS * HEAD_DIMENSION), MODEL_DIMENSION ** -0.5, 0.1875),
        "key_weight": scatter_about(arg_keys[6], (MODEL_DIMENSION, KEY_VALUE_HEADS * HEAD_DIMENSION), MODEL_DIMENSION ** -0.5, 0.1875),
        "value_weight": scatter_about(arg_keys[7], (MODEL_DIMENSION, KEY_VALUE_HEADS * HEAD_DIMENSION), MODEL_DIMENSION ** -0.5, 0.1875),
        "w_out": scatter_about(arg_keys[8], (QUERY_HEADS * HEAD_DIMENSION, MODEL_DIMENSION), (QUERY_HEADS * HEAD_DIMENSION // 16) ** -0.5, 0.75),
        "w_gate": scatter_about(arg_keys[9], (MODEL_DIMENSION, FF), MODEL_DIMENSION ** -0.5, 0.1875),
        "w_up": scatter_about(arg_keys[10], (MODEL_DIMENSION, FF), MODEL_DIMENSION ** -0.5, 0.1875),
        "w_down": scatter_about(arg_keys[11], (FF, MODEL_DIMENSION), FF ** -0.5, 0.125),
        "w_router": scatter_about(arg_keys[12], (MODEL_DIMENSION, RECUR), MODEL_DIMENSION ** -0.5, 0.1875),
        "cotangent": scatter_about(arg_keys[13], (ROWS, PACKED_LENGTH, MODEL_DIMENSION), 1.0, 6.0, ((0, 4), (1, 8))),
    }


epsilon = 1e-05
highest_precision = lax.Precision.HIGHEST
masked_score = -1e+30

@jax.custom_vjp
def lowered_dtype(v):
    return lax.optimization_barrier(v.astype(jnp.bfloat16)).astype(jnp.float32)

@jax.custom_vjp
def lowered_backward(v):
    return v

def low_keep(v):
    return (lowered_dtype(v), None)

def low_pass(kept, grad):
    return (grad,)

def back_keep(v):
    return (v, None)

def back_low(kept, grad):
    return (lowered_dtype(grad),)
lowered_dtype.defvjp(low_keep, low_pass)
lowered_backward.defvjp(back_keep, back_low)

def frequencies(head_size):
    return jnp.exp(jnp.arange(head_size // 2, dtype=jnp.float32) * (-2.0 * math.log(10000.0) / head_size))

def rms_scale(values):
    return lax.rsqrt(lax.optimization_barrier(jnp.mean(values * values, axis=-1, keepdims=True)) + epsilon)

def rotate(values, cosine_table, sine_values):
    half_width = values.shape[-1] // 2
    first_half = values[..., :half_width]
    second = values[..., half_width:]
    return jnp.concatenate([first_half * cosine_table - second * sine_values, second * cosine_table + first_half * sine_values], axis=-1)

def attention(query_rows, key_rows, rows_of_values, row_segments, active):
    block_of_queries = min(512, PACKED_LENGTH)
    query_group_width = QUERY_HEADS // KEY_VALUE_HEADS
    positions = jnp.arange(PACKED_LENGTH, dtype=jnp.int32)

    def one_block(block_index):
        leading_row = (block_index * block_of_queries).astype(jnp.int32)
        queries_per_block = lax.dynamic_slice_in_dim(query_rows, leading_row, block_of_queries, 0).reshape(block_of_queries, KEY_VALUE_HEADS, query_group_width, HEAD_DIMENSION)
        query_positions = leading_row + jnp.arange(block_of_queries, dtype=jnp.int32)
        query_segments = lax.dynamic_slice_in_dim(row_segments, leading_row, block_of_queries, 0)
        allowed = (query_segments[:, None] == row_segments[None, :]) & (positions[None, :] <= query_positions[:, None])
        allowed = allowed & (active[None, :] | (positions[None, :] == query_positions[:, None]))
        scores = jnp.einsum('qkgd,jkd->kgqj', queries_per_block, key_rows, precision=highest_precision) * HEAD_DIMENSION ** (-0.5)
        scores = jnp.where(allowed[None, None], lowered_backward(scores), masked_score)
        top_score = lax.optimization_barrier(jnp.max(scores, axis=-1, keepdims=True))
        raised = jnp.exp(scores - top_score)
        probability = lowered_dtype(raised / lax.optimization_barrier(jnp.sum(raised, axis=-1, keepdims=True)))
        return jnp.einsum('kgqj,jkd->qkgd', probability, rows_of_values, precision=highest_precision).reshape(block_of_queries, QUERY_HEADS * HEAD_DIMENSION)
    blocks = lax.map(jax.checkpoint(one_block), jnp.arange(PACKED_LENGTH // block_of_queries, dtype=jnp.int32))
    return blocks.reshape(PACKED_LENGTH, QUERY_HEADS * HEAD_DIMENSION)

def row_forward(params, row_tokens, row_depths, row_segments):
    gain_attn, gain_ffn, w_query, key_weight, value_weight, w_out, w_gate, w_up, w_down, w_router = params
    positions = jnp.arange(PACKED_LENGTH, dtype=jnp.int32)
    angles = positions.astype(jnp.float32)[:, None] * frequencies(HEAD_DIMENSION)[None, :]
    cosine_table = jnp.cos(angles)[:, None, :]
    sine_values = jnp.sin(angles)[:, None, :]
    hidden = row_tokens
    for level_index in range(RECUR):
        active = row_depths > level_index
        normalized_input = lowered_dtype(hidden * rms_scale(hidden) * gain_attn)
        query_pre = lowered_backward(jnp.dot(normalized_input, w_query, precision=highest_precision)).reshape(PACKED_LENGTH, QUERY_HEADS, HEAD_DIMENSION)
        query_rows = lowered_dtype(rotate(query_pre, cosine_table, sine_values))
        key_before_rotation = lowered_backward(jnp.dot(normalized_input, key_weight, precision=highest_precision)).reshape(PACKED_LENGTH, KEY_VALUE_HEADS, HEAD_DIMENSION)
        key_rows = lowered_dtype(rotate(key_before_rotation, cosine_table, sine_values))
        rows_of_values = lowered_dtype(lowered_backward(jnp.dot(normalized_input, value_weight, precision=highest_precision))).reshape(PACKED_LENGTH, KEY_VALUE_HEADS, HEAD_DIMENSION)
        attended = lowered_dtype(lowered_backward(attention(query_rows, key_rows, rows_of_values, row_segments, active)))
        attn = lowered_backward(jnp.dot(attended, w_out, precision=highest_precision))
        middle = hidden + attn
        normed_ffn = lowered_dtype(middle * rms_scale(middle) * gain_ffn)
        gate_pre = lowered_backward(jnp.dot(normed_ffn, w_gate, precision=highest_precision))
        up_pre = lowered_backward(jnp.dot(normed_ffn, w_up, precision=highest_precision))
        inner_low = lowered_dtype(gate_pre * jax.nn.sigmoid(gate_pre) * up_pre)
        ffn = lowered_backward(jnp.dot(inner_low, w_down, precision=highest_precision))
        chosen = jax.nn.sigmoid(jnp.dot(hidden, w_router[:, level_index], precision=highest_precision))
        weight = jnp.where(active, chosen, 0.0)
        hidden = hidden + weight[:, None] * (attn + ffn)
    return hidden

def reference(tokens, depths, segments, norm_attn, norm_ffn, w_query, key_weight, value_weight, w_out, w_gate, w_up, w_down, w_router, cotangent):
    params = tuple((item.astype(jnp.float32) for item in (norm_attn, norm_ffn, w_query, key_weight, value_weight, w_out, w_gate, w_up, w_down, w_router)))

    def forward(tokens_float, weights):

        def row_function(operands):
            return row_forward(weights, operands[0], operands[1], operands[2])
        return lax.map(jax.checkpoint(row_function), (tokens_float, depths, segments))
    output, pullback = jax.vjp(forward, tokens.astype(jnp.float32), params)
    grad_tokens, grads = pullback(cotangent.astype(jnp.float32))
    return (output, grad_tokens, grads[0], grads[1], grads[2], grads[3], grads[4], grads[5], grads[6], grads[7], grads[8], grads[9])
```

```python
import functools
import itertools
import math

import jax
import jax.numpy as jnp
from jax import lax
from jax.experimental import pallas as pl
from jax.experimental.pallas import tpu as pltpu
from jax.sharding import PartitionSpec as P

QUERY_HEADS = 15
KEY_VALUE_HEADS = 5
HEAD_DIMENSION = 64
RECUR = 2


epsilon = 1e-05
highest_precision = lax.Precision.HIGHEST
masked_score = -1e30


def frequencies(head_size):
    return jnp.exp(
        jnp.arange(head_size // 2, dtype=jnp.float32) * (-2.0 * math.log(10000.0) / head_size)
    )


def rms_scale(values):
    return lax.rsqrt(jnp.mean(values * values, axis=-1, keepdims=True) + epsilon)


def norm_back(grad_norm, values, inverse_rms, gain_vec):
    weighted = grad_norm * gain_vec
    grad_values = inverse_rms * weighted - values * (
        inverse_rms * inverse_rms * inverse_rms
    ) * jnp.mean(weighted * values, axis=-1, keepdims=True)
    grad_gain = jnp.sum((grad_norm * values * inverse_rms).reshape(-1, values.shape[-1]), axis=0)
    return (grad_values, grad_gain)


def rotate(values, cosine_table, sine_values):
    half_width = values.shape[-1] // 2
    first_half = values[..., :half_width]
    second = values[..., half_width:]
    return jnp.concatenate(
        [
            first_half * cosine_table - second * sine_values,
            second * cosine_table + first_half * sine_values,
        ],
        axis=-1,
    )


def inverse_rotation(grads, cosine_table, sine_values):
    half_width = grads.shape[-1] // 2
    first_half = grads[..., :half_width]
    second = grads[..., half_width:]
    return jnp.concatenate(
        [
            first_half * cosine_table + second * sine_values,
            second * cosine_table - first_half * sine_values,
        ],
        axis=-1,
    )


UNIT_COLUMNS = 256


def bits_of(number, count):
    return tuple((number >> (count - 1 - at)) & 1 for at in range(count))


def bit_of(position, bit):
    return lax.rem(position // (1 << bit), 2)


def flipped(position, bit):
    return position + (1 << bit) * (1 - 2 * bit_of(position, bit))


class Piece:
    def __init__(self, at, kept_at, slot, flavour, family, sems, bits):
        self.at, self.kept_at, self.slot, self.family, self.sems = at, kept_at, slot, family, sems
        self.m, self.n = bits
        left = list(range(self.m - 1, -1, -1))
        self.order = []
        for stage in range(self.m):
            place = len(left) - 1 if stage == 0 or flavour == 0 else 0
            self.order.append((left.pop(place), place, len(left)))
        self.last = self.m + self.n
        self.copies = []
        self.blk, self.dp = lax.axis_index("blk"), lax.axis_index("dp")

    def half(self, ref, side):
        rows, columns = self.family["shape"]
        if self.family["split"] == 0:
            return ref.at[pl.ds(pl.multiple_of(side * (rows // 2), rows // 2), rows // 2), :]
        return ref.at[:, pl.ds(pl.multiple_of(side * (columns // 2), columns // 2), columns // 2)]

    def held(self, stage):
        if stage == 0:
            return self.family["part"], self.slot
        return self.family["blk"][stage - 1], self.kept_at

    def start(self, stage):
        m, family = self.m, self.family
        if stage < m:
            bit, place, others = self.order[stage]
            ref, index = self.held(stage)
            chosen = [slice(None)] * (others + 1)
            chosen[place] = 1 - bit_of(self.blk, bit)
            source = ref.at[(index, *chosen)]
            target = family["blk"][stage].at[self.kept_at]
            device = {"blk": flipped(self.blk, bit)}
        elif stage < self.last:
            bit = stage - m
            if bit == 0:
                source = self.half(family["blk"][m - 1].at[self.kept_at], 1 - bit_of(self.dp, 0))
            else:
                source = family["dp"][bit - 1].at[self.kept_at]
            target = family["dp"][bit].at[self.kept_at]
            device = {"dp": flipped(self.dp, bit)}
        else:
            source = self.half(family["out"].at[self.kept_at], bit_of(self.dp, 0))
            target = source
            device = {"dp": flipped(self.dp, 0)}
        copy = pltpu.make_async_remote_copy(
            src_ref=source,
            dst_ref=target,
            send_sem=self.sems[0].at[self.at, stage],
            recv_sem=self.sems[1].at[self.at, stage],
            device_id=device,
            device_id_type=pl.DeviceIdType.MESH,
        )
        copy.start()
        self.copies.append(copy)

    def finish(self, stage):
        m, family = self.m, self.family
        self.copies[stage].wait_recv()
        if stage < m:
            bit, place, others = self.order[stage]
            ref, index = self.held(stage)
            for combo in itertools.product(range(2), repeat=others):
                chosen = list(combo)
                chosen.insert(place, bit_of(self.blk, bit))
                into = family["blk"][stage].at[(self.kept_at, *combo)]
                self.add(into, into, ref.at[(index, *chosen)])
            if stage == 0:
                self.copies[0].wait_send()
        elif stage < self.last:
            bit = stage - m
            got = family["dp"][bit].at[self.kept_at]
            if bit == 0:
                own = self.half(family["blk"][m - 1].at[self.kept_at], bit_of(self.dp, 0))
            else:
                own = family["dp"][bit - 1].at[self.kept_at]
            into = got
            if stage == self.last - 1:
                into = self.half(family["out"].at[self.kept_at], bit_of(self.dp, 0))
            self.add(into, got, own)

    def add(self, into, left, right):
        rows = left.shape[0]
        step = 16 if rows % 16 == 0 else 8

        @pl.loop(0, rows // step)
        def _(at):
            here = pl.ds(pl.multiple_of(at * step, step), step)
            into[here, :] = left[here, :] + right[here, :]

    def drained(self):
        for copy in self.copies[1:]:
            copy.wait_send()


def reduce_kernel(
    sizes,
    inner_hbm, dffn_hbm, nffn_hbm, dgate_hbm, dup_hbm, normed_hbm, attended_hbm, near_hbm, far_hbm, small_hbm,
    out_wide, out_down, out_small,
    inner, dffn, nffn, dgate, dup, normed, attended, near, far,
    nffn_turned, normed_turned, attended_turned,
    part_wide, part_down, part_small,
    *others,
):
    nb, nd, m, n, padded = sizes
    blk_wide, others = others[:m], others[m:]
    blk_down, others = others[:m], others[m:]
    blk_small, others = others[:m], others[m:]
    dp_wide, others = others[:n], others[n:]
    dp_down, others = others[:n], others[n:]
    dp_small, others = others[:n], others[n:]
    load_sems, send_sems, recv_sems = others
    blk, dp = lax.axis_index("blk"), lax.axis_index("dp")

    sources = (inner_hbm, dffn_hbm, nffn_hbm, dgate_hbm, dup_hbm, normed_hbm, attended_hbm, near_hbm, far_hbm, small_hbm)
    places = (inner, dffn, nffn, dgate, dup, normed, attended, near, far, part_small.at[0])
    loads = [
        pltpu.make_async_copy(source, place, load_sems.at[at])
        for at, (source, place) in enumerate(zip(sources, places))
    ]
    for load in loads:
        load.start()

    barrier = pltpu.get_barrier_semaphore()
    partners = [{"blk": flipped(blk, bit)} for bit in range(m)] + [{"dp": flipped(dp, bit)} for bit in range(n)]
    for partner in partners:
        pl.semaphore_signal(barrier, inc=1, device_id=partner, device_id_type=pl.DeviceIdType.MESH)
    pl.semaphore_wait(barrier, len(partners))

    down_rows = part_down.shape[-2]
    wide = {"part": part_wide, "blk": blk_wide, "dp": dp_wide, "out": out_wide,
            "shape": (2 * padded, UNIT_COLUMNS), "split": 1}
    down = {"part": part_down, "blk": blk_down, "dp": dp_down, "out": out_down,
            "shape": (down_rows, dffn.shape[1]), "split": 0}
    small = {"part": part_small, "blk": blk_small, "dp": dp_small, "out": out_small,
             "shape": (16, 128), "split": 0}
    slots = part_wide.shape[0]
    sems = (send_sems, recv_sems)
    pieces = []
    for at in range(5):
        pieces.append(Piece(len(pieces), at, at, len(pieces) % 2, down, sems, (m, n)))
    for at in range(15):
        pieces.append(Piece(len(pieces), at, at % slots, len(pieces) % 2, wide, sems, (m, n)))
    pieces.append(Piece(len(pieces), 0, 0, 0, small, sems, (m, n)))

    def turned_dot(left, right):
        return lax.dot_general(left, right, (((0,), (0,)), ((), ())), preferred_element_type=jnp.float32)

    def plain_dot(left, right):
        return jnp.dot(left, right, preferred_element_type=jnp.float32)

    def compute_down():
        loads[0].wait()
        loads[1].wait()
        width = 640
        group = width // (5 * down_rows)
        for at in range(inner.shape[1] // width):
            result = turned_dot(inner[:, at * width:(at + 1) * width], dffn[...])
            for member in range(group):
                target = bits_of(at * group + member, m)
                for unit in range(5):
                    first = (member * 5 + unit) * down_rows
                    part_down[(unit, *target)] = result[first:first + down_rows].astype(jnp.bfloat16)

    def compute_wide(at):
        slot = at % slots
        if at == 0:
            loads[2].wait()
            nffn_turned[...] = nffn[...].T
            loads[3].wait()
        if at == 5:
            loads[4].wait()
        if at == 10:
            for load in loads[5:9]:
                load.wait()
            normed_turned[...] = normed[...].T
            attended_turned[...] = attended[...].T
        block, at_column = at // 5, (at % 5) * UNIT_COLUMNS
        if block < 2:
            right = dgate if block == 0 else dup
            upper = plain_dot(nffn_turned[...], right[:, at_column:at_column + UNIT_COLUMNS])
            second = 1280 + at_column
            lower = plain_dot(nffn_turned[...], right[:, second:second + UNIT_COLUMNS])
        else:
            upper = plain_dot(normed_turned[...], near[:, at_column:at_column + UNIT_COLUMNS])
            second = 1280 + at_column
            lower = None
            if second < 1600:
                lower = plain_dot(normed_turned[...], near[:, second:second + UNIT_COLUMNS])
            if second >= 1536:
                more = plain_dot(attended_turned[...], far[:, second - 1536:second - 1536 + UNIT_COLUMNS])
                lower = more if lower is None else lower + more
        for target in range(nb):
            here = slice(target * padded, (target + 1) * padded)
            both = jnp.concatenate([upper[here], lower[here]], axis=0)
            part_wide[(slot, *bits_of(target, m))] = both.astype(jnp.bfloat16)

    def compute(piece):
        if piece.family is wide:
            compute_wide(piece.kept_at)
        elif piece.family is small:
            loads[9].wait()
        piece.start(0)

    groups = [pieces[at:at + 2] for at in range(0, 18, 2)] + [pieces[18:]]
    compute_down()
    for piece in groups[0] + groups[1]:
        compute(piece)

    def move(group, stage):
        for piece in group:
            piece.finish(stage)
            piece.start(stage + 1)

    count = len(groups)
    for tick in range(count + 1):
        if tick < count:
            move(groups[tick], 0)
        if tick + 2 < count:
            for piece in groups[tick + 2]:
                compute(piece)
        if tick >= 1:
            move(groups[tick - 1], 1)
        if tick >= 2:
            move(groups[tick - 2], m + n - 1)
        if tick >= 1:
            for stage in range(2, m + n - 1):
                move(groups[tick - 1], stage)
    move(groups[-1], m + n - 1)
    for piece in pieces:
        piece.finish(m + n)
    for piece in pieces:
        piece.drained()


def reduced_weight_grads(sides, small, mesh_sizes):
    nb, nd = mesh_sizes
    m, n = nb.bit_length() - 1, nd.bit_length() - 1
    inner, dffn, nffn, dgate, dup, normed, attended, dkey, dvalue, dquery, dattn = sides
    tokens, width = normed.shape
    rows = width // nb
    padded = -(-rows // 8) * 8
    down_rows = inner.shape[1] // nb // 5

    def spread(array):
        if padded == rows:
            return array
        split = array.reshape(tokens, nb, rows)
        return jnp.pad(split, ((0, 0), (0, 0), (0, padded - rows))).reshape(tokens, nb * padded)

    near_width = dkey.shape[1] + dvalue.shape[1] + dquery.shape[1]
    near = jnp.concatenate([dkey, dvalue, dquery, jnp.zeros((tokens, 1792 - near_width), jnp.bfloat16)], axis=1)
    far = jnp.concatenate([jnp.zeros((tokens, near_width - 1536), jnp.bfloat16), dattn], axis=1)
    small_parts = jnp.pad(small.reshape(4, nb, rows).transpose(1, 0, 2), ((0, 0), (0, 12), (0, 128 - rows)))
    operands = (inner, dffn, spread(nffn), dgate, dup, spread(normed), spread(attended), near, far,
                small_parts.reshape((2,) * m + (16, 128)))
    wide_shape, down_shape = (2 * padded, UNIT_COLUMNS), (down_rows, dffn.shape[1])
    scratch = [pltpu.VMEM(array.shape, array.dtype) for array in operands[:9]]
    scratch += [pltpu.VMEM((nb * padded, tokens), jnp.bfloat16)] * 3
    families = ((15, wide_shape, jnp.bfloat16, 6, 1), (5, down_shape, jnp.bfloat16, 5, 0), (1, (16, 128), jnp.float32, 1, 0))
    for count, shape, dtype, slots, _ in families:
        scratch.append(pltpu.VMEM((slots, *(2,) * m, *shape), dtype))
    for count, shape, dtype, _, _ in families:
        for stage in range(m):
            scratch.append(pltpu.VMEM((count, *(2,) * (m - 1 - stage), *shape), dtype))
    for count, shape, dtype, _, split in families:
        half = (shape[0], shape[1] // 2) if split else (shape[0] // 2, shape[1])
        scratch += [pltpu.VMEM((count, *half), dtype)] * n
    scratch += [pltpu.SemaphoreType.DMA((10,)), pltpu.SemaphoreType.DMA((21, m + n + 1)), pltpu.SemaphoreType.DMA((21, m + n + 1))]
    wide, down, little = pl.pallas_call(
        functools.partial(reduce_kernel, (nb, nd, m, n, padded)),
        out_shape=(
            jax.ShapeDtypeStruct((15, *wide_shape), jnp.bfloat16),
            jax.ShapeDtypeStruct((5, *down_shape), jnp.bfloat16),
            jax.ShapeDtypeStruct((1, 16, 128), jnp.float32),
        ),
        in_specs=[pl.BlockSpec(memory_space=pl.ANY)] * 10,
        out_specs=[pl.BlockSpec(memory_space=pltpu.VMEM)] * 3,
        scratch_shapes=scratch,
        compiler_params=pltpu.CompilerParams(
            collective_id=0, has_side_effects=True, vmem_limit_bytes=60 * 1024 * 1024
        ),
        cost_estimate=pl.CostEstimate(
            flops=2 * tokens * width * 10240, bytes_accessed=20 * 1024 * 1024, transcendentals=0
        ),
        name="weight_grads",
    )(*operands)

    def columns(first):
        five = wide[first:first + 5].reshape(5, 2, padded, UNIT_COLUMNS)
        return five.transpose(2, 1, 0, 3).reshape(padded, 2560)[:rows].astype(jnp.float32)

    gate, up, rest = columns(0), columns(5), columns(10)
    return (
        little[0, 0, :rows],
        little[0, 1, :rows],
        rest[:, 640:1600],
        rest[:, :320],
        rest[:, 320:640],
        rest[:, 1600:],
        gate,
        up,
        down.reshape(5 * down_rows, dffn.shape[1]).astype(jnp.float32),
        little[0, 2:4, :rows].T,
    )


def across(grad_rows, matrix):
    return lax.dot_general(
        grad_rows, matrix, (((1,), (1,)), ((), ())), preferred_element_type=jnp.float32
    )


def allowed_pairs(
    query_segments, key_segments, key_depths, query_positions, key_positions, level_index
):
    same_doc = query_segments[:, None] == key_segments[None, :]
    causal = key_positions[None, :] <= query_positions[:, None]
    live_keys = (key_depths[None, :] > level_index) | (
        key_positions[None, :] == query_positions[:, None]
    )
    return same_doc & causal & live_keys


def score_block(query_rows, key_rows, allowed):
    scores = jnp.einsum(
        "qkgd,jkd->kgqj", query_rows, key_rows, preferred_element_type=jnp.float32
    ) * HEAD_DIMENSION ** (-0.5)
    return jnp.where(allowed[None, None], scores, masked_score)


def attend_row(operands):
    query_rows, key_rows, rows_of_values, allowed = operands
    scores = score_block(query_rows, key_rows, allowed)
    top_score = jnp.max(scores, axis=-1, keepdims=True)
    raised = jnp.exp(scores - top_score)
    totals = jnp.sum(raised, axis=-1, keepdims=True)
    probability = (raised / totals).astype(jnp.bfloat16)
    attended = jnp.einsum(
        "kgqj,jkd->qkgd", probability, rows_of_values, preferred_element_type=jnp.float32
    )
    return (attended, top_score[..., 0] + jnp.log(totals[..., 0]))


def attend_back(operands):
    query_rows, key_rows, rows_of_values, allowed, log_total, grad_attended, carried = operands
    scores = score_block(query_rows, key_rows, allowed)
    probability = jnp.exp(scores - log_total[..., None])
    grad_prob = jnp.einsum(
        "qkgd,jkd->kgqj", grad_attended, rows_of_values, preferred_element_type=jnp.float32
    )
    grad_scores = (probability * (grad_prob - carried[..., None])).astype(jnp.bfloat16)
    grad_queries = jnp.einsum(
        "kgqj,jkd->qkgd", grad_scores, key_rows, preferred_element_type=jnp.float32
    ) * HEAD_DIMENSION ** (-0.5)
    grad_keys = jnp.einsum(
        "kgqj,qkgd->jkd", grad_scores, query_rows, preferred_element_type=jnp.float32
    ) * HEAD_DIMENSION ** (-0.5)
    grad_values = jnp.einsum(
        "kgqj,qkgd->jkd",
        probability.astype(jnp.bfloat16),
        grad_attended,
        preferred_element_type=jnp.float32,
    )
    return (grad_queries, grad_keys, grad_values)


def local(
    tokens,
    depths,
    segments,
    norm_attn,
    norm_ffn,
    w_query,
    key_weight,
    value_weight,
    w_out,
    w_gate,
    w_up,
    w_down,
    w_router,
    cotangent,
    mesh_sizes,
):
    count_of_rows, piece_length, model_width = tokens.shape
    complete_length = piece_length * lax.axis_size("blk")
    query_group_width = QUERY_HEADS // KEY_VALUE_HEADS
    token_count = count_of_rows * piece_length
    width_of_keys = KEY_VALUE_HEADS * HEAD_DIMENSION
    query_positions = lax.axis_index("blk") * piece_length + jnp.arange(
        piece_length, dtype=jnp.int32
    )
    key_positions = jnp.arange(complete_length, dtype=jnp.int32)
    angles = query_positions.astype(jnp.float32)[:, None] * frequencies(HEAD_DIMENSION)[None, :]
    cosine_table = jnp.cos(angles)[:, None, :]
    sine_values = jnp.sin(angles)[:, None, :]
    gain_attn = norm_attn.astype(jnp.float32)
    gain_ffn = norm_ffn.astype(jnp.float32)
    router_float = w_router.astype(jnp.float32)

    def recursion(hidden_in, level_index, kept_keys):
        scale_attn = rms_scale(hidden_in)
        flat_normed = (
            (hidden_in * scale_attn * gain_attn)
            .astype(jnp.bfloat16)
            .reshape(token_count, model_width)
        )
        query_pre = jnp.dot(flat_normed, w_query, preferred_element_type=jnp.float32).reshape(
            count_of_rows, piece_length, QUERY_HEADS, HEAD_DIMENSION
        )
        query_rows = rotate(query_pre, cosine_table, sine_values).astype(jnp.bfloat16)
        key_before_rotation = jnp.dot(
            flat_normed, key_weight, preferred_element_type=jnp.float32
        ).reshape(count_of_rows, piece_length, KEY_VALUE_HEADS, HEAD_DIMENSION)
        key_rows = (
            rotate(key_before_rotation, cosine_table, sine_values)
            .astype(jnp.bfloat16)
            .reshape(count_of_rows, piece_length, width_of_keys)
        )
        rows_of_values = (
            jnp.dot(flat_normed, value_weight, preferred_element_type=jnp.float32)
            .astype(jnp.bfloat16)
            .reshape(count_of_rows, piece_length, width_of_keys)
        )
        kept_keys = (
            lax.all_gather(key_rows, "blk", axis=1, tiled=True),
            lax.all_gather(rows_of_values, "blk", axis=1, tiled=True),
            lax.all_gather(depths, "blk", axis=1, tiled=True),
            lax.all_gather(segments, "blk", axis=1, tiled=True),
        )
        gathered_keys, gathered_values, all_depths, all_segments = kept_keys

        def row_mask(query_segments, key_segments, key_depths):
            return allowed_pairs(
                query_segments,
                key_segments,
                key_depths,
                query_positions,
                key_positions,
                level_index,
            )

        allowed = jax.vmap(row_mask)(segments, all_segments, all_depths)
        grouped_queries = query_rows.reshape(
            count_of_rows, piece_length, KEY_VALUE_HEADS, query_group_width, HEAD_DIMENSION
        )
        heads_of_keys = gathered_keys.reshape(
            count_of_rows, complete_length, KEY_VALUE_HEADS, HEAD_DIMENSION
        )
        heads_of_values = gathered_values.reshape(
            count_of_rows, complete_length, KEY_VALUE_HEADS, HEAD_DIMENSION
        )
        attended, log_total = lax.map(
            attend_row, (grouped_queries, heads_of_keys, heads_of_values, allowed)
        )
        attended_low = attended.reshape(token_count, QUERY_HEADS * HEAD_DIMENSION).astype(
            jnp.bfloat16
        )
        attn = jnp.dot(attended_low, w_out, preferred_element_type=jnp.float32).reshape(
            count_of_rows, piece_length, model_width
        )
        middle = hidden_in + attn
        scale_ffn = rms_scale(middle)
        normed_ffn = (
            (middle * scale_ffn * gain_ffn).astype(jnp.bfloat16).reshape(token_count, model_width)
        )
        gate_pre = jnp.dot(normed_ffn, w_gate, preferred_element_type=jnp.float32)
        up_pre = jnp.dot(normed_ffn, w_up, preferred_element_type=jnp.float32)
        activated = jax.nn.sigmoid(gate_pre)
        inner_low = (gate_pre * activated * up_pre).astype(jnp.bfloat16)
        ffn = jnp.dot(inner_low, w_down, preferred_element_type=jnp.float32).reshape(
            count_of_rows, piece_length, model_width
        )
        router_logit = jnp.dot(
            hidden_in.reshape(token_count, model_width),
            router_float[:, level_index],
            precision=highest_precision,
        ).reshape(count_of_rows, piece_length)
        chosen = jax.nn.sigmoid(router_logit)
        active = depths > level_index
        weight = jnp.where(active, chosen, 0.0)
        branch = attn + ffn
        hidden_next = hidden_in + weight[..., None] * branch
        pieces = {
            "scale_attn": scale_attn,
            "flat_normed": flat_normed,
            "grouped": grouped_queries,
            "key_heads": heads_of_keys,
            "value_heads": heads_of_values,
            "allowed": allowed,
            "attended": attended,
            "log_total": log_total,
            "attended_low": attended_low,
            "middle": middle,
            "scale_ffn": scale_ffn,
            "normed_ffn": normed_ffn,
            "gate_pre": gate_pre,
            "up_pre": up_pre,
            "activated": activated,
            "inner_low": inner_low,
            "chosen": chosen,
            "active": active,
            "weight": weight,
            "branch": branch,
        }
        return (hidden_next, kept_keys, pieces)

    hidden = tokens.astype(jnp.float32)
    stored_hidden = []
    stored_list = []
    for level_index in range(RECUR):
        stored_hidden.append(hidden)
        hidden, kept_keys, unused_pieces = recursion(hidden, level_index, None)
        stored_list.append(kept_keys)
    acc_norm_attn = jnp.zeros((model_width,), jnp.float32)
    acc_norm_ffn = jnp.zeros((model_width,), jnp.float32)
    sides = []
    router_parts = [None] * RECUR
    gradient = cotangent.astype(jnp.float32)
    for level_index in reversed(range(RECUR)):
        hidden_in = stored_hidden[level_index]
        unused_next, unused_keys, pieces = recursion(hidden_in, level_index, None)
        chosen = pieces["chosen"]
        d_branch = pieces["weight"][..., None] * gradient
        grad_chosen = jnp.where(
            pieces["active"], jnp.sum(gradient * pieces["branch"], axis=-1), 0.0
        )
        grad_logit = grad_chosen * chosen * (1.0 - chosen)
        flat_in = hidden_in.reshape(token_count, model_width)
        router_parts[level_index] = jnp.dot(
            grad_logit.reshape(token_count), flat_in, precision=highest_precision
        )
        grad_hidden = gradient + grad_logit[..., None] * router_float[:, level_index]
        grad_ffn_low = d_branch.reshape(token_count, model_width).astype(jnp.bfloat16)
        grad_inner = across(grad_ffn_low, w_down)
        gate_pre = pieces["gate_pre"]
        activated = pieces["activated"]
        grad_gate_low = (
            grad_inner * pieces["up_pre"] * activated * (1.0 + gate_pre * (1.0 - activated))
        ).astype(jnp.bfloat16)
        grad_up_low = (grad_inner * gate_pre * activated).astype(jnp.bfloat16)
        grad_normed_ffn = (across(grad_gate_low, w_gate) + across(grad_up_low, w_up)).reshape(
            count_of_rows, piece_length, model_width
        )
        grad_middle, gain_part = norm_back(
            grad_normed_ffn, pieces["middle"], pieces["scale_ffn"], gain_ffn
        )
        acc_norm_ffn = acc_norm_ffn + gain_part
        grad_hidden = grad_hidden + grad_middle
        grad_attn_low = (
            (d_branch + grad_middle).reshape(token_count, model_width).astype(jnp.bfloat16)
        )
        grad_attended = (
            across(grad_attn_low, w_out)
            .astype(jnp.bfloat16)
            .reshape(
                count_of_rows, piece_length, KEY_VALUE_HEADS, query_group_width, HEAD_DIMENSION
            )
        )
        carried = jnp.transpose(
            jnp.sum(grad_attended.astype(jnp.float32) * pieces["attended"], axis=-1), (0, 2, 3, 1)
        )
        grouped_queries = pieces["grouped"]
        heads_of_keys = pieces["key_heads"]
        heads_of_values = pieces["value_heads"]
        allowed = pieces["allowed"]
        log_total = pieces["log_total"]
        grad_queries, grad_keys, grad_values = lax.map(
            attend_back,
            (
                grouped_queries,
                heads_of_keys,
                heads_of_values,
                allowed,
                log_total,
                grad_attended,
                carried,
            ),
        )
        summed_keys, value_sum = (
            lax.psum_scatter(
                grad_keys.reshape(count_of_rows, complete_length, width_of_keys).astype(
                    jnp.bfloat16
                ),
                "blk",
                scatter_dimension=1,
                tiled=True,
            ).astype(jnp.float32),
            lax.psum_scatter(
                grad_values.reshape(count_of_rows, complete_length, width_of_keys).astype(
                    jnp.bfloat16
                ),
                "blk",
                scatter_dimension=1,
                tiled=True,
            ).astype(jnp.float32),
        )
        grad_query_low = (
            inverse_rotation(
                grad_queries.reshape(count_of_rows, piece_length, QUERY_HEADS, HEAD_DIMENSION),
                cosine_table,
                sine_values,
            )
            .astype(jnp.bfloat16)
            .reshape(token_count, QUERY_HEADS * HEAD_DIMENSION)
        )
        grad_key_low = (
            inverse_rotation(
                summed_keys.reshape(count_of_rows, piece_length, KEY_VALUE_HEADS, HEAD_DIMENSION),
                cosine_table,
                sine_values,
            )
            .astype(jnp.bfloat16)
            .reshape(token_count, width_of_keys)
        )
        grad_value_low = value_sum.astype(jnp.bfloat16).reshape(token_count, width_of_keys)
        flat_normed = pieces["flat_normed"]
        sides.append(
            (
                pieces["inner_low"],
                grad_ffn_low,
                pieces["normed_ffn"],
                grad_gate_low,
                grad_up_low,
                flat_normed,
                pieces["attended_low"],
                grad_key_low,
                grad_value_low,
                grad_query_low,
                grad_attn_low,
            )
        )
        grad_normed = (
            across(grad_query_low, w_query)
            + across(grad_key_low, key_weight)
            + across(grad_value_low, value_weight)
        )
        grad_input, gain_part = norm_back(
            grad_normed.reshape(count_of_rows, piece_length, model_width),
            hidden_in,
            pieces["scale_attn"],
            gain_attn,
        )
        acc_norm_attn = acc_norm_attn + gain_part
        gradient = grad_hidden + grad_input
    small = jnp.stack([acc_norm_attn, acc_norm_ffn] + router_parts)
    shares = reduced_weight_grads(
        tuple(jnp.concatenate(pair, axis=0) for pair in zip(*sides)), small, mesh_sizes
    )
    return (
        hidden,
        gradient,
        shares[0],
        shares[1],
        shares[2],
        shares[3],
        shares[4],
        shares[5],
        shares[6],
        shares[7],
        shares[8],
        shares[9],
    )


def solution(mesh):
    sizes = (mesh.shape["blk"], mesh.shape["dp"])
    return jax.shard_map(
        functools.partial(local, mesh_sizes=sizes),
        mesh=mesh,
        in_specs=(
            P("dp", "blk", None),
            P("dp", "blk"),
            P("dp", "blk"),
            P(),
            P(),
            P(),
            P(),
            P(),
            P(),
            P(),
            P(),
            P(),
            P(),
            P("dp", "blk", None),
        ),
        out_specs=(
            P("dp", "blk", None),
            P("dp", "blk", None),
            P("blk"),
            P("blk"),
            P("blk", None),
            P("blk", None),
            P("blk", None),
            P("blk", None),
            P("blk", None),
            P("blk", None),
            P("blk", None),
            P("blk", None),
        ),
        check_vma=False,
    )
```

```python
import functools
import itertools
import math

import jax
import jax.numpy as jnp
from jax import lax
from jax.experimental import pallas as pl
from jax.experimental.pallas import tpu as pltpu
from jax.sharding import PartitionSpec as P

QUERY_HEADS = 15
KEY_VALUE_HEADS = 5
HEAD_DIMENSION = 64
RECUR = 2


epsilon = 1e-05
highest_precision = lax.Precision.HIGHEST
masked_score = -1e30


def frequencies(head_size):
    return jnp.exp(
        jnp.arange(head_size // 2, dtype=jnp.float32) * (-2.0 * math.log(10000.0) / head_size)
    )


def rms_scale(values):
    return lax.rsqrt(jnp.mean(values * values, axis=-1, keepdims=True) + epsilon)


def norm_back(grad_norm, values, inverse_rms, gain_vec):
    weighted = grad_norm * gain_vec
    grad_values = inverse_rms * weighted - values * (
        inverse_rms * inverse_rms * inverse_rms
    ) * jnp.mean(weighted * values, axis=-1, keepdims=True)
    grad_gain = jnp.sum((grad_norm * values * inverse_rms).reshape(-1, values.shape[-1]), axis=0)
    return (grad_values, grad_gain)


def rotate(values, cosine_table, sine_values):
    half_width = values.shape[-1] // 2
    first_half = values[..., :half_width]
    second = values[..., half_width:]
    return jnp.concatenate(
        [
            first_half * cosine_table - second * sine_values,
            second * cosine_table + first_half * sine_values,
        ],
        axis=-1,
    )


def inverse_rotation(grads, cosine_table, sine_values):
    half_width = grads.shape[-1] // 2
    first_half = grads[..., :half_width]
    second = grads[..., half_width:]
    return jnp.concatenate(
        [
            first_half * cosine_table + second * sine_values,
            second * cosine_table - first_half * sine_values,
        ],
        axis=-1,
    )


UNIT_COLUMNS = 256


def bits_of(number, count):
    return tuple((number >> (count - 1 - at)) & 1 for at in range(count))


def bit_of(position, bit):
    return lax.rem(position // (1 << bit), 2)


def flipped(position, bit):
    return position + (1 << bit) * (1 - 2 * bit_of(position, bit))


class Piece:
    def __init__(self, at, kept_at, slot, flavour, family, sems, bits):
        self.at, self.kept_at, self.slot, self.family, self.sems = at, kept_at, slot, family, sems
        self.m, self.n = bits
        left = list(range(self.m - 1, -1, -1))
        self.order = []
        for stage in range(self.m):
            place = len(left) - 1 if stage == 0 or flavour == 0 else 0
            self.order.append((left.pop(place), place, len(left)))
        self.last = self.m + self.n
        self.copies = []
        self.blk, self.dp = lax.axis_index("blk"), lax.axis_index("dp")

    def half(self, ref, side):
        rows, columns = self.family["shape"]
        if self.family["split"] == 0:
            return ref.at[pl.ds(pl.multiple_of(side * (rows // 2), rows // 2), rows // 2), :]
        return ref.at[:, pl.ds(pl.multiple_of(side * (columns // 2), columns // 2), columns // 2)]

    def held(self, stage):
        if stage == 0:
            return self.family["part"], self.slot
        return self.family["blk"][stage - 1], self.kept_at

    def start(self, stage):
        m, family = self.m, self.family
        if stage < m:
            bit, place, others = self.order[stage]
            ref, index = self.held(stage)
            chosen = [slice(None)] * (others + 1)
            chosen[place] = 1 - bit_of(self.blk, bit)
            source = ref.at[(index, *chosen)]
            target = family["blk"][stage].at[self.kept_at]
            device = {"blk": flipped(self.blk, bit)}
        elif stage < self.last:
            bit = stage - m
            if bit == 0:
                source = self.half(family["blk"][m - 1].at[self.kept_at], 1 - bit_of(self.dp, 0))
            else:
                source = family["dp"][bit - 1].at[self.kept_at]
            target = family["dp"][bit].at[self.kept_at]
            device = {"dp": flipped(self.dp, bit)}
        else:
            source = self.half(family["out"].at[self.kept_at], bit_of(self.dp, 0))
            target = source
            device = {"dp": flipped(self.dp, 0)}
        copy = pltpu.make_async_remote_copy(
            src_ref=source,
            dst_ref=target,
            send_sem=self.sems[0].at[self.at, stage],
            recv_sem=self.sems[1].at[self.at, stage],
            device_id=device,
            device_id_type=pl.DeviceIdType.MESH,
        )
        copy.start()
        self.copies.append(copy)

    def finish(self, stage):
        m, family = self.m, self.family
        self.copies[stage].wait_recv()
        if stage < m:
            bit, place, others = self.order[stage]
            ref, index = self.held(stage)
            for combo in itertools.product(range(2), repeat=others):
                chosen = list(combo)
                chosen.insert(place, bit_of(self.blk, bit))
                into = family["blk"][stage].at[(self.kept_at, *combo)]
                self.add(into, into, ref.at[(index, *chosen)])
            if stage == 0:
                self.copies[0].wait_send()
        elif stage < self.last:
            bit = stage - m
            got = family["dp"][bit].at[self.kept_at]
            if bit == 0:
                own = self.half(family["blk"][m - 1].at[self.kept_at], bit_of(self.dp, 0))
            else:
                own = family["dp"][bit - 1].at[self.kept_at]
            into = got
            if stage == self.last - 1:
                into = self.half(family["out"].at[self.kept_at], bit_of(self.dp, 0))
            self.add(into, got, own)

    def add(self, into, left, right):
        into[...] = left[...] + right[...]

    def drained(self):
        for copy in self.copies[1:]:
            copy.wait_send()


def reduce_kernel(
    sizes,
    inner_hbm, dffn_hbm, nffn_hbm, dgate_hbm, dup_hbm, normed_hbm, attended_hbm, near_hbm, far_hbm, small_hbm,
    out_wide, out_down, out_small,
    inner, dffn, nffn, dgate, dup, normed, attended, near, far,
    nffn_turned, normed_turned, attended_turned,
    part_wide, part_down, part_small,
    *others,
):
    nb, nd, m, n, padded = sizes
    blk_wide, others = others[:m], others[m:]
    blk_down, others = others[:m], others[m:]
    blk_small, others = others[:m], others[m:]
    dp_wide, others = others[:n], others[n:]
    dp_down, others = others[:n], others[n:]
    dp_small, others = others[:n], others[n:]
    load_sems, send_sems, recv_sems = others
    blk, dp = lax.axis_index("blk"), lax.axis_index("dp")

    sources = (inner_hbm, dffn_hbm, nffn_hbm, dgate_hbm, dup_hbm, normed_hbm, attended_hbm, near_hbm, far_hbm, small_hbm)
    places = (inner, dffn, nffn, dgate, dup, normed, attended, near, far, part_small.at[0])
    loads = [
        pltpu.make_async_copy(source, place, load_sems.at[at])
        for at, (source, place) in enumerate(zip(sources, places))
    ]
    for load in loads:
        load.start()

    barrier = pltpu.get_barrier_semaphore()
    partners = [{"blk": flipped(blk, bit)} for bit in range(m)] + [{"dp": flipped(dp, bit)} for bit in range(n)]
    for partner in partners:
        pl.semaphore_signal(barrier, inc=1, device_id=partner, device_id_type=pl.DeviceIdType.MESH)
    pl.semaphore_wait(barrier, len(partners))

    down_rows = part_down.shape[-2]
    wide = {"part": part_wide, "blk": blk_wide, "dp": dp_wide, "out": out_wide,
            "shape": (2 * padded, UNIT_COLUMNS), "split": 1}
    down = {"part": part_down, "blk": blk_down, "dp": dp_down, "out": out_down,
            "shape": (down_rows, dffn.shape[1]), "split": 0}
    small = {"part": part_small, "blk": blk_small, "dp": dp_small, "out": out_small,
             "shape": (16, 128), "split": 0}
    slots = part_wide.shape[0]
    sems = (send_sems, recv_sems)
    pieces = []
    for at in range(5):
        pieces.append(Piece(len(pieces), at, at, len(pieces) % 2, down, sems, (m, n)))
    for at in range(15):
        pieces.append(Piece(len(pieces), at, at % slots, len(pieces) % 2, wide, sems, (m, n)))
    pieces.append(Piece(len(pieces), 0, 0, 0, small, sems, (m, n)))

    def turned_dot(left, right):
        return lax.dot_general(left, right, (((0,), (0,)), ((), ())), preferred_element_type=jnp.float32)

    def plain_dot(left, right):
        return jnp.dot(left, right, preferred_element_type=jnp.float32)

    def compute_down():
        loads[0].wait()
        loads[1].wait()
        width = 640
        group = width // (5 * down_rows)
        for at in range(inner.shape[1] // width):
            result = turned_dot(inner[:, at * width:(at + 1) * width], dffn[...])
            for member in range(group):
                target = bits_of(at * group + member, m)
                for unit in range(5):
                    first = (member * 5 + unit) * down_rows
                    part_down[(unit, *target)] = result[first:first + down_rows].astype(jnp.bfloat16)

    def compute_wide(at):
        slot = at % slots
        if at == 0:
            loads[2].wait()
            nffn_turned[...] = nffn[...].T
            loads[3].wait()
        if at == 5:
            loads[4].wait()
        if at == 10:
            for load in loads[5:9]:
                load.wait()
            normed_turned[...] = normed[...].T
            attended_turned[...] = attended[...].T
        block, at_column = at // 5, (at % 5) * UNIT_COLUMNS
        if block < 2:
            right = dgate if block == 0 else dup
            upper = plain_dot(nffn_turned[...], right[:, at_column:at_column + UNIT_COLUMNS])
            second = 1280 + at_column
            lower = plain_dot(nffn_turned[...], right[:, second:second + UNIT_COLUMNS])
        else:
            upper = plain_dot(normed_turned[...], near[:, at_column:at_column + UNIT_COLUMNS])
            second = 1280 + at_column
            lower = None
            if second < 1600:
                lower = plain_dot(normed_turned[...], near[:, second:second + UNIT_COLUMNS])
            if second >= 1536:
                more = plain_dot(attended_turned[...], far[:, second - 1536:second - 1536 + UNIT_COLUMNS])
                lower = more if lower is None else lower + more
        for target in range(nb):
            here = slice(target * padded, (target + 1) * padded)
            both = jnp.concatenate([upper[here], lower[here]], axis=0)
            part_wide[(slot, *bits_of(target, m))] = both.astype(jnp.bfloat16)

    def compute(piece):
        if piece.family is wide:
            compute_wide(piece.kept_at)
        elif piece.family is small:
            loads[9].wait()
        piece.start(0)

    groups = [pieces[at:at + 2] for at in range(0, 18, 2)] + [pieces[18:]]
    compute_down()
    for piece in groups[0] + groups[1]:
        compute(piece)

    def move(group, stage):
        for piece in group:
            piece.finish(stage)
            piece.start(stage + 1)

    count = len(groups)
    for tick in range(count + m + n - 1):
        for stage in range(m + n - 1, -1, -1):
            if 0 <= tick - stage < count:
                move(groups[tick - stage], stage)
        if tick + 2 < count:
            for piece in groups[tick + 2]:
                compute(piece)
    for piece in pieces:
        piece.finish(m + n)
    for piece in pieces:
        piece.drained()


def reduced_weight_grads(sides, small, mesh_sizes):
    nb, nd = mesh_sizes
    m, n = nb.bit_length() - 1, nd.bit_length() - 1
    inner, dffn, nffn, dgate, dup, normed, attended, dkey, dvalue, dquery, dattn = sides
    tokens, width = normed.shape
    rows = width // nb
    padded = -(-rows // 8) * 8
    down_rows = inner.shape[1] // nb // 5

    def spread(array):
        if padded == rows:
            return array
        split = array.reshape(tokens, nb, rows)
        return jnp.pad(split, ((0, 0), (0, 0), (0, padded - rows))).reshape(tokens, nb * padded)

    near_width = dkey.shape[1] + dvalue.shape[1] + dquery.shape[1]
    near = jnp.concatenate([dkey, dvalue, dquery, jnp.zeros((tokens, 1792 - near_width), jnp.bfloat16)], axis=1)
    far = jnp.concatenate([jnp.zeros((tokens, near_width - 1536), jnp.bfloat16), dattn], axis=1)
    small_parts = jnp.pad(small.reshape(4, nb, rows).transpose(1, 0, 2), ((0, 0), (0, 12), (0, 128 - rows)))
    operands = (inner, dffn, spread(nffn), dgate, dup, spread(normed), spread(attended), near, far,
                small_parts.reshape((2,) * m + (16, 128)))
    wide_shape, down_shape = (2 * padded, UNIT_COLUMNS), (down_rows, dffn.shape[1])
    scratch = [pltpu.VMEM(array.shape, array.dtype) for array in operands[:9]]
    scratch += [pltpu.VMEM((nb * padded, tokens), jnp.bfloat16)] * 3
    families = ((15, wide_shape, jnp.bfloat16, 6, 1), (5, down_shape, jnp.bfloat16, 5, 0), (1, (16, 128), jnp.float32, 1, 0))
    for count, shape, dtype, slots, _ in families:
        scratch.append(pltpu.VMEM((slots, *(2,) * m, *shape), dtype))
    for count, shape, dtype, _, _ in families:
        for stage in range(m):
            scratch.append(pltpu.VMEM((count, *(2,) * (m - 1 - stage), *shape), dtype))
    for count, shape, dtype, _, split in families:
        half = (shape[0], shape[1] // 2) if split else (shape[0] // 2, shape[1])
        scratch += [pltpu.VMEM((count, *half), dtype)] * n
    scratch += [pltpu.SemaphoreType.DMA((10,)), pltpu.SemaphoreType.DMA((21, m + n + 1)), pltpu.SemaphoreType.DMA((21, m + n + 1))]
    wide, down, little = pl.pallas_call(
        functools.partial(reduce_kernel, (nb, nd, m, n, padded)),
        out_shape=(
            jax.ShapeDtypeStruct((15, *wide_shape), jnp.bfloat16),
            jax.ShapeDtypeStruct((5, *down_shape), jnp.bfloat16),
            jax.ShapeDtypeStruct((1, 16, 128), jnp.float32),
        ),
        in_specs=[pl.BlockSpec(memory_space=pl.ANY)] * 10,
        out_specs=[pl.BlockSpec(memory_space=pltpu.VMEM)] * 3,
        scratch_shapes=scratch,
        compiler_params=pltpu.CompilerParams(
            collective_id=0, has_side_effects=True, vmem_limit_bytes=60 * 1024 * 1024
        ),
        cost_estimate=pl.CostEstimate(
            flops=2 * tokens * width * 10240, bytes_accessed=20 * 1024 * 1024, transcendentals=0
        ),
        name="weight_grads",
    )(*operands)

    def columns(first):
        five = wide[first:first + 5].reshape(5, 2, padded, UNIT_COLUMNS)
        return five.transpose(2, 1, 0, 3).reshape(padded, 2560)[:rows].astype(jnp.float32)

    gate, up, rest = columns(0), columns(5), columns(10)
    return (
        little[0, 0, :rows],
        little[0, 1, :rows],
        rest[:, 640:1600],
        rest[:, :320],
        rest[:, 320:640],
        rest[:, 1600:],
        gate,
        up,
        down.reshape(5 * down_rows, dffn.shape[1]).astype(jnp.float32),
        little[0, 2:4, :rows].T,
    )


def across(grad_rows, matrix):
    return lax.dot_general(
        grad_rows, matrix, (((1,), (1,)), ((), ())), preferred_element_type=jnp.float32
    )


def allowed_pairs(
    query_segments, key_segments, key_depths, query_positions, key_positions, level_index
):
    same_doc = query_segments[:, None] == key_segments[None, :]
    causal = key_positions[None, :] <= query_positions[:, None]
    live_keys = (key_depths[None, :] > level_index) | (
        key_positions[None, :] == query_positions[:, None]
    )
    return same_doc & causal & live_keys


def score_block(query_rows, key_rows, allowed):
    scores = jnp.einsum(
        "qkgd,jkd->kgqj", query_rows, key_rows, preferred_element_type=jnp.float32
    ) * HEAD_DIMENSION ** (-0.5)
    return jnp.where(allowed[None, None], scores, masked_score)


def attend_row(operands):
    query_rows, key_rows, rows_of_values, allowed = operands
    scores = score_block(query_rows, key_rows, allowed)
    top_score = jnp.max(scores, axis=-1, keepdims=True)
    raised = jnp.exp(scores - top_score)
    totals = jnp.sum(raised, axis=-1, keepdims=True)
    probability = (raised / totals).astype(jnp.bfloat16)
    attended = jnp.einsum(
        "kgqj,jkd->qkgd", probability, rows_of_values, preferred_element_type=jnp.float32
    )
    return (attended, top_score[..., 0] + jnp.log(totals[..., 0]))


def attend_back(operands):
    query_rows, key_rows, rows_of_values, allowed, log_total, grad_attended, carried = operands
    scores = score_block(query_rows, key_rows, allowed)
    probability = jnp.exp(scores - log_total[..., None])
    grad_prob = jnp.einsum(
        "qkgd,jkd->kgqj", grad_attended, rows_of_values, preferred_element_type=jnp.float32
    )
    grad_scores = (probability * (grad_prob - carried[..., None])).astype(jnp.bfloat16)
    grad_queries = jnp.einsum(
        "kgqj,jkd->qkgd", grad_scores, key_rows, preferred_element_type=jnp.float32
    ) * HEAD_DIMENSION ** (-0.5)
    grad_keys = jnp.einsum(
        "kgqj,qkgd->jkd", grad_scores, query_rows, preferred_element_type=jnp.float32
    ) * HEAD_DIMENSION ** (-0.5)
    grad_values = jnp.einsum(
        "kgqj,qkgd->jkd",
        probability.astype(jnp.bfloat16),
        grad_attended,
        preferred_element_type=jnp.float32,
    )
    return (grad_queries, grad_keys, grad_values)


def local(
    tokens,
    depths,
    segments,
    norm_attn,
    norm_ffn,
    w_query,
    key_weight,
    value_weight,
    w_out,
    w_gate,
    w_up,
    w_down,
    w_router,
    cotangent,
    mesh_sizes,
):
    count_of_rows, piece_length, model_width = tokens.shape
    complete_length = piece_length * lax.axis_size("blk")
    query_group_width = QUERY_HEADS // KEY_VALUE_HEADS
    token_count = count_of_rows * piece_length
    width_of_keys = KEY_VALUE_HEADS * HEAD_DIMENSION
    query_positions = lax.axis_index("blk") * piece_length + jnp.arange(
        piece_length, dtype=jnp.int32
    )
    key_positions = jnp.arange(complete_length, dtype=jnp.int32)
    angles = query_positions.astype(jnp.float32)[:, None] * frequencies(HEAD_DIMENSION)[None, :]
    cosine_table = jnp.cos(angles)[:, None, :]
    sine_values = jnp.sin(angles)[:, None, :]
    gain_attn = norm_attn.astype(jnp.float32)
    gain_ffn = norm_ffn.astype(jnp.float32)
    router_float = w_router.astype(jnp.float32)

    def recursion(hidden_in, level_index, kept_keys):
        scale_attn = rms_scale(hidden_in)
        flat_normed = (
            (hidden_in * scale_attn * gain_attn)
            .astype(jnp.bfloat16)
            .reshape(token_count, model_width)
        )
        query_pre = jnp.dot(flat_normed, w_query, preferred_element_type=jnp.float32).reshape(
            count_of_rows, piece_length, QUERY_HEADS, HEAD_DIMENSION
        )
        query_rows = rotate(query_pre, cosine_table, sine_values).astype(jnp.bfloat16)
        key_before_rotation = jnp.dot(
            flat_normed, key_weight, preferred_element_type=jnp.float32
        ).reshape(count_of_rows, piece_length, KEY_VALUE_HEADS, HEAD_DIMENSION)
        key_rows = (
            rotate(key_before_rotation, cosine_table, sine_values)
            .astype(jnp.bfloat16)
            .reshape(count_of_rows, piece_length, width_of_keys)
        )
        rows_of_values = (
            jnp.dot(flat_normed, value_weight, preferred_element_type=jnp.float32)
            .astype(jnp.bfloat16)
            .reshape(count_of_rows, piece_length, width_of_keys)
        )
        kept_keys = (
            lax.all_gather(key_rows, "blk", axis=1, tiled=True),
            lax.all_gather(rows_of_values, "blk", axis=1, tiled=True),
            lax.all_gather(depths, "blk", axis=1, tiled=True),
            lax.all_gather(segments, "blk", axis=1, tiled=True),
        )
        gathered_keys, gathered_values, all_depths, all_segments = kept_keys

        def row_mask(query_segments, key_segments, key_depths):
            return allowed_pairs(
                query_segments,
                key_segments,
                key_depths,
                query_positions,
                key_positions,
                level_index,
            )

        allowed = jax.vmap(row_mask)(segments, all_segments, all_depths)
        grouped_queries = query_rows.reshape(
            count_of_rows, piece_length, KEY_VALUE_HEADS, query_group_width, HEAD_DIMENSION
        )
        heads_of_keys = gathered_keys.reshape(
            count_of_rows, complete_length, KEY_VALUE_HEADS, HEAD_DIMENSION
        )
        heads_of_values = gathered_values.reshape(
            count_of_rows, complete_length, KEY_VALUE_HEADS, HEAD_DIMENSION
        )
        attended, log_total = lax.map(
            attend_row, (grouped_queries, heads_of_keys, heads_of_values, allowed)
        )
        attended_low = attended.reshape(token_count, QUERY_HEADS * HEAD_DIMENSION).astype(
            jnp.bfloat16
        )
        attn = jnp.dot(attended_low, w_out, preferred_element_type=jnp.float32).reshape(
            count_of_rows, piece_length, model_width
        )
        middle = hidden_in + attn
        scale_ffn = rms_scale(middle)
        normed_ffn = (
            (middle * scale_ffn * gain_ffn).astype(jnp.bfloat16).reshape(token_count, model_width)
        )
        gate_pre = jnp.dot(normed_ffn, w_gate, preferred_element_type=jnp.float32)
        up_pre = jnp.dot(normed_ffn, w_up, preferred_element_type=jnp.float32)
        activated = jax.nn.sigmoid(gate_pre)
        inner_low = (gate_pre * activated * up_pre).astype(jnp.bfloat16)
        ffn = jnp.dot(inner_low, w_down, preferred_element_type=jnp.float32).reshape(
            count_of_rows, piece_length, model_width
        )
        router_logit = jnp.dot(
            hidden_in.reshape(token_count, model_width),
            router_float[:, level_index],
            precision=highest_precision,
        ).reshape(count_of_rows, piece_length)
        chosen = jax.nn.sigmoid(router_logit)
        active = depths > level_index
        weight = jnp.where(active, chosen, 0.0)
        branch = attn + ffn
        hidden_next = hidden_in + weight[..., None] * branch
        pieces = {
            "scale_attn": scale_attn,
            "flat_normed": flat_normed,
            "grouped": grouped_queries,
            "key_heads": heads_of_keys,
            "value_heads": heads_of_values,
            "allowed": allowed,
            "attended": attended,
            "log_total": log_total,
            "attended_low": attended_low,
            "middle": middle,
            "scale_ffn": scale_ffn,
            "normed_ffn": normed_ffn,
            "gate_pre": gate_pre,
            "up_pre": up_pre,
            "activated": activated,
            "inner_low": inner_low,
            "chosen": chosen,
            "active": active,
            "weight": weight,
            "branch": branch,
        }
        return (hidden_next, kept_keys, pieces)

    hidden = tokens.astype(jnp.float32)
    stored_hidden = []
    stored_list = []
    for level_index in range(RECUR):
        stored_hidden.append(hidden)
        hidden, kept_keys, unused_pieces = recursion(hidden, level_index, None)
        stored_list.append(kept_keys)
    acc_norm_attn = jnp.zeros((model_width,), jnp.float32)
    acc_norm_ffn = jnp.zeros((model_width,), jnp.float32)
    sides = []
    router_parts = [None] * RECUR
    gradient = cotangent.astype(jnp.float32)
    for level_index in reversed(range(RECUR)):
        hidden_in = stored_hidden[level_index]
        unused_next, unused_keys, pieces = recursion(hidden_in, level_index, None)
        chosen = pieces["chosen"]
        d_branch = pieces["weight"][..., None] * gradient
        grad_chosen = jnp.where(
            pieces["active"], jnp.sum(gradient * pieces["branch"], axis=-1), 0.0
        )
        grad_logit = grad_chosen * chosen * (1.0 - chosen)
        flat_in = hidden_in.reshape(token_count, model_width)
        router_parts[level_index] = jnp.dot(
            grad_logit.reshape(token_count), flat_in, precision=highest_precision
        )
        grad_hidden = gradient + grad_logit[..., None] * router_float[:, level_index]
        grad_ffn_low = d_branch.reshape(token_count, model_width).astype(jnp.bfloat16)
        grad_inner = across(grad_ffn_low, w_down)
        gate_pre = pieces["gate_pre"]
        activated = pieces["activated"]
        grad_gate_low = (
            grad_inner * pieces["up_pre"] * activated * (1.0 + gate_pre * (1.0 - activated))
        ).astype(jnp.bfloat16)
        grad_up_low = (grad_inner * gate_pre * activated).astype(jnp.bfloat16)
        grad_normed_ffn = (across(grad_gate_low, w_gate) + across(grad_up_low, w_up)).reshape(
            count_of_rows, piece_length, model_width
        )
        grad_middle, gain_part = norm_back(
            grad_normed_ffn, pieces["middle"], pieces["scale_ffn"], gain_ffn
        )
        acc_norm_ffn = acc_norm_ffn + gain_part
        grad_hidden = grad_hidden + grad_middle
        grad_attn_low = (
            (d_branch + grad_middle).reshape(token_count, model_width).astype(jnp.bfloat16)
        )
        grad_attended = (
            across(grad_attn_low, w_out)
            .astype(jnp.bfloat16)
            .reshape(
                count_of_rows, piece_length, KEY_VALUE_HEADS, query_group_width, HEAD_DIMENSION
            )
        )
        carried = jnp.transpose(
            jnp.sum(grad_attended.astype(jnp.float32) * pieces["attended"], axis=-1), (0, 2, 3, 1)
        )
        grouped_queries = pieces["grouped"]
        heads_of_keys = pieces["key_heads"]
        heads_of_values = pieces["value_heads"]
        allowed = pieces["allowed"]
        log_total = pieces["log_total"]
        grad_queries, grad_keys, grad_values = lax.map(
            attend_back,
            (
                grouped_queries,
                heads_of_keys,
                heads_of_values,
                allowed,
                log_total,
                grad_attended,
                carried,
            ),
        )
        summed_keys, value_sum = (
            lax.psum_scatter(
                grad_keys.reshape(count_of_rows, complete_length, width_of_keys).astype(
                    jnp.bfloat16
                ),
                "blk",
                scatter_dimension=1,
                tiled=True,
            ).astype(jnp.float32),
            lax.psum_scatter(
                grad_values.reshape(count_of_rows, complete_length, width_of_keys).astype(
                    jnp.bfloat16
                ),
                "blk",
                scatter_dimension=1,
                tiled=True,
            ).astype(jnp.float32),
        )
        grad_query_low = (
            inverse_rotation(
                grad_queries.reshape(count_of_rows, piece_length, QUERY_HEADS, HEAD_DIMENSION),
                cosine_table,
                sine_values,
            )
            .astype(jnp.bfloat16)
            .reshape(token_count, QUERY_HEADS * HEAD_DIMENSION)
        )
        grad_key_low = (
            inverse_rotation(
                summed_keys.reshape(count_of_rows, piece_length, KEY_VALUE_HEADS, HEAD_DIMENSION),
                cosine_table,
                sine_values,
            )
            .astype(jnp.bfloat16)
            .reshape(token_count, width_of_keys)
        )
        grad_value_low = value_sum.astype(jnp.bfloat16).reshape(token_count, width_of_keys)
        flat_normed = pieces["flat_normed"]
        sides.append(
            (
                pieces["inner_low"],
                grad_ffn_low,
                pieces["normed_ffn"],
                grad_gate_low,
                grad_up_low,
                flat_normed,
                pieces["attended_low"],
                grad_key_low,
                grad_value_low,
                grad_query_low,
                grad_attn_low,
            )
        )
        grad_normed = (
            across(grad_query_low, w_query)
            + across(grad_key_low, key_weight)
            + across(grad_value_low, value_weight)
        )
        grad_input, gain_part = norm_back(
            grad_normed.reshape(count_of_rows, piece_length, model_width),
            hidden_in,
            pieces["scale_attn"],
            gain_attn,
        )
        acc_norm_attn = acc_norm_attn + gain_part
        gradient = grad_hidden + grad_input
    small = jnp.stack([acc_norm_attn, acc_norm_ffn] + router_parts)
    shares = reduced_weight_grads(
        tuple(jnp.concatenate(pair, axis=0) for pair in zip(*sides)), small, mesh_sizes
    )
    return (
        hidden,
        gradient,
        shares[0],
        shares[1],
        shares[2],
        shares[3],
        shares[4],
        shares[5],
        shares[6],
        shares[7],
        shares[8],
        shares[9],
    )


def solution(mesh):
    sizes = (mesh.shape["blk"], mesh.shape["dp"])
    return jax.shard_map(
        functools.partial(local, mesh_sizes=sizes),
        mesh=mesh,
        in_specs=(
            P("dp", "blk", None),
            P("dp", "blk"),
            P("dp", "blk"),
            P(),
            P(),
            P(),
            P(),
            P(),
            P(),
            P(),
            P(),
            P(),
            P(),
            P("dp", "blk", None),
        ),
        out_specs=(
            P("dp", "blk", None),
            P("dp", "blk", None),
            P("blk"),
            P("blk"),
            P("blk", None),
            P("blk", None),
            P("blk", None),
            P("blk", None),
            P("blk", None),
            P("blk", None),
            P("blk", None),
            P("blk", None),
        ),
        check_vma=False,
    )
```

```python
import functools
import itertools
import math

import jax
import jax.numpy as jnp
from jax import lax
from jax.experimental import pallas as pl
from jax.experimental.pallas import tpu as pltpu
from jax.sharding import PartitionSpec as P

QUERY_HEADS = 15
KEY_VALUE_HEADS = 5
HEAD_DIMENSION = 64
RECUR = 2


epsilon = 1e-05
highest_precision = lax.Precision.HIGHEST
masked_score = -1e30


def frequencies(head_size):
    return jnp.exp(
        jnp.arange(head_size // 2, dtype=jnp.float32) * (-2.0 * math.log(10000.0) / head_size)
    )


def rms_scale(values):
    return lax.rsqrt(jnp.mean(values * values, axis=-1, keepdims=True) + epsilon)


def norm_back(grad_norm, values, inverse_rms, gain_vec):
    weighted = grad_norm * gain_vec
    grad_values = inverse_rms * weighted - values * (
        inverse_rms * inverse_rms * inverse_rms
    ) * jnp.mean(weighted * values, axis=-1, keepdims=True)
    grad_gain = jnp.sum((grad_norm * values * inverse_rms).reshape(-1, values.shape[-1]), axis=0)
    return (grad_values, grad_gain)


def rotate(values, cosine_table, sine_values):
    half_width = values.shape[-1] // 2
    first_half = values[..., :half_width]
    second = values[..., half_width:]
    return jnp.concatenate(
        [
            first_half * cosine_table - second * sine_values,
            second * cosine_table + first_half * sine_values,
        ],
        axis=-1,
    )


def inverse_rotation(grads, cosine_table, sine_values):
    half_width = grads.shape[-1] // 2
    first_half = grads[..., :half_width]
    second = grads[..., half_width:]
    return jnp.concatenate(
        [
            first_half * cosine_table + second * sine_values,
            second * cosine_table - first_half * sine_values,
        ],
        axis=-1,
    )


HEAD_SHARE = QUERY_HEADS // KEY_VALUE_HEADS
FF_TILE = 512


def dot_last(left, right):
    return lax.dot_general(left, right, (((1,), (1,)), ((), ())), preferred_element_type=jnp.float32)


def plain_dot(left, right):
    return jnp.dot(left, right, preferred_element_type=jnp.float32)


def turned_dot(left, right):
    return lax.dot_general(left, right, (((0,), (0,)), ((), ())), preferred_element_type=jnp.float32)


def remote(source, target, sems, at, device):
    return pltpu.make_async_remote_copy(
        src_ref=source,
        dst_ref=target,
        send_sem=sems[0].at[at],
        recv_sem=sems[1].at[at],
        device_id=device,
        device_id_type=pl.DeviceIdType.MESH,
    )


def greet(partners):
    barrier = pltpu.get_barrier_semaphore()
    for partner in partners:
        pl.semaphore_signal(barrier, inc=1, device_id=partner, device_id_type=pl.DeviceIdType.MESH)
    pl.semaphore_wait(barrier, len(partners))


def turn_heads(turned, cosine, sine, heads):
    split = turned.reshape(heads, 2, HEAD_DIMENSION // 2, turned.shape[1])
    first, second = split[:, 0], split[:, 1]
    both = jnp.stack([first * cosine - second * sine, second * cosine + first * sine], axis=1)
    return both.reshape(turned.shape)


def turn_back(turned, cosine, sine, heads):
    return turn_heads(turned, cosine, -sine, heads)


def block_bits(block, m):
    return tuple(lax.rem(block // (1 << bit), 2) for bit in range(m - 1, -1, -1))


def fill_bias(bias, metas, own_meta, level, blk, m, piece):
    query_segments = own_meta[0:1, :]
    key_at = lax.broadcasted_iota(jnp.int32, (piece, piece), 0)
    query_at = lax.broadcasted_iota(jnp.int32, (piece, piece), 1)

    @pl.loop(0, blk + 1)
    def _(block):
        columns = metas[block_bits(block, m)].T
        live = jnp.where(columns[:, 1:2] > level.astype(jnp.float32), columns[:, 0:1], -1.0)
        shift = (blk - block) * piece
        allowed = (live == query_segments) & (key_at <= query_at + shift) | (key_at == query_at + shift)
        bias[block] = jnp.where(allowed, 0.0, masked_score)


def forward_kernel(
    sizes,
    tokens, meta, tables, gains,
    w_query_hbm, key_weight_hbm, value_weight_hbm, w_out_hbm, w_gate_hbm, w_up_hbm, w_down_hbm,
    hidden_out, hid_out, normed_out, turned_out, kv_out, lse_out, att_out, middle_out, nffn_out, gate_out, up_out,
    inner_out, branch_out, metas_out,
    w_query, key_weight, value_weight, w_out, w_gate, w_up, w_down,
    hid, normed, turned, kv, lse, att, middle, nffn, gate, up, inner, branch, metas,
    bias, query_pad, top, total, att_turned,
    load_sems, save_sems, kv_send, kv_recv, meta_send, meta_recv,
):
    m, piece = sizes
    blk = lax.axis_index("blk")
    mine = block_bits(blk, m)
    weights = (
        (key_weight_hbm, key_weight), (value_weight_hbm, value_weight), (w_query_hbm, w_query), (w_out_hbm, w_out),
        (w_gate_hbm, w_gate), (w_up_hbm, w_up), (w_down_hbm, w_down),
    )
    loads = [pltpu.make_async_copy(*pair, load_sems.at[at]) for at, pair in enumerate(weights)]
    for load in loads:
        load.start()
    saved = (
        (normed, normed_out), (turned, turned_out), (kv, kv_out), (lse, lse_out), (att, att_out),
        (middle, middle_out), (nffn, nffn_out), (gate, gate_out), (up, up_out), (inner, inner_out),
        (branch, branch_out),
    )

    def save(at, level):
        return pltpu.make_async_copy(saved[at][0].at[level], saved[at][1].at[level], save_sems.at[at, level])

    metas[mine] = meta[...]
    greet([{"blk": flipped(blk, bit)} for bit in range(m)])

    def place(known):
        return tuple(slice(None) if bit in known else mine[m - 1 - bit] for bit in range(m - 1, -1, -1))

    orders = (list(range(1, m)), list(range(m - 1, 0, -1)))

    def kv_copies(level, group, stage):
        if stage == m - 1:
            ref = kv.at[(level, group, *place(range(1, m)))]
            return [remote(ref, ref, (kv_send, kv_recv), (level, group, 2 * stage), {"blk": flipped(blk, 0)})]
        copies = []
        for side, order in enumerate(orders):
            rows = pl.ds(side * (piece // 2), piece // 2)
            ref = kv.at[(level, group, *place(order[:stage]), rows)]
            copies.append(remote(ref, ref, (kv_send, kv_recv), (level, group, 2 * stage + side),
                                 {"blk": flipped(blk, order[stage])}))
        return copies

    def kv_advance(level, group, stage):
        if stage > 0:
            for copy in kv_copies(level, group, stage - 1):
                copy.wait_recv()
        if stage < m:
            for copy in kv_copies(level, group, stage):
                copy.start()

    def meta_copy(stage):
        bits = list(range(1, m)) + [0]
        ref = metas.at[place(bits[:stage])]
        return remote(ref, ref, (meta_send, meta_recv), stage, {"blk": flipped(blk, bits[stage])})

    meta_copy(0).start()
    cosine, sine = tables[:HEAD_DIMENSION // 2, :], tables[HEAD_DIMENSION // 2:, :]
    hid[0] = tokens[...].astype(jnp.float32)
    query_pad[HEAD_DIMENSION:, :] = jnp.zeros_like(query_pad[HEAD_DIMENSION:, :])

    @pl.loop(0, RECUR)
    def _(level):
        hidden = hid[level]
        normed[level] = (hidden * rms_scale(hidden) * gains[0:1, :]).astype(jnp.bfloat16)

        @pl.when(level == 0)
        def _():
            for load in loads[:2]:
                load.wait()

        flat = normed[level]
        keys = turn_heads(plain_dot(flat, key_weight[...]).T, cosine, sine, KEY_VALUE_HEADS)
        values = plain_dot(flat, value_weight[...]).T
        for group in range(KEY_VALUE_HEADS):
            here = slice(group * HEAD_DIMENSION, (group + 1) * HEAD_DIMENSION)
            both = jnp.concatenate([keys[here], values[here]], axis=0)
            kv[(level, group, *mine)] = both.T.astype(jnp.bfloat16)
            kv_advance(level, group, 0)

        @pl.when(level == 0)
        def _():
            loads[2].wait()
            for stage in range(1, m - 1):
                meta_copy(stage - 1).wait_recv()
                meta_copy(stage).start()

        queries = turn_heads(plain_dot(flat, w_query[...]).T, cosine, sine, QUERY_HEADS)
        turned[level] = (queries * HEAD_DIMENSION ** (-0.5)).astype(jnp.bfloat16)

        @pl.when(level == 0)
        def _():
            for stage in range(max(1, m - 1), m):
                meta_copy(stage - 1).wait_recv()
                meta_copy(stage).start()

        for stage in range(1, m):
            for group in range(m - stage):
                kv_advance(level, group, stage)

        @pl.when(level == 0)
        def _():
            meta_copy(m - 1).wait_recv()

        fill_bias(bias, metas, meta, level, blk, m, piece)

        @pl.loop(0, KEY_VALUE_HEADS)
        def _(group):
            for stage in range(1, m):
                @pl.when(group + m - stage < KEY_VALUE_HEADS)
                def _():
                    kv_advance(level, group + m - stage, stage)

            kv_advance(level, group, m)
            for member in range(HEAD_SHARE):
                head = group * HEAD_SHARE + member
                rows = pl.ds(pl.multiple_of(head * HEAD_DIMENSION, HEAD_DIMENSION), HEAD_DIMENSION)
                query_pad[:HEAD_DIMENSION, member * piece:(member + 1) * piece] = turned[level, rows, :]
            top[...] = jnp.full_like(top, masked_score)
            total[...] = jnp.zeros_like(total)

            @pl.loop(0, blk + 1)
            def _(step):
                block = blk - step
                rows = kv[(level, group, *block_bits(block, m))]
                here = bias[block]
                scores = plain_dot(rows, query_pad[...]) + jnp.concatenate([here] * HEAD_SHARE, axis=1)
                before = top[0:1, :]
                after = jnp.maximum(before, jnp.max(scores, axis=0, keepdims=True))
                raised = jnp.exp(scores - after)
                shrink = jnp.exp(before - after)
                top[0:1, :] = after
                ones = jnp.ones((16, piece), jnp.bfloat16)
                left = jnp.concatenate([rows.T[HEAD_DIMENSION:], ones], axis=0)
                total[...] = total[...] * shrink + plain_dot(left, raised.astype(jnp.bfloat16))

            sums = total[HEAD_DIMENSION:HEAD_DIMENSION + 1, :]
            lse[level, pl.ds(group, 1), :] = top[0:1, :] + jnp.log(sums)
            out = total[:HEAD_DIMENSION, :] / sums
            for member in range(HEAD_SHARE):
                head = group * HEAD_SHARE + member
                rows = pl.ds(pl.multiple_of(head * HEAD_DIMENSION, HEAD_DIMENSION), HEAD_DIMENSION)
                att_turned[rows, :] = out[:, member * piece:(member + 1) * piece]

        for at in range(4):
            save(at, level).start()
        att[level] = att_turned[...].T.astype(jnp.bfloat16)
        save(4, level).start()

        @pl.when(level == 0)
        def _():
            loads[3].wait()

        attn = plain_dot(att[level], w_out[...])
        mid = hid[level] + attn
        middle[level] = mid
        branch[level] = attn
        save(5, level).start()
        nffn[level] = (mid * rms_scale(mid) * gains[1:2, :]).astype(jnp.bfloat16)
        save(6, level).start()

        @pl.when(level == 0)
        def _():
            loads[4].wait()
            loads[5].wait()

        @pl.loop(0, w_gate.shape[1] // FF_TILE)
        def _(tile):
            columns = pl.ds(pl.multiple_of(tile * FF_TILE, FF_TILE), FF_TILE)
            gate_pre = plain_dot(nffn[level], w_gate[:, columns])
            up_pre = plain_dot(nffn[level], w_up[:, columns])
            gate[level, :, columns] = gate_pre.astype(jnp.bfloat16)
            up[level, :, columns] = up_pre.astype(jnp.bfloat16)
            inner[level, :, columns] = (gate_pre * jax.nn.sigmoid(gate_pre) * up_pre).astype(jnp.bfloat16)

        for at in range(7, 10):
            save(at, level).start()

        @pl.when(level == 0)
        def _():
            loads[6].wait()

        branch[level] += plain_dot(inner[level], w_down[...])
        save(10, level).start()
        logit = jnp.sum(hid[level] * gains[pl.ds(2 + level, 1), :], axis=1, keepdims=True)
        weight = jnp.where(meta[...].T[:, 1:2] > level.astype(jnp.float32), jax.nn.sigmoid(logit), 0.0)
        hid[level + 1] = hid[level] + weight * branch[level]

    hidden_out[...] = hid[RECUR]
    last = [
        pltpu.make_async_copy(hid.at[pl.ds(0, RECUR)], hid_out, save_sems.at[len(saved), 0]),
        pltpu.make_async_copy(metas, metas_out, save_sems.at[len(saved), 1]),
    ]
    for copy in last:
        copy.start()
    for stage in range(m):
        meta_copy(stage).wait_send()
    for level in range(RECUR):
        for group in range(KEY_VALUE_HEADS):
            for stage in range(m):
                for copy in kv_copies(level, group, stage):
                    copy.wait_send()
        for at in range(len(saved)):
            save(at, level).wait()
    for copy in last:
        copy.wait()


def forward(tokens, meta, tables, gains, weights, nb):
    m = nb.bit_length() - 1
    piece, width = tokens.shape
    hidden_units = weights[4].shape[1]
    blocks = (2,) * m
    saved = {
        "hid": ((RECUR, piece, width), jnp.float32),
        "normed": ((RECUR, piece, width), jnp.bfloat16),
        "turned": ((RECUR, width, piece), jnp.bfloat16),
        "kv": ((RECUR, KEY_VALUE_HEADS, *blocks, piece, 2 * HEAD_DIMENSION), jnp.bfloat16),
        "lse": ((RECUR, 8, HEAD_SHARE * piece), jnp.float32),
        "att": ((RECUR, piece, width), jnp.bfloat16),
        "middle": ((RECUR, piece, width), jnp.float32),
        "nffn": ((RECUR, piece, width), jnp.bfloat16),
        "gate": ((RECUR, piece, hidden_units), jnp.bfloat16),
        "up": ((RECUR, piece, hidden_units), jnp.bfloat16),
        "inner": ((RECUR, piece, hidden_units), jnp.bfloat16),
        "branch": ((RECUR, piece, width), jnp.float32),
        "metas": ((*blocks, 8, piece), jnp.float32),
    }
    shapes = [jax.ShapeDtypeStruct(*entry) for entry in saved.values()]
    w_query, key_weight, value_weight, w_out, w_gate, w_up, w_down = weights
    vmem, anywhere = pl.BlockSpec(memory_space=pltpu.VMEM), pl.BlockSpec(memory_space=pl.ANY)
    scratch = [pltpu.VMEM(array.shape, array.dtype) for array in weights]
    scratch += [pltpu.VMEM((RECUR + 1, piece, width), jnp.float32)]
    scratch += [pltpu.VMEM(*entry) for entry in list(saved.values())[1:]]
    scratch += [
        pltpu.VMEM((nb, piece, piece), jnp.float32),
        pltpu.VMEM((2 * HEAD_DIMENSION, HEAD_SHARE * piece), jnp.bfloat16),
        pltpu.VMEM((8, HEAD_SHARE * piece), jnp.float32),
        pltpu.VMEM((HEAD_DIMENSION + 16, HEAD_SHARE * piece), jnp.float32),
        pltpu.VMEM((width, piece), jnp.float32),
        pltpu.SemaphoreType.DMA((7,)),
        pltpu.SemaphoreType.DMA((len(saved) - 1, RECUR)),
        pltpu.SemaphoreType.DMA((RECUR, KEY_VALUE_HEADS, 2 * m)),
        pltpu.SemaphoreType.DMA((RECUR, KEY_VALUE_HEADS, 2 * m)),
        pltpu.SemaphoreType.DMA((m,)),
        pltpu.SemaphoreType.DMA((m,)),
    ]
    outs = pl.pallas_call(
        functools.partial(forward_kernel, (m, piece)),
        out_shape=[jax.ShapeDtypeStruct((piece, width), jnp.float32)] + shapes,
        in_specs=[vmem] * 4 + [anywhere] * 7,
        out_specs=[vmem] + [anywhere] * len(shapes),
        scratch_shapes=scratch,
        compiler_params=pltpu.CompilerParams(
            collective_id=1, has_side_effects=True, vmem_limit_bytes=62 * 1024 * 1024
        ),
        cost_estimate=pl.CostEstimate(
            flops=2 * RECUR * piece * width * 10240, bytes_accessed=48 * 1024 * 1024, transcendentals=0
        ),
        name="forward_levels",
    )(tokens, meta, tables, gains, *weights)
    return outs[0], dict(zip(saved, outs[1:]))


UNIT_COLUMNS = 256


def bits_of(number, count):
    return tuple((number >> (count - 1 - at)) & 1 for at in range(count))


def bit_of(position, bit):
    return lax.rem(position // (1 << bit), 2)


def flipped(position, bit):
    return position + (1 << bit) * (1 - 2 * bit_of(position, bit))


class Piece:
    def __init__(self, at, kept_at, slot, flavour, family, sems, bits):
        self.at, self.kept_at, self.slot, self.family, self.sems = at, kept_at, slot, family, sems
        self.m, self.n = bits
        left = list(range(self.m - 1, -1, -1))
        self.order = []
        for stage in range(self.m):
            place = len(left) - 1 if stage == 0 or flavour == 0 else 0
            self.order.append((left.pop(place), place, len(left)))
        self.last = self.m + self.n
        self.copies = []
        self.blk, self.dp = lax.axis_index("blk"), lax.axis_index("dp")

    def half(self, ref, side):
        rows, columns = self.family["shape"]
        if self.family["split"] == 0:
            return ref.at[pl.ds(pl.multiple_of(side * (rows // 2), rows // 2), rows // 2), :]
        return ref.at[:, pl.ds(pl.multiple_of(side * (columns // 2), columns // 2), columns // 2)]

    def held(self, stage):
        if stage == 0:
            return self.family["part"], self.slot
        return self.family["blk"][stage - 1], self.kept_at

    def start(self, stage):
        m, family = self.m, self.family
        if stage < m:
            bit, place, others = self.order[stage]
            ref, index = self.held(stage)
            chosen = [slice(None)] * (others + 1)
            chosen[place] = 1 - bit_of(self.blk, bit)
            source = ref.at[(index, *chosen)]
            target = family["blk"][stage].at[self.kept_at]
            device = {"blk": flipped(self.blk, bit)}
        elif stage < self.last:
            bit = stage - m
            if bit == 0:
                source = self.half(family["blk"][m - 1].at[self.kept_at], 1 - bit_of(self.dp, 0))
            else:
                source = family["dp"][bit - 1].at[self.kept_at]
            target = family["dp"][bit].at[self.kept_at]
            device = {"dp": flipped(self.dp, bit)}
        else:
            source = self.half(family["out"].at[self.kept_at], bit_of(self.dp, 0))
            target = source
            device = {"dp": flipped(self.dp, 0)}
        copy = pltpu.make_async_remote_copy(
            src_ref=source,
            dst_ref=target,
            send_sem=self.sems[0].at[self.at, stage],
            recv_sem=self.sems[1].at[self.at, stage],
            device_id=device,
            device_id_type=pl.DeviceIdType.MESH,
        )
        copy.start()
        self.copies.append(copy)

    def finish(self, stage):
        m, family = self.m, self.family
        self.copies[stage].wait_recv()
        if stage < m:
            bit, place, others = self.order[stage]
            ref, index = self.held(stage)
            for combo in itertools.product(range(2), repeat=others):
                chosen = list(combo)
                chosen.insert(place, bit_of(self.blk, bit))
                into = family["blk"][stage].at[(self.kept_at, *combo)]
                self.add(into, into, ref.at[(index, *chosen)])
            if stage == 0:
                self.copies[0].wait_send()
        elif stage < self.last:
            bit = stage - m
            got = family["dp"][bit].at[self.kept_at]
            if bit == 0:
                own = self.half(family["blk"][m - 1].at[self.kept_at], bit_of(self.dp, 0))
            else:
                own = family["dp"][bit - 1].at[self.kept_at]
            into = got
            if stage == self.last - 1:
                into = self.half(family["out"].at[self.kept_at], bit_of(self.dp, 0))
            self.add(into, got, own)

    def add(self, into, left, right):
        into[...] = left[...] + right[...]

    def drained(self):
        for copy in self.copies[1:]:
            copy.wait_send()


def reduce_kernel(
    sizes,
    inner_hbm, dffn_hbm, nffn_hbm, dgate_hbm, dup_hbm, normed_hbm, attended_hbm, near_hbm, far_hbm, small_hbm,
    out_wide, out_down, out_small,
    inner, dffn, nffn, dgate, dup, normed, attended, near, far,
    nffn_turned, normed_turned, attended_turned,
    part_wide, part_down, part_small,
    *others,
):
    nb, nd, m, n, padded = sizes
    blk_wide, others = others[:m], others[m:]
    blk_down, others = others[:m], others[m:]
    blk_small, others = others[:m], others[m:]
    dp_wide, others = others[:n], others[n:]
    dp_down, others = others[:n], others[n:]
    dp_small, others = others[:n], others[n:]
    load_sems, send_sems, recv_sems = others
    blk, dp = lax.axis_index("blk"), lax.axis_index("dp")

    sources = (inner_hbm, dffn_hbm, nffn_hbm, dgate_hbm, dup_hbm, normed_hbm, attended_hbm, near_hbm, far_hbm, small_hbm)
    places = (inner, dffn, nffn, dgate, dup, normed, attended, near, far, part_small.at[0])
    loads = [
        pltpu.make_async_copy(source, place, load_sems.at[at])
        for at, (source, place) in enumerate(zip(sources, places))
    ]
    for load in loads:
        load.start()

    barrier = pltpu.get_barrier_semaphore()
    partners = [{"blk": flipped(blk, bit)} for bit in range(m)] + [{"dp": flipped(dp, bit)} for bit in range(n)]
    for partner in partners:
        pl.semaphore_signal(barrier, inc=1, device_id=partner, device_id_type=pl.DeviceIdType.MESH)
    pl.semaphore_wait(barrier, len(partners))

    down_rows = part_down.shape[-2]
    wide = {"part": part_wide, "blk": blk_wide, "dp": dp_wide, "out": out_wide,
            "shape": (2 * padded, UNIT_COLUMNS), "split": 1}
    down = {"part": part_down, "blk": blk_down, "dp": dp_down, "out": out_down,
            "shape": (down_rows, dffn.shape[1]), "split": 0}
    small = {"part": part_small, "blk": blk_small, "dp": dp_small, "out": out_small,
             "shape": (16, 128), "split": 0}
    slots = part_wide.shape[0]
    sems = (send_sems, recv_sems)
    pieces = []
    for at in range(5):
        pieces.append(Piece(len(pieces), at, at, len(pieces) % 2, down, sems, (m, n)))
    for at in range(15):
        pieces.append(Piece(len(pieces), at, at % slots, len(pieces) % 2, wide, sems, (m, n)))
    pieces.append(Piece(len(pieces), 0, 0, 0, small, sems, (m, n)))

    def compute_down():
        loads[0].wait()
        loads[1].wait()
        width = 640
        group = width // (5 * down_rows)
        for at in range(inner.shape[1] // width):
            result = turned_dot(inner[:, at * width:(at + 1) * width], dffn[...])
            for member in range(group):
                target = bits_of(at * group + member, m)
                for unit in range(5):
                    first = (member * 5 + unit) * down_rows
                    part_down[(unit, *target)] = result[first:first + down_rows].astype(jnp.bfloat16)

    def compute_wide(at):
        slot = at % slots
        if at == 0:
            loads[2].wait()
            nffn_turned[...] = nffn[...].T
            loads[3].wait()
        if at == 5:
            loads[4].wait()
        if at == 10:
            for load in loads[5:9]:
                load.wait()
            normed_turned[...] = normed[...].T
            attended_turned[...] = attended[...].T
        block, at_column = at // 5, (at % 5) * UNIT_COLUMNS
        if block < 2:
            right = dgate if block == 0 else dup
            upper = plain_dot(nffn_turned[...], right[:, at_column:at_column + UNIT_COLUMNS])
            second = 1280 + at_column
            lower = plain_dot(nffn_turned[...], right[:, second:second + UNIT_COLUMNS])
        else:
            upper = plain_dot(normed_turned[...], near[:, at_column:at_column + UNIT_COLUMNS])
            second = 1280 + at_column
            lower = None
            if second < 1600:
                lower = plain_dot(normed_turned[...], near[:, second:second + UNIT_COLUMNS])
            if second >= 1536:
                more = plain_dot(attended_turned[...], far[:, second - 1536:second - 1536 + UNIT_COLUMNS])
                lower = more if lower is None else lower + more
        for target in range(nb):
            here = slice(target * padded, (target + 1) * padded)
            both = jnp.concatenate([upper[here], lower[here]], axis=0)
            part_wide[(slot, *bits_of(target, m))] = both.astype(jnp.bfloat16)

    def compute(piece):
        if piece.family is wide:
            compute_wide(piece.kept_at)
        elif piece.family is small:
            loads[9].wait()
        piece.start(0)

    groups = [pieces[at:at + 2] for at in range(0, 18, 2)] + [pieces[18:]]
    compute_down()
    for piece in groups[0] + groups[1]:
        compute(piece)

    def move(group, stage):
        for piece in group:
            piece.finish(stage)
            piece.start(stage + 1)

    count = len(groups)
    for tick in range(count + m + n - 1):
        for stage in range(m + n - 1, -1, -1):
            if 0 <= tick - stage < count:
                move(groups[tick - stage], stage)
        if tick + 2 < count:
            for piece in groups[tick + 2]:
                compute(piece)
    for piece in pieces:
        piece.finish(m + n)
    for piece in pieces:
        piece.drained()


def reduced_weight_grads(sides, small, mesh_sizes):
    nb, nd = mesh_sizes
    m, n = nb.bit_length() - 1, nd.bit_length() - 1
    inner, dffn, nffn, dgate, dup, normed, attended, dkey, dvalue, dquery, dattn = sides
    tokens, width = normed.shape
    rows = width // nb
    padded = -(-rows // 8) * 8
    down_rows = inner.shape[1] // nb // 5

    def spread(array):
        if padded == rows:
            return array
        split = array.reshape(tokens, nb, rows)
        return jnp.pad(split, ((0, 0), (0, 0), (0, padded - rows))).reshape(tokens, nb * padded)

    near_width = dkey.shape[1] + dvalue.shape[1] + dquery.shape[1]
    near = jnp.concatenate([dkey, dvalue, dquery, jnp.zeros((tokens, 1792 - near_width), jnp.bfloat16)], axis=1)
    far = jnp.concatenate([jnp.zeros((tokens, near_width - 1536), jnp.bfloat16), dattn], axis=1)
    small_parts = jnp.pad(small.reshape(4, nb, rows).transpose(1, 0, 2), ((0, 0), (0, 12), (0, 128 - rows)))
    operands = (inner, dffn, spread(nffn), dgate, dup, spread(normed), spread(attended), near, far,
                small_parts.reshape((2,) * m + (16, 128)))
    wide_shape, down_shape = (2 * padded, UNIT_COLUMNS), (down_rows, dffn.shape[1])
    scratch = [pltpu.VMEM(array.shape, array.dtype) for array in operands[:9]]
    scratch += [pltpu.VMEM((nb * padded, tokens), jnp.bfloat16)] * 3
    families = ((15, wide_shape, jnp.bfloat16, 6, 1), (5, down_shape, jnp.bfloat16, 5, 0), (1, (16, 128), jnp.float32, 1, 0))
    for count, shape, dtype, slots, _ in families:
        scratch.append(pltpu.VMEM((slots, *(2,) * m, *shape), dtype))
    for count, shape, dtype, _, _ in families:
        for stage in range(m):
            scratch.append(pltpu.VMEM((count, *(2,) * (m - 1 - stage), *shape), dtype))
    for count, shape, dtype, _, split in families:
        half = (shape[0], shape[1] // 2) if split else (shape[0] // 2, shape[1])
        scratch += [pltpu.VMEM((count, *half), dtype)] * n
    scratch += [pltpu.SemaphoreType.DMA((10,)), pltpu.SemaphoreType.DMA((21, m + n + 1)), pltpu.SemaphoreType.DMA((21, m + n + 1))]
    wide, down, little = pl.pallas_call(
        functools.partial(reduce_kernel, (nb, nd, m, n, padded)),
        out_shape=(
            jax.ShapeDtypeStruct((15, *wide_shape), jnp.bfloat16),
            jax.ShapeDtypeStruct((5, *down_shape), jnp.bfloat16),
            jax.ShapeDtypeStruct((1, 16, 128), jnp.float32),
        ),
        in_specs=[pl.BlockSpec(memory_space=pl.ANY)] * 10,
        out_specs=[pl.BlockSpec(memory_space=pltpu.VMEM)] * 3,
        scratch_shapes=scratch,
        compiler_params=pltpu.CompilerParams(
            collective_id=0, has_side_effects=True, vmem_limit_bytes=60 * 1024 * 1024
        ),
        cost_estimate=pl.CostEstimate(
            flops=2 * tokens * width * 10240, bytes_accessed=20 * 1024 * 1024, transcendentals=0
        ),
        name="weight_grads",
    )(*operands)

    def columns(first):
        five = wide[first:first + 5].reshape(5, 2, padded, UNIT_COLUMNS)
        return five.transpose(2, 1, 0, 3).reshape(padded, 2560)[:rows].astype(jnp.float32)

    gate, up, rest = columns(0), columns(5), columns(10)
    return (
        little[0, 0, :rows],
        little[0, 1, :rows],
        rest[:, 640:1600],
        rest[:, :320],
        rest[:, 320:640],
        rest[:, 1600:],
        gate,
        up,
        down.reshape(5 * down_rows, dffn.shape[1]).astype(jnp.float32),
        little[0, 2:4, :rows].T,
    )


def across(grad_rows, matrix):
    return lax.dot_general(
        grad_rows, matrix, (((1,), (1,)), ((), ())), preferred_element_type=jnp.float32
    )


def allowed_pairs(
    query_segments, key_segments, key_depths, query_positions, key_positions, level_index
):
    same_doc = query_segments[:, None] == key_segments[None, :]
    causal = key_positions[None, :] <= query_positions[:, None]
    live_keys = (key_depths[None, :] > level_index) | (
        key_positions[None, :] == query_positions[:, None]
    )
    return same_doc & causal & live_keys


def score_block(query_rows, key_rows, allowed):
    scores = jnp.einsum(
        "qkgd,jkd->kgqj", query_rows, key_rows, preferred_element_type=jnp.float32
    ) * HEAD_DIMENSION ** (-0.5)
    return jnp.where(allowed[None, None], scores, masked_score)


def attend_back(operands):
    query_rows, key_rows, rows_of_values, allowed, log_total, grad_attended, carried = operands
    scores = score_block(query_rows, key_rows, allowed)
    probability = jnp.exp(scores - log_total[..., None])
    grad_prob = jnp.einsum(
        "qkgd,jkd->kgqj", grad_attended, rows_of_values, preferred_element_type=jnp.float32
    )
    grad_scores = (probability * (grad_prob - carried[..., None])).astype(jnp.bfloat16)
    grad_queries = jnp.einsum(
        "kgqj,jkd->qkgd", grad_scores, key_rows, preferred_element_type=jnp.float32
    ) * HEAD_DIMENSION ** (-0.5)
    grad_keys = jnp.einsum(
        "kgqj,qkgd->jkd", grad_scores, query_rows, preferred_element_type=jnp.float32
    ) * HEAD_DIMENSION ** (-0.5)
    grad_values = jnp.einsum(
        "kgqj,qkgd->jkd",
        probability.astype(jnp.bfloat16),
        grad_attended,
        preferred_element_type=jnp.float32,
    )
    return (grad_queries, grad_keys, grad_values)


def local(
    tokens,
    depths,
    segments,
    norm_attn,
    norm_ffn,
    w_query,
    key_weight,
    value_weight,
    w_out,
    w_gate,
    w_up,
    w_down,
    w_router,
    cotangent,
    mesh_sizes,
):
    count_of_rows, piece_length, model_width = tokens.shape
    complete_length = piece_length * lax.axis_size("blk")
    query_group_width = QUERY_HEADS // KEY_VALUE_HEADS
    token_count = count_of_rows * piece_length
    width_of_keys = KEY_VALUE_HEADS * HEAD_DIMENSION
    query_positions = lax.axis_index("blk") * piece_length + jnp.arange(
        piece_length, dtype=jnp.int32
    )
    key_positions = jnp.arange(complete_length, dtype=jnp.int32)
    angles = frequencies(HEAD_DIMENSION)[:, None] * query_positions.astype(jnp.float32)[None, :]
    tables = jnp.concatenate([jnp.cos(angles), jnp.sin(angles)], axis=0)
    cosine_table = jnp.cos(angles).T[:, None, :]
    sine_values = jnp.sin(angles).T[:, None, :]
    gain_attn = norm_attn.astype(jnp.float32)
    gain_ffn = norm_ffn.astype(jnp.float32)
    router_float = w_router.astype(jnp.float32)
    gains = jnp.pad(jnp.concatenate([jnp.stack([gain_attn, gain_ffn]), router_float.T]), ((0, 4), (0, 0)))
    meta = jnp.pad(jnp.concatenate([segments, depths]).astype(jnp.float32), ((0, 6), (0, 0)))
    weights = (w_query, key_weight, value_weight, w_out, w_gate, w_up, w_down)
    hidden, saved = forward(tokens[0], meta, tables, gains, weights, mesh_sizes[0])
    hidden = hidden[None]
    all_metas = saved["metas"].reshape(-1, 8, piece_length)
    all_segments = all_metas[:, 0].reshape(1, -1).astype(jnp.int32)
    all_depths = all_metas[:, 1].reshape(1, -1).astype(jnp.int32)

    def kept(level_index):
        hidden_in = saved["hid"][level_index][None]
        middle = saved["middle"][level_index][None]
        gate_pre = saved["gate"][level_index].astype(jnp.float32)
        chosen = jax.nn.sigmoid(jnp.sum(hidden_in * router_float[:, level_index], axis=-1))
        active = depths > level_index

        def row_mask(query_segments, key_segments, key_depths):
            return allowed_pairs(
                query_segments, key_segments, key_depths, query_positions, key_positions, level_index
            )

        both = saved["kv"][level_index].reshape(KEY_VALUE_HEADS, complete_length, 2 * HEAD_DIMENSION)
        both = both.transpose(1, 0, 2)[None]
        queries = (saved["turned"][level_index].T * 8.0).astype(jnp.bfloat16)
        attended = saved["att"][level_index]
        return {
            "scale_attn": rms_scale(hidden_in),
            "flat_normed": saved["normed"][level_index],
            "grouped": queries.reshape(1, piece_length, KEY_VALUE_HEADS, query_group_width, HEAD_DIMENSION),
            "key_heads": both[..., :HEAD_DIMENSION],
            "value_heads": both[..., HEAD_DIMENSION:],
            "allowed": jax.vmap(row_mask)(segments, all_segments, all_depths),
            "attended": attended.astype(jnp.float32).reshape(
                1, piece_length, KEY_VALUE_HEADS, query_group_width, HEAD_DIMENSION
            ),
            "log_total": saved["lse"][level_index][:KEY_VALUE_HEADS].reshape(
                1, KEY_VALUE_HEADS, query_group_width, piece_length
            ),
            "attended_low": attended,
            "middle": middle,
            "scale_ffn": rms_scale(middle),
            "normed_ffn": saved["nffn"][level_index],
            "gate_pre": gate_pre,
            "up_pre": saved["up"][level_index].astype(jnp.float32),
            "activated": jax.nn.sigmoid(gate_pre),
            "inner_low": saved["inner"][level_index],
            "chosen": chosen,
            "active": active,
            "weight": jnp.where(active, chosen, 0.0),
            "branch": saved["branch"][level_index][None],
        }

    acc_norm_attn = jnp.zeros((model_width,), jnp.float32)
    acc_norm_ffn = jnp.zeros((model_width,), jnp.float32)
    sides = []
    router_parts = [None] * RECUR
    gradient = cotangent.astype(jnp.float32)
    for level_index in reversed(range(RECUR)):
        hidden_in = saved["hid"][level_index][None]
        pieces = kept(level_index)
        chosen = pieces["chosen"]
        d_branch = pieces["weight"][..., None] * gradient
        grad_chosen = jnp.where(
            pieces["active"], jnp.sum(gradient * pieces["branch"], axis=-1), 0.0
        )
        grad_logit = grad_chosen * chosen * (1.0 - chosen)
        flat_in = hidden_in.reshape(token_count, model_width)
        router_parts[level_index] = jnp.dot(
            grad_logit.reshape(token_count), flat_in, precision=highest_precision
        )
        grad_hidden = gradient + grad_logit[..., None] * router_float[:, level_index]
        grad_ffn_low = d_branch.reshape(token_count, model_width).astype(jnp.bfloat16)
        grad_inner = across(grad_ffn_low, w_down)
        gate_pre = pieces["gate_pre"]
        activated = pieces["activated"]
        grad_gate_low = (
            grad_inner * pieces["up_pre"] * activated * (1.0 + gate_pre * (1.0 - activated))
        ).astype(jnp.bfloat16)
        grad_up_low = (grad_inner * gate_pre * activated).astype(jnp.bfloat16)
        grad_normed_ffn = (across(grad_gate_low, w_gate) + across(grad_up_low, w_up)).reshape(
            count_of_rows, piece_length, model_width
        )
        grad_middle, gain_part = norm_back(
            grad_normed_ffn, pieces["middle"], pieces["scale_ffn"], gain_ffn
        )
        acc_norm_ffn = acc_norm_ffn + gain_part
        grad_hidden = grad_hidden + grad_middle
        grad_attn_low = (
            (d_branch + grad_middle).reshape(token_count, model_width).astype(jnp.bfloat16)
        )
        grad_attended = (
            across(grad_attn_low, w_out)
            .astype(jnp.bfloat16)
            .reshape(
                count_of_rows, piece_length, KEY_VALUE_HEADS, query_group_width, HEAD_DIMENSION
            )
        )
        carried = jnp.transpose(
            jnp.sum(grad_attended.astype(jnp.float32) * pieces["attended"], axis=-1), (0, 2, 3, 1)
        )
        grouped_queries = pieces["grouped"]
        heads_of_keys = pieces["key_heads"]
        heads_of_values = pieces["value_heads"]
        allowed = pieces["allowed"]
        log_total = pieces["log_total"]
        grad_queries, grad_keys, grad_values = lax.map(
            attend_back,
            (
                grouped_queries,
                heads_of_keys,
                heads_of_values,
                allowed,
                log_total,
                grad_attended,
                carried,
            ),
        )
        summed_keys, value_sum = (
            lax.psum_scatter(
                grad_keys.reshape(count_of_rows, complete_length, width_of_keys).astype(
                    jnp.bfloat16
                ),
                "blk",
                scatter_dimension=1,
                tiled=True,
            ).astype(jnp.float32),
            lax.psum_scatter(
                grad_values.reshape(count_of_rows, complete_length, width_of_keys).astype(
                    jnp.bfloat16
                ),
                "blk",
                scatter_dimension=1,
                tiled=True,
            ).astype(jnp.float32),
        )
        grad_query_low = (
            inverse_rotation(
                grad_queries.reshape(count_of_rows, piece_length, QUERY_HEADS, HEAD_DIMENSION),
                cosine_table,
                sine_values,
            )
            .astype(jnp.bfloat16)
            .reshape(token_count, QUERY_HEADS * HEAD_DIMENSION)
        )
        grad_key_low = (
            inverse_rotation(
                summed_keys.reshape(count_of_rows, piece_length, KEY_VALUE_HEADS, HEAD_DIMENSION),
                cosine_table,
                sine_values,
            )
            .astype(jnp.bfloat16)
            .reshape(token_count, width_of_keys)
        )
        grad_value_low = value_sum.astype(jnp.bfloat16).reshape(token_count, width_of_keys)
        flat_normed = pieces["flat_normed"]
        sides.insert(0, (grad_ffn_low, grad_gate_low, grad_up_low, grad_key_low, grad_value_low, grad_query_low, grad_attn_low))
        grad_normed = (
            across(grad_query_low, w_query)
            + across(grad_key_low, key_weight)
            + across(grad_value_low, value_weight)
        )
        grad_input, gain_part = norm_back(
            grad_normed.reshape(count_of_rows, piece_length, model_width),
            hidden_in,
            pieces["scale_attn"],
            gain_attn,
        )
        acc_norm_attn = acc_norm_attn + gain_part
        gradient = grad_hidden + grad_input
    small = jnp.stack([acc_norm_attn, acc_norm_ffn] + router_parts)
    dffn, dgate, dup, dkey, dvalue, dquery, dattn = (jnp.concatenate(pair, axis=0) for pair in zip(*sides))
    inner, nffn, normed, attended = (
        saved[name].reshape(RECUR * token_count, -1) for name in ("inner", "nffn", "normed", "att")
    )
    shares = reduced_weight_grads(
        (inner, dffn, nffn, dgate, dup, normed, attended, dkey, dvalue, dquery, dattn), small, mesh_sizes
    )
    return (
        hidden,
        gradient,
        shares[0],
        shares[1],
        shares[2],
        shares[3],
        shares[4],
        shares[5],
        shares[6],
        shares[7],
        shares[8],
        shares[9],
    )


def solution(mesh):
    sizes = (mesh.shape["blk"], mesh.shape["dp"])
    return jax.shard_map(
        functools.partial(local, mesh_sizes=sizes),
        mesh=mesh,
        in_specs=(
            P("dp", "blk", None),
            P("dp", "blk"),
            P("dp", "blk"),
            P(),
            P(),
            P(),
            P(),
            P(),
            P(),
            P(),
            P(),
            P(),
            P(),
            P("dp", "blk", None),
        ),
        out_specs=(
            P("dp", "blk", None),
            P("dp", "blk", None),
            P("blk"),
            P("blk"),
            P("blk", None),
            P("blk", None),
            P("blk", None),
            P("blk", None),
            P("blk", None),
            P("blk", None),
            P("blk", None),
            P("blk", None),
        ),
        check_vma=False,
    )
```

```python
import functools
import itertools
import math

import jax
import jax.numpy as jnp
from jax import lax
from jax.experimental import pallas as pl
from jax.experimental.pallas import tpu as pltpu
from jax.sharding import PartitionSpec as P

QUERY_HEADS = 15
KEY_VALUE_HEADS = 5
HEAD_DIMENSION = 64
RECUR = 2


epsilon = 1e-05
masked_score = -1e30


def frequencies(head_size):
    return jnp.exp(
        jnp.arange(head_size // 2, dtype=jnp.float32) * (-2.0 * math.log(10000.0) / head_size)
    )


def rms_scale(values):
    return lax.rsqrt(jnp.mean(values * values, axis=-1, keepdims=True) + epsilon)


HEAD_SHARE = QUERY_HEADS // KEY_VALUE_HEADS
FF_TILE = 512


def dot_last(left, right):
    return lax.dot_general(left, right, (((1,), (1,)), ((), ())), preferred_element_type=jnp.float32)


def plain_dot(left, right):
    return jnp.dot(left, right, preferred_element_type=jnp.float32)


def turned_dot(left, right):
    return lax.dot_general(left, right, (((0,), (0,)), ((), ())), preferred_element_type=jnp.float32)


def remote(source, target, sems, at, device):
    return pltpu.make_async_remote_copy(
        src_ref=source,
        dst_ref=target,
        send_sem=sems[0].at[at],
        recv_sem=sems[1].at[at],
        device_id=device,
        device_id_type=pl.DeviceIdType.MESH,
    )


def greet(partners):
    barrier = pltpu.get_barrier_semaphore()
    for partner in partners:
        pl.semaphore_signal(barrier, inc=1, device_id=partner, device_id_type=pl.DeviceIdType.MESH)
    pl.semaphore_wait(barrier, len(partners))


def turn_heads(turned, cosine, sine, heads):
    split = turned.reshape(heads, 2, HEAD_DIMENSION // 2, turned.shape[1])
    first, second = split[:, 0], split[:, 1]
    both = jnp.stack([first * cosine - second * sine, second * cosine + first * sine], axis=1)
    return both.reshape(turned.shape)


def turn_back(turned, cosine, sine, heads):
    return turn_heads(turned, cosine, -sine, heads)


def block_bits(block, m):
    return tuple(lax.rem(block // (1 << bit), 2) for bit in range(m - 1, -1, -1))


def fill_bias(bias, metas, own_meta, level, blk, m, piece):
    query_segments = own_meta[0:1, :]
    key_at = lax.broadcasted_iota(jnp.int32, (piece, piece), 0)
    query_at = lax.broadcasted_iota(jnp.int32, (piece, piece), 1)

    @pl.loop(0, blk + 1)
    def _(block):
        columns = metas[block_bits(block, m)].T
        live = jnp.where(columns[:, 1:2] > level.astype(jnp.float32), columns[:, 0:1], -1.0)
        shift = (blk - block) * piece
        allowed = (live == query_segments) & (key_at <= query_at + shift) | (key_at == query_at + shift)
        bias[block] = jnp.where(allowed, 0.0, masked_score)


def forward_kernel(
    sizes,
    tokens, meta, tables, gains,
    w_query_hbm, key_weight_hbm, value_weight_hbm, w_out_hbm, w_gate_hbm, w_up_hbm, w_down_hbm,
    hidden_out, hid_out, normed_out, turned_out, kv_out, lse_out, att_out, middle_out, nffn_out, gate_out, up_out,
    inner_out, branch_out, metas_out,
    w_query, key_weight, value_weight, w_out, w_gate, w_up, w_down,
    hid, normed, turned, kv, lse, att, middle, nffn, gate, up, inner, branch, metas,
    bias, query_pad, top, total, att_turned,
    load_sems, save_sems, kv_send, kv_recv, meta_send, meta_recv,
):
    m, piece = sizes
    blk = lax.axis_index("blk")
    mine = block_bits(blk, m)
    weights = (
        (key_weight_hbm, key_weight), (value_weight_hbm, value_weight), (w_query_hbm, w_query), (w_out_hbm, w_out),
        (w_gate_hbm, w_gate), (w_up_hbm, w_up), (w_down_hbm, w_down),
    )
    loads = [pltpu.make_async_copy(*pair, load_sems.at[at]) for at, pair in enumerate(weights)]
    for load in loads:
        load.start()
    saved = (
        (normed, normed_out), (turned, turned_out), (kv, kv_out), (lse, lse_out), (att, att_out),
        (middle, middle_out), (nffn, nffn_out), (gate, gate_out), (up, up_out), (inner, inner_out),
        (branch, branch_out),
    )

    def save(at, level):
        return pltpu.make_async_copy(saved[at][0].at[level], saved[at][1].at[level], save_sems.at[at, level])

    metas[mine] = meta[...]
    greet([{"blk": flipped(blk, bit)} for bit in range(m)])

    def place(known):
        return tuple(slice(None) if bit in known else mine[m - 1 - bit] for bit in range(m - 1, -1, -1))

    orders = (list(range(1, m)), list(range(m - 1, 0, -1)))

    def kv_copies(level, group, stage):
        if stage == m - 1:
            ref = kv.at[(level, group, *place(range(1, m)))]
            return [remote(ref, ref, (kv_send, kv_recv), (level, group, 2 * stage), {"blk": flipped(blk, 0)})]
        copies = []
        for side, order in enumerate(orders):
            rows = pl.ds(side * (piece // 2), piece // 2)
            ref = kv.at[(level, group, *place(order[:stage]), rows)]
            copies.append(remote(ref, ref, (kv_send, kv_recv), (level, group, 2 * stage + side),
                                 {"blk": flipped(blk, order[stage])}))
        return copies

    def kv_advance(level, group, stage):
        if stage > 0:
            for copy in kv_copies(level, group, stage - 1):
                copy.wait_recv()
        if stage < m:
            for copy in kv_copies(level, group, stage):
                copy.start()

    def meta_copy(stage):
        bits = list(range(1, m)) + [0]
        ref = metas.at[place(bits[:stage])]
        return remote(ref, ref, (meta_send, meta_recv), stage, {"blk": flipped(blk, bits[stage])})

    meta_copy(0).start()
    cosine, sine = tables[:HEAD_DIMENSION // 2, :], tables[HEAD_DIMENSION // 2:, :]
    hid[0] = tokens[...].T.astype(jnp.float32)
    query_pad[HEAD_DIMENSION:, :] = jnp.zeros_like(query_pad[HEAD_DIMENSION:, :])

    @pl.loop(0, RECUR)
    def _(level):
        hidden = hid[level]
        normed[level] = (hidden * rms_scale(hidden) * gains[0:1, :]).astype(jnp.bfloat16)

        @pl.when(level == 0)
        def _():
            for load in loads[:2]:
                load.wait()

        flat = normed[level]
        keys = turn_heads(dot_last(key_weight[...], flat), cosine, sine, KEY_VALUE_HEADS)
        values = dot_last(value_weight[...], flat)
        for group in range(KEY_VALUE_HEADS):
            here = slice(group * HEAD_DIMENSION, (group + 1) * HEAD_DIMENSION)
            both = jnp.concatenate([keys[here], values[here]], axis=0)
            kv[(level, group, *mine)] = both.T.astype(jnp.bfloat16)
            kv_advance(level, group, 0)

        @pl.when(level == 0)
        def _():
            loads[2].wait()
            for stage in range(1, m - 1):
                meta_copy(stage - 1).wait_recv()
                meta_copy(stage).start()

        queries = turn_heads(plain_dot(flat, w_query[...]).T, cosine, sine, QUERY_HEADS)
        turned[level] = (queries * HEAD_DIMENSION ** (-0.5)).astype(jnp.bfloat16)

        @pl.when(level == 0)
        def _():
            for stage in range(max(1, m - 1), m):
                meta_copy(stage - 1).wait_recv()
                meta_copy(stage).start()

        for stage in range(1, m):
            for group in range(m - stage):
                kv_advance(level, group, stage)

        @pl.when(level == 0)
        def _():
            meta_copy(m - 1).wait_recv()

        fill_bias(bias, metas, meta, level, blk, m, piece)

        @pl.loop(0, KEY_VALUE_HEADS)
        def _(group):
            for stage in range(1, m):
                @pl.when(group + m - stage < KEY_VALUE_HEADS)
                def _():
                    kv_advance(level, group + m - stage, stage)

            kv_advance(level, group, m)
            for member in range(HEAD_SHARE):
                head = group * HEAD_SHARE + member
                rows = pl.ds(pl.multiple_of(head * HEAD_DIMENSION, HEAD_DIMENSION), HEAD_DIMENSION)
                query_pad[:HEAD_DIMENSION, member * piece:(member + 1) * piece] = turned[level, rows, :]
            top[...] = jnp.full_like(top, masked_score)
            total[...] = jnp.zeros_like(total)

            @pl.loop(0, blk + 1)
            def _(step):
                block = blk - step
                rows = kv[(level, group, *block_bits(block, m))]
                here = bias[block]
                scores = plain_dot(rows, query_pad[...]) + jnp.concatenate([here] * HEAD_SHARE, axis=1)
                before = top[0:1, :]
                after = jnp.maximum(before, jnp.max(scores, axis=0, keepdims=True))
                raised = jnp.exp(scores - after)
                shrink = jnp.exp(before - after)
                top[0:1, :] = after
                ones = jnp.ones((16, piece), jnp.bfloat16)
                left = jnp.concatenate([rows.T[HEAD_DIMENSION:], ones], axis=0)
                total[...] = total[...] * shrink + plain_dot(left, raised.astype(jnp.bfloat16))

            sums = total[HEAD_DIMENSION:HEAD_DIMENSION + 1, :]
            lse[level, pl.ds(group, 1), :] = top[0:1, :] + jnp.log(sums)
            out = total[:HEAD_DIMENSION, :] / sums
            for member in range(HEAD_SHARE):
                head = group * HEAD_SHARE + member
                rows = pl.ds(pl.multiple_of(head * HEAD_DIMENSION, HEAD_DIMENSION), HEAD_DIMENSION)
                att_turned[rows, :] = out[:, member * piece:(member + 1) * piece]

        for at in range(4):
            save(at, level).start()
        att[level] = att_turned[...].T.astype(jnp.bfloat16)
        save(4, level).start()

        @pl.when(level == 0)
        def _():
            loads[3].wait()

        attn = plain_dot(att[level], w_out[...])
        mid = hid[level] + attn
        middle[level] = mid
        branch[level] = attn
        save(5, level).start()
        nffn[level] = (mid * rms_scale(mid) * gains[1:2, :]).astype(jnp.bfloat16)
        save(6, level).start()

        @pl.when(level == 0)
        def _():
            loads[4].wait()
            loads[5].wait()

        @pl.loop(0, w_gate.shape[1] // FF_TILE)
        def _(tile):
            columns = pl.ds(pl.multiple_of(tile * FF_TILE, FF_TILE), FF_TILE)
            gate_pre = plain_dot(nffn[level], w_gate[:, columns])
            up_pre = plain_dot(nffn[level], w_up[:, columns])
            gate[level, :, columns] = gate_pre.astype(jnp.bfloat16)
            up[level, :, columns] = up_pre.astype(jnp.bfloat16)
            inner[level, :, columns] = (gate_pre * jax.nn.sigmoid(gate_pre) * up_pre).astype(jnp.bfloat16)

        for at in range(7, 10):
            save(at, level).start()

        @pl.when(level == 0)
        def _():
            loads[6].wait()

        branch[level] += dot_last(inner[level], w_down[...])
        save(10, level).start()
        logit = jnp.sum(hid[level] * gains[pl.ds(2 + level, 1), :], axis=1, keepdims=True)
        weight = jnp.where(meta[...].T[:, 1:2] > level.astype(jnp.float32), jax.nn.sigmoid(logit), 0.0)
        hid[level + 1] = hid[level] + weight * branch[level]

    hidden_out[...] = hid[RECUR].T
    last = [
        pltpu.make_async_copy(hid.at[pl.ds(0, RECUR)], hid_out, save_sems.at[len(saved), 0]),
        pltpu.make_async_copy(metas, metas_out, save_sems.at[len(saved), 1]),
    ]
    for copy in last:
        copy.start()
    for stage in range(m):
        meta_copy(stage).wait_send()
    for level in range(RECUR):
        for group in range(KEY_VALUE_HEADS):
            for stage in range(m):
                for copy in kv_copies(level, group, stage):
                    copy.wait_send()
        for at in range(len(saved)):
            save(at, level).wait()
    for copy in last:
        copy.wait()


def forward(tokens, meta, tables, gains, weights, nb):
    m = nb.bit_length() - 1
    width, piece = tokens.shape
    hidden_units = weights[4].shape[1]
    blocks = (2,) * m
    saved = {
        "hid": ((RECUR, piece, width), jnp.float32),
        "normed": ((RECUR, piece, width), jnp.bfloat16),
        "turned": ((RECUR, width, piece), jnp.bfloat16),
        "kv": ((RECUR, KEY_VALUE_HEADS, *blocks, piece, 2 * HEAD_DIMENSION), jnp.bfloat16),
        "lse": ((RECUR, 8, HEAD_SHARE * piece), jnp.float32),
        "att": ((RECUR, piece, width), jnp.bfloat16),
        "middle": ((RECUR, piece, width), jnp.float32),
        "nffn": ((RECUR, piece, width), jnp.bfloat16),
        "gate": ((RECUR, piece, hidden_units), jnp.bfloat16),
        "up": ((RECUR, piece, hidden_units), jnp.bfloat16),
        "inner": ((RECUR, piece, hidden_units), jnp.bfloat16),
        "branch": ((RECUR, piece, width), jnp.float32),
        "metas": ((*blocks, 8, piece), jnp.float32),
    }
    shapes = [jax.ShapeDtypeStruct(*entry) for entry in saved.values()]
    w_query, key_weight, value_weight, w_out, w_gate, w_up, w_down = weights
    vmem, anywhere = pl.BlockSpec(memory_space=pltpu.VMEM), pl.BlockSpec(memory_space=pl.ANY)
    scratch = [pltpu.VMEM(array.shape, array.dtype) for array in weights]
    scratch += [pltpu.VMEM((RECUR + 1, piece, width), jnp.float32)]
    scratch += [pltpu.VMEM(*entry) for entry in list(saved.values())[1:]]
    scratch += [
        pltpu.VMEM((nb, piece, piece), jnp.float32),
        pltpu.VMEM((2 * HEAD_DIMENSION, HEAD_SHARE * piece), jnp.bfloat16),
        pltpu.VMEM((8, HEAD_SHARE * piece), jnp.float32),
        pltpu.VMEM((HEAD_DIMENSION + 16, HEAD_SHARE * piece), jnp.float32),
        pltpu.VMEM((width, piece), jnp.float32),
        pltpu.SemaphoreType.DMA((7,)),
        pltpu.SemaphoreType.DMA((len(saved) - 1, RECUR)),
        pltpu.SemaphoreType.DMA((RECUR, KEY_VALUE_HEADS, 2 * m)),
        pltpu.SemaphoreType.DMA((RECUR, KEY_VALUE_HEADS, 2 * m)),
        pltpu.SemaphoreType.DMA((m,)),
        pltpu.SemaphoreType.DMA((m,)),
    ]
    outs = pl.pallas_call(
        functools.partial(forward_kernel, (m, piece)),
        out_shape=[jax.ShapeDtypeStruct((width, piece), jnp.float32)] + shapes,
        in_specs=[vmem] * 4 + [anywhere] * 7,
        out_specs=[vmem] + [anywhere] * len(shapes),
        scratch_shapes=scratch,
        compiler_params=pltpu.CompilerParams(
            collective_id=1, has_side_effects=True, vmem_limit_bytes=62 * 1024 * 1024
        ),
        cost_estimate=pl.CostEstimate(
            flops=2 * RECUR * piece * width * 10240, bytes_accessed=48 * 1024 * 1024, transcendentals=0
        ),
        name="forward_levels",
    )(tokens, meta, tables, gains, *weights)
    return outs[0], dict(zip(saved, outs[1:]))


UNIT_COLUMNS = 256


def bits_of(number, count):
    return tuple((number >> (count - 1 - at)) & 1 for at in range(count))


def bit_of(position, bit):
    return lax.rem(position // (1 << bit), 2)


def flipped(position, bit):
    return position + (1 << bit) * (1 - 2 * bit_of(position, bit))


class Piece:
    def __init__(self, at, kept_at, slot, flavour, family, sems, bits):
        self.at, self.kept_at, self.slot, self.family, self.sems = at, kept_at, slot, family, sems
        self.m, self.n = bits
        left = list(range(self.m - 1, -1, -1))
        self.order = []
        for stage in range(self.m):
            place = len(left) - 1 if stage == 0 or flavour == 0 else 0
            self.order.append((left.pop(place), place, len(left)))
        self.last = self.m + self.n
        self.blk = lax.axis_index("blk")
        self.dp = lax.axis_index("dp") if self.n else None

    def half(self, ref, side):
        rows, columns = self.family["shape"]
        if self.family["split"] == 0:
            return ref.at[pl.ds(pl.multiple_of(side * (rows // 2), rows // 2), rows // 2), :]
        return ref.at[:, pl.ds(pl.multiple_of(side * (columns // 2), columns // 2), columns // 2)]

    def held(self, stage):
        if stage == 0:
            return self.family["part"], self.slot
        return self.family["blk"][stage - 1], self.kept_at

    def copy(self, stage):
        m, family = self.m, self.family
        if stage < m:
            bit, place, others = self.order[stage]
            ref, index = self.held(stage)
            chosen = [slice(None)] * (others + 1)
            chosen[place] = 1 - bit_of(self.blk, bit)
            source = ref.at[(index, *chosen)]
            target = family["blk"][stage].at[self.kept_at]
            device = {"blk": flipped(self.blk, bit)}
        elif stage < self.last:
            bit = stage - m
            if bit == 0:
                source = self.half(family["blk"][m - 1].at[self.kept_at], 1 - bit_of(self.dp, 0))
            else:
                source = family["dp"][bit - 1].at[self.kept_at]
            target = family["dp"][bit].at[self.kept_at]
            device = {"dp": flipped(self.dp, bit)}
        else:
            source = self.half(family["out"].at[self.kept_at], bit_of(self.dp, 0))
            target = source
            device = {"dp": flipped(self.dp, 0)}
        return remote(source, target, self.sems, (self.at, stage), device)

    def start(self, stage):
        self.copy(stage).start()

    def finish(self, stage):
        m, family = self.m, self.family
        self.copy(stage).wait_recv()
        if stage < m:
            bit, place, others = self.order[stage]
            ref, index = self.held(stage)
            for combo in itertools.product(range(2), repeat=others):
                chosen = list(combo)
                chosen.insert(place, bit_of(self.blk, bit))
                into = family["blk"][stage].at[(self.kept_at, *combo)]
                self.add(into, into, ref.at[(index, *chosen)])
            if stage == 0:
                self.copy(0).wait_send()
        elif stage < self.last:
            bit = stage - m
            got = family["dp"][bit].at[self.kept_at]
            if bit == 0:
                own = self.half(family["blk"][m - 1].at[self.kept_at], bit_of(self.dp, 0))
            else:
                own = family["dp"][bit - 1].at[self.kept_at]
            into = got
            if stage == self.last - 1:
                into = self.half(family["out"].at[self.kept_at], bit_of(self.dp, 0))
            self.add(into, got, own)

    def add(self, into, left, right):
        into[...] = left[...] + right[...]

    def drained(self, stages):
        for stage in stages:
            self.copy(stage).wait_send()


def norm_gradient(grad_norm, values, gain):
    scale = rms_scale(values)
    weighted = grad_norm * gain
    grad_values = scale * weighted - values * (scale * scale * scale) * jnp.mean(
        weighted * values, axis=-1, keepdims=True
    )
    return grad_values, jnp.sum(grad_norm * values * scale, axis=0, keepdims=True)


def backward_kernel(
    sizes,
    grad_in, meta, tables, gains,
    hid_hbm, branch_hbm, w_down_hbm, gate_hbm, up_hbm, w_gate_hbm, w_up_hbm, middle_hbm, w_out_hbm, att_hbm,
    turned_hbm, kv_hbm, lse_hbm, metas_hbm, w_query_hbm, key_weight_hbm, value_weight_hbm,
    grad_out, small_out, dffn_out, dgate_out, dup_out, far_out, near_out,
    hid, branch, w_down, gate, up, w_gate, w_up, middle, w_out, att,
    turned, kv, lse, metas, w_query, key_weight, value_weight,
    dffn, dgate, dup, far, near,
    grad_hidden, dnorm, dbranch, dat_turned, att_turned, dq_turned,
    bias, query_pad, dat_pad, query_rows, dat_rows, dq_sum, part,
    *others,
):
    m, piece, level = sizes
    halves, (load_sems, save_sems, send_sems, recv_sems) = others[:m], others[m:]
    blk = lax.axis_index("blk")
    sources = (
        hid_hbm.at[level], branch_hbm.at[level], w_down_hbm, gate_hbm.at[level], up_hbm.at[level], w_gate_hbm, w_up_hbm,
        middle_hbm.at[level], w_out_hbm, att_hbm.at[level], turned_hbm.at[level], kv_hbm.at[level], lse_hbm.at[level],
        metas_hbm, w_query_hbm, key_weight_hbm, value_weight_hbm,
    )
    targets = (
        hid, branch, w_down, gate, up, w_gate, w_up, middle, w_out, att, turned, kv, lse, metas, w_query, key_weight,
        value_weight,
    )
    loads = [
        pltpu.make_async_copy(source, target, load_sems.at[at])
        for at, (source, target) in enumerate(zip(sources, targets))
    ]
    for load in loads:
        load.start()
    saves = [
        pltpu.make_async_copy(source, target, save_sems.at[at])
        for at, (source, target) in enumerate(
            ((dffn, dffn_out), (dgate, dgate_out), (dup, dup_out), (far, far_out), (near, near_out))
        )
    ]
    greet([{"blk": flipped(blk, bit)} for bit in range(m)])

    small_out[...] = jnp.zeros_like(small_out)
    router = gains[2 + level:3 + level, :]
    for at in range(2):
        loads[at].wait()
    active = meta[...].T[:, 1:2] > float(level)
    gradient = grad_in[...].T.astype(jnp.float32) if level == RECUR - 1 else grad_in[...]
    chosen = jax.nn.sigmoid(jnp.sum(hid[...] * router, axis=1, keepdims=True))
    dbranch[...] = jnp.where(active, chosen, 0.0) * gradient
    dchosen = jnp.where(active, jnp.sum(gradient * branch[...], axis=1, keepdims=True), 0.0)
    dlogit = dchosen * chosen * (1.0 - chosen)
    small_out[2 + level:3 + level, :] = jnp.sum(hid[...] * dlogit, axis=0, keepdims=True)
    grad_hidden[...] = gradient + dlogit * router
    dffn[...] = dbranch[...].astype(jnp.bfloat16)
    saves[0].start()
    dnorm[...] = jnp.zeros_like(dnorm)
    for at in range(2, 7):
        loads[at].wait()

    @pl.loop(0, w_gate.shape[1] // FF_TILE)
    def _(tile):
        columns = pl.ds(pl.multiple_of(tile * FF_TILE, FF_TILE), FF_TILE)
        dinner = plain_dot(dffn[...], w_down[:, columns])
        gate_pre, up_pre = gate[:, columns].astype(jnp.float32), up[:, columns].astype(jnp.float32)
        opened = jax.nn.sigmoid(gate_pre)
        dgate_tile = (dinner * up_pre * opened * (1.0 + gate_pre * (1.0 - opened))).astype(jnp.bfloat16)
        dup_tile = (dinner * gate_pre * opened).astype(jnp.bfloat16)
        dgate[:, columns] = dgate_tile
        dup[:, columns] = dup_tile
        dnorm[...] += dot_last(dgate_tile, w_gate[:, columns]) + dot_last(dup_tile, w_up[:, columns])

    saves[1].start()
    saves[2].start()
    for at in range(7, 10):
        loads[at].wait()
    dmiddle, gain_share = norm_gradient(dnorm[...], middle[...], gains[1:2, :])
    small_out[1:2, :] = gain_share
    grad_hidden[...] += dmiddle
    dattn = (dbranch[...] + dmiddle).astype(jnp.bfloat16)
    lead = far.shape[1] - dattn.shape[1]
    far[:, :lead] = jnp.zeros((piece, lead), jnp.bfloat16)
    far[:, lead:] = dattn
    saves[3].start()
    dat_turned[...] = dot_last(w_out[...], dattn).astype(jnp.bfloat16)
    att_turned[...] = att[...].T
    for at in range(10, 14):
        loads[at].wait()
    fill_bias(bias, metas, meta, jnp.int32(level), blk, m, piece)
    query_pad[HEAD_DIMENSION:, :] = jnp.zeros_like(query_pad[HEAD_DIMENSION:, :])
    dat_pad[:HEAD_DIMENSION, :] = jnp.zeros_like(dat_pad[:HEAD_DIMENSION, :])

    family = {"part": part, "blk": halves, "dp": (), "out": None, "shape": (piece // 2, 2 * HEAD_DIMENSION), "split": 0}

    def pieces(group):
        return [
            Piece(2 * group + side, 2 * group + side, 2 * group + side, side, family, (send_sems, recv_sems), (m, 0))
            for side in range(2)
        ]

    def move(group, stage):
        for piece_of in pieces(group):
            piece_of.finish(stage)
            if stage + 1 < m:
                piece_of.start(stage + 1)

    nb = 1 << m

    @pl.loop(0, KEY_VALUE_HEADS)
    def _(group):
        for member in range(HEAD_SHARE):
            head = group * HEAD_SHARE + member
            rows = pl.ds(pl.multiple_of(head * HEAD_DIMENSION, HEAD_DIMENSION), HEAD_DIMENSION)
            lanes = slice(member * piece, (member + 1) * piece)
            query_pad[:HEAD_DIMENSION, lanes] = turned[rows, :]
            dat_pad[HEAD_DIMENSION:, lanes] = dat_turned[rows, :]
        query_rows[...] = query_pad[...].T
        dat_rows[...] = dat_pad[...].T
        carried = []
        for member in range(HEAD_SHARE):
            head = group * HEAD_SHARE + member
            rows = pl.ds(pl.multiple_of(head * HEAD_DIMENSION, HEAD_DIMENSION), HEAD_DIMENSION)
            product = dat_turned[rows, :].astype(jnp.float32) * att_turned[rows, :].astype(jnp.float32)
            carried.append(jnp.sum(product, axis=0, keepdims=True))
        carried = jnp.concatenate(carried, axis=1)
        log_total = lse[pl.ds(group, 1), :]
        dq_sum[...] = jnp.zeros_like(dq_sum)

        @pl.loop(0, blk + 1)
        def _(block):
            rows = kv[(group, *block_bits(block, m))]
            here = jnp.concatenate([bias[block]] * HEAD_SHARE, axis=1)
            probability = jnp.exp(plain_dot(rows, query_pad[...]) + here - log_total)
            dprob = plain_dot(rows, dat_pad[...])
            dscores = (probability * (dprob - carried)).astype(jnp.bfloat16)
            share = plain_dot(dscores, query_rows[...]) + plain_dot(probability.astype(jnp.bfloat16), dat_rows[...])
            share = share.astype(jnp.bfloat16)
            for side in range(2):
                part[(2 * group + side, *block_bits(block, m))] = share[side * (piece // 2):(side + 1) * (piece // 2)]
            dq_sum[...] += plain_dot(rows.T[:HEAD_DIMENSION], dscores)

        @pl.loop(blk + 1, nb)
        def _(block):
            for side in range(2):
                part[(2 * group + side, *block_bits(block, m))] = jnp.zeros(family["shape"], jnp.bfloat16)

        for piece_of in pieces(group):
            piece_of.start(0)
        for member in range(HEAD_SHARE):
            head = group * HEAD_SHARE + member
            rows = pl.ds(pl.multiple_of(head * HEAD_DIMENSION, HEAD_DIMENSION), HEAD_DIMENSION)
            dq_turned[rows, :] = dq_sum[:, member * piece:(member + 1) * piece]
        for stage in range(m - 1):
            @pl.when(group - 1 - stage >= 0)
            def _():
                move(group - 1 - stage, stage)

    cosine, sine = tables[:HEAD_DIMENSION // 2, :], tables[HEAD_DIMENSION // 2:, :]
    keys_width = KEY_VALUE_HEADS * HEAD_DIMENSION
    for virtual in range(KEY_VALUE_HEADS, KEY_VALUE_HEADS + m - 1):
        for stage in range(m - 1):
            if 0 <= virtual - 1 - stage < KEY_VALUE_HEADS:
                move(virtual - 1 - stage, stage)
        if virtual == KEY_VALUE_HEADS:
            for at in range(14, 17):
                loads[at].wait()
            dqueries = turn_back(dq_turned[...] * HEAD_DIMENSION ** (-0.5), cosine, sine, QUERY_HEADS)
            dqueries = dqueries.T.astype(jnp.bfloat16)
            near[:, 2 * keys_width:2 * keys_width + dqueries.shape[1]] = dqueries
            dnorm[...] = dot_last(dqueries, w_query[...])
    tail = near.shape[1] - 2 * keys_width - dqueries.shape[1]
    near[:, near.shape[1] - tail:] = jnp.zeros((piece, tail), jnp.bfloat16)
    dkeys, dvalues = [], []
    for group in range(KEY_VALUE_HEADS):
        move(group, m - 1)
        both = jnp.concatenate([halves[m - 1][2 * group], halves[m - 1][2 * group + 1]], axis=0)
        both = both.astype(jnp.float32).T
        dkeys.append(both[:HEAD_DIMENSION])
        dvalues.append(both[HEAD_DIMENSION:])
    dkeys = turn_back(jnp.concatenate(dkeys, axis=0), cosine, sine, KEY_VALUE_HEADS).T.astype(jnp.bfloat16)
    dvalues = jnp.concatenate(dvalues, axis=0).T.astype(jnp.bfloat16)
    near[:, :keys_width] = dkeys
    near[:, keys_width:2 * keys_width] = dvalues
    saves[4].start()
    dinput = dnorm[...] + plain_dot(dkeys, key_weight[...]) + plain_dot(dvalues, value_weight[...])
    dhidden, gain_share = norm_gradient(dinput, hid[...], gains[0:1, :])
    small_out[0:1, :] = gain_share
    result = grad_hidden[...] + dhidden
    grad_out[...] = result.T if level == 0 else result
    for group in range(KEY_VALUE_HEADS):
        for piece_of in pieces(group):
            piece_of.drained(range(1, m))
    for save in saves:
        save.wait()


def backward(level, grad_in, meta, tables, gains, saved, weights, nb):
    m = nb.bit_length() - 1
    width = weights[0].shape[0]
    piece = meta.shape[1]
    w_query, key_weight, value_weight, w_out, w_gate, w_up, w_down = weights
    hidden_units = w_gate.shape[1]
    keys_width = KEY_VALUE_HEADS * HEAD_DIMENSION
    operands = (
        saved["hid"], saved["branch"], w_down, saved["gate"], saved["up"], w_gate, w_up, saved["middle"], w_out,
        saved["att"], saved["turned"], saved["kv"], saved["lse"], saved["metas"], w_query, key_weight, value_weight,
    )
    unsliced = {2, 5, 6, 8, 13, 14, 15, 16}
    sides = [
        ((piece, width), jnp.bfloat16), ((piece, hidden_units), jnp.bfloat16), ((piece, hidden_units), jnp.bfloat16),
        ((piece, width + 2 * keys_width + width - 1536), jnp.bfloat16), ((piece, 1792), jnp.bfloat16),
    ]
    wide, pad = HEAD_SHARE * piece, 2 * HEAD_DIMENSION
    vmem, anywhere = pl.BlockSpec(memory_space=pltpu.VMEM), pl.BlockSpec(memory_space=pl.ANY)
    scratch = [
        pltpu.VMEM(array.shape if at in unsliced else array.shape[1:], array.dtype) for at, array in enumerate(operands)
    ]
    scratch += [pltpu.VMEM(*side) for side in sides]
    scratch += [pltpu.VMEM((piece, width), jnp.float32)] * 3
    scratch += [pltpu.VMEM((width, piece), jnp.bfloat16)] * 2
    scratch += [
        pltpu.VMEM((width, piece), jnp.float32),
        pltpu.VMEM((nb, piece, piece), jnp.float32),
        pltpu.VMEM((pad, wide), jnp.bfloat16),
        pltpu.VMEM((pad, wide), jnp.bfloat16),
        pltpu.VMEM((wide, pad), jnp.bfloat16),
        pltpu.VMEM((wide, pad), jnp.bfloat16),
        pltpu.VMEM((HEAD_DIMENSION, wide), jnp.float32),
        pltpu.VMEM((2 * KEY_VALUE_HEADS, *(2,) * m, piece // 2, pad), jnp.bfloat16),
    ]
    for stage in range(m):
        scratch.append(pltpu.VMEM((2 * KEY_VALUE_HEADS, *(2,) * (m - 1 - stage), piece // 2, pad), jnp.bfloat16))
    scratch += [
        pltpu.SemaphoreType.DMA((len(operands),)),
        pltpu.SemaphoreType.DMA((len(sides),)),
        pltpu.SemaphoreType.DMA((2 * KEY_VALUE_HEADS, m)),
        pltpu.SemaphoreType.DMA((2 * KEY_VALUE_HEADS, m)),
    ]
    result = (width, piece) if level == 0 else (piece, width)
    outs = pl.pallas_call(
        functools.partial(backward_kernel, (m, piece, level)),
        out_shape=[jax.ShapeDtypeStruct(result, jnp.float32), jax.ShapeDtypeStruct((8, width), jnp.float32)]
        + [jax.ShapeDtypeStruct(*side) for side in sides],
        in_specs=[vmem] * 4 + [anywhere] * len(operands),
        out_specs=[vmem] * 2 + [anywhere] * len(sides),
        scratch_shapes=scratch,
        compiler_params=pltpu.CompilerParams(
            collective_id=2 + level, has_side_effects=True, vmem_limit_bytes=62 * 1024 * 1024
        ),
        cost_estimate=pl.CostEstimate(
            flops=2 * piece * width * 10240, bytes_accessed=48 * 1024 * 1024, transcendentals=0
        ),
        name="backward_level_%d" % level,
    )(grad_in, meta, tables, gains, *operands)
    return outs


def reduce_kernel(
    sizes,
    inner_hbm, nffn_hbm, normed_hbm, attended_hbm,
    dffn_near, dgate_near, dup_near, far_near, near_near,
    dffn_deep, dgate_deep, dup_deep, far_deep, near_deep,
    small_hbm,
    out_wide, out_down, out_small,
    inner, nffn, normed, attended, dffn, dgate, dup, far, near,
    nffn_turned, normed_turned, attended_turned,
    part_wide, part_down, part_small,
    *others,
):
    nb, nd, m, n, padded = sizes
    blk_wide, others = others[:m], others[m:]
    blk_down, others = others[:m], others[m:]
    blk_small, others = others[:m], others[m:]
    dp_wide, others = others[:n], others[n:]
    dp_down, others = others[:n], others[n:]
    dp_small, others = others[:n], others[n:]
    load_sems, send_sems, recv_sems = others
    blk, dp = lax.axis_index("blk"), lax.axis_index("dp")

    half = dffn.shape[0] // RECUR
    pairs = []
    for low, deep, place in (
        (dffn_near, dffn_deep, dffn), (dgate_near, dgate_deep, dgate), (dup_near, dup_deep, dup),
        (far_near, far_deep, far), (near_near, near_deep, near),
    ):
        pairs += [(low, place.at[pl.ds(0, half)]), (deep, place.at[pl.ds(half, half)])]
    pairs = [(inner_hbm, inner)] + pairs[:2] + [(nffn_hbm, nffn)] + pairs[2:6] + [
        (normed_hbm, normed), (attended_hbm, attended)] + pairs[6:] + [(small_hbm, part_small.at[0])]
    loads = [
        pltpu.make_async_copy(source, place, load_sems.at[at])
        for at, (source, place) in enumerate(pairs)
    ]
    for load in loads:
        load.start()

    greet([{"blk": flipped(blk, bit)} for bit in range(m)] + [{"dp": flipped(dp, bit)} for bit in range(n)])

    down_rows = part_down.shape[-2]
    wide = {"part": part_wide, "blk": blk_wide, "dp": dp_wide, "out": out_wide,
            "shape": (2 * padded, UNIT_COLUMNS), "split": 1}
    down = {"part": part_down, "blk": blk_down, "dp": dp_down, "out": out_down,
            "shape": (down_rows, dffn.shape[1]), "split": 0}
    small = {"part": part_small, "blk": blk_small, "dp": dp_small, "out": out_small,
             "shape": (16, 128), "split": 0}
    slots = part_wide.shape[0]
    sems = (send_sems, recv_sems)
    pieces = []
    for at in range(5):
        pieces.append(Piece(len(pieces), at, at, len(pieces) % 2, down, sems, (m, n)))
    for at in range(15):
        pieces.append(Piece(len(pieces), at, at % slots, len(pieces) % 2, wide, sems, (m, n)))
    pieces.append(Piece(len(pieces), 0, 0, 0, small, sems, (m, n)))

    def compute_down():
        for load in loads[:3]:
            load.wait()
        width = 640
        group = width // (5 * down_rows)
        for at in range(inner.shape[1] // width):
            result = turned_dot(inner[:, at * width:(at + 1) * width], dffn[...])
            for member in range(group):
                target = bits_of(at * group + member, m)
                for unit in range(5):
                    first = (member * 5 + unit) * down_rows
                    part_down[(unit, *target)] = result[first:first + down_rows].astype(jnp.bfloat16)

    def compute_wide(at):
        slot = at % slots
        if at == 0:
            loads[3].wait()
            nffn_turned[...] = nffn[...].T
            for load in loads[4:6]:
                load.wait()
        if at == 5:
            for load in loads[6:8]:
                load.wait()
        if at == 10:
            for load in loads[8:14]:
                load.wait()
            normed_turned[...] = normed[...].T
            attended_turned[...] = attended[...].T
        block, at_column = at // 5, (at % 5) * UNIT_COLUMNS
        if block < 2:
            right = dgate if block == 0 else dup
            upper = plain_dot(nffn_turned[...], right[:, at_column:at_column + UNIT_COLUMNS])
            second = 1280 + at_column
            lower = plain_dot(nffn_turned[...], right[:, second:second + UNIT_COLUMNS])
        else:
            upper = plain_dot(normed_turned[...], near[:, at_column:at_column + UNIT_COLUMNS])
            second = 1280 + at_column
            lower = None
            if second < 1600:
                lower = plain_dot(normed_turned[...], near[:, second:second + UNIT_COLUMNS])
            if second >= 1536:
                more = plain_dot(attended_turned[...], far[:, second - 1536:second - 1536 + UNIT_COLUMNS])
                lower = more if lower is None else lower + more
        for target in range(nb):
            here = slice(target * padded, (target + 1) * padded)
            both = jnp.concatenate([upper[here], lower[here]], axis=0)
            part_wide[(slot, *bits_of(target, m))] = both.astype(jnp.bfloat16)

    def compute(piece):
        if piece.family is wide:
            compute_wide(piece.kept_at)
        elif piece.family is small:
            loads[14].wait()
        piece.start(0)

    groups = [pieces[at:at + 2] for at in range(0, 18, 2)] + [pieces[18:]]
    compute_down()
    for piece in groups[0] + groups[1]:
        compute(piece)

    def move(group, stage):
        for piece in group:
            piece.finish(stage)
            piece.start(stage + 1)

    count = len(groups)
    for tick in range(count + m + n - 1):
        for stage in range(m + n - 1, -1, -1):
            if 0 <= tick - stage < count:
                move(groups[tick - stage], stage)
        if tick + 2 < count:
            for piece in groups[tick + 2]:
                compute(piece)
    for piece in pieces:
        piece.finish(m + n)
    for piece in pieces:
        piece.drained(range(1, m + n + 1))


def unpack_kernel(sizes, wide, down, little, norm_attn, norm_ffn, query, key, value, out, gate, up, down_out, router, rest):
    rows, padded = sizes
    norm_attn[...] = little[0, 0:1, :rows]
    norm_ffn[...] = little[0, 1:2, :rows]
    router[...] = little[0, 2:4, :rows]
    for unit in range(5):
        for first, target in ((0, gate), (5, up), (10, rest)):
            tile = wide[first + unit].astype(jnp.float32)
            for side in range(2):
                column = side * 1280 + unit * UNIT_COLUMNS
                target[:, column:column + UNIT_COLUMNS] = tile[side * padded:side * padded + rows]
        down_rows = down.shape[1]
        down_out[unit * down_rows:(unit + 1) * down_rows, :] = down[unit].astype(jnp.float32)
    keys_width, width = key.shape[0], query.shape[1]
    key[...] = rest[:, :keys_width].T
    value[...] = rest[:, keys_width:2 * keys_width].T
    query[...] = rest[:, 2 * keys_width:2 * keys_width + width]
    out[...] = rest[:, 2 * keys_width + width:]


def reduced_weight_grads(kept, sides, small, mesh_sizes):
    nb, nd = mesh_sizes
    m, n = nb.bit_length() - 1, nd.bit_length() - 1
    inner, nffn, normed, attended = kept
    tokens, width = normed.shape
    rows = width // nb
    padded = -(-rows // 8) * 8
    hidden_units = inner.shape[1]
    down_rows = hidden_units // nb // 5
    keys_width = KEY_VALUE_HEADS * HEAD_DIMENSION

    def spread(array):
        if padded == rows:
            return array
        split = array.reshape(tokens, nb, rows)
        return jnp.pad(split, ((0, 0), (0, 0), (0, padded - rows))).reshape(tokens, nb * padded)

    small_parts = jnp.pad(small.reshape(4, nb, rows).transpose(1, 0, 2), ((0, 0), (0, 12), (0, 128 - rows)))
    operands = (inner, spread(nffn), spread(normed), spread(attended), *sides[0], *sides[1],
                small_parts.reshape((2,) * m + (16, 128)))
    wide_shape, down_shape = (2 * padded, UNIT_COLUMNS), (down_rows, width)
    scratch = [pltpu.VMEM(array.shape, array.dtype) for array in operands[:4]]
    scratch += [pltpu.VMEM((tokens, array.shape[1]), array.dtype) for array in sides[0]]
    scratch += [pltpu.VMEM((nb * padded, tokens), jnp.bfloat16)] * 3
    families = ((15, wide_shape, jnp.bfloat16, 6, 1), (5, down_shape, jnp.bfloat16, 5, 0), (1, (16, 128), jnp.float32, 1, 0))
    for count, shape, dtype, slots, _ in families:
        scratch.append(pltpu.VMEM((slots, *(2,) * m, *shape), dtype))
    for count, shape, dtype, _, _ in families:
        for stage in range(m):
            scratch.append(pltpu.VMEM((count, *(2,) * (m - 1 - stage), *shape), dtype))
    for count, shape, dtype, _, split in families:
        half = (shape[0], shape[1] // 2) if split else (shape[0] // 2, shape[1])
        scratch += [pltpu.VMEM((count, *half), dtype)] * n
    scratch += [pltpu.SemaphoreType.DMA((15,)), pltpu.SemaphoreType.DMA((21, m + n + 1)), pltpu.SemaphoreType.DMA((21, m + n + 1))]
    vmem = pl.BlockSpec(memory_space=pltpu.VMEM)
    packed = pl.pallas_call(
        functools.partial(reduce_kernel, (nb, nd, m, n, padded)),
        out_shape=(
            jax.ShapeDtypeStruct((15, *wide_shape), jnp.bfloat16),
            jax.ShapeDtypeStruct((5, *down_shape), jnp.bfloat16),
            jax.ShapeDtypeStruct((1, 16, 128), jnp.float32),
        ),
        in_specs=[pl.BlockSpec(memory_space=pl.ANY)] * len(operands),
        out_specs=[vmem] * 3,
        scratch_shapes=scratch,
        compiler_params=pltpu.CompilerParams(
            collective_id=0, has_side_effects=True, vmem_limit_bytes=60 * 1024 * 1024
        ),
        cost_estimate=pl.CostEstimate(
            flops=2 * tokens * width * 10240, bytes_accessed=20 * 1024 * 1024, transcendentals=0
        ),
        name="weight_grads",
    )(*operands)
    shapes = (
        (1, rows), (1, rows), (rows, width), (keys_width, rows), (keys_width, rows), (rows, width),
        (rows, hidden_units), (rows, hidden_units), (5 * down_rows, width), (2, rows),
    )
    outs = pl.pallas_call(
        functools.partial(unpack_kernel, (rows, padded)),
        out_shape=[jax.ShapeDtypeStruct(shape, jnp.float32) for shape in shapes],
        in_specs=[vmem] * 3,
        out_specs=[vmem] * len(shapes),
        scratch_shapes=[pltpu.VMEM((rows, 2560), jnp.float32)],
        compiler_params=pltpu.CompilerParams(vmem_limit_bytes=32 * 1024 * 1024),
        name="unpack",
    )(*packed)
    norm_attn, norm_ffn, query, key, value, out, gate, up, down, router = outs
    return norm_attn[0], norm_ffn[0], query, key.T, value.T, out, gate, up, down, router.T


def local(
    tokens,
    depths,
    segments,
    norm_attn,
    norm_ffn,
    w_query,
    key_weight,
    value_weight,
    w_out,
    w_gate,
    w_up,
    w_down,
    w_router,
    cotangent,
    mesh_sizes,
):
    piece, width = tokens.shape[1:]
    positions = lax.axis_index("blk") * piece + jnp.arange(piece, dtype=jnp.int32)
    angles = frequencies(HEAD_DIMENSION)[:, None] * positions.astype(jnp.float32)[None, :]
    tables = jnp.concatenate([jnp.cos(angles), jnp.sin(angles)], axis=0)
    gains = jnp.concatenate([norm_attn[None], norm_ffn[None], w_router.T]).astype(jnp.float32)
    gains = jnp.pad(gains, ((0, 4), (0, 0)))
    meta = jnp.pad(jnp.concatenate([segments, depths]).astype(jnp.float32), ((0, 6), (0, 0)))
    weights = (w_query, key_weight.T, value_weight.T, w_out, w_gate, w_up, w_down.T)
    hidden, saved = forward(tokens[0].T, meta, tables, gains, weights, mesh_sizes[0])
    gradient, small, sides = cotangent[0].T, 0.0, []
    for level in reversed(range(RECUR)):
        gradient, share, *side = backward(level, gradient, meta, tables, gains, saved, weights, mesh_sizes[0])
        small = small + share
        sides.insert(0, side)
    kept = [saved[name].reshape(RECUR * piece, -1) for name in ("inner", "nffn", "normed", "att")]
    shares = reduced_weight_grads(kept, sides, small[:4], mesh_sizes)
    return (hidden.T[None], gradient.T[None], *shares)


def solution(mesh):
    sizes = (mesh.shape["blk"], mesh.shape["dp"])
    return jax.shard_map(
        functools.partial(local, mesh_sizes=sizes),
        mesh=mesh,
        in_specs=(
            P("dp", "blk", None),
            P("dp", "blk"),
            P("dp", "blk"),
            P(),
            P(),
            P(),
            P(),
            P(),
            P(),
            P(),
            P(),
            P(),
            P(),
            P("dp", "blk", None),
        ),
        out_specs=(
            P("dp", "blk", None),
            P("dp", "blk", None),
            P("blk"),
            P("blk"),
            P("blk", None),
            P("blk", None),
            P("blk", None),
            P("blk", None),
            P("blk", None),
            P("blk", None),
            P("blk", None),
            P("blk", None),
        ),
        check_vma=False,
    )
```

```python
import functools
import itertools
import math
import types

import jax
import jax.numpy as jnp
from jax import lax
from jax.experimental import pallas as pl
from jax.experimental.pallas import tpu as pltpu
from jax.sharding import PartitionSpec as P

QUERY_HEADS = 15
KEY_VALUE_HEADS = 5
HEAD_DIMENSION = 64
RECUR = 2
HEAD_SHARE = QUERY_HEADS // KEY_VALUE_HEADS
KEYS_WIDTH = KEY_VALUE_HEADS * HEAD_DIMENSION
PAIR = 2 * HEAD_DIMENSION
FF_TILE = 512
UNIT_COLUMNS = 256
VMEM_LIMIT = 62 * 1024 * 1024

epsilon = 1e-05
masked_score = -1e30
low = jnp.bfloat16


def frequencies(head_size):
    return jnp.exp(
        jnp.arange(head_size // 2, dtype=jnp.float32) * (-2.0 * math.log(10000.0) / head_size)
    )


def rms_scale(values):
    return lax.rsqrt(jnp.mean(values * values, axis=-1, keepdims=True) + epsilon)


def norm_gradient(grad_norm, values, gain):
    scale = rms_scale(values)
    weighted = grad_norm * gain
    grad_values = scale * weighted - values * (scale * scale * scale) * jnp.mean(
        weighted * values, axis=-1, keepdims=True
    )
    return grad_values, jnp.sum(grad_norm * values * scale, axis=0, keepdims=True)


def dot_last(left, right):
    return lax.dot_general(left, right, (((1,), (1,)), ((), ())), preferred_element_type=jnp.float32)


def plain_dot(left, right):
    return jnp.dot(left, right, preferred_element_type=jnp.float32)


def bits_of(number, count):
    return tuple((number >> (count - 1 - at)) & 1 for at in range(count))


def bit_of(position, bit):
    return lax.rem(position // (1 << bit), 2)


def block_bits(block, m):
    return tuple(bit_of(block, bit) for bit in range(m - 1, -1, -1))


def flipped(position, bit):
    return position + (1 << bit) * (1 - 2 * bit_of(position, bit))


def remote(source, target, sems, at, device):
    return pltpu.make_async_remote_copy(
        src_ref=source,
        dst_ref=target,
        send_sem=sems[0].at[at],
        recv_sem=sems[1].at[at],
        device_id=device,
        device_id_type=pl.DeviceIdType.MESH,
    )


def greet(partners):
    barrier = pltpu.get_barrier_semaphore()
    for partner in partners:
        pl.semaphore_signal(barrier, inc=1, device_id=partner, device_id_type=pl.DeviceIdType.MESH)
    pl.semaphore_wait(barrier, len(partners))


def turn_heads(turned, cosine, sine, heads):
    split = turned.reshape(heads, 2, HEAD_DIMENSION // 2, turned.shape[1])
    first, second = split[:, 0], split[:, 1]
    both = jnp.stack([first * cosine - second * sine, second * cosine + first * sine], axis=1)
    return both.reshape(turned.shape)


def turn_back(turned, cosine, sine, heads):
    return turn_heads(turned, cosine, -sine, heads)


def head_rows(group, member):
    head = group * HEAD_SHARE + member
    return pl.ds(pl.multiple_of(head * HEAD_DIMENSION, HEAD_DIMENSION), HEAD_DIMENSION)


def as_column(row):
    wide = jnp.broadcast_to(row.astype(jnp.float32), (8, row.shape[1]))
    return wide.T[:, 0:1]


def fill_bias(bias, metas, query_segments, level, blk, m, piece):
    key_at = lax.broadcasted_iota(jnp.int32, (piece, piece), 0)
    query_at = lax.broadcasted_iota(jnp.int32, (piece, piece), 1)

    @pl.loop(0, blk + 1)
    def _(block):
        columns = metas[block_bits(block, m)].T
        live = jnp.where(columns[:, 1:2] > level, columns[:, 0:1], -1.0)
        shift = (blk - block) * piece
        allowed = (live == query_segments) & (key_at <= query_at + shift) | (key_at == query_at + shift)
        bias[block] = jnp.where(allowed, 0.0, masked_score).astype(bias.dtype)


def spec(memory):
    return pl.BlockSpec(memory_space=memory)


def shaped(entry):
    return jax.ShapeDtypeStruct(*entry)


def spaces(entries):
    return [pltpu.VMEM(*entry) for entry in entries]


def dma_semaphores(*shapes):
    return [pltpu.SemaphoreType.DMA(shape) for shape in shapes]


class Piece:
    def __init__(self, at, kept_at, slot, flavour, family, sems, bits):
        self.at, self.kept_at, self.slot, self.family, self.sems = at, kept_at, slot, family, sems
        self.m, self.n = bits
        left = list(range(self.m - 1, -1, -1))
        self.order = []
        for stage in range(self.m):
            place = len(left) - 1 if stage == 0 or flavour == 0 else 0
            self.order.append((left.pop(place), place, len(left)))
        self.last = self.m + self.n
        self.blk = lax.axis_index("blk")
        self.dp = lax.axis_index("dp") if self.n else None

    def half(self, ref, side):
        rows, columns = self.family["shape"]
        if self.family["split"] == 0:
            return ref.at[pl.ds(pl.multiple_of(side * (rows // 2), rows // 2), rows // 2), :]
        return ref.at[:, pl.ds(pl.multiple_of(side * (columns // 2), columns // 2), columns // 2)]

    def held(self, stage):
        if stage == 0:
            return self.family["part"], self.slot
        return self.family["blk"][stage - 1], self.kept_at

    def copy(self, stage):
        m, family = self.m, self.family
        if stage < m:
            bit, place, others = self.order[stage]
            ref, index = self.held(stage)
            chosen = [slice(None)] * (others + 1)
            chosen[place] = 1 - bit_of(self.blk, bit)
            source = ref.at[(index, *chosen)]
            target = family["blk"][stage].at[self.kept_at]
            device = {"blk": flipped(self.blk, bit)}
        elif stage < self.last:
            bit = stage - m
            if bit == 0:
                source = self.half(family["blk"][m - 1].at[self.kept_at], 1 - bit_of(self.dp, 0))
            else:
                source = family["dp"][bit - 1].at[self.kept_at]
            target = family["dp"][bit].at[self.kept_at]
            device = {"dp": flipped(self.dp, bit)}
        else:
            source = self.half(family["out"].at[self.kept_at], bit_of(self.dp, 0))
            target = source
            device = {"dp": flipped(self.dp, 0)}
        return remote(source, target, self.sems, (self.at, stage), device)

    def start(self, stage):
        self.copy(stage).start()

    def finish(self, stage):
        m, family = self.m, self.family
        self.copy(stage).wait_recv()
        if stage < m:
            bit, place, others = self.order[stage]
            ref, index = self.held(stage)
            for combo in itertools.product(range(2), repeat=others):
                chosen = list(combo)
                chosen.insert(place, bit_of(self.blk, bit))
                into = family["blk"][stage].at[(self.kept_at, *combo)]
                self.add(into, into, ref.at[(index, *chosen)])
            if stage == 0:
                self.copy(0).wait_send()
        elif stage < self.last:
            bit = stage - m
            got = family["dp"][bit].at[self.kept_at]
            if bit == 0:
                own = self.half(family["blk"][m - 1].at[self.kept_at], bit_of(self.dp, 0))
            else:
                own = family["dp"][bit - 1].at[self.kept_at]
            into = got
            if stage == self.last - 1:
                into = self.half(family["out"].at[self.kept_at], bit_of(self.dp, 0))
            self.add(into, got, own)

    def add(self, into, left, right):
        into[...] = left[...] + right[...]

    def drained(self, stages):
        for stage in stages:
            self.copy(stage).wait_send()


def forward_kernel(
    sizes,
    tokens, segments, depths, cosines, sines, norm_attn, norm_ffn, router,
    w_query_hbm, key_weight_hbm, value_weight_hbm, w_out_hbm, w_gate_hbm, w_up_hbm, w_down_hbm,
    hidden_out, hid_out, normed_out, turned_out, kv_out, lse_out, att_out, middle_out, nffn_out, gate_out, up_out,
    inner_out, branch_out, metas_out,
    w_query, key_weight, value_weight, w_out, w_gate, w_up, w_down,
    hid, normed, turned, kv, lse, att, middle, nffn, gate, up, inner, branch, metas,
    flat, mixture, bias, query_pad, top, total,
    load_sems, save_sems, kv_send, kv_recv, meta_send, meta_recv,
):
    m, piece = sizes
    blk = lax.axis_index("blk")
    mine = block_bits(blk, m)
    weights = (
        (key_weight_hbm, key_weight), (value_weight_hbm, value_weight), (w_query_hbm, w_query), (w_out_hbm, w_out),
        (w_gate_hbm, w_gate), (w_up_hbm, w_up), (w_down_hbm, w_down),
    )
    loads = [pltpu.make_async_copy(*pair, load_sems.at[at]) for at, pair in enumerate(weights)]
    for load in loads:
        load.start()
    saved = (
        (normed, normed_out), (turned, turned_out), (kv, kv_out), (lse, lse_out), (att, att_out),
        (middle, middle_out), (nffn, nffn_out), (gate, gate_out), (up, up_out), (inner, inner_out),
        (branch, branch_out),
    )

    def save(at, level):
        return pltpu.make_async_copy(saved[at][0].at[level], saved[at][1].at[level], save_sems.at[at, level])

    segment_row = segments[...].astype(jnp.float32)
    depth_column = as_column(depths[...])
    metas[mine] = jnp.concatenate(
        [segment_row, depths[...].astype(jnp.float32), jnp.zeros((6, piece), jnp.float32)], axis=0
    )
    greet([{"blk": flipped(blk, bit)} for bit in range(m)])

    def place(known):
        return tuple(slice(None) if bit in known else mine[m - 1 - bit] for bit in range(m - 1, -1, -1))

    orders = (list(range(1, m)), list(range(m - 1, 0, -1)))

    def kv_copies(level, group, stage):
        if stage == m - 1:
            ref = kv.at[(level, group, *place(range(1, m)))]
            return [remote(ref, ref, (kv_send, kv_recv), (level, group, 2 * stage), {"blk": flipped(blk, 0)})]
        copies = []
        for side, order in enumerate(orders):
            rows = pl.ds(side * (piece // 2), piece // 2)
            ref = kv.at[(level, group, *place(order[:stage]), rows)]
            copies.append(remote(ref, ref, (kv_send, kv_recv), (level, group, 2 * stage + side),
                                 {"blk": flipped(blk, order[stage])}))
        return copies

    def kv_advance(level, group, stage):
        if stage > 0:
            for copy in kv_copies(level, group, stage - 1):
                copy.wait_recv()
        if stage < m:
            for copy in kv_copies(level, group, stage):
                copy.start()

    def meta_copy(stage):
        bits = list(range(1, m)) + [0]
        ref = metas.at[place(bits[:stage])]
        return remote(ref, ref, (meta_send, meta_recv), stage, {"blk": flipped(blk, bits[stage])})

    meta_copy(0).start()
    cosine, sine = cosines[...], sines[...]
    gain_attn, gain_ffn = norm_attn[...].astype(jnp.float32), norm_ffn[...].astype(jnp.float32)
    routers = router[...].astype(jnp.float32)
    hid[0] = tokens[...].T.astype(jnp.float32)
    query_pad[HEAD_DIMENSION:, :] = jnp.zeros_like(query_pad[HEAD_DIMENSION:, :])

    @pl.loop(0, RECUR)
    def _(level):
        hidden = hid[level]
        flat[...] = (hidden * rms_scale(hidden) * gain_attn).astype(low)

        @pl.when(level == 0)
        def _():
            for load in loads[:2]:
                load.wait()

        keys = turn_heads(dot_last(key_weight[...], flat[...]), cosine, sine, KEY_VALUE_HEADS)
        values = dot_last(value_weight[...], flat[...])
        for group in range(KEY_VALUE_HEADS):
            here = slice(group * HEAD_DIMENSION, (group + 1) * HEAD_DIMENSION)
            both = jnp.concatenate([keys[here], values[here]], axis=0)
            kv[(level, group, *mine)] = both.T.astype(low)
            kv_advance(level, group, 0)

        @pl.when(level == 0)
        def _():
            loads[2].wait()
            for stage in range(1, m - 1):
                meta_copy(stage - 1).wait_recv()
                meta_copy(stage).start()

        queries = turn_heads(plain_dot(flat[...], w_query[...]).T, cosine, sine, QUERY_HEADS)
        turned[level] = (queries * HEAD_DIMENSION ** (-0.5)).astype(low)
        normed[level] = flat[...].T

        @pl.when(level == 0)
        def _():
            for stage in range(max(1, m - 1), m):
                meta_copy(stage - 1).wait_recv()
                meta_copy(stage).start()

        for stage in range(1, m):
            for group in range(m - stage):
                kv_advance(level, group, stage)

        @pl.when(level == 0)
        def _():
            meta_copy(m - 1).wait_recv()

        fill_bias(bias, metas, segment_row, level.astype(jnp.float32), blk, m, piece)

        @pl.loop(0, KEY_VALUE_HEADS)
        def _(group):
            for stage in range(1, m):
                @pl.when(group + m - stage < KEY_VALUE_HEADS)
                def _():
                    kv_advance(level, group + m - stage, stage)

            kv_advance(level, group, m)
            for member in range(HEAD_SHARE):
                query_pad[:HEAD_DIMENSION, member * piece:(member + 1) * piece] = turned[level, head_rows(group, member), :]
            top[...] = jnp.full_like(top, masked_score)
            total[...] = jnp.zeros_like(total)

            @pl.loop(0, blk + 1)
            def _(step):
                block = blk - step
                rows = kv[(level, group, *block_bits(block, m))]
                here = bias[block]
                scores = plain_dot(rows, query_pad[...]) + jnp.concatenate([here] * HEAD_SHARE, axis=1)
                before = top[0:1, :]
                after = jnp.maximum(before, jnp.max(scores, axis=0, keepdims=True))
                raised = jnp.exp(scores - after)
                shrink = jnp.exp(before - after)
                top[0:1, :] = after
                ones = jnp.ones((16, piece), low)
                left = jnp.concatenate([rows.T[HEAD_DIMENSION:], ones], axis=0)
                total[...] = total[...] * shrink + plain_dot(left, raised.astype(low))

            sums = total[HEAD_DIMENSION:HEAD_DIMENSION + 1, :]
            lse[level, pl.ds(group, 1), :] = top[0:1, :] + jnp.log(sums)
            out = total[:HEAD_DIMENSION, :] / sums
            for member in range(HEAD_SHARE):
                att[level, head_rows(group, member), :] = out[:, member * piece:(member + 1) * piece].astype(low)

        for at in range(5):
            save(at, level).start()

        @pl.when(level == 0)
        def _():
            loads[3].wait()

        attn = plain_dot(att[level].T, w_out[...])
        mid = hid[level] + attn
        middle[level] = mid
        branch[level] = attn
        save(5, level).start()
        flat[...] = (mid * rms_scale(mid) * gain_ffn).astype(low)
        nffn[level] = flat[...].T
        save(6, level).start()

        @pl.when(level == 0)
        def _():
            loads[4].wait()
            loads[5].wait()

        @pl.loop(0, w_gate.shape[1] // FF_TILE)
        def _(tile):
            columns = pl.ds(pl.multiple_of(tile * FF_TILE, FF_TILE), FF_TILE)
            gate_pre = plain_dot(flat[...], w_gate[:, columns])
            up_pre = plain_dot(flat[...], w_up[:, columns])
            gate[level, :, columns] = gate_pre.astype(low)
            up[level, :, columns] = up_pre.astype(low)
            mixed = (gate_pre * jax.nn.sigmoid(gate_pre) * up_pre).astype(low)
            mixture[:, columns] = mixed
            inner[level, columns, :] = mixed.T

        for at in range(7, 10):
            save(at, level).start()

        @pl.when(level == 0)
        def _():
            loads[6].wait()

        branch[level] += dot_last(mixture[...], w_down[...])
        save(10, level).start()
        column = jnp.where(level == 0, routers[0:1, :], routers[1:2, :])
        logit = jnp.sum(hid[level] * column, axis=1, keepdims=True)
        weight = jnp.where(depth_column > level.astype(jnp.float32), jax.nn.sigmoid(logit), 0.0)
        hid[level + 1] = hid[level] + weight * branch[level]

    hidden_out[...] = hid[RECUR].T
    last = [
        pltpu.make_async_copy(hid.at[pl.ds(0, RECUR)], hid_out, save_sems.at[len(saved), 0]),
        pltpu.make_async_copy(metas, metas_out, save_sems.at[len(saved), 1]),
    ]
    for copy in last:
        copy.start()
    for stage in range(m):
        meta_copy(stage).wait_send()
    for level in range(RECUR):
        for group in range(KEY_VALUE_HEADS):
            for stage in range(m):
                for copy in kv_copies(level, group, stage):
                    copy.wait_send()
        for at in range(len(saved)):
            save(at, level).wait()
    for copy in last:
        copy.wait()


def forward(small, weights, nb):
    m = nb.bit_length() - 1
    width, piece = small[0].shape
    hidden_units = weights[4].shape[1]
    blocks, wide = (2,) * m, HEAD_SHARE * piece
    saved = {
        "hid": ((RECUR, piece, width), jnp.float32),
        "normed": ((RECUR, width, piece), low),
        "turned": ((RECUR, width, piece), low),
        "kv": ((RECUR, KEY_VALUE_HEADS, *blocks, piece, PAIR), low),
        "lse": ((RECUR, 8, wide), jnp.float32),
        "att": ((RECUR, width, piece), low),
        "middle": ((RECUR, piece, width), jnp.float32),
        "nffn": ((RECUR, width, piece), low),
        "gate": ((RECUR, piece, hidden_units), low),
        "up": ((RECUR, piece, hidden_units), low),
        "inner": ((RECUR, hidden_units, piece), low),
        "branch": ((RECUR, piece, width), jnp.float32),
        "metas": ((*blocks, 8, piece), jnp.float32),
    }
    scratch = [pltpu.VMEM(array.shape, array.dtype) for array in weights]
    scratch += spaces([((RECUR + 1, piece, width), jnp.float32)] + list(saved.values())[1:])
    scratch += spaces([
        ((piece, width), low),
        ((piece, hidden_units), low),
        ((nb, piece, piece), jnp.float32),
        ((PAIR, wide), low),
        ((8, wide), jnp.float32),
        ((HEAD_DIMENSION + 16, wide), jnp.float32),
    ])
    scratch += dma_semaphores(
        (7,), (len(saved) - 1, RECUR), (RECUR, KEY_VALUE_HEADS, 2 * m), (RECUR, KEY_VALUE_HEADS, 2 * m), (m,), (m,)
    )
    outs = pl.pallas_call(
        functools.partial(forward_kernel, (m, piece)),
        out_shape=[jax.ShapeDtypeStruct((width, piece), jnp.float32)] + [shaped(entry) for entry in saved.values()],
        in_specs=[spec(pltpu.VMEM)] * len(small) + [spec(pl.ANY)] * len(weights),
        out_specs=[spec(pltpu.VMEM)] + [spec(pl.ANY)] * len(saved),
        scratch_shapes=scratch,
        compiler_params=pltpu.CompilerParams(
            collective_id=1, has_side_effects=True, vmem_limit_bytes=VMEM_LIMIT
        ),
        cost_estimate=pl.CostEstimate(
            flops=2 * RECUR * piece * width * 10240, bytes_accessed=48 * 1024 * 1024, transcendentals=0
        ),
        name="forward_levels",
    )(*small, *weights)
    return outs[0], dict(zip(saved, outs[1:]))


def ffn_backward_kernel(
    sizes,
    grad_in, depths, norm_ffn, router,
    w_down_hbm, w_gate_hbm, w_up_hbm, gate_hbm, up_hbm, hid_hbm, branch_hbm, middle_hbm, w_out_hbm,
    grad_out, small_out, dffn_out, dat_out, far_out, dgate_out, dup_out,
    w_down, w_gate, w_up, gate, up, hid, branch, middle, w_out,
    dnorm, dbranch, dgate, dup,
    load_sems, tile_sems, save_sems,
):
    level, tiles = sizes

    def tile_loads(tile):
        columns = pl.ds(pl.multiple_of(tile * FF_TILE, FF_TILE), FF_TILE)
        pairs = (
            (w_down_hbm, w_down), (gate_hbm.at[level], gate), (up_hbm.at[level], up), (w_gate_hbm, w_gate),
            (w_up_hbm, w_up),
        )
        return [
            pltpu.make_async_copy(source.at[:, columns], target.at[:, columns], tile_sems.at[tile, at])
            for at, (source, target) in enumerate(pairs)
        ]

    loads = [
        pltpu.make_async_copy(source, target, load_sems.at[at])
        for at, (source, target) in enumerate((
            (hid_hbm.at[level], hid), (branch_hbm.at[level], branch), (middle_hbm.at[level], middle), (w_out_hbm, w_out),
        ))
    ]
    loads[0].start()
    loads[1].start()
    for tile in range(tiles):
        for load in tile_loads(tile):
            load.start()
    loads[2].start()
    loads[3].start()

    def saves(tile):
        columns = pl.ds(pl.multiple_of(tile * FF_TILE, FF_TILE), FF_TILE)
        return [
            pltpu.make_async_copy(source.at[:, columns], target.at[:, columns], save_sems.at[tile, at])
            for at, (source, target) in enumerate(((dgate, dgate_out), (dup, dup_out)))
        ]

    small_out[...] = jnp.zeros_like(small_out)
    column = router[level:level + 1, :].astype(jnp.float32)
    active = as_column(depths[...]) > float(level)
    gradient = grad_in[...].T.astype(jnp.float32) if level == RECUR - 1 else grad_in[...]
    loads[0].wait()
    loads[1].wait()
    chosen = jax.nn.sigmoid(jnp.sum(hid[...] * column, axis=1, keepdims=True))
    dbranch[...] = jnp.where(active, chosen, 0.0) * gradient
    dchosen = jnp.where(active, jnp.sum(gradient * branch[...], axis=1, keepdims=True), 0.0)
    dlogit = dchosen * chosen * (1.0 - chosen)
    small_out[2 + level:3 + level, :] = jnp.sum(hid[...] * dlogit, axis=0, keepdims=True)
    grad_out[...] = gradient + dlogit * column
    dffn_out[...] = dbranch[...].astype(low)
    dnorm[...] = jnp.zeros_like(dnorm)

    @pl.loop(0, tiles)
    def _(tile):
        columns = pl.ds(pl.multiple_of(tile * FF_TILE, FF_TILE), FF_TILE)
        for load in tile_loads(tile):
            load.wait()
        dinner = plain_dot(dffn_out[...], w_down[:, columns])
        gate_pre, up_pre = gate[:, columns].astype(jnp.float32), up[:, columns].astype(jnp.float32)
        opened = jax.nn.sigmoid(gate_pre)
        dgate_tile = (dinner * up_pre * opened * (1.0 + gate_pre * (1.0 - opened))).astype(low)
        dup_tile = (dinner * gate_pre * opened).astype(low)
        dgate[:, columns] = dgate_tile
        dup[:, columns] = dup_tile
        for save in saves(tile):
            save.start()
        dnorm[...] += dot_last(dgate_tile, w_gate[:, columns]) + dot_last(dup_tile, w_up[:, columns])

    loads[2].wait()
    loads[3].wait()
    dmiddle, gain_share = norm_gradient(dnorm[...], middle[...], norm_ffn[...].astype(jnp.float32))
    small_out[1:2, :] = gain_share
    grad_out[...] += dmiddle
    dattn = (dbranch[...] + dmiddle).astype(low)
    lead = far_out.shape[1] - dattn.shape[1]
    far_out[:, :lead] = jnp.zeros((dattn.shape[0], lead), low)
    far_out[:, lead:] = dattn
    dat_out[...] = dot_last(w_out[...], dattn).astype(low)
    for tile in range(tiles):
        for save in saves(tile):
            save.wait()


def ffn_backward(level, grad_in, depths, norm_ffn, router, saved, weights):
    _, _, _, w_out, w_gate, w_up, w_down = weights
    width, hidden_units = w_gate.shape
    piece = depths.shape[1]
    tiles = hidden_units // FF_TILE
    operands = (
        w_down, w_gate, w_up, saved["gate"], saved["up"], saved["hid"], saved["branch"], saved["middle"], w_out,
    )
    rows, hidden = ((piece, width), jnp.float32), ((piece, hidden_units), low)
    outs = [
        rows, ((8, width), jnp.float32), ((piece, width), low), ((width, piece), low),
        ((piece, 2 * width + 2 * KEYS_WIDTH - 1536), low), hidden, hidden,
    ]
    scratch = spaces([(array.shape if at in (0, 1, 2, 8) else array.shape[1:], array.dtype) for at, array in enumerate(operands)])
    scratch += spaces([rows, rows, hidden, hidden])
    scratch += dma_semaphores((4,), (tiles, 5), (tiles, 2))
    return pl.pallas_call(
        functools.partial(ffn_backward_kernel, (level, tiles)),
        out_shape=[shaped(entry) for entry in outs],
        in_specs=[spec(pltpu.VMEM)] * 4 + [spec(pl.ANY)] * len(operands),
        out_specs=[spec(pltpu.VMEM)] * 5 + [spec(pl.ANY)] * 2,
        scratch_shapes=scratch,
        compiler_params=pltpu.CompilerParams(vmem_limit_bytes=VMEM_LIMIT),
        cost_estimate=pl.CostEstimate(
            flops=2 * piece * width * 8640, bytes_accessed=24 * 1024 * 1024, transcendentals=0
        ),
        name="ffn_backward_%d" % level,
    )(grad_in, depths, norm_ffn, router, *operands)


class AttentionBackward:
    def __init__(self, at, m, piece, level):
        self.at, self.m, self.piece, self.level = at, m, piece, level
        self.blk = lax.axis_index("blk")
        self.family = {"part": at.part, "blk": at.halves, "dp": (), "out": None, "shape": (piece // 2, PAIR), "split": 0}

    def pieces(self, group):
        sems = (self.at.kv_send, self.at.kv_recv)
        return [
            Piece(2 * group + side, 2 * group + side, 2 * group + side, side, self.family, sems, (self.m, 0))
            for side in range(2)
        ]

    def move(self, group, stage):
        for piece_of in self.pieces(group):
            piece_of.finish(stage)
            if stage + 1 < self.m:
                piece_of.start(stage + 1)

    def begin(self):
        at = self.at
        query_segments = at.metas[block_bits(self.blk, self.m)][0:1, :]
        fill_bias(at.bias, at.metas, query_segments, float(self.level), self.blk, self.m, self.piece)
        at.query_pad[HEAD_DIMENSION:, :] = jnp.zeros_like(at.query_pad[HEAD_DIMENSION:, :])
        at.dat_pad[:HEAD_DIMENSION, :] = jnp.zeros_like(at.dat_pad[:HEAD_DIMENSION, :])

    def group(self, group):
        at, m, piece, blk = self.at, self.m, self.piece, self.blk
        half = piece // 2
        carried = []
        for member in range(HEAD_SHARE):
            rows, lanes = head_rows(group, member), slice(member * piece, (member + 1) * piece)
            at.query_pad[:HEAD_DIMENSION, lanes] = at.turned[rows, :]
            at.dat_pad[HEAD_DIMENSION:, lanes] = at.dat_turned[rows, :]
            product = at.dat_turned[rows, :].astype(jnp.float32) * at.att_turned[rows, :].astype(jnp.float32)
            carried.append(jnp.sum(product, axis=0, keepdims=True))
        carried = jnp.concatenate(carried, axis=1)
        at.query_rows[...] = at.query_pad[...].T
        at.dat_rows[...] = at.dat_pad[...].T
        log_total = at.lse[pl.ds(group, 1), :]
        at.dq_sum[...] = jnp.zeros_like(at.dq_sum)

        @pl.loop(0, blk + 1)
        def _(block):
            rows = at.kv[(group, *block_bits(block, m))]
            here = jnp.concatenate([at.bias[block].astype(jnp.float32)] * HEAD_SHARE, axis=1)
            probability = jnp.exp(plain_dot(rows, at.query_pad[...]) + here - log_total)
            dprob = plain_dot(rows, at.dat_pad[...])
            dscores = (probability * (dprob - carried)).astype(low)
            share = plain_dot(dscores, at.query_rows[...]) + plain_dot(probability.astype(low), at.dat_rows[...])
            share = share.astype(low)
            for side in range(2):
                at.part[(2 * group + side, *block_bits(block, m))] = share[side * half:(side + 1) * half]
            at.dq_sum[...] += plain_dot(rows.T[:HEAD_DIMENSION], dscores)

        @pl.loop(blk + 1, 1 << m)
        def _(block):
            for side in range(2):
                at.part[(2 * group + side, *block_bits(block, m))] = jnp.zeros((half, PAIR), low)

        for piece_of in self.pieces(group):
            piece_of.start(0)
        for member in range(HEAD_SHARE):
            at.dq_turned[head_rows(group, member), :] = at.dq_sum[:, member * piece:(member + 1) * piece]

    def follow(self, group):
        for stage in range(self.m - 1):
            earlier = group - 1 - stage
            if isinstance(group, int):
                if 0 <= earlier < KEY_VALUE_HEADS:
                    self.move(earlier, stage)
            else:
                @pl.when(earlier >= 0)
                def _():
                    self.move(earlier, stage)

    def queries(self, cosine, sine, w_query, dnorm):
        dqueries = turn_back(self.at.dq_turned[...] * HEAD_DIMENSION ** (-0.5), cosine, sine, QUERY_HEADS)
        dqueries = dqueries.T.astype(low)
        self.put(2 * KEYS_WIDTH, dqueries)
        dnorm[...] = dot_last(dqueries, w_query[...])

    def put(self, column, values):
        self.at.near[self.at.near_rows, column:column + values.shape[1]] = values

    def keys(self, cosine, sine, key_weight, value_weight, dnorm):
        at, m = self.at, self.m
        filled = 2 * KEYS_WIDTH + QUERY_HEADS * HEAD_DIMENSION
        self.put(filled, jnp.zeros((self.piece, at.near_width - filled), low))
        dkeys, dvalues = [], []
        for group in range(KEY_VALUE_HEADS):
            self.move(group, m - 1)
            both = jnp.concatenate([at.halves[m - 1][2 * group], at.halves[m - 1][2 * group + 1]], axis=0)
            both = both.astype(jnp.float32).T
            dkeys.append(both[:HEAD_DIMENSION])
            dvalues.append(both[HEAD_DIMENSION:])
        dkeys = turn_back(jnp.concatenate(dkeys, axis=0), cosine, sine, KEY_VALUE_HEADS).T.astype(low)
        dvalues = jnp.concatenate(dvalues, axis=0).T.astype(low)
        self.put(0, dkeys)
        self.put(KEYS_WIDTH, dvalues)
        dnorm[...] += plain_dot(dkeys, key_weight[...]) + plain_dot(dvalues, value_weight[...])

    def drained(self):
        for group in range(KEY_VALUE_HEADS):
            for piece_of in self.pieces(group):
                piece_of.drained(range(1, self.m))


def attention_buffers(nb, piece, width, bias_type):
    m, wide, heads = nb.bit_length() - 1, HEAD_SHARE * piece, 2 * KEY_VALUE_HEADS
    buffers = {
        "turned": ((width, piece), low),
        "dat_turned": ((width, piece), low),
        "kv": ((KEY_VALUE_HEADS, *(2,) * m, piece, PAIR), low),
        "lse": ((8, wide), jnp.float32),
        "metas": ((*(2,) * m, 8, piece), jnp.float32),
        "w_query": ((width, width), low),
        "key_weight": ((KEYS_WIDTH, width), low),
        "value_weight": ((KEYS_WIDTH, width), low),
        "dq_turned": ((width, piece), jnp.float32),
        "bias": ((nb, piece, piece), bias_type),
        "query_pad": ((PAIR, wide), low),
        "dat_pad": ((PAIR, wide), low),
        "query_rows": ((wide, PAIR), low),
        "dat_rows": ((wide, PAIR), low),
        "dq_sum": ((HEAD_DIMENSION, wide), jnp.float32),
        "part": ((heads, *(2,) * m, piece // 2, PAIR), low),
        "dnorm": ((piece, width), jnp.float32),
    }
    for stage in range(m):
        buffers["half_%d" % stage] = ((heads, *(2,) * (m - 1 - stage), piece // 2, PAIR), low)
    return buffers


def attention_backward_kernel(sizes, names, *refs):
    m, piece, level = sizes
    at = types.SimpleNamespace(**dict(zip(names, refs)))
    at.halves = [getattr(at, "half_%d" % stage) for stage in range(m)]
    at.near, at.near_rows, at.near_width = at.near_out, slice(None), at.near_out.shape[1]
    blk = lax.axis_index("blk")
    pairs = (
        (at.metas_hbm, at.metas), (at.turned_hbm.at[level], at.turned), (at.dat_hbm, at.dat_turned),
        (at.att_hbm.at[level], at.att_turned), (at.lse_hbm.at[level], at.lse), (at.kv_hbm.at[level], at.kv),
        (at.w_query_hbm, at.w_query), (at.key_weight_hbm, at.key_weight), (at.value_weight_hbm, at.value_weight),
        (at.hid_hbm.at[level], at.hid), (at.grad_hbm, at.grad),
    )
    loads = [pltpu.make_async_copy(*pair, at.load_sems.at[index]) for index, pair in enumerate(pairs)]
    for load in loads:
        load.start()
    greet([{"blk": flipped(blk, bit)} for bit in range(m)])
    work = AttentionBackward(at, m, piece, level)
    loads[0].wait()
    work.begin()
    for load in loads[1:6]:
        load.wait()

    @pl.loop(0, KEY_VALUE_HEADS)
    def _(group):
        work.group(group)
        work.follow(group)

    cosine, sine = at.cosines[...], at.sines[...]
    for virtual in range(KEY_VALUE_HEADS, KEY_VALUE_HEADS + m - 1):
        work.follow(virtual)
        if virtual == KEY_VALUE_HEADS:
            loads[6].wait()
            work.queries(cosine, sine, at.w_query, at.dnorm)
    for load in loads[7:]:
        load.wait()
    work.keys(cosine, sine, at.key_weight, at.value_weight, at.dnorm)
    dhidden, gain_share = norm_gradient(at.dnorm[...], at.hid[...], at.norm_attn[...].astype(jnp.float32))
    at.small_out[...] = jnp.zeros_like(at.small_out)
    at.small_out[0:1, :] = gain_share
    at.grad_out[...] = at.grad[...] + dhidden
    work.drained()


def attention_backward(level, grad, dat_turned, cosines, sines, norm_attn, saved, weights, nb):
    m = nb.bit_length() - 1
    piece, width = grad.shape
    rows = ((piece, width), jnp.float32)
    inputs = {"cosines": cosines, "sines": sines, "norm_attn": norm_attn}
    operands = {
        "metas_hbm": saved["metas"], "turned_hbm": saved["turned"], "dat_hbm": dat_turned, "att_hbm": saved["att"],
        "lse_hbm": saved["lse"], "kv_hbm": saved["kv"], "w_query_hbm": weights[0], "key_weight_hbm": weights[1],
        "value_weight_hbm": weights[2], "hid_hbm": saved["hid"], "grad_hbm": grad,
    }
    outs = {"grad_out": rows, "small_out": ((8, width), jnp.float32), "near_out": ((piece, 1792), low)}
    buffers = attention_buffers(nb, piece, width, jnp.float32)
    buffers.update({"att_turned": ((width, piece), low), "hid": rows, "grad": rows})
    semaphores = {"load_sems": (len(operands),), "kv_send": (2 * KEY_VALUE_HEADS, m), "kv_recv": (2 * KEY_VALUE_HEADS, m)}
    return pl.pallas_call(
        functools.partial(
            attention_backward_kernel, (m, piece, level), (*inputs, *operands, *outs, *buffers, *semaphores)
        ),
        out_shape=[shaped(entry) for entry in outs.values()],
        in_specs=[spec(pltpu.VMEM)] * len(inputs) + [spec(pl.ANY)] * len(operands),
        out_specs=[spec(pltpu.VMEM)] * len(outs),
        scratch_shapes=spaces(buffers.values()) + dma_semaphores(*semaphores.values()),
        compiler_params=pltpu.CompilerParams(
            collective_id=2, has_side_effects=True, vmem_limit_bytes=VMEM_LIMIT
        ),
        cost_estimate=pl.CostEstimate(
            flops=2 * piece * width * 12000, bytes_accessed=16 * 1024 * 1024, transcendentals=0
        ),
        name="attention_backward_%d" % level,
    )(*inputs.values(), *operands.values())


WIDE_SLOTS, DOWN_SLOTS = 4, 2


def final_kernel(sizes, names, *refs):
    nb, m, n, piece, rows, padded, near_width = sizes
    at = types.SimpleNamespace(**dict(zip(names, refs)))
    at.halves = [getattr(at, "half_%d" % stage) for stage in range(m)]
    blk, dp = lax.axis_index("blk"), lax.axis_index("dp")
    at.near, at.near_rows, at.near_width = at.gate_side, slice(0, piece), near_width
    counter = itertools.count()

    def load(source, target):
        return pltpu.make_async_copy(source, target, at.load_sems.at[next(counter)])

    def both_lanes(ref, target):
        return [load(ref.at[level], target.at[:, pl.ds(level * piece, piece)]) for level in range(RECUR)]

    def both_rows(low_ref, deep_ref, target, width):
        pairs = ((low_ref, 0), (deep_ref, piece))
        return [load(ref, target.at[pl.ds(first, piece), pl.ds(0, width)]) for ref, first in pairs]

    hidden_units, width = at.gate_side.shape[1], at.dffn.shape[1]
    far_width = at.far_0_hbm.shape[1]
    loads = {
        "nffn": both_lanes(at.nffn_hbm, at.left),
        "dgate": both_rows(at.dgate_0_hbm, at.dgate_1_hbm, at.gate_side, hidden_units),
        "inner": both_lanes(at.inner_hbm, at.inner),
        "dffn": both_rows(at.dffn_0_hbm, at.dffn_1_hbm, at.dffn, width),
        "metas": [load(at.metas_hbm, at.metas)],
        "heads": [
            load(at.turned_hbm.at[0], at.turned), load(at.dat_hbm, at.dat_turned), load(at.att_hbm.at[0], at.att_turned),
            load(at.lse_hbm.at[0], at.lse), load(at.kv_hbm.at[0], at.kv),
        ],
        "dup": both_rows(at.dup_0_hbm, at.dup_1_hbm, at.up_side, hidden_units),
        "w_query": [load(at.w_query_hbm, at.w_query)],
        "rest": [
            load(at.key_weight_hbm, at.key_weight), load(at.value_weight_hbm, at.value_weight),
            load(at.hid_hbm.at[0], at.hid), load(at.grad_hbm, at.grad),
        ],
        "attended": both_lanes(at.attended_hbm, at.left_attended),
    }
    late = {
        "near": [load(at.near_1_hbm, at.gate_side.at[pl.ds(piece, piece), pl.ds(0, near_width)])],
        "far": both_rows(at.far_0_hbm, at.far_1_hbm, at.up_side, far_width),
        "normed": both_lanes(at.normed_hbm, at.left),
    }

    def begin(copies):
        for copy in copies:
            copy.start()

    def ready(copies):
        for copy in copies:
            copy.wait()

    for copies in loads.values():
        begin(copies)
    greet([{"blk": flipped(blk, bit)} for bit in range(m)] + [{"dp": flipped(dp, bit)} for bit in range(n)])

    down_rows = at.part_down.shape[-2]

    def family(name, shape, split):
        return {
            "part": getattr(at, "part_" + name), "out": getattr(at, "out_" + name), "shape": shape, "split": split,
            "blk": [getattr(at, "blk_%s_%d" % (name, stage)) for stage in range(m)],
            "dp": [getattr(at, "dp_%s_%d" % (name, stage)) for stage in range(n)],
        }

    wide = family("wide", (2 * padded, UNIT_COLUMNS), 1)
    down = family("down", (down_rows, width), 0)
    little = family("small", (16, 128), 0)
    sems = (at.send_sems, at.recv_sems)
    units = itertools.count()

    def unit(kind, index, flavour):
        slots = {"wide": WIDE_SLOTS, "down": DOWN_SLOTS, "small": 1}[kind]
        holder = {"wide": wide, "down": down, "small": little}[kind]
        piece_of = Piece(next(units), index, index % slots, flavour, holder, sems, (m, n))
        piece_of.kind = kind
        return piece_of

    pairs = [[unit("wide", index, 0), unit("down", index, 1)] for index in range(5)]
    pairs += [[unit("wide", index, 0), unit("wide", index + 1, 1)] for index in (5, 7, 9, 11)]
    pairs += [[unit("wide", 13, 0), unit("wide", 14, 1), unit("small", 0, 0)]]

    def compute_wide(index, slot):
        if index == 0:
            ready(loads["nffn"])
            ready(loads["dgate"])
        if index == 5:
            begin(late["near"])
            ready(loads["dup"])
        if index == 10:
            begin(late["far"])
            begin(late["normed"])
            ready(late["near"])
            ready(late["normed"])
            ready(loads["attended"])
            ready(late["far"])
        block, column = index // 5, (index % 5) * UNIT_COLUMNS
        second = 1280 + column
        upper_columns, lower_columns = slice(column, column + UNIT_COLUMNS), slice(second, second + UNIT_COLUMNS)
        if block < 2:
            right = at.gate_side if block == 0 else at.up_side
            upper = plain_dot(at.left[...], right[:, upper_columns])
            lower = plain_dot(at.left[...], right[:, lower_columns])
        else:
            upper = plain_dot(at.left[...], at.gate_side[:, upper_columns])
            lower = None
            if second < 1600:
                lower = plain_dot(at.left[...], at.gate_side[:, lower_columns])
            if second >= 1536:
                more = plain_dot(at.left_attended[...], at.up_side[:, second - 1536:second - 1536 + UNIT_COLUMNS])
                lower = more if lower is None else lower + more
        for target in range(nb):
            here = slice(target * padded, (target + 1) * padded)
            both = jnp.concatenate([upper[here], lower[here]], axis=0)
            at.part_wide[(slot, *bits_of(target, m))] = both.astype(low)

    def compute_down(index, slot):
        if index == 0:
            ready(loads["inner"])
            ready(loads["dffn"])
        firsts = [(target * 5 + index) * down_rows for target in range(nb)]
        left = jnp.concatenate([at.inner[first:first + down_rows, :] for first in firsts], axis=0)
        result = plain_dot(left, at.dffn[...])
        for target in range(nb):
            at.part_down[(slot, *bits_of(target, m))] = result[target * down_rows:(target + 1) * down_rows].astype(low)

    def compute_small():
        total = at.small_ffn_1[...] + at.small_ffn_0[...] + at.small_att_1[...]
        total = total + jnp.concatenate([at.gain_row[...], jnp.zeros((7, width), jnp.float32)], axis=0)
        at.part_small[...] = jnp.zeros_like(at.part_small)
        for target in range(nb):
            at.part_small[(0, *bits_of(target, m), slice(0, 8), slice(0, rows))] = total[:, target * rows:(target + 1) * rows]

    def compute(piece_of):
        if piece_of.kind == "wide":
            compute_wide(piece_of.kept_at, piece_of.slot)
        elif piece_of.kind == "down":
            compute_down(piece_of.kept_at, piece_of.slot)
        else:
            compute_small()
        piece_of.start(0)

    def moves(tick):
        for stage in range(m + n - 1, -1, -1):
            if 0 <= tick - stage < len(pairs):
                for piece_of in pairs[tick - stage]:
                    piece_of.finish(stage)
                    piece_of.start(stage + 1)

    work = AttentionBackward(at, m, piece, 0)
    for pair in pairs[:2]:
        for piece_of in pair:
            compute(piece_of)
    ready(loads["metas"])
    work.begin()
    ready(loads["heads"])
    for group in range(KEY_VALUE_HEADS):
        moves(group)
        for piece_of in pairs[group + 2]:
            compute(piece_of)
        work.group(group)
        work.follow(group)
    cosine, sine = at.cosines[...], at.sines[...]
    moves(5)
    compute(pairs[7][0])
    ready(loads["w_query"])
    for virtual in range(KEY_VALUE_HEADS, KEY_VALUE_HEADS + m - 1):
        work.follow(virtual)
        if virtual == KEY_VALUE_HEADS:
            work.queries(cosine, sine, at.w_query, at.dnorm)
    moves(6)
    ready(loads["rest"])
    work.keys(cosine, sine, at.key_weight, at.value_weight, at.dnorm)
    compute(pairs[7][1])
    moves(7)
    for piece_of in pairs[8] + pairs[9][:2]:
        compute(piece_of)
    dhidden, gain_share = norm_gradient(at.dnorm[...], at.hid[...], at.norm_attn[...].astype(jnp.float32))
    at.gain_row[...] = gain_share
    at.grad_out[...] = (at.grad[...] + dhidden).T
    compute(pairs[9][2])
    for tick in range(8, len(pairs) + m + n - 1):
        moves(tick)
    for pair in pairs:
        for piece_of in pair:
            piece_of.finish(m + n)
    for pair in pairs:
        for piece_of in pair:
            piece_of.drained(range(1, m + n + 1))
    work.drained()


def unpack_kernel(sizes, wide_hbm, down_hbm, little_hbm, hidden_in, gradient_in, *refs):
    rows, padded = sizes
    norm_attn, norm_ffn, query, key, value, out, gate, up, down_out, router, hidden, gradient = refs[:12]
    wide, down, little, rest, sems = refs[12:]
    carried = [
        pltpu.make_async_copy(source, target, sems.at[at])
        for at, (source, target) in enumerate(((hidden_in, hidden), (gradient_in, gradient)))
    ]
    loads = [
        pltpu.make_async_copy(source, target, sems.at[2 + at])
        for at, (source, target) in enumerate(((wide_hbm, wide), (down_hbm, down), (little_hbm, little)))
    ]
    for copy in loads + carried:
        copy.start()
    for load in loads:
        load.wait()
    norm_attn[...] = little[0, 0:1, :rows]
    norm_ffn[...] = little[0, 1:2, :rows]
    router[...] = little[0, 2:4, :rows]
    for unit in range(5):
        for first, target in ((0, gate), (5, up), (10, rest)):
            tile = wide[first + unit].astype(jnp.float32)
            for side in range(2):
                column = side * 1280 + unit * UNIT_COLUMNS
                target[:, column:column + UNIT_COLUMNS] = tile[side * padded:side * padded + rows]
        down_rows = down.shape[1]
        down_out[unit * down_rows:(unit + 1) * down_rows, :] = down[unit].astype(jnp.float32)
    width = query.shape[1]
    key[...] = rest[:, :KEYS_WIDTH].T
    value[...] = rest[:, KEYS_WIDTH:2 * KEYS_WIDTH].T
    query[...] = rest[:, 2 * KEYS_WIDTH:2 * KEYS_WIDTH + width]
    out[...] = rest[:, 2 * KEYS_WIDTH + width:]
    for copy in carried:
        copy.wait()


def final(tables, norm_attn, saved, feeds, near_1, smalls, weights, hidden, mesh_sizes):
    nb, nd = mesh_sizes
    m, n = nb.bit_length() - 1, nd.bit_length() - 1
    (grad, _, dffn_0, dat_0, far_0, dgate_0, dup_0), (_, _, dffn_1, _, far_1, dgate_1, dup_1) = feeds
    piece, width = grad.shape
    hidden_units = dgate_0.shape[1]
    rows = width // nb
    padded = -(-rows // 8) * 8
    down_rows = hidden_units // nb // 5
    tokens = RECUR * piece

    def spread(array):
        if padded == rows:
            return array
        split = array.reshape(RECUR, nb, rows, piece)
        return jnp.pad(split, ((0, 0), (0, 0), (0, padded - rows), (0, 0))).reshape(RECUR, nb * padded, piece)

    inputs = {
        "cosines": tables[0], "sines": tables[1], "norm_attn": norm_attn, "small_ffn_0": smalls[0],
        "small_ffn_1": smalls[1], "small_att_1": smalls[2],
    }
    operands = {
        "metas_hbm": saved["metas"], "turned_hbm": saved["turned"], "dat_hbm": dat_0, "att_hbm": saved["att"],
        "lse_hbm": saved["lse"], "kv_hbm": saved["kv"], "w_query_hbm": weights[0], "key_weight_hbm": weights[1],
        "value_weight_hbm": weights[2], "hid_hbm": saved["hid"], "grad_hbm": grad,
        "inner_hbm": saved["inner"], "nffn_hbm": spread(saved["nffn"]), "normed_hbm": spread(saved["normed"]),
        "attended_hbm": spread(saved["att"]), "dffn_0_hbm": dffn_0, "dffn_1_hbm": dffn_1, "dgate_0_hbm": dgate_0,
        "dgate_1_hbm": dgate_1, "dup_0_hbm": dup_0, "dup_1_hbm": dup_1, "far_0_hbm": far_0, "far_1_hbm": far_1,
        "near_1_hbm": near_1,
    }
    families = (
        ("wide", 15, (2 * padded, UNIT_COLUMNS), low, WIDE_SLOTS, 1), ("down", 5, (down_rows, width), low, DOWN_SLOTS, 0),
        ("small", 1, (16, 128), jnp.float32, 1, 0),
    )
    outs = {"grad_out": ((width, piece), jnp.float32)}
    buffers = attention_buffers(nb, piece, width, low)
    buffers.update({
        "att_turned": ((width, piece), low), "hid": ((piece, width), jnp.float32), "grad": ((piece, width), jnp.float32),
        "gate_side": ((tokens, hidden_units), low), "up_side": ((tokens, hidden_units), low),
        "inner": ((hidden_units, tokens), low), "left": ((nb * padded, tokens), low),
        "left_attended": ((nb * padded, tokens), low), "dffn": ((tokens, width), low),
        "gain_row": ((1, width), jnp.float32),
    })
    for name, count, shape, dtype, slots, split in families:
        outs["out_" + name] = ((count, *shape), dtype)
        buffers["part_" + name] = ((slots, *(2,) * m, *shape), dtype)
        for stage in range(m):
            buffers["blk_%s_%d" % (name, stage)] = ((count, *(2,) * (m - 1 - stage), *shape), dtype)
        half = (shape[0], shape[1] // 2) if split else (shape[0] // 2, shape[1])
        for stage in range(n):
            buffers["dp_%s_%d" % (name, stage)] = ((count, *half), dtype)
    semaphores = {
        "load_sems": (32,), "kv_send": (2 * KEY_VALUE_HEADS, m), "kv_recv": (2 * KEY_VALUE_HEADS, m),
        "send_sems": (21, m + n + 1), "recv_sems": (21, m + n + 1),
    }
    names = (*inputs, *operands, *outs, *buffers, *semaphores)
    gradient, wide, down, little = pl.pallas_call(
        functools.partial(final_kernel, (nb, m, n, piece, rows, padded, near_1.shape[1]), names),
        out_shape=[shaped(entry) for entry in outs.values()],
        in_specs=[spec(pltpu.VMEM)] * len(inputs) + [spec(pl.ANY)] * len(operands),
        out_specs=[spec(pltpu.VMEM)] * len(outs),
        scratch_shapes=spaces(buffers.values()) + dma_semaphores(*semaphores.values()),
        compiler_params=pltpu.CompilerParams(
            collective_id=0, has_side_effects=True, vmem_limit_bytes=VMEM_LIMIT
        ),
        cost_estimate=pl.CostEstimate(
            flops=2 * tokens * width * 14000, bytes_accessed=30 * 1024 * 1024, transcendentals=0
        ),
        name="weight_grads",
    )(*inputs.values(), *operands.values())
    shapes = (
        (1, rows), (1, rows), (rows, width), (KEYS_WIDTH, rows), (KEYS_WIDTH, rows), (rows, width),
        (rows, hidden_units), (rows, hidden_units), (5 * down_rows, width), (2, rows), (width, piece), (width, piece),
    )
    outs = pl.pallas_call(
        functools.partial(unpack_kernel, (rows, padded)),
        out_shape=[jax.ShapeDtypeStruct(shape, jnp.float32) for shape in shapes],
        in_specs=[spec(pl.ANY)] * 5,
        out_specs=[spec(pltpu.VMEM)] * 10 + [spec(pl.ANY)] * 2,
        scratch_shapes=[pltpu.VMEM(array.shape, array.dtype) for array in (wide, down, little)]
        + spaces([((rows, 2560), jnp.float32)]) + dma_semaphores((5,)),
        compiler_params=pltpu.CompilerParams(vmem_limit_bytes=32 * 1024 * 1024),
        name="unpack",
    )(wide, down, little, hidden, gradient)
    norm_a, norm_f, query, key, value, out, gate, up, down, router, hidden, gradient = outs
    return (
        hidden.T[None], gradient.T[None], norm_a[0], norm_f[0], query, key.T, value.T, out, gate, up, down, router.T,
    )


def local(
    tokens,
    depths,
    segments,
    norm_attn,
    norm_ffn,
    w_query,
    key_weight,
    value_weight,
    w_out,
    w_gate,
    w_up,
    w_down,
    w_router,
    cotangent,
    mesh_sizes,
):
    piece = tokens.shape[1]
    positions = lax.axis_index("blk") * piece + jnp.arange(piece, dtype=jnp.int32)
    angles = frequencies(HEAD_DIMENSION)[:, None] * positions.astype(jnp.float32)[None, :]
    tables = (jnp.cos(angles), jnp.sin(angles))
    norm_attn, norm_ffn, router = norm_attn[None], norm_ffn[None], w_router.T
    weights = (w_query, key_weight.T, value_weight.T, w_out, w_gate, w_up, w_down.T)
    hidden, saved = forward(
        (tokens[0].T, segments, depths, *tables, norm_attn, norm_ffn, router), weights, mesh_sizes[0]
    )
    gradient, feeds, smalls = cotangent[0].T, [], []
    for level in reversed(range(RECUR)):
        feed = ffn_backward(level, gradient, depths, norm_ffn, router, saved, weights)
        feeds.insert(0, feed)
        smalls.insert(0, feed[1])
        if level > 0:
            gradient, small, near = attention_backward(
                level, feed[0], feed[3], *tables, norm_attn, saved, weights, mesh_sizes[0]
            )
            smalls.append(small)
    return final(tables, norm_attn, saved, feeds, near, smalls, weights, hidden, mesh_sizes)


def solution(mesh):
    sizes = (mesh.shape["blk"], mesh.shape["dp"])
    return jax.shard_map(
        functools.partial(local, mesh_sizes=sizes),
        mesh=mesh,
        in_specs=(
            P("dp", "blk", None),
            P("dp", "blk"),
            P("dp", "blk"),
            P(),
            P(),
            P(),
            P(),
            P(),
            P(),
            P(),
            P(),
            P(),
            P(),
            P("dp", "blk", None),
        ),
        out_specs=(
            P("dp", "blk", None),
            P("dp", "blk", None),
            P("blk"),
            P("blk"),
            P("blk", None),
            P("blk", None),
            P("blk", None),
            P("blk", None),
            P("blk", None),
            P("blk", None),
            P("blk", None),
            P("blk", None),
        ),
        check_vma=False,
    )
```

```python
import functools
import itertools
import math
import types

import jax
import jax.numpy as jnp
from jax import lax
from jax.experimental import pallas as pl
from jax.experimental.pallas import tpu as pltpu
from jax.sharding import PartitionSpec as P

QUERY_HEADS = 15
KEY_VALUE_HEADS = 5
HEAD_DIMENSION = 64
RECUR = 2
HEAD_SHARE = QUERY_HEADS // KEY_VALUE_HEADS
KEYS_WIDTH = KEY_VALUE_HEADS * HEAD_DIMENSION
PAIR = 2 * HEAD_DIMENSION
FF_TILE = 512
UNIT_COLUMNS = 256
VMEM_LIMIT = 63 * 1024 * 1024

epsilon = 1e-05
masked_score = -1e30
low = jnp.bfloat16


def frequencies(head_size):
    return jnp.exp(
        jnp.arange(head_size // 2, dtype=jnp.float32) * (-2.0 * math.log(10000.0) / head_size)
    )


def rms_scale(values):
    return lax.rsqrt(jnp.mean(values * values, axis=-1, keepdims=True) + epsilon)


def norm_gradient(grad_norm, values, gain):
    scale = rms_scale(values)
    weighted = grad_norm * gain
    grad_values = scale * weighted - values * (scale * scale * scale) * jnp.mean(
        weighted * values, axis=-1, keepdims=True
    )
    return grad_values, jnp.sum(grad_norm * values * scale, axis=0, keepdims=True)


def dot_last(left, right):
    return lax.dot_general(left, right, (((1,), (1,)), ((), ())), preferred_element_type=jnp.float32)


def plain_dot(left, right):
    return jnp.dot(left, right, preferred_element_type=jnp.float32)


def bits_of(number, count):
    return tuple((number >> (count - 1 - at)) & 1 for at in range(count))


def bit_of(position, bit):
    return lax.rem(position // (1 << bit), 2)


def block_bits(block, m):
    return tuple(bit_of(block, bit) for bit in range(m - 1, -1, -1))


def flipped(position, bit):
    return position + (1 << bit) * (1 - 2 * bit_of(position, bit))


def remote(source, target, sems, at, device):
    return pltpu.make_async_remote_copy(
        src_ref=source,
        dst_ref=target,
        send_sem=sems[0].at[at],
        recv_sem=sems[1].at[at],
        device_id=device,
        device_id_type=pl.DeviceIdType.MESH,
    )


def greet(partners):
    barrier = pltpu.get_barrier_semaphore()
    for partner in partners:
        pl.semaphore_signal(barrier, inc=1, device_id=partner, device_id_type=pl.DeviceIdType.MESH)
    pl.semaphore_wait(barrier, len(partners))


def turn_heads(turned, cosine, sine, heads):
    split = turned.reshape(heads, 2, HEAD_DIMENSION // 2, turned.shape[1])
    first, second = split[:, 0], split[:, 1]
    both = jnp.stack([first * cosine - second * sine, second * cosine + first * sine], axis=1)
    return both.reshape(turned.shape)


def turn_back(turned, cosine, sine, heads):
    return turn_heads(turned, cosine, -sine, heads)


def head_rows(group, member):
    head = group * HEAD_SHARE + member
    return pl.ds(pl.multiple_of(head * HEAD_DIMENSION, HEAD_DIMENSION), HEAD_DIMENSION)


def as_column(row):
    wide = jnp.broadcast_to(row.astype(jnp.float32), (8, row.shape[1]))
    return wide.T[:, 0:1]


def fill_bias(bias, metas, query_segments, level, blk, m, piece):
    key_at = lax.broadcasted_iota(jnp.int32, (piece, piece), 0)
    query_at = lax.broadcasted_iota(jnp.int32, (piece, piece), 1)

    @pl.loop(0, blk + 1)
    def _(block):
        columns = metas[block_bits(block, m)].T
        live = jnp.where(columns[:, 1:2] > level, columns[:, 0:1], -1.0)
        shift = (blk - block) * piece
        allowed = (live == query_segments) & (key_at <= query_at + shift) | (key_at == query_at + shift)
        bias[block] = jnp.where(allowed, 0.0, masked_score)


def fill_bias_by_rows(bias, metas, level, blk, m, piece):
    query_at = lax.broadcasted_iota(jnp.int32, (piece, piece), 0)
    key_at = lax.broadcasted_iota(jnp.int32, (piece, piece), 1)
    query_segments = metas[block_bits(blk, m)].T[:, 0:1]

    @pl.loop(0, blk + 1)
    def _(block):
        meta = metas[block_bits(block, m)]
        live = jnp.where(meta[1:2, :] > level, meta[0:1, :], -1.0)
        shift = (blk - block) * piece
        allowed = (live == query_segments) & (key_at <= query_at + shift) | (key_at == query_at + shift)
        bias[block] = jnp.where(allowed, 0.0, masked_score).astype(bias.dtype)


def spec(memory):
    return pl.BlockSpec(memory_space=memory)


def shaped(entry):
    return jax.ShapeDtypeStruct(*entry)


def spaces(entries):
    return [pltpu.VMEM(*entry) for entry in entries]


def dma_semaphores(*shapes):
    return [pltpu.SemaphoreType.DMA(shape) for shape in shapes]


class Piece:
    def __init__(self, at, kept_at, slot, flavour, family, sems, bits):
        self.at, self.kept_at, self.slot, self.family, self.sems = at, kept_at, slot, family, sems
        self.m, self.n = bits
        left = list(range(self.m - 1, -1, -1))
        self.order = []
        for stage in range(self.m):
            place = len(left) - 1 if stage == 0 or flavour == 0 else 0
            self.order.append((left.pop(place), place, len(left)))
        self.last = self.m + self.n
        self.blk = lax.axis_index("blk")
        self.dp = lax.axis_index("dp") if self.n else None

    def half(self, ref, side):
        rows, columns = self.family.shape
        if self.family.split == 0:
            return ref.at[pl.ds(pl.multiple_of(side * (rows // 2), rows // 2), rows // 2), :]
        return ref.at[:, pl.ds(pl.multiple_of(side * (columns // 2), columns // 2), columns // 2)]

    def held(self, stage):
        if stage == 0:
            return self.family.part, self.slot
        return self.family.blk[stage - 1], self.kept_at

    def copy(self, stage):
        m, family = self.m, self.family
        if stage < m:
            bit, place, others = self.order[stage]
            ref, index = self.held(stage)
            chosen = [slice(None)] * (others + 1)
            chosen[place] = 1 - bit_of(self.blk, bit)
            source = ref.at[(index, *chosen)]
            target = family.blk[stage].at[self.kept_at]
            device = {"blk": flipped(self.blk, bit)}
        elif stage < self.last:
            bit = stage - m
            if bit == 0:
                source = self.half(family.blk[m - 1].at[self.kept_at], 1 - bit_of(self.dp, 0))
            else:
                source = family.dp[bit - 1].at[self.kept_at]
            target = family.dp[bit].at[self.kept_at]
            device = {"dp": flipped(self.dp, bit)}
        else:
            source = self.half(family.out.at[self.kept_at], bit_of(self.dp, 0))
            target = source
            device = {"dp": flipped(self.dp, 0)}
        return remote(source, target, self.sems, (self.at, stage), device)

    def start(self, stage):
        self.copy(stage).start()

    def finish(self, stage):
        m, family = self.m, self.family
        self.copy(stage).wait_recv()
        if stage < m:
            bit, place, others = self.order[stage]
            ref, index = self.held(stage)
            for combo in itertools.product(range(2), repeat=others):
                chosen = list(combo)
                chosen.insert(place, bit_of(self.blk, bit))
                into = family.blk[stage].at[(self.kept_at, *combo)]
                self.add(into, into, ref.at[(index, *chosen)])
            if stage == 0:
                self.copy(0).wait_send()
        elif stage < self.last:
            bit = stage - m
            got = family.dp[bit].at[self.kept_at]
            if bit == 0:
                own = self.half(family.blk[m - 1].at[self.kept_at], bit_of(self.dp, 0))
            else:
                own = family.dp[bit - 1].at[self.kept_at]
            into = got
            if stage == self.last - 1:
                into = self.half(family.out.at[self.kept_at], bit_of(self.dp, 0))
            self.add(into, got, own)

    def add(self, into, left, right):
        into[...] = left[...] + right[...]

    def drained(self, stages):
        for stage in stages:
            self.copy(stage).wait_send()


def feed_forward_backward(at, level, gradient, ready, done):
    tiles = at.w_gate.shape[1] // FF_TILE
    column = at.router[level:level + 1, :].astype(jnp.float32)
    active = as_column(at.depths[...]) > float(level)
    hidden = at.hid_level[...]
    chosen = jax.nn.sigmoid(jnp.sum(hidden * column, axis=1, keepdims=True))
    at.dbranch[...] = jnp.where(active, chosen, 0.0) * gradient
    dchosen = jnp.where(active, jnp.sum(gradient * at.branch_level[...], axis=1, keepdims=True), 0.0)
    dlogit = dchosen * chosen * (1.0 - chosen)
    at.small[2 + level:3 + level, :] = jnp.sum(hidden * dlogit, axis=0, keepdims=True)
    at.grad_hidden[...] = gradient + dlogit * column
    at.dffn[...] = at.dbranch[...].astype(low)

    def dinner_of(tile):
        ready(tile)
        return plain_dot(at.dffn[...], at.w_down[:, tile * FF_TILE:(tile + 1) * FF_TILE])

    dinner = dinner_of(0)
    for tile in range(tiles):
        following = dinner_of(tile + 1) if tile + 1 < tiles else None
        columns = slice(tile * FF_TILE, (tile + 1) * FF_TILE)
        dgate = (dinner * at.slope_level[:, columns].astype(jnp.float32)).astype(low)
        dup = (dinner * at.silu_level[:, columns].astype(jnp.float32)).astype(low)
        at.dgate[:, columns] = dgate
        at.dup[:, columns] = dup
        done(tile)
        share = plain_dot(at.w_gate[:, columns], dgate.T) + plain_dot(at.w_up[:, columns], dup.T)
        if tile == 0:
            at.dnorm_turned[...] = share
        else:
            at.dnorm_turned[...] += share
        dinner = following
    ready(None)
    dnorm = at.dnorm_turned[...].T
    dmiddle, gain_share = norm_gradient(dnorm, at.middle_level[...], at.norms[1:2, :].astype(jnp.float32))
    at.small[1:2, :] += gain_share
    at.grad_hidden[...] += dmiddle
    dattn = (at.dbranch[...] + dmiddle).astype(low)
    lead = at.far.shape[1] - dattn.shape[1]
    at.far[:, :lead] = jnp.zeros((dattn.shape[0], lead), low)
    at.far[:, lead:] = dattn
    at.dat[...] = plain_dot(at.w_out[...], dattn.T).astype(low)


def forward_kernel(sizes, names, *refs):
    m, piece = sizes
    at = types.SimpleNamespace(**dict(zip(names, refs)))
    blk = lax.axis_index("blk")
    mine = block_bits(blk, m)
    kv, metas = at.kv, at.metas
    weights = (
        (at.key_weight_hbm, at.key_weight), (at.value_weight_hbm, at.value_weight), (at.w_query_hbm, at.w_query),
        (at.w_out_hbm, at.w_out), (at.w_gate_hbm, at.w_gate), (at.w_up_hbm, at.w_up), (at.w_down_hbm, at.w_down),
    )
    loads = [pltpu.make_async_copy(*pair, at.load_sems.at[index]) for index, pair in enumerate(weights)]
    for load in loads:
        load.start()
    saved = (
        (at.normed, at.normed_out), (at.turned, at.turned_out), (kv, at.kv_out), (at.lse, at.lse_out),
        (at.att, at.att_out), (at.nffn, at.nffn_out), (at.inner, at.inner_out),
    )

    def save(index, level):
        return pltpu.make_async_copy(
            saved[index][0].at[level], saved[index][1].at[level], at.save_sems.at[index, level]
        )

    first = (
        (at.hid.at[0], at.hid_out), (at.middle.at[0], at.middle_out), (at.silu.at[0], at.silu_out),
        (at.slope.at[0], at.slope_out), (at.branch.at[0], at.branch_out), (metas, at.metas_out),
        (at.far, at.far_out), (at.dat, at.dat_out), (at.dffn, at.dffn_out), (at.dgate, at.dgate_out), (at.dup, at.dup_out),
        (at.hid.at[1], at.hid_1_out),
    )
    late = [pltpu.make_async_copy(*pair, at.late_sems.at[index]) for index, pair in enumerate(first)]
    segment_row = at.segments[...].astype(jnp.float32)
    depth_column = as_column(at.depths[...])
    metas[mine] = jnp.concatenate(
        [segment_row, at.depths[...].astype(jnp.float32), jnp.zeros((6, piece), jnp.float32)], axis=0
    )
    greet([{"blk": flipped(blk, bit)} for bit in range(m)])

    def place(known):
        return tuple(slice(None) if bit in known else mine[m - 1 - bit] for bit in range(m - 1, -1, -1))

    orders = (list(range(1, m)), list(range(m - 1, 0, -1)))
    kv_sems = (at.kv_send, at.kv_recv)

    def kv_copies(level, group, stage):
        if stage == m - 1:
            ref = kv.at[(level, group, *place(range(1, m)))]
            return [remote(ref, ref, kv_sems, (level, group, 2 * stage), {"blk": flipped(blk, 0)})]
        copies = []
        for side, order in enumerate(orders):
            rows = pl.ds(side * (piece // 2), piece // 2)
            ref = kv.at[(level, group, *place(order[:stage]), rows)]
            copies.append(remote(ref, ref, kv_sems, (level, group, 2 * stage + side), {"blk": flipped(blk, order[stage])}))
        return copies

    def kv_advance(level, group, stage):
        if stage > 0:
            for copy in kv_copies(level, group, stage - 1):
                copy.wait_recv()
        if stage < m:
            for copy in kv_copies(level, group, stage):
                copy.start()

    def meta_copy(stage):
        bits = list(range(1, m)) + [0]
        ref = metas.at[place(bits[:stage])]
        return remote(ref, ref, (at.meta_send, at.meta_recv), stage, {"blk": flipped(blk, bits[stage])})

    meta_copy(0).start()
    cosine, sine = at.cosines[...], at.sines[...]
    gain_attn, gain_ffn = at.norms[0:1, :].astype(jnp.float32), at.norms[1:2, :].astype(jnp.float32)
    routers = at.router[...].astype(jnp.float32)
    at.hid[0] = at.tokens[...].T.astype(jnp.float32)
    late[0].start()
    at.query_pad[HEAD_DIMENSION:, :] = jnp.zeros_like(at.query_pad[HEAD_DIMENSION:, :])

    @pl.loop(0, RECUR)
    def _(level):
        hidden = at.hid[level]
        at.flat[...] = (hidden * rms_scale(hidden) * gain_attn).astype(low)
        at.normed[level] = at.flat[...].T

        @pl.when(level == 0)
        def _():
            for load in loads[:2]:
                load.wait()

        keys = turn_heads(plain_dot(at.key_weight[...], at.normed[level]), cosine, sine, KEY_VALUE_HEADS)
        values = plain_dot(at.value_weight[...], at.normed[level])
        for group in range(KEY_VALUE_HEADS):
            here = slice(group * HEAD_DIMENSION, (group + 1) * HEAD_DIMENSION)
            both = jnp.concatenate([keys[here], values[here]], axis=0)
            kv[(level, group, *mine)] = both.T.astype(low)
            kv_advance(level, group, 0)

        @pl.when(level == 0)
        def _():
            loads[2].wait()
            for stage in range(1, m - 1):
                meta_copy(stage - 1).wait_recv()
                meta_copy(stage).start()

        queries = turn_heads(plain_dot(at.flat[...], at.w_query[...]).T, cosine, sine, QUERY_HEADS)
        at.turned[level] = (queries * HEAD_DIMENSION ** (-0.5)).astype(low)

        @pl.when(level == 0)
        def _():
            for stage in range(max(1, m - 1), m):
                meta_copy(stage - 1).wait_recv()
                meta_copy(stage).start()

        for stage in range(1, m):
            for group in range(m - stage):
                kv_advance(level, group, stage)

        @pl.when(level == 0)
        def _():
            meta_copy(m - 1).wait_recv()
            late[5].start()

        fill_bias(at.bias, metas, segment_row, level.astype(jnp.float32), blk, m, piece)

        @pl.loop(0, KEY_VALUE_HEADS)
        def _(group):
            for stage in range(1, m):
                @pl.when(group + m - stage < KEY_VALUE_HEADS)
                def _():
                    kv_advance(level, group + m - stage, stage)

            kv_advance(level, group, m)
            for member in range(HEAD_SHARE):
                at.query_pad[:HEAD_DIMENSION, member * piece:(member + 1) * piece] = at.turned[level, head_rows(group, member), :]
            at.top[...] = jnp.full_like(at.top, masked_score)
            at.total[...] = jnp.zeros_like(at.total)

            @pl.loop(0, blk + 1)
            def _(step):
                block = blk - step
                rows = kv[(level, group, *block_bits(block, m))]
                here = at.bias[block]
                scores = plain_dot(rows, at.query_pad[...]) + jnp.concatenate([here] * HEAD_SHARE, axis=1)
                before = at.top[0:1, :]
                after = jnp.maximum(before, jnp.max(scores, axis=0, keepdims=True))
                raised = jnp.exp(scores - after)
                shrink = jnp.exp(before - after)
                at.top[0:1, :] = after
                ones = jnp.ones((16, piece), low)
                left = jnp.concatenate([rows.T[HEAD_DIMENSION:], ones], axis=0)
                at.total[...] = at.total[...] * shrink + plain_dot(left, raised.astype(low))

            sums = at.total[HEAD_DIMENSION:HEAD_DIMENSION + 1, :]
            at.lse[level, pl.ds(group, 1), :] = at.top[0:1, :] + jnp.log(sums)
            out = at.total[:HEAD_DIMENSION, :] / sums
            for member in range(HEAD_SHARE):
                at.att[level, head_rows(group, member), :] = out[:, member * piece:(member + 1) * piece].astype(low)

        for index in range(5):
            save(index, level).start()

        @pl.when(level == 0)
        def _():
            loads[3].wait()

        attn = plain_dot(at.att[level].T, at.w_out[...])
        mid = at.hid[level] + attn
        at.middle[level] = mid
        at.branch[level] = attn
        at.flat[...] = (mid * rms_scale(mid) * gain_ffn).astype(low)
        at.nffn[level] = at.flat[...].T
        save(5, level).start()

        @pl.when(level == 0)
        def _():
            loads[4].wait()
            loads[5].wait()

        for tile in range(at.w_gate.shape[1] // FF_TILE):
            columns = slice(tile * FF_TILE, (tile + 1) * FF_TILE)
            gate_pre = plain_dot(at.flat[...], at.w_gate[:, columns])
            up_pre = plain_dot(at.flat[...], at.w_up[:, columns])
            opened = jax.nn.sigmoid(gate_pre)
            passed = gate_pre * opened
            at.silu[level, :, columns] = passed.astype(low)
            at.slope[level, :, columns] = (up_pre * (opened + passed - passed * opened)).astype(low)
            at.inner[level, columns, :] = (passed * up_pre).astype(low).T

        save(6, level).start()

        @pl.when(level == 0)
        def _():
            loads[6].wait()

        at.branch[level] += plain_dot(at.w_down[...], at.inner[level]).T
        column = jnp.where(level == 0, routers[0:1, :], routers[1:2, :])
        logit = jnp.sum(at.hid[level] * column, axis=1, keepdims=True)
        weight = jnp.where(depth_column > level.astype(jnp.float32), jax.nn.sigmoid(logit), 0.0)
        at.hid[level + 1] = at.hid[level] + weight * at.branch[level]

        @pl.when(level == 0)
        def _():
            for copy in late[1:5]:
                copy.start()

    at.hidden_out[...] = at.hid[RECUR].T
    top = RECUR - 1
    at.hid_level, at.branch_level, at.middle_level = at.hid.at[top], at.branch.at[top], at.middle.at[top]
    at.silu_level, at.slope_level = at.silu.at[top], at.slope.at[top]
    at.small[...] = jnp.zeros_like(at.small)
    feed_forward_backward(at, top, at.cotangent[...].T.astype(jnp.float32), lambda tile: None, lambda tile: None)
    for copy in late[6:]:
        copy.start()
    for stage in range(m):
        meta_copy(stage).wait_send()
    for level in range(RECUR):
        for group in range(KEY_VALUE_HEADS):
            for stage in range(m):
                for copy in kv_copies(level, group, stage):
                    copy.wait_send()
        for index in range(len(saved)):
            save(index, level).wait()
    for copy in late:
        copy.wait()


def far_width(width):
    return 2 * width + 2 * KEYS_WIDTH - 1536


def forward(small, weights, nb):
    m = nb.bit_length() - 1
    width, piece = small["tokens"].shape
    hidden_units = weights["w_gate_hbm"].shape[1]
    blocks, wide = (2,) * m, HEAD_SHARE * piece
    rows, turned = ((piece, width), jnp.float32), ((RECUR, width, piece), low)
    hidden = ((piece, hidden_units), low)
    saved = dict(
        normed=turned, turned=turned, kv=((RECUR, KEY_VALUE_HEADS, *blocks, piece, PAIR), low),
        lse=((RECUR, 8, wide), jnp.float32), att=turned, nffn=turned, inner=((RECUR, hidden_units, piece), low),
        metas=((*blocks, 8, piece), jnp.float32), far=((piece, far_width(width)), low), dat=((width, piece), low),
        dffn=((piece, width), low), dgate=hidden, dup=hidden,
    )
    first = dict(hid=rows, middle=rows, silu=hidden, slope=hidden, branch=rows)
    outs = dict(hidden_out=((width, piece), jnp.float32), grad_hidden=rows, small=((8, width), jnp.float32))
    anywhere = {name + "_out": entry for name, entry in (saved | first | dict(hid_1=rows)).items()}
    both = {name: ((RECUR, *shape), dtype) for name, (shape, dtype) in first.items()}
    buffers = {name[:-4]: (array.shape, array.dtype) for name, array in weights.items()} | saved | both | dict(
        hid=((RECUR + 1, piece, width), jnp.float32), flat=((piece, width), low),
        bias=((nb, piece, piece), jnp.float32), query_pad=((PAIR, wide), low), top=((8, wide), jnp.float32),
        total=((HEAD_DIMENSION + 16, wide), jnp.float32), dbranch=rows, dnorm_turned=((width, piece), jnp.float32),
    )
    semaphores = dict(
        load_sems=(7,), save_sems=(7, RECUR), late_sems=(12,), kv_send=(RECUR, KEY_VALUE_HEADS, 2 * m),
        kv_recv=(RECUR, KEY_VALUE_HEADS, 2 * m), meta_send=(m,), meta_recv=(m,),
    )
    results = pl.pallas_call(
        functools.partial(forward_kernel, (m, piece), (*small, *weights, *outs, *anywhere, *buffers, *semaphores)),
        out_shape=[shaped(entry) for entry in (outs | anywhere).values()],
        in_specs=[spec(pltpu.VMEM)] * len(small) + [spec(pl.ANY)] * len(weights),
        out_specs=[spec(pltpu.VMEM)] * len(outs) + [spec(pl.ANY)] * len(anywhere),
        scratch_shapes=spaces(buffers.values()) + dma_semaphores(*semaphores.values()),
        compiler_params=pltpu.CompilerParams(
            collective_id=1, has_side_effects=True, vmem_limit_bytes=VMEM_LIMIT
        ),
        cost_estimate=pl.CostEstimate(
            flops=3 * RECUR * piece * width * 10240, bytes_accessed=48 * 1024 * 1024, transcendentals=0
        ),
        name="forward_levels",
    )(*small.values(), *weights.values())
    return dict(zip((*outs, *(name[:-4] for name in anywhere)), results))


class AttentionBackward:
    def __init__(self, at, m, piece, level):
        self.at, self.m, self.piece, self.level = at, m, piece, level
        self.blk = lax.axis_index("blk")
        self.family = types.SimpleNamespace(part=at.part, blk=at.halves, dp=(), out=None, shape=(HEAD_DIMENSION, piece), split=0)

    def pieces(self, group):
        sems = (self.at.kv_send, self.at.kv_recv)
        return [
            Piece(2 * group + side, 2 * group + side, 2 * group + side, side, self.family, sems, (self.m, 0))
            for side in range(2)
        ]

    def move(self, group, stage):
        for piece_of in self.pieces(group):
            piece_of.finish(stage)
            if stage + 1 < self.m:
                piece_of.start(stage + 1)

    def begin(self):
        at = self.at
        fill_bias_by_rows(at.bias, at.metas, float(self.level), self.blk, self.m, self.piece)
        at.query_pad[HEAD_DIMENSION:, :] = jnp.zeros_like(at.query_pad[HEAD_DIMENSION:, :])
        at.dat_pad[:HEAD_DIMENSION, :] = jnp.zeros_like(at.dat_pad[:HEAD_DIMENSION, :])

    def group(self, group):
        at, m, piece, blk = self.at, self.m, self.piece, self.blk
        carried = []
        for member in range(HEAD_SHARE):
            rows, lanes = head_rows(group, member), slice(member * piece, (member + 1) * piece)
            at.query_pad[:HEAD_DIMENSION, lanes] = at.turned[rows, :]
            at.dat_pad[HEAD_DIMENSION:, lanes] = at.dat_turned[rows, :]
            product = at.dat_turned[rows, :].astype(jnp.float32) * at.att_turned[rows, :].astype(jnp.float32)
            carried.append(jnp.sum(product, axis=0, keepdims=True))
        wide = HEAD_SHARE * piece
        at.query_rows[...] = at.query_pad[...].T
        at.dat_rows[...] = at.dat_pad[...].T
        at.log_total[...] = jnp.broadcast_to(at.lse[pl.ds(group, 1), :], (128, wide)).T
        at.carried[...] = jnp.broadcast_to(jnp.concatenate(carried, axis=1), (128, wide)).T
        at.dq_sum[...] = jnp.zeros_like(at.dq_sum)

        def over_keys(column):
            return jnp.concatenate([column] * (piece // 128), axis=1)

        @pl.loop(0, blk + 1)
        def _(block):
            rows = at.kv[(group, *block_bits(block, m))]
            columns = rows.T
            here = jnp.concatenate([at.bias[block].astype(jnp.float32)] * HEAD_SHARE, axis=0)
            scores = plain_dot(at.query_rows[...], columns) + here
            probability = jnp.exp(scores - over_keys(at.log_total[...]))
            dprob = plain_dot(at.dat_rows[...], columns)
            dscores = (probability * (dprob - over_keys(at.carried[...]))).astype(low)
            dkeys = plain_dot(at.query_pad[:HEAD_DIMENSION, :], dscores)
            dvalues = plain_dot(at.dat_pad[HEAD_DIMENSION:, :], probability.astype(low))
            at.part[(2 * group, *block_bits(block, m))] = dkeys.astype(low)
            at.part[(2 * group + 1, *block_bits(block, m))] = dvalues.astype(low)
            at.dq_sum[...] += plain_dot(dscores, rows)

        @pl.loop(blk + 1, 1 << m)
        def _(block):
            for side in range(2):
                at.part[(2 * group + side, *block_bits(block, m))] = jnp.zeros((HEAD_DIMENSION, piece), low)

        for piece_of in self.pieces(group):
            piece_of.start(0)
        turned = at.dq_sum[...].T
        for member in range(HEAD_SHARE):
            at.dq_turned[head_rows(group, member), :] = turned[:HEAD_DIMENSION, member * piece:(member + 1) * piece]

    def follow(self, group):
        for stage in range(self.m - 1):
            earlier = group - 1 - stage
            if isinstance(group, int):
                if 0 <= earlier < KEY_VALUE_HEADS:
                    self.move(earlier, stage)
            else:
                @pl.when(earlier >= 0)
                def _():
                    self.move(earlier, stage)

    def queries(self, cosine, sine):
        at = self.at
        dqueries = turn_back(at.dq_turned[...] * HEAD_DIMENSION ** (-0.5), cosine, sine, QUERY_HEADS).astype(low)
        self.put(2 * KEYS_WIDTH, dqueries.T)
        at.dnorm[...] = plain_dot(at.w_query[...], dqueries).T

    def put(self, column, values):
        self.at.near[self.at.near_rows, column:column + values.shape[1]] = values

    def keys(self, cosine, sine):
        at, m = self.at, self.m
        filled = 2 * KEYS_WIDTH + QUERY_HEADS * HEAD_DIMENSION
        self.put(filled, jnp.zeros((self.piece, at.near_width - filled), low))
        dkeys, dvalues = [], []
        for group in range(KEY_VALUE_HEADS):
            self.move(group, m - 1)
            dkeys.append(at.halves[m - 1][2 * group].astype(jnp.float32))
            dvalues.append(at.halves[m - 1][2 * group + 1])
        dkeys = turn_back(jnp.concatenate(dkeys, axis=0), cosine, sine, KEY_VALUE_HEADS).astype(low).T
        dvalues = jnp.concatenate(dvalues, axis=0).T
        self.put(0, dkeys)
        self.put(KEYS_WIDTH, dvalues)
        at.dnorm[...] += plain_dot(dkeys, at.key_weight[...]) + plain_dot(dvalues, at.value_weight[...])

    def drained(self):
        for group in range(KEY_VALUE_HEADS):
            for piece_of in self.pieces(group):
                piece_of.drained(range(1, self.m))


def attention_buffers(nb, piece, width, bias_type):
    m, wide, heads = nb.bit_length() - 1, HEAD_SHARE * piece, 2 * KEY_VALUE_HEADS
    turned, weight = ((width, piece), low), ((KEYS_WIDTH, width), low)
    pad, pad_rows, stat = ((PAIR, wide), low), ((wide, PAIR), low), ((wide, 128), jnp.float32)
    buffers = dict(
        turned=turned, dat_turned=turned, att_turned=turned, kv=((KEY_VALUE_HEADS, *(2,) * m, piece, PAIR), low),
        lse=((8, wide), jnp.float32), metas=((*(2,) * m, 8, piece), jnp.float32), w_query=((width, width), low),
        key_weight=weight, value_weight=weight, dq_turned=((width, piece), jnp.float32),
        bias=((nb, piece, piece), bias_type), query_pad=pad, dat_pad=pad, query_rows=pad_rows, dat_rows=pad_rows,
        log_total=stat, carried=stat, dq_sum=stat, part=((heads, *(2,) * m, HEAD_DIMENSION, piece), low),
        dnorm=((piece, width), jnp.float32), hid=((piece, width), jnp.float32),
    )
    for stage in range(m):
        buffers["half_%d" % stage] = ((heads, *(2,) * (m - 1 - stage), HEAD_DIMENSION, piece), low)
    return buffers


def backward_kernel(sizes, names, *refs):
    m, piece, level = sizes
    at = types.SimpleNamespace(**dict(zip(names, refs)))
    at.halves = [getattr(at, "half_%d" % stage) for stage in range(m)]
    at.near, at.near_rows, at.near_width = at.near_out, slice(None), at.near_out.shape[1]
    blk = lax.axis_index("blk")
    pairs = (
        (at.metas_hbm, at.metas), (at.turned_hbm.at[level], at.turned), (at.dat_hbm, at.dat_turned),
        (at.att_hbm.at[level], at.att_turned), (at.lse_hbm.at[level], at.lse), (at.kv_hbm.at[level], at.kv),
        (at.w_query_hbm, at.w_query), (at.key_weight_hbm, at.key_weight), (at.value_weight_hbm, at.value_weight),
        (at.grad_hbm, at.grad_hidden), (at.hid_1_hbm, at.hid),
        (at.hid_0_hbm, at.hid_level), (at.branch_hbm, at.branch_level), (at.w_down_hbm, at.w_down),
        (at.slope_hbm, at.slope_level), (at.silu_hbm, at.silu_level), (at.w_gate_hbm, at.w_gate), (at.w_up_hbm, at.w_up),
        (at.middle_hbm, at.middle_level), (at.w_out_hbm, at.w_out),
    )
    loads = [pltpu.make_async_copy(*pair, at.load_sems.at[index]) for index, pair in enumerate(pairs)]
    for load in loads:
        load.start()
    saves = [
        pltpu.make_async_copy(*pair, at.save_sems.at[index])
        for index, pair in enumerate(((at.dgate, at.dgate_out), (at.dup, at.dup_out)))
    ]
    greet([{"blk": flipped(blk, bit)} for bit in range(m)])
    work = AttentionBackward(at, m, piece, level)
    loads[0].wait()
    work.begin()
    for load in loads[1:6]:
        load.wait()

    @pl.loop(0, KEY_VALUE_HEADS)
    def _(group):
        work.group(group)
        work.follow(group)

    cosine, sine = at.cosines[...], at.sines[...]
    for virtual in range(KEY_VALUE_HEADS, KEY_VALUE_HEADS + m - 1):
        work.follow(virtual)
        if virtual == KEY_VALUE_HEADS:
            loads[6].wait()
            work.queries(cosine, sine)
    for load in loads[7:]:
        load.wait()
    work.keys(cosine, sine)
    dhidden, gain_share = norm_gradient(at.dnorm[...], at.hid[...], at.norms[0:1, :].astype(jnp.float32))
    at.small[...] = at.small_before[...]
    at.small[0:1, :] = gain_share
    gradient = at.grad_hidden[...] + dhidden
    at.dnorm[...] = gradient
    feed_forward_backward(at, level - 1, at.dnorm[...], lambda tile: None, lambda tile: None)
    for save in saves:
        save.start()
    work.drained()
    for save in saves:
        save.wait()


def backward(level, small, operands, nb):
    m = nb.bit_length() - 1
    piece, width = operands["grad_hbm"].shape
    hidden_units = operands["w_gate_hbm"].shape[1]
    rows, flat, hidden = ((piece, width), jnp.float32), ((piece, width), low), ((piece, hidden_units), low)
    outs = dict(
        grad_hidden=rows, small=((8, width), jnp.float32), near_out=((piece, 1792), low), dffn=flat,
        dat=((width, piece), low), far=((piece, far_width(width)), low),
    )
    anywhere = dict(dgate_out=hidden, dup_out=hidden)
    buffers = attention_buffers(nb, piece, width, jnp.float32) | dict(
        hid_level=rows, branch_level=rows, middle_level=rows, w_down=((width, hidden_units), low), slope_level=hidden,
        silu_level=hidden, w_gate=((width, hidden_units), low), w_up=((width, hidden_units), low),
        w_out=((width, width), low), dbranch=rows, dnorm_turned=((width, piece), jnp.float32), dgate=hidden, dup=hidden,
    )
    sums = (2 * KEY_VALUE_HEADS, m)
    semaphores = dict(load_sems=(20,), save_sems=(2,), kv_send=sums, kv_recv=sums)
    results = pl.pallas_call(
        functools.partial(
            backward_kernel, (m, piece, level), (*small, *operands, *outs, *anywhere, *buffers, *semaphores)
        ),
        out_shape=[shaped(entry) for entry in (outs | anywhere).values()],
        in_specs=[spec(pltpu.VMEM)] * len(small) + [spec(pl.ANY)] * len(operands),
        out_specs=[spec(pltpu.VMEM)] * len(outs) + [spec(pl.ANY)] * len(anywhere),
        scratch_shapes=spaces(buffers.values()) + dma_semaphores(*semaphores.values()),
        compiler_params=pltpu.CompilerParams(
            collective_id=2, has_side_effects=True, vmem_limit_bytes=VMEM_LIMIT
        ),
        cost_estimate=pl.CostEstimate(
            flops=2 * piece * width * 20000, bytes_accessed=32 * 1024 * 1024, transcendentals=0
        ),
        name="backward_level",
    )(*small.values(), *operands.values())
    return dict(zip((*outs, *anywhere), results))


WIDE_SLOTS, DOWN_SLOTS = 4, 2


def final_kernel(sizes, names, *refs):
    nb, m, n, piece, rows, padded, near_width = sizes
    at = types.SimpleNamespace(**dict(zip(names, refs)))
    at.halves = [getattr(at, "half_%d" % stage) for stage in range(m)]
    blk, dp = lax.axis_index("blk"), lax.axis_index("dp")
    at.near, at.near_rows, at.near_width = at.gate_side, slice(0, piece), near_width
    counter = itertools.count()

    def load(source, target):
        return pltpu.make_async_copy(source, target, at.load_sems.at[next(counter)])

    def both_lanes(ref, target):
        return [load(ref.at[level], target.at[:, pl.ds(level * piece, piece)]) for level in range(RECUR)]

    def both_rows(low_ref, deep_ref, target, width):
        pairs = ((low_ref, 0), (deep_ref, piece))
        return [load(ref, target.at[pl.ds(first, piece), pl.ds(0, width)]) for ref, first in pairs]

    hidden_units, width = at.gate_side.shape[1], at.dffn.shape[1]
    far_lanes = at.far_0_hbm.shape[1]
    loads = types.SimpleNamespace(
        nffn=both_lanes(at.nffn_hbm, at.left),
        dgate=both_rows(at.dgate_0_hbm, at.dgate_1_hbm, at.gate_side, hidden_units),
        inner=both_lanes(at.inner_hbm, at.inner),
        dffn=both_rows(at.dffn_0_hbm, at.dffn_1_hbm, at.dffn, width),
        metas=[load(at.metas_hbm, at.metas)],
        heads=[
            load(at.turned_hbm.at[0], at.turned), load(at.dat_hbm, at.dat_turned), load(at.att_hbm.at[0], at.att_turned),
            load(at.lse_hbm.at[0], at.lse), load(at.kv_hbm.at[0], at.kv),
        ],
        dup=both_rows(at.dup_0_hbm, at.dup_1_hbm, at.up_side, hidden_units),
        w_query=[load(at.w_query_hbm, at.w_query)],
        rest=[
            load(at.key_weight_hbm, at.key_weight), load(at.value_weight_hbm, at.value_weight),
            load(at.hid_hbm, at.hid), load(at.grad_hbm, at.grad),
        ],
        attended=both_lanes(at.attended_hbm, at.left_attended),
    )
    late = types.SimpleNamespace(
        near=[load(at.near_1_hbm, at.gate_side.at[pl.ds(piece, piece), pl.ds(0, near_width)])],
        far=both_rows(at.far_0_hbm, at.far_1_hbm, at.up_side, far_lanes),
        normed=both_lanes(at.normed_hbm, at.left),
    )

    def begin(copies):
        for copy in copies:
            copy.start()

    def ready(copies):
        for copy in copies:
            copy.wait()

    for copies in vars(loads).values():
        begin(copies)
    greet([{"blk": flipped(blk, bit)} for bit in range(m)] + [{"dp": flipped(dp, bit)} for bit in range(n)])

    down_rows = at.part_down.shape[-2]

    def family(name, shape, split):
        return types.SimpleNamespace(
            part=getattr(at, "part_" + name), out=getattr(at, "out_" + name), shape=shape, split=split,
            blk=[getattr(at, "blk_%s_%d" % (name, stage)) for stage in range(m)],
            dp=[getattr(at, "dp_%s_%d" % (name, stage)) for stage in range(n)],
        )

    wide = family("wide", (2 * padded, UNIT_COLUMNS), 1)
    down = family("down", (down_rows, width), 0)
    little = family("small", (16, 128), 0)
    sems = (at.send_sems, at.recv_sems)
    units = itertools.count()

    def unit(holder, index, flavour):
        return Piece(next(units), index, index % holder.part.shape[0], flavour, holder, sems, (m, n))

    pairs = [[unit(wide, index, 0), unit(down, index, 1)] for index in range(5)]
    pairs += [[unit(wide, index, 0), unit(wide, index + 1, 1)] for index in (5, 7, 9, 11)]
    pairs += [[unit(wide, 13, 0), unit(wide, 14, 1), unit(little, 0, 0)]]

    def compute_wide(index, slot):
        if index == 0:
            ready(loads.nffn)
            ready(loads.dgate)
        if index == 5:
            begin(late.near)
            ready(loads.dup)
        if index == 10:
            begin(late.far)
            begin(late.normed)
            ready(late.near)
            ready(late.normed)
            ready(loads.attended)
            ready(late.far)
        block, column = index // 5, (index % 5) * UNIT_COLUMNS
        second = 1280 + column
        upper_columns, lower_columns = slice(column, column + UNIT_COLUMNS), slice(second, second + UNIT_COLUMNS)
        if block < 2:
            right = at.gate_side if block == 0 else at.up_side
            upper = plain_dot(at.left[...], right[:, upper_columns])
            lower = plain_dot(at.left[...], right[:, lower_columns])
        else:
            upper = plain_dot(at.left[...], at.gate_side[:, upper_columns])
            lower = None
            if second < 1600:
                lower = plain_dot(at.left[...], at.gate_side[:, lower_columns])
            if second >= 1536:
                more = plain_dot(at.left_attended[...], at.up_side[:, second - 1536:second - 1536 + UNIT_COLUMNS])
                lower = more if lower is None else lower + more
        for target in range(nb):
            here = slice(target * padded, (target + 1) * padded)
            both = jnp.concatenate([upper[here], lower[here]], axis=0)
            at.part_wide[(slot, *bits_of(target, m))] = both.astype(low)

    def compute_down(index, slot):
        if index == 0:
            ready(loads.inner)
            ready(loads.dffn)
        firsts = [(target * 5 + index) * down_rows for target in range(nb)]
        left = jnp.concatenate([at.inner[first:first + down_rows, :] for first in firsts], axis=0)
        result = plain_dot(left, at.dffn[...])
        for target in range(nb):
            at.part_down[(slot, *bits_of(target, m))] = result[target * down_rows:(target + 1) * down_rows].astype(low)

    def compute_small():
        total = at.small_before[...]
        total = total + jnp.concatenate([at.gain_row[...], jnp.zeros((7, width), jnp.float32)], axis=0)
        at.part_small[...] = jnp.zeros_like(at.part_small)
        for target in range(nb):
            at.part_small[(0, *bits_of(target, m), slice(0, 8), slice(0, rows))] = total[:, target * rows:(target + 1) * rows]

    def compute(piece_of):
        if piece_of.family is wide:
            compute_wide(piece_of.kept_at, piece_of.slot)
        elif piece_of.family is down:
            compute_down(piece_of.kept_at, piece_of.slot)
        else:
            compute_small()
        piece_of.start(0)

    def moves(tick):
        for stage in range(m + n - 1, -1, -1):
            if 0 <= tick - stage < len(pairs):
                for piece_of in pairs[tick - stage]:
                    piece_of.finish(stage)
                    piece_of.start(stage + 1)

    work = AttentionBackward(at, m, piece, 0)
    for pair in pairs[:2]:
        for piece_of in pair:
            compute(piece_of)
    ready(loads.metas)
    work.begin()
    ready(loads.heads)
    for group in range(KEY_VALUE_HEADS):
        moves(group)
        for piece_of in pairs[group + 2]:
            compute(piece_of)
        work.group(group)
        work.follow(group)
    cosine, sine = at.cosines[...], at.sines[...]
    moves(5)
    compute(pairs[7][0])
    ready(loads.w_query)
    for virtual in range(KEY_VALUE_HEADS, KEY_VALUE_HEADS + m - 1):
        work.follow(virtual)
        if virtual == KEY_VALUE_HEADS:
            work.queries(cosine, sine)
    moves(6)
    ready(loads.rest)
    work.keys(cosine, sine)
    compute(pairs[7][1])
    moves(7)
    for piece_of in pairs[8] + pairs[9][:2]:
        compute(piece_of)
    dhidden, gain_share = norm_gradient(at.dnorm[...], at.hid[...], at.norms[0:1, :].astype(jnp.float32))
    at.gain_row[...] = gain_share
    at.grad_out[...] = (at.grad[...] + dhidden).T
    compute(pairs[9][2])
    for tick in range(8, len(pairs) + m + n - 1):
        moves(tick)
    for pair in pairs:
        for piece_of in pair:
            piece_of.finish(m + n)
    for pair in pairs:
        for piece_of in pair:
            piece_of.drained(range(1, m + n + 1))
    work.drained()


def unpack_kernel(sizes, wide_hbm, down_hbm, little_hbm, hidden_in, gradient_in, *refs):
    rows, padded = sizes
    norm_attn, norm_ffn, query, key, value, out, gate, up, down_out, router, hidden, gradient = refs[:12]
    wide, down, little, rest, sems = refs[12:]
    carried = [
        pltpu.make_async_copy(source, target, sems.at[at])
        for at, (source, target) in enumerate(((hidden_in, hidden), (gradient_in, gradient)))
    ]
    loads = [
        pltpu.make_async_copy(source, target, sems.at[2 + at])
        for at, (source, target) in enumerate(((wide_hbm, wide), (down_hbm, down), (little_hbm, little)))
    ]
    for copy in loads + carried:
        copy.start()
    for load in loads:
        load.wait()
    norm_attn[...] = little[0, 0:1, :rows]
    norm_ffn[...] = little[0, 1:2, :rows]
    router[...] = little[0, 2:4, :rows]
    for unit in range(5):
        for first, target in ((0, gate), (5, up), (10, rest)):
            tile = wide[first + unit].astype(jnp.float32)
            for side in range(2):
                column = side * 1280 + unit * UNIT_COLUMNS
                target[:, column:column + UNIT_COLUMNS] = tile[side * padded:side * padded + rows]
        down_rows = down.shape[1]
        down_out[unit * down_rows:(unit + 1) * down_rows, :] = down[unit].astype(jnp.float32)
    width = query.shape[1]
    key[...] = rest[:, :KEYS_WIDTH].T
    value[...] = rest[:, KEYS_WIDTH:2 * KEYS_WIDTH].T
    query[...] = rest[:, 2 * KEYS_WIDTH:2 * KEYS_WIDTH + width]
    out[...] = rest[:, 2 * KEYS_WIDTH + width:]
    for copy in carried:
        copy.wait()


def final(small, saved, top, bottom, weights, mesh_sizes):
    nb, nd = mesh_sizes
    m, n = nb.bit_length() - 1, nd.bit_length() - 1
    grad = bottom["grad_hidden"]
    piece, width = grad.shape
    hidden_units = weights["w_gate_hbm"].shape[1]
    rows = width // nb
    padded = -(-rows // 8) * 8
    down_rows = hidden_units // nb // 5
    tokens = RECUR * piece

    def spread(array):
        if padded == rows:
            return array
        split = array.reshape(RECUR, nb, rows, piece)
        return jnp.pad(split, ((0, 0), (0, 0), (0, padded - rows), (0, 0))).reshape(RECUR, nb * padded, piece)

    inputs = small | dict(small_before=bottom["small"])
    operands = dict(
        metas_hbm=saved["metas"], turned_hbm=saved["turned"], dat_hbm=bottom["dat"], att_hbm=saved["att"],
        lse_hbm=saved["lse"], kv_hbm=saved["kv"], w_query_hbm=weights["w_query_hbm"],
        key_weight_hbm=weights["key_weight_hbm"], value_weight_hbm=weights["value_weight_hbm"], hid_hbm=saved["hid"],
        grad_hbm=grad, inner_hbm=saved["inner"], nffn_hbm=spread(saved["nffn"]), normed_hbm=spread(saved["normed"]),
        attended_hbm=spread(saved["att"]), dffn_0_hbm=bottom["dffn"], dffn_1_hbm=top["dffn"],
        dgate_0_hbm=bottom["dgate_out"], dgate_1_hbm=top["dgate"], dup_0_hbm=bottom["dup_out"], dup_1_hbm=top["dup"],
        far_0_hbm=bottom["far"], far_1_hbm=top["far"], near_1_hbm=bottom["near_out"],
    )
    near_width = bottom["near_out"].shape[1]
    families = (
        ("wide", 15, (2 * padded, UNIT_COLUMNS), low, WIDE_SLOTS, 1), ("down", 5, (down_rows, width), low, DOWN_SLOTS, 0),
        ("small", 1, (16, 128), jnp.float32, 1, 0),
    )
    outs = dict(grad_out=((width, piece), jnp.float32))
    buffers = attention_buffers(nb, piece, width, low) | dict(
        grad=((piece, width), jnp.float32), gate_side=((tokens, hidden_units), low), up_side=((tokens, hidden_units), low),
        inner=((hidden_units, tokens), low), left=((nb * padded, tokens), low), left_attended=((nb * padded, tokens), low),
        dffn=((tokens, width), low), gain_row=((1, width), jnp.float32),
    )
    for name, count, shape, dtype, slots, split in families:
        outs["out_" + name] = ((count, *shape), dtype)
        buffers["part_" + name] = ((slots, *(2,) * m, *shape), dtype)
        for stage in range(m):
            buffers["blk_%s_%d" % (name, stage)] = ((count, *(2,) * (m - 1 - stage), *shape), dtype)
        half = (shape[0], shape[1] // 2) if split else (shape[0] // 2, shape[1])
        for stage in range(n):
            buffers["dp_%s_%d" % (name, stage)] = ((count, *half), dtype)
    sums, hops = (2 * KEY_VALUE_HEADS, m), (21, m + n + 1)
    semaphores = dict(load_sems=(32,), kv_send=sums, kv_recv=sums, send_sems=hops, recv_sems=hops)
    names = (*inputs, *operands, *outs, *buffers, *semaphores)
    gradient, wide, down, little = pl.pallas_call(
        functools.partial(final_kernel, (nb, m, n, piece, rows, padded, near_width), names),
        out_shape=[shaped(entry) for entry in outs.values()],
        in_specs=[spec(pltpu.VMEM)] * len(inputs) + [spec(pl.ANY)] * len(operands),
        out_specs=[spec(pltpu.VMEM)] * len(outs),
        scratch_shapes=spaces(buffers.values()) + dma_semaphores(*semaphores.values()),
        compiler_params=pltpu.CompilerParams(
            collective_id=0, has_side_effects=True, vmem_limit_bytes=VMEM_LIMIT
        ),
        cost_estimate=pl.CostEstimate(
            flops=2 * tokens * width * 14000, bytes_accessed=30 * 1024 * 1024, transcendentals=0
        ),
        name="weight_grads",
    )(*inputs.values(), *operands.values())
    shapes = (
        (1, rows), (1, rows), (rows, width), (KEYS_WIDTH, rows), (KEYS_WIDTH, rows), (rows, width),
        (rows, hidden_units), (rows, hidden_units), (5 * down_rows, width), (2, rows), (width, piece), (width, piece),
    )
    outs = pl.pallas_call(
        functools.partial(unpack_kernel, (rows, padded)),
        out_shape=[jax.ShapeDtypeStruct(shape, jnp.float32) for shape in shapes],
        in_specs=[spec(pl.ANY)] * 5,
        out_specs=[spec(pltpu.VMEM)] * 10 + [spec(pl.ANY)] * 2,
        scratch_shapes=[pltpu.VMEM(array.shape, array.dtype) for array in (wide, down, little)]
        + spaces([((rows, 2560), jnp.float32)]) + dma_semaphores((5,)),
        compiler_params=pltpu.CompilerParams(vmem_limit_bytes=VMEM_LIMIT),
        name="unpack",
    )(wide, down, little, saved["hidden_out"], gradient)
    norm_a, norm_f, query, key, value, out, gate, up, down, router, hidden, gradient = outs
    return (
        hidden.T[None], gradient.T[None], norm_a[0], norm_f[0], query, key.T, value.T, out, gate, up, down, router.T,
    )


def local(
    tokens,
    depths,
    segments,
    norm_attn,
    norm_ffn,
    w_query,
    key_weight,
    value_weight,
    w_out,
    w_gate,
    w_up,
    w_down,
    w_router,
    cotangent,
    mesh_sizes,
):
    piece = tokens.shape[1]
    positions = lax.axis_index("blk") * piece + jnp.arange(piece, dtype=jnp.int32)
    angles = frequencies(HEAD_DIMENSION)[:, None] * positions.astype(jnp.float32)[None, :]
    tables = dict(cosines=jnp.cos(angles), sines=jnp.sin(angles), norms=jnp.stack([norm_attn, norm_ffn]))
    routing = dict(router=w_router.T, depths=depths)
    heads = dict(w_query_hbm=w_query, key_weight_hbm=key_weight.T, value_weight_hbm=value_weight.T)
    weights = heads | dict(w_out_hbm=w_out, w_gate_hbm=w_gate, w_up_hbm=w_up, w_down_hbm=w_down.T)
    nb = mesh_sizes[0]
    saved = forward(
        tables | routing | dict(tokens=tokens[0].T, cotangent=cotangent[0].T, segments=segments), weights, nb
    )
    operands = dict(
        metas_hbm=saved["metas"], turned_hbm=saved["turned"], dat_hbm=saved["dat"], att_hbm=saved["att"],
        lse_hbm=saved["lse"], kv_hbm=saved["kv"], grad_hbm=saved["grad_hidden"], hid_1_hbm=saved["hid_1"],
        hid_0_hbm=saved["hid"], branch_hbm=saved["branch"], slope_hbm=saved["slope"], silu_hbm=saved["silu"],
        middle_hbm=saved["middle"],
    )
    bottom = backward(1, tables | routing | dict(small_before=saved["small"]), weights | operands, nb)
    return final(tables, saved, saved, bottom, weights, mesh_sizes)


def solution(mesh):
    sizes = (mesh.shape["blk"], mesh.shape["dp"])
    return jax.shard_map(
        functools.partial(local, mesh_sizes=sizes),
        mesh=mesh,
        in_specs=(
            P("dp", "blk", None),
            P("dp", "blk"),
            P("dp", "blk"),
            P(),
            P(),
            P(),
            P(),
            P(),
            P(),
            P(),
            P(),
            P(),
            P(),
            P("dp", "blk", None),
        ),
        out_specs=(
            P("dp", "blk", None),
            P("dp", "blk", None),
            P("blk"),
            P("blk"),
            P("blk", None),
            P("blk", None),
            P("blk", None),
            P("blk", None),
            P("blk", None),
            P("blk", None),
            P("blk", None),
            P("blk", None),
        ),
        check_vma=False,
    )
```

```python
import functools
import itertools
import math
import types

import jax
import jax.numpy as jnp
from jax import lax
from jax.experimental import pallas as pl
from jax.experimental.pallas import tpu as pltpu
from jax.sharding import PartitionSpec as P

QUERY_HEADS = 15
KEY_VALUE_HEADS = 5
HEAD_DIMENSION = 64
RECUR = 2
HEAD_SHARE = QUERY_HEADS // KEY_VALUE_HEADS
KEYS_WIDTH = KEY_VALUE_HEADS * HEAD_DIMENSION
PAIR = 2 * HEAD_DIMENSION
FF_TILE = 512
UNIT_COLUMNS = 256
ROW_CHUNK = 32
KEY_CHUNK = 64
QUERY_CHUNK = 64
VMEM_LIMIT = 63 * 1024 * 1024

epsilon = 1e-05
masked_score = -1e30
low = jnp.bfloat16


def frequencies(head_size):
    return jnp.exp(
        jnp.arange(head_size // 2, dtype=jnp.float32) * (-2.0 * math.log(10000.0) / head_size)
    )


def rms_scale(values):
    return lax.rsqrt(jnp.mean(values * values, axis=-1, keepdims=True) + epsilon)


def plain_dot(left, right):
    return jnp.dot(left, right, preferred_element_type=jnp.float32)


def bits_of(number, count):
    return tuple((number >> (count - 1 - at)) & 1 for at in range(count))


def bit_of(position, bit):
    return lax.rem(position // (1 << bit), 2)


def block_bits(block, m):
    return tuple(bit_of(block, bit) for bit in range(m - 1, -1, -1))


def flipped(position, bit):
    return position + (1 << bit) * (1 - 2 * bit_of(position, bit))


def remote(source, target, sems, at, device):
    return pltpu.make_async_remote_copy(
        src_ref=source,
        dst_ref=target,
        send_sem=sems[0].at[at],
        recv_sem=sems[1].at[at],
        device_id=device,
        device_id_type=pl.DeviceIdType.MESH,
    )


def greet(partners):
    barrier = pltpu.get_barrier_semaphore()
    for partner in partners:
        pl.semaphore_signal(barrier, inc=1, device_id=partner, device_id_type=pl.DeviceIdType.MESH)
    pl.semaphore_wait(barrier, len(partners))


def head_rows(group, member):
    head = group * HEAD_SHARE + member
    return pl.ds(pl.multiple_of(head * HEAD_DIMENSION, HEAD_DIMENSION), HEAD_DIMENSION)


def as_column(row):
    wide = jnp.broadcast_to(row.astype(jnp.float32), (8, row.shape[1]))
    return wide.T[:, 0:1]


def fill_bias(bias, metas, query_segments, level, blk, m, piece):
    key_at = lax.broadcasted_iota(jnp.int32, (piece, piece), 0)
    query_at = lax.broadcasted_iota(jnp.int32, (piece, piece), 1)

    @pl.loop(0, blk + 1)
    def _(block):
        columns = metas[block_bits(block, m)].T
        live = jnp.where(columns[:, 1:2] > level, columns[:, 0:1], -1.0)
        shift = (blk - block) * piece
        allowed = (live == query_segments) & (key_at <= query_at + shift) | (key_at == query_at + shift)
        bias[block] = jnp.where(allowed, 0.0, masked_score)


def fill_bias_by_rows(bias, metas, level, blk, m, piece):
    query_at = lax.broadcasted_iota(jnp.int32, (piece, piece), 0)
    key_at = lax.broadcasted_iota(jnp.int32, (piece, piece), 1)
    query_segments = metas[block_bits(blk, m)].T[:, 0:1]

    @pl.loop(0, blk + 1)
    def _(block):
        meta = metas[block_bits(block, m)]
        live = jnp.where(meta[1:2, :] > level, meta[0:1, :], -1.0)
        shift = (blk - block) * piece
        allowed = (live == query_segments) & (key_at <= query_at + shift) | (key_at == query_at + shift)
        bias[block] = jnp.where(allowed, 0.0, masked_score).astype(bias.dtype)


def spec(memory):
    return pl.BlockSpec(memory_space=memory)


def shaped(entry):
    return jax.ShapeDtypeStruct(*entry)


def spaces(entries):
    return [pltpu.VMEM(*entry) for entry in entries]


def dma_semaphores(*shapes):
    return [pltpu.SemaphoreType.DMA(shape) for shape in shapes]


class Piece:
    def __init__(self, at, kept_at, slot, flavour, family, sems, bits):
        self.at, self.kept_at, self.slot, self.family, self.sems = at, kept_at, slot, family, sems
        self.m, self.n = bits
        left = list(range(self.m - 1, -1, -1))
        self.order = []
        for stage in range(self.m):
            place = len(left) - 1 if stage == 0 or flavour == 0 else 0
            self.order.append((left.pop(place), place, len(left)))
        self.last = self.m + self.n
        self.blk = lax.axis_index("blk")
        self.dp = lax.axis_index("dp") if self.n else None

    def half(self, ref, side):
        rows, columns = self.family.shape
        if self.family.split == 0:
            return ref.at[pl.ds(pl.multiple_of(side * (rows // 2), rows // 2), rows // 2), :]
        return ref.at[:, pl.ds(pl.multiple_of(side * (columns // 2), columns // 2), columns // 2)]

    def held(self, stage):
        if stage == 0:
            return self.family.part, self.slot
        return self.family.blk[stage - 1], self.kept_at

    def copy(self, stage):
        m, family = self.m, self.family
        if stage < m:
            bit, place, others = self.order[stage]
            ref, index = self.held(stage)
            chosen = [slice(None)] * (others + 1)
            chosen[place] = 1 - bit_of(self.blk, bit)
            source = ref.at[(index, *chosen)]
            target = family.blk[stage].at[self.kept_at]
            device = {"blk": flipped(self.blk, bit)}
        elif stage < self.last:
            bit = stage - m
            if bit == 0:
                source = self.half(family.blk[m - 1].at[self.kept_at], 1 - bit_of(self.dp, 0))
            else:
                source = family.dp[bit - 1].at[self.kept_at]
            target = family.dp[bit].at[self.kept_at]
            device = {"dp": flipped(self.dp, bit)}
        else:
            source = self.half(family.out.at[self.kept_at], bit_of(self.dp, 0))
            target = source
            device = {"dp": flipped(self.dp, 0)}
        return remote(source, target, self.sems, (self.at, stage), device)

    def start(self, stage):
        self.copy(stage).start()

    def finish(self, stage):
        m, family = self.m, self.family
        self.copy(stage).wait_recv()
        if stage < m:
            bit, place, others = self.order[stage]
            ref, index = self.held(stage)
            for combo in itertools.product(range(2), repeat=others):
                chosen = list(combo)
                chosen.insert(place, bit_of(self.blk, bit))
                into = family.blk[stage].at[(self.kept_at, *combo)]
                self.add(into, into, ref.at[(index, *chosen)])
            if stage == 0:
                self.copy(0).wait_send()
        elif stage < self.last:
            bit = stage - m
            got = family.dp[bit].at[self.kept_at]
            if bit == 0:
                own = self.half(family.blk[m - 1].at[self.kept_at], bit_of(self.dp, 0))
            else:
                own = family.dp[bit - 1].at[self.kept_at]
            into = got
            if stage == self.last - 1:
                into = self.half(family.out.at[self.kept_at], bit_of(self.dp, 0))
            self.add(into, got, own)

    def add(self, into, left, right):
        into[...] = left[...] + right[...]

    def drained(self, stages):
        for stage in stages:
            self.copy(stage).wait_send()


def chunks(total, size):
    return [slice(first, min(first + size, total)) for first in range(0, total, size)]


def turn_into(target, source, column=0):
    for part in chunks(source.shape[0], 128):
        target[:, column + part.start:column + part.stop] = source[part, :].T


def turn_rows_into(target, source):
    for part in chunks(source.shape[1], 128):
        target[part, :] = source[:, part].T


def fold_rows(values):
    return jnp.sum(values.reshape(values.shape[0] // 8, 8, values.shape[1]), axis=0)


def row_loop(rows, body):
    @pl.loop(0, rows // ROW_CHUNK)
    def _(index):
        body(pl.ds(pl.multiple_of(index * ROW_CHUNK, ROW_CHUNK), ROW_CHUNK))


def rope_head(head, cosine, sine):
    first, second = head[:HEAD_DIMENSION // 2], head[HEAD_DIMENSION // 2:]
    return jnp.concatenate([first * cosine - second * sine, second * cosine + first * sine], axis=0)


def feed_forward_backward(at, level, gradient):
    tiles = at.w_gate.shape[1] // FF_TILE
    piece = at.dffn.shape[0]
    column = at.router[level:level + 1, :].astype(jnp.float32)
    gain = at.norms[1:2, :].astype(jnp.float32)
    at.row_sums[...] = jnp.zeros_like(at.row_sums)

    def prologue(rows):
        hidden, grad = at.hid_level[rows, :], gradient[rows, :]
        active = at.depth_column[rows, :] > float(level)
        chosen = jax.nn.sigmoid(jnp.sum(hidden * column, axis=1, keepdims=True))
        dbranch = jnp.where(active, chosen, 0.0) * grad
        dchosen = jnp.where(active, jnp.sum(grad * at.branch_level[rows, :], axis=1, keepdims=True), 0.0)
        dlogit = dchosen * chosen * (1.0 - chosen)
        at.row_sums[...] += fold_rows(hidden * dlogit)
        at.dbranch[rows, :] = dbranch
        at.dffn[rows, :] = dbranch.astype(low)
        at.grad_hidden[rows, :] = grad + dlogit * column

    row_loop(piece, prologue)
    at.small[2 + level:3 + level, :] = jnp.sum(at.row_sums[...], axis=0, keepdims=True)

    def dinner_into(tile):
        at.first[tile % 2] = plain_dot(at.dffn[...], at.w_down[:, tile * FF_TILE:(tile + 1) * FF_TILE])

    dinner_into(0)
    for tile in range(tiles):
        if tile + 1 < tiles:
            dinner_into(tile + 1)
        columns = slice(tile * FF_TILE, (tile + 1) * FF_TILE)
        for rows in chunks(piece, ROW_CHUNK):
            dinner = at.first[tile % 2, rows, :]
            dgate = (dinner * at.slope_level[rows, columns].astype(jnp.float32)).astype(low)
            dup = (dinner * at.silu_level[rows, columns].astype(jnp.float32)).astype(low)
            at.dgate[rows, columns] = dgate
            at.dup[rows, columns] = dup
        turn_rows_into(at.dgate_turned, at.dgate.at[:, columns])
        turn_rows_into(at.dup_turned, at.dup.at[:, columns])
        for rows in chunks(at.w_gate.shape[0], 240):
            share = plain_dot(at.w_gate[rows, columns], at.dgate_turned[...])
            share = share + plain_dot(at.w_up[rows, columns], at.dup_turned[...])
            if tile == 0:
                at.dnorm_turned[rows, :] = share
            else:
                at.dnorm_turned[rows, :] += share
    turn_into(at.dbuffer, at.dnorm_turned)
    at.row_sums[...] = jnp.zeros_like(at.row_sums)
    lead = at.far.shape[1] - at.dffn.shape[1]

    def epilogue(rows):
        dnorm, middle = at.dbuffer[rows, :], at.middle_level[rows, :]
        scale = rms_scale(middle)
        weighted = dnorm * gain
        dmiddle = scale * weighted - middle * (scale * scale * scale) * jnp.mean(
            weighted * middle, axis=-1, keepdims=True
        )
        at.row_sums[...] += fold_rows(dnorm * middle * scale)
        at.grad_hidden[rows, :] += dmiddle
        dattn = (at.dbranch[rows, :] + dmiddle).astype(low)
        at.flat[rows, :] = dattn
        at.far[rows, :lead] = jnp.zeros((ROW_CHUNK, lead), low)
        at.far[rows, lead:] = dattn

    row_loop(piece, epilogue)
    at.small[1:2, :] += jnp.sum(at.row_sums[...], axis=0, keepdims=True)
    turn_rows_into(at.flat_turned, at.flat)
    for rows in chunks(at.w_out.shape[0], 240):
        at.dat[rows, :] = plain_dot(at.w_out[rows, :], at.flat_turned[...]).astype(low)


def feed_forward_buffers(piece, width, hidden_units):
    rows, hidden = ((piece, width), jnp.float32), ((piece, hidden_units), low)
    return dict(
        w_down=((width, hidden_units), low), w_gate=((width, hidden_units), low), w_up=((width, hidden_units), low),
        w_out=((width, width), low), dbranch=rows, dbuffer=rows, dnorm_turned=((width, piece), jnp.float32),
        flat=((piece, width), low), flat_turned=((width, piece), low), first=((2, piece, FF_TILE), jnp.float32),
        dgate=hidden, dup=hidden, dgate_turned=((FF_TILE, piece), low), dup_turned=((FF_TILE, piece), low),
        row_sums=((8, width), jnp.float32), depth_column=((piece, 1), jnp.float32),
    )


def forward_kernel(sizes, names, *refs):
    m, piece = sizes
    at = types.SimpleNamespace(**dict(zip(names, refs)))
    blk = lax.axis_index("blk")
    mine = block_bits(blk, m)
    kv, metas = at.kv, at.metas
    width = at.flat.shape[1]
    weights = (
        (at.key_weight_hbm, at.key_weight), (at.value_weight_hbm, at.value_weight), (at.w_query_hbm, at.w_query),
        (at.w_out_hbm, at.w_out), (at.w_gate_hbm, at.w_gate), (at.w_up_hbm, at.w_up), (at.w_down_hbm, at.w_down),
    )
    loads = [pltpu.make_async_copy(*pair, at.load_sems.at[index]) for index, pair in enumerate(weights)]
    for load in loads:
        load.start()
    saved = (
        (at.normed, at.normed_out), (at.turned, at.turned_out), (kv, at.kv_out), (at.lse, at.lse_out),
        (at.att, at.att_out), (at.nffn, at.nffn_out), (at.inner, at.inner_out),
    )

    def save(index, level):
        return pltpu.make_async_copy(
            saved[index][0].at[level], saved[index][1].at[level], at.save_sems.at[index, level]
        )

    first = (
        (at.hid.at[0], at.hid_out), (at.middle.at[0], at.middle_out), (at.silu.at[0], at.silu_out),
        (at.slope.at[0], at.slope_out), (at.branch.at[0], at.branch_out), (metas, at.metas_out),
        (at.far, at.far_out), (at.dat, at.dat_out), (at.dffn, at.dffn_out), (at.dgate, at.dgate_out), (at.dup, at.dup_out),
        (at.hid.at[1], at.hid_1_out),
    )
    late = [pltpu.make_async_copy(*pair, at.late_sems.at[index]) for index, pair in enumerate(first)]
    segment_row = at.segments[...].astype(jnp.float32)
    at.depth_column[...] = as_column(at.depths[...])
    metas[mine] = jnp.concatenate(
        [segment_row, at.depths[...].astype(jnp.float32), jnp.zeros((6, piece), jnp.float32)], axis=0
    )
    greet([{"blk": flipped(blk, bit)} for bit in range(m)])

    def place(known):
        return tuple(slice(None) if bit in known else mine[m - 1 - bit] for bit in range(m - 1, -1, -1))

    orders = (list(range(1, m)), list(range(m - 1, 0, -1)))
    kv_sems = (at.kv_send, at.kv_recv)

    def kv_copies(level, group, stage):
        if stage == m - 1:
            ref = kv.at[(level, group, *place(range(1, m)))]
            return [remote(ref, ref, kv_sems, (level, group, 2 * stage), {"blk": flipped(blk, 0)})]
        copies = []
        for side, order in enumerate(orders):
            rows = pl.ds(side * (piece // 2), piece // 2)
            ref = kv.at[(level, group, *place(order[:stage]), rows)]
            copies.append(remote(ref, ref, kv_sems, (level, group, 2 * stage + side), {"blk": flipped(blk, order[stage])}))
        return copies

    def kv_advance(level, group, stage):
        if stage > 0:
            for copy in kv_copies(level, group, stage - 1):
                copy.wait_recv()
        if stage < m:
            for copy in kv_copies(level, group, stage):
                copy.start()

    def meta_copy(stage):
        bits = list(range(1, m)) + [0]
        ref = metas.at[place(bits[:stage])]
        return remote(ref, ref, (at.meta_send, at.meta_recv), stage, {"blk": flipped(blk, bits[stage])})

    meta_copy(0).start()
    cosine, sine = at.cosines[...], at.sines[...]
    gain_attn, gain_ffn = at.norms[0:1, :].astype(jnp.float32), at.norms[1:2, :].astype(jnp.float32)
    routers = at.router[...].astype(jnp.float32)
    for part in chunks(width, 128):
        at.hid[0, :, part] = at.tokens[part, :].T.astype(jnp.float32)
    late[0].start()
    at.query_pad[HEAD_DIMENSION:, :] = jnp.zeros_like(at.query_pad[HEAD_DIMENSION:, :])

    @pl.loop(0, RECUR)
    def _(level):
        def norm_rows(rows):
            hidden = at.hid[level, rows, :]
            at.flat[rows, :] = (hidden * rms_scale(hidden) * gain_attn).astype(low)

        row_loop(piece, norm_rows)
        turn_rows_into(at.normed.at[level], at.flat)

        @pl.when(level == 0)
        def _():
            for load in loads[:2]:
                load.wait()

        at.dnorm_turned[:KEYS_WIDTH, :] = plain_dot(at.key_weight[...], at.normed[level])
        at.dnorm_turned[KEYS_WIDTH:2 * KEYS_WIDTH, :] = plain_dot(at.value_weight[...], at.normed[level])
        for group in range(KEY_VALUE_HEADS):
            key_at, value_at = group * HEAD_DIMENSION, KEYS_WIDTH + group * HEAD_DIMENSION
            keys = rope_head(at.dnorm_turned[key_at:key_at + HEAD_DIMENSION, :], cosine, sine)
            values = at.dnorm_turned[value_at:value_at + HEAD_DIMENSION, :]
            kv[(level, group, *mine)] = jnp.concatenate([keys, values], axis=0).T.astype(low)
            kv_advance(level, group, 0)

        @pl.when(level == 0)
        def _():
            loads[2].wait()
            for stage in range(1, m - 1):
                meta_copy(stage - 1).wait_recv()
                meta_copy(stage).start()

        at.dbuffer[...] = plain_dot(at.flat[...], at.w_query[...])
        for part in chunks(width, PAIR):
            both = at.dbuffer[:, part].T
            for start in range(0, part.stop - part.start, HEAD_DIMENSION):
                head = rope_head(both[start:start + HEAD_DIMENSION], cosine, sine) * HEAD_DIMENSION ** (-0.5)
                at.turned[level, part.start + start:part.start + start + HEAD_DIMENSION, :] = head.astype(low)

        @pl.when(level == 0)
        def _():
            for stage in range(max(1, m - 1), m):
                meta_copy(stage - 1).wait_recv()
                meta_copy(stage).start()

        for stage in range(1, m):
            for group in range(m - stage):
                kv_advance(level, group, stage)

        @pl.when(level == 0)
        def _():
            meta_copy(m - 1).wait_recv()
            late[5].start()

        fill_bias(at.bias, metas, segment_row, level.astype(jnp.float32), blk, m, piece)

        @pl.loop(0, KEY_VALUE_HEADS)
        def _(group):
            for stage in range(1, m):
                @pl.when(group + m - stage < KEY_VALUE_HEADS)
                def _():
                    kv_advance(level, group + m - stage, stage)

            kv_advance(level, group, m)
            for member in range(HEAD_SHARE):
                at.query_pad[:HEAD_DIMENSION, member * piece:(member + 1) * piece] = at.turned[level, head_rows(group, member), :]
            at.top[...] = jnp.full_like(at.top, masked_score)
            at.total[...] = jnp.zeros_like(at.total)

            @pl.loop(0, blk + 1)
            def _(step):
                block = blk - step
                rows = kv[(level, group, *block_bits(block, m))]
                ones = jnp.ones((16, piece), low)
                left = jnp.concatenate([rows.T[HEAD_DIMENSION:], ones], axis=0)
                for member in range(HEAD_SHARE):
                    lanes = slice(member * piece, (member + 1) * piece)
                    before = at.top[0:1, lanes]
                    highest = None
                    for part in chunks(piece, KEY_CHUNK):
                        scores = plain_dot(rows[part], at.query_pad[:, lanes]) + at.bias[block, part, :]
                        at.scores[member, part, :] = scores
                        peak = jnp.max(scores.reshape(KEY_CHUNK // 8, 8, piece), axis=0)
                        highest = peak if highest is None else jnp.maximum(highest, peak)
                    after = jnp.maximum(before, jnp.max(highest, axis=0, keepdims=True))
                    shrink = jnp.exp(before - after)
                    at.top[0:1, lanes] = after
                    for part in chunks(piece, KEY_CHUNK):
                        at.raised[member, part, :] = jnp.exp(at.scores[member, part, :] - after).astype(low)
                    at.total[:, lanes] = at.total[:, lanes] * shrink + plain_dot(left, at.raised[member])

            at.lse[level, pl.ds(group, 1), :] = at.top[0:1, :] + jnp.log(at.total[HEAD_DIMENSION:HEAD_DIMENSION + 1, :])
            for member in range(HEAD_SHARE):
                lanes = slice(member * piece, (member + 1) * piece)
                out = at.total[:HEAD_DIMENSION, lanes] / at.total[HEAD_DIMENSION:HEAD_DIMENSION + 1, lanes]
                at.att[level, head_rows(group, member), :] = out.astype(low)

        for index in range(5):
            save(index, level).start()

        @pl.when(level == 0)
        def _():
            loads[3].wait()

        turn_into(at.flat, at.att.at[level])
        at.branch[level] = plain_dot(at.flat[...], at.w_out[...])

        def middle_rows(rows):
            mid = at.hid[level, rows, :] + at.branch[level, rows, :]
            at.middle[level, rows, :] = mid
            at.flat[rows, :] = (mid * rms_scale(mid) * gain_ffn).astype(low)

        row_loop(piece, middle_rows)
        turn_rows_into(at.nffn.at[level], at.flat)
        save(5, level).start()

        @pl.when(level == 0)
        def _():
            loads[4].wait()
            loads[5].wait()

        def gate_up_into(tile):
            columns = slice(tile * FF_TILE, (tile + 1) * FF_TILE)
            at.first[tile % 2] = plain_dot(at.flat[...], at.w_gate[:, columns])
            at.second[tile % 2] = plain_dot(at.flat[...], at.w_up[:, columns])

        tiles = at.w_gate.shape[1] // FF_TILE
        gate_up_into(0)
        for tile in range(tiles):
            if tile + 1 < tiles:
                gate_up_into(tile + 1)
            columns = slice(tile * FF_TILE, (tile + 1) * FF_TILE)
            for rows in chunks(piece, ROW_CHUNK):
                gate_pre, up_pre = at.first[tile % 2, rows, :], at.second[tile % 2, rows, :]
                opened = jax.nn.sigmoid(gate_pre)
                passed = gate_pre * opened
                at.silu[level, rows, columns] = passed.astype(low)
                at.slope[level, rows, columns] = (up_pre * (opened + passed - passed * opened)).astype(low)
                at.mixed[rows, :] = (passed * up_pre).astype(low)
            turn_rows_into(at.inner.at[level, columns], at.mixed)

        save(6, level).start()

        @pl.when(level == 0)
        def _():
            loads[6].wait()

        at.dnorm_turned[...] = plain_dot(at.w_down[...], at.inner[level])
        for part in chunks(width, 128):
            at.branch[level, :, part] += at.dnorm_turned[part, :].T
        column = jnp.where(level == 0, routers[0:1, :], routers[1:2, :])

        def next_rows(rows):
            hidden = at.hid[level, rows, :]
            logit = jnp.sum(hidden * column, axis=1, keepdims=True)
            active = at.depth_column[rows, :] > level.astype(jnp.float32)
            weight = jnp.where(active, jax.nn.sigmoid(logit), 0.0)
            at.hid[level + 1, rows, :] = hidden + weight * at.branch[level, rows, :]

        row_loop(piece, next_rows)

        @pl.when(level == 0)
        def _():
            for copy in late[1:5]:
                copy.start()

    turn_rows_into(at.hidden_out, at.hid.at[RECUR])
    top = RECUR - 1
    at.hid_level, at.branch_level, at.middle_level = at.hid.at[top], at.branch.at[top], at.middle.at[top]
    at.silu_level, at.slope_level = at.silu.at[top], at.slope.at[top]
    at.small[...] = jnp.zeros_like(at.small)
    for part in chunks(width, 128):
        at.dbuffer[:, part] = at.cotangent[part, :].T.astype(jnp.float32)
    feed_forward_backward(at, top, at.dbuffer)
    for copy in late[6:]:
        copy.start()
    for stage in range(m):
        meta_copy(stage).wait_send()
    for level in range(RECUR):
        for group in range(KEY_VALUE_HEADS):
            for stage in range(m):
                for copy in kv_copies(level, group, stage):
                    copy.wait_send()
        for index in range(len(saved)):
            save(index, level).wait()
    for copy in late:
        copy.wait()


def far_width(width):
    return 2 * width + 2 * KEYS_WIDTH - 1536


def forward(small, weights, nb):
    m = nb.bit_length() - 1
    width, piece = small["tokens"].shape
    hidden_units = weights["w_gate_hbm"].shape[1]
    blocks, wide = (2,) * m, HEAD_SHARE * piece
    rows, turned = ((piece, width), jnp.float32), ((RECUR, width, piece), low)
    hidden = ((piece, hidden_units), low)
    saved = dict(
        normed=turned, turned=turned, kv=((RECUR, KEY_VALUE_HEADS, *blocks, piece, PAIR), low),
        lse=((RECUR, 8, wide), jnp.float32), att=turned, nffn=turned, inner=((RECUR, hidden_units, piece), low),
        metas=((*blocks, 8, piece), jnp.float32), far=((piece, far_width(width)), low), dat=((width, piece), low),
        dffn=((piece, width), low), dgate=hidden, dup=hidden,
    )
    first = dict(hid=rows, middle=rows, silu=hidden, slope=hidden, branch=rows)
    outs = dict(hidden_out=((width, piece), jnp.float32), grad_hidden=rows, small=((8, width), jnp.float32))
    anywhere = {name + "_out": entry for name, entry in (saved | first | dict(hid_1=rows)).items()}
    both = {name: ((RECUR, *shape), dtype) for name, (shape, dtype) in first.items()}
    buffers = {name[:-4]: (array.shape, array.dtype) for name, array in weights.items()} | saved | both
    buffers |= feed_forward_buffers(piece, width, hidden_units) | dict(
        hid=((RECUR + 1, piece, width), jnp.float32), second=((2, piece, FF_TILE), jnp.float32),
        mixed=((piece, FF_TILE), low), bias=((nb, piece, piece), jnp.float32), query_pad=((PAIR, wide), low),
        top=((8, wide), jnp.float32), total=((HEAD_DIMENSION + 16, wide), jnp.float32),
        scores=((HEAD_SHARE, piece, piece), jnp.float32), raised=((HEAD_SHARE, piece, piece), low),
    )
    semaphores = dict(
        load_sems=(7,), save_sems=(7, RECUR), late_sems=(12,), kv_send=(RECUR, KEY_VALUE_HEADS, 2 * m),
        kv_recv=(RECUR, KEY_VALUE_HEADS, 2 * m), meta_send=(m,), meta_recv=(m,),
    )
    results = pl.pallas_call(
        functools.partial(forward_kernel, (m, piece), (*small, *weights, *outs, *anywhere, *buffers, *semaphores)),
        out_shape=[shaped(entry) for entry in (outs | anywhere).values()],
        in_specs=[spec(pltpu.VMEM)] * len(small) + [spec(pl.ANY)] * len(weights),
        out_specs=[spec(pltpu.VMEM)] * len(outs) + [spec(pl.ANY)] * len(anywhere),
        scratch_shapes=spaces(buffers.values()) + dma_semaphores(*semaphores.values()),
        compiler_params=pltpu.CompilerParams(
            collective_id=1, has_side_effects=True, vmem_limit_bytes=VMEM_LIMIT
        ),
        cost_estimate=pl.CostEstimate(
            flops=3 * RECUR * piece * width * 10240, bytes_accessed=48 * 1024 * 1024, transcendentals=0
        ),
        name="forward_levels",
    )(*small.values(), *weights.values())
    return dict(zip((*outs, *(name[:-4] for name in anywhere)), results))


class AttentionBackward:
    def __init__(self, at, m, piece, level):
        self.at, self.m, self.piece, self.level = at, m, piece, level
        self.blk = lax.axis_index("blk")
        self.family = types.SimpleNamespace(part=at.part, blk=at.halves, dp=(), out=None, shape=(HEAD_DIMENSION, piece), split=0)

    def pieces(self, group):
        sems = (self.at.kv_send, self.at.kv_recv)
        return [
            Piece(2 * group + side, 2 * group + side, 2 * group + side, side, self.family, sems, (self.m, 0))
            for side in range(2)
        ]

    def move(self, group, stage):
        for piece_of in self.pieces(group):
            piece_of.finish(stage)
            if stage + 1 < self.m:
                piece_of.start(stage + 1)

    def begin(self):
        at = self.at
        fill_bias_by_rows(at.bias, at.metas, float(self.level), self.blk, self.m, self.piece)
        at.mixed_rows[...] = jnp.zeros_like(at.mixed_rows)

    def group(self, group):
        at, m, piece, blk = self.at, self.m, self.piece, self.blk
        log_total = at.lse[pl.ds(group, 1), :]
        for member in range(HEAD_SHARE):
            rows = head_rows(group, member)
            here = slice(member * piece, (member + 1) * piece)
            queries, dat = at.turned[rows, :], at.dat_turned[rows, :]
            at.query_part[:, here] = queries
            at.dat_part[:, here] = dat
            queries, dats = queries.T, dat.T
            for part in chunks(piece, QUERY_CHUNK):
                first = 2 * (member * piece + part.start)
                at.mixed_rows[first:first + QUERY_CHUNK, :HEAD_DIMENSION] = queries[part]
                at.mixed_rows[first + QUERY_CHUNK:first + 2 * QUERY_CHUNK, HEAD_DIMENSION:] = dats[part]
            carried = jnp.sum(
                dat.astype(jnp.float32) * at.att_turned[rows, :].astype(jnp.float32), axis=0, keepdims=True
            )
            at.carried[here, :] = jnp.broadcast_to(carried, (128, piece)).T
            at.log_total[here, :] = jnp.broadcast_to(log_total[:, here], (128, piece)).T
        at.dq_sum[...] = jnp.zeros_like(at.dq_sum)

        def over_keys(column):
            return jnp.concatenate([column] * (piece // 128), axis=1)

        @pl.loop(0, blk + 1)
        def _(block):
            rows = at.kv[(group, *block_bits(block, m))]
            columns = rows.T
            for part in chunks(HEAD_SHARE * piece, QUERY_CHUNK):
                both = plain_dot(at.mixed_rows[2 * part.start:2 * part.stop, :], columns)
                inside = part.start % piece
                scores = both[:QUERY_CHUNK] + at.bias[block, inside:inside + QUERY_CHUNK, :].astype(jnp.float32)
                probability = jnp.exp(scores - over_keys(at.log_total[part, :]))
                dscores = probability * (both[QUERY_CHUNK:] - over_keys(at.carried[part, :]))
                at.probability[part, :] = probability.astype(low)
                at.dscores[part, :] = dscores.astype(low)
            at.part[(2 * group, *block_bits(block, m))] = plain_dot(at.query_part[...], at.dscores[...]).astype(low)
            at.part[(2 * group + 1, *block_bits(block, m))] = plain_dot(at.dat_part[...], at.probability[...]).astype(low)
            for part in chunks(HEAD_SHARE * piece, 256):
                at.dq_sum[part, :] += plain_dot(at.dscores[part, :], rows)

        @pl.loop(blk + 1, 1 << m)
        def _(block):
            for side in range(2):
                at.part[(2 * group + side, *block_bits(block, m))] = jnp.zeros((HEAD_DIMENSION, piece), low)

        for piece_of in self.pieces(group):
            piece_of.start(0)
        for member in range(HEAD_SHARE):
            turned = at.dq_sum[member * piece:(member + 1) * piece, :].T
            at.dq_turned[head_rows(group, member), :] = turned[:HEAD_DIMENSION]

    def follow(self, group):
        for stage in range(self.m - 1):
            earlier = group - 1 - stage
            if isinstance(group, int):
                if 0 <= earlier < KEY_VALUE_HEADS:
                    self.move(earlier, stage)
            else:
                @pl.when(earlier >= 0)
                def _():
                    self.move(earlier, stage)

    def queries(self, cosine, sine):
        at = self.at
        for head in range(QUERY_HEADS):
            rows = slice(head * HEAD_DIMENSION, (head + 1) * HEAD_DIMENSION)
            at.dq_low[rows, :] = rope_head(at.dq_turned[rows, :] * HEAD_DIMENSION ** (-0.5), cosine, -sine).astype(low)
        turn_into(at.near, at.dq_low, 2 * KEYS_WIDTH)
        at.dq_turned[...] = plain_dot(at.w_query[...], at.dq_low[...])
        turn_into(at.dnorm, at.dq_turned)

    def keys(self, cosine, sine):
        at, m = self.at, self.m
        filled = 2 * KEYS_WIDTH + QUERY_HEADS * HEAD_DIMENSION
        at.near[:, filled:] = jnp.zeros((self.piece, at.near.shape[1] - filled), low)
        for group in range(KEY_VALUE_HEADS):
            self.move(group, m - 1)
            rows = slice(group * HEAD_DIMENSION, (group + 1) * HEAD_DIMENSION)
            dkeys = at.halves[m - 1][2 * group].astype(jnp.float32)
            at.dk_low[rows, :] = rope_head(dkeys, cosine, -sine).astype(low)
            rows = slice(KEYS_WIDTH + group * HEAD_DIMENSION, KEYS_WIDTH + (group + 1) * HEAD_DIMENSION)
            at.dk_low[rows, :] = at.halves[m - 1][2 * group + 1]
        turn_into(at.near, at.dk_low)
        dkeys, dvalues = at.near[:, :KEYS_WIDTH], at.near[:, KEYS_WIDTH:2 * KEYS_WIDTH]
        at.dnorm[...] += plain_dot(dkeys, at.key_weight[...]) + plain_dot(dvalues, at.value_weight[...])

    def gradient(self, target, before):
        at = self.at
        gain = at.norms[0:1, :].astype(jnp.float32)
        at.row_sums[...] = jnp.zeros_like(at.row_sums)

        def rows_of(rows):
            dnorm, hidden = at.dnorm[rows, :], at.hid[rows, :]
            scale = rms_scale(hidden)
            weighted = dnorm * gain
            dhidden = scale * weighted - hidden * (scale * scale * scale) * jnp.mean(
                weighted * hidden, axis=-1, keepdims=True
            )
            at.row_sums[...] += fold_rows(dnorm * hidden * scale)
            target[rows, :] = before[rows, :] + dhidden

        row_loop(self.piece, rows_of)
        return jnp.sum(at.row_sums[...], axis=0, keepdims=True)

    def drained(self):
        for group in range(KEY_VALUE_HEADS):
            for piece_of in self.pieces(group):
                piece_of.drained(range(1, self.m))


def attention_buffers(nb, piece, width, bias_type):
    m, wide, heads = nb.bit_length() - 1, HEAD_SHARE * piece, 2 * KEY_VALUE_HEADS
    turned, weight = ((width, piece), low), ((KEYS_WIDTH, width), low)
    part, stat, square = ((HEAD_DIMENSION, wide), low), ((wide, 128), jnp.float32), ((wide, piece), low)
    buffers = dict(
        turned=turned, dat_turned=turned, att_turned=turned, kv=((KEY_VALUE_HEADS, *(2,) * m, piece, PAIR), low),
        lse=((8, wide), jnp.float32), metas=((*(2,) * m, 8, piece), jnp.float32), w_query=((width, width), low),
        key_weight=weight, value_weight=weight, dq_turned=((width, piece), jnp.float32), dq_low=turned,
        dk_low=((2 * KEYS_WIDTH, piece), low), bias=((nb, piece, piece), bias_type), query_part=part, dat_part=part,
        mixed_rows=((2 * wide, PAIR), low), log_total=stat, carried=stat, dq_sum=stat, probability=square,
        dscores=square, part=((heads, *(2,) * m, HEAD_DIMENSION, piece), low), dnorm=((piece, width), jnp.float32),
        hid=((piece, width), jnp.float32), row_sums=((8, width), jnp.float32),
    )
    for stage in range(m):
        buffers["half_%d" % stage] = ((heads, *(2,) * (m - 1 - stage), HEAD_DIMENSION, piece), low)
    return buffers


def backward_kernel(sizes, names, *refs):
    m, piece, level = sizes
    at = types.SimpleNamespace(**dict(zip(names, refs)))
    at.halves = [getattr(at, "half_%d" % stage) for stage in range(m)]
    at.near = at.near_out
    blk = lax.axis_index("blk")
    pairs = (
        (at.metas_hbm, at.metas), (at.turned_hbm.at[level], at.turned), (at.dat_hbm, at.dat_turned),
        (at.att_hbm.at[level], at.att_turned), (at.lse_hbm.at[level], at.lse), (at.kv_hbm.at[level], at.kv),
        (at.w_query_hbm, at.w_query), (at.key_weight_hbm, at.key_weight), (at.value_weight_hbm, at.value_weight),
        (at.grad_hbm, at.grad_hidden), (at.hid_1_hbm, at.hid),
        (at.hid_0_hbm, at.hid_level), (at.branch_hbm, at.branch_level), (at.w_down_hbm, at.w_down),
        (at.slope_hbm, at.slope_level), (at.silu_hbm, at.silu_level), (at.w_gate_hbm, at.w_gate), (at.w_up_hbm, at.w_up),
        (at.middle_hbm, at.middle_level), (at.w_out_hbm, at.w_out),
    )
    loads = [pltpu.make_async_copy(*pair, at.load_sems.at[index]) for index, pair in enumerate(pairs)]
    for load in loads:
        load.start()
    saves = [
        pltpu.make_async_copy(*pair, at.save_sems.at[index])
        for index, pair in enumerate(((at.dgate, at.dgate_out), (at.dup, at.dup_out)))
    ]
    greet([{"blk": flipped(blk, bit)} for bit in range(m)])
    work = AttentionBackward(at, m, piece, level)
    loads[0].wait()
    work.begin()
    for load in loads[1:6]:
        load.wait()

    @pl.loop(0, KEY_VALUE_HEADS)
    def _(group):
        work.group(group)
        work.follow(group)

    cosine, sine = at.cosines[...], at.sines[...]
    for virtual in range(KEY_VALUE_HEADS, KEY_VALUE_HEADS + m - 1):
        work.follow(virtual)
        if virtual == KEY_VALUE_HEADS:
            loads[6].wait()
            work.queries(cosine, sine)
    for load in loads[7:]:
        load.wait()
    work.keys(cosine, sine)
    at.small[...] = at.small_before[...]
    at.small[0:1, :] = work.gradient(at.dnorm, at.grad_hidden)
    at.depth_column[...] = as_column(at.depths[...])
    feed_forward_backward(at, level - 1, at.dnorm)
    for save in saves:
        save.start()
    work.drained()
    for save in saves:
        save.wait()


def backward(level, small, operands, nb):
    m = nb.bit_length() - 1
    piece, width = operands["grad_hbm"].shape
    hidden_units = operands["w_gate_hbm"].shape[1]
    rows, flat, hidden = ((piece, width), jnp.float32), ((piece, width), low), ((piece, hidden_units), low)
    outs = dict(
        grad_hidden=rows, small=((8, width), jnp.float32), near_out=((piece, 1792), low), dffn=flat,
        dat=((width, piece), low), far=((piece, far_width(width)), low),
    )
    anywhere = dict(dgate_out=hidden, dup_out=hidden)
    buffers = attention_buffers(nb, piece, width, jnp.float32) | feed_forward_buffers(piece, width, hidden_units)
    buffers |= dict(hid_level=rows, branch_level=rows, middle_level=rows, slope_level=hidden, silu_level=hidden)
    sums = (2 * KEY_VALUE_HEADS, m)
    semaphores = dict(load_sems=(20,), save_sems=(2,), kv_send=sums, kv_recv=sums)
    results = pl.pallas_call(
        functools.partial(
            backward_kernel, (m, piece, level), (*small, *operands, *outs, *anywhere, *buffers, *semaphores)
        ),
        out_shape=[shaped(entry) for entry in (outs | anywhere).values()],
        in_specs=[spec(pltpu.VMEM)] * len(small) + [spec(pl.ANY)] * len(operands),
        out_specs=[spec(pltpu.VMEM)] * len(outs) + [spec(pl.ANY)] * len(anywhere),
        scratch_shapes=spaces(buffers.values()) + dma_semaphores(*semaphores.values()),
        compiler_params=pltpu.CompilerParams(
            collective_id=2, has_side_effects=True, vmem_limit_bytes=VMEM_LIMIT
        ),
        cost_estimate=pl.CostEstimate(
            flops=2 * piece * width * 20000, bytes_accessed=32 * 1024 * 1024, transcendentals=0
        ),
        name="backward_level",
    )(*small.values(), *operands.values())
    return dict(zip((*outs, *anywhere), results))


WIDE_SLOTS, DOWN_SLOTS = 4, 2


def final_kernel(sizes, names, *refs):
    nb, m, n, piece, rows, padded, near_width = sizes
    at = types.SimpleNamespace(**dict(zip(names, refs)))
    at.halves = [getattr(at, "half_%d" % stage) for stage in range(m)]
    blk, dp = lax.axis_index("blk"), lax.axis_index("dp")
    at.near = at.gate_side.at[pl.ds(0, piece), pl.ds(0, near_width)]
    counter = itertools.count()

    def load(source, target):
        return pltpu.make_async_copy(source, target, at.load_sems.at[next(counter)])

    def both_lanes(ref, target):
        return [load(ref.at[level], target.at[:, pl.ds(level * piece, piece)]) for level in range(RECUR)]

    def both_rows(low_ref, deep_ref, target, width):
        pairs = ((low_ref, 0), (deep_ref, piece))
        return [load(ref, target.at[pl.ds(first, piece), pl.ds(0, width)]) for ref, first in pairs]

    hidden_units, width = at.gate_side.shape[1], at.dffn.shape[1]
    far_lanes = at.far_0_hbm.shape[1]
    loads = types.SimpleNamespace(
        nffn=both_lanes(at.nffn_hbm, at.left),
        dgate=both_rows(at.dgate_0_hbm, at.dgate_1_hbm, at.gate_side, hidden_units),
        inner=both_lanes(at.inner_hbm, at.inner),
        dffn=both_rows(at.dffn_0_hbm, at.dffn_1_hbm, at.dffn, width),
        metas=[load(at.metas_hbm, at.metas)],
        heads=[
            load(at.turned_hbm.at[0], at.turned), load(at.dat_hbm, at.dat_turned), load(at.att_hbm.at[0], at.att_turned),
            load(at.lse_hbm.at[0], at.lse), load(at.kv_hbm.at[0], at.kv),
        ],
        dup=both_rows(at.dup_0_hbm, at.dup_1_hbm, at.up_side, hidden_units),
        w_query=[load(at.w_query_hbm, at.w_query)],
        rest=[
            load(at.key_weight_hbm, at.key_weight), load(at.value_weight_hbm, at.value_weight),
            load(at.hid_hbm, at.hid), load(at.grad_hbm, at.grad),
        ],
        attended=both_lanes(at.attended_hbm, at.left_attended),
    )
    late = types.SimpleNamespace(
        near=[load(at.near_1_hbm, at.gate_side.at[pl.ds(piece, piece), pl.ds(0, near_width)])],
        far=both_rows(at.far_0_hbm, at.far_1_hbm, at.up_side, far_lanes),
        normed=both_lanes(at.normed_hbm, at.left),
    )

    def begin(copies):
        for copy in copies:
            copy.start()

    def ready(copies):
        for copy in copies:
            copy.wait()

    for copies in vars(loads).values():
        begin(copies)
    greet([{"blk": flipped(blk, bit)} for bit in range(m)] + [{"dp": flipped(dp, bit)} for bit in range(n)])

    down_rows = at.part_down.shape[-2]

    def family(name, shape, split):
        return types.SimpleNamespace(
            part=getattr(at, "part_" + name), out=getattr(at, "out_" + name), shape=shape, split=split,
            blk=[getattr(at, "blk_%s_%d" % (name, stage)) for stage in range(m)],
            dp=[getattr(at, "dp_%s_%d" % (name, stage)) for stage in range(n)],
        )

    wide = family("wide", (2 * padded, UNIT_COLUMNS), 1)
    down = family("down", (down_rows, width), 0)
    little = family("small", (16, 128), 0)
    sems = (at.send_sems, at.recv_sems)
    units = itertools.count()

    def unit(holder, index, flavour):
        return Piece(next(units), index, index % holder.part.shape[0], flavour, holder, sems, (m, n))

    pairs = [[unit(wide, index, 0), unit(down, index, 1)] for index in range(5)]
    pairs += [[unit(wide, index, 0), unit(wide, index + 1, 1)] for index in (5, 7, 9, 11)]
    pairs += [[unit(wide, 13, 0), unit(wide, 14, 1), unit(little, 0, 0)]]

    def compute_wide(index, slot):
        if index == 0:
            ready(loads.nffn)
            ready(loads.dgate)
        if index == 5:
            begin(late.near)
            ready(loads.dup)
        if index == 10:
            begin(late.far)
            begin(late.normed)
            ready(late.near)
            ready(late.normed)
            ready(loads.attended)
            ready(late.far)
        block, column = index // 5, (index % 5) * UNIT_COLUMNS
        second = 1280 + column
        upper_columns, lower_columns = slice(column, column + UNIT_COLUMNS), slice(second, second + UNIT_COLUMNS)
        if block < 2:
            right = at.gate_side if block == 0 else at.up_side
            upper = plain_dot(at.left[...], right[:, upper_columns])
            lower = plain_dot(at.left[...], right[:, lower_columns])
        else:
            upper = plain_dot(at.left[...], at.gate_side[:, upper_columns])
            lower = None
            if second < 1600:
                lower = plain_dot(at.left[...], at.gate_side[:, lower_columns])
            if second >= 1536:
                more = plain_dot(at.left_attended[...], at.up_side[:, second - 1536:second - 1536 + UNIT_COLUMNS])
                lower = more if lower is None else lower + more
        for target in range(nb):
            here = slice(target * padded, (target + 1) * padded)
            both = jnp.concatenate([upper[here], lower[here]], axis=0)
            at.part_wide[(slot, *bits_of(target, m))] = both.astype(low)

    def compute_down(index, slot):
        if index == 0:
            ready(loads.inner)
            ready(loads.dffn)
        firsts = [(target * 5 + index) * down_rows for target in range(nb)]
        left = jnp.concatenate([at.inner[first:first + down_rows, :] for first in firsts], axis=0)
        result = plain_dot(left, at.dffn[...])
        for target in range(nb):
            at.part_down[(slot, *bits_of(target, m))] = result[target * down_rows:(target + 1) * down_rows].astype(low)

    def compute_small():
        total = at.small_before[...]
        total = total + jnp.concatenate([at.gain_row[...], jnp.zeros((7, width), jnp.float32)], axis=0)
        at.part_small[...] = jnp.zeros_like(at.part_small)
        for target in range(nb):
            at.part_small[(0, *bits_of(target, m), slice(0, 8), slice(0, rows))] = total[:, target * rows:(target + 1) * rows]

    def compute(piece_of):
        if piece_of.family is wide:
            compute_wide(piece_of.kept_at, piece_of.slot)
        elif piece_of.family is down:
            compute_down(piece_of.kept_at, piece_of.slot)
        else:
            compute_small()
        piece_of.start(0)

    def moves(tick):
        for stage in range(m + n - 1, -1, -1):
            if 0 <= tick - stage < len(pairs):
                for piece_of in pairs[tick - stage]:
                    piece_of.finish(stage)
                    piece_of.start(stage + 1)

    work = AttentionBackward(at, m, piece, 0)
    for pair in pairs[:2]:
        for piece_of in pair:
            compute(piece_of)
    ready(loads.metas)
    work.begin()
    ready(loads.heads)
    for group in range(KEY_VALUE_HEADS):
        moves(group)
        for piece_of in pairs[group + 2]:
            compute(piece_of)
        work.group(group)
        work.follow(group)
    cosine, sine = at.cosines[...], at.sines[...]
    moves(5)
    compute(pairs[7][0])
    ready(loads.w_query)
    for virtual in range(KEY_VALUE_HEADS, KEY_VALUE_HEADS + m - 1):
        work.follow(virtual)
        if virtual == KEY_VALUE_HEADS:
            work.queries(cosine, sine)
    moves(6)
    ready(loads.rest)
    work.keys(cosine, sine)
    compute(pairs[7][1])
    moves(7)
    for piece_of in pairs[8] + pairs[9][:2]:
        compute(piece_of)
    at.gain_row[...] = work.gradient(at.dnorm, at.grad)
    turn_rows_into(at.grad_out, at.dnorm)
    compute(pairs[9][2])
    for tick in range(8, len(pairs) + m + n - 1):
        moves(tick)
    for pair in pairs:
        for piece_of in pair:
            piece_of.finish(m + n)
    for pair in pairs:
        for piece_of in pair:
            piece_of.drained(range(1, m + n + 1))
    work.drained()


def unpack_kernel(sizes, wide_hbm, down_hbm, little_hbm, hidden_in, gradient_in, *refs):
    rows, padded = sizes
    norm_attn, norm_ffn, query, key, value, out, gate, up, down_out, router, hidden, gradient = refs[:12]
    wide, down, little, rest, sems = refs[12:]
    carried = [
        pltpu.make_async_copy(source, target, sems.at[at])
        for at, (source, target) in enumerate(((hidden_in, hidden), (gradient_in, gradient)))
    ]
    loads = [
        pltpu.make_async_copy(source, target, sems.at[2 + at])
        for at, (source, target) in enumerate(((wide_hbm, wide), (down_hbm, down), (little_hbm, little)))
    ]
    for copy in loads + carried:
        copy.start()
    for load in loads:
        load.wait()
    norm_attn[...] = little[0, 0:1, :rows]
    norm_ffn[...] = little[0, 1:2, :rows]
    router[...] = little[0, 2:4, :rows]
    for unit in range(5):
        for first, target in ((0, gate), (5, up), (10, rest)):
            tile = wide[first + unit].astype(jnp.float32)
            for side in range(2):
                column = side * 1280 + unit * UNIT_COLUMNS
                target[:, column:column + UNIT_COLUMNS] = tile[side * padded:side * padded + rows]
        down_rows = down.shape[1]
        down_out[unit * down_rows:(unit + 1) * down_rows, :] = down[unit].astype(jnp.float32)
    width = query.shape[1]
    key[...] = rest[:, :KEYS_WIDTH].T
    value[...] = rest[:, KEYS_WIDTH:2 * KEYS_WIDTH].T
    query[...] = rest[:, 2 * KEYS_WIDTH:2 * KEYS_WIDTH + width]
    out[...] = rest[:, 2 * KEYS_WIDTH + width:]
    for copy in carried:
        copy.wait()


def final(small, saved, top, bottom, weights, mesh_sizes):
    nb, nd = mesh_sizes
    m, n = nb.bit_length() - 1, nd.bit_length() - 1
    grad = bottom["grad_hidden"]
    piece, width = grad.shape
    hidden_units = weights["w_gate_hbm"].shape[1]
    rows = width // nb
    padded = -(-rows // 8) * 8
    down_rows = hidden_units // nb // 5
    tokens = RECUR * piece

    def spread(array):
        if padded == rows:
            return array
        split = array.reshape(RECUR, nb, rows, piece)
        return jnp.pad(split, ((0, 0), (0, 0), (0, padded - rows), (0, 0))).reshape(RECUR, nb * padded, piece)

    inputs = small | dict(small_before=bottom["small"])
    operands = dict(
        metas_hbm=saved["metas"], turned_hbm=saved["turned"], dat_hbm=bottom["dat"], att_hbm=saved["att"],
        lse_hbm=saved["lse"], kv_hbm=saved["kv"], w_query_hbm=weights["w_query_hbm"],
        key_weight_hbm=weights["key_weight_hbm"], value_weight_hbm=weights["value_weight_hbm"], hid_hbm=saved["hid"],
        grad_hbm=grad, inner_hbm=saved["inner"], nffn_hbm=spread(saved["nffn"]), normed_hbm=spread(saved["normed"]),
        attended_hbm=spread(saved["att"]), dffn_0_hbm=bottom["dffn"], dffn_1_hbm=top["dffn"],
        dgate_0_hbm=bottom["dgate_out"], dgate_1_hbm=top["dgate"], dup_0_hbm=bottom["dup_out"], dup_1_hbm=top["dup"],
        far_0_hbm=bottom["far"], far_1_hbm=top["far"], near_1_hbm=bottom["near_out"],
    )
    near_width = bottom["near_out"].shape[1]
    families = (
        ("wide", 15, (2 * padded, UNIT_COLUMNS), low, WIDE_SLOTS, 1), ("down", 5, (down_rows, width), low, DOWN_SLOTS, 0),
        ("small", 1, (16, 128), jnp.float32, 1, 0),
    )
    outs = dict(grad_out=((width, piece), jnp.float32))
    buffers = attention_buffers(nb, piece, width, low) | dict(
        grad=((piece, width), jnp.float32), gate_side=((tokens, hidden_units), low), up_side=((tokens, hidden_units), low),
        inner=((hidden_units, tokens), low), left=((nb * padded, tokens), low), left_attended=((nb * padded, tokens), low),
        dffn=((tokens, width), low), gain_row=((1, width), jnp.float32),
    )
    for name, count, shape, dtype, slots, split in families:
        outs["out_" + name] = ((count, *shape), dtype)
        buffers["part_" + name] = ((slots, *(2,) * m, *shape), dtype)
        for stage in range(m):
            buffers["blk_%s_%d" % (name, stage)] = ((count, *(2,) * (m - 1 - stage), *shape), dtype)
        half = (shape[0], shape[1] // 2) if split else (shape[0] // 2, shape[1])
        for stage in range(n):
            buffers["dp_%s_%d" % (name, stage)] = ((count, *half), dtype)
    sums, hops = (2 * KEY_VALUE_HEADS, m), (21, m + n + 1)
    semaphores = dict(load_sems=(32,), kv_send=sums, kv_recv=sums, send_sems=hops, recv_sems=hops)
    names = (*inputs, *operands, *outs, *buffers, *semaphores)
    gradient, wide, down, little = pl.pallas_call(
        functools.partial(final_kernel, (nb, m, n, piece, rows, padded, near_width), names),
        out_shape=[shaped(entry) for entry in outs.values()],
        in_specs=[spec(pltpu.VMEM)] * len(inputs) + [spec(pl.ANY)] * len(operands),
        out_specs=[spec(pltpu.VMEM)] * len(outs),
        scratch_shapes=spaces(buffers.values()) + dma_semaphores(*semaphores.values()),
        compiler_params=pltpu.CompilerParams(
            collective_id=0, has_side_effects=True, vmem_limit_bytes=VMEM_LIMIT
        ),
        cost_estimate=pl.CostEstimate(
            flops=2 * tokens * width * 14000, bytes_accessed=30 * 1024 * 1024, transcendentals=0
        ),
        name="weight_grads",
    )(*inputs.values(), *operands.values())
    shapes = (
        (1, rows), (1, rows), (rows, width), (KEYS_WIDTH, rows), (KEYS_WIDTH, rows), (rows, width),
        (rows, hidden_units), (rows, hidden_units), (5 * down_rows, width), (2, rows), (width, piece), (width, piece),
    )
    outs = pl.pallas_call(
        functools.partial(unpack_kernel, (rows, padded)),
        out_shape=[jax.ShapeDtypeStruct(shape, jnp.float32) for shape in shapes],
        in_specs=[spec(pl.ANY)] * 5,
        out_specs=[spec(pltpu.VMEM)] * 12,
        scratch_shapes=[pltpu.VMEM(array.shape, array.dtype) for array in (wide, down, little)]
        + spaces([((rows, 2560), jnp.float32)]) + dma_semaphores((5,)),
        compiler_params=pltpu.CompilerParams(vmem_limit_bytes=VMEM_LIMIT),
        name="unpack",
    )(wide, down, little, saved["hidden_out"], gradient)
    norm_a, norm_f, query, key, value, out, gate, up, down, router, hidden, gradient = outs
    return (
        hidden.T[None], gradient.T[None], norm_a[0], norm_f[0], query, key.T, value.T, out, gate, up, down, router.T,
    )


def local(
    tokens,
    depths,
    segments,
    norm_attn,
    norm_ffn,
    w_query,
    key_weight,
    value_weight,
    w_out,
    w_gate,
    w_up,
    w_down,
    w_router,
    cotangent,
    mesh_sizes,
):
    piece = tokens.shape[1]
    positions = lax.axis_index("blk") * piece + jnp.arange(piece, dtype=jnp.int32)
    angles = frequencies(HEAD_DIMENSION)[:, None] * positions.astype(jnp.float32)[None, :]
    tables = dict(cosines=jnp.cos(angles), sines=jnp.sin(angles), norms=jnp.stack([norm_attn, norm_ffn]))
    routing = dict(router=w_router.T, depths=depths)
    heads = dict(w_query_hbm=w_query, key_weight_hbm=key_weight.T, value_weight_hbm=value_weight.T)
    weights = heads | dict(w_out_hbm=w_out, w_gate_hbm=w_gate, w_up_hbm=w_up, w_down_hbm=w_down.T)
    nb = mesh_sizes[0]
    saved = forward(
        tables | routing | dict(tokens=tokens[0].T, cotangent=cotangent[0].T, segments=segments), weights, nb
    )
    operands = dict(
        metas_hbm=saved["metas"], turned_hbm=saved["turned"], dat_hbm=saved["dat"], att_hbm=saved["att"],
        lse_hbm=saved["lse"], kv_hbm=saved["kv"], grad_hbm=saved["grad_hidden"], hid_1_hbm=saved["hid_1"],
        hid_0_hbm=saved["hid"], branch_hbm=saved["branch"], slope_hbm=saved["slope"], silu_hbm=saved["silu"],
        middle_hbm=saved["middle"],
    )
    bottom = backward(1, tables | routing | dict(small_before=saved["small"]), weights | operands, nb)
    return final(tables, saved, saved, bottom, weights, mesh_sizes)


def solution(mesh):
    sizes = (mesh.shape["blk"], mesh.shape["dp"])
    return jax.shard_map(
        functools.partial(local, mesh_sizes=sizes),
        mesh=mesh,
        in_specs=(
            P("dp", "blk", None),
            P("dp", "blk"),
            P("dp", "blk"),
            P(),
            P(),
            P(),
            P(),
            P(),
            P(),
            P(),
            P(),
            P(),
            P(),
            P("dp", "blk", None),
        ),
        out_specs=(
            P("dp", "blk", None),
            P("dp", "blk", None),
            P("blk"),
            P("blk"),
            P("blk", None),
            P("blk", None),
            P("blk", None),
            P("blk", None),
            P("blk", None),
            P("blk", None),
            P("blk", None),
            P("blk", None),
        ),
        check_vma=False,
    )
```

```python
import functools
import itertools
import math
import types

import jax
import jax.numpy as jnp
from jax import lax
from jax.experimental import pallas as pl
from jax.experimental.pallas import tpu as pltpu
from jax.sharding import PartitionSpec as P

QUERY_HEADS = 15
KEY_VALUE_HEADS = 5
HEAD_DIMENSION = 64
RECUR = 2
HEAD_SHARE = QUERY_HEADS // KEY_VALUE_HEADS
KEYS_WIDTH = KEY_VALUE_HEADS * HEAD_DIMENSION
PAIR = 2 * HEAD_DIMENSION
FF_TILE = 512
UNIT_COLUMNS = 256
VMEM_LIMIT = 63 * 1024 * 1024

epsilon = 1e-05
masked_score = -1e30
low = jnp.bfloat16


def frequencies(head_size):
    return jnp.exp(
        jnp.arange(head_size // 2, dtype=jnp.float32) * (-2.0 * math.log(10000.0) / head_size)
    )


def rms_scale(values):
    return lax.rsqrt(jnp.mean(values * values, axis=-1, keepdims=True) + epsilon)


def norm_gradient(grad_norm, values, gain):
    scale = rms_scale(values)
    weighted = grad_norm * gain
    grad_values = scale * weighted - values * (scale * scale * scale) * jnp.mean(
        weighted * values, axis=-1, keepdims=True
    )
    return grad_values, jnp.sum(grad_norm * values * scale, axis=0, keepdims=True)


def dot_last(left, right):
    return lax.dot_general(left, right, (((1,), (1,)), ((), ())), preferred_element_type=jnp.float32)


def plain_dot(left, right):
    return jnp.dot(left, right, preferred_element_type=jnp.float32)


def bits_of(number, count):
    return tuple((number >> (count - 1 - at)) & 1 for at in range(count))


def bit_of(position, bit):
    return lax.rem(position // (1 << bit), 2)


def block_bits(block, m):
    return tuple(bit_of(block, bit) for bit in range(m - 1, -1, -1))


def flipped(position, bit):
    return position + (1 << bit) * (1 - 2 * bit_of(position, bit))


def remote(source, target, sems, at, device):
    return pltpu.make_async_remote_copy(
        src_ref=source,
        dst_ref=target,
        send_sem=sems[0].at[at],
        recv_sem=sems[1].at[at],
        device_id=device,
        device_id_type=pl.DeviceIdType.MESH,
    )


def greet(partners):
    barrier = pltpu.get_barrier_semaphore()
    for partner in partners:
        pl.semaphore_signal(barrier, inc=1, device_id=partner, device_id_type=pl.DeviceIdType.MESH)
    pl.semaphore_wait(barrier, len(partners))


def turn_heads(turned, cosine, sine, heads):
    split = turned.reshape(heads, 2, HEAD_DIMENSION // 2, turned.shape[1])
    first, second = split[:, 0], split[:, 1]
    both = jnp.stack([first * cosine - second * sine, second * cosine + first * sine], axis=1)
    return both.reshape(turned.shape)


def turn_back(turned, cosine, sine, heads):
    return turn_heads(turned, cosine, -sine, heads)


def head_rows(group, member):
    head = group * HEAD_SHARE + member
    return pl.ds(pl.multiple_of(head * HEAD_DIMENSION, HEAD_DIMENSION), HEAD_DIMENSION)


def as_column(row):
    wide = jnp.broadcast_to(row.astype(jnp.float32), (8, row.shape[1]))
    return wide.T[:, 0:1]


def key_pairs(blk):
    return (blk + 2) // 2


def fill_bias(bias, metas, query_segments, level, blk, m, piece):
    key_at = lax.broadcasted_iota(jnp.int32, (piece, piece), 0)
    query_at = lax.broadcasted_iota(jnp.int32, (piece, piece), 1)

    @pl.loop(0, 2 * key_pairs(blk))
    def _(block):
        columns = metas[block_bits(block, m)].T
        live = jnp.where(columns[:, 1:2] > level, columns[:, 0:1], -1.0)
        shift = (blk - block) * piece
        allowed = (live == query_segments) & (key_at <= query_at + shift) | (key_at == query_at + shift)
        bias[block] = jnp.where(allowed, 0.0, masked_score).astype(bias.dtype)


def pair_bias(bias, pair, piece):
    here = bias[pl.ds(2 * pair, 2)].reshape(2 * piece, piece).astype(jnp.float32)
    return jnp.concatenate([here] * HEAD_SHARE, axis=1)


def spec(memory):
    return pl.BlockSpec(memory_space=memory)


def shaped(entry):
    return jax.ShapeDtypeStruct(*entry)


def spaces(entries):
    return [pltpu.VMEM(*entry) for entry in entries]


def dma_semaphores(*shapes):
    return [pltpu.SemaphoreType.DMA(shape) for shape in shapes]


class Piece:
    def __init__(self, at, kept_at, slot, flavour, family, sems, bits):
        self.at, self.kept_at, self.slot, self.family, self.sems = at, kept_at, slot, family, sems
        self.m, self.n = bits
        left = list(range(self.m - 1, -1, -1))
        self.order = []
        for stage in range(self.m):
            place = len(left) - 1 if stage == 0 or flavour == 0 else 0
            self.order.append((left.pop(place), place, len(left)))
        self.last = self.m + self.n
        self.blk = lax.axis_index("blk")
        self.dp = lax.axis_index("dp") if self.n else None

    def half(self, ref, side):
        rows, columns = self.family.shape
        if self.family.split == 0:
            return ref.at[pl.ds(pl.multiple_of(side * (rows // 2), rows // 2), rows // 2), :]
        return ref.at[:, pl.ds(pl.multiple_of(side * (columns // 2), columns // 2), columns // 2)]

    def held(self, stage):
        if stage == 0:
            return self.family.part, self.slot
        return self.family.blk[stage - 1], self.kept_at

    def copy(self, stage):
        m, family = self.m, self.family
        if stage < m:
            bit, place, others = self.order[stage]
            ref, index = self.held(stage)
            chosen = [slice(None)] * (others + 1)
            chosen[place] = 1 - bit_of(self.blk, bit)
            source = ref.at[(index, *chosen)]
            target = family.blk[stage].at[self.kept_at]
            device = {"blk": flipped(self.blk, bit)}
        elif stage < self.last:
            bit = stage - m
            if bit == 0:
                source = self.half(family.blk[m - 1].at[self.kept_at], 1 - bit_of(self.dp, 0))
            else:
                source = family.dp[bit - 1].at[self.kept_at]
            target = family.dp[bit].at[self.kept_at]
            device = {"dp": flipped(self.dp, bit)}
        else:
            source = self.half(family.out.at[self.kept_at], bit_of(self.dp, 0))
            target = source
            device = {"dp": flipped(self.dp, 0)}
        return remote(source, target, self.sems, (self.at, stage), device)

    def start(self, stage):
        self.copy(stage).start()

    def finish(self, stage):
        m, family = self.m, self.family
        self.copy(stage).wait_recv()
        if stage < m:
            bit, place, others = self.order[stage]
            ref, index = self.held(stage)
            for combo in itertools.product(range(2), repeat=others):
                chosen = list(combo)
                chosen.insert(place, bit_of(self.blk, bit))
                into = family.blk[stage].at[(self.kept_at, *combo)]
                self.add(into, into, ref.at[(index, *chosen)])
            if stage == 0:
                self.copy(0).wait_send()
        elif stage < self.last:
            bit = stage - m
            got = family.dp[bit].at[self.kept_at]
            if bit == 0:
                own = self.half(family.blk[m - 1].at[self.kept_at], bit_of(self.dp, 0))
            else:
                own = family.dp[bit - 1].at[self.kept_at]
            into = got
            if stage == self.last - 1:
                into = self.half(family.out.at[self.kept_at], bit_of(self.dp, 0))
            self.add(into, got, own)

    def add(self, into, left, right):
        into[...] = left[...] + right[...]

    def drained(self, stages):
        for stage in stages:
            self.copy(stage).wait_send()


def feed_forward_backward(at, level, gradient, ready, done):
    tiles = at.w_gate.shape[1] // FF_TILE
    column = at.router[level:level + 1, :].astype(jnp.float32)
    active = as_column(at.depths[...]) > float(level)
    hidden = at.hid_level[...]
    chosen = jax.nn.sigmoid(jnp.sum(hidden * column, axis=1, keepdims=True))
    at.dbranch[...] = jnp.where(active, chosen, 0.0) * gradient
    dchosen = jnp.where(active, jnp.sum(gradient * at.branch_level[...], axis=1, keepdims=True), 0.0)
    dlogit = dchosen * chosen * (1.0 - chosen)
    at.small[2 + level:3 + level, :] = jnp.sum(hidden * dlogit, axis=0, keepdims=True)
    at.grad_hidden[...] = gradient + dlogit * column
    at.dffn[...] = at.dbranch[...].astype(low)

    def dinner_of(tile):
        ready(tile)
        return plain_dot(at.dffn[...], at.w_down[:, tile * FF_TILE:(tile + 1) * FF_TILE])

    dinner = dinner_of(0)
    for tile in range(tiles):
        following = dinner_of(tile + 1) if tile + 1 < tiles else None
        columns = slice(tile * FF_TILE, (tile + 1) * FF_TILE)
        dgate = (dinner * at.slope_level[:, columns].astype(jnp.float32)).astype(low)
        dup = (dinner * at.silu_level[:, columns].astype(jnp.float32)).astype(low)
        at.dgate[:, columns] = dgate
        at.dup[:, columns] = dup
        done(tile)
        share = plain_dot(at.w_gate[:, columns], dgate.T) + plain_dot(at.w_up[:, columns], dup.T)
        if tile == 0:
            at.dnorm_turned[...] = share
        else:
            at.dnorm_turned[...] += share
        dinner = following
    ready(None)
    dnorm = at.dnorm_turned[...].T
    dmiddle, gain_share = norm_gradient(dnorm, at.middle_level[...], at.norms[1:2, :].astype(jnp.float32))
    at.small[1:2, :] += gain_share
    at.grad_hidden[...] += dmiddle
    dattn = (at.dbranch[...] + dmiddle).astype(low)
    lead = at.far.shape[1] - dattn.shape[1]
    at.far[:, :lead] = jnp.zeros((dattn.shape[0], lead), low)
    at.far[:, lead:] = dattn
    at.dat[...] = plain_dot(at.w_out[...], dattn.T).astype(low)


def forward_kernel(sizes, names, *refs):
    m, piece = sizes
    at = types.SimpleNamespace(**dict(zip(names, refs)))
    blk = lax.axis_index("blk")
    mine = block_bits(blk, m)
    kv, metas = at.kv, at.metas
    weights = (
        (at.key_weight_hbm, at.key_weight), (at.value_weight_hbm, at.value_weight), (at.w_query_hbm, at.w_query),
        (at.w_out_hbm, at.w_out), (at.w_gate_hbm, at.w_gate), (at.w_up_hbm, at.w_up), (at.w_down_hbm, at.w_down),
    )
    loads = [pltpu.make_async_copy(*pair, at.load_sems.at[index]) for index, pair in enumerate(weights)]
    for load in loads:
        load.start()
    saved = (
        (at.normed, at.normed_out), (at.turned, at.turned_out), (kv, at.kv_out), (at.lse, at.lse_out),
        (at.att, at.att_out), (at.nffn, at.nffn_out), (at.inner, at.inner_out),
    )

    def save(index, level):
        return pltpu.make_async_copy(
            saved[index][0].at[level], saved[index][1].at[level], at.save_sems.at[index, level]
        )

    first = (
        (at.hid.at[0], at.hid_out), (at.middle.at[0], at.middle_out), (at.silu.at[0], at.silu_out),
        (at.slope.at[0], at.slope_out), (at.branch.at[0], at.branch_out), (metas, at.metas_out),
        (at.far, at.far_out), (at.dat, at.dat_out), (at.dffn, at.dffn_out), (at.dgate, at.dgate_out), (at.dup, at.dup_out),
        (at.hid.at[1], at.hid_1_out),
    )
    late = [pltpu.make_async_copy(*pair, at.late_sems.at[index]) for index, pair in enumerate(first)]
    segment_row = at.segments[...].astype(jnp.float32)
    depth_column = as_column(at.depths[...])
    metas[mine] = jnp.concatenate(
        [segment_row, at.depths[...].astype(jnp.float32), jnp.zeros((6, piece), jnp.float32)], axis=0
    )
    greet([{"blk": flipped(blk, bit)} for bit in range(m)])

    def place(known):
        return tuple(slice(None) if bit in known else mine[m - 1 - bit] for bit in range(m - 1, -1, -1))

    orders = (list(range(1, m)), list(range(m - 1, 0, -1)))
    kv_sems = (at.kv_send, at.kv_recv)

    def kv_copies(level, group, stage):
        if stage == m - 1:
            ref = kv.at[(level, group, *place(range(1, m)))]
            return [remote(ref, ref, kv_sems, (level, group, 2 * stage), {"blk": flipped(blk, 0)})]
        copies = []
        for side, order in enumerate(orders):
            rows = pl.ds(side * (piece // 2), piece // 2)
            ref = kv.at[(level, group, *place(order[:stage]), rows)]
            copies.append(remote(ref, ref, kv_sems, (level, group, 2 * stage + side), {"blk": flipped(blk, order[stage])}))
        return copies

    def kv_advance(level, group, stage):
        if stage > 0:
            for copy in kv_copies(level, group, stage - 1):
                copy.wait_recv()
        if stage < m:
            for copy in kv_copies(level, group, stage):
                copy.start()

    def meta_copy(stage):
        bits = list(range(1, m)) + [0]
        ref = metas.at[place(bits[:stage])]
        return remote(ref, ref, (at.meta_send, at.meta_recv), stage, {"blk": flipped(blk, bits[stage])})

    meta_copy(0).start()
    cosine, sine = at.cosines[...], at.sines[...]
    gain_attn, gain_ffn = at.norms[0:1, :].astype(jnp.float32), at.norms[1:2, :].astype(jnp.float32)
    routers = at.router[...].astype(jnp.float32)
    at.hid[0] = at.tokens[...].T.astype(jnp.float32)
    late[0].start()
    at.query_pad[HEAD_DIMENSION:, :] = jnp.zeros_like(at.query_pad[HEAD_DIMENSION:, :])

    @pl.loop(0, RECUR)
    def _(level):
        hidden = at.hid[level]
        at.flat[...] = (hidden * rms_scale(hidden) * gain_attn).astype(low)
        at.normed[level] = at.flat[...].T

        @pl.when(level == 0)
        def _():
            for load in loads[:2]:
                load.wait()

        keys = turn_heads(plain_dot(at.key_weight[...], at.normed[level]), cosine, sine, KEY_VALUE_HEADS)
        values = plain_dot(at.value_weight[...], at.normed[level])
        for group in range(KEY_VALUE_HEADS):
            here = slice(group * HEAD_DIMENSION, (group + 1) * HEAD_DIMENSION)
            both = jnp.concatenate([keys[here], values[here]], axis=0)
            kv[(level, group, *mine)] = both.T.astype(low)
            kv_advance(level, group, 0)

        @pl.when(level == 0)
        def _():
            loads[2].wait()
            for stage in range(1, m - 1):
                meta_copy(stage - 1).wait_recv()
                meta_copy(stage).start()

        queries = turn_heads(plain_dot(at.flat[...], at.w_query[...]).T, cosine, sine, QUERY_HEADS)
        at.turned[level] = (queries * HEAD_DIMENSION ** (-0.5)).astype(low)

        @pl.when(level == 0)
        def _():
            for stage in range(max(1, m - 1), m):
                meta_copy(stage - 1).wait_recv()
                meta_copy(stage).start()

        for stage in range(1, m - 1):
            for group in range(KEY_VALUE_HEADS):
                kv_advance(level, group, stage)
        kv_advance(level, 0, m - 1)

        @pl.when(level == 0)
        def _():
            meta_copy(m - 1).wait_recv()
            late[5].start()

        fill_bias(at.bias, metas, segment_row, level.astype(jnp.float32), blk, m, piece)

        @pl.loop(0, KEY_VALUE_HEADS)
        def _(group):
            @pl.when(group + 1 < KEY_VALUE_HEADS)
            def _():
                kv_advance(level, group + 1, m - 1)

            kv_advance(level, group, m)
            for member in range(HEAD_SHARE):
                at.query_pad[:HEAD_DIMENSION, member * piece:(member + 1) * piece] = at.turned[level, head_rows(group, member), :]
            at.top[...] = jnp.full_like(at.top, masked_score)
            at.total[...] = jnp.zeros_like(at.total)

            @pl.loop(0, key_pairs(blk))
            def _(step):
                pair = key_pairs(blk) - 1 - step
                rows = kv[(level, group, *block_bits(pair, m - 1))].reshape(2 * piece, PAIR)
                scores = plain_dot(rows, at.query_pad[...]) + pair_bias(at.bias, pair, piece)
                before = at.top[0:1, :]
                after = jnp.maximum(before, jnp.max(scores, axis=0, keepdims=True))
                raised = jnp.exp(scores - after)
                shrink = jnp.exp(before - after)
                at.top[0:1, :] = after
                ones = jnp.ones((16, 2 * piece), low)
                left = jnp.concatenate([rows.T[HEAD_DIMENSION:], ones], axis=0)
                at.total[...] = at.total[...] * shrink + plain_dot(left, raised.astype(low))

            sums = at.total[HEAD_DIMENSION:HEAD_DIMENSION + 1, :]
            at.lse[level, pl.ds(group, 1), :] = at.top[0:1, :] + jnp.log(sums)
            out = at.total[:HEAD_DIMENSION, :] / sums
            for member in range(HEAD_SHARE):
                at.att[level, head_rows(group, member), :] = out[:, member * piece:(member + 1) * piece].astype(low)

        for index in range(5):
            save(index, level).start()

        @pl.when(level == 0)
        def _():
            loads[3].wait()

        attn = plain_dot(at.att[level].T, at.w_out[...])
        mid = at.hid[level] + attn
        at.middle[level] = mid
        at.branch[level] = attn
        at.flat[...] = (mid * rms_scale(mid) * gain_ffn).astype(low)
        at.nffn[level] = at.flat[...].T
        save(5, level).start()

        @pl.when(level == 0)
        def _():
            loads[4].wait()
            loads[5].wait()

        for tile in range(at.w_gate.shape[1] // FF_TILE):
            columns = slice(tile * FF_TILE, (tile + 1) * FF_TILE)
            gate_pre = plain_dot(at.flat[...], at.w_gate[:, columns])
            up_pre = plain_dot(at.flat[...], at.w_up[:, columns])
            opened = jax.nn.sigmoid(gate_pre)
            passed = gate_pre * opened
            at.silu[level, :, columns] = passed.astype(low)
            at.slope[level, :, columns] = (up_pre * (opened + passed - passed * opened)).astype(low)
            at.inner[level, columns, :] = (passed * up_pre).astype(low).T

        save(6, level).start()

        @pl.when(level == 0)
        def _():
            loads[6].wait()

        at.branch[level] += plain_dot(at.w_down[...], at.inner[level]).T
        column = jnp.where(level == 0, routers[0:1, :], routers[1:2, :])
        logit = jnp.sum(at.hid[level] * column, axis=1, keepdims=True)
        weight = jnp.where(depth_column > level.astype(jnp.float32), jax.nn.sigmoid(logit), 0.0)
        at.hid[level + 1] = at.hid[level] + weight * at.branch[level]

        @pl.when(level == 0)
        def _():
            for copy in late[1:5]:
                copy.start()

    at.hidden_out[...] = at.hid[RECUR].T
    top = RECUR - 1
    at.hid_level, at.branch_level, at.middle_level = at.hid.at[top], at.branch.at[top], at.middle.at[top]
    at.silu_level, at.slope_level = at.silu.at[top], at.slope.at[top]
    at.small[...] = jnp.zeros_like(at.small)
    feed_forward_backward(at, top, at.cotangent[...].T.astype(jnp.float32), lambda tile: None, lambda tile: None)
    for copy in late[6:]:
        copy.start()
    for stage in range(m):
        meta_copy(stage).wait_send()
    for level in range(RECUR):
        for group in range(KEY_VALUE_HEADS):
            for stage in range(m):
                for copy in kv_copies(level, group, stage):
                    copy.wait_send()
        for index in range(len(saved)):
            save(index, level).wait()
    for copy in late:
        copy.wait()


def far_width(width):
    return 2 * width + 2 * KEYS_WIDTH - 1536


def forward(small, weights, nb):
    m = nb.bit_length() - 1
    width, piece = small["tokens"].shape
    hidden_units = weights["w_gate_hbm"].shape[1]
    blocks, wide = (2,) * m, HEAD_SHARE * piece
    rows, turned = ((piece, width), jnp.float32), ((RECUR, width, piece), low)
    hidden = ((piece, hidden_units), low)
    saved = dict(
        normed=turned, turned=turned, kv=((RECUR, KEY_VALUE_HEADS, *blocks, piece, PAIR), low),
        lse=((RECUR, 8, wide), jnp.float32), att=turned, nffn=turned, inner=((RECUR, hidden_units, piece), low),
        metas=((*blocks, 8, piece), jnp.float32), far=((piece, far_width(width)), low), dat=((width, piece), low),
        dffn=((piece, width), low), dgate=hidden, dup=hidden,
    )
    first = dict(hid=rows, middle=rows, silu=hidden, slope=hidden, branch=rows)
    outs = dict(hidden_out=((width, piece), jnp.float32), grad_hidden=rows, small=((8, width), jnp.float32))
    anywhere = {name + "_out": entry for name, entry in (saved | first | dict(hid_1=rows)).items()}
    both = {name: ((RECUR, *shape), dtype) for name, (shape, dtype) in first.items()}
    buffers = {name[:-4]: (array.shape, array.dtype) for name, array in weights.items()} | saved | both | dict(
        hid=((RECUR + 1, piece, width), jnp.float32), flat=((piece, width), low),
        bias=((nb, piece, piece), jnp.float32), query_pad=((PAIR, wide), low), top=((8, wide), jnp.float32),
        total=((HEAD_DIMENSION + 16, wide), jnp.float32), dbranch=rows, dnorm_turned=((width, piece), jnp.float32),
    )
    semaphores = dict(
        load_sems=(7,), save_sems=(7, RECUR), late_sems=(12,), kv_send=(RECUR, KEY_VALUE_HEADS, 2 * m),
        kv_recv=(RECUR, KEY_VALUE_HEADS, 2 * m), meta_send=(m,), meta_recv=(m,),
    )
    results = pl.pallas_call(
        functools.partial(forward_kernel, (m, piece), (*small, *weights, *outs, *anywhere, *buffers, *semaphores)),
        out_shape=[shaped(entry) for entry in (outs | anywhere).values()],
        in_specs=[spec(pltpu.VMEM)] * len(small) + [spec(pl.ANY)] * len(weights),
        out_specs=[spec(pltpu.VMEM)] * len(outs) + [spec(pl.ANY)] * len(anywhere),
        scratch_shapes=spaces(buffers.values()) + dma_semaphores(*semaphores.values()),
        compiler_params=pltpu.CompilerParams(
            collective_id=1, has_side_effects=True, vmem_limit_bytes=VMEM_LIMIT
        ),
        cost_estimate=pl.CostEstimate(
            flops=3 * RECUR * piece * width * 10240, bytes_accessed=48 * 1024 * 1024, transcendentals=0
        ),
        name="forward_levels",
    )(*small.values(), *weights.values())
    return dict(zip((*outs, *(name[:-4] for name in anywhere)), results))


class AttentionBackward:
    def __init__(self, at, m, piece, level):
        self.at, self.m, self.piece, self.level = at, m, piece, level
        self.blk = lax.axis_index("blk")
        self.family = types.SimpleNamespace(part=at.part, blk=at.halves, dp=(), out=None, shape=(piece // 2, PAIR), split=0)

    def pieces(self, group):
        sems = (self.at.kv_send, self.at.kv_recv)
        return [
            Piece(2 * group + side, 2 * group + side, 2 * group + side, side, self.family, sems, (self.m, 0))
            for side in range(2)
        ]

    def move(self, group, stage):
        for piece_of in self.pieces(group):
            piece_of.finish(stage)
            if stage + 1 < self.m:
                piece_of.start(stage + 1)

    def begin(self):
        at = self.at
        query_segments = at.metas[block_bits(self.blk, self.m)][0:1, :]
        fill_bias(at.bias, at.metas, query_segments, float(self.level), self.blk, self.m, self.piece)
        at.query_pad[HEAD_DIMENSION:, :] = jnp.zeros_like(at.query_pad[HEAD_DIMENSION:, :])
        at.dat_pad[:HEAD_DIMENSION, :] = jnp.zeros_like(at.dat_pad[:HEAD_DIMENSION, :])

    def group(self, group):
        at, m, piece, blk = self.at, self.m, self.piece, self.blk
        half = piece // 2
        carried = []
        for member in range(HEAD_SHARE):
            rows, lanes = head_rows(group, member), slice(member * piece, (member + 1) * piece)
            at.query_pad[:HEAD_DIMENSION, lanes] = at.turned[rows, :]
            at.dat_pad[HEAD_DIMENSION:, lanes] = at.dat_turned[rows, :]
            product = at.dat_turned[rows, :].astype(jnp.float32) * at.att_turned[rows, :].astype(jnp.float32)
            carried.append(jnp.sum(product, axis=0, keepdims=True))
        carried = jnp.concatenate(carried, axis=1)
        at.query_rows[...] = at.query_pad[...].T
        at.dat_rows[...] = at.dat_pad[...].T
        log_total = at.lse[pl.ds(group, 1), :]
        at.dq_sum[...] = jnp.zeros_like(at.dq_sum)

        @pl.loop(0, key_pairs(blk))
        def _(pair):
            rows = at.kv[(group, *block_bits(pair, m - 1))].reshape(2 * piece, PAIR)
            probability = jnp.exp(plain_dot(rows, at.query_pad[...]) + pair_bias(at.bias, pair, piece) - log_total)
            dprob = plain_dot(rows, at.dat_pad[...])
            dscores = (probability * (dprob - carried)).astype(low)
            share = plain_dot(dscores, at.query_rows[...]) + plain_dot(probability.astype(low), at.dat_rows[...])
            share = share.astype(low)
            for block in range(2):
                for side in range(2):
                    first = block * piece + side * half
                    at.part[(2 * group + side, *block_bits(pair, m - 1), block)] = share[first:first + half]
            at.dq_sum[...] += plain_dot(rows.T[:HEAD_DIMENSION], dscores)

        @pl.loop(key_pairs(blk), 1 << (m - 1))
        def _(pair):
            for block in range(2):
                for side in range(2):
                    at.part[(2 * group + side, *block_bits(pair, m - 1), block)] = jnp.zeros((half, PAIR), low)

        for piece_of in self.pieces(group):
            piece_of.start(0)
        for member in range(HEAD_SHARE):
            at.dq_turned[head_rows(group, member), :] = at.dq_sum[:, member * piece:(member + 1) * piece]

    def follow(self, group):
        for stage in range(self.m - 1):
            earlier = group - 1 - stage
            if isinstance(group, int):
                if 0 <= earlier < KEY_VALUE_HEADS:
                    self.move(earlier, stage)
            else:
                @pl.when(earlier >= 0)
                def _():
                    self.move(earlier, stage)

    def queries(self, cosine, sine):
        at = self.at
        dqueries = turn_back(at.dq_turned[...] * HEAD_DIMENSION ** (-0.5), cosine, sine, QUERY_HEADS).astype(low)
        self.put(2 * KEYS_WIDTH, dqueries.T)
        at.dnorm[...] = plain_dot(at.w_query[...], dqueries).T

    def put(self, column, values):
        self.at.near[:, column:column + values.shape[1]] = values

    def keys(self, cosine, sine):
        at, m = self.at, self.m
        filled = 2 * KEYS_WIDTH + QUERY_HEADS * HEAD_DIMENSION
        self.put(filled, jnp.zeros((self.piece, at.near.shape[1] - filled), low))
        dkeys, dvalues = [], []
        for group in range(KEY_VALUE_HEADS):
            self.move(group, m - 1)
            both = jnp.concatenate([at.halves[m - 1][2 * group], at.halves[m - 1][2 * group + 1]], axis=0).T
            dkeys.append(both[:HEAD_DIMENSION].astype(jnp.float32))
            dvalues.append(both[HEAD_DIMENSION:])
        dkeys = turn_back(jnp.concatenate(dkeys, axis=0), cosine, sine, KEY_VALUE_HEADS).astype(low).T
        dvalues = jnp.concatenate(dvalues, axis=0).T
        self.put(0, dkeys)
        self.put(KEYS_WIDTH, dvalues)
        at.dnorm[...] += plain_dot(dkeys, at.key_weight[...]) + plain_dot(dvalues, at.value_weight[...])

    def drained(self):
        for group in range(KEY_VALUE_HEADS):
            for piece_of in self.pieces(group):
                piece_of.drained(range(1, self.m))


def attention_buffers(nb, piece, width, bias_type):
    m, wide, heads = nb.bit_length() - 1, HEAD_SHARE * piece, 2 * KEY_VALUE_HEADS
    turned, weight = ((width, piece), low), ((KEYS_WIDTH, width), low)
    pad, pad_rows = ((PAIR, wide), low), ((wide, PAIR), low)
    buffers = dict(
        turned=turned, dat_turned=turned, att_turned=turned, kv=((KEY_VALUE_HEADS, *(2,) * m, piece, PAIR), low),
        lse=((8, wide), jnp.float32), metas=((*(2,) * m, 8, piece), jnp.float32), w_query=((width, width), low),
        key_weight=weight, value_weight=weight, dq_turned=((width, piece), jnp.float32),
        bias=((nb, piece, piece), bias_type), query_pad=pad, dat_pad=pad, query_rows=pad_rows, dat_rows=pad_rows,
        dq_sum=((HEAD_DIMENSION, wide), jnp.float32), part=((heads, *(2,) * m, piece // 2, PAIR), low),
        dnorm=((piece, width), jnp.float32), hid=((piece, width), jnp.float32),
    )
    for stage in range(m):
        buffers["half_%d" % stage] = ((heads, *(2,) * (m - 1 - stage), piece // 2, PAIR), low)
    return buffers


def backward_kernel(sizes, names, *refs):
    m, piece, level = sizes
    at = types.SimpleNamespace(**dict(zip(names, refs)))
    at.halves = [getattr(at, "half_%d" % stage) for stage in range(m)]
    at.near = at.near_out
    blk = lax.axis_index("blk")
    pairs = (
        (at.metas_hbm, at.metas), (at.turned_hbm.at[level], at.turned), (at.dat_hbm, at.dat_turned),
        (at.att_hbm.at[level], at.att_turned), (at.lse_hbm.at[level], at.lse), (at.kv_hbm.at[level], at.kv),
        (at.w_query_hbm, at.w_query), (at.key_weight_hbm, at.key_weight), (at.value_weight_hbm, at.value_weight),
        (at.grad_hbm, at.grad_hidden), (at.hid_1_hbm, at.hid),
        (at.hid_0_hbm, at.hid_level), (at.branch_hbm, at.branch_level), (at.w_down_hbm, at.w_down),
        (at.slope_hbm, at.slope_level), (at.silu_hbm, at.silu_level), (at.w_gate_hbm, at.w_gate), (at.w_up_hbm, at.w_up),
        (at.middle_hbm, at.middle_level), (at.w_out_hbm, at.w_out),
    )
    loads = [pltpu.make_async_copy(*pair, at.load_sems.at[index]) for index, pair in enumerate(pairs)]
    for load in loads:
        load.start()
    saves = [
        pltpu.make_async_copy(*pair, at.save_sems.at[index])
        for index, pair in enumerate(((at.dgate, at.dgate_out), (at.dup, at.dup_out)))
    ]
    greet([{"blk": flipped(blk, bit)} for bit in range(m)])
    work = AttentionBackward(at, m, piece, level)
    loads[0].wait()
    work.begin()
    for load in loads[1:6]:
        load.wait()

    @pl.loop(0, KEY_VALUE_HEADS)
    def _(group):
        work.group(group)
        work.follow(group)

    cosine, sine = at.cosines[...], at.sines[...]
    for virtual in range(KEY_VALUE_HEADS, KEY_VALUE_HEADS + m - 1):
        work.follow(virtual)
        if virtual == KEY_VALUE_HEADS:
            loads[6].wait()
            work.queries(cosine, sine)
    for load in loads[7:]:
        load.wait()
    work.keys(cosine, sine)
    dhidden, gain_share = norm_gradient(at.dnorm[...], at.hid[...], at.norms[0:1, :].astype(jnp.float32))
    at.small[...] = at.small_before[...]
    at.small[0:1, :] = gain_share
    gradient = at.grad_hidden[...] + dhidden
    at.dnorm[...] = gradient
    feed_forward_backward(at, level - 1, at.dnorm[...], lambda tile: None, lambda tile: None)
    for save in saves:
        save.start()
    work.drained()
    for save in saves:
        save.wait()


def backward(level, small, operands, nb):
    m = nb.bit_length() - 1
    piece, width = operands["grad_hbm"].shape
    hidden_units = operands["w_gate_hbm"].shape[1]
    rows, flat, hidden = ((piece, width), jnp.float32), ((piece, width), low), ((piece, hidden_units), low)
    outs = dict(
        grad_hidden=rows, small=((8, width), jnp.float32), near_out=((piece, 1792), low), dffn=flat,
        dat=((width, piece), low), far=((piece, far_width(width)), low),
    )
    anywhere = dict(dgate_out=hidden, dup_out=hidden)
    buffers = attention_buffers(nb, piece, width, jnp.float32) | dict(
        hid_level=rows, branch_level=rows, middle_level=rows, w_down=((width, hidden_units), low), slope_level=hidden,
        silu_level=hidden, w_gate=((width, hidden_units), low), w_up=((width, hidden_units), low),
        w_out=((width, width), low), dbranch=rows, dnorm_turned=((width, piece), jnp.float32), dgate=hidden, dup=hidden,
    )
    sums = (2 * KEY_VALUE_HEADS, m)
    semaphores = dict(load_sems=(20,), save_sems=(2,), kv_send=sums, kv_recv=sums)
    results = pl.pallas_call(
        functools.partial(
            backward_kernel, (m, piece, level), (*small, *operands, *outs, *anywhere, *buffers, *semaphores)
        ),
        out_shape=[shaped(entry) for entry in (outs | anywhere).values()],
        in_specs=[spec(pltpu.VMEM)] * len(small) + [spec(pl.ANY)] * len(operands),
        out_specs=[spec(pltpu.VMEM)] * len(outs) + [spec(pl.ANY)] * len(anywhere),
        scratch_shapes=spaces(buffers.values()) + dma_semaphores(*semaphores.values()),
        compiler_params=pltpu.CompilerParams(
            collective_id=2, has_side_effects=True, vmem_limit_bytes=VMEM_LIMIT
        ),
        cost_estimate=pl.CostEstimate(
            flops=2 * piece * width * 20000, bytes_accessed=32 * 1024 * 1024, transcendentals=0
        ),
        name="backward_level",
    )(*small.values(), *operands.values())
    return dict(zip((*outs, *anywhere), results))


WIDE_SLOTS, DOWN_SLOTS = 4, 2


def final_kernel(sizes, names, *refs):
    nb, m, n, piece, rows, padded, near_width = sizes
    at = types.SimpleNamespace(**dict(zip(names, refs)))
    at.halves = [getattr(at, "half_%d" % stage) for stage in range(m)]
    blk, dp = lax.axis_index("blk"), lax.axis_index("dp")
    at.near = at.gate_side.at[pl.ds(0, piece), pl.ds(0, near_width)]
    counter = itertools.count()

    def load(source, target):
        return pltpu.make_async_copy(source, target, at.load_sems.at[next(counter)])

    def both_lanes(ref, target):
        return [load(ref.at[level], target.at[:, pl.ds(level * piece, piece)]) for level in range(RECUR)]

    def both_rows(low_ref, deep_ref, target, width):
        pairs = ((low_ref, 0), (deep_ref, piece))
        return [load(ref, target.at[pl.ds(first, piece), pl.ds(0, width)]) for ref, first in pairs]

    hidden_units, width = at.gate_side.shape[1], at.dffn.shape[1]
    far_lanes = at.far_0_hbm.shape[1]
    loads = types.SimpleNamespace(
        nffn=both_lanes(at.nffn_hbm, at.left),
        dgate=both_rows(at.dgate_0_hbm, at.dgate_1_hbm, at.gate_side, hidden_units),
        inner=both_lanes(at.inner_hbm, at.inner),
        dffn=both_rows(at.dffn_0_hbm, at.dffn_1_hbm, at.dffn, width),
        metas=[load(at.metas_hbm, at.metas)],
        heads=[
            load(at.turned_hbm.at[0], at.turned), load(at.dat_hbm, at.dat_turned), load(at.att_hbm.at[0], at.att_turned),
            load(at.lse_hbm.at[0], at.lse), load(at.kv_hbm.at[0], at.kv),
        ],
        dup=both_rows(at.dup_0_hbm, at.dup_1_hbm, at.up_side, hidden_units),
        w_query=[load(at.w_query_hbm, at.w_query)],
        rest=[
            load(at.key_weight_hbm, at.key_weight), load(at.value_weight_hbm, at.value_weight),
            load(at.hid_hbm, at.hid), load(at.grad_hbm, at.grad),
        ],
        attended=both_lanes(at.attended_hbm, at.left_attended),
    )
    late = types.SimpleNamespace(
        near=[load(at.near_1_hbm, at.gate_side.at[pl.ds(piece, piece), pl.ds(0, near_width)])],
        far=both_rows(at.far_0_hbm, at.far_1_hbm, at.up_side, far_lanes),
        normed=both_lanes(at.normed_hbm, at.left),
    )

    def begin(copies):
        for copy in copies:
            copy.start()

    def ready(copies):
        for copy in copies:
            copy.wait()

    for copies in vars(loads).values():
        begin(copies)
    greet([{"blk": flipped(blk, bit)} for bit in range(m)] + [{"dp": flipped(dp, bit)} for bit in range(n)])

    down_rows = at.part_down.shape[-2]

    def family(name, shape, split):
        return types.SimpleNamespace(
            part=getattr(at, "part_" + name), out=getattr(at, "out_" + name), shape=shape, split=split,
            blk=[getattr(at, "blk_%s_%d" % (name, stage)) for stage in range(m)],
            dp=[getattr(at, "dp_%s_%d" % (name, stage)) for stage in range(n)],
        )

    wide = family("wide", (2 * padded, UNIT_COLUMNS), 1)
    down = family("down", (down_rows, width), 0)
    little = family("small", (16, 128), 0)
    sems = (at.send_sems, at.recv_sems)
    units = itertools.count()

    def unit(holder, index, flavour):
        return Piece(next(units), index, index % holder.part.shape[0], flavour, holder, sems, (m, n))

    pairs = [[unit(wide, index, 0), unit(down, index, 1)] for index in range(5)]
    pairs += [[unit(wide, index, 0), unit(wide, index + 1, 1)] for index in (5, 7, 9, 11)]
    pairs += [[unit(wide, 13, 0), unit(wide, 14, 1), unit(little, 0, 0)]]

    def compute_wide(index, slot):
        if index == 0:
            ready(loads.nffn)
            ready(loads.dgate)
        if index == 5:
            begin(late.near)
            ready(loads.dup)
        if index == 10:
            begin(late.far)
            begin(late.normed)
            ready(late.near)
            ready(late.normed)
            ready(loads.attended)
            ready(late.far)
        block, column = index // 5, (index % 5) * UNIT_COLUMNS
        second = 1280 + column
        upper_columns, lower_columns = slice(column, column + UNIT_COLUMNS), slice(second, second + UNIT_COLUMNS)
        if block < 2:
            right = at.gate_side if block == 0 else at.up_side
            upper = plain_dot(at.left[...], right[:, upper_columns])
            lower = plain_dot(at.left[...], right[:, lower_columns])
        else:
            upper = plain_dot(at.left[...], at.gate_side[:, upper_columns])
            lower = None
            if second < 1600:
                lower = plain_dot(at.left[...], at.gate_side[:, lower_columns])
            if second >= 1536:
                more = plain_dot(at.left_attended[...], at.up_side[:, second - 1536:second - 1536 + UNIT_COLUMNS])
                lower = more if lower is None else lower + more
        for target in range(nb):
            here = slice(target * padded, (target + 1) * padded)
            both = jnp.concatenate([upper[here], lower[here]], axis=0)
            at.part_wide[(slot, *bits_of(target, m))] = both.astype(low)

    def compute_down(index, slot):
        if index == 0:
            ready(loads.inner)
            ready(loads.dffn)
        firsts = [(target * 5 + index) * down_rows for target in range(nb)]
        left = jnp.concatenate([at.inner[first:first + down_rows, :] for first in firsts], axis=0)
        result = plain_dot(left, at.dffn[...])
        for target in range(nb):
            at.part_down[(slot, *bits_of(target, m))] = result[target * down_rows:(target + 1) * down_rows].astype(low)

    def compute_small():
        total = at.small_before[...]
        total = total + jnp.concatenate([at.gain_row[...], jnp.zeros((7, width), jnp.float32)], axis=0)
        at.part_small[...] = jnp.zeros_like(at.part_small)
        for target in range(nb):
            at.part_small[(0, *bits_of(target, m), slice(0, 8), slice(0, rows))] = total[:, target * rows:(target + 1) * rows]

    def compute(piece_of):
        if piece_of.family is wide:
            compute_wide(piece_of.kept_at, piece_of.slot)
        elif piece_of.family is down:
            compute_down(piece_of.kept_at, piece_of.slot)
        else:
            compute_small()
        piece_of.start(0)

    def moves(tick):
        for stage in range(m + n - 1, -1, -1):
            if 0 <= tick - stage < len(pairs):
                for piece_of in pairs[tick - stage]:
                    piece_of.finish(stage)
                    piece_of.start(stage + 1)

    work = AttentionBackward(at, m, piece, 0)
    for pair in pairs[:2]:
        for piece_of in pair:
            compute(piece_of)
    ready(loads.metas)
    work.begin()
    ready(loads.heads)
    for group in range(KEY_VALUE_HEADS):
        moves(group)
        for piece_of in pairs[group + 2]:
            compute(piece_of)
        work.group(group)
        work.follow(group)
    cosine, sine = at.cosines[...], at.sines[...]
    moves(5)
    compute(pairs[7][0])
    ready(loads.w_query)
    for virtual in range(KEY_VALUE_HEADS, KEY_VALUE_HEADS + m - 1):
        work.follow(virtual)
        if virtual == KEY_VALUE_HEADS:
            work.queries(cosine, sine)
    moves(6)
    ready(loads.rest)
    work.keys(cosine, sine)
    compute(pairs[7][1])
    moves(7)
    for piece_of in pairs[8] + pairs[9][:2]:
        compute(piece_of)
    dhidden, gain_share = norm_gradient(at.dnorm[...], at.hid[...], at.norms[0:1, :].astype(jnp.float32))
    at.gain_row[...] = gain_share
    at.grad_out[...] = (at.grad[...] + dhidden).T
    compute(pairs[9][2])
    for tick in range(8, len(pairs) + m + n - 1):
        moves(tick)
    for pair in pairs:
        for piece_of in pair:
            piece_of.finish(m + n)
    for pair in pairs:
        for piece_of in pair:
            piece_of.drained(range(1, m + n + 1))
    work.drained()


def unpack_kernel(sizes, wide_hbm, down_hbm, little_hbm, hidden_in, gradient_in, *refs):
    rows, padded = sizes
    norm_attn, norm_ffn, query, key, value, out, gate, up, down_out, router, hidden, gradient = refs[:12]
    wide, down, little, rest, sems = refs[12:]
    carried = [
        pltpu.make_async_copy(source, target, sems.at[at])
        for at, (source, target) in enumerate(((hidden_in, hidden), (gradient_in, gradient)))
    ]
    loads = [
        pltpu.make_async_copy(source, target, sems.at[2 + at])
        for at, (source, target) in enumerate(((wide_hbm, wide), (down_hbm, down), (little_hbm, little)))
    ]
    for copy in loads + carried:
        copy.start()
    for load in loads:
        load.wait()
    norm_attn[...] = little[0, 0:1, :rows]
    norm_ffn[...] = little[0, 1:2, :rows]
    router[...] = little[0, 2:4, :rows]
    for unit in range(5):
        for first, target in ((0, gate), (5, up), (10, rest)):
            tile = wide[first + unit].astype(jnp.float32)
            for side in range(2):
                column = side * 1280 + unit * UNIT_COLUMNS
                target[:, column:column + UNIT_COLUMNS] = tile[side * padded:side * padded + rows]
        down_rows = down.shape[1]
        down_out[unit * down_rows:(unit + 1) * down_rows, :] = down[unit].astype(jnp.float32)
    width = query.shape[1]
    key[...] = rest[:, :KEYS_WIDTH].T
    value[...] = rest[:, KEYS_WIDTH:2 * KEYS_WIDTH].T
    query[...] = rest[:, 2 * KEYS_WIDTH:2 * KEYS_WIDTH + width]
    out[...] = rest[:, 2 * KEYS_WIDTH + width:]
    for copy in carried:
        copy.wait()


def final(small, saved, top, bottom, weights, mesh_sizes):
    nb, nd = mesh_sizes
    m, n = nb.bit_length() - 1, nd.bit_length() - 1
    grad = bottom["grad_hidden"]
    piece, width = grad.shape
    hidden_units = weights["w_gate_hbm"].shape[1]
    rows = width // nb
    padded = -(-rows // 8) * 8
    down_rows = hidden_units // nb // 5
    tokens = RECUR * piece

    def spread(array):
        if padded == rows:
            return array
        split = array.reshape(RECUR, nb, rows, piece)
        return jnp.pad(split, ((0, 0), (0, 0), (0, padded - rows), (0, 0))).reshape(RECUR, nb * padded, piece)

    inputs = small | dict(small_before=bottom["small"])
    operands = dict(
        metas_hbm=saved["metas"], turned_hbm=saved["turned"], dat_hbm=bottom["dat"], att_hbm=saved["att"],
        lse_hbm=saved["lse"], kv_hbm=saved["kv"], w_query_hbm=weights["w_query_hbm"],
        key_weight_hbm=weights["key_weight_hbm"], value_weight_hbm=weights["value_weight_hbm"], hid_hbm=saved["hid"],
        grad_hbm=grad, inner_hbm=saved["inner"], nffn_hbm=spread(saved["nffn"]), normed_hbm=spread(saved["normed"]),
        attended_hbm=spread(saved["att"]), dffn_0_hbm=bottom["dffn"], dffn_1_hbm=top["dffn"],
        dgate_0_hbm=bottom["dgate_out"], dgate_1_hbm=top["dgate"], dup_0_hbm=bottom["dup_out"], dup_1_hbm=top["dup"],
        far_0_hbm=bottom["far"], far_1_hbm=top["far"], near_1_hbm=bottom["near_out"],
    )
    near_width = bottom["near_out"].shape[1]
    families = (
        ("wide", 15, (2 * padded, UNIT_COLUMNS), low, WIDE_SLOTS, 1), ("down", 5, (down_rows, width), low, DOWN_SLOTS, 0),
        ("small", 1, (16, 128), jnp.float32, 1, 0),
    )
    outs = dict(grad_out=((width, piece), jnp.float32))
    buffers = attention_buffers(nb, piece, width, low) | dict(
        grad=((piece, width), jnp.float32), gate_side=((tokens, hidden_units), low), up_side=((tokens, hidden_units), low),
        inner=((hidden_units, tokens), low), left=((nb * padded, tokens), low), left_attended=((nb * padded, tokens), low),
        dffn=((tokens, width), low), gain_row=((1, width), jnp.float32),
    )
    for name, count, shape, dtype, slots, split in families:
        outs["out_" + name] = ((count, *shape), dtype)
        buffers["part_" + name] = ((slots, *(2,) * m, *shape), dtype)
        for stage in range(m):
            buffers["blk_%s_%d" % (name, stage)] = ((count, *(2,) * (m - 1 - stage), *shape), dtype)
        half = (shape[0], shape[1] // 2) if split else (shape[0] // 2, shape[1])
        for stage in range(n):
            buffers["dp_%s_%d" % (name, stage)] = ((count, *half), dtype)
    sums, hops = (2 * KEY_VALUE_HEADS, m), (21, m + n + 1)
    semaphores = dict(load_sems=(32,), kv_send=sums, kv_recv=sums, send_sems=hops, recv_sems=hops)
    names = (*inputs, *operands, *outs, *buffers, *semaphores)
    gradient, wide, down, little = pl.pallas_call(
        functools.partial(final_kernel, (nb, m, n, piece, rows, padded, near_width), names),
        out_shape=[shaped(entry) for entry in outs.values()],
        in_specs=[spec(pltpu.VMEM)] * len(inputs) + [spec(pl.ANY)] * len(operands),
        out_specs=[spec(pltpu.VMEM)] * len(outs),
        scratch_shapes=spaces(buffers.values()) + dma_semaphores(*semaphores.values()),
        compiler_params=pltpu.CompilerParams(
            collective_id=0, has_side_effects=True, vmem_limit_bytes=VMEM_LIMIT
        ),
        cost_estimate=pl.CostEstimate(
            flops=2 * tokens * width * 14000, bytes_accessed=30 * 1024 * 1024, transcendentals=0
        ),
        name="weight_grads",
    )(*inputs.values(), *operands.values())
    shapes = (
        (1, rows), (1, rows), (rows, width), (KEYS_WIDTH, rows), (KEYS_WIDTH, rows), (rows, width),
        (rows, hidden_units), (rows, hidden_units), (5 * down_rows, width), (2, rows), (width, piece), (width, piece),
    )
    outs = pl.pallas_call(
        functools.partial(unpack_kernel, (rows, padded)),
        out_shape=[jax.ShapeDtypeStruct(shape, jnp.float32) for shape in shapes],
        in_specs=[spec(pl.ANY)] * 5,
        out_specs=[spec(pltpu.VMEM)] * 12,
        scratch_shapes=[pltpu.VMEM(array.shape, array.dtype) for array in (wide, down, little)]
        + spaces([((rows, 2560), jnp.float32)]) + dma_semaphores((5,)),
        compiler_params=pltpu.CompilerParams(vmem_limit_bytes=VMEM_LIMIT),
        name="unpack",
    )(wide, down, little, saved["hidden_out"], gradient)
    norm_a, norm_f, query, key, value, out, gate, up, down, router, hidden, gradient = outs
    return (
        hidden.T[None], gradient.T[None], norm_a[0], norm_f[0], query, key.T, value.T, out, gate, up, down, router.T,
    )


def local(
    tokens,
    depths,
    segments,
    norm_attn,
    norm_ffn,
    w_query,
    key_weight,
    value_weight,
    w_out,
    w_gate,
    w_up,
    w_down,
    w_router,
    cotangent,
    mesh_sizes,
):
    piece = tokens.shape[1]
    positions = lax.axis_index("blk") * piece + jnp.arange(piece, dtype=jnp.int32)
    angles = frequencies(HEAD_DIMENSION)[:, None] * positions.astype(jnp.float32)[None, :]
    tables = dict(cosines=jnp.cos(angles), sines=jnp.sin(angles), norms=jnp.stack([norm_attn, norm_ffn]))
    routing = dict(router=w_router.T, depths=depths)
    heads = dict(w_query_hbm=w_query, key_weight_hbm=key_weight.T, value_weight_hbm=value_weight.T)
    weights = heads | dict(w_out_hbm=w_out, w_gate_hbm=w_gate, w_up_hbm=w_up, w_down_hbm=w_down.T)
    nb = mesh_sizes[0]
    saved = forward(
        tables | routing | dict(tokens=tokens[0].T, cotangent=cotangent[0].T, segments=segments), weights, nb
    )
    operands = dict(
        metas_hbm=saved["metas"], turned_hbm=saved["turned"], dat_hbm=saved["dat"], att_hbm=saved["att"],
        lse_hbm=saved["lse"], kv_hbm=saved["kv"], grad_hbm=saved["grad_hidden"], hid_1_hbm=saved["hid_1"],
        hid_0_hbm=saved["hid"], branch_hbm=saved["branch"], slope_hbm=saved["slope"], silu_hbm=saved["silu"],
        middle_hbm=saved["middle"],
    )
    bottom = backward(1, tables | routing | dict(small_before=saved["small"]), weights | operands, nb)
    return final(tables, saved, saved, bottom, weights, mesh_sizes)


def solution(mesh):
    sizes = (mesh.shape["blk"], mesh.shape["dp"])
    return jax.shard_map(
        functools.partial(local, mesh_sizes=sizes),
        mesh=mesh,
        in_specs=(
            P("dp", "blk", None),
            P("dp", "blk"),
            P("dp", "blk"),
            P(),
            P(),
            P(),
            P(),
            P(),
            P(),
            P(),
            P(),
            P(),
            P(),
            P("dp", "blk", None),
        ),
        out_specs=(
            P("dp", "blk", None),
            P("dp", "blk", None),
            P("blk"),
            P("blk"),
            P("blk", None),
            P("blk", None),
            P("blk", None),
            P("blk", None),
            P("blk", None),
            P("blk", None),
            P("blk", None),
            P("blk", None),
        ),
        check_vma=False,
    )
```

```python
import functools
import itertools
import math
import types

import jax
import jax.numpy as jnp
from jax import lax
from jax.experimental import pallas as pl
from jax.experimental.pallas import tpu as pltpu
from jax.sharding import PartitionSpec as P

QUERY_HEADS = 15
KEY_VALUE_HEADS = 5
HEAD_DIMENSION = 64
RECUR = 2
HEAD_SHARE = QUERY_HEADS // KEY_VALUE_HEADS
KEYS_WIDTH = KEY_VALUE_HEADS * HEAD_DIMENSION
PAIR = 2 * HEAD_DIMENSION
FF_TILE = 512
UNIT_COLUMNS = 256
VMEM_LIMIT = 63 * 1024 * 1024

epsilon = 1e-05
masked_score = -1e30
low = jnp.bfloat16


def frequencies(head_size):
    return jnp.exp(
        jnp.arange(head_size // 2, dtype=jnp.float32) * (-2.0 * math.log(10000.0) / head_size)
    )


def rms_scale(values):
    return lax.rsqrt(jnp.mean(values * values, axis=-1, keepdims=True) + epsilon)


def norm_gradient(grad_norm, values, gain):
    scale = rms_scale(values)
    weighted = grad_norm * gain
    grad_values = scale * weighted - values * (scale * scale * scale) * jnp.mean(
        weighted * values, axis=-1, keepdims=True
    )
    return grad_values, jnp.sum(grad_norm * values * scale, axis=0, keepdims=True)


def dot_last(left, right):
    return lax.dot_general(left, right, (((1,), (1,)), ((), ())), preferred_element_type=jnp.float32)


def plain_dot(left, right):
    return jnp.dot(left, right, preferred_element_type=jnp.float32)


def bits_of(number, count):
    return tuple((number >> (count - 1 - at)) & 1 for at in range(count))


def bit_of(position, bit):
    return lax.rem(position // (1 << bit), 2)


def block_bits(block, m):
    return tuple(bit_of(block, bit) for bit in range(m - 1, -1, -1))


def flipped(position, bit):
    return position + (1 << bit) * (1 - 2 * bit_of(position, bit))


def remote(source, target, sems, at, device):
    return pltpu.make_async_remote_copy(
        src_ref=source,
        dst_ref=target,
        send_sem=sems[0].at[at],
        recv_sem=sems[1].at[at],
        device_id=device,
        device_id_type=pl.DeviceIdType.MESH,
    )


def greet(partners):
    barrier = pltpu.get_barrier_semaphore()
    for partner in partners:
        pl.semaphore_signal(barrier, inc=1, device_id=partner, device_id_type=pl.DeviceIdType.MESH)
    pl.semaphore_wait(barrier, len(partners))


def turn_heads(turned, cosine, sine, heads):
    split = turned.reshape(heads, 2, HEAD_DIMENSION // 2, turned.shape[1])
    first, second = split[:, 0], split[:, 1]
    both = jnp.stack([first * cosine - second * sine, second * cosine + first * sine], axis=1)
    return both.reshape(turned.shape)


def turn_back(turned, cosine, sine, heads):
    return turn_heads(turned, cosine, -sine, heads)


def head_rows(group, member):
    head = group * HEAD_SHARE + member
    return pl.ds(pl.multiple_of(head * HEAD_DIMENSION, HEAD_DIMENSION), HEAD_DIMENSION)


def as_column(row):
    wide = jnp.broadcast_to(row.astype(jnp.float32), (8, row.shape[1]))
    return wide.T[:, 0:1]


def key_pairs(blk):
    return (blk + 2) // 2


def fill_bias(bias, metas, query_segments, level, blk, m, piece):
    key_at = lax.broadcasted_iota(jnp.int32, (piece, piece), 0)
    query_at = lax.broadcasted_iota(jnp.int32, (piece, piece), 1)

    @pl.loop(0, 2 * key_pairs(blk))
    def _(block):
        columns = metas[block_bits(block, m)].T
        live = jnp.where(columns[:, 1:2] > level, columns[:, 0:1], -1.0)
        shift = (blk - block) * piece
        allowed = (live == query_segments) & (key_at <= query_at + shift) | (key_at == query_at + shift)
        bias[block] = jnp.where(allowed, 0.0, masked_score).astype(bias.dtype)


def pair_bias(bias, pair, piece):
    here = bias[pl.ds(2 * pair, 2)].reshape(2 * piece, piece).astype(jnp.float32)
    return jnp.concatenate([here] * HEAD_SHARE, axis=1)


def spec(memory):
    return pl.BlockSpec(memory_space=memory)


def shaped(entry):
    return jax.ShapeDtypeStruct(*entry)


def spaces(entries):
    return [pltpu.VMEM(*entry) for entry in entries]


def dma_semaphores(*shapes):
    return [pltpu.SemaphoreType.DMA(shape) for shape in shapes]


class Piece:
    def __init__(self, at, kept_at, slot, flavour, family, sems, bits):
        self.at, self.kept_at, self.slot, self.family, self.sems = at, kept_at, slot, family, sems
        self.m, self.n = bits
        left = list(range(self.m - 1, -1, -1))
        self.order = []
        for stage in range(self.m):
            place = len(left) - 1 if stage == 0 or flavour == 0 else 0
            self.order.append((left.pop(place), place, len(left)))
        self.last = self.m + self.n
        self.blk = lax.axis_index("blk")
        self.dp = lax.axis_index("dp") if self.n else None

    def half(self, ref, side):
        rows, columns = self.family.shape
        if self.family.split == 0:
            return ref.at[pl.ds(pl.multiple_of(side * (rows // 2), rows // 2), rows // 2), :]
        return ref.at[:, pl.ds(pl.multiple_of(side * (columns // 2), columns // 2), columns // 2)]

    def held(self, stage):
        if stage == 0:
            return self.family.part, self.slot
        return self.family.blk[stage - 1], self.kept_at

    def copy(self, stage):
        m, family = self.m, self.family
        if stage < m:
            bit, place, others = self.order[stage]
            ref, index = self.held(stage)
            chosen = [slice(None)] * (others + 1)
            chosen[place] = 1 - bit_of(self.blk, bit)
            source = ref.at[(index, *chosen)]
            target = family.blk[stage].at[self.kept_at]
            device = {"blk": flipped(self.blk, bit)}
        elif stage < self.last:
            bit = stage - m
            if bit == 0:
                source = self.half(family.blk[m - 1].at[self.kept_at], 1 - bit_of(self.dp, 0))
            else:
                source = family.dp[bit - 1].at[self.kept_at]
            target = family.dp[bit].at[self.kept_at]
            device = {"dp": flipped(self.dp, bit)}
        else:
            source = self.half(family.out.at[self.kept_at], bit_of(self.dp, 0))
            target = source
            device = {"dp": flipped(self.dp, 0)}
        return remote(source, target, self.sems, (self.at, stage), device)

    def start(self, stage):
        self.copy(stage).start()

    def finish(self, stage):
        m, family = self.m, self.family
        self.copy(stage).wait_recv()
        if stage < m:
            bit, place, others = self.order[stage]
            ref, index = self.held(stage)
            for combo in itertools.product(range(2), repeat=others):
                chosen = list(combo)
                chosen.insert(place, bit_of(self.blk, bit))
                into = family.blk[stage].at[(self.kept_at, *combo)]
                self.add(into, into, ref.at[(index, *chosen)])
            if stage == 0:
                self.copy(0).wait_send()
        elif stage < self.last:
            bit = stage - m
            got = family.dp[bit].at[self.kept_at]
            if bit == 0:
                own = self.half(family.blk[m - 1].at[self.kept_at], bit_of(self.dp, 0))
            else:
                own = family.dp[bit - 1].at[self.kept_at]
            into = got
            if stage == self.last - 1:
                into = self.half(family.out.at[self.kept_at], bit_of(self.dp, 0))
            self.add(into, got, own)

    def add(self, into, left, right):
        into[...] = left[...] + right[...]

    def drained(self, stages):
        for stage in stages:
            self.copy(stage).wait_send()


def feed_forward_backward(at, level, gradient, ready, done):
    tiles = at.w_gate.shape[1] // FF_TILE
    column = at.router[level:level + 1, :].astype(jnp.float32)
    active = as_column(at.depths[...]) > float(level)
    hidden = at.hid_level[...]
    chosen = jax.nn.sigmoid(jnp.sum(hidden * column, axis=1, keepdims=True))
    at.dbranch[...] = jnp.where(active, chosen, 0.0) * gradient
    dchosen = jnp.where(active, jnp.sum(gradient * at.branch_level[...], axis=1, keepdims=True), 0.0)
    dlogit = dchosen * chosen * (1.0 - chosen)
    at.small[2 + level:3 + level, :] = jnp.sum(hidden * dlogit, axis=0, keepdims=True)
    at.grad_hidden[...] = gradient + dlogit * column
    at.dffn[...] = at.dbranch[...].astype(low)

    def dinner_of(tile):
        ready(tile)
        return plain_dot(at.dffn[...], at.w_down[:, tile * FF_TILE:(tile + 1) * FF_TILE])

    dinner = dinner_of(0)
    for tile in range(tiles):
        following = dinner_of(tile + 1) if tile + 1 < tiles else None
        columns = slice(tile * FF_TILE, (tile + 1) * FF_TILE)
        dgate = (dinner * at.slope_level[:, columns].astype(jnp.float32)).astype(low)
        dup = (dinner * at.silu_level[:, columns].astype(jnp.float32)).astype(low)
        at.dgate[:, columns] = dgate
        at.dup[:, columns] = dup
        done(tile)
        share = plain_dot(at.w_gate[:, columns], dgate.T) + plain_dot(at.w_up[:, columns], dup.T)
        if tile == 0:
            at.dnorm_turned[...] = share
        else:
            at.dnorm_turned[...] += share
        dinner = following
    ready(None)
    dnorm = at.dnorm_turned[...].T
    dmiddle, gain_share = norm_gradient(dnorm, at.middle_level[...], at.norms[1:2, :].astype(jnp.float32))
    at.small[1:2, :] += gain_share
    at.grad_hidden[...] += dmiddle
    dattn = (at.dbranch[...] + dmiddle).astype(low)
    lead = at.far.shape[1] - dattn.shape[1]
    at.far[:, :lead] = jnp.zeros((dattn.shape[0], lead), low)
    at.far[:, lead:] = dattn
    at.dat[...] = plain_dot(at.w_out[...], dattn.T).astype(low)


def forward_kernel(sizes, names, *refs):
    m, piece = sizes
    at = types.SimpleNamespace(**dict(zip(names, refs)))
    blk = lax.axis_index("blk")
    mine = block_bits(blk, m)
    kv, metas = at.kv, at.metas
    weights = (
        (at.key_weight_hbm, at.key_weight), (at.value_weight_hbm, at.value_weight), (at.w_query_hbm, at.w_query),
        (at.w_out_hbm, at.w_out), (at.w_gate_hbm, at.w_gate), (at.w_up_hbm, at.w_up), (at.w_down_hbm, at.w_down),
    )
    loads = [pltpu.make_async_copy(*pair, at.load_sems.at[index]) for index, pair in enumerate(weights)]
    for load in loads:
        load.start()
    saved = (
        (at.normed, at.normed_out), (at.turned, at.turned_out), (kv, at.kv_out), (at.lse, at.lse_out),
        (at.att, at.att_out), (at.nffn, at.nffn_out), (at.inner, at.inner_out),
    )

    def save(index, level):
        return pltpu.make_async_copy(
            saved[index][0].at[level], saved[index][1].at[level], at.save_sems.at[index, level]
        )

    first = (
        (at.hid.at[0], at.hid_out), (at.middle.at[0], at.middle_out), (at.silu.at[0], at.silu_out),
        (at.slope.at[0], at.slope_out), (at.branch.at[0], at.branch_out), (metas, at.metas_out),
        (at.far, at.far_out), (at.dat, at.dat_out), (at.dffn, at.dffn_out), (at.dgate, at.dgate_out), (at.dup, at.dup_out),
        (at.hid.at[1], at.hid_1_out),
    )
    late = [pltpu.make_async_copy(*pair, at.late_sems.at[index]) for index, pair in enumerate(first)]
    segment_row = at.segments[...].astype(jnp.float32)
    depth_column = as_column(at.depths[...])
    metas[mine] = jnp.concatenate(
        [segment_row, at.depths[...].astype(jnp.float32), jnp.zeros((6, piece), jnp.float32)], axis=0
    )
    greet([{"blk": flipped(blk, bit)} for bit in range(m)])

    def place(known):
        return tuple(slice(None) if bit in known else mine[m - 1 - bit] for bit in range(m - 1, -1, -1))

    orders = (list(range(1, m)), list(range(m - 1, 0, -1)))
    kv_sems = (at.kv_send, at.kv_recv)

    def kv_copies(level, group, stage):
        if stage == m - 1:
            ref = kv.at[(level, group, *place(range(1, m)))]
            return [remote(ref, ref, kv_sems, (level, group, 2 * stage), {"blk": flipped(blk, 0)})]
        copies = []
        for side, order in enumerate(orders):
            rows = pl.ds(side * (piece // 2), piece // 2)
            ref = kv.at[(level, group, *place(order[:stage]), rows)]
            copies.append(remote(ref, ref, kv_sems, (level, group, 2 * stage + side), {"blk": flipped(blk, order[stage])}))
        return copies

    def kv_advance(level, group, stage):
        if stage > 0:
            for copy in kv_copies(level, group, stage - 1):
                copy.wait_recv()
        if stage < m:
            for copy in kv_copies(level, group, stage):
                copy.start()

    def meta_copy(stage):
        bits = list(range(1, m)) + [0]
        ref = metas.at[place(bits[:stage])]
        return remote(ref, ref, (at.meta_send, at.meta_recv), stage, {"blk": flipped(blk, bits[stage])})

    meta_copy(0).start()
    cosine, sine = at.cosines[...], at.sines[...]
    gain_attn, gain_ffn = at.norms[0:1, :].astype(jnp.float32), at.norms[1:2, :].astype(jnp.float32)
    routers = at.router[...].astype(jnp.float32)
    at.hid[0] = at.tokens[...].T.astype(jnp.float32)
    late[0].start()
    at.query_pad[HEAD_DIMENSION:, :] = jnp.zeros_like(at.query_pad[HEAD_DIMENSION:, :])

    @pl.loop(0, RECUR)
    def _(level):
        hidden = at.hid[level]
        at.flat[...] = (hidden * rms_scale(hidden) * gain_attn).astype(low)
        at.normed[level] = at.flat[...].T

        @pl.when(level == 0)
        def _():
            for load in loads[:2]:
                load.wait()

        keys = turn_heads(plain_dot(at.key_weight[...], at.normed[level]), cosine, sine, KEY_VALUE_HEADS)
        values = plain_dot(at.value_weight[...], at.normed[level])
        for group in range(KEY_VALUE_HEADS):
            here = slice(group * HEAD_DIMENSION, (group + 1) * HEAD_DIMENSION)
            both = jnp.concatenate([keys[here], values[here]], axis=0)
            kv[(level, group, *mine)] = both.T.astype(low)
            kv_advance(level, group, 0)

        @pl.when(level == 0)
        def _():
            loads[2].wait()
            for stage in range(1, m - 1):
                meta_copy(stage - 1).wait_recv()
                meta_copy(stage).start()

        queries = turn_heads(plain_dot(at.flat[...], at.w_query[...]).T, cosine, sine, QUERY_HEADS)
        at.turned[level] = (queries * HEAD_DIMENSION ** (-0.5)).astype(low)

        @pl.when(level == 0)
        def _():
            for stage in range(max(1, m - 1), m):
                meta_copy(stage - 1).wait_recv()
                meta_copy(stage).start()

        for stage in range(1, m - 1):
            for group in range(KEY_VALUE_HEADS):
                kv_advance(level, group, stage)
        kv_advance(level, 0, m - 1)

        @pl.when(level == 0)
        def _():
            meta_copy(m - 1).wait_recv()
            late[5].start()

        fill_bias(at.bias, metas, segment_row, level.astype(jnp.float32), blk, m, piece)

        @pl.loop(0, KEY_VALUE_HEADS)
        def _(group):
            @pl.when(group + 1 < KEY_VALUE_HEADS)
            def _():
                kv_advance(level, group + 1, m - 1)

            kv_advance(level, group, m)
            for member in range(HEAD_SHARE):
                at.query_pad[:HEAD_DIMENSION, member * piece:(member + 1) * piece] = at.turned[level, head_rows(group, member), :]
            at.top[...] = jnp.full_like(at.top, masked_score)
            at.total[...] = jnp.zeros_like(at.total)

            @pl.loop(0, key_pairs(blk))
            def _(step):
                pair = key_pairs(blk) - 1 - step
                rows = kv[(level, group, *block_bits(pair, m - 1))].reshape(2 * piece, PAIR)
                scores = plain_dot(rows, at.query_pad[...]) + pair_bias(at.bias, pair, piece)
                before = at.top[0:1, :]
                after = jnp.maximum(before, jnp.max(scores, axis=0, keepdims=True))
                raised = jnp.exp(scores - after)
                shrink = jnp.exp(before - after)
                at.top[0:1, :] = after
                ones = jnp.ones((16, 2 * piece), low)
                left = jnp.concatenate([rows.T[HEAD_DIMENSION:], ones], axis=0)
                at.total[...] = at.total[...] * shrink + plain_dot(left, raised.astype(low))

            sums = at.total[HEAD_DIMENSION:HEAD_DIMENSION + 1, :]
            at.lse[level, pl.ds(group, 1), :] = at.top[0:1, :] + jnp.log(sums)
            out = at.total[:HEAD_DIMENSION, :] / sums
            for member in range(HEAD_SHARE):
                at.att[level, head_rows(group, member), :] = out[:, member * piece:(member + 1) * piece].astype(low)

        for index in range(5):
            save(index, level).start()

        @pl.when(level == 0)
        def _():
            loads[3].wait()

        attn = plain_dot(at.att[level].T, at.w_out[...])
        mid = at.hid[level] + attn
        at.middle[level] = mid
        at.branch[level] = attn
        at.flat[...] = (mid * rms_scale(mid) * gain_ffn).astype(low)
        at.nffn[level] = at.flat[...].T
        save(5, level).start()

        @pl.when(level == 0)
        def _():
            loads[4].wait()
            loads[5].wait()

        for tile in range(at.w_gate.shape[1] // FF_TILE):
            columns = slice(tile * FF_TILE, (tile + 1) * FF_TILE)
            gate_pre = plain_dot(at.flat[...], at.w_gate[:, columns])
            up_pre = plain_dot(at.flat[...], at.w_up[:, columns])
            opened = jax.nn.sigmoid(gate_pre)
            passed = gate_pre * opened
            at.silu[level, :, columns] = passed.astype(low)
            at.slope[level, :, columns] = (up_pre * (opened + passed - passed * opened)).astype(low)
            at.inner[level, columns, :] = (passed * up_pre).astype(low).T

        save(6, level).start()

        @pl.when(level == 0)
        def _():
            loads[6].wait()

        at.branch[level] += plain_dot(at.w_down[...], at.inner[level]).T
        column = jnp.where(level == 0, routers[0:1, :], routers[1:2, :])
        logit = jnp.sum(at.hid[level] * column, axis=1, keepdims=True)
        weight = jnp.where(depth_column > level.astype(jnp.float32), jax.nn.sigmoid(logit), 0.0)
        at.hid[level + 1] = at.hid[level] + weight * at.branch[level]

        @pl.when(level == 0)
        def _():
            for copy in late[1:5]:
                copy.start()

    at.hidden_out[...] = at.hid[RECUR].T
    top = RECUR - 1
    at.hid_level, at.branch_level, at.middle_level = at.hid.at[top], at.branch.at[top], at.middle.at[top]
    at.silu_level, at.slope_level = at.silu.at[top], at.slope.at[top]
    at.small[...] = jnp.zeros_like(at.small)
    feed_forward_backward(at, top, at.cotangent[...].T.astype(jnp.float32), lambda tile: None, lambda tile: None)
    for copy in late[6:]:
        copy.start()
    for stage in range(m):
        meta_copy(stage).wait_send()
    for level in range(RECUR):
        for group in range(KEY_VALUE_HEADS):
            for stage in range(m):
                for copy in kv_copies(level, group, stage):
                    copy.wait_send()
        for index in range(len(saved)):
            save(index, level).wait()
    for copy in late:
        copy.wait()


def far_width(width):
    return 2 * width + 2 * KEYS_WIDTH - 1536


def forward(small, weights, nb):
    m = nb.bit_length() - 1
    width, piece = small["tokens"].shape
    hidden_units = weights["w_gate_hbm"].shape[1]
    blocks, wide = (2,) * m, HEAD_SHARE * piece
    rows, turned = ((piece, width), jnp.float32), ((RECUR, width, piece), low)
    hidden = ((piece, hidden_units), low)
    saved = dict(
        normed=turned, turned=turned, kv=((RECUR, KEY_VALUE_HEADS, *blocks, piece, PAIR), low),
        lse=((RECUR, 8, wide), jnp.float32), att=turned, nffn=turned, inner=((RECUR, hidden_units, piece), low),
        metas=((*blocks, 8, piece), jnp.float32), far=((piece, far_width(width)), low), dat=((width, piece), low),
        dffn=((piece, width), low), dgate=hidden, dup=hidden,
    )
    first = dict(hid=rows, middle=rows, silu=hidden, slope=hidden, branch=rows)
    outs = dict(hidden_out=((width, piece), jnp.float32), grad_hidden=rows, small=((8, width), jnp.float32))
    anywhere = {name + "_out": entry for name, entry in (saved | first | dict(hid_1=rows)).items()}
    both = {name: ((RECUR, *shape), dtype) for name, (shape, dtype) in first.items()}
    buffers = {name[:-4]: (array.shape, array.dtype) for name, array in weights.items()} | saved | both | dict(
        hid=((RECUR + 1, piece, width), jnp.float32), flat=((piece, width), low),
        bias=((nb, piece, piece), jnp.float32), query_pad=((PAIR, wide), low), top=((8, wide), jnp.float32),
        total=((HEAD_DIMENSION + 16, wide), jnp.float32), dbranch=rows, dnorm_turned=((width, piece), jnp.float32),
    )
    semaphores = dict(
        load_sems=(7,), save_sems=(7, RECUR), late_sems=(12,), kv_send=(RECUR, KEY_VALUE_HEADS, 2 * m),
        kv_recv=(RECUR, KEY_VALUE_HEADS, 2 * m), meta_send=(m,), meta_recv=(m,),
    )
    results = pl.pallas_call(
        functools.partial(forward_kernel, (m, piece), (*small, *weights, *outs, *anywhere, *buffers, *semaphores)),
        out_shape=[shaped(entry) for entry in (outs | anywhere).values()],
        in_specs=[spec(pltpu.VMEM)] * len(small) + [spec(pl.ANY)] * len(weights),
        out_specs=[spec(pltpu.VMEM)] * len(outs) + [spec(pl.ANY)] * len(anywhere),
        scratch_shapes=spaces(buffers.values()) + dma_semaphores(*semaphores.values()),
        compiler_params=pltpu.CompilerParams(
            collective_id=1, has_side_effects=True, vmem_limit_bytes=VMEM_LIMIT
        ),
        cost_estimate=pl.CostEstimate(
            flops=3 * RECUR * piece * width * 10240, bytes_accessed=48 * 1024 * 1024, transcendentals=0
        ),
        name="forward_levels",
    )(*small.values(), *weights.values())
    return dict(zip((*outs, *(name[:-4] for name in anywhere)), results))


class AttentionBackward:
    def __init__(self, at, m, piece, level):
        self.at, self.m, self.piece, self.level = at, m, piece, level
        self.blk = lax.axis_index("blk")
        self.family = types.SimpleNamespace(part=at.part, blk=at.halves, dp=(), out=None, shape=(piece // 2, PAIR), split=0)

    def pieces(self, group):
        sems = (self.at.kv_send, self.at.kv_recv)
        return [
            Piece(2 * group + side, 2 * group + side, 2 * group + side, side, self.family, sems, (self.m, 0))
            for side in range(2)
        ]

    def move(self, group, stage):
        for piece_of in self.pieces(group):
            piece_of.finish(stage)
            if stage + 1 < self.m:
                piece_of.start(stage + 1)

    def begin(self):
        at = self.at
        query_segments = at.metas[block_bits(self.blk, self.m)][0:1, :]
        fill_bias(at.bias, at.metas, query_segments, float(self.level), self.blk, self.m, self.piece)
        at.query_pad[HEAD_DIMENSION:, :] = jnp.zeros_like(at.query_pad[HEAD_DIMENSION:, :])
        at.dat_pad[:HEAD_DIMENSION, :] = jnp.zeros_like(at.dat_pad[:HEAD_DIMENSION, :])

    def group(self, group):
        at, m, piece, blk = self.at, self.m, self.piece, self.blk
        half = piece // 2
        carried = []
        for member in range(HEAD_SHARE):
            rows, lanes = head_rows(group, member), slice(member * piece, (member + 1) * piece)
            at.query_pad[:HEAD_DIMENSION, lanes] = at.turned[rows, :]
            at.dat_pad[HEAD_DIMENSION:, lanes] = at.dat_turned[rows, :]
            product = at.dat_turned[rows, :].astype(jnp.float32) * at.att_turned[rows, :].astype(jnp.float32)
            carried.append(jnp.sum(product, axis=0, keepdims=True))
        carried = jnp.concatenate(carried, axis=1)
        at.query_rows[...] = at.query_pad[...].T
        at.dat_rows[...] = at.dat_pad[...].T
        log_total = at.lse[pl.ds(group, 1), :]
        at.dq_sum[...] = jnp.zeros_like(at.dq_sum)

        @pl.loop(0, key_pairs(blk))
        def _(pair):
            rows = at.kv[(group, *block_bits(pair, m - 1))].reshape(2 * piece, PAIR)
            probability = jnp.exp(plain_dot(rows, at.query_pad[...]) + pair_bias(at.bias, pair, piece) - log_total)
            dprob = plain_dot(rows, at.dat_pad[...])
            dscores = (probability * (dprob - carried)).astype(low)
            share = plain_dot(dscores, at.query_rows[...]) + plain_dot(probability.astype(low), at.dat_rows[...])
            share = share.astype(low)
            for block in range(2):
                for side in range(2):
                    first = block * piece + side * half
                    at.part[(2 * group + side, *block_bits(pair, m - 1), block)] = share[first:first + half]
            at.dq_sum[...] += plain_dot(rows.T[:HEAD_DIMENSION], dscores)

        @pl.loop(key_pairs(blk), 1 << (m - 1))
        def _(pair):
            for block in range(2):
                for side in range(2):
                    at.part[(2 * group + side, *block_bits(pair, m - 1), block)] = jnp.zeros((half, PAIR), low)

        for piece_of in self.pieces(group):
            piece_of.start(0)
        for member in range(HEAD_SHARE):
            at.dq_turned[head_rows(group, member), :] = at.dq_sum[:, member * piece:(member + 1) * piece]

    def follow(self, group):
        for stage in range(self.m - 1):
            earlier = group - 1 - stage
            if isinstance(group, int):
                if 0 <= earlier < KEY_VALUE_HEADS:
                    self.move(earlier, stage)
            else:
                @pl.when(earlier >= 0)
                def _():
                    self.move(earlier, stage)

    def queries(self, cosine, sine):
        at = self.at
        dqueries = turn_back(at.dq_turned[...] * HEAD_DIMENSION ** (-0.5), cosine, sine, QUERY_HEADS).astype(low)
        self.put(2 * KEYS_WIDTH, dqueries.T)
        at.dnorm[...] = plain_dot(at.w_query[...], dqueries).T

    def put(self, column, values):
        self.at.near[:, column:column + values.shape[1]] = values

    def keys(self, cosine, sine):
        at, m = self.at, self.m
        filled = 2 * KEYS_WIDTH + QUERY_HEADS * HEAD_DIMENSION
        self.put(filled, jnp.zeros((self.piece, at.near.shape[1] - filled), low))
        dkeys, dvalues = [], []
        for group in range(KEY_VALUE_HEADS):
            self.move(group, m - 1)
            both = jnp.concatenate([at.halves[m - 1][2 * group], at.halves[m - 1][2 * group + 1]], axis=0).T
            dkeys.append(both[:HEAD_DIMENSION].astype(jnp.float32))
            dvalues.append(both[HEAD_DIMENSION:])
        dkeys = turn_back(jnp.concatenate(dkeys, axis=0), cosine, sine, KEY_VALUE_HEADS).astype(low).T
        dvalues = jnp.concatenate(dvalues, axis=0).T
        self.put(0, dkeys)
        self.put(KEYS_WIDTH, dvalues)
        at.dnorm[...] += plain_dot(dkeys, at.key_weight[...]) + plain_dot(dvalues, at.value_weight[...])

    def drained(self):
        for group in range(KEY_VALUE_HEADS):
            for piece_of in self.pieces(group):
                piece_of.drained(range(1, self.m))


def attention_buffers(nb, piece, width, bias_type):
    m, wide, heads = nb.bit_length() - 1, HEAD_SHARE * piece, 2 * KEY_VALUE_HEADS
    turned, weight = ((width, piece), low), ((KEYS_WIDTH, width), low)
    pad, pad_rows = ((PAIR, wide), low), ((wide, PAIR), low)
    buffers = dict(
        turned=turned, dat_turned=turned, att_turned=turned, kv=((KEY_VALUE_HEADS, *(2,) * m, piece, PAIR), low),
        lse=((8, wide), jnp.float32), metas=((*(2,) * m, 8, piece), jnp.float32), w_query=((width, width), low),
        key_weight=weight, value_weight=weight, dq_turned=((width, piece), jnp.float32),
        bias=((nb, piece, piece), bias_type), query_pad=pad, dat_pad=pad, query_rows=pad_rows, dat_rows=pad_rows,
        dq_sum=((HEAD_DIMENSION, wide), jnp.float32), part=((heads, *(2,) * m, piece // 2, PAIR), low),
        dnorm=((piece, width), jnp.float32), hid=((piece, width), jnp.float32),
    )
    for stage in range(m):
        buffers["half_%d" % stage] = ((heads, *(2,) * (m - 1 - stage), piece // 2, PAIR), low)
    return buffers


def backward_kernel(sizes, names, *refs):
    m, piece, level = sizes
    at = types.SimpleNamespace(**dict(zip(names, refs)))
    at.halves = [getattr(at, "half_%d" % stage) for stage in range(m)]
    at.near = at.near_out
    blk = lax.axis_index("blk")
    pairs = (
        (at.metas_hbm, at.metas), (at.turned_hbm.at[level], at.turned), (at.dat_hbm, at.dat_turned),
        (at.att_hbm.at[level], at.att_turned), (at.lse_hbm.at[level], at.lse), (at.kv_hbm.at[level], at.kv),
        (at.w_query_hbm, at.w_query), (at.key_weight_hbm, at.key_weight), (at.value_weight_hbm, at.value_weight),
        (at.grad_hbm, at.grad_hidden), (at.hid_1_hbm, at.hid),
        (at.hid_0_hbm, at.hid_level), (at.branch_hbm, at.branch_level), (at.w_down_hbm, at.w_down),
        (at.slope_hbm, at.slope_level), (at.silu_hbm, at.silu_level), (at.w_gate_hbm, at.w_gate), (at.w_up_hbm, at.w_up),
        (at.middle_hbm, at.middle_level), (at.w_out_hbm, at.w_out),
    )
    loads = [pltpu.make_async_copy(*pair, at.load_sems.at[index]) for index, pair in enumerate(pairs)]
    for load in loads:
        load.start()
    saves = [
        pltpu.make_async_copy(*pair, at.save_sems.at[index])
        for index, pair in enumerate(((at.dgate, at.dgate_out), (at.dup, at.dup_out)))
    ]
    greet([{"blk": flipped(blk, bit)} for bit in range(m)])
    work = AttentionBackward(at, m, piece, level)
    loads[0].wait()
    work.begin()
    for load in loads[1:6]:
        load.wait()

    @pl.loop(0, KEY_VALUE_HEADS)
    def _(group):
        work.group(group)
        work.follow(group)

    cosine, sine = at.cosines[...], at.sines[...]
    for virtual in range(KEY_VALUE_HEADS, KEY_VALUE_HEADS + m - 1):
        work.follow(virtual)
        if virtual == KEY_VALUE_HEADS:
            loads[6].wait()
            work.queries(cosine, sine)
    for load in loads[7:]:
        load.wait()
    work.keys(cosine, sine)
    dhidden, gain_share = norm_gradient(at.dnorm[...], at.hid[...], at.norms[0:1, :].astype(jnp.float32))
    at.small[...] = at.small_before[...]
    at.small[0:1, :] = gain_share
    gradient = at.grad_hidden[...] + dhidden
    at.dnorm[...] = gradient
    feed_forward_backward(at, level - 1, at.dnorm[...], lambda tile: None, lambda tile: None)
    for save in saves:
        save.start()
    work.drained()
    for save in saves:
        save.wait()


def backward(level, small, operands, nb):
    m = nb.bit_length() - 1
    piece, width = operands["grad_hbm"].shape
    hidden_units = operands["w_gate_hbm"].shape[1]
    rows, flat, hidden = ((piece, width), jnp.float32), ((piece, width), low), ((piece, hidden_units), low)
    outs = dict(
        grad_hidden=rows, small=((8, width), jnp.float32), near_out=((piece, 1792), low), dffn=flat,
        dat=((width, piece), low), far=((piece, far_width(width)), low),
    )
    anywhere = dict(dgate_out=hidden, dup_out=hidden)
    buffers = attention_buffers(nb, piece, width, jnp.float32) | dict(
        hid_level=rows, branch_level=rows, middle_level=rows, w_down=((width, hidden_units), low), slope_level=hidden,
        silu_level=hidden, w_gate=((width, hidden_units), low), w_up=((width, hidden_units), low),
        w_out=((width, width), low), dbranch=rows, dnorm_turned=((width, piece), jnp.float32), dgate=hidden, dup=hidden,
    )
    sums = (2 * KEY_VALUE_HEADS, m)
    semaphores = dict(load_sems=(20,), save_sems=(2,), kv_send=sums, kv_recv=sums)
    results = pl.pallas_call(
        functools.partial(
            backward_kernel, (m, piece, level), (*small, *operands, *outs, *anywhere, *buffers, *semaphores)
        ),
        out_shape=[shaped(entry) for entry in (outs | anywhere).values()],
        in_specs=[spec(pltpu.VMEM)] * len(small) + [spec(pl.ANY)] * len(operands),
        out_specs=[spec(pltpu.VMEM)] * len(outs) + [spec(pl.ANY)] * len(anywhere),
        scratch_shapes=spaces(buffers.values()) + dma_semaphores(*semaphores.values()),
        compiler_params=pltpu.CompilerParams(
            collective_id=2, has_side_effects=True, vmem_limit_bytes=VMEM_LIMIT
        ),
        cost_estimate=pl.CostEstimate(
            flops=2 * piece * width * 20000, bytes_accessed=32 * 1024 * 1024, transcendentals=0
        ),
        name="backward_level",
    )(*small.values(), *operands.values())
    return dict(zip((*outs, *anywhere), results))


WIDE_SLOTS, DOWN_SLOTS = 4, 2


def final_kernel(sizes, names, *refs):
    nb, m, n, piece, rows, padded, near_width = sizes
    at = types.SimpleNamespace(**dict(zip(names, refs)))
    at.halves = [getattr(at, "half_%d" % stage) for stage in range(m)]
    blk, dp = lax.axis_index("blk"), lax.axis_index("dp")
    at.near = at.gate_side.at[pl.ds(0, piece), pl.ds(0, near_width)]
    counter = itertools.count()

    def load(source, target):
        return pltpu.make_async_copy(source, target, at.load_sems.at[next(counter)])

    def both_lanes(ref, target):
        return [load(ref.at[level], target.at[:, pl.ds(level * piece, piece)]) for level in range(RECUR)]

    def both_rows(low_ref, deep_ref, target, width):
        pairs = ((low_ref, 0), (deep_ref, piece))
        return [load(ref, target.at[pl.ds(first, piece), pl.ds(0, width)]) for ref, first in pairs]

    hidden_units, width = at.gate_side.shape[1], at.dffn.shape[1]
    far_lanes = at.far_0_hbm.shape[1]
    loads = types.SimpleNamespace(
        nffn=both_lanes(at.nffn_hbm, at.left),
        dgate=both_rows(at.dgate_0_hbm, at.dgate_1_hbm, at.gate_side, hidden_units),
        inner=both_lanes(at.inner_hbm, at.inner),
        dffn=both_rows(at.dffn_0_hbm, at.dffn_1_hbm, at.dffn, width),
        metas=[load(at.metas_hbm, at.metas)],
        heads=[
            load(at.turned_hbm.at[0], at.turned), load(at.dat_hbm, at.dat_turned), load(at.att_hbm.at[0], at.att_turned),
            load(at.lse_hbm.at[0], at.lse), load(at.kv_hbm.at[0], at.kv),
        ],
        dup=both_rows(at.dup_0_hbm, at.dup_1_hbm, at.up_side, hidden_units),
        w_query=[load(at.w_query_hbm, at.w_query)],
        rest=[
            load(at.key_weight_hbm, at.key_weight), load(at.value_weight_hbm, at.value_weight),
            load(at.hid_hbm, at.hid), load(at.grad_hbm, at.grad),
        ],
        attended=both_lanes(at.attended_hbm, at.left_attended),
    )
    late = types.SimpleNamespace(
        near=[load(at.near_1_hbm, at.gate_side.at[pl.ds(piece, piece), pl.ds(0, near_width)])],
        far=both_rows(at.far_0_hbm, at.far_1_hbm, at.up_side, far_lanes),
        normed=both_lanes(at.normed_hbm, at.left),
    )

    def begin(copies):
        for copy in copies:
            copy.start()

    def ready(copies):
        for copy in copies:
            copy.wait()

    for copies in vars(loads).values():
        begin(copies)
    greet([{"blk": flipped(blk, bit)} for bit in range(m)] + [{"dp": flipped(dp, bit)} for bit in range(n)])

    down_rows = at.part_down.shape[-2]

    def family(name, shape, split):
        return types.SimpleNamespace(
            part=getattr(at, "part_" + name), out=getattr(at, "out_" + name), shape=shape, split=split,
            blk=[getattr(at, "blk_%s_%d" % (name, stage)) for stage in range(m)],
            dp=[getattr(at, "dp_%s_%d" % (name, stage)) for stage in range(n)],
        )

    wide = family("wide", (2 * padded, UNIT_COLUMNS), 1)
    down = family("down", (down_rows, width), 0)
    little = family("small", (16, 128), 0)
    sems = (at.send_sems, at.recv_sems)
    units = itertools.count()

    def unit(holder, index, flavour):
        return Piece(next(units), index, index % holder.part.shape[0], flavour, holder, sems, (m, n))

    pairs = [[unit(wide, 0, 0), unit(wide, 1, 1)]]
    pairs += [[unit(wide, index, 0), unit(down, index - 2, 1)] for index in range(2, 7)]
    pairs += [[unit(wide, index, 0), unit(wide, index + 1, 1)] for index in (7, 9, 11)]
    pairs += [[unit(wide, 13, 0), unit(wide, 14, 1), unit(little, 0, 0)]]

    def compute_wide(index, slot):
        if index == 0:
            ready(loads.nffn)
            ready(loads.dgate)
        if index == 5:
            begin(late.near)
            ready(loads.dup)
        if index == 10:
            begin(late.far)
            begin(late.normed)
            ready(late.near)
            ready(late.normed)
            ready(loads.attended)
            ready(late.far)
        block, column = index // 5, (index % 5) * UNIT_COLUMNS
        second = 1280 + column
        upper_columns, lower_columns = slice(column, column + UNIT_COLUMNS), slice(second, second + UNIT_COLUMNS)
        if block < 2:
            right = at.gate_side if block == 0 else at.up_side
            upper = plain_dot(at.left[...], right[:, upper_columns])
            lower = plain_dot(at.left[...], right[:, lower_columns])
        else:
            upper = plain_dot(at.left[...], at.gate_side[:, upper_columns])
            lower = None
            if second < 1600:
                lower = plain_dot(at.left[...], at.gate_side[:, lower_columns])
            if second >= 1536:
                more = plain_dot(at.left_attended[...], at.up_side[:, second - 1536:second - 1536 + UNIT_COLUMNS])
                lower = more if lower is None else lower + more
        for target in range(nb):
            here = slice(target * padded, (target + 1) * padded)
            both = jnp.concatenate([upper[here], lower[here]], axis=0)
            at.part_wide[(slot, *bits_of(target, m))] = both.astype(low)

    def compute_down(index, slot):
        if index == 0:
            ready(loads.inner)
            ready(loads.dffn)
        firsts = [(target * 5 + index) * down_rows for target in range(nb)]
        left = jnp.concatenate([at.inner[first:first + down_rows, :] for first in firsts], axis=0)
        result = plain_dot(left, at.dffn[...])
        for target in range(nb):
            at.part_down[(slot, *bits_of(target, m))] = result[target * down_rows:(target + 1) * down_rows].astype(low)

    def compute_small():
        total = at.small_before[...]
        total = total + jnp.concatenate([at.gain_row[...], jnp.zeros((7, width), jnp.float32)], axis=0)
        at.part_small[...] = jnp.zeros_like(at.part_small)
        for target in range(nb):
            at.part_small[(0, *bits_of(target, m), slice(0, 8), slice(0, rows))] = total[:, target * rows:(target + 1) * rows]

    def compute(piece_of):
        if piece_of.family is wide:
            compute_wide(piece_of.kept_at, piece_of.slot)
        elif piece_of.family is down:
            compute_down(piece_of.kept_at, piece_of.slot)
        else:
            compute_small()
        piece_of.start(0)

    def moves(tick):
        for stage in [0] + list(range(m + n - 1, 0, -1)):
            if 0 <= tick - stage < len(pairs):
                for piece_of in pairs[tick - stage]:
                    piece_of.finish(stage)
                    piece_of.start(stage + 1)

    work = AttentionBackward(at, m, piece, 0)
    for pair in pairs[:2]:
        for piece_of in pair:
            compute(piece_of)
    moves(0)
    for piece_of in pairs[2]:
        compute(piece_of)
    ready(loads.metas)
    work.begin()
    ready(loads.heads)
    for group in range(KEY_VALUE_HEADS):
        if group > 0:
            moves(group)
            for piece_of in pairs[group + 2]:
                compute(piece_of)
        work.group(group)
        work.follow(group)
    cosine, sine = at.cosines[...], at.sines[...]
    moves(5)
    compute(pairs[7][0])
    ready(loads.w_query)
    for virtual in range(KEY_VALUE_HEADS, KEY_VALUE_HEADS + m - 1):
        work.follow(virtual)
        if virtual == KEY_VALUE_HEADS:
            work.queries(cosine, sine)
    moves(6)
    ready(loads.rest)
    work.keys(cosine, sine)
    compute(pairs[7][1])
    moves(7)
    for piece_of in pairs[8] + pairs[9][:2]:
        compute(piece_of)
    dhidden, gain_share = norm_gradient(at.dnorm[...], at.hid[...], at.norms[0:1, :].astype(jnp.float32))
    at.gain_row[...] = gain_share
    at.grad_out[...] = (at.grad[...] + dhidden).T
    compute(pairs[9][2])
    for tick in range(8, len(pairs) + m + n - 1):
        moves(tick)
    for pair in pairs:
        for piece_of in pair:
            piece_of.finish(m + n)
    for pair in pairs:
        for piece_of in pair:
            piece_of.drained(range(1, m + n + 1))
    work.drained()


def unpack_kernel(sizes, wide_hbm, down_hbm, little_hbm, hidden_in, gradient_in, *refs):
    rows, padded = sizes
    norm_attn, norm_ffn, query, key, value, out, gate, up, down_out, router, hidden, gradient = refs[:12]
    wide, down, little, rest, sems = refs[12:]
    carried = [
        pltpu.make_async_copy(source, target, sems.at[at])
        for at, (source, target) in enumerate(((hidden_in, hidden), (gradient_in, gradient)))
    ]
    loads = [
        pltpu.make_async_copy(source, target, sems.at[2 + at])
        for at, (source, target) in enumerate(((wide_hbm, wide), (down_hbm, down), (little_hbm, little)))
    ]
    for copy in loads + carried:
        copy.start()
    for load in loads:
        load.wait()
    norm_attn[...] = little[0, 0:1, :rows]
    norm_ffn[...] = little[0, 1:2, :rows]
    router[...] = little[0, 2:4, :rows]
    for unit in range(5):
        for first, target in ((0, gate), (5, up), (10, rest)):
            tile = wide[first + unit].astype(jnp.float32)
            for side in range(2):
                column = side * 1280 + unit * UNIT_COLUMNS
                target[:, column:column + UNIT_COLUMNS] = tile[side * padded:side * padded + rows]
        down_rows = down.shape[1]
        down_out[unit * down_rows:(unit + 1) * down_rows, :] = down[unit].astype(jnp.float32)
    width = query.shape[1]
    key[...] = rest[:, :KEYS_WIDTH].T
    value[...] = rest[:, KEYS_WIDTH:2 * KEYS_WIDTH].T
    query[...] = rest[:, 2 * KEYS_WIDTH:2 * KEYS_WIDTH + width]
    out[...] = rest[:, 2 * KEYS_WIDTH + width:]
    for copy in carried:
        copy.wait()


def final(small, saved, top, bottom, weights, mesh_sizes):
    nb, nd = mesh_sizes
    m, n = nb.bit_length() - 1, nd.bit_length() - 1
    grad = bottom["grad_hidden"]
    piece, width = grad.shape
    hidden_units = weights["w_gate_hbm"].shape[1]
    rows = width // nb
    padded = -(-rows // 8) * 8
    down_rows = hidden_units // nb // 5
    tokens = RECUR * piece

    def spread(array):
        if padded == rows:
            return array
        split = array.reshape(RECUR, nb, rows, piece)
        return jnp.pad(split, ((0, 0), (0, 0), (0, padded - rows), (0, 0))).reshape(RECUR, nb * padded, piece)

    inputs = small | dict(small_before=bottom["small"])
    operands = dict(
        metas_hbm=saved["metas"], turned_hbm=saved["turned"], dat_hbm=bottom["dat"], att_hbm=saved["att"],
        lse_hbm=saved["lse"], kv_hbm=saved["kv"], w_query_hbm=weights["w_query_hbm"],
        key_weight_hbm=weights["key_weight_hbm"], value_weight_hbm=weights["value_weight_hbm"], hid_hbm=saved["hid"],
        grad_hbm=grad, inner_hbm=saved["inner"], nffn_hbm=spread(saved["nffn"]), normed_hbm=spread(saved["normed"]),
        attended_hbm=spread(saved["att"]), dffn_0_hbm=bottom["dffn"], dffn_1_hbm=top["dffn"],
        dgate_0_hbm=bottom["dgate_out"], dgate_1_hbm=top["dgate"], dup_0_hbm=bottom["dup_out"], dup_1_hbm=top["dup"],
        far_0_hbm=bottom["far"], far_1_hbm=top["far"], near_1_hbm=bottom["near_out"],
    )
    near_width = bottom["near_out"].shape[1]
    families = (
        ("wide", 15, (2 * padded, UNIT_COLUMNS), low, WIDE_SLOTS, 1), ("down", 5, (down_rows, width), low, DOWN_SLOTS, 0),
        ("small", 1, (16, 128), jnp.float32, 1, 0),
    )
    outs = dict(grad_out=((width, piece), jnp.float32))
    buffers = attention_buffers(nb, piece, width, low) | dict(
        grad=((piece, width), jnp.float32), gate_side=((tokens, hidden_units), low), up_side=((tokens, hidden_units), low),
        inner=((hidden_units, tokens), low), left=((nb * padded, tokens), low), left_attended=((nb * padded, tokens), low),
        dffn=((tokens, width), low), gain_row=((1, width), jnp.float32),
    )
    for name, count, shape, dtype, slots, split in families:
        outs["out_" + name] = ((count, *shape), dtype)
        buffers["part_" + name] = ((slots, *(2,) * m, *shape), dtype)
        for stage in range(m):
            buffers["blk_%s_%d" % (name, stage)] = ((count, *(2,) * (m - 1 - stage), *shape), dtype)
        half = (shape[0], shape[1] // 2) if split else (shape[0] // 2, shape[1])
        for stage in range(n):
            buffers["dp_%s_%d" % (name, stage)] = ((count, *half), dtype)
    sums, hops = (2 * KEY_VALUE_HEADS, m), (21, m + n + 1)
    semaphores = dict(load_sems=(32,), kv_send=sums, kv_recv=sums, send_sems=hops, recv_sems=hops)
    names = (*inputs, *operands, *outs, *buffers, *semaphores)
    gradient, wide, down, little = pl.pallas_call(
        functools.partial(final_kernel, (nb, m, n, piece, rows, padded, near_width), names),
        out_shape=[shaped(entry) for entry in outs.values()],
        in_specs=[spec(pltpu.VMEM)] * len(inputs) + [spec(pl.ANY)] * len(operands),
        out_specs=[spec(pltpu.VMEM)] * len(outs),
        scratch_shapes=spaces(buffers.values()) + dma_semaphores(*semaphores.values()),
        compiler_params=pltpu.CompilerParams(
            collective_id=0, has_side_effects=True, vmem_limit_bytes=VMEM_LIMIT
        ),
        cost_estimate=pl.CostEstimate(
            flops=2 * tokens * width * 14000, bytes_accessed=30 * 1024 * 1024, transcendentals=0
        ),
        name="weight_grads",
    )(*inputs.values(), *operands.values())
    shapes = (
        (1, rows), (1, rows), (rows, width), (KEYS_WIDTH, rows), (KEYS_WIDTH, rows), (rows, width),
        (rows, hidden_units), (rows, hidden_units), (5 * down_rows, width), (2, rows), (width, piece), (width, piece),
    )
    outs = pl.pallas_call(
        functools.partial(unpack_kernel, (rows, padded)),
        out_shape=[jax.ShapeDtypeStruct(shape, jnp.float32) for shape in shapes],
        in_specs=[spec(pl.ANY)] * 5,
        out_specs=[spec(pltpu.VMEM)] * 12,
        scratch_shapes=[pltpu.VMEM(array.shape, array.dtype) for array in (wide, down, little)]
        + spaces([((rows, 2560), jnp.float32)]) + dma_semaphores((5,)),
        compiler_params=pltpu.CompilerParams(vmem_limit_bytes=VMEM_LIMIT),
        name="unpack",
    )(wide, down, little, saved["hidden_out"], gradient)
    norm_a, norm_f, query, key, value, out, gate, up, down, router, hidden, gradient = outs
    return (
        hidden.T[None], gradient.T[None], norm_a[0], norm_f[0], query, key.T, value.T, out, gate, up, down, router.T,
    )


def local(
    tokens,
    depths,
    segments,
    norm_attn,
    norm_ffn,
    w_query,
    key_weight,
    value_weight,
    w_out,
    w_gate,
    w_up,
    w_down,
    w_router,
    cotangent,
    mesh_sizes,
):
    piece = tokens.shape[1]
    positions = lax.axis_index("blk") * piece + jnp.arange(piece, dtype=jnp.int32)
    angles = frequencies(HEAD_DIMENSION)[:, None] * positions.astype(jnp.float32)[None, :]
    tables = dict(cosines=jnp.cos(angles), sines=jnp.sin(angles), norms=jnp.stack([norm_attn, norm_ffn]))
    routing = dict(router=w_router.T, depths=depths)
    heads = dict(w_query_hbm=w_query, key_weight_hbm=key_weight.T, value_weight_hbm=value_weight.T)
    weights = heads | dict(w_out_hbm=w_out, w_gate_hbm=w_gate, w_up_hbm=w_up, w_down_hbm=w_down.T)
    nb = mesh_sizes[0]
    saved = forward(
        tables | routing | dict(tokens=tokens[0].T, cotangent=cotangent[0].T, segments=segments), weights, nb
    )
    operands = dict(
        metas_hbm=saved["metas"], turned_hbm=saved["turned"], dat_hbm=saved["dat"], att_hbm=saved["att"],
        lse_hbm=saved["lse"], kv_hbm=saved["kv"], grad_hbm=saved["grad_hidden"], hid_1_hbm=saved["hid_1"],
        hid_0_hbm=saved["hid"], branch_hbm=saved["branch"], slope_hbm=saved["slope"], silu_hbm=saved["silu"],
        middle_hbm=saved["middle"],
    )
    bottom = backward(1, tables | routing | dict(small_before=saved["small"]), weights | operands, nb)
    return final(tables, saved, saved, bottom, weights, mesh_sizes)


def solution(mesh):
    sizes = (mesh.shape["blk"], mesh.shape["dp"])
    return jax.shard_map(
        functools.partial(local, mesh_sizes=sizes),
        mesh=mesh,
        in_specs=(
            P("dp", "blk", None),
            P("dp", "blk"),
            P("dp", "blk"),
            P(),
            P(),
            P(),
            P(),
            P(),
            P(),
            P(),
            P(),
            P(),
            P(),
            P("dp", "blk", None),
        ),
        out_specs=(
            P("dp", "blk", None),
            P("dp", "blk", None),
            P("blk"),
            P("blk"),
            P("blk", None),
            P("blk", None),
            P("blk", None),
            P("blk", None),
            P("blk", None),
            P("blk", None),
            P("blk", None),
            P("blk", None),
        ),
        check_vma=False,
    )
```

```python
import functools
import itertools
import math
import types

import jax
import jax.numpy as jnp
from jax import lax
from jax.experimental import pallas as pl
from jax.experimental.pallas import tpu as pltpu
from jax.sharding import PartitionSpec as P

QUERY_HEADS = 15
KEY_VALUE_HEADS = 5
HEAD_DIMENSION = 64
RECUR = 2
HEAD_SHARE = QUERY_HEADS // KEY_VALUE_HEADS
KEYS_WIDTH = KEY_VALUE_HEADS * HEAD_DIMENSION
PAIR = 2 * HEAD_DIMENSION
FF_TILE = 512
UNIT_COLUMNS = 256
VMEM_LIMIT = 63 * 1024 * 1024

epsilon = 1e-05
masked_score = -1e30
low = jnp.bfloat16


def frequencies(head_size):
    return jnp.exp(
        jnp.arange(head_size // 2, dtype=jnp.float32) * (-2.0 * math.log(10000.0) / head_size)
    )


def rms_scale(values):
    return lax.rsqrt(jnp.mean(values * values, axis=-1, keepdims=True) + epsilon)


def norm_gradient(grad_norm, values, gain):
    scale = rms_scale(values)
    weighted = grad_norm * gain
    grad_values = scale * weighted - values * (scale * scale * scale) * jnp.mean(
        weighted * values, axis=-1, keepdims=True
    )
    return grad_values, jnp.sum(grad_norm * values * scale, axis=0, keepdims=True)


def dot_last(left, right):
    return lax.dot_general(left, right, (((1,), (1,)), ((), ())), preferred_element_type=jnp.float32)


def plain_dot(left, right):
    return jnp.dot(left, right, preferred_element_type=jnp.float32)


def bits_of(number, count):
    return tuple((number >> (count - 1 - at)) & 1 for at in range(count))


def bit_of(position, bit):
    return lax.rem(position // (1 << bit), 2)


def block_bits(block, m):
    return tuple(bit_of(block, bit) for bit in range(m - 1, -1, -1))


def flipped(position, bit):
    return position + (1 << bit) * (1 - 2 * bit_of(position, bit))


def remote(source, target, sems, at, device):
    return pltpu.make_async_remote_copy(
        src_ref=source,
        dst_ref=target,
        send_sem=sems[0].at[at],
        recv_sem=sems[1].at[at],
        device_id=device,
        device_id_type=pl.DeviceIdType.MESH,
    )


def greet(partners):
    barrier = pltpu.get_barrier_semaphore()
    for partner in partners:
        pl.semaphore_signal(barrier, inc=1, device_id=partner, device_id_type=pl.DeviceIdType.MESH)
    pl.semaphore_wait(barrier, len(partners))


def turn_heads(turned, cosine, sine, heads):
    split = turned.reshape(heads, 2, HEAD_DIMENSION // 2, turned.shape[1])
    first, second = split[:, 0], split[:, 1]
    both = jnp.stack([first * cosine - second * sine, second * cosine + first * sine], axis=1)
    return both.reshape(turned.shape)


def turn_back(turned, cosine, sine, heads):
    return turn_heads(turned, cosine, -sine, heads)


def head_rows(group, member):
    head = group * HEAD_SHARE + member
    return pl.ds(pl.multiple_of(head * HEAD_DIMENSION, HEAD_DIMENSION), HEAD_DIMENSION)


def as_column(row):
    wide = jnp.broadcast_to(row.astype(jnp.float32), (8, row.shape[1]))
    return wide.T[:, 0:1]


def key_pairs(blk):
    return (blk + 2) // 2


def fill_bias(bias, metas, query_segments, level, blk, m, piece):
    key_at = lax.broadcasted_iota(jnp.int32, (piece, piece), 0)
    query_at = lax.broadcasted_iota(jnp.int32, (piece, piece), 1)

    @pl.loop(0, 2 * key_pairs(blk))
    def _(block):
        columns = metas[block_bits(block, m)].T
        live = jnp.where(columns[:, 1:2] > level, columns[:, 0:1], -1.0)
        shift = (blk - block) * piece
        allowed = (live == query_segments) & (key_at <= query_at + shift) | (key_at == query_at + shift)
        bias[block] = jnp.where(allowed, 0.0, masked_score).astype(bias.dtype)


def pair_bias(bias, pair, piece):
    return bias[pl.ds(2 * pair, 2)].reshape(2 * piece, piece).astype(jnp.float32)


def spec(memory):
    return pl.BlockSpec(memory_space=memory)


def shaped(entry):
    return jax.ShapeDtypeStruct(*entry)


def spaces(entries):
    return [pltpu.VMEM(*entry) for entry in entries]


def dma_semaphores(*shapes):
    return [pltpu.SemaphoreType.DMA(shape) for shape in shapes]


class Piece:
    def __init__(self, at, kept_at, slot, flavour, family, sems, bits):
        self.at, self.kept_at, self.slot, self.family, self.sems = at, kept_at, slot, family, sems
        self.m, self.n = bits
        left = list(range(self.m - 1, -1, -1))
        self.order = []
        for stage in range(self.m):
            place = len(left) - 1 if stage == 0 or flavour == 0 else 0
            self.order.append((left.pop(place), place, len(left)))
        self.last = self.m + self.n
        self.blk = lax.axis_index("blk")
        self.dp = lax.axis_index("dp") if self.n else None

    def half(self, ref, side):
        rows, columns = self.family.shape
        if self.family.split == 0:
            return ref.at[pl.ds(pl.multiple_of(side * (rows // 2), rows // 2), rows // 2), :]
        return ref.at[:, pl.ds(pl.multiple_of(side * (columns // 2), columns // 2), columns // 2)]

    def held(self, stage):
        if stage == 0:
            return self.family.part, self.slot
        return self.family.blk[stage - 1], self.kept_at

    def copy(self, stage):
        m, family = self.m, self.family
        if stage < m:
            bit, place, others = self.order[stage]
            ref, index = self.held(stage)
            chosen = [slice(None)] * (others + 1)
            chosen[place] = 1 - bit_of(self.blk, bit)
            source = ref.at[(index, *chosen)]
            target = family.blk[stage].at[self.kept_at]
            device = {"blk": flipped(self.blk, bit)}
        elif stage < self.last:
            bit = stage - m
            if bit == 0:
                source = self.half(family.blk[m - 1].at[self.kept_at], 1 - bit_of(self.dp, 0))
            else:
                source = family.dp[bit - 1].at[self.kept_at]
            target = family.dp[bit].at[self.kept_at]
            device = {"dp": flipped(self.dp, bit)}
        else:
            source = self.half(family.out.at[self.kept_at], bit_of(self.dp, 0))
            target = source
            device = {"dp": flipped(self.dp, 0)}
        return remote(source, target, self.sems, (self.at, stage), device)

    def start(self, stage):
        self.copy(stage).start()

    def finish(self, stage):
        m, family = self.m, self.family
        self.copy(stage).wait_recv()
        if stage < m:
            bit, place, others = self.order[stage]
            ref, index = self.held(stage)
            for combo in itertools.product(range(2), repeat=others):
                chosen = list(combo)
                chosen.insert(place, bit_of(self.blk, bit))
                into = family.blk[stage].at[(self.kept_at, *combo)]
                self.add(into, into, ref.at[(index, *chosen)])
            if stage == 0:
                self.copy(0).wait_send()
        elif stage < self.last:
            bit = stage - m
            got = family.dp[bit].at[self.kept_at]
            if bit == 0:
                own = self.half(family.blk[m - 1].at[self.kept_at], bit_of(self.dp, 0))
            else:
                own = family.dp[bit - 1].at[self.kept_at]
            into = got
            if stage == self.last - 1:
                into = self.half(family.out.at[self.kept_at], bit_of(self.dp, 0))
            self.add(into, got, own)

    def add(self, into, left, right):
        into[...] = left[...] + right[...]

    def drained(self, stages):
        for stage in stages:
            self.copy(stage).wait_send()


def feed_forward_backward(at, level, gradient, ready, done):
    tiles = at.w_gate.shape[1] // FF_TILE
    column = at.router[level:level + 1, :].astype(jnp.float32)
    active = as_column(at.depths[...]) > float(level)
    hidden = at.hid_level[...]
    chosen = jax.nn.sigmoid(jnp.sum(hidden * column, axis=1, keepdims=True))
    at.dbranch[...] = jnp.where(active, chosen, 0.0) * gradient
    dchosen = jnp.where(active, jnp.sum(gradient * at.branch_level[...], axis=1, keepdims=True), 0.0)
    dlogit = dchosen * chosen * (1.0 - chosen)
    at.small[2 + level:3 + level, :] = jnp.sum(hidden * dlogit, axis=0, keepdims=True)
    at.grad_hidden[...] = gradient + dlogit * column
    at.dffn[...] = at.dbranch[...].astype(low)

    def dinner_of(tile):
        ready(tile)
        return plain_dot(at.dffn[...], at.w_down[:, tile * FF_TILE:(tile + 1) * FF_TILE])

    dinner = dinner_of(0)
    for tile in range(tiles):
        following = dinner_of(tile + 1) if tile + 1 < tiles else None
        columns = slice(tile * FF_TILE, (tile + 1) * FF_TILE)
        dgate = (dinner * at.slope_level[:, columns].astype(jnp.float32)).astype(low)
        dup = (dinner * at.silu_level[:, columns].astype(jnp.float32)).astype(low)
        at.dgate[:, columns] = dgate
        at.dup[:, columns] = dup
        done(tile)
        share = plain_dot(at.w_gate[:, columns], dgate.T) + plain_dot(at.w_up[:, columns], dup.T)
        if tile == 0:
            at.dnorm_turned[...] = share
        else:
            at.dnorm_turned[...] += share
        dinner = following
    ready(None)
    dnorm = at.dnorm_turned[...].T
    dmiddle, gain_share = norm_gradient(dnorm, at.middle_level[...], at.norms[1:2, :].astype(jnp.float32))
    at.small[1:2, :] += gain_share
    at.grad_hidden[...] += dmiddle
    dattn = (at.dbranch[...] + dmiddle).astype(low)
    lead = at.far.shape[1] - dattn.shape[1]
    at.far[:, :lead] = jnp.zeros((dattn.shape[0], lead), low)
    at.far[:, lead:] = dattn
    at.dat[...] = plain_dot(at.w_out[...], dattn.T).astype(low)


def forward_kernel(sizes, names, *refs):
    m, piece = sizes
    at = types.SimpleNamespace(**dict(zip(names, refs)))
    blk = lax.axis_index("blk")
    mine = block_bits(blk, m)
    kv, metas = at.kv, at.metas
    weights = (
        (at.key_weight_hbm, at.key_weight), (at.value_weight_hbm, at.value_weight), (at.w_query_hbm, at.w_query),
        (at.w_out_hbm, at.w_out), (at.w_gate_hbm, at.w_gate), (at.w_up_hbm, at.w_up), (at.w_down_hbm, at.w_down),
    )
    loads = [pltpu.make_async_copy(*pair, at.load_sems.at[index]) for index, pair in enumerate(weights)]
    for load in loads:
        load.start()
    saved = (
        (at.normed, at.normed_out), (at.turned, at.turned_out), (kv, at.kv_out), (at.lse, at.lse_out),
        (at.att, at.att_out), (at.nffn, at.nffn_out), (at.inner, at.inner_out),
    )

    def save(index, level):
        return pltpu.make_async_copy(
            saved[index][0].at[level], saved[index][1].at[level], at.save_sems.at[index, level]
        )

    first = (
        (at.hid.at[0], at.hid_out), (at.middle.at[0], at.middle_out), (at.silu.at[0], at.silu_out),
        (at.slope.at[0], at.slope_out), (at.branch.at[0], at.branch_out), (metas, at.metas_out),
        (at.far, at.far_out), (at.dat, at.dat_out), (at.dffn, at.dffn_out), (at.dgate, at.dgate_out), (at.dup, at.dup_out),
        (at.hid.at[1], at.hid_1_out),
    )
    late = [pltpu.make_async_copy(*pair, at.late_sems.at[index]) for index, pair in enumerate(first)]
    segment_row = at.segments[...].astype(jnp.float32)
    depth_column = as_column(at.depths[...])
    metas[mine] = jnp.concatenate(
        [segment_row, at.depths[...].astype(jnp.float32), jnp.zeros((6, piece), jnp.float32)], axis=0
    )
    greet([{"blk": flipped(blk, bit)} for bit in range(m)])

    def place(known):
        return tuple(slice(None) if bit in known else mine[m - 1 - bit] for bit in range(m - 1, -1, -1))

    orders = (list(range(1, m)), list(range(m - 1, 0, -1)))
    kv_sems = (at.kv_send, at.kv_recv)

    def kv_copies(level, group, stage):
        if stage == m - 1:
            ref = kv.at[(level, group, *place(range(1, m)))]
            return [remote(ref, ref, kv_sems, (level, group, 2 * stage), {"blk": flipped(blk, 0)})]
        copies = []
        for side, order in enumerate(orders):
            rows = pl.ds(side * (piece // 2), piece // 2)
            ref = kv.at[(level, group, *place(order[:stage]), rows)]
            copies.append(remote(ref, ref, kv_sems, (level, group, 2 * stage + side), {"blk": flipped(blk, order[stage])}))
        return copies

    def kv_advance(level, group, stage):
        if stage > 0:
            for copy in kv_copies(level, group, stage - 1):
                copy.wait_recv()
        if stage < m:
            for copy in kv_copies(level, group, stage):
                copy.start()

    def meta_copy(stage):
        bits = list(range(1, m)) + [0]
        ref = metas.at[place(bits[:stage])]
        return remote(ref, ref, (at.meta_send, at.meta_recv), stage, {"blk": flipped(blk, bits[stage])})

    meta_copy(0).start()
    cosine, sine = at.cosines[...], at.sines[...]
    gain_attn, gain_ffn = at.norms[0:1, :].astype(jnp.float32), at.norms[1:2, :].astype(jnp.float32)
    routers = at.router[...].astype(jnp.float32)
    at.hid[0] = at.tokens[...].T.astype(jnp.float32)
    late[0].start()
    at.query_pad[HEAD_DIMENSION:, :] = jnp.zeros_like(at.query_pad[HEAD_DIMENSION:, :])

    @pl.loop(0, RECUR)
    def _(level):
        hidden = at.hid[level]
        at.flat[...] = (hidden * rms_scale(hidden) * gain_attn).astype(low)
        at.normed[level] = at.flat[...].T

        @pl.when(level == 0)
        def _():
            for load in loads[:2]:
                load.wait()

        keys = turn_heads(plain_dot(at.key_weight[...], at.normed[level]), cosine, sine, KEY_VALUE_HEADS)
        values = plain_dot(at.value_weight[...], at.normed[level])
        for group in range(KEY_VALUE_HEADS):
            here = slice(group * HEAD_DIMENSION, (group + 1) * HEAD_DIMENSION)
            both = jnp.concatenate([keys[here], values[here]], axis=0)
            kv[(level, group, *mine)] = both.T.astype(low)
            kv_advance(level, group, 0)

        @pl.when(level == 0)
        def _():
            loads[2].wait()
            for stage in range(1, m - 1):
                meta_copy(stage - 1).wait_recv()
                meta_copy(stage).start()

        queries = turn_heads(plain_dot(at.flat[...], at.w_query[...]).T, cosine, sine, QUERY_HEADS)
        at.turned[level] = (queries * HEAD_DIMENSION ** (-0.5)).astype(low)

        @pl.when(level == 0)
        def _():
            for stage in range(max(1, m - 1), m):
                meta_copy(stage - 1).wait_recv()
                meta_copy(stage).start()

        for stage in range(1, m - 1):
            for group in range(KEY_VALUE_HEADS):
                kv_advance(level, group, stage)
        kv_advance(level, 0, m - 1)

        @pl.when(level == 0)
        def _():
            meta_copy(m - 1).wait_recv()
            late[5].start()

        fill_bias(at.bias, metas, segment_row, level.astype(jnp.float32), blk, m, piece)

        @pl.loop(0, KEY_VALUE_HEADS)
        def _(group):
            @pl.when(group + 1 < KEY_VALUE_HEADS)
            def _():
                kv_advance(level, group + 1, m - 1)

            kv_advance(level, group, m)
            for member in range(HEAD_SHARE):
                at.query_pad[:HEAD_DIMENSION, member * piece:(member + 1) * piece] = at.turned[level, head_rows(group, member), :]
            at.top[...] = jnp.full_like(at.top, masked_score)
            at.total[...] = jnp.zeros_like(at.total)

            @pl.loop(0, key_pairs(blk))
            def _(step):
                pair = key_pairs(blk) - 1 - step
                rows = kv[(level, group, *block_bits(pair, m - 1))].reshape(2 * piece, PAIR)
                bias = pair_bias(at.bias, pair, piece)
                left = jnp.concatenate([rows.T[HEAD_DIMENSION:], jnp.ones((16, 2 * piece), low)], axis=0)
                for member in range(HEAD_SHARE):
                    lanes = slice(member * piece, (member + 1) * piece)
                    scores = plain_dot(rows, at.query_pad[:, lanes]) + bias
                    before = at.top[0:1, lanes]
                    after = jnp.maximum(before, jnp.max(scores, axis=0, keepdims=True))
                    raised = jnp.exp(scores - after).astype(low)
                    at.top[0:1, lanes] = after
                    at.total[:, lanes] = at.total[:, lanes] * jnp.exp(before - after) + plain_dot(left, raised)

            sums = at.total[HEAD_DIMENSION:HEAD_DIMENSION + 1, :]
            at.lse[level, pl.ds(group, 1), :] = at.top[0:1, :] + jnp.log(sums)
            out = at.total[:HEAD_DIMENSION, :] / sums
            for member in range(HEAD_SHARE):
                at.att[level, head_rows(group, member), :] = out[:, member * piece:(member + 1) * piece].astype(low)

        for index in range(5):
            save(index, level).start()

        @pl.when(level == 0)
        def _():
            loads[3].wait()

        attn = plain_dot(at.att[level].T, at.w_out[...])
        mid = at.hid[level] + attn
        at.middle[level] = mid
        at.branch[level] = attn
        at.flat[...] = (mid * rms_scale(mid) * gain_ffn).astype(low)
        at.nffn[level] = at.flat[...].T
        save(5, level).start()

        @pl.when(level == 0)
        def _():
            loads[4].wait()
            loads[5].wait()

        for tile in range(at.w_gate.shape[1] // FF_TILE):
            columns = slice(tile * FF_TILE, (tile + 1) * FF_TILE)
            gate_pre = plain_dot(at.flat[...], at.w_gate[:, columns])
            up_pre = plain_dot(at.flat[...], at.w_up[:, columns])
            opened = jax.nn.sigmoid(gate_pre)
            passed = gate_pre * opened
            at.silu[level, :, columns] = passed.astype(low)
            at.slope[level, :, columns] = (up_pre * (opened + passed - passed * opened)).astype(low)
            at.inner[level, columns, :] = (passed * up_pre).astype(low).T

        save(6, level).start()

        @pl.when(level == 0)
        def _():
            loads[6].wait()

        at.branch[level] += plain_dot(at.w_down[...], at.inner[level]).T
        column = jnp.where(level == 0, routers[0:1, :], routers[1:2, :])
        logit = jnp.sum(at.hid[level] * column, axis=1, keepdims=True)
        weight = jnp.where(depth_column > level.astype(jnp.float32), jax.nn.sigmoid(logit), 0.0)
        at.hid[level + 1] = at.hid[level] + weight * at.branch[level]

        @pl.when(level == 0)
        def _():
            for copy in late[1:5]:
                copy.start()

    at.hidden_out[...] = at.hid[RECUR].T
    top = RECUR - 1
    at.hid_level, at.branch_level, at.middle_level = at.hid.at[top], at.branch.at[top], at.middle.at[top]
    at.silu_level, at.slope_level = at.silu.at[top], at.slope.at[top]
    at.small[...] = jnp.zeros_like(at.small)
    feed_forward_backward(at, top, at.cotangent[...].T.astype(jnp.float32), lambda tile: None, lambda tile: None)
    for copy in late[6:]:
        copy.start()
    for stage in range(m):
        meta_copy(stage).wait_send()
    for level in range(RECUR):
        for group in range(KEY_VALUE_HEADS):
            for stage in range(m):
                for copy in kv_copies(level, group, stage):
                    copy.wait_send()
        for index in range(len(saved)):
            save(index, level).wait()
    for copy in late:
        copy.wait()


def far_width(width):
    return 2 * width + 2 * KEYS_WIDTH - 1536


def forward(small, weights, nb):
    m = nb.bit_length() - 1
    width, piece = small["tokens"].shape
    hidden_units = weights["w_gate_hbm"].shape[1]
    blocks, wide = (2,) * m, HEAD_SHARE * piece
    rows, turned = ((piece, width), jnp.float32), ((RECUR, width, piece), low)
    hidden = ((piece, hidden_units), low)
    saved = dict(
        normed=turned, turned=turned, kv=((RECUR, KEY_VALUE_HEADS, *blocks, piece, PAIR), low),
        lse=((RECUR, 8, wide), jnp.float32), att=turned, nffn=turned, inner=((RECUR, hidden_units, piece), low),
        metas=((*blocks, 8, piece), jnp.float32), far=((piece, far_width(width)), low), dat=((width, piece), low),
        dffn=((piece, width), low), dgate=hidden, dup=hidden,
    )
    first = dict(hid=rows, middle=rows, silu=hidden, slope=hidden, branch=rows)
    outs = dict(hidden_out=((width, piece), jnp.float32), grad_hidden=rows, small=((8, width), jnp.float32))
    anywhere = {name + "_out": entry for name, entry in (saved | first | dict(hid_1=rows)).items()}
    both = {name: ((RECUR, *shape), dtype) for name, (shape, dtype) in first.items()}
    buffers = {name[:-4]: (array.shape, array.dtype) for name, array in weights.items()} | saved | both | dict(
        hid=((RECUR + 1, piece, width), jnp.float32), flat=((piece, width), low),
        bias=((nb, piece, piece), jnp.float32), query_pad=((PAIR, wide), low), top=((8, wide), jnp.float32),
        total=((HEAD_DIMENSION + 16, wide), jnp.float32), dbranch=rows, dnorm_turned=((width, piece), jnp.float32),
    )
    semaphores = dict(
        load_sems=(7,), save_sems=(7, RECUR), late_sems=(12,), kv_send=(RECUR, KEY_VALUE_HEADS, 2 * m),
        kv_recv=(RECUR, KEY_VALUE_HEADS, 2 * m), meta_send=(m,), meta_recv=(m,),
    )
    results = pl.pallas_call(
        functools.partial(forward_kernel, (m, piece), (*small, *weights, *outs, *anywhere, *buffers, *semaphores)),
        out_shape=[shaped(entry) for entry in (outs | anywhere).values()],
        in_specs=[spec(pltpu.VMEM)] * len(small) + [spec(pl.ANY)] * len(weights),
        out_specs=[spec(pltpu.VMEM)] * len(outs) + [spec(pl.ANY)] * len(anywhere),
        scratch_shapes=spaces(buffers.values()) + dma_semaphores(*semaphores.values()),
        compiler_params=pltpu.CompilerParams(
            collective_id=1, has_side_effects=True, vmem_limit_bytes=VMEM_LIMIT
        ),
        cost_estimate=pl.CostEstimate(
            flops=3 * RECUR * piece * width * 10240, bytes_accessed=48 * 1024 * 1024, transcendentals=0
        ),
        name="forward_levels",
    )(*small.values(), *weights.values())
    return dict(zip((*outs, *(name[:-4] for name in anywhere)), results))


class AttentionBackward:
    def __init__(self, at, m, piece, level):
        self.at, self.m, self.piece, self.level = at, m, piece, level
        self.blk = lax.axis_index("blk")
        self.family = types.SimpleNamespace(part=at.part, blk=at.halves, dp=(), out=None, shape=(piece // 2, PAIR), split=0)

    def pieces(self, group):
        sems = (self.at.kv_send, self.at.kv_recv)
        return [
            Piece(2 * group + side, 2 * group + side, 2 * group + side, side, self.family, sems, (self.m, 0))
            for side in range(2)
        ]

    def move(self, group, stage):
        for piece_of in self.pieces(group):
            piece_of.finish(stage)
            if stage + 1 < self.m:
                piece_of.start(stage + 1)

    def begin(self):
        at = self.at
        query_segments = at.metas[block_bits(self.blk, self.m)][0:1, :]
        fill_bias(at.bias, at.metas, query_segments, float(self.level), self.blk, self.m, self.piece)
        at.query_pad[HEAD_DIMENSION:, :] = jnp.zeros_like(at.query_pad[HEAD_DIMENSION:, :])
        at.dat_pad[:HEAD_DIMENSION, :] = jnp.zeros_like(at.dat_pad[:HEAD_DIMENSION, :])

    def group(self, group):
        at, m, piece, blk = self.at, self.m, self.piece, self.blk
        half = piece // 2
        carried = []
        for member in range(HEAD_SHARE):
            rows, lanes = head_rows(group, member), slice(member * piece, (member + 1) * piece)
            at.query_pad[:HEAD_DIMENSION, lanes] = at.turned[rows, :]
            at.dat_pad[HEAD_DIMENSION:, lanes] = at.dat_turned[rows, :]
            product = at.dat_turned[rows, :].astype(jnp.float32) * at.att_turned[rows, :].astype(jnp.float32)
            carried.append(jnp.sum(product, axis=0, keepdims=True))
        at.query_rows[...] = at.query_pad[...].T
        at.dat_rows[...] = at.dat_pad[...].T
        log_total = at.lse[pl.ds(group, 1), :]
        at.dq_sum[...] = jnp.zeros_like(at.dq_sum)

        @pl.loop(0, key_pairs(blk))
        def _(pair):
            rows = at.kv[(group, *block_bits(pair, m - 1))].reshape(2 * piece, PAIR)
            key_columns = rows.T[:HEAD_DIMENSION]
            bias = pair_bias(at.bias, pair, piece)
            share = None
            for member in range(HEAD_SHARE):
                lanes = slice(member * piece, (member + 1) * piece)
                scores = plain_dot(rows, at.query_pad[:, lanes]) + bias
                probability = jnp.exp(scores - log_total[:, lanes])
                dprob = plain_dot(rows, at.dat_pad[:, lanes])
                dscores = (probability * (dprob - carried[member])).astype(low)
                part = plain_dot(dscores, at.query_rows[lanes, :])
                part = part + plain_dot(probability.astype(low), at.dat_rows[lanes, :])
                share = part if share is None else share + part
                at.dq_sum[:, lanes] += plain_dot(key_columns, dscores)
            share = share.astype(low)
            for block in range(2):
                for side in range(2):
                    first = block * piece + side * half
                    at.part[(2 * group + side, *block_bits(pair, m - 1), block)] = share[first:first + half]

        @pl.loop(key_pairs(blk), 1 << (m - 1))
        def _(pair):
            for block in range(2):
                for side in range(2):
                    at.part[(2 * group + side, *block_bits(pair, m - 1), block)] = jnp.zeros((half, PAIR), low)

        for piece_of in self.pieces(group):
            piece_of.start(0)
        for member in range(HEAD_SHARE):
            at.dq_turned[head_rows(group, member), :] = at.dq_sum[:, member * piece:(member + 1) * piece]

    def follow(self, group):
        for stage in range(self.m - 1):
            earlier = group - 1 - stage
            if isinstance(group, int):
                if 0 <= earlier < KEY_VALUE_HEADS:
                    self.move(earlier, stage)
            else:
                @pl.when(earlier >= 0)
                def _():
                    self.move(earlier, stage)

    def queries(self, cosine, sine):
        at = self.at
        dqueries = turn_back(at.dq_turned[...] * HEAD_DIMENSION ** (-0.5), cosine, sine, QUERY_HEADS).astype(low)
        self.put(2 * KEYS_WIDTH, dqueries.T)
        at.dnorm[...] = plain_dot(at.w_query[...], dqueries).T

    def put(self, column, values):
        self.at.near[:, column:column + values.shape[1]] = values

    def keys(self, cosine, sine):
        at, m = self.at, self.m
        filled = 2 * KEYS_WIDTH + QUERY_HEADS * HEAD_DIMENSION
        self.put(filled, jnp.zeros((self.piece, at.near.shape[1] - filled), low))
        dkeys, dvalues = [], []
        for group in range(KEY_VALUE_HEADS):
            self.move(group, m - 1)
            both = jnp.concatenate([at.halves[m - 1][2 * group], at.halves[m - 1][2 * group + 1]], axis=0).T
            dkeys.append(both[:HEAD_DIMENSION].astype(jnp.float32))
            dvalues.append(both[HEAD_DIMENSION:])
        dkeys = turn_back(jnp.concatenate(dkeys, axis=0), cosine, sine, KEY_VALUE_HEADS).astype(low).T
        dvalues = jnp.concatenate(dvalues, axis=0).T
        self.put(0, dkeys)
        self.put(KEYS_WIDTH, dvalues)
        at.dnorm[...] += plain_dot(dkeys, at.key_weight[...]) + plain_dot(dvalues, at.value_weight[...])

    def drained(self):
        for group in range(KEY_VALUE_HEADS):
            for piece_of in self.pieces(group):
                piece_of.drained(range(1, self.m))


def attention_buffers(nb, piece, width, bias_type):
    m, wide, heads = nb.bit_length() - 1, HEAD_SHARE * piece, 2 * KEY_VALUE_HEADS
    turned, weight = ((width, piece), low), ((KEYS_WIDTH, width), low)
    pad, pad_rows = ((PAIR, wide), low), ((wide, PAIR), low)
    buffers = dict(
        turned=turned, dat_turned=turned, att_turned=turned, kv=((KEY_VALUE_HEADS, *(2,) * m, piece, PAIR), low),
        lse=((8, wide), jnp.float32), metas=((*(2,) * m, 8, piece), jnp.float32), w_query=((width, width), low),
        key_weight=weight, value_weight=weight, dq_turned=((width, piece), jnp.float32),
        bias=((nb, piece, piece), bias_type), query_pad=pad, dat_pad=pad, query_rows=pad_rows, dat_rows=pad_rows,
        dq_sum=((HEAD_DIMENSION, wide), jnp.float32), part=((heads, *(2,) * m, piece // 2, PAIR), low),
        dnorm=((piece, width), jnp.float32), hid=((piece, width), jnp.float32),
    )
    for stage in range(m):
        buffers["half_%d" % stage] = ((heads, *(2,) * (m - 1 - stage), piece // 2, PAIR), low)
    return buffers


def backward_kernel(sizes, names, *refs):
    m, piece, level = sizes
    at = types.SimpleNamespace(**dict(zip(names, refs)))
    at.halves = [getattr(at, "half_%d" % stage) for stage in range(m)]
    at.near = at.near_out
    blk = lax.axis_index("blk")
    pairs = (
        (at.metas_hbm, at.metas), (at.turned_hbm.at[level], at.turned), (at.dat_hbm, at.dat_turned),
        (at.att_hbm.at[level], at.att_turned), (at.lse_hbm.at[level], at.lse), (at.kv_hbm.at[level], at.kv),
        (at.w_query_hbm, at.w_query), (at.key_weight_hbm, at.key_weight), (at.value_weight_hbm, at.value_weight),
        (at.grad_hbm, at.grad_hidden), (at.hid_1_hbm, at.hid),
        (at.hid_0_hbm, at.hid_level), (at.branch_hbm, at.branch_level), (at.w_down_hbm, at.w_down),
        (at.slope_hbm, at.slope_level), (at.silu_hbm, at.silu_level), (at.w_gate_hbm, at.w_gate), (at.w_up_hbm, at.w_up),
        (at.middle_hbm, at.middle_level), (at.w_out_hbm, at.w_out),
    )
    loads = [pltpu.make_async_copy(*pair, at.load_sems.at[index]) for index, pair in enumerate(pairs)]
    for load in loads:
        load.start()
    saves = [
        pltpu.make_async_copy(*pair, at.save_sems.at[index])
        for index, pair in enumerate(((at.dgate, at.dgate_out), (at.dup, at.dup_out)))
    ]
    greet([{"blk": flipped(blk, bit)} for bit in range(m)])
    work = AttentionBackward(at, m, piece, level)
    loads[0].wait()
    work.begin()
    for load in loads[1:6]:
        load.wait()

    @pl.loop(0, KEY_VALUE_HEADS)
    def _(group):
        work.group(group)
        work.follow(group)

    cosine, sine = at.cosines[...], at.sines[...]
    for virtual in range(KEY_VALUE_HEADS, KEY_VALUE_HEADS + m - 1):
        work.follow(virtual)
        if virtual == KEY_VALUE_HEADS:
            loads[6].wait()
            work.queries(cosine, sine)
    for load in loads[7:]:
        load.wait()
    work.keys(cosine, sine)
    dhidden, gain_share = norm_gradient(at.dnorm[...], at.hid[...], at.norms[0:1, :].astype(jnp.float32))
    at.small[...] = at.small_before[...]
    at.small[0:1, :] = gain_share
    gradient = at.grad_hidden[...] + dhidden
    at.dnorm[...] = gradient
    feed_forward_backward(at, level - 1, at.dnorm[...], lambda tile: None, lambda tile: None)
    for save in saves:
        save.start()
    work.drained()
    for save in saves:
        save.wait()


def backward(level, small, operands, nb):
    m = nb.bit_length() - 1
    piece, width = operands["grad_hbm"].shape
    hidden_units = operands["w_gate_hbm"].shape[1]
    rows, flat, hidden = ((piece, width), jnp.float32), ((piece, width), low), ((piece, hidden_units), low)
    outs = dict(
        grad_hidden=rows, small=((8, width), jnp.float32), near_out=((piece, 1792), low), dffn=flat,
        dat=((width, piece), low), far=((piece, far_width(width)), low),
    )
    anywhere = dict(dgate_out=hidden, dup_out=hidden)
    buffers = attention_buffers(nb, piece, width, jnp.float32) | dict(
        hid_level=rows, branch_level=rows, middle_level=rows, w_down=((width, hidden_units), low), slope_level=hidden,
        silu_level=hidden, w_gate=((width, hidden_units), low), w_up=((width, hidden_units), low),
        w_out=((width, width), low), dbranch=rows, dnorm_turned=((width, piece), jnp.float32), dgate=hidden, dup=hidden,
    )
    sums = (2 * KEY_VALUE_HEADS, m)
    semaphores = dict(load_sems=(20,), save_sems=(2,), kv_send=sums, kv_recv=sums)
    results = pl.pallas_call(
        functools.partial(
            backward_kernel, (m, piece, level), (*small, *operands, *outs, *anywhere, *buffers, *semaphores)
        ),
        out_shape=[shaped(entry) for entry in (outs | anywhere).values()],
        in_specs=[spec(pltpu.VMEM)] * len(small) + [spec(pl.ANY)] * len(operands),
        out_specs=[spec(pltpu.VMEM)] * len(outs) + [spec(pl.ANY)] * len(anywhere),
        scratch_shapes=spaces(buffers.values()) + dma_semaphores(*semaphores.values()),
        compiler_params=pltpu.CompilerParams(
            collective_id=2, has_side_effects=True, vmem_limit_bytes=VMEM_LIMIT
        ),
        cost_estimate=pl.CostEstimate(
            flops=2 * piece * width * 20000, bytes_accessed=32 * 1024 * 1024, transcendentals=0
        ),
        name="backward_level",
    )(*small.values(), *operands.values())
    return dict(zip((*outs, *anywhere), results))


WIDE_SLOTS, DOWN_SLOTS = 4, 2


def final_kernel(sizes, names, *refs):
    nb, m, n, piece, rows, padded, near_width = sizes
    at = types.SimpleNamespace(**dict(zip(names, refs)))
    at.halves = [getattr(at, "half_%d" % stage) for stage in range(m)]
    blk, dp = lax.axis_index("blk"), lax.axis_index("dp")
    at.near = at.gate_side.at[pl.ds(0, piece), pl.ds(0, near_width)]
    counter = itertools.count()

    def load(source, target):
        return pltpu.make_async_copy(source, target, at.load_sems.at[next(counter)])

    def both_lanes(ref, target):
        return [load(ref.at[level], target.at[:, pl.ds(level * piece, piece)]) for level in range(RECUR)]

    def both_rows(low_ref, deep_ref, target, width):
        pairs = ((low_ref, 0), (deep_ref, piece))
        return [load(ref, target.at[pl.ds(first, piece), pl.ds(0, width)]) for ref, first in pairs]

    hidden_units, width = at.gate_side.shape[1], at.dffn.shape[1]
    far_lanes = at.far_0_hbm.shape[1]
    loads = types.SimpleNamespace(
        nffn=both_lanes(at.nffn_hbm, at.left),
        dgate=both_rows(at.dgate_0_hbm, at.dgate_1_hbm, at.gate_side, hidden_units),
        inner=both_lanes(at.inner_hbm, at.inner),
        dffn=both_rows(at.dffn_0_hbm, at.dffn_1_hbm, at.dffn, width),
        metas=[load(at.metas_hbm, at.metas)],
        heads=[
            load(at.turned_hbm.at[0], at.turned), load(at.dat_hbm, at.dat_turned), load(at.att_hbm.at[0], at.att_turned),
            load(at.lse_hbm.at[0], at.lse), load(at.kv_hbm.at[0], at.kv),
        ],
        dup=both_rows(at.dup_0_hbm, at.dup_1_hbm, at.up_side, hidden_units),
        w_query=[load(at.w_query_hbm, at.w_query)],
        rest=[
            load(at.key_weight_hbm, at.key_weight), load(at.value_weight_hbm, at.value_weight),
            load(at.hid_hbm, at.hid), load(at.grad_hbm, at.grad),
        ],
        attended=both_lanes(at.attended_hbm, at.left_attended),
    )
    late = types.SimpleNamespace(
        near=[load(at.near_1_hbm, at.gate_side.at[pl.ds(piece, piece), pl.ds(0, near_width)])],
        far=both_rows(at.far_0_hbm, at.far_1_hbm, at.up_side, far_lanes),
        normed=both_lanes(at.normed_hbm, at.left),
    )

    def begin(copies):
        for copy in copies:
            copy.start()

    def ready(copies):
        for copy in copies:
            copy.wait()

    for copies in vars(loads).values():
        begin(copies)
    greet([{"blk": flipped(blk, bit)} for bit in range(m)] + [{"dp": flipped(dp, bit)} for bit in range(n)])

    down_rows = at.part_down.shape[-2]

    def family(name, shape, split):
        return types.SimpleNamespace(
            part=getattr(at, "part_" + name), out=getattr(at, "out_" + name), shape=shape, split=split,
            blk=[getattr(at, "blk_%s_%d" % (name, stage)) for stage in range(m)],
            dp=[getattr(at, "dp_%s_%d" % (name, stage)) for stage in range(n)],
        )

    wide = family("wide", (2 * padded, UNIT_COLUMNS), 1)
    down = family("down", (down_rows, width), 0)
    little = family("small", (16, 128), 0)
    sems = (at.send_sems, at.recv_sems)
    units = itertools.count()

    def unit(holder, index, flavour):
        return Piece(next(units), index, index % holder.part.shape[0], flavour, holder, sems, (m, n))

    pairs = [[unit(wide, 0, 0), unit(wide, 1, 1)]]
    pairs += [[unit(wide, index, 0), unit(down, index - 2, 1)] for index in range(2, 7)]
    pairs += [[unit(wide, index, 0), unit(wide, index + 1, 1)] for index in (7, 9, 11)]
    pairs += [[unit(wide, 13, 0), unit(wide, 14, 1), unit(little, 0, 0)]]

    def compute_wide(index, slot):
        if index == 0:
            ready(loads.nffn)
            ready(loads.dgate)
        if index == 5:
            begin(late.near)
            ready(loads.dup)
        if index == 10:
            begin(late.far)
            begin(late.normed)
            ready(late.near)
            ready(late.normed)
            ready(loads.attended)
            ready(late.far)
        block, column = index // 5, (index % 5) * UNIT_COLUMNS
        second = 1280 + column
        upper_columns, lower_columns = slice(column, column + UNIT_COLUMNS), slice(second, second + UNIT_COLUMNS)
        if block < 2:
            right = at.gate_side if block == 0 else at.up_side
            upper = plain_dot(at.left[...], right[:, upper_columns])
            lower = plain_dot(at.left[...], right[:, lower_columns])
        else:
            upper = plain_dot(at.left[...], at.gate_side[:, upper_columns])
            lower = None
            if second < 1600:
                lower = plain_dot(at.left[...], at.gate_side[:, lower_columns])
            if second >= 1536:
                more = plain_dot(at.left_attended[...], at.up_side[:, second - 1536:second - 1536 + UNIT_COLUMNS])
                lower = more if lower is None else lower + more
        for target in range(nb):
            here = slice(target * padded, (target + 1) * padded)
            both = jnp.concatenate([upper[here], lower[here]], axis=0)
            at.part_wide[(slot, *bits_of(target, m))] = both.astype(low)

    def compute_down(index, slot):
        if index == 0:
            ready(loads.inner)
            ready(loads.dffn)
        firsts = [(target * 5 + index) * down_rows for target in range(nb)]
        left = jnp.concatenate([at.inner[first:first + down_rows, :] for first in firsts], axis=0)
        result = plain_dot(left, at.dffn[...])
        for target in range(nb):
            at.part_down[(slot, *bits_of(target, m))] = result[target * down_rows:(target + 1) * down_rows].astype(low)

    def compute_small():
        total = at.small_before[...]
        total = total + jnp.concatenate([at.gain_row[...], jnp.zeros((7, width), jnp.float32)], axis=0)
        at.part_small[...] = jnp.zeros_like(at.part_small)
        for target in range(nb):
            at.part_small[(0, *bits_of(target, m), slice(0, 8), slice(0, rows))] = total[:, target * rows:(target + 1) * rows]

    def compute(piece_of):
        if piece_of.family is wide:
            compute_wide(piece_of.kept_at, piece_of.slot)
        elif piece_of.family is down:
            compute_down(piece_of.kept_at, piece_of.slot)
        else:
            compute_small()
        piece_of.start(0)

    def moves(tick):
        for stage in range(m + n - 1, -1, -1):
            if 0 <= tick - stage < len(pairs):
                for piece_of in pairs[tick - stage]:
                    piece_of.finish(stage)
                    piece_of.start(stage + 1)

    work = AttentionBackward(at, m, piece, 0)
    for pair in pairs[:2]:
        for piece_of in pair:
            compute(piece_of)
    moves(0)
    for piece_of in pairs[2]:
        compute(piece_of)
    ready(loads.metas)
    work.begin()
    ready(loads.heads)
    for group in range(KEY_VALUE_HEADS):
        if group > 0:
            moves(group)
            for piece_of in pairs[group + 2]:
                compute(piece_of)
        work.group(group)
        work.follow(group)
    cosine, sine = at.cosines[...], at.sines[...]
    moves(5)
    compute(pairs[7][0])
    ready(loads.w_query)
    for virtual in range(KEY_VALUE_HEADS, KEY_VALUE_HEADS + m - 1):
        work.follow(virtual)
        if virtual == KEY_VALUE_HEADS:
            work.queries(cosine, sine)
    moves(6)
    ready(loads.rest)
    work.keys(cosine, sine)
    compute(pairs[7][1])
    moves(7)
    for piece_of in pairs[8] + pairs[9][:2]:
        compute(piece_of)
    dhidden, gain_share = norm_gradient(at.dnorm[...], at.hid[...], at.norms[0:1, :].astype(jnp.float32))
    at.gain_row[...] = gain_share
    at.grad_out[...] = (at.grad[...] + dhidden).T
    compute(pairs[9][2])
    for tick in range(8, len(pairs) + m + n - 1):
        moves(tick)
    for pair in pairs:
        for piece_of in pair:
            piece_of.finish(m + n)
    for pair in pairs:
        for piece_of in pair:
            piece_of.drained(range(1, m + n + 1))
    work.drained()


def unpack_kernel(sizes, wide_hbm, down_hbm, little_hbm, hidden_in, gradient_in, *refs):
    rows, padded = sizes
    norm_attn, norm_ffn, query, key, value, out, gate, up, down_out, router, hidden, gradient = refs[:12]
    wide, down, little, rest, sems = refs[12:]
    carried = [
        pltpu.make_async_copy(source, target, sems.at[at])
        for at, (source, target) in enumerate(((hidden_in, hidden), (gradient_in, gradient)))
    ]
    loads = [
        pltpu.make_async_copy(source, target, sems.at[2 + at])
        for at, (source, target) in enumerate(((wide_hbm, wide), (down_hbm, down), (little_hbm, little)))
    ]
    for copy in loads + carried:
        copy.start()
    for load in loads:
        load.wait()
    norm_attn[...] = little[0, 0:1, :rows]
    norm_ffn[...] = little[0, 1:2, :rows]
    router[...] = little[0, 2:4, :rows]
    for unit in range(5):
        for first, target in ((0, gate), (5, up), (10, rest)):
            tile = wide[first + unit].astype(jnp.float32)
            for side in range(2):
                column = side * 1280 + unit * UNIT_COLUMNS
                target[:, column:column + UNIT_COLUMNS] = tile[side * padded:side * padded + rows]
        down_rows = down.shape[1]
        down_out[unit * down_rows:(unit + 1) * down_rows, :] = down[unit].astype(jnp.float32)
    width = query.shape[1]
    key[...] = rest[:, :KEYS_WIDTH].T
    value[...] = rest[:, KEYS_WIDTH:2 * KEYS_WIDTH].T
    query[...] = rest[:, 2 * KEYS_WIDTH:2 * KEYS_WIDTH + width]
    out[...] = rest[:, 2 * KEYS_WIDTH + width:]
    for copy in carried:
        copy.wait()


def final(small, saved, top, bottom, weights, mesh_sizes):
    nb, nd = mesh_sizes
    m, n = nb.bit_length() - 1, nd.bit_length() - 1
    grad = bottom["grad_hidden"]
    piece, width = grad.shape
    hidden_units = weights["w_gate_hbm"].shape[1]
    rows = width // nb
    padded = -(-rows // 8) * 8
    down_rows = hidden_units // nb // 5
    tokens = RECUR * piece

    def spread(array):
        if padded == rows:
            return array
        split = array.reshape(RECUR, nb, rows, piece)
        return jnp.pad(split, ((0, 0), (0, 0), (0, padded - rows), (0, 0))).reshape(RECUR, nb * padded, piece)

    inputs = small | dict(small_before=bottom["small"])
    operands = dict(
        metas_hbm=saved["metas"], turned_hbm=saved["turned"], dat_hbm=bottom["dat"], att_hbm=saved["att"],
        lse_hbm=saved["lse"], kv_hbm=saved["kv"], w_query_hbm=weights["w_query_hbm"],
        key_weight_hbm=weights["key_weight_hbm"], value_weight_hbm=weights["value_weight_hbm"], hid_hbm=saved["hid"],
        grad_hbm=grad, inner_hbm=saved["inner"], nffn_hbm=spread(saved["nffn"]), normed_hbm=spread(saved["normed"]),
        attended_hbm=spread(saved["att"]), dffn_0_hbm=bottom["dffn"], dffn_1_hbm=top["dffn"],
        dgate_0_hbm=bottom["dgate_out"], dgate_1_hbm=top["dgate"], dup_0_hbm=bottom["dup_out"], dup_1_hbm=top["dup"],
        far_0_hbm=bottom["far"], far_1_hbm=top["far"], near_1_hbm=bottom["near_out"],
    )
    near_width = bottom["near_out"].shape[1]
    families = (
        ("wide", 15, (2 * padded, UNIT_COLUMNS), low, WIDE_SLOTS, 1), ("down", 5, (down_rows, width), low, DOWN_SLOTS, 0),
        ("small", 1, (16, 128), jnp.float32, 1, 0),
    )
    outs = dict(grad_out=((width, piece), jnp.float32))
    buffers = attention_buffers(nb, piece, width, low) | dict(
        grad=((piece, width), jnp.float32), gate_side=((tokens, hidden_units), low), up_side=((tokens, hidden_units), low),
        inner=((hidden_units, tokens), low), left=((nb * padded, tokens), low), left_attended=((nb * padded, tokens), low),
        dffn=((tokens, width), low), gain_row=((1, width), jnp.float32),
    )
    for name, count, shape, dtype, slots, split in families:
        outs["out_" + name] = ((count, *shape), dtype)
        buffers["part_" + name] = ((slots, *(2,) * m, *shape), dtype)
        for stage in range(m):
            buffers["blk_%s_%d" % (name, stage)] = ((count, *(2,) * (m - 1 - stage), *shape), dtype)
        half = (shape[0], shape[1] // 2) if split else (shape[0] // 2, shape[1])
        for stage in range(n):
            buffers["dp_%s_%d" % (name, stage)] = ((count, *half), dtype)
    sums, hops = (2 * KEY_VALUE_HEADS, m), (21, m + n + 1)
    semaphores = dict(load_sems=(32,), kv_send=sums, kv_recv=sums, send_sems=hops, recv_sems=hops)
    names = (*inputs, *operands, *outs, *buffers, *semaphores)
    gradient, wide, down, little = pl.pallas_call(
        functools.partial(final_kernel, (nb, m, n, piece, rows, padded, near_width), names),
        out_shape=[shaped(entry) for entry in outs.values()],
        in_specs=[spec(pltpu.VMEM)] * len(inputs) + [spec(pl.ANY)] * len(operands),
        out_specs=[spec(pltpu.VMEM)] * len(outs),
        scratch_shapes=spaces(buffers.values()) + dma_semaphores(*semaphores.values()),
        compiler_params=pltpu.CompilerParams(
            collective_id=0, has_side_effects=True, vmem_limit_bytes=VMEM_LIMIT
        ),
        cost_estimate=pl.CostEstimate(
            flops=2 * tokens * width * 14000, bytes_accessed=30 * 1024 * 1024, transcendentals=0
        ),
        name="weight_grads",
    )(*inputs.values(), *operands.values())
    shapes = (
        (1, rows), (1, rows), (rows, width), (KEYS_WIDTH, rows), (KEYS_WIDTH, rows), (rows, width),
        (rows, hidden_units), (rows, hidden_units), (5 * down_rows, width), (2, rows), (width, piece), (width, piece),
    )
    outs = pl.pallas_call(
        functools.partial(unpack_kernel, (rows, padded)),
        out_shape=[jax.ShapeDtypeStruct(shape, jnp.float32) for shape in shapes],
        in_specs=[spec(pl.ANY)] * 5,
        out_specs=[spec(pltpu.VMEM)] * 12,
        scratch_shapes=[pltpu.VMEM(array.shape, array.dtype) for array in (wide, down, little)]
        + spaces([((rows, 2560), jnp.float32)]) + dma_semaphores((5,)),
        compiler_params=pltpu.CompilerParams(vmem_limit_bytes=VMEM_LIMIT),
        name="unpack",
    )(wide, down, little, saved["hidden_out"], gradient)
    norm_a, norm_f, query, key, value, out, gate, up, down, router, hidden, gradient = outs
    return (
        hidden.T[None], gradient.T[None], norm_a[0], norm_f[0], query, key.T, value.T, out, gate, up, down, router.T,
    )


def local(
    tokens,
    depths,
    segments,
    norm_attn,
    norm_ffn,
    w_query,
    key_weight,
    value_weight,
    w_out,
    w_gate,
    w_up,
    w_down,
    w_router,
    cotangent,
    mesh_sizes,
):
    piece = tokens.shape[1]
    positions = lax.axis_index("blk") * piece + jnp.arange(piece, dtype=jnp.int32)
    angles = frequencies(HEAD_DIMENSION)[:, None] * positions.astype(jnp.float32)[None, :]
    tables = dict(cosines=jnp.cos(angles), sines=jnp.sin(angles), norms=jnp.stack([norm_attn, norm_ffn]))
    routing = dict(router=w_router.T, depths=depths)
    heads = dict(w_query_hbm=w_query, key_weight_hbm=key_weight.T, value_weight_hbm=value_weight.T)
    weights = heads | dict(w_out_hbm=w_out, w_gate_hbm=w_gate, w_up_hbm=w_up, w_down_hbm=w_down.T)
    nb = mesh_sizes[0]
    saved = forward(
        tables | routing | dict(tokens=tokens[0].T, cotangent=cotangent[0].T, segments=segments), weights, nb
    )
    operands = dict(
        metas_hbm=saved["metas"], turned_hbm=saved["turned"], dat_hbm=saved["dat"], att_hbm=saved["att"],
        lse_hbm=saved["lse"], kv_hbm=saved["kv"], grad_hbm=saved["grad_hidden"], hid_1_hbm=saved["hid_1"],
        hid_0_hbm=saved["hid"], branch_hbm=saved["branch"], slope_hbm=saved["slope"], silu_hbm=saved["silu"],
        middle_hbm=saved["middle"],
    )
    bottom = backward(1, tables | routing | dict(small_before=saved["small"]), weights | operands, nb)
    return final(tables, saved, saved, bottom, weights, mesh_sizes)


def solution(mesh):
    sizes = (mesh.shape["blk"], mesh.shape["dp"])
    return jax.shard_map(
        functools.partial(local, mesh_sizes=sizes),
        mesh=mesh,
        in_specs=(
            P("dp", "blk", None),
            P("dp", "blk"),
            P("dp", "blk"),
            P(),
            P(),
            P(),
            P(),
            P(),
            P(),
            P(),
            P(),
            P(),
            P(),
            P("dp", "blk", None),
        ),
        out_specs=(
            P("dp", "blk", None),
            P("dp", "blk", None),
            P("blk"),
            P("blk"),
            P("blk", None),
            P("blk", None),
            P("blk", None),
            P("blk", None),
            P("blk", None),
            P("blk", None),
            P("blk", None),
            P("blk", None),
        ),
        check_vma=False,
    )
```

```python
import functools
import itertools
import math
import types

import jax
import jax.numpy as jnp
from jax import lax
from jax.experimental import pallas as pl
from jax.experimental.pallas import tpu as pltpu
from jax.sharding import PartitionSpec as P

QUERY_HEADS = 15
KEY_VALUE_HEADS = 5
HEAD_DIMENSION = 64
RECUR = 2
HEAD_SHARE = QUERY_HEADS // KEY_VALUE_HEADS
KEYS_WIDTH = KEY_VALUE_HEADS * HEAD_DIMENSION
PAIR = 2 * HEAD_DIMENSION
UNIT_COLUMNS = 256
SPAN = 2
VMEM_LIMIT = 63 * 1024 * 1024

epsilon = 1e-05
masked_score = -1e30
low = jnp.bfloat16


def frequencies(head_size):
    return jnp.exp(
        jnp.arange(head_size // 2, dtype=jnp.float32) * (-2.0 * math.log(10000.0) / head_size)
    )


def rms_scale(values):
    return lax.rsqrt(jnp.mean(values * values, axis=-1, keepdims=True) + epsilon)


def norm_gradient(grad_norm, values, gain):
    scale = rms_scale(values)
    weighted = grad_norm * gain
    grad_values = scale * weighted - values * (scale * scale * scale) * jnp.mean(
        weighted * values, axis=-1, keepdims=True
    )
    return grad_values, jnp.sum(grad_norm * values * scale, axis=0, keepdims=True)


def dot_last(left, right):
    return lax.dot_general(left, right, (((1,), (1,)), ((), ())), preferred_element_type=jnp.float32)


def plain_dot(left, right):
    return jnp.dot(left, right, preferred_element_type=jnp.float32)


def bits_of(number, count):
    return tuple((number >> (count - 1 - at)) & 1 for at in range(count))


def bit_of(position, bit):
    return lax.rem(position // (1 << bit), 2)


def block_bits(block, m):
    return tuple(bit_of(block, bit) for bit in range(m - 1, -1, -1))


def flipped(position, bit):
    return position + (1 << bit) * (1 - 2 * bit_of(position, bit))


def remote(source, target, sems, at, device):
    return pltpu.make_async_remote_copy(
        src_ref=source,
        dst_ref=target,
        send_sem=sems[0].at[at],
        recv_sem=sems[1].at[at],
        device_id=device,
        device_id_type=pl.DeviceIdType.MESH,
    )


def greet(partners):
    barrier = pltpu.get_barrier_semaphore()
    for partner in partners:
        pl.semaphore_signal(barrier, inc=1, device_id=partner, device_id_type=pl.DeviceIdType.MESH)
    pl.semaphore_wait(barrier, len(partners))


def turn_heads(turned, cosine, sine, heads):
    split = turned.reshape(heads, 2, HEAD_DIMENSION // 2, turned.shape[1])
    first, second = split[:, 0], split[:, 1]
    both = jnp.stack([first * cosine - second * sine, second * cosine + first * sine], axis=1)
    return both.reshape(turned.shape)


def turn_back(turned, cosine, sine, heads):
    return turn_heads(turned, cosine, -sine, heads)


def head_rows(group, member):
    head = group * HEAD_SHARE + member
    return pl.ds(pl.multiple_of(head * HEAD_DIMENSION, HEAD_DIMENSION), HEAD_DIMENSION)


def as_column(row):
    wide = jnp.broadcast_to(row.astype(jnp.float32), (8, row.shape[1]))
    return wide.T[:, 0:1]


def key_steps(blk, span):
    return blk // (1 << span) + 1


def fill_bias(bias, metas, query_segments, level, blk, m, piece, span):
    many = 1 << span
    key_at = lax.broadcasted_iota(jnp.int32, (many * piece, piece), 0)
    query_at = lax.broadcasted_iota(jnp.int32, (many * piece, piece), 1)

    @pl.loop(0, key_steps(blk, span))
    def _(step):
        rows = metas[block_bits(step, m - span)].reshape(many, 8, piece)
        columns = jnp.concatenate([rows[block].T for block in range(many)], axis=0)
        live = jnp.where(columns[:, 1:2] > level, columns[:, 0:1], -1.0)
        shift = (blk - many * step) * piece
        allowed = (live == query_segments) & (key_at <= query_at + shift) | (key_at == query_at + shift)
        masked = jnp.where(allowed, 0.0, masked_score).astype(bias.dtype)
        bias[pl.ds(many * step, many)] = masked.reshape(many, piece, piece)


def step_bias(bias, step, piece, span):
    many = 1 << span
    here = bias[pl.ds(many * step, many)].reshape(many * piece, piece).astype(jnp.float32)
    return jnp.concatenate([here] * HEAD_SHARE, axis=1)


def kv_weight_loads(key_hbm, value_hbm, target, sems):
    copies = []
    for group in range(KEY_VALUE_HEADS):
        for side, source in enumerate((key_hbm, value_hbm)):
            rows = pl.ds(group * HEAD_DIMENSION, HEAD_DIMENSION)
            place = pl.ds(group * PAIR + side * HEAD_DIMENSION, HEAD_DIMENSION)
            copies.append(pltpu.make_async_copy(source.at[rows], target.at[place], sems.at[2 * group + side]))
    return copies


def turn_keys(both, cosine, sine):
    half = HEAD_DIMENSION // 2
    split = both.reshape(KEY_VALUE_HEADS, 4, half, both.shape[1])
    first, second = split[:, 0], split[:, 1]
    turned = [first * cosine - second * sine, second * cosine + first * sine, split[:, 2], split[:, 3]]
    return jnp.stack(turned, axis=1).reshape(both.shape)


def spec(memory):
    return pl.BlockSpec(memory_space=memory)


def shaped(entry):
    return jax.ShapeDtypeStruct(*entry)


def spaces(entries):
    return [pltpu.VMEM(*entry) for entry in entries]


def dma_semaphores(*shapes):
    return [pltpu.SemaphoreType.DMA(shape) for shape in shapes]


class Piece:
    def __init__(self, at, kept_at, slot, flavour, family, sems, bits):
        self.at, self.kept_at, self.slot, self.family, self.sems = at, kept_at, slot, family, sems
        self.m, self.n = bits
        left = list(range(self.m - 1, -1, -1))
        self.order = []
        for stage in range(self.m):
            place = len(left) - 1 if stage == 0 or flavour == 0 else 0
            self.order.append((left.pop(place), place, len(left)))
        self.last = self.m + self.n
        self.blk = lax.axis_index("blk")
        self.dp = lax.axis_index("dp") if self.n else None

    def half(self, ref, side):
        rows, columns = self.family.shape
        if self.family.split == 0:
            return ref.at[pl.ds(pl.multiple_of(side * (rows // 2), rows // 2), rows // 2), :]
        return ref.at[:, pl.ds(pl.multiple_of(side * (columns // 2), columns // 2), columns // 2)]

    def held(self, stage):
        if stage == 0:
            return self.family.part, self.slot
        return self.family.blk[stage - 1], self.kept_at

    def copy(self, stage):
        m, family = self.m, self.family
        if stage < m:
            bit, place, others = self.order[stage]
            ref, index = self.held(stage)
            chosen = [slice(None)] * (others + 1)
            chosen[place] = 1 - bit_of(self.blk, bit)
            source = ref.at[(index, *chosen)]
            target = family.blk[stage].at[self.kept_at]
            device = {"blk": flipped(self.blk, bit)}
        elif stage < self.last:
            bit = stage - m
            if bit == 0:
                source = self.half(family.blk[m - 1].at[self.kept_at], 1 - bit_of(self.dp, 0))
            else:
                source = family.dp[bit - 1].at[self.kept_at]
            target = family.dp[bit].at[self.kept_at]
            device = {"dp": flipped(self.dp, bit)}
        else:
            source = self.half(family.out.at[self.kept_at], bit_of(self.dp, 0))
            target = source
            device = {"dp": flipped(self.dp, 0)}
        return remote(source, target, self.sems, (self.at, stage), device)

    def start(self, stage):
        self.copy(stage).start()

    def finish(self, stage):
        m, family = self.m, self.family
        self.copy(stage).wait_recv()
        if stage < m:
            bit, place, others = self.order[stage]
            ref, index = self.held(stage)
            for combo in itertools.product(range(2), repeat=others):
                chosen = list(combo)
                chosen.insert(place, bit_of(self.blk, bit))
                into = family.blk[stage].at[(self.kept_at, *combo)]
                self.add(into, into, ref.at[(index, *chosen)])
            if stage == 0:
                self.copy(0).wait_send()
        elif stage < self.last:
            bit = stage - m
            got = family.dp[bit].at[self.kept_at]
            if bit == 0:
                own = self.half(family.blk[m - 1].at[self.kept_at], bit_of(self.dp, 0))
            else:
                own = family.dp[bit - 1].at[self.kept_at]
            into = got
            if stage == self.last - 1:
                into = self.half(family.out.at[self.kept_at], bit_of(self.dp, 0))
            self.add(into, got, own)

    def add(self, into, left, right):
        into[...] = left[...] + right[...]

    def drained(self, stages):
        for stage in stages:
            self.copy(stage).wait_send()


def feed_forward_backward(at, level, gradient, ready, done):
    column = at.router[level:level + 1, :].astype(jnp.float32)
    active = as_column(at.depths[...]) > float(level)
    hidden = at.hid_level[...]
    chosen = jax.nn.sigmoid(jnp.sum(hidden * column, axis=1, keepdims=True))
    at.dbranch[...] = jnp.where(active, chosen, 0.0) * gradient
    dchosen = jnp.where(active, jnp.sum(gradient * at.branch_level[...], axis=1, keepdims=True), 0.0)
    dlogit = dchosen * chosen * (1.0 - chosen)
    at.small[2 + level:3 + level, :] = jnp.sum(hidden * dlogit, axis=0, keepdims=True)
    at.grad_hidden[...] = gradient + dlogit * column
    at.dffn[...] = at.dbranch[...].astype(low)

    ready(0)
    dinner = plain_dot(at.dffn[...], at.w_down[...])
    at.dgate[...] = (dinner * at.slope_level[...].astype(jnp.float32)).astype(low)
    at.dup[...] = (dinner * at.silu_level[...].astype(jnp.float32)).astype(low)
    done()
    at.dnorm_turned[...] = plain_dot(at.w_gate[...], at.dgate[...].T) + plain_dot(at.w_up[...], at.dup[...].T)
    ready(1)
    dnorm = at.dnorm_turned[...].T
    dmiddle, gain_share = norm_gradient(dnorm, at.middle_level[...], at.norms[1:2, :].astype(jnp.float32))
    at.small[1:2, :] += gain_share
    at.grad_hidden[...] += dmiddle
    dattn = (at.dbranch[...] + dmiddle).astype(low)
    lead = at.far.shape[1] - dattn.shape[1]
    at.far[:, :lead] = jnp.zeros((dattn.shape[0], lead), low)
    at.far[:, lead:] = dattn
    at.dat[...] = plain_dot(at.w_out[...], dattn.T).astype(low)


def forward_kernel(sizes, names, *refs):
    m, piece = sizes
    at = types.SimpleNamespace(**dict(zip(names, refs)))
    blk = lax.axis_index("blk")
    mine = block_bits(blk, m)
    kv, metas = at.kv, at.metas
    weights = (
        (at.w_query_hbm, at.w_query), (at.w_out_hbm, at.w_out), (at.w_gate_hbm, at.w_gate), (at.w_up_hbm, at.w_up), (at.w_down_hbm, at.w_down),
    )
    loads = [pltpu.make_async_copy(*pair, at.load_sems.at[index]) for index, pair in enumerate(weights)]
    kv_loads = kv_weight_loads(at.key_weight_hbm, at.value_weight_hbm, at.kv_weight, at.weight_sems)
    for load in kv_loads + loads:
        load.start()
    saved = (
        (at.normed, at.normed_out), (at.turned, at.turned_out), (kv, at.kv_out), (at.lse, at.lse_out),
        (at.att, at.att_out), (at.nffn, at.nffn_out), (at.inner, at.inner_out),
    )

    def save(index, level):
        return pltpu.make_async_copy(
            saved[index][0].at[level] if index == 2 else saved[index][0], saved[index][1].at[level], at.save_sems.at[index, level]
        )

    first = (
        (at.hid.at[0], at.hid_out), (at.middle, at.middle_out), (at.silu, at.silu_out),
        (at.slope, at.slope_out), (at.branch, at.branch_out), (metas, at.metas_out),
        (at.far, at.far_out), (at.dat, at.dat_out), (at.dffn, at.dffn_out), (at.dgate, at.dgate_out), (at.dup, at.dup_out),
        (at.hid.at[1], at.hid_1_out),
    )
    late = [pltpu.make_async_copy(*pair, at.late_sems.at[index]) for index, pair in enumerate(first)]
    segment_row = at.segments[...].astype(jnp.float32)
    depth_column = as_column(at.depths[...])
    metas[mine] = jnp.concatenate(
        [segment_row, at.depths[...].astype(jnp.float32), jnp.zeros((6, piece), jnp.float32)], axis=0
    )
    greet([{"blk": flipped(blk, bit)} for bit in range(m)])

    def place(known):
        return tuple(slice(None) if bit in known else mine[m - 1 - bit] for bit in range(m - 1, -1, -1))

    orders = (list(range(1, m)), list(range(m - 1, 0, -1)))
    kv_sems = (at.kv_send, at.kv_recv)

    def kv_copies(level, group, stage):
        if stage == m - 1:
            ref = kv.at[(level, group, *place(range(1, m)))]
            return [remote(ref, ref, kv_sems, (level, group, 2 * stage), {"blk": flipped(blk, 0)})]
        copies = []
        for side, order in enumerate(orders):
            rows = pl.ds(side * (piece // 2), piece // 2)
            ref = kv.at[(level, group, *place(order[:stage]), rows)]
            copies.append(remote(ref, ref, kv_sems, (level, group, 2 * stage + side), {"blk": flipped(blk, order[stage])}))
        return copies

    def kv_advance(level, group, stage):
        if stage > 0:
            for copy in kv_copies(level, group, stage - 1):
                copy.wait_recv()
        if stage < m:
            for copy in kv_copies(level, group, stage):
                copy.start()

    def meta_copy(stage):
        bits = list(range(1, m)) + [0]
        ref = metas.at[place(bits[:stage])]
        return remote(ref, ref, (at.meta_send, at.meta_recv), stage, {"blk": flipped(blk, bits[stage])})

    meta_copy(0).start()
    cosine, sine = at.cosines[...], at.sines[...]
    gain_attn, gain_ffn = at.norms[0:1, :].astype(jnp.float32), at.norms[1:2, :].astype(jnp.float32)
    routers = at.router[...].astype(jnp.float32)
    at.hid[0] = at.tokens[...].T.astype(jnp.float32)
    late[0].start()
    at.query_pad[HEAD_DIMENSION:, :] = jnp.zeros_like(at.query_pad[HEAD_DIMENSION:, :])

    @pl.loop(0, RECUR)
    def _(level):
        @pl.when(level > 0)
        def _():
            for index in range(5):
                save(index, 0).wait()

        hidden = at.hid[level]
        at.flat[...] = (hidden * rms_scale(hidden) * gain_attn).astype(low)
        at.normed[...] = at.flat[...].T

        @pl.when(level == 0)
        def _():
            for load in kv_loads:
                load.wait()

        both = turn_keys(plain_dot(at.kv_weight[...], at.normed[...]), cosine, sine).T.astype(low)
        for group in range(KEY_VALUE_HEADS):
            kv[(level, group, *mine)] = both[:, group * PAIR:(group + 1) * PAIR]
            kv_advance(level, group, 0)

        @pl.when(level == 0)
        def _():
            loads[0].wait()
            for stage in range(1, m - 1):
                meta_copy(stage - 1).wait_recv()
                meta_copy(stage).start()

        queries = turn_heads(plain_dot(at.flat[...], at.w_query[...]).T, cosine, sine, QUERY_HEADS)
        at.turned[...] = (queries * HEAD_DIMENSION ** (-0.5)).astype(low)

        @pl.when(level == 0)
        def _():
            for stage in range(max(1, m - 1), m):
                meta_copy(stage - 1).wait_recv()
                meta_copy(stage).start()

        for stage in range(1, m - 1):
            for group in range(KEY_VALUE_HEADS):
                kv_advance(level, group, stage)
        kv_advance(level, 0, m - 1)

        @pl.when(level == 0)
        def _():
            meta_copy(m - 1).wait_recv()
            late[5].start()

        fill_bias(at.bias, metas, segment_row, level.astype(jnp.float32), blk, m, piece, SPAN)

        @pl.loop(0, KEY_VALUE_HEADS)
        def _(group):
            @pl.when(group + 1 < KEY_VALUE_HEADS)
            def _():
                kv_advance(level, group + 1, m - 1)

            kv_advance(level, group, m)
            for member in range(HEAD_SHARE):
                at.query_pad[:HEAD_DIMENSION, member * piece:(member + 1) * piece] = at.turned[head_rows(group, member), :]
            at.top[...] = jnp.full_like(at.top, masked_score)
            at.total[...] = jnp.zeros_like(at.total)

            @pl.loop(0, key_steps(blk, SPAN))
            def _(index):
                step = key_steps(blk, SPAN) - 1 - index
                rows = kv[(level, group, *block_bits(step, m - SPAN))].reshape((1 << SPAN) * piece, PAIR)
                scores = plain_dot(rows, at.query_pad[...]) + step_bias(at.bias, step, piece, SPAN)
                before = at.top[0:1, :]
                after = jnp.maximum(before, jnp.max(scores, axis=0, keepdims=True))
                raised = jnp.exp(scores - after)
                shrink = jnp.exp(before - after)
                at.top[0:1, :] = after
                ones = jnp.ones((16, rows.shape[0]), low)
                left = jnp.concatenate([rows.T[HEAD_DIMENSION:], ones], axis=0)
                at.total[...] = at.total[...] * shrink + plain_dot(left, raised.astype(low))

            sums = at.total[HEAD_DIMENSION:HEAD_DIMENSION + 1, :]
            at.lse[pl.ds(group, 1), :] = at.top[0:1, :] + jnp.log(sums)
            out = at.total[:HEAD_DIMENSION, :] / sums
            for member in range(HEAD_SHARE):
                at.att[head_rows(group, member), :] = out[:, member * piece:(member + 1) * piece].astype(low)

        for index in range(5):
            save(index, level).start()

        @pl.when(level == 0)
        def _():
            loads[1].wait()

        @pl.when(level > 0)
        def _():
            save(5, 0).wait()
            save(6, 0).wait()
            for copy in late[1:5]:
                copy.wait()

        attn = plain_dot(at.att[...].T, at.w_out[...])
        mid = at.hid[level] + attn
        at.middle[...] = mid
        at.branch[...] = attn
        at.flat[...] = (mid * rms_scale(mid) * gain_ffn).astype(low)
        at.nffn[...] = at.flat[...].T
        save(5, level).start()

        @pl.when(level == 0)
        def _():
            loads[2].wait()
            loads[3].wait()

        gate_pre = plain_dot(at.flat[...], at.w_gate[...])
        up_pre = plain_dot(at.flat[...], at.w_up[...])
        opened = jax.nn.sigmoid(gate_pre)
        passed = gate_pre * opened
        at.silu[...] = passed.astype(low)
        at.slope[...] = (up_pre * (opened + passed - passed * opened)).astype(low)
        at.inner[...] = (passed * up_pre).astype(low).T
        save(6, level).start()

        @pl.when(level == 0)
        def _():
            loads[4].wait()

        at.branch[...] += plain_dot(at.w_down[...], at.inner[...]).T
        column = jnp.where(level == 0, routers[0:1, :], routers[1:2, :])
        logit = jnp.sum(at.hid[level] * column, axis=1, keepdims=True)
        weight = jnp.where(depth_column > level.astype(jnp.float32), jax.nn.sigmoid(logit), 0.0)
        at.hid[level + 1] = at.hid[level] + weight * at.branch[...]

        @pl.when(level == 0)
        def _():
            for copy in late[1:5]:
                copy.start()

    at.hidden_out[...] = at.hid[RECUR].T
    top = RECUR - 1
    at.hid_level, at.branch_level, at.middle_level = at.hid.at[top], at.branch, at.middle
    at.silu_level, at.slope_level = at.silu, at.slope
    at.small[...] = jnp.zeros_like(at.small)
    feed_forward_backward(at, top, at.cotangent[...].T.astype(jnp.float32), lambda part: None, lambda: None)
    for copy in late[6:]:
        copy.start()
    for stage in range(m):
        meta_copy(stage).wait_send()
    for level in range(RECUR):
        for group in range(KEY_VALUE_HEADS):
            for stage in range(m):
                for copy in kv_copies(level, group, stage):
                    copy.wait_send()
    for index in range(len(saved)):
        save(index, RECUR - 1).wait()
    for copy in late[:1] + late[5:]:
        copy.wait()


def far_width(width):
    return 2 * width + 2 * KEYS_WIDTH - 1536


def forward(small, weights, nb):
    m = nb.bit_length() - 1
    width, piece = small["tokens"].shape
    hidden_units = weights["w_gate_hbm"].shape[1]
    blocks, wide = (2,) * m, HEAD_SHARE * piece
    rows, turned = ((piece, width), jnp.float32), ((RECUR, width, piece), low)
    hidden = ((piece, hidden_units), low)
    saved = dict(
        normed=turned, turned=turned, kv=((RECUR, KEY_VALUE_HEADS, *blocks, piece, PAIR), low),
        lse=((RECUR, 8, wide), jnp.float32), att=turned, nffn=turned, inner=((RECUR, hidden_units, piece), low),
        metas=((*blocks, 8, piece), jnp.float32), far=((piece, far_width(width)), low), dat=((width, piece), low),
        dffn=((piece, width), low), dgate=hidden, dup=hidden,
    )
    first = dict(hid=rows, middle=rows, silu=hidden, slope=hidden, branch=rows)
    outs = dict(hidden_out=((width, piece), jnp.float32), grad_hidden=rows, small=((8, width), jnp.float32))
    anywhere = {name + "_out": entry for name, entry in (saved | first | dict(hid_1=rows)).items()}
    single = {name: (shape[1:], dtype) for name, (shape, dtype) in saved.items() if shape[0] == RECUR and name not in ("kv", "metas")}
    buffers = {name[:-4]: (array.shape, array.dtype) for name, array in weights.items()} | saved | single | first | dict(
        kv_weight=((2 * KEYS_WIDTH, width), low),
        hid=((RECUR + 1, piece, width), jnp.float32), flat=((piece, width), low),
        bias=((nb, piece, piece), jnp.float32), query_pad=((PAIR, wide), low), top=((8, wide), jnp.float32),
        total=((HEAD_DIMENSION + 16, wide), jnp.float32), dbranch=rows, dnorm_turned=((width, piece), jnp.float32),
    )
    semaphores = dict(
        load_sems=(5,), weight_sems=(2 * KEY_VALUE_HEADS,), save_sems=(7, RECUR), late_sems=(12,), kv_send=(RECUR, KEY_VALUE_HEADS, 2 * m),
        kv_recv=(RECUR, KEY_VALUE_HEADS, 2 * m), meta_send=(m,), meta_recv=(m,),
    )
    results = pl.pallas_call(
        functools.partial(forward_kernel, (m, piece), (*small, *weights, *outs, *anywhere, *buffers, *semaphores)),
        out_shape=[shaped(entry) for entry in (outs | anywhere).values()],
        in_specs=[spec(pltpu.VMEM)] * len(small) + [spec(pl.ANY)] * len(weights),
        out_specs=[spec(pltpu.VMEM)] * len(outs) + [spec(pl.ANY)] * len(anywhere),
        scratch_shapes=spaces(buffers.values()) + dma_semaphores(*semaphores.values()),
        compiler_params=pltpu.CompilerParams(
            collective_id=1, has_side_effects=True, vmem_limit_bytes=VMEM_LIMIT
        ),
        cost_estimate=pl.CostEstimate(
            flops=3 * RECUR * piece * width * 10240, bytes_accessed=48 * 1024 * 1024, transcendentals=0
        ),
        name="forward_levels",
    )(*small.values(), *weights.values())
    return dict(zip((*outs, *(name[:-4] for name in anywhere)), results))


class AttentionBackward:
    def __init__(self, at, m, piece, level, span):
        self.at, self.m, self.piece, self.level, self.span = at, m, piece, level, span
        self.blk = lax.axis_index("blk")
        self.family = types.SimpleNamespace(part=at.part, blk=at.halves, dp=(), out=None, shape=(piece // 2, PAIR), split=0)

    def pieces(self, group):
        sems = (self.at.kv_send, self.at.kv_recv)
        return [
            Piece(2 * group + side, 2 * group + side, 2 * group + side, side, self.family, sems, (self.m, 0))
            for side in range(2)
        ]

    def move(self, group, stage):
        for piece_of in self.pieces(group):
            piece_of.finish(stage)
            if stage + 1 < self.m:
                piece_of.start(stage + 1)

    def begin(self):
        at = self.at
        query_segments = at.metas[block_bits(self.blk, self.m)][0:1, :]
        fill_bias(at.bias, at.metas, query_segments, float(self.level), self.blk, self.m, self.piece, self.span)
        at.query_pad[HEAD_DIMENSION:, :] = jnp.zeros_like(at.query_pad[HEAD_DIMENSION:, :])
        at.dat_pad[:HEAD_DIMENSION, :] = jnp.zeros_like(at.dat_pad[:HEAD_DIMENSION, :])

    def group(self, group):
        at, m, piece, blk = self.at, self.m, self.piece, self.blk
        half = piece // 2
        carried = []
        for member in range(HEAD_SHARE):
            rows, lanes = head_rows(group, member), slice(member * piece, (member + 1) * piece)
            at.query_pad[:HEAD_DIMENSION, lanes] = at.turned[rows, :]
            at.dat_pad[HEAD_DIMENSION:, lanes] = at.dat_turned[rows, :]
            product = at.dat_turned[rows, :].astype(jnp.float32) * at.att_turned[rows, :].astype(jnp.float32)
            carried.append(jnp.sum(product, axis=0, keepdims=True))
        carried = jnp.concatenate(carried, axis=1)
        at.query_rows[...] = at.query_pad[...].T
        at.dat_rows[...] = at.dat_pad[...].T
        log_total = at.lse[pl.ds(group, 1), :]
        at.dq_sum[...] = jnp.zeros_like(at.dq_sum)

        span, lead = self.span, m - self.span

        @pl.loop(0, key_steps(blk, span))
        def _(step):
            rows = at.kv[(group, *block_bits(step, lead))].reshape((1 << span) * piece, PAIR)
            probability = jnp.exp(plain_dot(rows, at.query_pad[...]) + step_bias(at.bias, step, piece, span) - log_total)
            dprob = plain_dot(rows, at.dat_pad[...])
            dscores = (probability * (dprob - carried)).astype(low)
            share = plain_dot(dscores, at.query_rows[...]) + plain_dot(probability.astype(low), at.dat_rows[...])
            share = share.astype(low)
            for block in range(1 << span):
                for side in range(2):
                    first = block * piece + side * half
                    place = (2 * group + side, *block_bits(step, lead), *bits_of(block, span))
                    at.part[place] = share[first:first + half]
            at.dq_sum[...] += plain_dot(rows.T[:HEAD_DIMENSION], dscores)

        @pl.loop(key_steps(blk, span), 1 << lead)
        def _(step):
            for block in range(1 << span):
                for side in range(2):
                    place = (2 * group + side, *block_bits(step, lead), *bits_of(block, span))
                    at.part[place] = jnp.zeros((half, PAIR), low)

        for piece_of in self.pieces(group):
            piece_of.start(0)
        for member in range(HEAD_SHARE):
            at.dq_turned[head_rows(group, member), :] = at.dq_sum[:, member * piece:(member + 1) * piece]

    def follow(self, group):
        for stage in range(self.m - 1):
            earlier = group - 1 - stage
            if isinstance(group, int):
                if 0 <= earlier < KEY_VALUE_HEADS:
                    self.move(earlier, stage)
            else:
                @pl.when(earlier >= 0)
                def _():
                    self.move(earlier, stage)

    def queries(self, cosine, sine):
        at = self.at
        dqueries = turn_back(at.dq_turned[...] * HEAD_DIMENSION ** (-0.5), cosine, sine, QUERY_HEADS).astype(low)
        self.put(2 * KEYS_WIDTH, dqueries.T)
        at.dnorm[...] = plain_dot(at.w_query[...], dqueries).T

    def put(self, column, values):
        self.at.near[:, column:column + values.shape[1]] = values

    def keys(self, cosine, sine):
        at, m = self.at, self.m
        filled = 2 * KEYS_WIDTH + QUERY_HEADS * HEAD_DIMENSION
        self.put(filled, jnp.zeros((self.piece, at.near.shape[1] - filled), low))
        sums = []
        for group in range(KEY_VALUE_HEADS):
            self.move(group, m - 1)
            sums.append(jnp.concatenate([at.halves[m - 1][2 * group], at.halves[m - 1][2 * group + 1]], axis=0))
        both = jnp.concatenate(sums, axis=1).astype(jnp.float32).T
        both = turn_keys(both, cosine, -sine).astype(low).T
        self.put(0, both)
        at.dnorm[...] += plain_dot(both, at.kv_weight[...])

    def drained(self):
        for group in range(KEY_VALUE_HEADS):
            for piece_of in self.pieces(group):
                piece_of.drained(range(1, self.m))


def attention_buffers(nb, piece, width, bias_type):
    m, wide, heads = nb.bit_length() - 1, HEAD_SHARE * piece, 2 * KEY_VALUE_HEADS
    turned = ((width, piece), low)
    pad, pad_rows = ((PAIR, wide), low), ((wide, PAIR), low)
    buffers = dict(
        turned=turned, dat_turned=turned, att_turned=turned, kv=((KEY_VALUE_HEADS, *(2,) * m, piece, PAIR), low),
        lse=((8, wide), jnp.float32), metas=((*(2,) * m, 8, piece), jnp.float32), w_query=((width, width), low),
        kv_weight=((2 * KEYS_WIDTH, width), low), dq_turned=((width, piece), jnp.float32),
        bias=((nb, piece, piece), bias_type), query_pad=pad, dat_pad=pad, query_rows=pad_rows, dat_rows=pad_rows,
        dq_sum=((HEAD_DIMENSION, wide), jnp.float32), part=((heads, *(2,) * m, piece // 2, PAIR), low),
        dnorm=((piece, width), jnp.float32), hid=((piece, width), jnp.float32),
    )
    for stage in range(m):
        buffers["half_%d" % stage] = ((heads, *(2,) * (m - 1 - stage), piece // 2, PAIR), low)
    return buffers


def backward_kernel(sizes, names, *refs):
    m, piece, level = sizes
    at = types.SimpleNamespace(**dict(zip(names, refs)))
    at.halves = [getattr(at, "half_%d" % stage) for stage in range(m)]
    at.near = at.near_out
    blk = lax.axis_index("blk")
    pairs = (
        (at.metas_hbm, at.metas), (at.turned_hbm.at[level], at.turned), (at.dat_hbm, at.dat_turned),
        (at.att_hbm.at[level], at.att_turned), (at.lse_hbm.at[level], at.lse), (at.kv_hbm.at[level], at.kv),
        (at.w_query_hbm, at.w_query),
        (at.grad_hbm, at.grad_hidden), (at.hid_1_hbm, at.hid),
        (at.hid_0_hbm, at.hid_level), (at.branch_hbm, at.branch_level), (at.w_down_hbm, at.w_down),
        (at.slope_hbm, at.slope_level), (at.silu_hbm, at.silu_level), (at.w_gate_hbm, at.w_gate), (at.w_up_hbm, at.w_up),
        (at.middle_hbm, at.middle_level), (at.w_out_hbm, at.w_out),
    )
    loads = [pltpu.make_async_copy(*pair, at.load_sems.at[index]) for index, pair in enumerate(pairs)]
    loads += kv_weight_loads(at.key_weight_hbm, at.value_weight_hbm, at.kv_weight, at.weight_sems)
    for load in loads:
        load.start()
    saves = [
        pltpu.make_async_copy(*pair, at.save_sems.at[index])
        for index, pair in enumerate(((at.dgate, at.dgate_out), (at.dup, at.dup_out)))
    ]
    greet([{"blk": flipped(blk, bit)} for bit in range(m)])
    work = AttentionBackward(at, m, piece, level, SPAN)
    loads[0].wait()
    work.begin()
    for load in loads[1:6]:
        load.wait()

    @pl.loop(0, KEY_VALUE_HEADS)
    def _(group):
        work.group(group)
        work.follow(group)

    cosine, sine = at.cosines[...], at.sines[...]
    for virtual in range(KEY_VALUE_HEADS, KEY_VALUE_HEADS + m - 1):
        work.follow(virtual)
        if virtual == KEY_VALUE_HEADS:
            loads[6].wait()
            work.queries(cosine, sine)
    for load in loads[7:]:
        load.wait()
    work.keys(cosine, sine)
    dhidden, gain_share = norm_gradient(at.dnorm[...], at.hid[...], at.norms[0:1, :].astype(jnp.float32))
    at.small[...] = at.small_before[...]
    at.small[0:1, :] = gain_share
    gradient = at.grad_hidden[...] + dhidden
    at.dnorm[...] = gradient
    feed_forward_backward(at, level - 1, at.dnorm[...], lambda part: None, lambda: [save.start() for save in saves])
    work.drained()
    for save in saves:
        save.wait()


def backward(level, small, operands, nb):
    m = nb.bit_length() - 1
    piece, width = operands["grad_hbm"].shape
    hidden_units = operands["w_gate_hbm"].shape[1]
    rows, flat, hidden = ((piece, width), jnp.float32), ((piece, width), low), ((piece, hidden_units), low)
    outs = dict(
        grad_hidden=rows, small=((8, width), jnp.float32), near_out=((piece, 1792), low), dffn=flat,
        dat=((width, piece), low), far=((piece, far_width(width)), low),
    )
    anywhere = dict(dgate_out=hidden, dup_out=hidden)
    buffers = attention_buffers(nb, piece, width, jnp.float32) | dict(
        hid_level=rows, branch_level=rows, middle_level=rows, w_down=((width, hidden_units), low), slope_level=hidden,
        silu_level=hidden, w_gate=((width, hidden_units), low), w_up=((width, hidden_units), low),
        w_out=((width, width), low), dbranch=rows, dnorm_turned=((width, piece), jnp.float32), dgate=hidden, dup=hidden,
    )
    sums = (2 * KEY_VALUE_HEADS, m)
    semaphores = dict(load_sems=(18,), weight_sems=(2 * KEY_VALUE_HEADS,), save_sems=(2,), kv_send=sums, kv_recv=sums)
    results = pl.pallas_call(
        functools.partial(
            backward_kernel, (m, piece, level), (*small, *operands, *outs, *anywhere, *buffers, *semaphores)
        ),
        out_shape=[shaped(entry) for entry in (outs | anywhere).values()],
        in_specs=[spec(pltpu.VMEM)] * len(small) + [spec(pl.ANY)] * len(operands),
        out_specs=[spec(pltpu.VMEM)] * len(outs) + [spec(pl.ANY)] * len(anywhere),
        scratch_shapes=spaces(buffers.values()) + dma_semaphores(*semaphores.values()),
        compiler_params=pltpu.CompilerParams(
            collective_id=2, has_side_effects=True, vmem_limit_bytes=VMEM_LIMIT
        ),
        cost_estimate=pl.CostEstimate(
            flops=2 * piece * width * 20000, bytes_accessed=32 * 1024 * 1024, transcendentals=0
        ),
        name="backward_level",
    )(*small.values(), *operands.values())
    return dict(zip((*outs, *anywhere), results))


WIDE_SLOTS, DOWN_SLOTS = 4, 2


def final_kernel(sizes, names, *refs):
    nb, m, n, piece, rows, padded, near_width = sizes
    at = types.SimpleNamespace(**dict(zip(names, refs)))
    at.halves = [getattr(at, "half_%d" % stage) for stage in range(m)]
    blk, dp = lax.axis_index("blk"), lax.axis_index("dp")
    at.near = at.gate_side.at[pl.ds(0, piece), pl.ds(0, near_width)]
    counter = itertools.count()

    def load(source, target):
        return pltpu.make_async_copy(source, target, at.load_sems.at[next(counter)])

    def both_lanes(ref, target):
        return [load(ref.at[level], target.at[:, pl.ds(level * piece, piece)]) for level in range(RECUR)]

    def both_rows(low_ref, deep_ref, target, width):
        pairs = ((low_ref, 0), (deep_ref, piece))
        return [load(ref, target.at[pl.ds(first, piece), pl.ds(0, width)]) for ref, first in pairs]

    hidden_units, width = at.gate_side.shape[1], at.dffn.shape[1]
    far_lanes = at.far_0_hbm.shape[1]
    loads = types.SimpleNamespace(
        nffn=both_lanes(at.nffn_hbm, at.left),
        dgate=both_rows(at.dgate_0_hbm, at.dgate_1_hbm, at.gate_side, hidden_units),
        inner=both_lanes(at.inner_hbm, at.inner),
        dffn=both_rows(at.dffn_0_hbm, at.dffn_1_hbm, at.dffn, width),
        metas=[load(at.metas_hbm, at.metas)],
        heads=[
            load(at.turned_hbm.at[0], at.turned), load(at.dat_hbm, at.dat_turned), load(at.att_hbm.at[0], at.att_turned),
            load(at.lse_hbm.at[0], at.lse), load(at.kv_hbm.at[0], at.kv),
        ],
        dup=both_rows(at.dup_0_hbm, at.dup_1_hbm, at.up_side, hidden_units),
        w_query=[load(at.w_query_hbm, at.w_query)],
        rest=[
            load(at.hid_hbm, at.hid), load(at.grad_hbm, at.grad),
        ],
        attended=both_lanes(at.attended_hbm, at.left_attended),
        kv_weight=kv_weight_loads(at.key_weight_hbm, at.value_weight_hbm, at.kv_weight, at.weight_sems),
    )
    late = types.SimpleNamespace(
        near=[load(at.near_1_hbm, at.gate_side.at[pl.ds(piece, piece), pl.ds(0, near_width)])],
        far=both_rows(at.far_0_hbm, at.far_1_hbm, at.up_side, far_lanes),
        normed=both_lanes(at.normed_hbm, at.left),
    )

    def begin(copies):
        for copy in copies:
            copy.start()

    def ready(copies):
        for copy in copies:
            copy.wait()

    for copies in vars(loads).values():
        begin(copies)
    greet([{"blk": flipped(blk, bit)} for bit in range(m)] + [{"dp": flipped(dp, bit)} for bit in range(n)])

    down_rows = at.part_down.shape[-2]

    def family(name, shape, split):
        return types.SimpleNamespace(
            part=getattr(at, "part_" + name), out=getattr(at, "out_" + name), shape=shape, split=split,
            blk=[getattr(at, "blk_%s_%d" % (name, stage)) for stage in range(m)],
            dp=[getattr(at, "dp_%s_%d" % (name, stage)) for stage in range(n)],
        )

    wide = family("wide", (2 * padded, UNIT_COLUMNS), 1)
    down = family("down", (down_rows, width), 0)
    little = family("small", (16, 128), 0)
    sems = (at.send_sems, at.recv_sems)
    units = itertools.count()

    def unit(holder, index, flavour):
        return Piece(next(units), index, index % holder.part.shape[0], flavour, holder, sems, (m, n))

    pairs = [[unit(wide, 0, 0), unit(wide, 1, 1)]]
    pairs += [[unit(wide, index, 0), unit(down, index - 2, 1)] for index in range(2, 7)]
    pairs += [[unit(wide, index, 0), unit(wide, index + 1, 1)] for index in (7, 9, 11)]
    pairs += [[unit(wide, 13, 0), unit(wide, 14, 1), unit(little, 0, 0)]]

    def compute_wide(index, slot):
        if index == 0:
            ready(loads.nffn)
            ready(loads.dgate)
        if index == 5:
            begin(late.near)
            ready(loads.dup)
        if index == 10:
            begin(late.far)
            begin(late.normed)
            ready(late.near)
            ready(late.normed)
            ready(loads.attended)
            ready(late.far)
        block, column = index // 5, (index % 5) * UNIT_COLUMNS
        second = 1280 + column
        upper_columns, lower_columns = slice(column, column + UNIT_COLUMNS), slice(second, second + UNIT_COLUMNS)
        if block < 2:
            right = at.gate_side if block == 0 else at.up_side
            upper = plain_dot(at.left[...], right[:, upper_columns])
            lower = plain_dot(at.left[...], right[:, lower_columns])
        else:
            upper = plain_dot(at.left[...], at.gate_side[:, upper_columns])
            lower = None
            if second < 1600:
                lower = plain_dot(at.left[...], at.gate_side[:, lower_columns])
            if second >= 1536:
                more = plain_dot(at.left_attended[...], at.up_side[:, second - 1536:second - 1536 + UNIT_COLUMNS])
                lower = more if lower is None else lower + more
        for target in range(nb):
            here = slice(target * padded, (target + 1) * padded)
            both = jnp.concatenate([upper[here], lower[here]], axis=0)
            at.part_wide[(slot, *bits_of(target, m))] = both.astype(low)

    def compute_down(index, slot):
        if index == 0:
            ready(loads.inner)
            ready(loads.dffn)
        firsts = [(target * 5 + index) * down_rows for target in range(nb)]
        left = jnp.concatenate([at.inner[first:first + down_rows, :] for first in firsts], axis=0)
        result = plain_dot(left, at.dffn[...])
        for target in range(nb):
            at.part_down[(slot, *bits_of(target, m))] = result[target * down_rows:(target + 1) * down_rows].astype(low)

    def compute_small():
        total = at.small_before[...]
        total = total + jnp.concatenate([at.gain_row[...], jnp.zeros((7, width), jnp.float32)], axis=0)
        at.part_small[...] = jnp.zeros_like(at.part_small)
        for target in range(nb):
            at.part_small[(0, *bits_of(target, m), slice(0, 8), slice(0, rows))] = total[:, target * rows:(target + 1) * rows]

    def compute(piece_of):
        if piece_of.family is wide:
            compute_wide(piece_of.kept_at, piece_of.slot)
        elif piece_of.family is down:
            compute_down(piece_of.kept_at, piece_of.slot)
        else:
            compute_small()
        piece_of.start(0)

    def moves(tick):
        for stage in range(m + n - 1, -1, -1):
            if 0 <= tick - stage < len(pairs):
                for piece_of in pairs[tick - stage]:
                    piece_of.finish(stage)
                    piece_of.start(stage + 1)

    work = AttentionBackward(at, m, piece, 0, 1)
    for pair in pairs[:2]:
        for piece_of in pair:
            compute(piece_of)
    moves(0)
    for piece_of in pairs[2]:
        compute(piece_of)
    ready(loads.metas)
    work.begin()
    ready(loads.heads)
    for group in range(KEY_VALUE_HEADS):
        if group > 0:
            moves(group)
            for piece_of in pairs[group + 2]:
                compute(piece_of)
        work.group(group)
        work.follow(group)
    cosine, sine = at.cosines[...], at.sines[...]
    moves(5)
    compute(pairs[7][0])
    ready(loads.w_query)
    for virtual in range(KEY_VALUE_HEADS, KEY_VALUE_HEADS + m - 1):
        work.follow(virtual)
        if virtual == KEY_VALUE_HEADS:
            work.queries(cosine, sine)
    moves(6)
    ready(loads.rest)
    ready(loads.kv_weight)
    work.keys(cosine, sine)
    compute(pairs[7][1])
    moves(7)
    for piece_of in pairs[8] + pairs[9][:2]:
        compute(piece_of)
    dhidden, gain_share = norm_gradient(at.dnorm[...], at.hid[...], at.norms[0:1, :].astype(jnp.float32))
    at.gain_row[...] = gain_share
    at.grad_out[...] = (at.grad[...] + dhidden).T
    compute(pairs[9][2])
    for tick in range(8, len(pairs) + m + n - 1):
        moves(tick)
    for pair in pairs:
        for piece_of in pair:
            piece_of.finish(m + n)
    for pair in pairs:
        for piece_of in pair:
            piece_of.drained(range(1, m + n + 1))
    work.drained()


def unpack_kernel(sizes, wide_hbm, down_hbm, little_hbm, hidden_in, gradient_in, *refs):
    rows, padded = sizes
    norm_attn, norm_ffn, query, key, value, out, gate, up, down_out, router, hidden, gradient = refs[:12]
    wide, down, little, rest, sems = refs[12:]
    carried = [
        pltpu.make_async_copy(source, target, sems.at[at])
        for at, (source, target) in enumerate(((hidden_in, hidden), (gradient_in, gradient)))
    ]
    loads = [
        pltpu.make_async_copy(source, target, sems.at[2 + at])
        for at, (source, target) in enumerate(((wide_hbm, wide), (down_hbm, down), (little_hbm, little)))
    ]
    for copy in loads + carried:
        copy.start()
    for load in loads:
        load.wait()
    norm_attn[...] = little[0, 0:1, :rows]
    norm_ffn[...] = little[0, 1:2, :rows]
    router[...] = little[0, 2:4, :rows]
    for unit in range(5):
        for first, target in ((0, gate), (5, up), (10, rest)):
            tile = wide[first + unit].astype(jnp.float32)
            for side in range(2):
                column = side * 1280 + unit * UNIT_COLUMNS
                target[:, column:column + UNIT_COLUMNS] = tile[side * padded:side * padded + rows]
        down_rows = down.shape[1]
        down_out[unit * down_rows:(unit + 1) * down_rows, :] = down[unit].astype(jnp.float32)
    width = query.shape[1]
    both = rest[:, :2 * KEYS_WIDTH].T
    for group in range(KEY_VALUE_HEADS):
        here, first = slice(group * HEAD_DIMENSION, (group + 1) * HEAD_DIMENSION), group * PAIR
        key[here, :] = both[first:first + HEAD_DIMENSION]
        value[here, :] = both[first + HEAD_DIMENSION:first + PAIR]
    query[...] = rest[:, 2 * KEYS_WIDTH:2 * KEYS_WIDTH + width]
    out[...] = rest[:, 2 * KEYS_WIDTH + width:]
    for copy in carried:
        copy.wait()


def final(small, saved, top, bottom, weights, mesh_sizes):
    nb, nd = mesh_sizes
    m, n = nb.bit_length() - 1, nd.bit_length() - 1
    grad = bottom["grad_hidden"]
    piece, width = grad.shape
    hidden_units = weights["w_gate_hbm"].shape[1]
    rows = width // nb
    padded = -(-rows // 8) * 8
    down_rows = hidden_units // nb // 5
    tokens = RECUR * piece

    def spread(array):
        if padded == rows:
            return array
        split = array.reshape(RECUR, nb, rows, piece)
        return jnp.pad(split, ((0, 0), (0, 0), (0, padded - rows), (0, 0))).reshape(RECUR, nb * padded, piece)

    inputs = small | dict(small_before=bottom["small"])
    operands = dict(
        metas_hbm=saved["metas"], turned_hbm=saved["turned"], dat_hbm=bottom["dat"], att_hbm=saved["att"],
        lse_hbm=saved["lse"], kv_hbm=saved["kv"], w_query_hbm=weights["w_query_hbm"],
        key_weight_hbm=weights["key_weight_hbm"], value_weight_hbm=weights["value_weight_hbm"], hid_hbm=saved["hid"],
        grad_hbm=grad, inner_hbm=saved["inner"], nffn_hbm=spread(saved["nffn"]), normed_hbm=spread(saved["normed"]),
        attended_hbm=spread(saved["att"]), dffn_0_hbm=bottom["dffn"], dffn_1_hbm=top["dffn"],
        dgate_0_hbm=bottom["dgate_out"], dgate_1_hbm=top["dgate"], dup_0_hbm=bottom["dup_out"], dup_1_hbm=top["dup"],
        far_0_hbm=bottom["far"], far_1_hbm=top["far"], near_1_hbm=bottom["near_out"],
    )
    near_width = bottom["near_out"].shape[1]
    families = (
        ("wide", 15, (2 * padded, UNIT_COLUMNS), low, WIDE_SLOTS, 1), ("down", 5, (down_rows, width), low, DOWN_SLOTS, 0),
        ("small", 1, (16, 128), jnp.float32, 1, 0),
    )
    outs = dict(grad_out=((width, piece), jnp.float32))
    buffers = attention_buffers(nb, piece, width, low) | dict(
        grad=((piece, width), jnp.float32), gate_side=((tokens, hidden_units), low), up_side=((tokens, hidden_units), low),
        inner=((hidden_units, tokens), low), left=((nb * padded, tokens), low), left_attended=((nb * padded, tokens), low),
        dffn=((tokens, width), low), gain_row=((1, width), jnp.float32),
    )
    for name, count, shape, dtype, slots, split in families:
        outs["out_" + name] = ((count, *shape), dtype)
        buffers["part_" + name] = ((slots, *(2,) * m, *shape), dtype)
        for stage in range(m):
            buffers["blk_%s_%d" % (name, stage)] = ((count, *(2,) * (m - 1 - stage), *shape), dtype)
        half = (shape[0], shape[1] // 2) if split else (shape[0] // 2, shape[1])
        for stage in range(n):
            buffers["dp_%s_%d" % (name, stage)] = ((count, *half), dtype)
    sums, hops = (2 * KEY_VALUE_HEADS, m), (21, m + n + 1)
    semaphores = dict(load_sems=(32,), weight_sems=(2 * KEY_VALUE_HEADS,), kv_send=sums, kv_recv=sums, send_sems=hops, recv_sems=hops)
    names = (*inputs, *operands, *outs, *buffers, *semaphores)
    gradient, wide, down, little = pl.pallas_call(
        functools.partial(final_kernel, (nb, m, n, piece, rows, padded, near_width), names),
        out_shape=[shaped(entry) for entry in outs.values()],
        in_specs=[spec(pltpu.VMEM)] * len(inputs) + [spec(pl.ANY)] * len(operands),
        out_specs=[spec(pltpu.VMEM)] * len(outs),
        scratch_shapes=spaces(buffers.values()) + dma_semaphores(*semaphores.values()),
        compiler_params=pltpu.CompilerParams(
            collective_id=0, has_side_effects=True, vmem_limit_bytes=VMEM_LIMIT
        ),
        cost_estimate=pl.CostEstimate(
            flops=2 * tokens * width * 14000, bytes_accessed=30 * 1024 * 1024, transcendentals=0
        ),
        name="weight_grads",
    )(*inputs.values(), *operands.values())
    shapes = (
        (1, rows), (1, rows), (rows, width), (KEYS_WIDTH, rows), (KEYS_WIDTH, rows), (rows, width),
        (rows, hidden_units), (rows, hidden_units), (5 * down_rows, width), (2, rows), (width, piece), (width, piece),
    )
    outs = pl.pallas_call(
        functools.partial(unpack_kernel, (rows, padded)),
        out_shape=[jax.ShapeDtypeStruct(shape, jnp.float32) for shape in shapes],
        in_specs=[spec(pl.ANY)] * 5,
        out_specs=[spec(pltpu.VMEM)] * 12,
        scratch_shapes=[pltpu.VMEM(array.shape, array.dtype) for array in (wide, down, little)]
        + spaces([((rows, 2560), jnp.float32)]) + dma_semaphores((5,)),
        compiler_params=pltpu.CompilerParams(vmem_limit_bytes=VMEM_LIMIT),
        name="unpack",
    )(wide, down, little, saved["hidden_out"], gradient)
    norm_a, norm_f, query, key, value, out, gate, up, down, router, hidden, gradient = outs
    return (
        hidden.T[None], gradient.T[None], norm_a[0], norm_f[0], query, key.T, value.T, out, gate, up, down, router.T,
    )


def local(
    tokens,
    depths,
    segments,
    norm_attn,
    norm_ffn,
    w_query,
    key_weight,
    value_weight,
    w_out,
    w_gate,
    w_up,
    w_down,
    w_router,
    cotangent,
    mesh_sizes,
):
    piece = tokens.shape[1]
    positions = lax.axis_index("blk") * piece + jnp.arange(piece, dtype=jnp.int32)
    angles = frequencies(HEAD_DIMENSION)[:, None] * positions.astype(jnp.float32)[None, :]
    tables = dict(cosines=jnp.cos(angles), sines=jnp.sin(angles), norms=jnp.stack([norm_attn, norm_ffn]))
    routing = dict(router=w_router.T, depths=depths)
    heads = dict(w_query_hbm=w_query, key_weight_hbm=key_weight.T, value_weight_hbm=value_weight.T)
    weights = heads | dict(w_out_hbm=w_out, w_gate_hbm=w_gate, w_up_hbm=w_up, w_down_hbm=w_down.T)
    nb = mesh_sizes[0]
    saved = forward(
        tables | routing | dict(tokens=tokens[0].T, cotangent=cotangent[0].T, segments=segments), weights, nb
    )
    operands = dict(
        metas_hbm=saved["metas"], turned_hbm=saved["turned"], dat_hbm=saved["dat"], att_hbm=saved["att"],
        lse_hbm=saved["lse"], kv_hbm=saved["kv"], grad_hbm=saved["grad_hidden"], hid_1_hbm=saved["hid_1"],
        hid_0_hbm=saved["hid"], branch_hbm=saved["branch"], slope_hbm=saved["slope"], silu_hbm=saved["silu"],
        middle_hbm=saved["middle"],
    )
    bottom = backward(1, tables | routing | dict(small_before=saved["small"]), weights | operands, nb)
    return final(tables, saved, saved, bottom, weights, mesh_sizes)


def solution(mesh):
    sizes = (mesh.shape["blk"], mesh.shape["dp"])
    return jax.shard_map(
        functools.partial(local, mesh_sizes=sizes),
        mesh=mesh,
        in_specs=(
            P("dp", "blk", None),
            P("dp", "blk"),
            P("dp", "blk"),
            P(),
            P(),
            P(),
            P(),
            P(),
            P(),
            P(),
            P(),
            P(),
            P(),
            P("dp", "blk", None),
        ),
        out_specs=(
            P("dp", "blk", None),
            P("dp", "blk", None),
            P("blk"),
            P("blk"),
            P("blk", None),
            P("blk", None),
            P("blk", None),
            P("blk", None),
            P("blk", None),
            P("blk", None),
            P("blk", None),
            P("blk", None),
        ),
        check_vma=False,
    )
```

```python
import functools
import itertools
import math
import types

import jax
import jax.numpy as jnp
from jax import lax
from jax.experimental import pallas as pl
from jax.experimental.pallas import tpu as pltpu
from jax.sharding import PartitionSpec as P

QUERY_HEADS = 15
KEY_VALUE_HEADS = 5
HEAD_DIMENSION = 64
RECUR = 2
HEAD_SHARE = QUERY_HEADS // KEY_VALUE_HEADS
KEYS_WIDTH = KEY_VALUE_HEADS * HEAD_DIMENSION
PAIR = 2 * HEAD_DIMENSION
UNIT_COLUMNS = 256
SPAN = 2
VMEM_LIMIT = 63 * 1024 * 1024

epsilon = 1e-05
masked_score = -1e30
low = jnp.bfloat16


def frequencies(head_size):
    return jnp.exp(
        jnp.arange(head_size // 2, dtype=jnp.float32) * (-2.0 * math.log(10000.0) / head_size)
    )


def rms_scale(values):
    return lax.rsqrt(jnp.mean(values * values, axis=-1, keepdims=True) + epsilon)


def norm_gradient(grad_norm, values, gain):
    scale = rms_scale(values)
    weighted = grad_norm * gain
    grad_values = scale * weighted - values * (scale * scale * scale) * jnp.mean(
        weighted * values, axis=-1, keepdims=True
    )
    return grad_values, jnp.sum(grad_norm * values * scale, axis=0, keepdims=True)


def dot_last(left, right):
    return lax.dot_general(left, right, (((1,), (1,)), ((), ())), preferred_element_type=jnp.float32)


def plain_dot(left, right):
    return jnp.dot(left, right, preferred_element_type=jnp.float32)


def bits_of(number, count):
    return tuple((number >> (count - 1 - at)) & 1 for at in range(count))


def bit_of(position, bit):
    return lax.rem(position // (1 << bit), 2)


def block_bits(block, m):
    return tuple(bit_of(block, bit) for bit in range(m - 1, -1, -1))


def flipped(position, bit):
    return position + (1 << bit) * (1 - 2 * bit_of(position, bit))


def remote(source, target, sems, at, device):
    return pltpu.make_async_remote_copy(
        src_ref=source,
        dst_ref=target,
        send_sem=sems[0].at[at],
        recv_sem=sems[1].at[at],
        device_id=device,
        device_id_type=pl.DeviceIdType.MESH,
    )


def greet(partners):
    barrier = pltpu.get_barrier_semaphore()
    for partner in partners:
        pl.semaphore_signal(barrier, inc=1, device_id=partner, device_id_type=pl.DeviceIdType.MESH)
    pl.semaphore_wait(barrier, len(partners))


def turn_heads(turned, cosine, sine, heads):
    split = turned.reshape(heads, 2, HEAD_DIMENSION // 2, turned.shape[1])
    first, second = split[:, 0], split[:, 1]
    both = jnp.stack([first * cosine - second * sine, second * cosine + first * sine], axis=1)
    return both.reshape(turned.shape)


def turn_back(turned, cosine, sine, heads):
    return turn_heads(turned, cosine, -sine, heads)


def head_rows(group, member):
    head = group * HEAD_SHARE + member
    return pl.ds(pl.multiple_of(head * HEAD_DIMENSION, HEAD_DIMENSION), HEAD_DIMENSION)


def as_column(row):
    wide = jnp.broadcast_to(row.astype(jnp.float32), (8, row.shape[1]))
    return wide.T[:, 0:1]


def key_steps(blk, span):
    return blk // (1 << span) + 1


def fill_bias(bias, metas, query_segments, level, blk, m, piece, span):
    many = 1 << span
    key_at = lax.broadcasted_iota(jnp.int32, (many * piece, piece), 0)
    query_at = lax.broadcasted_iota(jnp.int32, (many * piece, piece), 1)

    @pl.loop(0, key_steps(blk, span))
    def _(step):
        rows = metas[block_bits(step, m - span)].reshape(many, 8, piece)
        columns = jnp.concatenate([rows[block].T for block in range(many)], axis=0)
        live = jnp.where(columns[:, 1:2] > level, columns[:, 0:1], -1.0)
        shift = (blk - many * step) * piece
        allowed = (live == query_segments) & (key_at <= query_at + shift) | (key_at == query_at + shift)
        masked = jnp.where(allowed, 0.0, masked_score).astype(bias.dtype)
        bias[pl.ds(many * step, many)] = masked.reshape(many, piece, piece)


def step_bias(bias, step, piece, span):
    many = 1 << span
    here = bias[pl.ds(many * step, many)].reshape(many * piece, piece).astype(jnp.float32)
    return jnp.concatenate([here] * HEAD_SHARE, axis=1)


def kv_weight_loads(key_hbm, value_hbm, target, sems):
    copies = []
    for group in range(KEY_VALUE_HEADS):
        for side, source in enumerate((key_hbm, value_hbm)):
            rows = pl.ds(group * HEAD_DIMENSION, HEAD_DIMENSION)
            place = pl.ds(group * PAIR + side * HEAD_DIMENSION, HEAD_DIMENSION)
            copies.append(pltpu.make_async_copy(source.at[rows], target.at[place], sems.at[2 * group + side]))
    return copies


def turn_keys(both, cosine, sine):
    half = HEAD_DIMENSION // 2
    split = both.reshape(KEY_VALUE_HEADS, 4, half, both.shape[1])
    first, second = split[:, 0], split[:, 1]
    turned = [first * cosine - second * sine, second * cosine + first * sine, split[:, 2], split[:, 3]]
    return jnp.stack(turned, axis=1).reshape(both.shape)


def spec(memory):
    return pl.BlockSpec(memory_space=memory)


def shaped(entry):
    return jax.ShapeDtypeStruct(*entry)


def spaces(entries):
    return [pltpu.VMEM(*entry) for entry in entries]


def dma_semaphores(*shapes):
    return [pltpu.SemaphoreType.DMA(shape) for shape in shapes]


class Piece:
    def __init__(self, at, kept_at, slot, flavour, family, sems, bits):
        self.at, self.kept_at, self.slot, self.family, self.sems = at, kept_at, slot, family, sems
        self.m, self.n = bits
        left = list(range(self.m - 1, -1, -1))
        self.order = []
        for stage in range(self.m):
            place = len(left) - 1 if stage == 0 or flavour == 0 else 0
            self.order.append((left.pop(place), place, len(left)))
        self.last = self.m + self.n
        self.blk = lax.axis_index("blk")
        self.dp = lax.axis_index("dp") if self.n else None

    def half(self, ref, side):
        rows, columns = self.family.shape
        if self.family.split == 0:
            return ref.at[pl.ds(pl.multiple_of(side * (rows // 2), rows // 2), rows // 2), :]
        return ref.at[:, pl.ds(pl.multiple_of(side * (columns // 2), columns // 2), columns // 2)]

    def held(self, stage):
        if stage == 0:
            return self.family.part, self.slot
        return self.family.blk[stage - 1], self.kept_at

    def copy(self, stage):
        m, family = self.m, self.family
        if stage < m:
            bit, place, others = self.order[stage]
            ref, index = self.held(stage)
            chosen = [slice(None)] * (others + 1)
            chosen[place] = 1 - bit_of(self.blk, bit)
            source = ref.at[(index, *chosen)]
            target = family.blk[stage].at[self.kept_at]
            device = {"blk": flipped(self.blk, bit)}
        elif stage < self.last:
            bit = stage - m
            if bit == 0:
                source = self.half(family.blk[m - 1].at[self.kept_at], 1 - bit_of(self.dp, 0))
            else:
                source = family.dp[bit - 1].at[self.kept_at]
            target = family.dp[bit].at[self.kept_at]
            device = {"dp": flipped(self.dp, bit)}
        else:
            source = self.half(family.out.at[self.kept_at], bit_of(self.dp, 0))
            target = source
            device = {"dp": flipped(self.dp, 0)}
        return remote(source, target, self.sems, (self.at, stage), device)

    def start(self, stage):
        self.copy(stage).start()

    def finish(self, stage):
        m, family = self.m, self.family
        self.copy(stage).wait_recv()
        if stage < m:
            bit, place, others = self.order[stage]
            ref, index = self.held(stage)
            for combo in itertools.product(range(2), repeat=others):
                chosen = list(combo)
                chosen.insert(place, bit_of(self.blk, bit))
                into = family.blk[stage].at[(self.kept_at, *combo)]
                self.add(into, into, ref.at[(index, *chosen)])
            if stage == 0:
                self.copy(0).wait_send()
        elif stage < self.last:
            bit = stage - m
            got = family.dp[bit].at[self.kept_at]
            if bit == 0:
                own = self.half(family.blk[m - 1].at[self.kept_at], bit_of(self.dp, 0))
            else:
                own = family.dp[bit - 1].at[self.kept_at]
            into = got
            if stage == self.last - 1:
                into = self.half(family.out.at[self.kept_at], bit_of(self.dp, 0))
            self.add(into, got, own)

    def add(self, into, left, right):
        into[...] = left[...] + right[...]

    def drained(self, stages):
        for stage in stages:
            self.copy(stage).wait_send()


def feed_forward_backward(at, level, gradient, ready, done):
    column = at.router[level:level + 1, :].astype(jnp.float32)
    active = as_column(at.depths[...]) > float(level)
    hidden = at.hid_level[...]
    chosen = jax.nn.sigmoid(jnp.sum(hidden * column, axis=1, keepdims=True))
    at.dbranch[...] = jnp.where(active, chosen, 0.0) * gradient
    dchosen = jnp.where(active, jnp.sum(gradient * at.branch_level[...], axis=1, keepdims=True), 0.0)
    dlogit = dchosen * chosen * (1.0 - chosen)
    at.small[2 + level:3 + level, :] = jnp.sum(hidden * dlogit, axis=0, keepdims=True)
    at.grad_hidden[...] = gradient + dlogit * column
    at.dffn[...] = at.dbranch[...].astype(low)

    ready(0)
    dinner = plain_dot(at.dffn[...], at.w_down[...])
    at.dgate[...] = (dinner * at.slope_level[...].astype(jnp.float32)).astype(low)
    at.dup[...] = (dinner * at.silu_level[...].astype(jnp.float32)).astype(low)
    done()
    at.dnorm_turned[...] = plain_dot(at.w_gate[...], at.dgate[...].T) + plain_dot(at.w_up[...], at.dup[...].T)
    ready(1)
    dnorm = at.dnorm_turned[...].T
    dmiddle, gain_share = norm_gradient(dnorm, at.middle_level[...], at.norms[1:2, :].astype(jnp.float32))
    at.small[1:2, :] += gain_share
    at.grad_hidden[...] += dmiddle
    dattn = (at.dbranch[...] + dmiddle).astype(low)
    lead = at.far.shape[1] - dattn.shape[1]
    at.far[:, :lead] = jnp.zeros((dattn.shape[0], lead), low)
    at.far[:, lead:] = dattn
    at.dat[...] = plain_dot(at.w_out[...], dattn.T).astype(low)


def forward_kernel(sizes, names, *refs):
    m, piece = sizes
    at = types.SimpleNamespace(**dict(zip(names, refs)))
    blk = lax.axis_index("blk")
    mine = block_bits(blk, m)
    kv, metas = at.kv, at.metas
    weights = (
        (at.w_query_hbm, at.w_query), (at.w_out_hbm, at.w_out), (at.w_gate_hbm, at.w_gate), (at.w_up_hbm, at.w_up), (at.w_down_hbm, at.w_down),
    )
    loads = [pltpu.make_async_copy(*pair, at.load_sems.at[index]) for index, pair in enumerate(weights)]
    kv_loads = kv_weight_loads(at.key_weight_hbm, at.value_weight_hbm, at.kv_weight, at.weight_sems)
    for load in kv_loads + loads:
        load.start()
    saved = (
        (at.normed, at.normed_out), (at.turned, at.turned_out), (kv, at.kv_out), (at.lse, at.lse_out),
        (at.att, at.att_out), (at.nffn, at.nffn_out), (at.inner, at.inner_out),
    )

    def save(index, level):
        return pltpu.make_async_copy(
            saved[index][0].at[level] if index == 2 else saved[index][0], saved[index][1].at[level], at.save_sems.at[index, level]
        )

    first = (
        (at.hid.at[0], at.hid_out), (at.middle, at.middle_out), (at.silu, at.silu_out),
        (at.slope, at.slope_out), (at.branch, at.branch_out), (metas, at.metas_out),
        (at.far, at.far_out), (at.dat, at.dat_out), (at.dffn, at.dffn_out), (at.dgate, at.dgate_out), (at.dup, at.dup_out),
        (at.hid.at[1], at.hid_1_out),
    )
    late = [pltpu.make_async_copy(*pair, at.late_sems.at[index]) for index, pair in enumerate(first)]
    segment_row = at.segments[...].astype(jnp.float32)
    depth_column = as_column(at.depths[...])
    metas[mine] = jnp.concatenate(
        [segment_row, at.depths[...].astype(jnp.float32), jnp.zeros((6, piece), jnp.float32)], axis=0
    )
    greet([{"blk": flipped(blk, bit)} for bit in range(m)])

    def place(known):
        return tuple(slice(None) if bit in known else mine[m - 1 - bit] for bit in range(m - 1, -1, -1))

    orders = (list(range(1, m)), list(range(m - 1, 0, -1)))
    kv_sems = (at.kv_send, at.kv_recv)

    def kv_copies(level, group, stage):
        if stage == m - 1:
            ref = kv.at[(level, group, *place(range(1, m)))]
            return [remote(ref, ref, kv_sems, (level, group, 2 * stage), {"blk": flipped(blk, 0)})]
        copies = []
        for side, order in enumerate(orders):
            rows = pl.ds(side * (piece // 2), piece // 2)
            ref = kv.at[(level, group, *place(order[:stage]), rows)]
            copies.append(remote(ref, ref, kv_sems, (level, group, 2 * stage + side), {"blk": flipped(blk, order[stage])}))
        return copies

    def kv_advance(level, group, stage):
        if stage > 0:
            for copy in kv_copies(level, group, stage - 1):
                copy.wait_recv()
        if stage < m:
            for copy in kv_copies(level, group, stage):
                copy.start()

    def meta_copy(stage):
        bits = list(range(1, m)) + [0]
        ref = metas.at[place(bits[:stage])]
        return remote(ref, ref, (at.meta_send, at.meta_recv), stage, {"blk": flipped(blk, bits[stage])})

    meta_copy(0).start()
    cosine, sine = at.cosines[...], at.sines[...]
    gain_attn, gain_ffn = at.norms[0:1, :].astype(jnp.float32), at.norms[1:2, :].astype(jnp.float32)
    routers = at.router[...].astype(jnp.float32)
    at.hid[0] = at.tokens[...].T.astype(jnp.float32)
    late[0].start()
    at.query_pad[HEAD_DIMENSION:, :] = jnp.zeros_like(at.query_pad[HEAD_DIMENSION:, :])

    @pl.loop(0, RECUR)
    def _(level):
        @pl.when(level > 0)
        def _():
            for index in range(5):
                save(index, 0).wait()

        hidden = at.hid[level]
        at.flat[...] = (hidden * rms_scale(hidden) * gain_attn).astype(low)
        at.normed[...] = at.flat[...].T

        @pl.when(level == 0)
        def _():
            for load in kv_loads:
                load.wait()

        both = turn_keys(plain_dot(at.kv_weight[...], at.normed[...]), cosine, sine).T.astype(low)
        for group in range(KEY_VALUE_HEADS):
            kv[(level, group, *mine)] = both[:, group * PAIR:(group + 1) * PAIR]
            kv_advance(level, group, 0)

        @pl.when(level == 0)
        def _():
            loads[0].wait()
            for stage in range(1, m - 1):
                meta_copy(stage - 1).wait_recv()
                meta_copy(stage).start()

        queries = turn_heads(plain_dot(at.flat[...], at.w_query[...]).T, cosine, sine, QUERY_HEADS)
        at.turned[...] = (queries * HEAD_DIMENSION ** (-0.5)).astype(low)

        @pl.when(level == 0)
        def _():
            for stage in range(max(1, m - 1), m):
                meta_copy(stage - 1).wait_recv()
                meta_copy(stage).start()

        for stage in range(1, m - 1):
            for group in range(KEY_VALUE_HEADS):
                kv_advance(level, group, stage)
        kv_advance(level, 0, m - 1)

        @pl.when(level == 0)
        def _():
            meta_copy(m - 1).wait_recv()
            late[5].start()

        fill_bias(at.bias, metas, segment_row, level.astype(jnp.float32), blk, m, piece, SPAN)

        @pl.loop(0, KEY_VALUE_HEADS)
        def _(group):
            @pl.when(group + 1 < KEY_VALUE_HEADS)
            def _():
                kv_advance(level, group + 1, m - 1)

            kv_advance(level, group, m)
            for member in range(HEAD_SHARE):
                at.query_pad[:HEAD_DIMENSION, member * piece:(member + 1) * piece] = at.turned[head_rows(group, member), :]
            at.top[...] = jnp.full_like(at.top, masked_score)
            at.total[...] = jnp.zeros_like(at.total)

            @pl.loop(0, key_steps(blk, SPAN))
            def _(index):
                step = key_steps(blk, SPAN) - 1 - index
                rows = kv[(level, group, *block_bits(step, m - SPAN))].reshape((1 << SPAN) * piece, PAIR)
                scores = plain_dot(rows, at.query_pad[...]) + step_bias(at.bias, step, piece, SPAN)
                before = at.top[0:1, :]
                after = jnp.maximum(before, jnp.max(scores, axis=0, keepdims=True))
                raised = jnp.exp(scores - after)
                shrink = jnp.exp(before - after)
                at.top[0:1, :] = after
                ones = jnp.ones((16, rows.shape[0]), low)
                left = jnp.concatenate([rows.T[HEAD_DIMENSION:], ones], axis=0)
                at.total[...] = at.total[...] * shrink + plain_dot(left, raised.astype(low))

            sums = at.total[HEAD_DIMENSION:HEAD_DIMENSION + 1, :]
            at.lse[pl.ds(group, 1), :] = at.top[0:1, :] + jnp.log(sums)
            out = at.total[:HEAD_DIMENSION, :] / sums
            for member in range(HEAD_SHARE):
                at.att[head_rows(group, member), :] = out[:, member * piece:(member + 1) * piece].astype(low)

        for index in range(5):
            save(index, level).start()

        @pl.when(level == 0)
        def _():
            loads[1].wait()

        @pl.when(level > 0)
        def _():
            save(5, 0).wait()
            save(6, 0).wait()
            for copy in late[1:5]:
                copy.wait()

        attn = plain_dot(at.att[...].T, at.w_out[...])
        mid = at.hid[level] + attn
        at.middle[...] = mid
        at.branch[...] = attn
        at.flat[...] = (mid * rms_scale(mid) * gain_ffn).astype(low)
        at.nffn[...] = at.flat[...].T
        save(5, level).start()

        @pl.when(level == 0)
        def _():
            loads[2].wait()
            loads[3].wait()

        gate_pre = plain_dot(at.flat[...], at.w_gate[...])
        up_pre = plain_dot(at.flat[...], at.w_up[...])
        opened = jax.nn.sigmoid(gate_pre)
        passed = gate_pre * opened
        at.silu[...] = passed.astype(low)
        at.slope[...] = (up_pre * (opened + passed - passed * opened)).astype(low)
        at.inner[...] = (passed * up_pre).astype(low).T
        save(6, level).start()

        @pl.when(level == 0)
        def _():
            loads[4].wait()

        at.branch[...] += plain_dot(at.w_down[...], at.inner[...]).T
        column = jnp.where(level == 0, routers[0:1, :], routers[1:2, :])
        logit = jnp.sum(at.hid[level] * column, axis=1, keepdims=True)
        weight = jnp.where(depth_column > level.astype(jnp.float32), jax.nn.sigmoid(logit), 0.0)
        at.hid[level + 1] = at.hid[level] + weight * at.branch[...]

        @pl.when(level == 0)
        def _():
            for copy in late[1:5]:
                copy.start()

    at.hidden_out[...] = at.hid[RECUR].T
    top = RECUR - 1
    at.hid_level, at.branch_level, at.middle_level = at.hid.at[top], at.branch, at.middle
    at.silu_level, at.slope_level = at.silu, at.slope
    at.small[...] = jnp.zeros_like(at.small)
    feed_forward_backward(at, top, at.cotangent[...].T.astype(jnp.float32), lambda part: None, lambda: None)
    for copy in late[6:]:
        copy.start()
    for stage in range(m):
        meta_copy(stage).wait_send()
    for level in range(RECUR):
        for group in range(KEY_VALUE_HEADS):
            for stage in range(m):
                for copy in kv_copies(level, group, stage):
                    copy.wait_send()
    for index in range(len(saved)):
        save(index, RECUR - 1).wait()
    for copy in late[:1] + late[5:]:
        copy.wait()


def far_width(width):
    return 2 * width + 2 * KEYS_WIDTH - 1536


def forward(small, weights, nb):
    m = nb.bit_length() - 1
    width, piece = small["tokens"].shape
    hidden_units = weights["w_gate_hbm"].shape[1]
    blocks, wide = (2,) * m, HEAD_SHARE * piece
    rows, turned = ((piece, width), jnp.float32), ((RECUR, width, piece), low)
    hidden = ((piece, hidden_units), low)
    saved = dict(
        normed=turned, turned=turned, kv=((RECUR, KEY_VALUE_HEADS, *blocks, piece, PAIR), low),
        lse=((RECUR, 8, wide), jnp.float32), att=turned, nffn=turned, inner=((RECUR, hidden_units, piece), low),
        metas=((*blocks, 8, piece), jnp.float32), far=((piece, far_width(width)), low), dat=((width, piece), low),
        dffn=((piece, width), low), dgate=hidden, dup=hidden,
    )
    first = dict(hid=rows, middle=rows, silu=hidden, slope=hidden, branch=rows)
    outs = dict(hidden_out=((width, piece), jnp.float32), grad_hidden=rows, small=((8, width), jnp.float32))
    anywhere = {name + "_out": entry for name, entry in (saved | first | dict(hid_1=rows)).items()}
    single = {name: (shape[1:], dtype) for name, (shape, dtype) in saved.items() if shape[0] == RECUR and name not in ("kv", "metas")}
    buffers = {name[:-4]: (array.shape, array.dtype) for name, array in weights.items()} | saved | single | first | dict(
        kv_weight=((2 * KEYS_WIDTH, width), low),
        hid=((RECUR + 1, piece, width), jnp.float32), flat=((piece, width), low),
        bias=((nb, piece, piece), jnp.float32), query_pad=((PAIR, wide), low), top=((8, wide), jnp.float32),
        total=((HEAD_DIMENSION + 16, wide), jnp.float32), dbranch=rows, dnorm_turned=((width, piece), jnp.float32),
    )
    semaphores = dict(
        load_sems=(5,), weight_sems=(2 * KEY_VALUE_HEADS,), save_sems=(7, RECUR), late_sems=(12,), kv_send=(RECUR, KEY_VALUE_HEADS, 2 * m),
        kv_recv=(RECUR, KEY_VALUE_HEADS, 2 * m), meta_send=(m,), meta_recv=(m,),
    )
    results = pl.pallas_call(
        functools.partial(forward_kernel, (m, piece), (*small, *weights, *outs, *anywhere, *buffers, *semaphores)),
        out_shape=[shaped(entry) for entry in (outs | anywhere).values()],
        in_specs=[spec(pltpu.VMEM)] * len(small) + [spec(pl.ANY)] * len(weights),
        out_specs=[spec(pltpu.VMEM)] * len(outs) + [spec(pl.ANY)] * len(anywhere),
        scratch_shapes=spaces(buffers.values()) + dma_semaphores(*semaphores.values()),
        compiler_params=pltpu.CompilerParams(
            collective_id=1, has_side_effects=True, vmem_limit_bytes=VMEM_LIMIT
        ),
        cost_estimate=pl.CostEstimate(
            flops=3 * RECUR * piece * width * 10240, bytes_accessed=48 * 1024 * 1024, transcendentals=0
        ),
        name="forward_levels",
    )(*small.values(), *weights.values())
    return dict(zip((*outs, *(name[:-4] for name in anywhere)), results))


class AttentionBackward:
    def __init__(self, at, m, piece, level, span):
        self.at, self.m, self.piece, self.level, self.span = at, m, piece, level, span
        self.blk = lax.axis_index("blk")
        self.family = types.SimpleNamespace(part=at.part, blk=at.halves, dp=(), out=None, shape=(piece // 2, PAIR), split=0)

    def pieces(self, group):
        sems = (self.at.kv_send, self.at.kv_recv)
        return [
            Piece(2 * group + side, 2 * group + side, 2 * group + side, side, self.family, sems, (self.m, 0))
            for side in range(2)
        ]

    def move(self, group, stage):
        for piece_of in self.pieces(group):
            piece_of.finish(stage)
            if stage + 1 < self.m:
                piece_of.start(stage + 1)

    def begin(self):
        at = self.at
        query_segments = at.metas[block_bits(self.blk, self.m)][0:1, :]
        fill_bias(at.bias, at.metas, query_segments, float(self.level), self.blk, self.m, self.piece, self.span)
        at.query_pad[HEAD_DIMENSION:, :] = jnp.zeros_like(at.query_pad[HEAD_DIMENSION:, :])
        at.dat_pad[:HEAD_DIMENSION, :] = jnp.zeros_like(at.dat_pad[:HEAD_DIMENSION, :])

    def group(self, group):
        at, m, piece, blk = self.at, self.m, self.piece, self.blk
        half = piece // 2
        carried = []
        for member in range(HEAD_SHARE):
            rows, lanes = head_rows(group, member), slice(member * piece, (member + 1) * piece)
            at.query_pad[:HEAD_DIMENSION, lanes] = at.turned[rows, :]
            at.dat_pad[HEAD_DIMENSION:, lanes] = at.dat_turned[rows, :]
            product = at.dat_turned[rows, :].astype(jnp.float32) * at.att_turned[rows, :].astype(jnp.float32)
            carried.append(jnp.sum(product, axis=0, keepdims=True))
        carried = jnp.concatenate(carried, axis=1)
        at.query_rows[...] = at.query_pad[...].T
        at.dat_rows[...] = at.dat_pad[...].T
        log_total = at.lse[pl.ds(group, 1), :]
        at.dq_sum[...] = jnp.zeros_like(at.dq_sum)

        span, lead = self.span, m - self.span

        @pl.loop(0, key_steps(blk, span))
        def _(step):
            rows = at.kv[(group, *block_bits(step, lead))].reshape((1 << span) * piece, PAIR)
            probability = jnp.exp(plain_dot(rows, at.query_pad[...]) + step_bias(at.bias, step, piece, span) - log_total)
            dprob = plain_dot(rows, at.dat_pad[...])
            dscores = (probability * (dprob - carried)).astype(low)
            share = plain_dot(dscores, at.query_rows[...]) + plain_dot(probability.astype(low), at.dat_rows[...])
            share = share.astype(low)
            for block in range(1 << span):
                for side in range(2):
                    first = block * piece + side * half
                    place = (2 * group + side, *block_bits(step, lead), *bits_of(block, span))
                    at.part[place] = share[first:first + half]
            at.dq_sum[...] += plain_dot(rows.T[:HEAD_DIMENSION], dscores)

        @pl.loop(key_steps(blk, span), 1 << lead)
        def _(step):
            for block in range(1 << span):
                for side in range(2):
                    place = (2 * group + side, *block_bits(step, lead), *bits_of(block, span))
                    at.part[place] = jnp.zeros((half, PAIR), low)

        for piece_of in self.pieces(group):
            piece_of.start(0)
        for member in range(HEAD_SHARE):
            at.dq_turned[head_rows(group, member), :] = at.dq_sum[:, member * piece:(member + 1) * piece]

    def follow(self, group):
        for stage in range(self.m - 1):
            earlier = group - 1 - stage
            if isinstance(group, int):
                if 0 <= earlier < KEY_VALUE_HEADS:
                    self.move(earlier, stage)
            else:
                @pl.when(earlier >= 0)
                def _():
                    self.move(earlier, stage)

    def queries(self, cosine, sine):
        at = self.at
        dqueries = turn_back(at.dq_turned[...] * HEAD_DIMENSION ** (-0.5), cosine, sine, QUERY_HEADS).astype(low)
        self.put(2 * KEYS_WIDTH, dqueries.T)
        at.dnorm[...] = plain_dot(at.w_query[...], dqueries).T

    def put(self, column, values):
        self.at.near[:, column:column + values.shape[1]] = values

    def keys(self, cosine, sine):
        at, m = self.at, self.m
        filled = 2 * KEYS_WIDTH + QUERY_HEADS * HEAD_DIMENSION
        self.put(filled, jnp.zeros((self.piece, at.near.shape[1] - filled), low))
        sums = []
        for group in range(KEY_VALUE_HEADS):
            self.move(group, m - 1)
            sums.append(jnp.concatenate([at.halves[m - 1][2 * group], at.halves[m - 1][2 * group + 1]], axis=0))
        both = jnp.concatenate(sums, axis=1).astype(jnp.float32).T
        both = turn_keys(both, cosine, -sine).astype(low).T
        self.put(0, both)
        at.dnorm[...] += plain_dot(both, at.kv_weight[...])

    def drained(self):
        for group in range(KEY_VALUE_HEADS):
            for piece_of in self.pieces(group):
                piece_of.drained(range(1, self.m))


def attention_buffers(nb, piece, width, bias_type):
    m, wide, heads = nb.bit_length() - 1, HEAD_SHARE * piece, 2 * KEY_VALUE_HEADS
    turned = ((width, piece), low)
    pad, pad_rows = ((PAIR, wide), low), ((wide, PAIR), low)
    buffers = dict(
        turned=turned, dat_turned=turned, att_turned=turned, kv=((KEY_VALUE_HEADS, *(2,) * m, piece, PAIR), low),
        lse=((8, wide), jnp.float32), metas=((*(2,) * m, 8, piece), jnp.float32), w_query=((width, width), low),
        kv_weight=((2 * KEYS_WIDTH, width), low), dq_turned=((width, piece), jnp.float32),
        bias=((nb, piece, piece), bias_type), query_pad=pad, dat_pad=pad, query_rows=pad_rows, dat_rows=pad_rows,
        dq_sum=((HEAD_DIMENSION, wide), jnp.float32), part=((heads, *(2,) * m, piece // 2, PAIR), low),
        dnorm=((piece, width), jnp.float32), hid=((piece, width), jnp.float32),
    )
    for stage in range(m):
        buffers["half_%d" % stage] = ((heads, *(2,) * (m - 1 - stage), piece // 2, PAIR), low)
    return buffers


def backward_kernel(sizes, names, *refs):
    m, piece, level = sizes
    at = types.SimpleNamespace(**dict(zip(names, refs)))
    at.halves = [getattr(at, "half_%d" % stage) for stage in range(m)]
    at.near = at.near_out
    blk = lax.axis_index("blk")
    pairs = (
        (at.metas_hbm, at.metas), (at.turned_hbm.at[level], at.turned), (at.dat_hbm, at.dat_turned),
        (at.att_hbm.at[level], at.att_turned), (at.lse_hbm.at[level], at.lse), (at.kv_hbm.at[level], at.kv),
        (at.w_query_hbm, at.w_query),
        (at.grad_hbm, at.grad_hidden), (at.hid_1_hbm, at.hid),
        (at.hid_0_hbm, at.hid_level), (at.branch_hbm, at.branch_level), (at.w_down_hbm, at.w_down),
        (at.slope_hbm, at.slope_level), (at.silu_hbm, at.silu_level), (at.w_gate_hbm, at.w_gate), (at.w_up_hbm, at.w_up),
        (at.middle_hbm, at.middle_level), (at.w_out_hbm, at.w_out),
    )
    loads = [pltpu.make_async_copy(*pair, at.load_sems.at[index]) for index, pair in enumerate(pairs)]
    loads += kv_weight_loads(at.key_weight_hbm, at.value_weight_hbm, at.kv_weight, at.weight_sems)
    for load in loads:
        load.start()
    saves = [
        pltpu.make_async_copy(*pair, at.save_sems.at[index])
        for index, pair in enumerate(((at.dgate, at.dgate_out), (at.dup, at.dup_out)))
    ]
    greet([{"blk": flipped(blk, bit)} for bit in range(m)])
    work = AttentionBackward(at, m, piece, level, SPAN)
    loads[0].wait()
    work.begin()
    for load in loads[1:6]:
        load.wait()

    @pl.loop(0, KEY_VALUE_HEADS)
    def _(group):
        work.group(group)
        work.follow(group)

    cosine, sine = at.cosines[...], at.sines[...]
    for virtual in range(KEY_VALUE_HEADS, KEY_VALUE_HEADS + m - 1):
        work.follow(virtual)
        if virtual == KEY_VALUE_HEADS:
            loads[6].wait()
            work.queries(cosine, sine)
    for load in loads[7:]:
        load.wait()
    work.keys(cosine, sine)
    dhidden, gain_share = norm_gradient(at.dnorm[...], at.hid[...], at.norms[0:1, :].astype(jnp.float32))
    at.small[...] = at.small_before[...]
    at.small[0:1, :] = gain_share
    gradient = at.grad_hidden[...] + dhidden
    at.dnorm[...] = gradient
    feed_forward_backward(at, level - 1, at.dnorm[...], lambda part: None, lambda: [save.start() for save in saves])
    work.drained()
    for save in saves:
        save.wait()


def backward(level, small, operands, nb):
    m = nb.bit_length() - 1
    piece, width = operands["grad_hbm"].shape
    hidden_units = operands["w_gate_hbm"].shape[1]
    rows, flat, hidden = ((piece, width), jnp.float32), ((piece, width), low), ((piece, hidden_units), low)
    outs = dict(
        grad_hidden=rows, small=((8, width), jnp.float32), near_out=((piece, 1792), low), dffn=flat,
        dat=((width, piece), low), far=((piece, far_width(width)), low),
    )
    anywhere = dict(dgate_out=hidden, dup_out=hidden)
    buffers = attention_buffers(nb, piece, width, jnp.float32) | dict(
        hid_level=rows, branch_level=rows, middle_level=rows, w_down=((width, hidden_units), low), slope_level=hidden,
        silu_level=hidden, w_gate=((width, hidden_units), low), w_up=((width, hidden_units), low),
        w_out=((width, width), low), dbranch=rows, dnorm_turned=((width, piece), jnp.float32), dgate=hidden, dup=hidden,
    )
    sums = (2 * KEY_VALUE_HEADS, m)
    semaphores = dict(load_sems=(18,), weight_sems=(2 * KEY_VALUE_HEADS,), save_sems=(2,), kv_send=sums, kv_recv=sums)
    results = pl.pallas_call(
        functools.partial(
            backward_kernel, (m, piece, level), (*small, *operands, *outs, *anywhere, *buffers, *semaphores)
        ),
        out_shape=[shaped(entry) for entry in (outs | anywhere).values()],
        in_specs=[spec(pltpu.VMEM)] * len(small) + [spec(pl.ANY)] * len(operands),
        out_specs=[spec(pltpu.VMEM)] * len(outs) + [spec(pl.ANY)] * len(anywhere),
        scratch_shapes=spaces(buffers.values()) + dma_semaphores(*semaphores.values()),
        compiler_params=pltpu.CompilerParams(
            collective_id=2, has_side_effects=True, vmem_limit_bytes=VMEM_LIMIT
        ),
        cost_estimate=pl.CostEstimate(
            flops=2 * piece * width * 20000, bytes_accessed=32 * 1024 * 1024, transcendentals=0
        ),
        name="backward_level",
    )(*small.values(), *operands.values())
    return dict(zip((*outs, *anywhere), results))


WIDE_SLOTS, DOWN_SLOTS = 4, 2


def final_kernel(sizes, names, *refs):
    nb, m, n, piece, rows, padded, near_width = sizes
    at = types.SimpleNamespace(**dict(zip(names, refs)))
    at.halves = [getattr(at, "half_%d" % stage) for stage in range(m)]
    blk, dp = lax.axis_index("blk"), lax.axis_index("dp")
    at.near = at.gate_side.at[pl.ds(0, piece), pl.ds(0, near_width)]
    counter = itertools.count()

    def load(source, target):
        return pltpu.make_async_copy(source, target, at.load_sems.at[next(counter)])

    def both_lanes(ref, target):
        return [load(ref.at[level], target.at[:, pl.ds(level * piece, piece)]) for level in range(RECUR)]

    def both_rows(low_ref, deep_ref, target, width):
        pairs = ((low_ref, 0), (deep_ref, piece))
        return [load(ref, target.at[pl.ds(first, piece), pl.ds(0, width)]) for ref, first in pairs]

    hidden_units, width = at.gate_side.shape[1], at.dffn.shape[1]
    far_lanes = at.far_0_hbm.shape[1]
    loads = types.SimpleNamespace(
        nffn=both_lanes(at.nffn_hbm, at.left),
        dgate=both_rows(at.dgate_0_hbm, at.dgate_1_hbm, at.gate_side, hidden_units),
        inner=both_lanes(at.inner_hbm, at.inner),
        dffn=both_rows(at.dffn_0_hbm, at.dffn_1_hbm, at.dffn, width),
        metas=[load(at.metas_hbm, at.metas)],
        heads=[
            load(at.turned_hbm.at[0], at.turned), load(at.dat_hbm, at.dat_turned), load(at.att_hbm.at[0], at.att_turned),
            load(at.lse_hbm.at[0], at.lse), load(at.kv_hbm.at[0], at.kv),
        ],
        dup=both_rows(at.dup_0_hbm, at.dup_1_hbm, at.up_side, hidden_units),
        w_query=[load(at.w_query_hbm, at.w_query)],
        rest=[
            load(at.hid_hbm, at.hid), load(at.grad_hbm, at.grad),
        ],
        attended=both_lanes(at.attended_hbm, at.left_attended),
        kv_weight=kv_weight_loads(at.key_weight_hbm, at.value_weight_hbm, at.kv_weight, at.weight_sems),
    )
    late = types.SimpleNamespace(
        near=[load(at.near_1_hbm, at.gate_side.at[pl.ds(piece, piece), pl.ds(0, near_width)])],
        far=both_rows(at.far_0_hbm, at.far_1_hbm, at.up_side, far_lanes),
        normed=both_lanes(at.normed_hbm, at.left),
    )

    def begin(copies):
        for copy in copies:
            copy.start()

    def ready(copies):
        for copy in copies:
            copy.wait()

    for copies in vars(loads).values():
        begin(copies)
    greet([{"blk": flipped(blk, bit)} for bit in range(m)] + [{"dp": flipped(dp, bit)} for bit in range(n)])

    down_rows = at.part_down.shape[-2]

    def family(name, shape, split):
        return types.SimpleNamespace(
            part=getattr(at, "part_" + name), out=getattr(at, "out_" + name), shape=shape, split=split,
            blk=[getattr(at, "blk_%s_%d" % (name, stage)) for stage in range(m)],
            dp=[getattr(at, "dp_%s_%d" % (name, stage)) for stage in range(n)],
        )

    wide = family("wide", (2 * padded, UNIT_COLUMNS), 1)
    down = family("down", (down_rows, width), 0)
    little = family("small", (16, 128), 0)
    sems = (at.send_sems, at.recv_sems)
    units = itertools.count()

    def unit(holder, index, flavour):
        return Piece(next(units), index, index % holder.part.shape[0], flavour, holder, sems, (m, n))

    pairs = [[unit(wide, index, 0), unit(down, index, 1)] for index in range(5)]
    pairs += [[unit(wide, index, 0), unit(wide, index + 1, 1)] for index in (5, 7, 9, 11)]
    pairs += [[unit(wide, 13, 0), unit(wide, 14, 1), unit(little, 0, 0)]]

    def compute_wide(index, slot):
        if index == 0:
            ready(loads.nffn)
            ready(loads.dgate)
        if index == 5:
            begin(late.near)
            ready(loads.dup)
        if index == 10:
            begin(late.far)
            begin(late.normed)
            ready(late.near)
            ready(late.normed)
            ready(loads.attended)
            ready(late.far)
        block, column = index // 5, (index % 5) * UNIT_COLUMNS
        second = 1280 + column
        upper_columns, lower_columns = slice(column, column + UNIT_COLUMNS), slice(second, second + UNIT_COLUMNS)
        if block < 2:
            right = at.gate_side if block == 0 else at.up_side
            upper = plain_dot(at.left[...], right[:, upper_columns])
            lower = plain_dot(at.left[...], right[:, lower_columns])
        else:
            upper = plain_dot(at.left[...], at.gate_side[:, upper_columns])
            lower = None
            if second < 1600:
                lower = plain_dot(at.left[...], at.gate_side[:, lower_columns])
            if second >= 1536:
                more = plain_dot(at.left_attended[...], at.up_side[:, second - 1536:second - 1536 + UNIT_COLUMNS])
                lower = more if lower is None else lower + more
        for target in range(nb):
            here = slice(target * padded, (target + 1) * padded)
            both = jnp.concatenate([upper[here], lower[here]], axis=0)
            at.part_wide[(slot, *bits_of(target, m))] = both.astype(low)

    def compute_down(index, slot):
        if index == 0:
            ready(loads.inner)
            ready(loads.dffn)
        firsts = [(target * 5 + index) * down_rows for target in range(nb)]
        left = jnp.concatenate([at.inner[first:first + down_rows, :] for first in firsts], axis=0)
        result = plain_dot(left, at.dffn[...])
        for target in range(nb):
            at.part_down[(slot, *bits_of(target, m))] = result[target * down_rows:(target + 1) * down_rows].astype(low)

    def compute_small():
        total = at.small_before[...]
        total = total + jnp.concatenate([at.gain_row[...], jnp.zeros((7, width), jnp.float32)], axis=0)
        at.part_small[...] = jnp.zeros_like(at.part_small)
        for target in range(nb):
            at.part_small[(0, *bits_of(target, m), slice(0, 8), slice(0, rows))] = total[:, target * rows:(target + 1) * rows]

    def compute(piece_of):
        if piece_of.family is wide:
            compute_wide(piece_of.kept_at, piece_of.slot)
        elif piece_of.family is down:
            compute_down(piece_of.kept_at, piece_of.slot)
        else:
            compute_small()
        piece_of.start(0)

    def moves(tick):
        for stage in range(m + n - 1, -1, -1):
            if 0 <= tick - stage < len(pairs):
                for piece_of in pairs[tick - stage]:
                    piece_of.finish(stage)
                    piece_of.start(stage + 1)

    work = AttentionBackward(at, m, piece, 0, SPAN)
    for pair in pairs[:2]:
        for piece_of in pair:
            compute(piece_of)
    ready(loads.metas)
    work.begin()
    ready(loads.heads)
    for group in range(KEY_VALUE_HEADS):
        moves(group)
        for piece_of in pairs[group + 2]:
            compute(piece_of)
        work.group(group)
        work.follow(group)
    cosine, sine = at.cosines[...], at.sines[...]
    moves(5)
    compute(pairs[7][0])
    ready(loads.w_query)
    for virtual in range(KEY_VALUE_HEADS, KEY_VALUE_HEADS + m - 1):
        work.follow(virtual)
        if virtual == KEY_VALUE_HEADS:
            work.queries(cosine, sine)
    moves(6)
    ready(loads.rest)
    ready(loads.kv_weight)
    work.keys(cosine, sine)
    compute(pairs[7][1])
    moves(7)
    for piece_of in pairs[8] + pairs[9][:2]:
        compute(piece_of)
    dhidden, gain_share = norm_gradient(at.dnorm[...], at.hid[...], at.norms[0:1, :].astype(jnp.float32))
    at.gain_row[...] = gain_share
    at.grad_out[...] = (at.grad[...] + dhidden).T
    compute(pairs[9][2])
    for tick in range(8, len(pairs) + m + n - 1):
        moves(tick)
    for pair in pairs:
        for piece_of in pair:
            piece_of.finish(m + n)
    for pair in pairs:
        for piece_of in pair:
            piece_of.drained(range(1, m + n + 1))
    work.drained()


def unpack_kernel(sizes, wide_hbm, down_hbm, little_hbm, hidden_in, gradient_in, *refs):
    rows, padded = sizes
    norm_attn, norm_ffn, query, key, value, out, gate, up, down_out, router, hidden, gradient = refs[:12]
    wide, down, little, rest, sems = refs[12:]
    carried = [
        pltpu.make_async_copy(source, target, sems.at[at])
        for at, (source, target) in enumerate(((hidden_in, hidden), (gradient_in, gradient)))
    ]
    loads = [
        pltpu.make_async_copy(source, target, sems.at[2 + at])
        for at, (source, target) in enumerate(((wide_hbm, wide), (down_hbm, down), (little_hbm, little)))
    ]
    for copy in loads + carried:
        copy.start()
    for load in loads:
        load.wait()
    norm_attn[...] = little[0, 0:1, :rows]
    norm_ffn[...] = little[0, 1:2, :rows]
    router[...] = little[0, 2:4, :rows]
    for unit in range(5):
        for first, target in ((0, gate), (5, up), (10, rest)):
            tile = wide[first + unit].astype(jnp.float32)
            for side in range(2):
                column = side * 1280 + unit * UNIT_COLUMNS
                target[:, column:column + UNIT_COLUMNS] = tile[side * padded:side * padded + rows]
        down_rows = down.shape[1]
        down_out[unit * down_rows:(unit + 1) * down_rows, :] = down[unit].astype(jnp.float32)
    width = query.shape[1]
    both = rest[:, :2 * KEYS_WIDTH].T
    for group in range(KEY_VALUE_HEADS):
        here, first = slice(group * HEAD_DIMENSION, (group + 1) * HEAD_DIMENSION), group * PAIR
        key[here, :] = both[first:first + HEAD_DIMENSION]
        value[here, :] = both[first + HEAD_DIMENSION:first + PAIR]
    query[...] = rest[:, 2 * KEYS_WIDTH:2 * KEYS_WIDTH + width]
    out[...] = rest[:, 2 * KEYS_WIDTH + width:]
    for copy in carried:
        copy.wait()


def final(small, saved, top, bottom, weights, mesh_sizes):
    nb, nd = mesh_sizes
    m, n = nb.bit_length() - 1, nd.bit_length() - 1
    grad = bottom["grad_hidden"]
    piece, width = grad.shape
    hidden_units = weights["w_gate_hbm"].shape[1]
    rows = width // nb
    padded = -(-rows // 8) * 8
    down_rows = hidden_units // nb // 5
    tokens = RECUR * piece

    def spread(array):
        if padded == rows:
            return array
        split = array.reshape(RECUR, nb, rows, piece)
        return jnp.pad(split, ((0, 0), (0, 0), (0, padded - rows), (0, 0))).reshape(RECUR, nb * padded, piece)

    inputs = small | dict(small_before=bottom["small"])
    operands = dict(
        metas_hbm=saved["metas"], turned_hbm=saved["turned"], dat_hbm=bottom["dat"], att_hbm=saved["att"],
        lse_hbm=saved["lse"], kv_hbm=saved["kv"], w_query_hbm=weights["w_query_hbm"],
        key_weight_hbm=weights["key_weight_hbm"], value_weight_hbm=weights["value_weight_hbm"], hid_hbm=saved["hid"],
        grad_hbm=grad, inner_hbm=saved["inner"], nffn_hbm=spread(saved["nffn"]), normed_hbm=spread(saved["normed"]),
        attended_hbm=spread(saved["att"]), dffn_0_hbm=bottom["dffn"], dffn_1_hbm=top["dffn"],
        dgate_0_hbm=bottom["dgate_out"], dgate_1_hbm=top["dgate"], dup_0_hbm=bottom["dup_out"], dup_1_hbm=top["dup"],
        far_0_hbm=bottom["far"], far_1_hbm=top["far"], near_1_hbm=bottom["near_out"],
    )
    near_width = bottom["near_out"].shape[1]
    families = (
        ("wide", 15, (2 * padded, UNIT_COLUMNS), low, WIDE_SLOTS, 1), ("down", 5, (down_rows, width), low, DOWN_SLOTS, 0),
        ("small", 1, (16, 128), jnp.float32, 1, 0),
    )
    outs = dict(grad_out=((width, piece), jnp.float32))
    buffers = attention_buffers(nb, piece, width, low) | dict(
        grad=((piece, width), jnp.float32), gate_side=((tokens, hidden_units), low), up_side=((tokens, hidden_units), low),
        inner=((hidden_units, tokens), low), left=((nb * padded, tokens), low), left_attended=((nb * padded, tokens), low),
        dffn=((tokens, width), low), gain_row=((1, width), jnp.float32),
    )
    for name, count, shape, dtype, slots, split in families:
        outs["out_" + name] = ((count, *shape), dtype)
        buffers["part_" + name] = ((slots, *(2,) * m, *shape), dtype)
        for stage in range(m):
            buffers["blk_%s_%d" % (name, stage)] = ((count, *(2,) * (m - 1 - stage), *shape), dtype)
        half = (shape[0], shape[1] // 2) if split else (shape[0] // 2, shape[1])
        for stage in range(n):
            buffers["dp_%s_%d" % (name, stage)] = ((count, *half), dtype)
    sums, hops = (2 * KEY_VALUE_HEADS, m), (21, m + n + 1)
    semaphores = dict(load_sems=(32,), weight_sems=(2 * KEY_VALUE_HEADS,), kv_send=sums, kv_recv=sums, send_sems=hops, recv_sems=hops)
    names = (*inputs, *operands, *outs, *buffers, *semaphores)
    gradient, wide, down, little = pl.pallas_call(
        functools.partial(final_kernel, (nb, m, n, piece, rows, padded, near_width), names),
        out_shape=[shaped(entry) for entry in outs.values()],
        in_specs=[spec(pltpu.VMEM)] * len(inputs) + [spec(pl.ANY)] * len(operands),
        out_specs=[spec(pltpu.VMEM)] * len(outs),
        scratch_shapes=spaces(buffers.values()) + dma_semaphores(*semaphores.values()),
        compiler_params=pltpu.CompilerParams(
            collective_id=0, has_side_effects=True, vmem_limit_bytes=VMEM_LIMIT
        ),
        cost_estimate=pl.CostEstimate(
            flops=2 * tokens * width * 14000, bytes_accessed=30 * 1024 * 1024, transcendentals=0
        ),
        name="weight_grads",
    )(*inputs.values(), *operands.values())
    shapes = (
        (1, rows), (1, rows), (rows, width), (KEYS_WIDTH, rows), (KEYS_WIDTH, rows), (rows, width),
        (rows, hidden_units), (rows, hidden_units), (5 * down_rows, width), (2, rows), (width, piece), (width, piece),
    )
    outs = pl.pallas_call(
        functools.partial(unpack_kernel, (rows, padded)),
        out_shape=[jax.ShapeDtypeStruct(shape, jnp.float32) for shape in shapes],
        in_specs=[spec(pl.ANY)] * 5,
        out_specs=[spec(pltpu.VMEM)] * 12,
        scratch_shapes=[pltpu.VMEM(array.shape, array.dtype) for array in (wide, down, little)]
        + spaces([((rows, 2560), jnp.float32)]) + dma_semaphores((5,)),
        compiler_params=pltpu.CompilerParams(vmem_limit_bytes=VMEM_LIMIT),
        name="unpack",
    )(wide, down, little, saved["hidden_out"], gradient)
    norm_a, norm_f, query, key, value, out, gate, up, down, router, hidden, gradient = outs
    return (
        hidden.T[None], gradient.T[None], norm_a[0], norm_f[0], query, key.T, value.T, out, gate, up, down, router.T,
    )


def local(
    tokens,
    depths,
    segments,
    norm_attn,
    norm_ffn,
    w_query,
    key_weight,
    value_weight,
    w_out,
    w_gate,
    w_up,
    w_down,
    w_router,
    cotangent,
    mesh_sizes,
):
    piece = tokens.shape[1]
    positions = lax.axis_index("blk") * piece + jnp.arange(piece, dtype=jnp.int32)
    angles = frequencies(HEAD_DIMENSION)[:, None] * positions.astype(jnp.float32)[None, :]
    tables = dict(cosines=jnp.cos(angles), sines=jnp.sin(angles), norms=jnp.stack([norm_attn, norm_ffn]))
    routing = dict(router=w_router.T, depths=depths)
    heads = dict(w_query_hbm=w_query, key_weight_hbm=key_weight.T, value_weight_hbm=value_weight.T)
    weights = heads | dict(w_out_hbm=w_out, w_gate_hbm=w_gate, w_up_hbm=w_up, w_down_hbm=w_down.T)
    nb = mesh_sizes[0]
    saved = forward(
        tables | routing | dict(tokens=tokens[0].T, cotangent=cotangent[0].T, segments=segments), weights, nb
    )
    operands = dict(
        metas_hbm=saved["metas"], turned_hbm=saved["turned"], dat_hbm=saved["dat"], att_hbm=saved["att"],
        lse_hbm=saved["lse"], kv_hbm=saved["kv"], grad_hbm=saved["grad_hidden"], hid_1_hbm=saved["hid_1"],
        hid_0_hbm=saved["hid"], branch_hbm=saved["branch"], slope_hbm=saved["slope"], silu_hbm=saved["silu"],
        middle_hbm=saved["middle"],
    )
    bottom = backward(1, tables | routing | dict(small_before=saved["small"]), weights | operands, nb)
    return final(tables, saved, saved, bottom, weights, mesh_sizes)


def solution(mesh):
    sizes = (mesh.shape["blk"], mesh.shape["dp"])
    return jax.shard_map(
        functools.partial(local, mesh_sizes=sizes),
        mesh=mesh,
        in_specs=(
            P("dp", "blk", None),
            P("dp", "blk"),
            P("dp", "blk"),
            P(),
            P(),
            P(),
            P(),
            P(),
            P(),
            P(),
            P(),
            P(),
            P(),
            P("dp", "blk", None),
        ),
        out_specs=(
            P("dp", "blk", None),
            P("dp", "blk", None),
            P("blk"),
            P("blk"),
            P("blk", None),
            P("blk", None),
            P("blk", None),
            P("blk", None),
            P("blk", None),
            P("blk", None),
            P("blk", None),
            P("blk", None),
        ),
        check_vma=False,
    )
```

```python
import functools
import itertools
import math
import types

import jax
import jax.numpy as jnp
from jax import lax
from jax.experimental import pallas as pl
from jax.experimental.pallas import tpu as pltpu
from jax.sharding import PartitionSpec as P

QUERY_HEADS = 15
KEY_VALUE_HEADS = 5
HEAD_DIMENSION = 64
RECUR = 2
HEAD_SHARE = QUERY_HEADS // KEY_VALUE_HEADS
KEYS_WIDTH = KEY_VALUE_HEADS * HEAD_DIMENSION
PAIR = 2 * HEAD_DIMENSION
UNIT_COLUMNS = 256
SPAN = 2
VMEM_LIMIT = 63 * 1024 * 1024

epsilon = 1e-05
masked_score = -1e30
low = jnp.bfloat16


def frequencies(head_size):
    return jnp.exp(
        jnp.arange(head_size // 2, dtype=jnp.float32) * (-2.0 * math.log(10000.0) / head_size)
    )


def rms_scale(values):
    return lax.rsqrt(jnp.mean(values * values, axis=-1, keepdims=True) + epsilon)


def norm_gradient(grad_norm, values, gain):
    scale = rms_scale(values)
    weighted = grad_norm * gain
    grad_values = scale * weighted - values * (scale * scale * scale) * jnp.mean(
        weighted * values, axis=-1, keepdims=True
    )
    return grad_values, jnp.sum(grad_norm * values * scale, axis=0, keepdims=True)


def dot_last(left, right):
    return lax.dot_general(left, right, (((1,), (1,)), ((), ())), preferred_element_type=jnp.float32)


def plain_dot(left, right):
    return jnp.dot(left, right, preferred_element_type=jnp.float32)


def bits_of(number, count):
    return tuple((number >> (count - 1 - at)) & 1 for at in range(count))


def bit_of(position, bit):
    return lax.rem(position // (1 << bit), 2)


def block_bits(block, m):
    return tuple(bit_of(block, bit) for bit in range(m - 1, -1, -1))


def flipped(position, bit):
    return position + (1 << bit) * (1 - 2 * bit_of(position, bit))


def remote(source, target, sems, at, device):
    return pltpu.make_async_remote_copy(
        src_ref=source,
        dst_ref=target,
        send_sem=sems[0].at[at],
        recv_sem=sems[1].at[at],
        device_id=device,
        device_id_type=pl.DeviceIdType.MESH,
    )


def greet(partners):
    barrier = pltpu.get_barrier_semaphore()
    for partner in partners:
        pl.semaphore_signal(barrier, inc=1, device_id=partner, device_id_type=pl.DeviceIdType.MESH)
    pl.semaphore_wait(barrier, len(partners))


def turn_heads(turned, cosine, sine, heads):
    split = turned.reshape(heads, 2, HEAD_DIMENSION // 2, turned.shape[1])
    first, second = split[:, 0], split[:, 1]
    both = jnp.stack([first * cosine - second * sine, second * cosine + first * sine], axis=1)
    return both.reshape(turned.shape)


def turn_back(turned, cosine, sine, heads):
    return turn_heads(turned, cosine, -sine, heads)


def head_rows(group, member):
    head = group * HEAD_SHARE + member
    return pl.ds(pl.multiple_of(head * HEAD_DIMENSION, HEAD_DIMENSION), HEAD_DIMENSION)


def as_column(row):
    wide = jnp.broadcast_to(row.astype(jnp.float32), (8, row.shape[1]))
    return wide.T[:, 0:1]


def key_steps(blk, span):
    return blk // (1 << span) + 1


def fill_bias(bias, metas, query_segments, level, blk, m, piece, span):
    many = 1 << span
    key_at = lax.broadcasted_iota(jnp.int32, (many * piece, piece), 0)
    query_at = lax.broadcasted_iota(jnp.int32, (many * piece, piece), 1)

    @pl.loop(0, key_steps(blk, span))
    def _(step):
        rows = metas[block_bits(step, m - span)].reshape(many, 8, piece)
        columns = jnp.concatenate([rows[block].T for block in range(many)], axis=0)
        live = jnp.where(columns[:, 1:2] > level, columns[:, 0:1], -1.0)
        shift = (blk - many * step) * piece
        allowed = (live == query_segments) & (key_at <= query_at + shift) | (key_at == query_at + shift)
        masked = jnp.where(allowed, 0.0, masked_score).astype(bias.dtype)
        bias[pl.ds(many * step, many)] = masked.reshape(many, piece, piece)


def step_bias(bias, step, piece, span):
    many = 1 << span
    here = bias[pl.ds(many * step, many)].reshape(many * piece, piece).astype(jnp.float32)
    return jnp.concatenate([here] * HEAD_SHARE, axis=1)


def kv_weight_loads(key_hbm, value_hbm, target, sems):
    copies = []
    for group in range(KEY_VALUE_HEADS):
        for side, source in enumerate((key_hbm, value_hbm)):
            rows = pl.ds(group * HEAD_DIMENSION, HEAD_DIMENSION)
            place = pl.ds(group * PAIR + side * HEAD_DIMENSION, HEAD_DIMENSION)
            copies.append(pltpu.make_async_copy(source.at[rows], target.at[place], sems.at[2 * group + side]))
    return copies


def turn_keys(both, cosine, sine):
    half = HEAD_DIMENSION // 2
    split = both.reshape(KEY_VALUE_HEADS, 4, half, both.shape[1])
    first, second = split[:, 0], split[:, 1]
    turned = [first * cosine - second * sine, second * cosine + first * sine, split[:, 2], split[:, 3]]
    return jnp.stack(turned, axis=1).reshape(both.shape)


def spec(memory):
    return pl.BlockSpec(memory_space=memory)


def shaped(entry):
    return jax.ShapeDtypeStruct(*entry)


def spaces(entries):
    return [pltpu.VMEM(*entry) for entry in entries]


def dma_semaphores(*shapes):
    return [pltpu.SemaphoreType.DMA(shape) for shape in shapes]


class Piece:
    def __init__(self, at, kept_at, slot, flavour, family, sems, bits, middle=False):
        self.at, self.kept_at, self.slot, self.family, self.sems = at, kept_at, slot, family, sems
        self.m, self.n = bits
        left = list(range(self.m - 1, -1, -1))
        self.order = []
        for stage in range(self.m):
            place = len(left) - 1 if stage == 0 or flavour == 0 else 0
            self.order.append((left.pop(place), place, len(left)))
        self.last = self.m + self.n
        self.blk = lax.axis_index("blk")
        self.dp = lax.axis_index("dp") if self.n else None
        self.middle = middle
        if middle:
            inner = bit_of(self.dp, 0) != bit_of(self.dp, 1)
            outer = jnp.logical_not(inner)
            self.sends, self.receives = (outer, inner, inner), (inner, inner, outer)

    def half(self, ref, side):
        size = self.family.shape[self.family.split] // 2
        here = pl.ds(0 if isinstance(side, int) else pl.multiple_of(side * size, size), size)
        return ref.at[here, :] if self.family.split == 0 else ref.at[:, here]

    def held(self, stage):
        if stage == 0:
            return self.family.part, self.slot
        return self.family.blk[stage - 1], self.kept_at

    def copy(self, stage):
        m, family = self.m, self.family
        if stage < m:
            bit, place, others = self.order[stage]
            ref, index = self.held(stage)
            chosen = [slice(None)] * (others + 1)
            chosen[place] = 1 - bit_of(self.blk, bit)
            source = ref.at[(index, *chosen)]
            target = family.blk[stage].at[self.kept_at]
            device = {"blk": flipped(self.blk, bit)}
        elif self.middle:
            source, target, device = (
                (family.blk[m - 1], family.dp[0], {"dp": flipped(self.dp, 0)}),
                (family.dp[0], family.dp[1], {"dp": 3 - self.dp}),
                (family.out, family.out, {"dp": flipped(self.dp, 0)}),
            )[stage - m]
            source, target = source.at[self.kept_at], target.at[self.kept_at]
        elif stage < self.last:
            bit = stage - m
            if bit == 0:
                source = self.half(family.blk[m - 1].at[self.kept_at], 1 - bit_of(self.dp, 0))
            else:
                source = self.half(family.dp[bit - 1].at[self.kept_at], 0)
            target = self.half(family.dp[bit].at[self.kept_at], 0)
            device = {"dp": flipped(self.dp, bit)}
        else:
            source = self.half(family.out.at[self.kept_at], bit_of(self.dp, 0))
            target = source
            device = {"dp": flipped(self.dp, 0)}
        return remote(source, target, self.sems, (self.at, stage), device)

    def where(self, roles, stage, body):
        if self.middle and stage >= self.m:
            pl.when(roles[stage - self.m])(body)
        else:
            body()

    def start(self, stage):
        self.where(self.sends if self.middle else None, stage, lambda: self.copy(stage).start())

    def finish(self, stage):
        self.where(self.receives if self.middle else None, stage, lambda: self.receive(stage))

    def receive(self, stage):
        m, family = self.m, self.family
        self.copy(stage).wait_recv()
        if stage < m:
            bit, place, others = self.order[stage]
            ref, index = self.held(stage)
            for combo in itertools.product(range(2), repeat=others):
                chosen = list(combo)
                chosen.insert(place, bit_of(self.blk, bit))
                into = family.blk[stage].at[(self.kept_at, *combo)]
                self.add(into, into, ref.at[(index, *chosen)])
            if stage == 0:
                self.copy(0).wait_send()
        elif stage < self.last and self.middle:
            kept, sums = self.kept_at, family.dp
            if stage == m:
                self.add(sums[0].at[kept], sums[0].at[kept], family.blk[m - 1].at[kept])
            else:
                self.add(family.out.at[kept], sums[0].at[kept], sums[1].at[kept])
        elif stage < self.last:
            bit = stage - m
            got = self.half(family.dp[bit].at[self.kept_at], 0)
            if bit == 0:
                own = self.half(family.blk[m - 1].at[self.kept_at], bit_of(self.dp, 0))
            else:
                own = self.half(family.dp[bit - 1].at[self.kept_at], 0)
            into = got
            if stage == self.last - 1:
                into = self.half(family.out.at[self.kept_at], bit_of(self.dp, 0))
            self.add(into, got, own)

    def add(self, into, left, right):
        into[...] = left[...] + right[...]

    def drained(self, stages):
        for stage in stages:
            self.where(self.sends if self.middle else None, stage, lambda: self.copy(stage).wait_send())


def feed_forward_backward(at, level, gradient, ready, done):
    column = at.router[level:level + 1, :].astype(jnp.float32)
    active = as_column(at.depths[...]) > float(level)
    hidden = at.hid_level[...]
    chosen = jax.nn.sigmoid(jnp.sum(hidden * column, axis=1, keepdims=True))
    at.dbranch[...] = jnp.where(active, chosen, 0.0) * gradient
    dchosen = jnp.where(active, jnp.sum(gradient * at.branch_level[...], axis=1, keepdims=True), 0.0)
    dlogit = dchosen * chosen * (1.0 - chosen)
    at.small[2 + level:3 + level, :] = jnp.sum(hidden * dlogit, axis=0, keepdims=True)
    at.grad_hidden[...] = gradient + dlogit * column
    at.dffn[...] = at.dbranch[...].astype(low)

    ready(0)
    dinner = plain_dot(at.dffn[...], at.w_down[...])
    at.dgate[...] = (dinner * at.slope_level[...].astype(jnp.float32)).astype(low)
    at.dup[...] = (dinner * at.silu_level[...].astype(jnp.float32)).astype(low)
    done()
    at.dnorm_turned[...] = plain_dot(at.w_gate[...], at.dgate[...].T) + plain_dot(at.w_up[...], at.dup[...].T)
    ready(1)
    dnorm = at.dnorm_turned[...].T
    dmiddle, gain_share = norm_gradient(dnorm, at.middle_level[...], at.norms[1:2, :].astype(jnp.float32))
    at.small[1:2, :] += gain_share
    at.grad_hidden[...] += dmiddle
    dattn = (at.dbranch[...] + dmiddle).astype(low)
    lead = at.far.shape[1] - dattn.shape[1]
    at.far[:, :lead] = jnp.zeros((dattn.shape[0], lead), low)
    at.far[:, lead:] = dattn
    at.dat[...] = plain_dot(at.w_out[...], dattn.T).astype(low)


def forward_kernel(sizes, names, *refs):
    m, piece = sizes
    at = types.SimpleNamespace(**dict(zip(names, refs)))
    blk = lax.axis_index("blk")
    mine = block_bits(blk, m)
    kv, metas = at.kv, at.metas
    weights = (
        (at.w_query_hbm, at.w_query), (at.w_out_hbm, at.w_out), (at.w_gate_hbm, at.w_gate), (at.w_up_hbm, at.w_up), (at.w_down_hbm, at.w_down),
    )
    loads = [pltpu.make_async_copy(*pair, at.load_sems.at[index]) for index, pair in enumerate(weights)]
    kv_loads = kv_weight_loads(at.key_weight_hbm, at.value_weight_hbm, at.kv_weight, at.weight_sems)
    for load in kv_loads + loads:
        load.start()
    saved = (
        (at.normed, at.normed_out), (at.turned, at.turned_out), (kv, at.kv_out), (at.lse, at.lse_out),
        (at.att, at.att_out), (at.nffn, at.nffn_out), (at.inner, at.inner_out),
    )

    def save(index, level):
        return pltpu.make_async_copy(
            saved[index][0].at[level] if index == 2 else saved[index][0], saved[index][1].at[level], at.save_sems.at[index, level]
        )

    first = (
        (at.hid.at[0], at.hid_out), (at.middle, at.middle_out), (at.silu, at.silu_out),
        (at.slope, at.slope_out), (at.branch, at.branch_out), (metas, at.metas_out),
        (at.far, at.far_out), (at.dat, at.dat_out), (at.dffn, at.dffn_out), (at.dgate, at.dgate_out), (at.dup, at.dup_out),
        (at.hid.at[1], at.hid_1_out),
    )
    late = [pltpu.make_async_copy(*pair, at.late_sems.at[index]) for index, pair in enumerate(first)]
    segment_row = at.segments[...].astype(jnp.float32)
    depth_column = as_column(at.depths[...])
    metas[mine] = jnp.concatenate(
        [segment_row, at.depths[...].astype(jnp.float32), jnp.zeros((6, piece), jnp.float32)], axis=0
    )
    greet([{"blk": flipped(blk, bit)} for bit in range(m)])

    def place(known):
        return tuple(slice(None) if bit in known else mine[m - 1 - bit] for bit in range(m - 1, -1, -1))

    orders = (list(range(1, m)), list(range(m - 1, 0, -1)))
    kv_sems = (at.kv_send, at.kv_recv)

    def kv_copies(level, group, stage):
        if stage == m - 1:
            ref = kv.at[(level, group, *place(range(1, m)))]
            return [remote(ref, ref, kv_sems, (level, group, 2 * stage), {"blk": flipped(blk, 0)})]
        copies = []
        for side, order in enumerate(orders):
            rows = pl.ds(side * (piece // 2), piece // 2)
            ref = kv.at[(level, group, *place(order[:stage]), rows)]
            copies.append(remote(ref, ref, kv_sems, (level, group, 2 * stage + side), {"blk": flipped(blk, order[stage])}))
        return copies

    def kv_advance(level, group, stage):
        if stage > 0:
            for copy in kv_copies(level, group, stage - 1):
                copy.wait_recv()
        if stage < m:
            for copy in kv_copies(level, group, stage):
                copy.start()

    def meta_copy(stage):
        bits = list(range(1, m)) + [0]
        ref = metas.at[place(bits[:stage])]
        return remote(ref, ref, (at.meta_send, at.meta_recv), stage, {"blk": flipped(blk, bits[stage])})

    meta_copy(0).start()
    cosine, sine = at.cosines[...], at.sines[...]
    gain_attn, gain_ffn = at.norms[0:1, :].astype(jnp.float32), at.norms[1:2, :].astype(jnp.float32)
    routers = at.router[...].astype(jnp.float32)
    at.hid[0] = at.tokens[...].T.astype(jnp.float32)
    late[0].start()
    at.query_pad[HEAD_DIMENSION:, :] = jnp.zeros_like(at.query_pad[HEAD_DIMENSION:, :])

    @pl.loop(0, RECUR)
    def _(level):
        @pl.when(level > 0)
        def _():
            for index in range(5):
                save(index, 0).wait()

        hidden = at.hid[level]
        at.flat[...] = (hidden * rms_scale(hidden) * gain_attn).astype(low)
        at.normed[...] = at.flat[...].T

        @pl.when(level == 0)
        def _():
            for load in kv_loads:
                load.wait()

        both = turn_keys(plain_dot(at.kv_weight[...], at.normed[...]), cosine, sine).T.astype(low)
        for group in range(KEY_VALUE_HEADS):
            kv[(level, group, *mine)] = both[:, group * PAIR:(group + 1) * PAIR]
            kv_advance(level, group, 0)

        @pl.when(level == 0)
        def _():
            loads[0].wait()
            for stage in range(1, m - 1):
                meta_copy(stage - 1).wait_recv()
                meta_copy(stage).start()

        queries = turn_heads(plain_dot(at.flat[...], at.w_query[...]).T, cosine, sine, QUERY_HEADS)
        at.turned[...] = (queries * HEAD_DIMENSION ** (-0.5)).astype(low)

        @pl.when(level == 0)
        def _():
            for stage in range(max(1, m - 1), m):
                meta_copy(stage - 1).wait_recv()
                meta_copy(stage).start()

        for stage in range(1, m - 1):
            for group in range(KEY_VALUE_HEADS):
                kv_advance(level, group, stage)
        kv_advance(level, 0, m - 1)

        @pl.when(level == 0)
        def _():
            meta_copy(m - 1).wait_recv()
            late[5].start()

        fill_bias(at.bias, metas, segment_row, level.astype(jnp.float32), blk, m, piece, SPAN)

        @pl.loop(0, KEY_VALUE_HEADS)
        def _(group):
            @pl.when(group + 1 < KEY_VALUE_HEADS)
            def _():
                kv_advance(level, group + 1, m - 1)

            kv_advance(level, group, m)
            for member in range(HEAD_SHARE):
                at.query_pad[:HEAD_DIMENSION, member * piece:(member + 1) * piece] = at.turned[head_rows(group, member), :]
            at.top[...] = jnp.full_like(at.top, masked_score)
            at.total[...] = jnp.zeros_like(at.total)

            @pl.loop(0, key_steps(blk, SPAN))
            def _(index):
                step = key_steps(blk, SPAN) - 1 - index
                rows = kv[(level, group, *block_bits(step, m - SPAN))].reshape((1 << SPAN) * piece, PAIR)
                scores = plain_dot(rows, at.query_pad[...]) + step_bias(at.bias, step, piece, SPAN)
                before = at.top[0:1, :]
                after = jnp.maximum(before, jnp.max(scores, axis=0, keepdims=True))
                raised = jnp.exp(scores - after)
                shrink = jnp.exp(before - after)
                at.top[0:1, :] = after
                ones = jnp.ones((16, rows.shape[0]), low)
                left = jnp.concatenate([rows.T[HEAD_DIMENSION:], ones], axis=0)
                at.total[...] = at.total[...] * shrink + plain_dot(left, raised.astype(low))

            sums = at.total[HEAD_DIMENSION:HEAD_DIMENSION + 1, :]
            at.lse[pl.ds(group, 1), :] = at.top[0:1, :] + jnp.log(sums)
            out = at.total[:HEAD_DIMENSION, :] / sums
            for member in range(HEAD_SHARE):
                at.att[head_rows(group, member), :] = out[:, member * piece:(member + 1) * piece].astype(low)

        for index in range(5):
            save(index, level).start()

        @pl.when(level == 0)
        def _():
            loads[1].wait()

        @pl.when(level > 0)
        def _():
            save(5, 0).wait()
            save(6, 0).wait()
            for copy in late[1:5]:
                copy.wait()

        attn = plain_dot(at.att[...].T, at.w_out[...])
        mid = at.hid[level] + attn
        at.middle[...] = mid
        at.branch[...] = attn
        at.flat[...] = (mid * rms_scale(mid) * gain_ffn).astype(low)
        at.nffn[...] = at.flat[...].T
        save(5, level).start()

        @pl.when(level == 0)
        def _():
            loads[2].wait()
            loads[3].wait()

        gate_pre = plain_dot(at.flat[...], at.w_gate[...])
        up_pre = plain_dot(at.flat[...], at.w_up[...])
        opened = jax.nn.sigmoid(gate_pre)
        passed = gate_pre * opened
        at.silu[...] = passed.astype(low)
        at.slope[...] = (up_pre * (opened + passed - passed * opened)).astype(low)
        at.inner[...] = (passed * up_pre).astype(low).T
        save(6, level).start()

        @pl.when(level == 0)
        def _():
            loads[4].wait()

        at.branch[...] += plain_dot(at.w_down[...], at.inner[...]).T
        column = jnp.where(level == 0, routers[0:1, :], routers[1:2, :])
        logit = jnp.sum(at.hid[level] * column, axis=1, keepdims=True)
        weight = jnp.where(depth_column > level.astype(jnp.float32), jax.nn.sigmoid(logit), 0.0)
        at.hid[level + 1] = at.hid[level] + weight * at.branch[...]

        @pl.when(level == 0)
        def _():
            for copy in late[1:5]:
                copy.start()

    at.hidden_out[...] = at.hid[RECUR].T
    top = RECUR - 1
    at.hid_level, at.branch_level, at.middle_level = at.hid.at[top], at.branch, at.middle
    at.silu_level, at.slope_level = at.silu, at.slope
    at.small[...] = jnp.zeros_like(at.small)
    feed_forward_backward(at, top, at.cotangent[...].T.astype(jnp.float32), lambda part: None, lambda: None)
    for copy in late[6:]:
        copy.start()
    for stage in range(m):
        meta_copy(stage).wait_send()
    for level in range(RECUR):
        for group in range(KEY_VALUE_HEADS):
            for stage in range(m):
                for copy in kv_copies(level, group, stage):
                    copy.wait_send()
    for index in range(len(saved)):
        save(index, RECUR - 1).wait()
    for copy in late[:1] + late[5:]:
        copy.wait()


def far_width(width):
    return 2 * width + 2 * KEYS_WIDTH - 1536


def forward(small, weights, nb):
    m = nb.bit_length() - 1
    width, piece = small["tokens"].shape
    hidden_units = weights["w_gate_hbm"].shape[1]
    blocks, wide = (2,) * m, HEAD_SHARE * piece
    rows, turned = ((piece, width), jnp.float32), ((RECUR, width, piece), low)
    hidden = ((piece, hidden_units), low)
    saved = dict(
        normed=turned, turned=turned, kv=((RECUR, KEY_VALUE_HEADS, *blocks, piece, PAIR), low),
        lse=((RECUR, 8, wide), jnp.float32), att=turned, nffn=turned, inner=((RECUR, hidden_units, piece), low),
        metas=((*blocks, 8, piece), jnp.float32), far=((piece, far_width(width)), low), dat=((width, piece), low),
        dffn=((piece, width), low), dgate=hidden, dup=hidden,
    )
    first = dict(hid=rows, middle=rows, silu=hidden, slope=hidden, branch=rows)
    outs = dict(hidden_out=((width, piece), jnp.float32), grad_hidden=rows, small=((8, width), jnp.float32))
    anywhere = {name + "_out": entry for name, entry in (saved | first | dict(hid_1=rows)).items()}
    single = {name: (shape[1:], dtype) for name, (shape, dtype) in saved.items() if shape[0] == RECUR and name not in ("kv", "metas")}
    buffers = {name[:-4]: (array.shape, array.dtype) for name, array in weights.items()} | saved | single | first | dict(
        kv_weight=((2 * KEYS_WIDTH, width), low),
        hid=((RECUR + 1, piece, width), jnp.float32), flat=((piece, width), low),
        bias=((nb, piece, piece), jnp.float32), query_pad=((PAIR, wide), low), top=((8, wide), jnp.float32),
        total=((HEAD_DIMENSION + 16, wide), jnp.float32), dbranch=rows, dnorm_turned=((width, piece), jnp.float32),
    )
    semaphores = dict(
        load_sems=(5,), weight_sems=(2 * KEY_VALUE_HEADS,), save_sems=(7, RECUR), late_sems=(12,), kv_send=(RECUR, KEY_VALUE_HEADS, 2 * m),
        kv_recv=(RECUR, KEY_VALUE_HEADS, 2 * m), meta_send=(m,), meta_recv=(m,),
    )
    results = pl.pallas_call(
        functools.partial(forward_kernel, (m, piece), (*small, *weights, *outs, *anywhere, *buffers, *semaphores)),
        out_shape=[shaped(entry) for entry in (outs | anywhere).values()],
        in_specs=[spec(pltpu.VMEM)] * len(small) + [spec(pl.ANY)] * len(weights),
        out_specs=[spec(pltpu.VMEM)] * len(outs) + [spec(pl.ANY)] * len(anywhere),
        scratch_shapes=spaces(buffers.values()) + dma_semaphores(*semaphores.values()),
        compiler_params=pltpu.CompilerParams(
            collective_id=1, has_side_effects=True, vmem_limit_bytes=VMEM_LIMIT
        ),
        cost_estimate=pl.CostEstimate(
            flops=3 * RECUR * piece * width * 10240, bytes_accessed=48 * 1024 * 1024, transcendentals=0
        ),
        name="forward_levels",
    )(*small.values(), *weights.values())
    return dict(zip((*outs, *(name[:-4] for name in anywhere)), results))


class AttentionBackward:
    def __init__(self, at, m, piece, level, span):
        self.at, self.m, self.piece, self.level, self.span = at, m, piece, level, span
        self.blk = lax.axis_index("blk")
        self.family = types.SimpleNamespace(part=at.part, blk=at.halves, dp=(), out=None, shape=(piece // 2, PAIR), split=0)

    def pieces(self, group):
        sems = (self.at.kv_send, self.at.kv_recv)
        return [
            Piece(2 * group + side, 2 * group + side, 2 * group + side, side, self.family, sems, (self.m, 0))
            for side in range(2)
        ]

    def move(self, group, stage):
        for piece_of in self.pieces(group):
            piece_of.finish(stage)
            if stage + 1 < self.m:
                piece_of.start(stage + 1)

    def begin(self):
        at = self.at
        query_segments = at.metas[block_bits(self.blk, self.m)][0:1, :]
        fill_bias(at.bias, at.metas, query_segments, float(self.level), self.blk, self.m, self.piece, self.span)
        at.query_pad[HEAD_DIMENSION:, :] = jnp.zeros_like(at.query_pad[HEAD_DIMENSION:, :])
        at.dat_pad[:HEAD_DIMENSION, :] = jnp.zeros_like(at.dat_pad[:HEAD_DIMENSION, :])

    def group(self, group):
        at, m, piece, blk = self.at, self.m, self.piece, self.blk
        half = piece // 2
        carried = []
        for member in range(HEAD_SHARE):
            rows, lanes = head_rows(group, member), slice(member * piece, (member + 1) * piece)
            at.query_pad[:HEAD_DIMENSION, lanes] = at.turned[rows, :]
            at.dat_pad[HEAD_DIMENSION:, lanes] = at.dat_turned[rows, :]
            product = at.dat_turned[rows, :].astype(jnp.float32) * at.att_turned[rows, :].astype(jnp.float32)
            carried.append(jnp.sum(product, axis=0, keepdims=True))
        carried = jnp.concatenate(carried, axis=1)
        at.query_rows[...] = at.query_pad[...].T
        at.dat_rows[...] = at.dat_pad[...].T
        log_total = at.lse[pl.ds(group, 1), :]
        at.dq_sum[...] = jnp.zeros_like(at.dq_sum)

        span, lead = self.span, m - self.span

        @pl.loop(0, key_steps(blk, span))
        def _(step):
            rows = at.kv[(group, *block_bits(step, lead))].reshape((1 << span) * piece, PAIR)
            probability = jnp.exp(plain_dot(rows, at.query_pad[...]) + step_bias(at.bias, step, piece, span) - log_total)
            dprob = plain_dot(rows, at.dat_pad[...])
            dscores = (probability * (dprob - carried)).astype(low)
            share = plain_dot(dscores, at.query_rows[...]) + plain_dot(probability.astype(low), at.dat_rows[...])
            share = share.astype(low)
            for block in range(1 << span):
                for side in range(2):
                    first = block * piece + side * half
                    place = (2 * group + side, *block_bits(step, lead), *bits_of(block, span))
                    at.part[place] = share[first:first + half]
            at.dq_sum[...] += plain_dot(rows.T[:HEAD_DIMENSION], dscores)

        @pl.loop(key_steps(blk, span), 1 << lead)
        def _(step):
            for block in range(1 << span):
                for side in range(2):
                    place = (2 * group + side, *block_bits(step, lead), *bits_of(block, span))
                    at.part[place] = jnp.zeros((half, PAIR), low)

        for piece_of in self.pieces(group):
            piece_of.start(0)
        for member in range(HEAD_SHARE):
            at.dq_turned[head_rows(group, member), :] = at.dq_sum[:, member * piece:(member + 1) * piece]

    def follow(self, group):
        for stage in range(self.m - 1):
            earlier = group - 1 - stage
            if isinstance(group, int):
                if 0 <= earlier < KEY_VALUE_HEADS:
                    self.move(earlier, stage)
            else:
                @pl.when(earlier >= 0)
                def _():
                    self.move(earlier, stage)

    def queries(self, cosine, sine):
        at = self.at
        dqueries = turn_back(at.dq_turned[...] * HEAD_DIMENSION ** (-0.5), cosine, sine, QUERY_HEADS).astype(low)
        self.put(2 * KEYS_WIDTH, dqueries.T)
        at.dnorm[...] = plain_dot(at.w_query[...], dqueries).T

    def put(self, column, values):
        self.at.near[:, column:column + values.shape[1]] = values

    def keys(self, cosine, sine):
        at, m = self.at, self.m
        filled = 2 * KEYS_WIDTH + QUERY_HEADS * HEAD_DIMENSION
        self.put(filled, jnp.zeros((self.piece, at.near.shape[1] - filled), low))
        sums = []
        for group in range(KEY_VALUE_HEADS):
            self.move(group, m - 1)
            sums.append(jnp.concatenate([at.halves[m - 1][2 * group], at.halves[m - 1][2 * group + 1]], axis=0))
        both = jnp.concatenate(sums, axis=1).astype(jnp.float32).T
        both = turn_keys(both, cosine, -sine).astype(low).T
        self.put(0, both)
        at.dnorm[...] += plain_dot(both, at.kv_weight[...])

    def drained(self):
        for group in range(KEY_VALUE_HEADS):
            for piece_of in self.pieces(group):
                piece_of.drained(range(1, self.m))


def attention_buffers(nb, piece, width, bias_type):
    m, wide, heads = nb.bit_length() - 1, HEAD_SHARE * piece, 2 * KEY_VALUE_HEADS
    turned = ((width, piece), low)
    pad, pad_rows = ((PAIR, wide), low), ((wide, PAIR), low)
    buffers = dict(
        turned=turned, dat_turned=turned, att_turned=turned, kv=((KEY_VALUE_HEADS, *(2,) * m, piece, PAIR), low),
        lse=((8, wide), jnp.float32), metas=((*(2,) * m, 8, piece), jnp.float32), w_query=((width, width), low),
        kv_weight=((2 * KEYS_WIDTH, width), low), dq_turned=((width, piece), jnp.float32),
        bias=((nb, piece, piece), bias_type), query_pad=pad, dat_pad=pad, query_rows=pad_rows, dat_rows=pad_rows,
        dq_sum=((HEAD_DIMENSION, wide), jnp.float32), part=((heads, *(2,) * m, piece // 2, PAIR), low),
        dnorm=((piece, width), jnp.float32), hid=((piece, width), jnp.float32),
    )
    for stage in range(m):
        buffers["half_%d" % stage] = ((heads, *(2,) * (m - 1 - stage), piece // 2, PAIR), low)
    return buffers


def backward_kernel(sizes, names, *refs):
    m, piece, level = sizes
    at = types.SimpleNamespace(**dict(zip(names, refs)))
    at.halves = [getattr(at, "half_%d" % stage) for stage in range(m)]
    at.near = at.near_out
    blk = lax.axis_index("blk")
    pairs = (
        (at.metas_hbm, at.metas), (at.turned_hbm.at[level], at.turned), (at.dat_hbm, at.dat_turned),
        (at.att_hbm.at[level], at.att_turned), (at.lse_hbm.at[level], at.lse), (at.kv_hbm.at[level], at.kv),
        (at.w_query_hbm, at.w_query),
        (at.grad_hbm, at.grad_hidden), (at.hid_1_hbm, at.hid),
        (at.hid_0_hbm, at.hid_level), (at.branch_hbm, at.branch_level), (at.w_down_hbm, at.w_down),
        (at.slope_hbm, at.slope_level), (at.silu_hbm, at.silu_level), (at.w_gate_hbm, at.w_gate), (at.w_up_hbm, at.w_up),
        (at.middle_hbm, at.middle_level), (at.w_out_hbm, at.w_out),
    )
    loads = [pltpu.make_async_copy(*pair, at.load_sems.at[index]) for index, pair in enumerate(pairs)]
    loads += kv_weight_loads(at.key_weight_hbm, at.value_weight_hbm, at.kv_weight, at.weight_sems)
    for load in loads:
        load.start()
    saves = [
        pltpu.make_async_copy(*pair, at.save_sems.at[index])
        for index, pair in enumerate(((at.dgate, at.dgate_out), (at.dup, at.dup_out)))
    ]
    greet([{"blk": flipped(blk, bit)} for bit in range(m)])
    work = AttentionBackward(at, m, piece, level, SPAN)
    loads[0].wait()
    work.begin()
    for load in loads[1:6]:
        load.wait()

    @pl.loop(0, KEY_VALUE_HEADS)
    def _(group):
        work.group(group)
        work.follow(group)

    cosine, sine = at.cosines[...], at.sines[...]
    for virtual in range(KEY_VALUE_HEADS, KEY_VALUE_HEADS + m - 1):
        work.follow(virtual)
        if virtual == KEY_VALUE_HEADS:
            loads[6].wait()
            work.queries(cosine, sine)
    for load in loads[7:]:
        load.wait()
    work.keys(cosine, sine)
    dhidden, gain_share = norm_gradient(at.dnorm[...], at.hid[...], at.norms[0:1, :].astype(jnp.float32))
    at.small[...] = at.small_before[...]
    at.small[0:1, :] = gain_share
    gradient = at.grad_hidden[...] + dhidden
    at.dnorm[...] = gradient
    feed_forward_backward(at, level - 1, at.dnorm[...], lambda part: None, lambda: [save.start() for save in saves])
    work.drained()
    for save in saves:
        save.wait()


def backward(level, small, operands, nb):
    m = nb.bit_length() - 1
    piece, width = operands["grad_hbm"].shape
    hidden_units = operands["w_gate_hbm"].shape[1]
    rows, flat, hidden = ((piece, width), jnp.float32), ((piece, width), low), ((piece, hidden_units), low)
    outs = dict(
        grad_hidden=rows, small=((8, width), jnp.float32), near_out=((piece, 1792), low), dffn=flat,
        dat=((width, piece), low), far=((piece, far_width(width)), low),
    )
    anywhere = dict(dgate_out=hidden, dup_out=hidden)
    buffers = attention_buffers(nb, piece, width, jnp.float32) | dict(
        hid_level=rows, branch_level=rows, middle_level=rows, w_down=((width, hidden_units), low), slope_level=hidden,
        silu_level=hidden, w_gate=((width, hidden_units), low), w_up=((width, hidden_units), low),
        w_out=((width, width), low), dbranch=rows, dnorm_turned=((width, piece), jnp.float32), dgate=hidden, dup=hidden,
    )
    sums = (2 * KEY_VALUE_HEADS, m)
    semaphores = dict(load_sems=(18,), weight_sems=(2 * KEY_VALUE_HEADS,), save_sems=(2,), kv_send=sums, kv_recv=sums)
    results = pl.pallas_call(
        functools.partial(
            backward_kernel, (m, piece, level), (*small, *operands, *outs, *anywhere, *buffers, *semaphores)
        ),
        out_shape=[shaped(entry) for entry in (outs | anywhere).values()],
        in_specs=[spec(pltpu.VMEM)] * len(small) + [spec(pl.ANY)] * len(operands),
        out_specs=[spec(pltpu.VMEM)] * len(outs) + [spec(pl.ANY)] * len(anywhere),
        scratch_shapes=spaces(buffers.values()) + dma_semaphores(*semaphores.values()),
        compiler_params=pltpu.CompilerParams(
            collective_id=2, has_side_effects=True, vmem_limit_bytes=VMEM_LIMIT
        ),
        cost_estimate=pl.CostEstimate(
            flops=2 * piece * width * 20000, bytes_accessed=32 * 1024 * 1024, transcendentals=0
        ),
        name="backward_level",
    )(*small.values(), *operands.values())
    return dict(zip((*outs, *anywhere), results))


WIDE_SLOTS, DOWN_SLOTS = 4, 2


def final_kernel(sizes, names, *refs):
    nb, m, n, piece, rows, padded, near_width = sizes
    at = types.SimpleNamespace(**dict(zip(names, refs)))
    at.halves = [getattr(at, "half_%d" % stage) for stage in range(m)]
    blk, dp = lax.axis_index("blk"), lax.axis_index("dp")
    at.near = at.gate_side.at[pl.ds(0, piece), pl.ds(0, near_width)]
    counter = itertools.count()

    def load(source, target):
        return pltpu.make_async_copy(source, target, at.load_sems.at[next(counter)])

    def both_lanes(ref, target):
        return [load(ref.at[level], target.at[:, pl.ds(level * piece, piece)]) for level in range(RECUR)]

    def both_rows(low_ref, deep_ref, target, width):
        pairs = ((low_ref, 0), (deep_ref, piece))
        return [load(ref, target.at[pl.ds(first, piece), pl.ds(0, width)]) for ref, first in pairs]

    hidden_units, width = at.gate_side.shape[1], at.dffn.shape[1]
    far_lanes = at.far_0_hbm.shape[1]
    loads = types.SimpleNamespace(
        nffn=both_lanes(at.nffn_hbm, at.left),
        dgate=both_rows(at.dgate_0_hbm, at.dgate_1_hbm, at.gate_side, hidden_units),
        inner=both_lanes(at.inner_hbm, at.inner),
        dffn=both_rows(at.dffn_0_hbm, at.dffn_1_hbm, at.dffn, width),
        metas=[load(at.metas_hbm, at.metas)],
        heads=[
            load(at.turned_hbm.at[0], at.turned), load(at.dat_hbm, at.dat_turned), load(at.att_hbm.at[0], at.att_turned),
            load(at.lse_hbm.at[0], at.lse), load(at.kv_hbm.at[0], at.kv),
        ],
        dup=both_rows(at.dup_0_hbm, at.dup_1_hbm, at.up_side, hidden_units),
        w_query=[load(at.w_query_hbm, at.w_query)],
        rest=[
            load(at.hid_hbm, at.hid), load(at.grad_hbm, at.grad),
        ],
        attended=both_lanes(at.attended_hbm, at.left_attended),
        kv_weight=kv_weight_loads(at.key_weight_hbm, at.value_weight_hbm, at.kv_weight, at.weight_sems),
    )
    late = types.SimpleNamespace(
        near=[load(at.near_1_hbm, at.gate_side.at[pl.ds(piece, piece), pl.ds(0, near_width)])],
        far=both_rows(at.far_0_hbm, at.far_1_hbm, at.up_side, far_lanes),
        normed=both_lanes(at.normed_hbm, at.left),
    )

    def begin(copies):
        for copy in copies:
            copy.start()

    def ready(copies):
        for copy in copies:
            copy.wait()

    for copies in vars(loads).values():
        begin(copies)
    greet([{"blk": flipped(blk, bit)} for bit in range(m)] + [{"dp": flipped(dp, bit)} for bit in range(n)])

    down_rows = at.part_down.shape[-2]

    def family(name, shape, split):
        return types.SimpleNamespace(
            part=getattr(at, "part_" + name), out=getattr(at, "out_" + name), shape=shape, split=split,
            blk=[getattr(at, "blk_%s_%d" % (name, stage)) for stage in range(m)],
            dp=[getattr(at, "dp_%s_%d" % (name, stage)) for stage in range(n)],
        )

    wide = family("wide", (2 * padded, UNIT_COLUMNS), 1)
    down = family("down", (down_rows, width), 0)
    little = family("small", (16, 128), 0)
    sems = (at.send_sems, at.recv_sems)
    units = itertools.count()

    def unit(holder, index, flavour, halves=n != 2):
        return Piece(next(units), index, index % holder.part.shape[0], flavour, holder, sems, (m, n), not halves)

    pairs = [[unit(wide, index, 0), unit(down, index, 1)] for index in range(5)]
    pairs += [[unit(wide, index, 0), unit(wide, index + 1, 1)] for index in (5, 7, 9)]
    pairs += [[unit(wide, 11, 0, True), unit(wide, 12, 1, True)]]
    pairs += [[unit(wide, 13, 0, True), unit(wide, 14, 1, True), unit(little, 0, 0, True)]]

    def compute_wide(index, slot):
        if index == 0:
            ready(loads.nffn)
            ready(loads.dgate)
        if index == 5:
            begin(late.near)
            ready(loads.dup)
        if index == 10:
            begin(late.far)
            begin(late.normed)
            ready(late.near)
            ready(late.normed)
            ready(loads.attended)
            ready(late.far)
        block, column = index // 5, (index % 5) * UNIT_COLUMNS
        second = 1280 + column
        upper_columns, lower_columns = slice(column, column + UNIT_COLUMNS), slice(second, second + UNIT_COLUMNS)
        if block < 2:
            right = at.gate_side if block == 0 else at.up_side
            upper = plain_dot(at.left[...], right[:, upper_columns])
            lower = plain_dot(at.left[...], right[:, lower_columns])
        else:
            upper = plain_dot(at.left[...], at.gate_side[:, upper_columns])
            lower = None
            if second < 1600:
                lower = plain_dot(at.left[...], at.gate_side[:, lower_columns])
            if second >= 1536:
                more = plain_dot(at.left_attended[...], at.up_side[:, second - 1536:second - 1536 + UNIT_COLUMNS])
                lower = more if lower is None else lower + more
        for target in range(nb):
            here = slice(target * padded, (target + 1) * padded)
            both = jnp.concatenate([upper[here], lower[here]], axis=0)
            at.part_wide[(slot, *bits_of(target, m))] = both.astype(low)

    def compute_down(index, slot):
        if index == 0:
            ready(loads.inner)
            ready(loads.dffn)
        firsts = [(target * 5 + index) * down_rows for target in range(nb)]
        left = jnp.concatenate([at.inner[first:first + down_rows, :] for first in firsts], axis=0)
        result = plain_dot(left, at.dffn[...])
        for target in range(nb):
            at.part_down[(slot, *bits_of(target, m))] = result[target * down_rows:(target + 1) * down_rows].astype(low)

    def compute_small():
        total = at.small_before[...]
        total = total + jnp.concatenate([at.gain_row[...], jnp.zeros((7, width), jnp.float32)], axis=0)
        at.part_small[...] = jnp.zeros_like(at.part_small)
        for target in range(nb):
            at.part_small[(0, *bits_of(target, m), slice(0, 8), slice(0, rows))] = total[:, target * rows:(target + 1) * rows]

    def compute(piece_of):
        if piece_of.family is wide:
            compute_wide(piece_of.kept_at, piece_of.slot)
        elif piece_of.family is down:
            compute_down(piece_of.kept_at, piece_of.slot)
        else:
            compute_small()
        piece_of.start(0)

    def moves(tick):
        for stage in range(m + n - 1, -1, -1):
            if 0 <= tick - stage < len(pairs):
                for piece_of in pairs[tick - stage]:
                    piece_of.finish(stage)
                    piece_of.start(stage + 1)

    work = AttentionBackward(at, m, piece, 0, 1)
    for pair in pairs[:2]:
        for piece_of in pair:
            compute(piece_of)
    ready(loads.metas)
    work.begin()
    ready(loads.heads)
    for group in range(KEY_VALUE_HEADS):
        moves(group)
        for piece_of in pairs[group + 2]:
            compute(piece_of)
        work.group(group)
        work.follow(group)
    cosine, sine = at.cosines[...], at.sines[...]
    moves(5)
    compute(pairs[7][0])
    ready(loads.w_query)
    for virtual in range(KEY_VALUE_HEADS, KEY_VALUE_HEADS + m - 1):
        work.follow(virtual)
        if virtual == KEY_VALUE_HEADS:
            work.queries(cosine, sine)
    moves(6)
    ready(loads.rest)
    ready(loads.kv_weight)
    work.keys(cosine, sine)
    compute(pairs[7][1])
    moves(7)
    for piece_of in pairs[8] + pairs[9][:2]:
        compute(piece_of)
    dhidden, gain_share = norm_gradient(at.dnorm[...], at.hid[...], at.norms[0:1, :].astype(jnp.float32))
    at.gain_row[...] = gain_share
    at.grad_out[...] = (at.grad[...] + dhidden).T
    compute(pairs[9][2])
    for tick in range(8, len(pairs) + m + n - 1):
        moves(tick)
    for pair in pairs:
        for piece_of in pair:
            piece_of.finish(m + n)
    for pair in pairs:
        for piece_of in pair:
            piece_of.drained(range(1, m + n + 1))
    work.drained()


def unpack_kernel(sizes, wide_hbm, down_hbm, little_hbm, hidden_in, gradient_in, *refs):
    rows, padded = sizes
    norm_attn, norm_ffn, query, key, value, out, gate, up, down_out, router, hidden, gradient = refs[:12]
    wide, down, little, rest, sems = refs[12:]
    carried = [
        pltpu.make_async_copy(source, target, sems.at[at])
        for at, (source, target) in enumerate(((hidden_in, hidden), (gradient_in, gradient)))
    ]
    loads = [
        pltpu.make_async_copy(source, target, sems.at[2 + at])
        for at, (source, target) in enumerate(((wide_hbm, wide), (down_hbm, down), (little_hbm, little)))
    ]
    for copy in loads + carried:
        copy.start()
    for load in loads:
        load.wait()
    norm_attn[...] = little[0, 0:1, :rows]
    norm_ffn[...] = little[0, 1:2, :rows]
    router[...] = little[0, 2:4, :rows]
    for unit in range(5):
        for first, target in ((0, gate), (5, up), (10, rest)):
            tile = wide[first + unit].astype(jnp.float32)
            for side in range(2):
                column = side * 1280 + unit * UNIT_COLUMNS
                target[:, column:column + UNIT_COLUMNS] = tile[side * padded:side * padded + rows]
        down_rows = down.shape[1]
        down_out[unit * down_rows:(unit + 1) * down_rows, :] = down[unit].astype(jnp.float32)
    width = query.shape[1]
    both = rest[:, :2 * KEYS_WIDTH].T
    for group in range(KEY_VALUE_HEADS):
        here, first = slice(group * HEAD_DIMENSION, (group + 1) * HEAD_DIMENSION), group * PAIR
        key[here, :] = both[first:first + HEAD_DIMENSION]
        value[here, :] = both[first + HEAD_DIMENSION:first + PAIR]
    query[...] = rest[:, 2 * KEYS_WIDTH:2 * KEYS_WIDTH + width]
    out[...] = rest[:, 2 * KEYS_WIDTH + width:]
    for copy in carried:
        copy.wait()


def final(small, saved, top, bottom, weights, mesh_sizes):
    nb, nd = mesh_sizes
    m, n = nb.bit_length() - 1, nd.bit_length() - 1
    grad = bottom["grad_hidden"]
    piece, width = grad.shape
    hidden_units = weights["w_gate_hbm"].shape[1]
    rows = width // nb
    padded = -(-rows // 8) * 8
    down_rows = hidden_units // nb // 5
    tokens = RECUR * piece

    def spread(array):
        if padded == rows:
            return array
        split = array.reshape(RECUR, nb, rows, piece)
        return jnp.pad(split, ((0, 0), (0, 0), (0, padded - rows), (0, 0))).reshape(RECUR, nb * padded, piece)

    inputs = small | dict(small_before=bottom["small"])
    operands = dict(
        metas_hbm=saved["metas"], turned_hbm=saved["turned"], dat_hbm=bottom["dat"], att_hbm=saved["att"],
        lse_hbm=saved["lse"], kv_hbm=saved["kv"], w_query_hbm=weights["w_query_hbm"],
        key_weight_hbm=weights["key_weight_hbm"], value_weight_hbm=weights["value_weight_hbm"], hid_hbm=saved["hid"],
        grad_hbm=grad, inner_hbm=saved["inner"], nffn_hbm=spread(saved["nffn"]), normed_hbm=spread(saved["normed"]),
        attended_hbm=spread(saved["att"]), dffn_0_hbm=bottom["dffn"], dffn_1_hbm=top["dffn"],
        dgate_0_hbm=bottom["dgate_out"], dgate_1_hbm=top["dgate"], dup_0_hbm=bottom["dup_out"], dup_1_hbm=top["dup"],
        far_0_hbm=bottom["far"], far_1_hbm=top["far"], near_1_hbm=bottom["near_out"],
    )
    near_width = bottom["near_out"].shape[1]
    families = (
        ("wide", 15, (2 * padded, UNIT_COLUMNS), low, WIDE_SLOTS, 1), ("down", 5, (down_rows, width), low, DOWN_SLOTS, 0),
        ("small", 1, (16, 128), jnp.float32, 1, 0),
    )
    outs = dict(grad_out=((width, piece), jnp.float32))
    buffers = attention_buffers(nb, piece, width, low) | dict(
        grad=((piece, width), jnp.float32), gate_side=((tokens, hidden_units), low), up_side=((tokens, hidden_units), low),
        inner=((hidden_units, tokens), low), left=((nb * padded, tokens), low), left_attended=((nb * padded, tokens), low),
        dffn=((tokens, width), low), gain_row=((1, width), jnp.float32),
    )
    for name, count, shape, dtype, slots, split in families:
        outs["out_" + name] = ((count, *shape), dtype)
        buffers["part_" + name] = ((slots, *(2,) * m, *shape), dtype)
        for stage in range(m):
            buffers["blk_%s_%d" % (name, stage)] = ((count, *(2,) * (m - 1 - stage), *shape), dtype)
        for stage in range(n):
            buffers["dp_%s_%d" % (name, stage)] = ((count, *shape), dtype)
    sums, hops = (2 * KEY_VALUE_HEADS, m), (21, m + n + 1)
    semaphores = dict(load_sems=(32,), weight_sems=(2 * KEY_VALUE_HEADS,), kv_send=sums, kv_recv=sums, send_sems=hops, recv_sems=hops)
    names = (*inputs, *operands, *outs, *buffers, *semaphores)
    gradient, wide, down, little = pl.pallas_call(
        functools.partial(final_kernel, (nb, m, n, piece, rows, padded, near_width), names),
        out_shape=[shaped(entry) for entry in outs.values()],
        in_specs=[spec(pltpu.VMEM)] * len(inputs) + [spec(pl.ANY)] * len(operands),
        out_specs=[spec(pltpu.VMEM)] * len(outs),
        scratch_shapes=spaces(buffers.values()) + dma_semaphores(*semaphores.values()),
        compiler_params=pltpu.CompilerParams(
            collective_id=0, has_side_effects=True, vmem_limit_bytes=VMEM_LIMIT
        ),
        cost_estimate=pl.CostEstimate(
            flops=2 * tokens * width * 14000, bytes_accessed=30 * 1024 * 1024, transcendentals=0
        ),
        name="weight_grads",
    )(*inputs.values(), *operands.values())
    shapes = (
        (1, rows), (1, rows), (rows, width), (KEYS_WIDTH, rows), (KEYS_WIDTH, rows), (rows, width),
        (rows, hidden_units), (rows, hidden_units), (5 * down_rows, width), (2, rows), (width, piece), (width, piece),
    )
    outs = pl.pallas_call(
        functools.partial(unpack_kernel, (rows, padded)),
        out_shape=[jax.ShapeDtypeStruct(shape, jnp.float32) for shape in shapes],
        in_specs=[spec(pl.ANY)] * 5,
        out_specs=[spec(pltpu.VMEM)] * 12,
        scratch_shapes=[pltpu.VMEM(array.shape, array.dtype) for array in (wide, down, little)]
        + spaces([((rows, 2560), jnp.float32)]) + dma_semaphores((5,)),
        compiler_params=pltpu.CompilerParams(vmem_limit_bytes=VMEM_LIMIT),
        name="unpack",
    )(wide, down, little, saved["hidden_out"], gradient)
    norm_a, norm_f, query, key, value, out, gate, up, down, router, hidden, gradient = outs
    return (
        hidden.T[None], gradient.T[None], norm_a[0], norm_f[0], query, key.T, value.T, out, gate, up, down, router.T,
    )


def local(
    tokens,
    depths,
    segments,
    norm_attn,
    norm_ffn,
    w_query,
    key_weight,
    value_weight,
    w_out,
    w_gate,
    w_up,
    w_down,
    w_router,
    cotangent,
    mesh_sizes,
):
    piece = tokens.shape[1]
    positions = lax.axis_index("blk") * piece + jnp.arange(piece, dtype=jnp.int32)
    angles = frequencies(HEAD_DIMENSION)[:, None] * positions.astype(jnp.float32)[None, :]
    tables = dict(cosines=jnp.cos(angles), sines=jnp.sin(angles), norms=jnp.stack([norm_attn, norm_ffn]))
    routing = dict(router=w_router.T, depths=depths)
    heads = dict(w_query_hbm=w_query, key_weight_hbm=key_weight.T, value_weight_hbm=value_weight.T)
    weights = heads | dict(w_out_hbm=w_out, w_gate_hbm=w_gate, w_up_hbm=w_up, w_down_hbm=w_down.T)
    nb = mesh_sizes[0]
    saved = forward(
        tables | routing | dict(tokens=tokens[0].T, cotangent=cotangent[0].T, segments=segments), weights, nb
    )
    operands = dict(
        metas_hbm=saved["metas"], turned_hbm=saved["turned"], dat_hbm=saved["dat"], att_hbm=saved["att"],
        lse_hbm=saved["lse"], kv_hbm=saved["kv"], grad_hbm=saved["grad_hidden"], hid_1_hbm=saved["hid_1"],
        hid_0_hbm=saved["hid"], branch_hbm=saved["branch"], slope_hbm=saved["slope"], silu_hbm=saved["silu"],
        middle_hbm=saved["middle"],
    )
    bottom = backward(1, tables | routing | dict(small_before=saved["small"]), weights | operands, nb)
    return final(tables, saved, saved, bottom, weights, mesh_sizes)


def solution(mesh):
    sizes = (mesh.shape["blk"], mesh.shape["dp"])
    return jax.shard_map(
        functools.partial(local, mesh_sizes=sizes),
        mesh=mesh,
        in_specs=(
            P("dp", "blk", None),
            P("dp", "blk"),
            P("dp", "blk"),
            P(),
            P(),
            P(),
            P(),
            P(),
            P(),
            P(),
            P(),
            P(),
            P(),
            P("dp", "blk", None),
        ),
        out_specs=(
            P("dp", "blk", None),
            P("dp", "blk", None),
            P("blk"),
            P("blk"),
            P("blk", None),
            P("blk", None),
            P("blk", None),
            P("blk", None),
            P("blk", None),
            P("blk", None),
            P("blk", None),
            P("blk", None),
        ),
        check_vma=False,
    )
```

```python
import functools
import itertools
import math
import types

import jax
import jax.numpy as jnp
from jax import lax
from jax.experimental import pallas as pl
from jax.experimental.pallas import tpu as pltpu
from jax.sharding import PartitionSpec as P

QUERY_HEADS = 15
KEY_VALUE_HEADS = 5
HEAD_DIMENSION = 64
RECUR = 2
HEAD_SHARE = QUERY_HEADS // KEY_VALUE_HEADS
KEYS_WIDTH = KEY_VALUE_HEADS * HEAD_DIMENSION
PAIR = 2 * HEAD_DIMENSION
UNIT_COLUMNS = 256
SPAN = 2
VMEM_LIMIT = 63 * 1024 * 1024

epsilon = 1e-05
masked_score = -1e30
low = jnp.bfloat16


def frequencies(head_size):
    return jnp.exp(
        jnp.arange(head_size // 2, dtype=jnp.float32) * (-2.0 * math.log(10000.0) / head_size)
    )


def rms_scale(values):
    return lax.rsqrt(jnp.mean(values * values, axis=-1, keepdims=True) + epsilon)


def norm_gradient(grad_norm, values, gain):
    scale = rms_scale(values)
    weighted = grad_norm * gain
    grad_values = scale * weighted - values * (scale * scale * scale) * jnp.mean(
        weighted * values, axis=-1, keepdims=True
    )
    return grad_values, jnp.sum(grad_norm * values * scale, axis=0, keepdims=True)


def dot_last(left, right):
    return lax.dot_general(left, right, (((1,), (1,)), ((), ())), preferred_element_type=jnp.float32)


def plain_dot(left, right):
    return jnp.dot(left, right, preferred_element_type=jnp.float32)


def bits_of(number, count):
    return tuple((number >> (count - 1 - at)) & 1 for at in range(count))


def bit_of(position, bit):
    return lax.rem(position // (1 << bit), 2)


def block_bits(block, m):
    return tuple(bit_of(block, bit) for bit in range(m - 1, -1, -1))


def flipped(position, bit):
    return position + (1 << bit) * (1 - 2 * bit_of(position, bit))


def remote(source, target, sems, at, device):
    return pltpu.make_async_remote_copy(
        src_ref=source,
        dst_ref=target,
        send_sem=sems[0].at[at],
        recv_sem=sems[1].at[at],
        device_id=device,
        device_id_type=pl.DeviceIdType.MESH,
    )


def greet(partners):
    barrier = pltpu.get_barrier_semaphore()
    for partner in partners:
        pl.semaphore_signal(barrier, inc=1, device_id=partner, device_id_type=pl.DeviceIdType.MESH)
    pl.semaphore_wait(barrier, len(partners))


def turn_heads(turned, cosine, sine, heads):
    split = turned.reshape(heads, 2, HEAD_DIMENSION // 2, turned.shape[1])
    first, second = split[:, 0], split[:, 1]
    both = jnp.stack([first * cosine - second * sine, second * cosine + first * sine], axis=1)
    return both.reshape(turned.shape)


def turn_back(turned, cosine, sine, heads):
    return turn_heads(turned, cosine, -sine, heads)


def head_rows(group, member):
    head = group * HEAD_SHARE + member
    return pl.ds(pl.multiple_of(head * HEAD_DIMENSION, HEAD_DIMENSION), HEAD_DIMENSION)


def as_column(row):
    wide = jnp.broadcast_to(row.astype(jnp.float32), (8, row.shape[1]))
    return wide.T[:, 0:1]


def key_steps(blk, span):
    return blk // (1 << span) + 1


def fill_bias(bias, metas, query_segments, level, blk, m, piece, span):
    many = 1 << span
    key_at = lax.broadcasted_iota(jnp.int32, (many * piece, piece), 0)
    query_at = lax.broadcasted_iota(jnp.int32, (many * piece, piece), 1)

    @pl.loop(0, key_steps(blk, span))
    def _(step):
        rows = metas[block_bits(step, m - span)].reshape(many, 8, piece)
        columns = jnp.concatenate([rows[block].T for block in range(many)], axis=0)
        live = jnp.where(columns[:, 1:2] > level, columns[:, 0:1], -1.0)
        shift = (blk - many * step) * piece
        allowed = (live == query_segments) & (key_at <= query_at + shift) | (key_at == query_at + shift)
        masked = jnp.where(allowed, 0.0, masked_score).astype(bias.dtype)
        bias[pl.ds(many * step, many)] = masked.reshape(many, piece, piece)


def step_bias(bias, step, piece, span):
    many = 1 << span
    here = bias[pl.ds(many * step, many)].reshape(many * piece, piece).astype(jnp.float32)
    return jnp.concatenate([here] * HEAD_SHARE, axis=1)


def kv_weight_loads(key_hbm, value_hbm, target, sems):
    copies = []
    for group in range(KEY_VALUE_HEADS):
        for side, source in enumerate((key_hbm, value_hbm)):
            rows = pl.ds(group * HEAD_DIMENSION, HEAD_DIMENSION)
            place = pl.ds(group * PAIR + side * HEAD_DIMENSION, HEAD_DIMENSION)
            copies.append(pltpu.make_async_copy(source.at[rows], target.at[place], sems.at[2 * group + side]))
    return copies


def turn_keys(both, cosine, sine):
    half = HEAD_DIMENSION // 2
    split = both.reshape(KEY_VALUE_HEADS, 4, half, both.shape[1])
    first, second = split[:, 0], split[:, 1]
    turned = [first * cosine - second * sine, second * cosine + first * sine, split[:, 2], split[:, 3]]
    return jnp.stack(turned, axis=1).reshape(both.shape)


def spec(memory):
    return pl.BlockSpec(memory_space=memory)


def shaped(entry):
    return jax.ShapeDtypeStruct(*entry)


def spaces(entries):
    return [pltpu.VMEM(*entry) for entry in entries]


def dma_semaphores(*shapes):
    return [pltpu.SemaphoreType.DMA(shape) for shape in shapes]


class Piece:
    def __init__(self, at, kept_at, slot, flavour, family, sems, bits, middle=False):
        self.at, self.kept_at, self.slot, self.family, self.sems = at, kept_at, slot, family, sems
        self.m, self.n = bits
        left = list(range(self.m - 1, -1, -1))
        self.order = []
        for stage in range(self.m):
            place = len(left) - 1 if stage == 0 or flavour == 0 else 0
            self.order.append((left.pop(place), place, len(left)))
        self.last = self.m + self.n
        self.blk = lax.axis_index("blk")
        self.dp = lax.axis_index("dp") if self.n else None
        self.middle, self.stages = middle, self.last + 1
        if middle:
            inner = bit_of(self.dp, 0) != bit_of(self.dp, 1)
            outer = jnp.logical_not(inner)
            self.sends, self.receives = (outer, inner, inner), (inner, inner, outer)

    def half(self, ref, side):
        size = self.family.shape[self.family.split] // 2
        here = pl.ds(0 if isinstance(side, int) else pl.multiple_of(side * size, size), size)
        return ref.at[here, :] if self.family.split == 0 else ref.at[:, here]

    def held(self, stage):
        if stage == 0:
            return self.family.part, self.slot
        return self.family.blk[stage - 1], self.kept_at

    def copy(self, stage):
        m, family = self.m, self.family
        if stage < m:
            bit, place, others = self.order[stage]
            ref, index = self.held(stage)
            chosen = [slice(None)] * (others + 1)
            chosen[place] = 1 - bit_of(self.blk, bit)
            source = ref.at[(index, *chosen)]
            target = family.blk[stage].at[self.kept_at]
            device = {"blk": flipped(self.blk, bit)}
        elif self.middle:
            source, target, device = (
                (family.blk[m - 1], family.dp[0], {"dp": flipped(self.dp, 0)}),
                (family.dp[0], family.dp[1], {"dp": 3 - self.dp}),
                (family.out, family.out, {"dp": flipped(self.dp, 0)}),
            )[stage - m]
            source, target = source.at[self.kept_at], target.at[self.kept_at]
        elif stage < self.last:
            bit = stage - m
            if bit == 0:
                source = self.half(family.blk[m - 1].at[self.kept_at], 1 - bit_of(self.dp, 0))
            else:
                source = self.half(family.dp[bit - 1].at[self.kept_at], 0)
            target = self.half(family.dp[bit].at[self.kept_at], 0)
            device = {"dp": flipped(self.dp, bit)}
        else:
            source = self.half(family.out.at[self.kept_at], bit_of(self.dp, 0))
            target = source
            device = {"dp": flipped(self.dp, 0)}
        return remote(source, target, self.sems, (self.at, stage), device)

    def where(self, roles, stage, body):
        if self.middle and stage >= self.m:
            pl.when(roles[stage - self.m])(body)
        else:
            body()

    def start(self, stage):
        self.where(self.sends if self.middle else None, stage, lambda: self.copy(stage).start())

    def finish(self, stage):
        self.where(self.receives if self.middle else None, stage, lambda: self.receive(stage))

    def receive(self, stage):
        m, family = self.m, self.family
        self.copy(stage).wait_recv()
        if stage < m:
            bit, place, others = self.order[stage]
            ref, index = self.held(stage)
            for combo in itertools.product(range(2), repeat=others):
                chosen = list(combo)
                chosen.insert(place, bit_of(self.blk, bit))
                into = family.blk[stage].at[(self.kept_at, *combo)]
                self.add(into, into, ref.at[(index, *chosen)])
            if stage == 0:
                self.copy(0).wait_send()
        elif stage < self.last and self.middle:
            kept, sums = self.kept_at, family.dp
            if stage == m:
                self.add(sums[0].at[kept], sums[0].at[kept], family.blk[m - 1].at[kept])
            else:
                self.add(family.out.at[kept], sums[0].at[kept], sums[1].at[kept])
        elif stage < self.last:
            bit = stage - m
            got = self.half(family.dp[bit].at[self.kept_at], 0)
            if bit == 0:
                own = self.half(family.blk[m - 1].at[self.kept_at], bit_of(self.dp, 0))
            else:
                own = self.half(family.dp[bit - 1].at[self.kept_at], 0)
            into = got
            if stage == self.last - 1:
                into = self.half(family.out.at[self.kept_at], bit_of(self.dp, 0))
            self.add(into, got, own)

    def add(self, into, left, right):
        into[...] = left[...] + right[...]

    def drained(self, stages):
        for stage in stages:
            self.where(self.sends if self.middle else None, stage, lambda: self.copy(stage).wait_send())


class EarlyPiece(Piece):
    def __init__(self, *parts):
        super().__init__(*parts)
        self.stages = 7

    def quarter(self, ref, bit, side):
        size = self.family.shape[0] // (2 << bit)
        here = pl.ds(pl.multiple_of(side * size, size), size)
        return ref.at[(slice(None),) * (len(ref.shape) - 2) + (here,)]

    def copy(self, stage):
        early, kept = self.family.early, self.kept_at
        if stage == 0:
            return super().copy(stage)
        if stage in (1, 2):
            bit = stage - 1
            source = (self.family.blk[0], early[0])[bit].at[kept]
            source, target = self.quarter(source, bit, 1 - bit_of(self.dp, bit)), early[bit].at[kept]
            device = {"dp": flipped(self.dp, bit)}
        elif stage in (3, 4):
            bit, place, others = self.order[stage - 2]
            chosen = [slice(None)] * (others + 1)
            chosen[place] = 1 - bit_of(self.blk, bit)
            source, target = early[stage - 2].at[(kept, *chosen)], early[stage - 1].at[kept]
            device = {"blk": flipped(self.blk, bit)}
        else:
            source = self.quarter(self.family.out.at[kept], 0, bit_of(self.dp, 0))
            if stage == 5:
                source = self.quarter(source, 1, bit_of(self.dp, 1))
            target = source
            device = {"dp": flipped(self.dp, 6 - stage)}
        return remote(source, target, self.sems, (self.at, stage), device)

    def receive(self, stage):
        early, kept = self.family.early, self.kept_at
        if stage == 0:
            super().receive(stage)
            return
        self.copy(stage).wait_recv()
        if stage in (1, 2):
            bit = stage - 1
            own = self.quarter((self.family.blk[0], early[0])[bit].at[kept], bit, bit_of(self.dp, bit))
            self.add(early[bit].at[kept], early[bit].at[kept], own)
        elif stage in (3, 4):
            bit, place, others = self.order[stage - 2]
            for combo in itertools.product(range(2), repeat=others):
                chosen = list(combo)
                chosen.insert(place, bit_of(self.blk, bit))
                got = early[stage - 1].at[(kept, *combo)]
                into = got
                if stage == 4:
                    into = self.quarter(self.family.out.at[kept], 0, bit_of(self.dp, 0))
                    into = self.quarter(into, 1, bit_of(self.dp, 1))
                self.add(into, got, early[stage - 2].at[(kept, *chosen)])


def feed_forward_backward(at, level, gradient, ready, done):
    column = at.router[level:level + 1, :].astype(jnp.float32)
    active = as_column(at.depths[...]) > float(level)
    hidden = at.hid_level[...]
    chosen = jax.nn.sigmoid(jnp.sum(hidden * column, axis=1, keepdims=True))
    at.dbranch[...] = jnp.where(active, chosen, 0.0) * gradient
    dchosen = jnp.where(active, jnp.sum(gradient * at.branch_level[...], axis=1, keepdims=True), 0.0)
    dlogit = dchosen * chosen * (1.0 - chosen)
    at.small[2 + level:3 + level, :] = jnp.sum(hidden * dlogit, axis=0, keepdims=True)
    at.grad_hidden[...] = gradient + dlogit * column
    at.dffn[...] = at.dbranch[...].astype(low)

    ready(0)
    dinner = plain_dot(at.dffn[...], at.w_down[...])
    at.dgate[...] = (dinner * at.slope_level[...].astype(jnp.float32)).astype(low)
    at.dup[...] = (dinner * at.silu_level[...].astype(jnp.float32)).astype(low)
    done()
    at.dnorm_turned[...] = plain_dot(at.w_gate[...], at.dgate[...].T) + plain_dot(at.w_up[...], at.dup[...].T)
    ready(1)
    dnorm = at.dnorm_turned[...].T
    dmiddle, gain_share = norm_gradient(dnorm, at.middle_level[...], at.norms[1:2, :].astype(jnp.float32))
    at.small[1:2, :] += gain_share
    at.grad_hidden[...] += dmiddle
    dattn = (at.dbranch[...] + dmiddle).astype(low)
    lead = at.far.shape[1] - dattn.shape[1]
    at.far[:, :lead] = jnp.zeros((dattn.shape[0], lead), low)
    at.far[:, lead:] = dattn
    at.dat[...] = plain_dot(at.w_out[...], dattn.T).astype(low)


def forward_kernel(sizes, names, *refs):
    m, piece = sizes
    at = types.SimpleNamespace(**dict(zip(names, refs)))
    blk = lax.axis_index("blk")
    mine = block_bits(blk, m)
    kv, metas = at.kv, at.metas
    weights = (
        (at.w_query_hbm, at.w_query), (at.w_out_hbm, at.w_out), (at.w_gate_hbm, at.w_gate), (at.w_up_hbm, at.w_up), (at.w_down_hbm, at.w_down),
    )
    loads = [pltpu.make_async_copy(*pair, at.load_sems.at[index]) for index, pair in enumerate(weights)]
    kv_loads = kv_weight_loads(at.key_weight_hbm, at.value_weight_hbm, at.kv_weight, at.weight_sems)
    for load in kv_loads + loads:
        load.start()
    saved = (
        (at.normed, at.normed_out), (at.turned, at.turned_out), (kv, at.kv_out), (at.lse, at.lse_out),
        (at.att, at.att_out), (at.nffn, at.nffn_out), (at.inner, at.inner_out),
    )

    def save(index, level):
        return pltpu.make_async_copy(
            saved[index][0].at[level] if index == 2 else saved[index][0], saved[index][1].at[level], at.save_sems.at[index, level]
        )

    first = (
        (at.hid.at[0], at.hid_out), (at.middle, at.middle_out), (at.silu, at.silu_out),
        (at.slope, at.slope_out), (at.branch, at.branch_out), (metas, at.metas_out),
        (at.far, at.far_out), (at.dat, at.dat_out), (at.dffn, at.dffn_out), (at.dgate, at.dgate_out), (at.dup, at.dup_out),
        (at.hid.at[1], at.hid_1_out),
    )
    late = [pltpu.make_async_copy(*pair, at.late_sems.at[index]) for index, pair in enumerate(first)]
    segment_row = at.segments[...].astype(jnp.float32)
    depth_column = as_column(at.depths[...])
    metas[mine] = jnp.concatenate(
        [segment_row, at.depths[...].astype(jnp.float32), jnp.zeros((6, piece), jnp.float32)], axis=0
    )
    greet([{"blk": flipped(blk, bit)} for bit in range(m)])

    def place(known):
        return tuple(slice(None) if bit in known else mine[m - 1 - bit] for bit in range(m - 1, -1, -1))

    orders = (list(range(1, m)), list(range(m - 1, 0, -1)))
    kv_sems = (at.kv_send, at.kv_recv)

    def kv_copies(level, group, stage):
        if stage == m - 1:
            ref = kv.at[(level, group, *place(range(1, m)))]
            return [remote(ref, ref, kv_sems, (level, group, 2 * stage), {"blk": flipped(blk, 0)})]
        copies = []
        for side, order in enumerate(orders):
            rows = pl.ds(side * (piece // 2), piece // 2)
            ref = kv.at[(level, group, *place(order[:stage]), rows)]
            copies.append(remote(ref, ref, kv_sems, (level, group, 2 * stage + side), {"blk": flipped(blk, order[stage])}))
        return copies

    def kv_advance(level, group, stage):
        if stage > 0:
            for copy in kv_copies(level, group, stage - 1):
                copy.wait_recv()
        if stage < m:
            for copy in kv_copies(level, group, stage):
                copy.start()

    def meta_copy(stage):
        bits = list(range(1, m)) + [0]
        ref = metas.at[place(bits[:stage])]
        return remote(ref, ref, (at.meta_send, at.meta_recv), stage, {"blk": flipped(blk, bits[stage])})

    meta_copy(0).start()
    cosine, sine = at.cosines[...], at.sines[...]
    gain_attn, gain_ffn = at.norms[0:1, :].astype(jnp.float32), at.norms[1:2, :].astype(jnp.float32)
    routers = at.router[...].astype(jnp.float32)
    at.hid[0] = at.tokens[...].T.astype(jnp.float32)
    late[0].start()
    at.query_pad[HEAD_DIMENSION:, :] = jnp.zeros_like(at.query_pad[HEAD_DIMENSION:, :])

    @pl.loop(0, RECUR)
    def _(level):
        @pl.when(level > 0)
        def _():
            for index in range(5):
                save(index, 0).wait()

        hidden = at.hid[level]
        at.flat[...] = (hidden * rms_scale(hidden) * gain_attn).astype(low)
        at.normed[...] = at.flat[...].T

        @pl.when(level == 0)
        def _():
            for load in kv_loads:
                load.wait()

        both = turn_keys(plain_dot(at.kv_weight[...], at.normed[...]), cosine, sine).T.astype(low)
        for group in range(KEY_VALUE_HEADS):
            kv[(level, group, *mine)] = both[:, group * PAIR:(group + 1) * PAIR]
            kv_advance(level, group, 0)

        @pl.when(level == 0)
        def _():
            loads[0].wait()
            for stage in range(1, m - 1):
                meta_copy(stage - 1).wait_recv()
                meta_copy(stage).start()

        queries = turn_heads(plain_dot(at.flat[...], at.w_query[...]).T, cosine, sine, QUERY_HEADS)
        at.turned[...] = (queries * HEAD_DIMENSION ** (-0.5)).astype(low)

        @pl.when(level == 0)
        def _():
            for stage in range(max(1, m - 1), m):
                meta_copy(stage - 1).wait_recv()
                meta_copy(stage).start()

        for stage in range(1, m - 1):
            for group in range(KEY_VALUE_HEADS):
                kv_advance(level, group, stage)
        kv_advance(level, 0, m - 1)

        @pl.when(level == 0)
        def _():
            meta_copy(m - 1).wait_recv()
            late[5].start()

        fill_bias(at.bias, metas, segment_row, level.astype(jnp.float32), blk, m, piece, SPAN)

        @pl.loop(0, KEY_VALUE_HEADS)
        def _(group):
            @pl.when(group + 1 < KEY_VALUE_HEADS)
            def _():
                kv_advance(level, group + 1, m - 1)

            kv_advance(level, group, m)
            for member in range(HEAD_SHARE):
                at.query_pad[:HEAD_DIMENSION, member * piece:(member + 1) * piece] = at.turned[head_rows(group, member), :]
            at.top[...] = jnp.full_like(at.top, masked_score)
            at.total[...] = jnp.zeros_like(at.total)

            @pl.loop(0, key_steps(blk, SPAN))
            def _(index):
                step = key_steps(blk, SPAN) - 1 - index
                rows = kv[(level, group, *block_bits(step, m - SPAN))].reshape((1 << SPAN) * piece, PAIR)
                scores = plain_dot(rows, at.query_pad[...]) + step_bias(at.bias, step, piece, SPAN)
                before = at.top[0:1, :]
                after = jnp.maximum(before, jnp.max(scores, axis=0, keepdims=True))
                raised = jnp.exp(scores - after)
                shrink = jnp.exp(before - after)
                at.top[0:1, :] = after
                ones = jnp.ones((16, rows.shape[0]), low)
                left = jnp.concatenate([rows.T[HEAD_DIMENSION:], ones], axis=0)
                at.total[...] = at.total[...] * shrink + plain_dot(left, raised.astype(low))

            sums = at.total[HEAD_DIMENSION:HEAD_DIMENSION + 1, :]
            at.lse[pl.ds(group, 1), :] = at.top[0:1, :] + jnp.log(sums)
            out = at.total[:HEAD_DIMENSION, :] / sums
            for member in range(HEAD_SHARE):
                at.att[head_rows(group, member), :] = out[:, member * piece:(member + 1) * piece].astype(low)

        for index in range(5):
            save(index, level).start()

        @pl.when(level == 0)
        def _():
            loads[1].wait()

        @pl.when(level > 0)
        def _():
            save(5, 0).wait()
            save(6, 0).wait()
            for copy in late[1:5]:
                copy.wait()

        attn = plain_dot(at.att[...].T, at.w_out[...])
        mid = at.hid[level] + attn
        at.middle[...] = mid
        at.branch[...] = attn
        at.flat[...] = (mid * rms_scale(mid) * gain_ffn).astype(low)
        at.nffn[...] = at.flat[...].T
        save(5, level).start()

        @pl.when(level == 0)
        def _():
            loads[2].wait()
            loads[3].wait()

        gate_pre = plain_dot(at.flat[...], at.w_gate[...])
        up_pre = plain_dot(at.flat[...], at.w_up[...])
        opened = jax.nn.sigmoid(gate_pre)
        passed = gate_pre * opened
        at.silu[...] = passed.astype(low)
        at.slope[...] = (up_pre * (opened + passed - passed * opened)).astype(low)
        at.inner[...] = (passed * up_pre).astype(low).T
        save(6, level).start()

        @pl.when(level == 0)
        def _():
            loads[4].wait()

        at.branch[...] += plain_dot(at.w_down[...], at.inner[...]).T
        column = jnp.where(level == 0, routers[0:1, :], routers[1:2, :])
        logit = jnp.sum(at.hid[level] * column, axis=1, keepdims=True)
        weight = jnp.where(depth_column > level.astype(jnp.float32), jax.nn.sigmoid(logit), 0.0)
        at.hid[level + 1] = at.hid[level] + weight * at.branch[...]

        @pl.when(level == 0)
        def _():
            for copy in late[1:5]:
                copy.start()

    at.hidden_out[...] = at.hid[RECUR].T
    top = RECUR - 1
    at.hid_level, at.branch_level, at.middle_level = at.hid.at[top], at.branch, at.middle
    at.silu_level, at.slope_level = at.silu, at.slope
    at.small[...] = jnp.zeros_like(at.small)
    feed_forward_backward(at, top, at.cotangent[...].T.astype(jnp.float32), lambda part: None, lambda: None)
    for copy in late[6:]:
        copy.start()
    for stage in range(m):
        meta_copy(stage).wait_send()
    for level in range(RECUR):
        for group in range(KEY_VALUE_HEADS):
            for stage in range(m):
                for copy in kv_copies(level, group, stage):
                    copy.wait_send()
    for index in range(len(saved)):
        save(index, RECUR - 1).wait()
    for copy in late[:1] + late[5:]:
        copy.wait()


def far_width(width):
    return 2 * width + 2 * KEYS_WIDTH - 1536


def forward(small, weights, nb):
    m = nb.bit_length() - 1
    width, piece = small["tokens"].shape
    hidden_units = weights["w_gate_hbm"].shape[1]
    blocks, wide = (2,) * m, HEAD_SHARE * piece
    rows, turned = ((piece, width), jnp.float32), ((RECUR, width, piece), low)
    hidden = ((piece, hidden_units), low)
    saved = dict(
        normed=turned, turned=turned, kv=((RECUR, KEY_VALUE_HEADS, *blocks, piece, PAIR), low),
        lse=((RECUR, 8, wide), jnp.float32), att=turned, nffn=turned, inner=((RECUR, hidden_units, piece), low),
        metas=((*blocks, 8, piece), jnp.float32), far=((piece, far_width(width)), low), dat=((width, piece), low),
        dffn=((piece, width), low), dgate=hidden, dup=hidden,
    )
    first = dict(hid=rows, middle=rows, silu=hidden, slope=hidden, branch=rows)
    outs = dict(hidden_out=((width, piece), jnp.float32), grad_hidden=rows, small=((8, width), jnp.float32))
    anywhere = {name + "_out": entry for name, entry in (saved | first | dict(hid_1=rows)).items()}
    single = {name: (shape[1:], dtype) for name, (shape, dtype) in saved.items() if shape[0] == RECUR and name not in ("kv", "metas")}
    buffers = {name[:-4]: (array.shape, array.dtype) for name, array in weights.items()} | saved | single | first | dict(
        kv_weight=((2 * KEYS_WIDTH, width), low),
        hid=((RECUR + 1, piece, width), jnp.float32), flat=((piece, width), low),
        bias=((nb, piece, piece), jnp.float32), query_pad=((PAIR, wide), low), top=((8, wide), jnp.float32),
        total=((HEAD_DIMENSION + 16, wide), jnp.float32), dbranch=rows, dnorm_turned=((width, piece), jnp.float32),
    )
    semaphores = dict(
        load_sems=(5,), weight_sems=(2 * KEY_VALUE_HEADS,), save_sems=(7, RECUR), late_sems=(12,), kv_send=(RECUR, KEY_VALUE_HEADS, 2 * m),
        kv_recv=(RECUR, KEY_VALUE_HEADS, 2 * m), meta_send=(m,), meta_recv=(m,),
    )
    results = pl.pallas_call(
        functools.partial(forward_kernel, (m, piece), (*small, *weights, *outs, *anywhere, *buffers, *semaphores)),
        out_shape=[shaped(entry) for entry in (outs | anywhere).values()],
        in_specs=[spec(pltpu.VMEM)] * len(small) + [spec(pl.ANY)] * len(weights),
        out_specs=[spec(pltpu.VMEM)] * len(outs) + [spec(pl.ANY)] * len(anywhere),
        scratch_shapes=spaces(buffers.values()) + dma_semaphores(*semaphores.values()),
        compiler_params=pltpu.CompilerParams(
            collective_id=1, has_side_effects=True, vmem_limit_bytes=VMEM_LIMIT
        ),
        cost_estimate=pl.CostEstimate(
            flops=3 * RECUR * piece * width * 10240, bytes_accessed=48 * 1024 * 1024, transcendentals=0
        ),
        name="forward_levels",
    )(*small.values(), *weights.values())
    return dict(zip((*outs, *(name[:-4] for name in anywhere)), results))


class AttentionBackward:
    def __init__(self, at, m, piece, level, span):
        self.at, self.m, self.piece, self.level, self.span = at, m, piece, level, span
        self.blk = lax.axis_index("blk")
        self.family = types.SimpleNamespace(part=at.part, blk=at.halves, dp=(), out=None, shape=(piece // 2, PAIR), split=0)

    def pieces(self, group):
        sems = (self.at.kv_send, self.at.kv_recv)
        return [
            Piece(2 * group + side, 2 * group + side, 2 * group + side, side, self.family, sems, (self.m, 0))
            for side in range(2)
        ]

    def move(self, group, stage):
        for piece_of in self.pieces(group):
            piece_of.finish(stage)
            if stage + 1 < self.m:
                piece_of.start(stage + 1)

    def begin(self):
        at = self.at
        query_segments = at.metas[block_bits(self.blk, self.m)][0:1, :]
        fill_bias(at.bias, at.metas, query_segments, float(self.level), self.blk, self.m, self.piece, self.span)
        at.query_pad[HEAD_DIMENSION:, :] = jnp.zeros_like(at.query_pad[HEAD_DIMENSION:, :])
        at.dat_pad[:HEAD_DIMENSION, :] = jnp.zeros_like(at.dat_pad[:HEAD_DIMENSION, :])

    def group(self, group):
        at, m, piece, blk = self.at, self.m, self.piece, self.blk
        half = piece // 2
        carried = []
        for member in range(HEAD_SHARE):
            rows, lanes = head_rows(group, member), slice(member * piece, (member + 1) * piece)
            at.query_pad[:HEAD_DIMENSION, lanes] = at.turned[rows, :]
            at.dat_pad[HEAD_DIMENSION:, lanes] = at.dat_turned[rows, :]
            product = at.dat_turned[rows, :].astype(jnp.float32) * at.att_turned[rows, :].astype(jnp.float32)
            carried.append(jnp.sum(product, axis=0, keepdims=True))
        carried = jnp.concatenate(carried, axis=1)
        at.query_rows[...] = at.query_pad[...].T
        at.dat_rows[...] = at.dat_pad[...].T
        log_total = at.lse[pl.ds(group, 1), :]
        at.dq_sum[...] = jnp.zeros_like(at.dq_sum)

        span, lead = self.span, m - self.span

        @pl.loop(0, key_steps(blk, span))
        def _(step):
            rows = at.kv[(group, *block_bits(step, lead))].reshape((1 << span) * piece, PAIR)
            probability = jnp.exp(plain_dot(rows, at.query_pad[...]) + step_bias(at.bias, step, piece, span) - log_total)
            dprob = plain_dot(rows, at.dat_pad[...])
            dscores = (probability * (dprob - carried)).astype(low)
            share = plain_dot(dscores, at.query_rows[...]) + plain_dot(probability.astype(low), at.dat_rows[...])
            share = share.astype(low)
            for block in range(1 << span):
                for side in range(2):
                    first = block * piece + side * half
                    place = (2 * group + side, *block_bits(step, lead), *bits_of(block, span))
                    at.part[place] = share[first:first + half]
            at.dq_sum[...] += plain_dot(rows.T[:HEAD_DIMENSION], dscores)

        @pl.loop(key_steps(blk, span), 1 << lead)
        def _(step):
            for block in range(1 << span):
                for side in range(2):
                    place = (2 * group + side, *block_bits(step, lead), *bits_of(block, span))
                    at.part[place] = jnp.zeros((half, PAIR), low)

        for piece_of in self.pieces(group):
            piece_of.start(0)
        for member in range(HEAD_SHARE):
            at.dq_turned[head_rows(group, member), :] = at.dq_sum[:, member * piece:(member + 1) * piece]

    def follow(self, group):
        for stage in range(self.m - 1):
            earlier = group - 1 - stage
            if isinstance(group, int):
                if 0 <= earlier < KEY_VALUE_HEADS:
                    self.move(earlier, stage)
            else:
                @pl.when(earlier >= 0)
                def _():
                    self.move(earlier, stage)

    def queries(self, cosine, sine):
        at = self.at
        dqueries = turn_back(at.dq_turned[...] * HEAD_DIMENSION ** (-0.5), cosine, sine, QUERY_HEADS).astype(low)
        self.put(2 * KEYS_WIDTH, dqueries.T)
        at.dnorm[...] = plain_dot(at.w_query[...], dqueries).T

    def put(self, column, values):
        self.at.near[:, column:column + values.shape[1]] = values

    def keys(self, cosine, sine):
        at, m = self.at, self.m
        filled = 2 * KEYS_WIDTH + QUERY_HEADS * HEAD_DIMENSION
        self.put(filled, jnp.zeros((self.piece, at.near.shape[1] - filled), low))
        sums = []
        for group in range(KEY_VALUE_HEADS):
            self.move(group, m - 1)
            sums.append(jnp.concatenate([at.halves[m - 1][2 * group], at.halves[m - 1][2 * group + 1]], axis=0))
        both = jnp.concatenate(sums, axis=1).astype(jnp.float32).T
        both = turn_keys(both, cosine, -sine).astype(low).T
        self.put(0, both)
        at.dnorm[...] += plain_dot(both, at.kv_weight[...])

    def drained(self):
        for group in range(KEY_VALUE_HEADS):
            for piece_of in self.pieces(group):
                piece_of.drained(range(1, self.m))


def attention_buffers(nb, piece, width, bias_type):
    m, wide, heads = nb.bit_length() - 1, HEAD_SHARE * piece, 2 * KEY_VALUE_HEADS
    turned = ((width, piece), low)
    pad, pad_rows = ((PAIR, wide), low), ((wide, PAIR), low)
    buffers = dict(
        turned=turned, dat_turned=turned, att_turned=turned, kv=((KEY_VALUE_HEADS, *(2,) * m, piece, PAIR), low),
        lse=((8, wide), jnp.float32), metas=((*(2,) * m, 8, piece), jnp.float32), w_query=((width, width), low),
        kv_weight=((2 * KEYS_WIDTH, width), low), dq_turned=((width, piece), jnp.float32),
        bias=((nb, piece, piece), bias_type), query_pad=pad, dat_pad=pad, query_rows=pad_rows, dat_rows=pad_rows,
        dq_sum=((HEAD_DIMENSION, wide), jnp.float32), part=((heads, *(2,) * m, piece // 2, PAIR), low),
        dnorm=((piece, width), jnp.float32), hid=((piece, width), jnp.float32),
    )
    for stage in range(m):
        buffers["half_%d" % stage] = ((heads, *(2,) * (m - 1 - stage), piece // 2, PAIR), low)
    return buffers


def backward_kernel(sizes, names, *refs):
    m, piece, level = sizes
    at = types.SimpleNamespace(**dict(zip(names, refs)))
    at.halves = [getattr(at, "half_%d" % stage) for stage in range(m)]
    at.near = at.near_out
    blk = lax.axis_index("blk")
    pairs = (
        (at.metas_hbm, at.metas), (at.turned_hbm.at[level], at.turned), (at.dat_hbm, at.dat_turned),
        (at.att_hbm.at[level], at.att_turned), (at.lse_hbm.at[level], at.lse), (at.kv_hbm.at[level], at.kv),
        (at.w_query_hbm, at.w_query),
        (at.grad_hbm, at.grad_hidden), (at.hid_1_hbm, at.hid),
        (at.hid_0_hbm, at.hid_level), (at.branch_hbm, at.branch_level), (at.w_down_hbm, at.w_down),
        (at.slope_hbm, at.slope_level), (at.silu_hbm, at.silu_level), (at.w_gate_hbm, at.w_gate), (at.w_up_hbm, at.w_up),
        (at.middle_hbm, at.middle_level), (at.w_out_hbm, at.w_out),
    )
    loads = [pltpu.make_async_copy(*pair, at.load_sems.at[index]) for index, pair in enumerate(pairs)]
    loads += kv_weight_loads(at.key_weight_hbm, at.value_weight_hbm, at.kv_weight, at.weight_sems)
    for load in loads:
        load.start()
    saves = [
        pltpu.make_async_copy(*pair, at.save_sems.at[index])
        for index, pair in enumerate(((at.dgate, at.dgate_out), (at.dup, at.dup_out)))
    ]
    greet([{"blk": flipped(blk, bit)} for bit in range(m)])
    work = AttentionBackward(at, m, piece, level, SPAN)
    loads[0].wait()
    work.begin()
    for load in loads[1:6]:
        load.wait()

    @pl.loop(0, KEY_VALUE_HEADS)
    def _(group):
        work.group(group)
        work.follow(group)

    cosine, sine = at.cosines[...], at.sines[...]
    for virtual in range(KEY_VALUE_HEADS, KEY_VALUE_HEADS + m - 1):
        work.follow(virtual)
        if virtual == KEY_VALUE_HEADS:
            loads[6].wait()
            work.queries(cosine, sine)
    for load in loads[7:]:
        load.wait()
    work.keys(cosine, sine)
    dhidden, gain_share = norm_gradient(at.dnorm[...], at.hid[...], at.norms[0:1, :].astype(jnp.float32))
    at.small[...] = at.small_before[...]
    at.small[0:1, :] = gain_share
    gradient = at.grad_hidden[...] + dhidden
    at.dnorm[...] = gradient
    feed_forward_backward(at, level - 1, at.dnorm[...], lambda part: None, lambda: [save.start() for save in saves])
    work.drained()
    for save in saves:
        save.wait()


def backward(level, small, operands, nb):
    m = nb.bit_length() - 1
    piece, width = operands["grad_hbm"].shape
    hidden_units = operands["w_gate_hbm"].shape[1]
    rows, flat, hidden = ((piece, width), jnp.float32), ((piece, width), low), ((piece, hidden_units), low)
    outs = dict(
        grad_hidden=rows, small=((8, width), jnp.float32), near_out=((piece, 1792), low), dffn=flat,
        dat=((width, piece), low), far=((piece, far_width(width)), low),
    )
    anywhere = dict(dgate_out=hidden, dup_out=hidden)
    buffers = attention_buffers(nb, piece, width, jnp.float32) | dict(
        hid_level=rows, branch_level=rows, middle_level=rows, w_down=((width, hidden_units), low), slope_level=hidden,
        silu_level=hidden, w_gate=((width, hidden_units), low), w_up=((width, hidden_units), low),
        w_out=((width, width), low), dbranch=rows, dnorm_turned=((width, piece), jnp.float32), dgate=hidden, dup=hidden,
    )
    sums = (2 * KEY_VALUE_HEADS, m)
    semaphores = dict(load_sems=(18,), weight_sems=(2 * KEY_VALUE_HEADS,), save_sems=(2,), kv_send=sums, kv_recv=sums)
    results = pl.pallas_call(
        functools.partial(
            backward_kernel, (m, piece, level), (*small, *operands, *outs, *anywhere, *buffers, *semaphores)
        ),
        out_shape=[shaped(entry) for entry in (outs | anywhere).values()],
        in_specs=[spec(pltpu.VMEM)] * len(small) + [spec(pl.ANY)] * len(operands),
        out_specs=[spec(pltpu.VMEM)] * len(outs) + [spec(pl.ANY)] * len(anywhere),
        scratch_shapes=spaces(buffers.values()) + dma_semaphores(*semaphores.values()),
        compiler_params=pltpu.CompilerParams(
            collective_id=2, has_side_effects=True, vmem_limit_bytes=VMEM_LIMIT
        ),
        cost_estimate=pl.CostEstimate(
            flops=2 * piece * width * 20000, bytes_accessed=32 * 1024 * 1024, transcendentals=0
        ),
        name="backward_level",
    )(*small.values(), *operands.values())
    return dict(zip((*outs, *anywhere), results))


WIDE_SLOTS, DOWN_SLOTS, EARLY = 4, 2, 3


def final_kernel(sizes, names, *refs):
    nb, m, n, piece, rows, padded, near_width = sizes
    at = types.SimpleNamespace(**dict(zip(names, refs)))
    at.halves = [getattr(at, "half_%d" % stage) for stage in range(m)]
    blk, dp = lax.axis_index("blk"), lax.axis_index("dp")
    at.near = at.gate_side.at[pl.ds(0, piece), pl.ds(0, near_width)]
    counter = itertools.count()

    def load(source, target):
        return pltpu.make_async_copy(source, target, at.load_sems.at[next(counter)])

    def both_lanes(ref, target):
        return [load(ref.at[level], target.at[:, pl.ds(level * piece, piece)]) for level in range(RECUR)]

    def both_rows(low_ref, deep_ref, target, width):
        pairs = ((low_ref, 0), (deep_ref, piece))
        return [load(ref, target.at[pl.ds(first, piece), pl.ds(0, width)]) for ref, first in pairs]

    hidden_units, width = at.gate_side.shape[1], at.dffn.shape[1]
    far_lanes = at.far_0_hbm.shape[1]
    loads = types.SimpleNamespace(
        nffn=both_lanes(at.nffn_hbm, at.left),
        dgate=both_rows(at.dgate_0_hbm, at.dgate_1_hbm, at.gate_side, hidden_units),
        inner=both_lanes(at.inner_hbm, at.inner),
        dffn=both_rows(at.dffn_0_hbm, at.dffn_1_hbm, at.dffn, width),
        metas=[load(at.metas_hbm, at.metas)],
        heads=[
            load(at.turned_hbm.at[0], at.turned), load(at.dat_hbm, at.dat_turned), load(at.att_hbm.at[0], at.att_turned),
            load(at.lse_hbm.at[0], at.lse), load(at.kv_hbm.at[0], at.kv),
        ],
        dup=both_rows(at.dup_0_hbm, at.dup_1_hbm, at.up_side, hidden_units),
        w_query=[load(at.w_query_hbm, at.w_query)],
        rest=[
            load(at.hid_hbm, at.hid), load(at.grad_hbm, at.grad),
        ],
        attended=both_lanes(at.attended_hbm, at.left_attended),
        kv_weight=kv_weight_loads(at.key_weight_hbm, at.value_weight_hbm, at.kv_weight, at.weight_sems),
    )
    late = types.SimpleNamespace(
        near=[load(at.near_1_hbm, at.gate_side.at[pl.ds(piece, piece), pl.ds(0, near_width)])],
        far=both_rows(at.far_0_hbm, at.far_1_hbm, at.up_side, far_lanes),
        normed=both_lanes(at.normed_hbm, at.left),
    )

    def begin(copies):
        for copy in copies:
            copy.start()

    def ready(copies):
        for copy in copies:
            copy.wait()

    for copies in vars(loads).values():
        begin(copies)
    greet([{"blk": flipped(blk, bit)} for bit in range(m)] + [{"dp": flipped(dp, bit)} for bit in range(n)])

    down_rows = at.part_down.shape[-2]

    def family(name, shape, split):
        return types.SimpleNamespace(
            part=getattr(at, "part_" + name), out=getattr(at, "out_" + name), shape=shape, split=split,
            blk=[getattr(at, "blk_%s_%d" % (name, stage)) for stage in range(m)],
            dp=[getattr(at, "dp_%s_%d" % (name, stage)) for stage in range(n)],
        )

    wide = family("wide", (2 * padded, UNIT_COLUMNS), 1)
    down = family("down", (down_rows, width), 0)
    little = family("small", (16, 128), 0)
    many = 5 - at.out_down.shape[0]
    if many:
        deep = types.SimpleNamespace(
            part=at.part_down, out=at.out_deep, shape=(down_rows, width), blk=[at.blk_deep],
            early=[at.early_0, at.early_1, at.early_2, at.early_3],
        )
    sems = (at.send_sems, at.recv_sems)
    units = itertools.count()

    def unit(holder, index, flavour, halves=n != 2):
        return Piece(next(units), index, index % holder.part.shape[0], flavour, holder, sems, (m, n), not halves)

    def down_unit(index):
        if index < many:
            return EarlyPiece(next(units), index, index % DOWN_SLOTS, 1, deep, sems, (m, n))
        return Piece(next(units), index - many, index % DOWN_SLOTS, 1, down, sems, (m, n), n == 2)

    pairs = [[unit(wide, index, 0), down_unit(index)] for index in range(5)]
    pairs += [[unit(wide, index, 0), unit(wide, index + 1, 1)] for index in (5, 7, 9)]
    pairs += [[unit(wide, 11, 0, True), unit(wide, 12, 1, True)]]
    pairs += [[unit(wide, 13, 0, True), unit(wide, 14, 1, True), unit(little, 0, 0, True)]]

    def compute_wide(index, slot):
        if index == 0:
            ready(loads.nffn)
            ready(loads.dgate)
        if index == 5:
            begin(late.near)
            ready(loads.dup)
        if index == 10:
            begin(late.far)
            begin(late.normed)
            ready(late.near)
            ready(late.normed)
            ready(loads.attended)
            ready(late.far)
        block, column = index // 5, (index % 5) * UNIT_COLUMNS
        second = 1280 + column
        upper_columns, lower_columns = slice(column, column + UNIT_COLUMNS), slice(second, second + UNIT_COLUMNS)
        if block < 2:
            right = at.gate_side if block == 0 else at.up_side
            upper = plain_dot(at.left[...], right[:, upper_columns])
            lower = plain_dot(at.left[...], right[:, lower_columns])
        else:
            upper = plain_dot(at.left[...], at.gate_side[:, upper_columns])
            lower = None
            if second < 1600:
                lower = plain_dot(at.left[...], at.gate_side[:, lower_columns])
            if second >= 1536:
                more = plain_dot(at.left_attended[...], at.up_side[:, second - 1536:second - 1536 + UNIT_COLUMNS])
                lower = more if lower is None else lower + more
        for target in range(nb):
            here = slice(target * padded, (target + 1) * padded)
            both = jnp.concatenate([upper[here], lower[here]], axis=0)
            at.part_wide[(slot, *bits_of(target, m))] = both.astype(low)

    def compute_down(index, slot):
        if index == 0:
            ready(loads.inner)
            ready(loads.dffn)
        firsts = [(target * 5 + index) * down_rows for target in range(nb)]
        left = jnp.concatenate([at.inner[first:first + down_rows, :] for first in firsts], axis=0)
        result = plain_dot(left, at.dffn[...])
        for target in range(nb):
            at.part_down[(slot, *bits_of(target, m))] = result[target * down_rows:(target + 1) * down_rows].astype(low)

    def compute_small():
        total = at.small_before[...]
        total = total + jnp.concatenate([at.gain_row[...], jnp.zeros((7, width), jnp.float32)], axis=0)
        at.part_small[...] = jnp.zeros_like(at.part_small)
        for target in range(nb):
            at.part_small[(0, *bits_of(target, m), slice(0, 8), slice(0, rows))] = total[:, target * rows:(target + 1) * rows]

    def compute(piece_of):
        if piece_of.family is wide:
            compute_wide(piece_of.kept_at, piece_of.slot)
        elif piece_of.family is little:
            compute_small()
        elif piece_of.family is down:
            compute_down(piece_of.kept_at + many, piece_of.slot)
        else:
            compute_down(piece_of.kept_at, piece_of.slot)
        piece_of.start(0)

    def moves(tick):
        for stage in range(m + n, -1, -1):
            if 0 <= tick - stage < len(pairs):
                for piece_of in pairs[tick - stage]:
                    if stage + 1 < piece_of.stages:
                        piece_of.finish(stage)
                        piece_of.start(stage + 1)

    work = AttentionBackward(at, m, piece, 0, 1)
    for pair in pairs[:2]:
        for piece_of in pair:
            compute(piece_of)
    ready(loads.metas)
    work.begin()
    ready(loads.heads)
    for group in range(KEY_VALUE_HEADS):
        moves(group)
        for piece_of in pairs[group + 2]:
            compute(piece_of)
        work.group(group)
        work.follow(group)
    cosine, sine = at.cosines[...], at.sines[...]
    moves(5)
    compute(pairs[7][0])
    ready(loads.w_query)
    for virtual in range(KEY_VALUE_HEADS, KEY_VALUE_HEADS + m - 1):
        work.follow(virtual)
        if virtual == KEY_VALUE_HEADS:
            work.queries(cosine, sine)
    moves(6)
    ready(loads.rest)
    ready(loads.kv_weight)
    work.keys(cosine, sine)
    compute(pairs[7][1])
    moves(7)
    for piece_of in pairs[8] + pairs[9][:2]:
        compute(piece_of)
    dhidden, gain_share = norm_gradient(at.dnorm[...], at.hid[...], at.norms[0:1, :].astype(jnp.float32))
    at.gain_row[...] = gain_share
    at.grad_out[...] = (at.grad[...] + dhidden).T
    compute(pairs[9][2])
    for tick in range(8, len(pairs) + m + n - 1):
        moves(tick)
    for pair in pairs:
        for piece_of in pair:
            piece_of.finish(piece_of.stages - 1)
    for pair in pairs:
        for piece_of in pair:
            piece_of.drained(range(1, piece_of.stages))
    work.drained()


def unpack_kernel(sizes, hidden_in, gradient_in, wide_hbm, little_hbm, *refs):
    rows, padded, counts = sizes
    down_hbm, refs = refs[:len(counts)], refs[len(counts):]
    norm_attn, norm_ffn, query, key, value, out, gate, up, down_out, router, hidden, gradient = refs[:12]
    wide, little, down, rest, sems = refs[12:]
    carried = [
        pltpu.make_async_copy(source, target, sems.at[at])
        for at, (source, target) in enumerate(((hidden_in, hidden), (gradient_in, gradient)))
    ]
    pairs, first = [(wide_hbm, wide), (little_hbm, little)], 0
    for source, count in zip(down_hbm, counts):
        pairs.append((source, down.at[pl.ds(first, count)]))
        first += count
    loads = [pltpu.make_async_copy(*pair, sems.at[2 + at]) for at, pair in enumerate(pairs)]
    for copy in loads + carried:
        copy.start()
    for load in loads:
        load.wait()
    norm_attn[...] = little[0, 0:1, :rows]
    norm_ffn[...] = little[0, 1:2, :rows]
    router[...] = little[0, 2:4, :rows]
    for unit in range(5):
        for first, target in ((0, gate), (5, up), (10, rest)):
            tile = wide[first + unit].astype(jnp.float32)
            for side in range(2):
                column = side * 1280 + unit * UNIT_COLUMNS
                target[:, column:column + UNIT_COLUMNS] = tile[side * padded:side * padded + rows]
        down_rows = down.shape[1]
        down_out[unit * down_rows:(unit + 1) * down_rows, :] = down[unit].astype(jnp.float32)
    width = query.shape[1]
    both = rest[:, :2 * KEYS_WIDTH].T
    for group in range(KEY_VALUE_HEADS):
        here, first = slice(group * HEAD_DIMENSION, (group + 1) * HEAD_DIMENSION), group * PAIR
        key[here, :] = both[first:first + HEAD_DIMENSION]
        value[here, :] = both[first + HEAD_DIMENSION:first + PAIR]
    query[...] = rest[:, 2 * KEYS_WIDTH:2 * KEYS_WIDTH + width]
    out[...] = rest[:, 2 * KEYS_WIDTH + width:]
    for copy in carried:
        copy.wait()


def final(small, saved, top, bottom, weights, mesh_sizes):
    nb, nd = mesh_sizes
    m, n = nb.bit_length() - 1, nd.bit_length() - 1
    grad = bottom["grad_hidden"]
    piece, width = grad.shape
    hidden_units = weights["w_gate_hbm"].shape[1]
    rows = width // nb
    padded = -(-rows // 8) * 8
    down_rows = hidden_units // nb // 5
    tokens = RECUR * piece

    def spread(array):
        if padded == rows:
            return array
        split = array.reshape(RECUR, nb, rows, piece)
        return jnp.pad(split, ((0, 0), (0, 0), (0, padded - rows), (0, 0))).reshape(RECUR, nb * padded, piece)

    inputs = small | dict(small_before=bottom["small"])
    operands = dict(
        metas_hbm=saved["metas"], turned_hbm=saved["turned"], dat_hbm=bottom["dat"], att_hbm=saved["att"],
        lse_hbm=saved["lse"], kv_hbm=saved["kv"], w_query_hbm=weights["w_query_hbm"],
        key_weight_hbm=weights["key_weight_hbm"], value_weight_hbm=weights["value_weight_hbm"], hid_hbm=saved["hid"],
        grad_hbm=grad, inner_hbm=saved["inner"], nffn_hbm=spread(saved["nffn"]), normed_hbm=spread(saved["normed"]),
        attended_hbm=spread(saved["att"]), dffn_0_hbm=bottom["dffn"], dffn_1_hbm=top["dffn"],
        dgate_0_hbm=bottom["dgate_out"], dgate_1_hbm=top["dgate"], dup_0_hbm=bottom["dup_out"], dup_1_hbm=top["dup"],
        far_0_hbm=bottom["far"], far_1_hbm=top["far"], near_1_hbm=bottom["near_out"],
    )
    near_width = bottom["near_out"].shape[1]
    many = EARLY if (m, n) == (3, 2) else 0
    families = (
        ("wide", 15, (2 * padded, UNIT_COLUMNS), low, WIDE_SLOTS, 1),
        ("down", 5 - many, (down_rows, width), low, DOWN_SLOTS, 0),
        ("small", 1, (16, 128), jnp.float32, 1, 0),
    )
    outs = dict(grad_out=((width, piece), jnp.float32))
    buffers = attention_buffers(nb, piece, width, low) | dict(
        grad=((piece, width), jnp.float32), gate_side=((tokens, hidden_units), low), up_side=((tokens, hidden_units), low),
        inner=((hidden_units, tokens), low), left=((nb * padded, tokens), low), left_attended=((nb * padded, tokens), low),
        dffn=((tokens, width), low), gain_row=((1, width), jnp.float32),
    )
    for name, count, shape, dtype, slots, split in families:
        outs["out_" + name] = ((count, *shape), dtype)
        buffers["part_" + name] = ((slots, *(2,) * m, *shape), dtype)
        for stage in range(m):
            buffers["blk_%s_%d" % (name, stage)] = ((count, *(2,) * (m - 1 - stage), *shape), dtype)
        for stage in range(n):
            buffers["dp_%s_%d" % (name, stage)] = ((count, *shape), dtype)
    if many:
        outs["out_deep"] = ((many, down_rows, width), low)
        buffers["blk_deep"] = ((many, 2, 2, down_rows, width), low)
        for stage, (lead, share) in enumerate((((2, 2), 2), ((2, 2), 4), ((2,), 4), ((), 4))):
            buffers["early_%d" % stage] = ((many, *lead, down_rows // share, width), low)
    sums, hops = (2 * KEY_VALUE_HEADS, m), (21, m + n + 2)
    semaphores = dict(load_sems=(32,), weight_sems=(2 * KEY_VALUE_HEADS,), kv_send=sums, kv_recv=sums, send_sems=hops, recv_sems=hops)
    names = (*inputs, *operands, *outs, *buffers, *semaphores)
    gradient, wide, down, little, *deep = pl.pallas_call(
        functools.partial(final_kernel, (nb, m, n, piece, rows, padded, near_width), names),
        out_shape=[shaped(entry) for entry in outs.values()],
        in_specs=[spec(pltpu.VMEM)] * len(inputs) + [spec(pl.ANY)] * len(operands),
        out_specs=[spec(pltpu.VMEM)] * len(outs),
        scratch_shapes=spaces(buffers.values()) + dma_semaphores(*semaphores.values()),
        compiler_params=pltpu.CompilerParams(
            collective_id=0, has_side_effects=True, vmem_limit_bytes=VMEM_LIMIT
        ),
        cost_estimate=pl.CostEstimate(
            flops=2 * tokens * width * 14000, bytes_accessed=30 * 1024 * 1024, transcendentals=0
        ),
        name="weight_grads",
    )(*inputs.values(), *operands.values())
    shapes = (
        (1, rows), (1, rows), (rows, width), (KEYS_WIDTH, rows), (KEYS_WIDTH, rows), (rows, width),
        (rows, hidden_units), (rows, hidden_units), (5 * down_rows, width), (2, rows), (width, piece), (width, piece),
    )
    outs = pl.pallas_call(
        functools.partial(unpack_kernel, (rows, padded, [array.shape[0] for array in (*deep, down)])),
        out_shape=[jax.ShapeDtypeStruct(shape, jnp.float32) for shape in shapes],
        in_specs=[spec(pl.ANY)] * (5 + len(deep)),
        out_specs=[spec(pltpu.VMEM)] * 12,
        scratch_shapes=[pltpu.VMEM(array.shape, array.dtype) for array in (wide, little)]
        + spaces([((5, down_rows, width), low), ((rows, 2560), jnp.float32)]) + dma_semaphores((6,)),
        compiler_params=pltpu.CompilerParams(vmem_limit_bytes=VMEM_LIMIT),
        name="unpack",
    )(saved["hidden_out"], gradient, wide, little, *deep, down)
    norm_a, norm_f, query, key, value, out, gate, up, down, router, hidden, gradient = outs
    return (
        hidden.T[None], gradient.T[None], norm_a[0], norm_f[0], query, key.T, value.T, out, gate, up, down, router.T,
    )


def local(
    tokens,
    depths,
    segments,
    norm_attn,
    norm_ffn,
    w_query,
    key_weight,
    value_weight,
    w_out,
    w_gate,
    w_up,
    w_down,
    w_router,
    cotangent,
    mesh_sizes,
):
    piece = tokens.shape[1]
    positions = lax.axis_index("blk") * piece + jnp.arange(piece, dtype=jnp.int32)
    angles = frequencies(HEAD_DIMENSION)[:, None] * positions.astype(jnp.float32)[None, :]
    tables = dict(cosines=jnp.cos(angles), sines=jnp.sin(angles), norms=jnp.stack([norm_attn, norm_ffn]))
    routing = dict(router=w_router.T, depths=depths)
    heads = dict(w_query_hbm=w_query, key_weight_hbm=key_weight.T, value_weight_hbm=value_weight.T)
    weights = heads | dict(w_out_hbm=w_out, w_gate_hbm=w_gate, w_up_hbm=w_up, w_down_hbm=w_down.T)
    nb = mesh_sizes[0]
    saved = forward(
        tables | routing | dict(tokens=tokens[0].T, cotangent=cotangent[0].T, segments=segments), weights, nb
    )
    operands = dict(
        metas_hbm=saved["metas"], turned_hbm=saved["turned"], dat_hbm=saved["dat"], att_hbm=saved["att"],
        lse_hbm=saved["lse"], kv_hbm=saved["kv"], grad_hbm=saved["grad_hidden"], hid_1_hbm=saved["hid_1"],
        hid_0_hbm=saved["hid"], branch_hbm=saved["branch"], slope_hbm=saved["slope"], silu_hbm=saved["silu"],
        middle_hbm=saved["middle"],
    )
    bottom = backward(1, tables | routing | dict(small_before=saved["small"]), weights | operands, nb)
    return final(tables, saved, saved, bottom, weights, mesh_sizes)


def solution(mesh):
    sizes = (mesh.shape["blk"], mesh.shape["dp"])
    return jax.shard_map(
        functools.partial(local, mesh_sizes=sizes),
        mesh=mesh,
        in_specs=(
            P("dp", "blk", None),
            P("dp", "blk"),
            P("dp", "blk"),
            P(),
            P(),
            P(),
            P(),
            P(),
            P(),
            P(),
            P(),
            P(),
            P(),
            P("dp", "blk", None),
        ),
        out_specs=(
            P("dp", "blk", None),
            P("dp", "blk", None),
            P("blk"),
            P("blk"),
            P("blk", None),
            P("blk", None),
            P("blk", None),
            P("blk", None),
            P("blk", None),
            P("blk", None),
            P("blk", None),
            P("blk", None),
        ),
        check_vma=False,
    )
```

```python
import functools
import itertools
import math
import types

import jax
import jax.numpy as jnp
from jax import lax
from jax.experimental import pallas as pl
from jax.experimental.pallas import tpu as pltpu
from jax.sharding import PartitionSpec as P

QUERY_HEADS = 15
KEY_VALUE_HEADS = 5
HEAD_DIMENSION = 64
RECUR = 2
HEAD_SHARE = QUERY_HEADS // KEY_VALUE_HEADS
KEYS_WIDTH = KEY_VALUE_HEADS * HEAD_DIMENSION
PAIR = 2 * HEAD_DIMENSION
UNIT_COLUMNS = 256
SPAN = 2
VMEM_LIMIT = 63 * 1024 * 1024

epsilon = 1e-05
masked_score = -1e30
low = jnp.bfloat16


def frequencies(head_size):
    return jnp.exp(
        jnp.arange(head_size // 2, dtype=jnp.float32) * (-2.0 * math.log(10000.0) / head_size)
    )


def rms_scale(values):
    return lax.rsqrt(jnp.mean(values * values, axis=-1, keepdims=True) + epsilon)


def norm_gradient(grad_norm, values, gain):
    scale = rms_scale(values)
    weighted = grad_norm * gain
    grad_values = scale * weighted - values * (scale * scale * scale) * jnp.mean(
        weighted * values, axis=-1, keepdims=True
    )
    return grad_values, jnp.sum(grad_norm * values * scale, axis=0, keepdims=True)


def dot_last(left, right):
    return lax.dot_general(left, right, (((1,), (1,)), ((), ())), preferred_element_type=jnp.float32)


def plain_dot(left, right):
    return jnp.dot(left, right, preferred_element_type=jnp.float32)


def bits_of(number, count):
    return tuple((number >> (count - 1 - at)) & 1 for at in range(count))


def bit_of(position, bit):
    return lax.rem(position // (1 << bit), 2)


def block_bits(block, m):
    return tuple(bit_of(block, bit) for bit in range(m - 1, -1, -1))


def flipped(position, bit):
    return position + (1 << bit) * (1 - 2 * bit_of(position, bit))


def remote(source, target, sems, at, device):
    return pltpu.make_async_remote_copy(
        src_ref=source,
        dst_ref=target,
        send_sem=sems[0].at[at],
        recv_sem=sems[1].at[at],
        device_id=device,
        device_id_type=pl.DeviceIdType.MESH,
    )


def greet(partners):
    barrier = pltpu.get_barrier_semaphore()
    for partner in partners:
        pl.semaphore_signal(barrier, inc=1, device_id=partner, device_id_type=pl.DeviceIdType.MESH)
    pl.semaphore_wait(barrier, len(partners))


def turn_heads(turned, cosine, sine, heads):
    split = turned.reshape(heads, 2, HEAD_DIMENSION // 2, turned.shape[1])
    first, second = split[:, 0], split[:, 1]
    both = jnp.stack([first * cosine - second * sine, second * cosine + first * sine], axis=1)
    return both.reshape(turned.shape)


def turn_back(turned, cosine, sine, heads):
    return turn_heads(turned, cosine, -sine, heads)


def head_rows(group, member):
    head = group * HEAD_SHARE + member
    return pl.ds(pl.multiple_of(head * HEAD_DIMENSION, HEAD_DIMENSION), HEAD_DIMENSION)


def as_column(row):
    wide = jnp.broadcast_to(row.astype(jnp.float32), (8, row.shape[1]))
    return wide.T[:, 0:1]


def key_steps(blk, span):
    return blk // (1 << span) + 1


def fill_bias(bias, metas, query_segments, level, blk, m, piece, span):
    many = 1 << span
    key_at = lax.broadcasted_iota(jnp.int32, (many * piece, piece), 0)
    query_at = lax.broadcasted_iota(jnp.int32, (many * piece, piece), 1)

    @pl.loop(0, key_steps(blk, span))
    def _(step):
        rows = metas[block_bits(step, m - span)].reshape(many, 8, piece)
        columns = jnp.concatenate([rows[block].T for block in range(many)], axis=0)
        live = jnp.where(columns[:, 1:2] > level, columns[:, 0:1], -1.0)
        shift = (blk - many * step) * piece
        allowed = (live == query_segments) & (key_at <= query_at + shift) | (key_at == query_at + shift)
        masked = jnp.where(allowed, 0.0, masked_score).astype(bias.dtype)
        bias[pl.ds(many * step, many)] = masked.reshape(many, piece, piece)


def step_bias(bias, step, piece, span):
    many = 1 << span
    here = bias[pl.ds(many * step, many)].reshape(many * piece, piece).astype(jnp.float32)
    return jnp.concatenate([here] * HEAD_SHARE, axis=1)


def kv_weight_loads(key_hbm, value_hbm, target, sems):
    copies = []
    for group in range(KEY_VALUE_HEADS):
        for side, source in enumerate((key_hbm, value_hbm)):
            rows = pl.ds(group * HEAD_DIMENSION, HEAD_DIMENSION)
            place = pl.ds(group * PAIR + side * HEAD_DIMENSION, HEAD_DIMENSION)
            copies.append(pltpu.make_async_copy(source.at[rows], target.at[place], sems.at[2 * group + side]))
    return copies


def turn_keys(both, cosine, sine):
    half = HEAD_DIMENSION // 2
    split = both.reshape(KEY_VALUE_HEADS, 4, half, both.shape[1])
    first, second = split[:, 0], split[:, 1]
    turned = [first * cosine - second * sine, second * cosine + first * sine, split[:, 2], split[:, 3]]
    return jnp.stack(turned, axis=1).reshape(both.shape)


def spec(memory):
    return pl.BlockSpec(memory_space=memory)


def shaped(entry):
    return jax.ShapeDtypeStruct(*entry)


def spaces(entries):
    return [pltpu.VMEM(*entry) for entry in entries]


def dma_semaphores(*shapes):
    return [pltpu.SemaphoreType.DMA(shape) for shape in shapes]


class Piece:
    def __init__(self, at, kept_at, slot, flavour, family, sems, bits, middle=False):
        self.at, self.kept_at, self.slot, self.family, self.sems = at, kept_at, slot, family, sems
        self.m, self.n = bits
        left = list(range(self.m - 1, -1, -1))
        self.order = []
        for stage in range(self.m):
            place = len(left) - 1 if stage == 0 or flavour == 0 else 0
            self.order.append((left.pop(place), place, len(left)))
        self.last = self.m + self.n
        self.blk = lax.axis_index("blk")
        self.dp = lax.axis_index("dp") if self.n else None
        self.middle = middle
        if middle:
            inner = bit_of(self.dp, 0) != bit_of(self.dp, 1)
            outer = jnp.logical_not(inner)
            self.sends, self.receives = (outer, inner, inner), (inner, inner, outer)

    def half(self, ref, side):
        size = self.family.shape[self.family.split] // 2
        here = pl.ds(0 if isinstance(side, int) else pl.multiple_of(side * size, size), size)
        return ref.at[here, :] if self.family.split == 0 else ref.at[:, here]

    def held(self, stage):
        if stage == 0:
            return self.family.part, self.slot
        return self.family.blk[stage - 1], self.kept_at

    def copies(self, stage):
        if stage > 0:
            return [self.copy(stage)]
        bit, place, others = self.order[0]
        ref, index = self.held(0)
        made = []
        for number, combo in enumerate(itertools.product(range(2), repeat=others)):
            chosen = list(combo)
            chosen.insert(place, 1 - bit_of(self.blk, bit))
            made.append(remote(
                ref.at[(index, *chosen)], self.family.blk[0].at[(self.kept_at, *combo)], self.sems,
                (self.at, 0 if number == 0 else self.last + number), {"blk": flipped(self.blk, bit)},
            ))
        return made

    def copy(self, stage):
        m, family = self.m, self.family
        if stage < m:
            bit, place, others = self.order[stage]
            ref, index = self.held(stage)
            chosen = [slice(None)] * (others + 1)
            chosen[place] = 1 - bit_of(self.blk, bit)
            source = ref.at[(index, *chosen)]
            target = family.blk[stage].at[self.kept_at]
            device = {"blk": flipped(self.blk, bit)}
        elif self.middle:
            source, target, device = (
                (family.blk[m - 1], family.dp[0], {"dp": flipped(self.dp, 0)}),
                (family.dp[0], family.dp[1], {"dp": 3 - self.dp}),
                (family.out, family.out, {"dp": flipped(self.dp, 0)}),
            )[stage - m]
            source, target = source.at[self.kept_at], target.at[self.kept_at]
        elif stage < self.last:
            bit = stage - m
            if bit == 0:
                source = self.half(family.blk[m - 1].at[self.kept_at], 1 - bit_of(self.dp, 0))
            else:
                source = self.half(family.dp[bit - 1].at[self.kept_at], 0)
            target = self.half(family.dp[bit].at[self.kept_at], 0)
            device = {"dp": flipped(self.dp, bit)}
        else:
            source = self.half(family.out.at[self.kept_at], bit_of(self.dp, 0))
            target = source
            device = {"dp": flipped(self.dp, 0)}
        return remote(source, target, self.sems, (self.at, stage), device)

    def where(self, roles, stage, body):
        if self.middle and stage >= self.m:
            pl.when(roles[stage - self.m])(body)
        else:
            body()

    def start(self, stage):
        def body():
            for copy in self.copies(stage):
                copy.start()

        self.where(self.sends if self.middle else None, stage, body)

    def finish(self, stage):
        self.where(self.receives if self.middle else None, stage, lambda: self.receive(stage))

    def receive(self, stage):
        m, family = self.m, self.family
        for copy in self.copies(stage):
            copy.wait_recv()
        if stage < m:
            bit, place, others = self.order[stage]
            ref, index = self.held(stage)
            for combo in itertools.product(range(2), repeat=others):
                chosen = list(combo)
                chosen.insert(place, bit_of(self.blk, bit))
                into = family.blk[stage].at[(self.kept_at, *combo)]
                self.add(into, into, ref.at[(index, *chosen)])
            if stage == 0:
                for copy in self.copies(0):
                    copy.wait_send()
        elif stage < self.last and self.middle:
            kept, sums = self.kept_at, family.dp
            if stage == m:
                self.add(sums[0].at[kept], sums[0].at[kept], family.blk[m - 1].at[kept])
            else:
                self.add(family.out.at[kept], sums[0].at[kept], sums[1].at[kept])
        elif stage < self.last:
            bit = stage - m
            got = self.half(family.dp[bit].at[self.kept_at], 0)
            if bit == 0:
                own = self.half(family.blk[m - 1].at[self.kept_at], bit_of(self.dp, 0))
            else:
                own = self.half(family.dp[bit - 1].at[self.kept_at], 0)
            into = got
            if stage == self.last - 1:
                into = self.half(family.out.at[self.kept_at], bit_of(self.dp, 0))
            self.add(into, got, own)

    def add(self, into, left, right):
        into[...] = left[...] + right[...]

    def drained(self, stages):
        for stage in stages:
            self.where(self.sends if self.middle else None, stage, lambda: self.copy(stage).wait_send())


def feed_forward_backward(at, level, gradient, ready, done):
    column = at.router[level:level + 1, :].astype(jnp.float32)
    active = as_column(at.depths[...]) > float(level)
    hidden = at.hid_level[...]
    chosen = jax.nn.sigmoid(jnp.sum(hidden * column, axis=1, keepdims=True))
    at.dbranch[...] = jnp.where(active, chosen, 0.0) * gradient
    dchosen = jnp.where(active, jnp.sum(gradient * at.branch_level[...], axis=1, keepdims=True), 0.0)
    dlogit = dchosen * chosen * (1.0 - chosen)
    at.small[2 + level:3 + level, :] = jnp.sum(hidden * dlogit, axis=0, keepdims=True)
    at.grad_hidden[...] = gradient + dlogit * column
    at.dffn[...] = at.dbranch[...].astype(low)

    ready(0)
    dinner = plain_dot(at.dffn[...], at.w_down[...])
    at.dgate[...] = (dinner * at.slope_level[...].astype(jnp.float32)).astype(low)
    at.dup[...] = (dinner * at.silu_level[...].astype(jnp.float32)).astype(low)
    done()
    at.dnorm_turned[...] = plain_dot(at.w_gate[...], at.dgate[...].T) + plain_dot(at.w_up[...], at.dup[...].T)
    ready(1)
    dnorm = at.dnorm_turned[...].T
    dmiddle, gain_share = norm_gradient(dnorm, at.middle_level[...], at.norms[1:2, :].astype(jnp.float32))
    at.small[1:2, :] += gain_share
    at.grad_hidden[...] += dmiddle
    dattn = (at.dbranch[...] + dmiddle).astype(low)
    lead = at.far.shape[1] - dattn.shape[1]
    at.far[:, :lead] = jnp.zeros((dattn.shape[0], lead), low)
    at.far[:, lead:] = dattn
    at.dat[...] = plain_dot(at.w_out[...], dattn.T).astype(low)


def forward_kernel(sizes, names, *refs):
    m, piece = sizes
    at = types.SimpleNamespace(**dict(zip(names, refs)))
    blk = lax.axis_index("blk")
    mine = block_bits(blk, m)
    kv, metas = at.kv, at.metas
    weights = (
        (at.w_query_hbm, at.w_query), (at.w_out_hbm, at.w_out), (at.w_gate_hbm, at.w_gate), (at.w_up_hbm, at.w_up), (at.w_down_hbm, at.w_down),
    )
    loads = [pltpu.make_async_copy(*pair, at.load_sems.at[index]) for index, pair in enumerate(weights)]
    kv_loads = kv_weight_loads(at.key_weight_hbm, at.value_weight_hbm, at.kv_weight, at.weight_sems)
    for load in kv_loads + loads:
        load.start()
    saved = (
        (at.normed, at.normed_out), (at.turned, at.turned_out), (kv, at.kv_out), (at.lse, at.lse_out),
        (at.att, at.att_out), (at.nffn, at.nffn_out), (at.inner, at.inner_out),
    )

    def save(index, level):
        return pltpu.make_async_copy(
            saved[index][0].at[level] if index == 2 else saved[index][0], saved[index][1].at[level], at.save_sems.at[index, level]
        )

    first = (
        (at.hid.at[0], at.hid_out), (at.middle, at.middle_out), (at.silu, at.silu_out),
        (at.slope, at.slope_out), (at.branch, at.branch_out), (metas, at.metas_out),
        (at.far, at.far_out), (at.dat, at.dat_out), (at.dffn, at.dffn_out), (at.dgate, at.dgate_out), (at.dup, at.dup_out),
        (at.hid.at[1], at.hid_1_out),
    )
    late = [pltpu.make_async_copy(*pair, at.late_sems.at[index]) for index, pair in enumerate(first)]
    segment_row = at.segments[...].astype(jnp.float32)
    depth_column = as_column(at.depths[...])
    metas[mine] = jnp.concatenate(
        [segment_row, at.depths[...].astype(jnp.float32), jnp.zeros((6, piece), jnp.float32)], axis=0
    )
    greet([{"blk": flipped(blk, bit)} for bit in range(m)])

    def place(known):
        return tuple(slice(None) if bit in known else mine[m - 1 - bit] for bit in range(m - 1, -1, -1))

    orders = (list(range(1, m)), list(range(m - 1, 0, -1)))
    kv_sems = (at.kv_send, at.kv_recv)

    def kv_copies(level, group, stage):
        if stage == m - 1:
            ref = kv.at[(level, group, *place(range(1, m)))]
            return [remote(ref, ref, kv_sems, (level, group, 2 * stage), {"blk": flipped(blk, 0)})]
        copies = []
        for side, order in enumerate(orders):
            rows = pl.ds(side * (piece // 2), piece // 2)
            ref = kv.at[(level, group, *place(order[:stage]), rows)]
            copies.append(remote(ref, ref, kv_sems, (level, group, 2 * stage + side), {"blk": flipped(blk, order[stage])}))
        return copies

    def kv_advance(level, group, stage):
        if stage > 0:
            for copy in kv_copies(level, group, stage - 1):
                copy.wait_recv()
        if stage < m:
            for copy in kv_copies(level, group, stage):
                copy.start()

    def meta_copy(stage):
        bits = list(range(1, m)) + [0]
        ref = metas.at[place(bits[:stage])]
        return remote(ref, ref, (at.meta_send, at.meta_recv), stage, {"blk": flipped(blk, bits[stage])})

    meta_copy(0).start()
    cosine, sine = at.cosines[...], at.sines[...]
    gain_attn, gain_ffn = at.norms[0:1, :].astype(jnp.float32), at.norms[1:2, :].astype(jnp.float32)
    routers = at.router[...].astype(jnp.float32)
    at.hid[0] = at.tokens[...].T.astype(jnp.float32)
    late[0].start()
    at.query_pad[HEAD_DIMENSION:, :] = jnp.zeros_like(at.query_pad[HEAD_DIMENSION:, :])

    @pl.loop(0, RECUR)
    def _(level):
        @pl.when(level > 0)
        def _():
            for index in range(5):
                save(index, 0).wait()

        hidden = at.hid[level]
        at.flat[...] = (hidden * rms_scale(hidden) * gain_attn).astype(low)
        at.normed[...] = at.flat[...].T

        @pl.when(level == 0)
        def _():
            for load in kv_loads:
                load.wait()

        both = turn_keys(plain_dot(at.kv_weight[...], at.normed[...]), cosine, sine).T.astype(low)
        for group in range(KEY_VALUE_HEADS):
            kv[(level, group, *mine)] = both[:, group * PAIR:(group + 1) * PAIR]
            kv_advance(level, group, 0)

        @pl.when(level == 0)
        def _():
            loads[0].wait()
            for stage in range(1, m - 1):
                meta_copy(stage - 1).wait_recv()
                meta_copy(stage).start()

        queries = turn_heads(plain_dot(at.flat[...], at.w_query[...]).T, cosine, sine, QUERY_HEADS)
        at.turned[...] = (queries * HEAD_DIMENSION ** (-0.5)).astype(low)

        @pl.when(level == 0)
        def _():
            for stage in range(max(1, m - 1), m):
                meta_copy(stage - 1).wait_recv()
                meta_copy(stage).start()

        for stage in range(1, m - 1):
            for group in range(KEY_VALUE_HEADS):
                kv_advance(level, group, stage)
        kv_advance(level, 0, m - 1)

        @pl.when(level == 0)
        def _():
            meta_copy(m - 1).wait_recv()
            late[5].start()

        fill_bias(at.bias, metas, segment_row, level.astype(jnp.float32), blk, m, piece, SPAN)

        @pl.loop(0, KEY_VALUE_HEADS)
        def _(group):
            @pl.when(group + 1 < KEY_VALUE_HEADS)
            def _():
                kv_advance(level, group + 1, m - 1)

            kv_advance(level, group, m)
            for member in range(HEAD_SHARE):
                at.query_pad[:HEAD_DIMENSION, member * piece:(member + 1) * piece] = at.turned[head_rows(group, member), :]
            at.top[...] = jnp.full_like(at.top, masked_score)
            at.total[...] = jnp.zeros_like(at.total)

            @pl.loop(0, key_steps(blk, SPAN))
            def _(index):
                step = key_steps(blk, SPAN) - 1 - index
                rows = kv[(level, group, *block_bits(step, m - SPAN))].reshape((1 << SPAN) * piece, PAIR)
                scores = plain_dot(rows, at.query_pad[...]) + step_bias(at.bias, step, piece, SPAN)
                before = at.top[0:1, :]
                after = jnp.maximum(before, jnp.max(scores, axis=0, keepdims=True))
                raised = jnp.exp(scores - after)
                shrink = jnp.exp(before - after)
                at.top[0:1, :] = after
                ones = jnp.ones((16, rows.shape[0]), low)
                left = jnp.concatenate([rows.T[HEAD_DIMENSION:], ones], axis=0)
                at.total[...] = at.total[...] * shrink + plain_dot(left, raised.astype(low))

            sums = at.total[HEAD_DIMENSION:HEAD_DIMENSION + 1, :]
            at.lse[pl.ds(group, 1), :] = at.top[0:1, :] + jnp.log(sums)
            out = at.total[:HEAD_DIMENSION, :] / sums
            for member in range(HEAD_SHARE):
                at.att[head_rows(group, member), :] = out[:, member * piece:(member + 1) * piece].astype(low)

        for index in range(5):
            save(index, level).start()

        @pl.when(level == 0)
        def _():
            loads[1].wait()

        @pl.when(level > 0)
        def _():
            save(5, 0).wait()
            save(6, 0).wait()
            for copy in late[1:5]:
                copy.wait()

        attn = plain_dot(at.att[...].T, at.w_out[...])
        mid = at.hid[level] + attn
        at.middle[...] = mid
        at.branch[...] = attn
        at.flat[...] = (mid * rms_scale(mid) * gain_ffn).astype(low)
        at.nffn[...] = at.flat[...].T
        save(5, level).start()

        @pl.when(level == 0)
        def _():
            loads[2].wait()
            loads[3].wait()

        gate_pre = plain_dot(at.flat[...], at.w_gate[...])
        up_pre = plain_dot(at.flat[...], at.w_up[...])
        opened = jax.nn.sigmoid(gate_pre)
        passed = gate_pre * opened
        at.silu[...] = passed.astype(low)
        at.slope[...] = (up_pre * (opened + passed - passed * opened)).astype(low)
        at.inner[...] = (passed * up_pre).astype(low).T
        save(6, level).start()

        @pl.when(level == 0)
        def _():
            loads[4].wait()

        at.branch[...] += plain_dot(at.w_down[...], at.inner[...]).T
        column = jnp.where(level == 0, routers[0:1, :], routers[1:2, :])
        logit = jnp.sum(at.hid[level] * column, axis=1, keepdims=True)
        weight = jnp.where(depth_column > level.astype(jnp.float32), jax.nn.sigmoid(logit), 0.0)
        at.hid[level + 1] = at.hid[level] + weight * at.branch[...]

        @pl.when(level == 0)
        def _():
            for copy in late[1:5]:
                copy.start()

    at.hidden_out[...] = at.hid[RECUR].T
    top = RECUR - 1
    at.hid_level, at.branch_level, at.middle_level = at.hid.at[top], at.branch, at.middle
    at.silu_level, at.slope_level = at.silu, at.slope
    at.small[...] = jnp.zeros_like(at.small)
    feed_forward_backward(at, top, at.cotangent[...].T.astype(jnp.float32), lambda part: None, lambda: None)
    for copy in late[6:]:
        copy.start()
    for stage in range(m):
        meta_copy(stage).wait_send()
    for level in range(RECUR):
        for group in range(KEY_VALUE_HEADS):
            for stage in range(m):
                for copy in kv_copies(level, group, stage):
                    copy.wait_send()
    for index in range(len(saved)):
        save(index, RECUR - 1).wait()
    for copy in late[:1] + late[5:]:
        copy.wait()


def far_width(width):
    return 2 * width + 2 * KEYS_WIDTH - 1536


def forward(small, weights, nb):
    m = nb.bit_length() - 1
    width, piece = small["tokens"].shape
    hidden_units = weights["w_gate_hbm"].shape[1]
    blocks, wide = (2,) * m, HEAD_SHARE * piece
    rows, turned = ((piece, width), jnp.float32), ((RECUR, width, piece), low)
    hidden = ((piece, hidden_units), low)
    saved = dict(
        normed=turned, turned=turned, kv=((RECUR, KEY_VALUE_HEADS, *blocks, piece, PAIR), low),
        lse=((RECUR, 8, wide), jnp.float32), att=turned, nffn=turned, inner=((RECUR, hidden_units, piece), low),
        metas=((*blocks, 8, piece), jnp.float32), far=((piece, far_width(width)), low), dat=((width, piece), low),
        dffn=((piece, width), low), dgate=hidden, dup=hidden,
    )
    first = dict(hid=rows, middle=rows, silu=hidden, slope=hidden, branch=rows)
    outs = dict(hidden_out=((width, piece), jnp.float32), grad_hidden=rows, small=((8, width), jnp.float32))
    anywhere = {name + "_out": entry for name, entry in (saved | first | dict(hid_1=rows)).items()}
    single = {name: (shape[1:], dtype) for name, (shape, dtype) in saved.items() if shape[0] == RECUR and name not in ("kv", "metas")}
    buffers = {name[:-4]: (array.shape, array.dtype) for name, array in weights.items()} | saved | single | first | dict(
        kv_weight=((2 * KEYS_WIDTH, width), low),
        hid=((RECUR + 1, piece, width), jnp.float32), flat=((piece, width), low),
        bias=((nb, piece, piece), jnp.float32), query_pad=((PAIR, wide), low), top=((8, wide), jnp.float32),
        total=((HEAD_DIMENSION + 16, wide), jnp.float32), dbranch=rows, dnorm_turned=((width, piece), jnp.float32),
    )
    semaphores = dict(
        load_sems=(5,), weight_sems=(2 * KEY_VALUE_HEADS,), save_sems=(7, RECUR), late_sems=(12,), kv_send=(RECUR, KEY_VALUE_HEADS, 2 * m),
        kv_recv=(RECUR, KEY_VALUE_HEADS, 2 * m), meta_send=(m,), meta_recv=(m,),
    )
    results = pl.pallas_call(
        functools.partial(forward_kernel, (m, piece), (*small, *weights, *outs, *anywhere, *buffers, *semaphores)),
        out_shape=[shaped(entry) for entry in (outs | anywhere).values()],
        in_specs=[spec(pltpu.VMEM)] * len(small) + [spec(pl.ANY)] * len(weights),
        out_specs=[spec(pltpu.VMEM)] * len(outs) + [spec(pl.ANY)] * len(anywhere),
        scratch_shapes=spaces(buffers.values()) + dma_semaphores(*semaphores.values()),
        compiler_params=pltpu.CompilerParams(
            collective_id=1, has_side_effects=True, vmem_limit_bytes=VMEM_LIMIT
        ),
        cost_estimate=pl.CostEstimate(
            flops=3 * RECUR * piece * width * 10240, bytes_accessed=48 * 1024 * 1024, transcendentals=0
        ),
        name="forward_levels",
    )(*small.values(), *weights.values())
    return dict(zip((*outs, *(name[:-4] for name in anywhere)), results))


class AttentionBackward:
    def __init__(self, at, m, piece, level, span):
        self.at, self.m, self.piece, self.level, self.span = at, m, piece, level, span
        self.blk = lax.axis_index("blk")
        self.family = types.SimpleNamespace(part=at.part, blk=at.halves, dp=(), out=None, shape=(piece // 2, PAIR), split=0)

    def pieces(self, group):
        sems = (self.at.kv_send, self.at.kv_recv)
        return [
            Piece(2 * group + side, 2 * group + side, 2 * group + side, side, self.family, sems, (self.m, 0))
            for side in range(2)
        ]

    def move(self, group, stage):
        for piece_of in self.pieces(group):
            piece_of.finish(stage)
            if stage + 1 < self.m:
                piece_of.start(stage + 1)

    def begin(self):
        at = self.at
        query_segments = at.metas[block_bits(self.blk, self.m)][0:1, :]
        fill_bias(at.bias, at.metas, query_segments, float(self.level), self.blk, self.m, self.piece, self.span)
        at.query_pad[HEAD_DIMENSION:, :] = jnp.zeros_like(at.query_pad[HEAD_DIMENSION:, :])
        at.dat_pad[:HEAD_DIMENSION, :] = jnp.zeros_like(at.dat_pad[:HEAD_DIMENSION, :])

    def group(self, group):
        at, m, piece, blk = self.at, self.m, self.piece, self.blk
        half = piece // 2
        carried = []
        for member in range(HEAD_SHARE):
            rows, lanes = head_rows(group, member), slice(member * piece, (member + 1) * piece)
            at.query_pad[:HEAD_DIMENSION, lanes] = at.turned[rows, :]
            at.dat_pad[HEAD_DIMENSION:, lanes] = at.dat_turned[rows, :]
            product = at.dat_turned[rows, :].astype(jnp.float32) * at.att_turned[rows, :].astype(jnp.float32)
            carried.append(jnp.sum(product, axis=0, keepdims=True))
        carried = jnp.concatenate(carried, axis=1)
        at.query_rows[...] = at.query_pad[...].T
        at.dat_rows[...] = at.dat_pad[...].T
        log_total = at.lse[pl.ds(group, 1), :]
        at.dq_sum[...] = jnp.zeros_like(at.dq_sum)

        span, lead = self.span, m - self.span

        @pl.loop(0, key_steps(blk, span))
        def _(step):
            rows = at.kv[(group, *block_bits(step, lead))].reshape((1 << span) * piece, PAIR)
            probability = jnp.exp(plain_dot(rows, at.query_pad[...]) + step_bias(at.bias, step, piece, span) - log_total)
            dprob = plain_dot(rows, at.dat_pad[...])
            dscores = (probability * (dprob - carried)).astype(low)
            share = plain_dot(dscores, at.query_rows[...]) + plain_dot(probability.astype(low), at.dat_rows[...])
            share = share.astype(low)
            for block in range(1 << span):
                for side in range(2):
                    first = block * piece + side * half
                    place = (2 * group + side, *block_bits(step, lead), *bits_of(block, span))
                    at.part[place] = share[first:first + half]
            at.dq_sum[...] += plain_dot(rows.T[:HEAD_DIMENSION], dscores)

        @pl.loop(key_steps(blk, span), 1 << lead)
        def _(step):
            for block in range(1 << span):
                for side in range(2):
                    place = (2 * group + side, *block_bits(step, lead), *bits_of(block, span))
                    at.part[place] = jnp.zeros((half, PAIR), low)

        for piece_of in self.pieces(group):
            piece_of.start(0)
        for member in range(HEAD_SHARE):
            at.dq_turned[head_rows(group, member), :] = at.dq_sum[:, member * piece:(member + 1) * piece]

    def follow(self, group):
        for stage in range(self.m - 1):
            earlier = group - 1 - stage
            if isinstance(group, int):
                if 0 <= earlier < KEY_VALUE_HEADS:
                    self.move(earlier, stage)
            else:
                @pl.when(earlier >= 0)
                def _():
                    self.move(earlier, stage)

    def queries(self, cosine, sine):
        at = self.at
        dqueries = turn_back(at.dq_turned[...] * HEAD_DIMENSION ** (-0.5), cosine, sine, QUERY_HEADS).astype(low)
        self.put(2 * KEYS_WIDTH, dqueries.T)
        at.dnorm[...] = plain_dot(at.w_query[...], dqueries).T

    def put(self, column, values):
        self.at.near[:, column:column + values.shape[1]] = values

    def keys(self, cosine, sine):
        at, m = self.at, self.m
        filled = 2 * KEYS_WIDTH + QUERY_HEADS * HEAD_DIMENSION
        self.put(filled, jnp.zeros((self.piece, at.near.shape[1] - filled), low))
        sums = []
        for group in range(KEY_VALUE_HEADS):
            self.move(group, m - 1)
            sums.append(jnp.concatenate([at.halves[m - 1][2 * group], at.halves[m - 1][2 * group + 1]], axis=0))
        both = jnp.concatenate(sums, axis=1).astype(jnp.float32).T
        both = turn_keys(both, cosine, -sine).astype(low).T
        self.put(0, both)
        at.dnorm[...] += plain_dot(both, at.kv_weight[...])

    def drained(self):
        for group in range(KEY_VALUE_HEADS):
            for piece_of in self.pieces(group):
                piece_of.drained(range(1, self.m))


def attention_buffers(nb, piece, width, bias_type):
    m, wide, heads = nb.bit_length() - 1, HEAD_SHARE * piece, 2 * KEY_VALUE_HEADS
    turned = ((width, piece), low)
    pad, pad_rows = ((PAIR, wide), low), ((wide, PAIR), low)
    buffers = dict(
        turned=turned, dat_turned=turned, att_turned=turned, kv=((KEY_VALUE_HEADS, *(2,) * m, piece, PAIR), low),
        lse=((8, wide), jnp.float32), metas=((*(2,) * m, 8, piece), jnp.float32), w_query=((width, width), low),
        kv_weight=((2 * KEYS_WIDTH, width), low), dq_turned=((width, piece), jnp.float32),
        bias=((nb, piece, piece), bias_type), query_pad=pad, dat_pad=pad, query_rows=pad_rows, dat_rows=pad_rows,
        dq_sum=((HEAD_DIMENSION, wide), jnp.float32), part=((heads, *(2,) * m, piece // 2, PAIR), low),
        dnorm=((piece, width), jnp.float32), hid=((piece, width), jnp.float32),
    )
    for stage in range(m):
        buffers["half_%d" % stage] = ((heads, *(2,) * (m - 1 - stage), piece // 2, PAIR), low)
    return buffers


def backward_kernel(sizes, names, *refs):
    m, piece, level = sizes
    at = types.SimpleNamespace(**dict(zip(names, refs)))
    at.halves = [getattr(at, "half_%d" % stage) for stage in range(m)]
    at.near = at.near_out
    blk = lax.axis_index("blk")
    pairs = (
        (at.metas_hbm, at.metas), (at.turned_hbm.at[level], at.turned), (at.dat_hbm, at.dat_turned),
        (at.att_hbm.at[level], at.att_turned), (at.lse_hbm.at[level], at.lse), (at.kv_hbm.at[level], at.kv),
        (at.w_query_hbm, at.w_query),
        (at.grad_hbm, at.grad_hidden), (at.hid_1_hbm, at.hid),
        (at.hid_0_hbm, at.hid_level), (at.branch_hbm, at.branch_level), (at.w_down_hbm, at.w_down),
        (at.slope_hbm, at.slope_level), (at.silu_hbm, at.silu_level), (at.w_gate_hbm, at.w_gate), (at.w_up_hbm, at.w_up),
        (at.middle_hbm, at.middle_level), (at.w_out_hbm, at.w_out),
    )
    loads = [pltpu.make_async_copy(*pair, at.load_sems.at[index]) for index, pair in enumerate(pairs)]
    loads += kv_weight_loads(at.key_weight_hbm, at.value_weight_hbm, at.kv_weight, at.weight_sems)
    for load in loads:
        load.start()
    saves = [
        pltpu.make_async_copy(*pair, at.save_sems.at[index])
        for index, pair in enumerate(((at.dgate, at.dgate_out), (at.dup, at.dup_out)))
    ]
    greet([{"blk": flipped(blk, bit)} for bit in range(m)])
    work = AttentionBackward(at, m, piece, level, SPAN)
    loads[0].wait()
    work.begin()
    for load in loads[1:6]:
        load.wait()

    @pl.loop(0, KEY_VALUE_HEADS)
    def _(group):
        work.group(group)
        work.follow(group)

    cosine, sine = at.cosines[...], at.sines[...]
    for virtual in range(KEY_VALUE_HEADS, KEY_VALUE_HEADS + m - 1):
        work.follow(virtual)
        if virtual == KEY_VALUE_HEADS:
            loads[6].wait()
            work.queries(cosine, sine)
    for load in loads[7:]:
        load.wait()
    work.keys(cosine, sine)
    dhidden, gain_share = norm_gradient(at.dnorm[...], at.hid[...], at.norms[0:1, :].astype(jnp.float32))
    at.small[...] = at.small_before[...]
    at.small[0:1, :] = gain_share
    gradient = at.grad_hidden[...] + dhidden
    at.dnorm[...] = gradient
    feed_forward_backward(at, level - 1, at.dnorm[...], lambda part: None, lambda: [save.start() for save in saves])
    work.drained()
    for save in saves:
        save.wait()


def backward(level, small, operands, nb):
    m = nb.bit_length() - 1
    piece, width = operands["grad_hbm"].shape
    hidden_units = operands["w_gate_hbm"].shape[1]
    rows, flat, hidden = ((piece, width), jnp.float32), ((piece, width), low), ((piece, hidden_units), low)
    outs = dict(
        grad_hidden=rows, small=((8, width), jnp.float32), near_out=((piece, 1792), low), dffn=flat,
        dat=((width, piece), low), far=((piece, far_width(width)), low),
    )
    anywhere = dict(dgate_out=hidden, dup_out=hidden)
    buffers = attention_buffers(nb, piece, width, jnp.float32) | dict(
        hid_level=rows, branch_level=rows, middle_level=rows, w_down=((width, hidden_units), low), slope_level=hidden,
        silu_level=hidden, w_gate=((width, hidden_units), low), w_up=((width, hidden_units), low),
        w_out=((width, width), low), dbranch=rows, dnorm_turned=((width, piece), jnp.float32), dgate=hidden, dup=hidden,
    )
    sums = (2 * KEY_VALUE_HEADS, m + nb // 2)
    semaphores = dict(load_sems=(18,), weight_sems=(2 * KEY_VALUE_HEADS,), save_sems=(2,), kv_send=sums, kv_recv=sums)
    results = pl.pallas_call(
        functools.partial(
            backward_kernel, (m, piece, level), (*small, *operands, *outs, *anywhere, *buffers, *semaphores)
        ),
        out_shape=[shaped(entry) for entry in (outs | anywhere).values()],
        in_specs=[spec(pltpu.VMEM)] * len(small) + [spec(pl.ANY)] * len(operands),
        out_specs=[spec(pltpu.VMEM)] * len(outs) + [spec(pl.ANY)] * len(anywhere),
        scratch_shapes=spaces(buffers.values()) + dma_semaphores(*semaphores.values()),
        compiler_params=pltpu.CompilerParams(
            collective_id=2, has_side_effects=True, vmem_limit_bytes=VMEM_LIMIT
        ),
        cost_estimate=pl.CostEstimate(
            flops=2 * piece * width * 20000, bytes_accessed=32 * 1024 * 1024, transcendentals=0
        ),
        name="backward_level",
    )(*small.values(), *operands.values())
    return dict(zip((*outs, *anywhere), results))


WIDE_SLOTS, DOWN_SLOTS = 4, 2


def final_kernel(sizes, names, *refs):
    nb, m, n, piece, rows, padded, near_width = sizes
    at = types.SimpleNamespace(**dict(zip(names, refs)))
    at.halves = [getattr(at, "half_%d" % stage) for stage in range(m)]
    blk, dp = lax.axis_index("blk"), lax.axis_index("dp")
    at.near = at.gate_side.at[pl.ds(0, piece), pl.ds(0, near_width)]
    counter = itertools.count()

    def load(source, target):
        return pltpu.make_async_copy(source, target, at.load_sems.at[next(counter)])

    def both_lanes(ref, target):
        return [load(ref.at[level], target.at[:, pl.ds(level * piece, piece)]) for level in range(RECUR)]

    def both_rows(low_ref, deep_ref, target, width):
        pairs = ((low_ref, 0), (deep_ref, piece))
        return [load(ref, target.at[pl.ds(first, piece), pl.ds(0, width)]) for ref, first in pairs]

    hidden_units, width = at.gate_side.shape[1], at.dffn.shape[1]
    far_lanes = at.far_0_hbm.shape[1]
    loads = types.SimpleNamespace(
        nffn=both_lanes(at.nffn_hbm, at.left),
        dgate=both_rows(at.dgate_0_hbm, at.dgate_1_hbm, at.gate_side, hidden_units),
        inner=both_lanes(at.inner_hbm, at.inner),
        dffn=both_rows(at.dffn_0_hbm, at.dffn_1_hbm, at.dffn, width),
        metas=[load(at.metas_hbm, at.metas)],
        heads=[
            load(at.turned_hbm.at[0], at.turned), load(at.dat_hbm, at.dat_turned), load(at.att_hbm.at[0], at.att_turned),
            load(at.lse_hbm.at[0], at.lse), load(at.kv_hbm.at[0], at.kv),
        ],
        dup=both_rows(at.dup_0_hbm, at.dup_1_hbm, at.up_side, hidden_units),
        w_query=[load(at.w_query_hbm, at.w_query)],
        rest=[
            load(at.hid_hbm, at.hid), load(at.grad_hbm, at.grad),
        ],
        attended=both_lanes(at.attended_hbm, at.left_attended),
        kv_weight=kv_weight_loads(at.key_weight_hbm, at.value_weight_hbm, at.kv_weight, at.weight_sems),
    )
    late = types.SimpleNamespace(
        near=[load(at.near_1_hbm, at.gate_side.at[pl.ds(piece, piece), pl.ds(0, near_width)])],
        far=both_rows(at.far_0_hbm, at.far_1_hbm, at.up_side, far_lanes),
        normed=both_lanes(at.normed_hbm, at.left),
    )

    def begin(copies):
        for copy in copies:
            copy.start()

    def ready(copies):
        for copy in copies:
            copy.wait()

    for copies in vars(loads).values():
        begin(copies)
    greet([{"blk": flipped(blk, bit)} for bit in range(m)] + [{"dp": flipped(dp, bit)} for bit in range(n)])

    down_rows = at.part_down.shape[-2]

    def family(name, shape, split):
        return types.SimpleNamespace(
            part=getattr(at, "part_" + name), out=getattr(at, "out_" + name), shape=shape, split=split,
            blk=[getattr(at, "blk_%s_%d" % (name, stage)) for stage in range(m)],
            dp=[getattr(at, "dp_%s_%d" % (name, stage)) for stage in range(n)],
        )

    wide = family("wide", (2 * padded, UNIT_COLUMNS), 1)
    down = family("down", (down_rows, width), 0)
    little = family("small", (16, 128), 0)
    sems = (at.send_sems, at.recv_sems)
    units = itertools.count()

    def unit(holder, index, flavour, halves=n != 2):
        return Piece(next(units), index, index % holder.part.shape[0], flavour, holder, sems, (m, n), not halves)

    pairs = [[unit(wide, index, 0), unit(down, index, 1)] for index in range(5)]
    pairs += [[unit(wide, index, 0), unit(wide, index + 1, 1)] for index in (5, 7, 9)]
    pairs += [[unit(wide, 11, 0, True), unit(wide, 12, 1, True)]]
    pairs += [[unit(wide, 13, 0, True), unit(wide, 14, 1, True), unit(little, 0, 0, True)]]

    def compute_wide(index, slot):
        if index == 0:
            ready(loads.nffn)
            ready(loads.dgate)
        if index == 5:
            begin(late.near)
            ready(loads.dup)
        if index == 10:
            begin(late.far)
            begin(late.normed)
            ready(late.near)
            ready(late.normed)
            ready(loads.attended)
            ready(late.far)
        block, column = index // 5, (index % 5) * UNIT_COLUMNS
        second = 1280 + column
        upper_columns, lower_columns = slice(column, column + UNIT_COLUMNS), slice(second, second + UNIT_COLUMNS)
        if block < 2:
            right = at.gate_side if block == 0 else at.up_side
            upper = plain_dot(at.left[...], right[:, upper_columns])
            lower = plain_dot(at.left[...], right[:, lower_columns])
        else:
            upper = plain_dot(at.left[...], at.gate_side[:, upper_columns])
            lower = None
            if second < 1600:
                lower = plain_dot(at.left[...], at.gate_side[:, lower_columns])
            if second >= 1536:
                more = plain_dot(at.left_attended[...], at.up_side[:, second - 1536:second - 1536 + UNIT_COLUMNS])
                lower = more if lower is None else lower + more
        for target in range(nb):
            here = slice(target * padded, (target + 1) * padded)
            both = jnp.concatenate([upper[here], lower[here]], axis=0)
            at.part_wide[(slot, *bits_of(target, m))] = both.astype(low)

    def compute_down(index, slot):
        if index == 0:
            ready(loads.inner)
            ready(loads.dffn)
        firsts = [(target * 5 + index) * down_rows for target in range(nb)]
        left = jnp.concatenate([at.inner[first:first + down_rows, :] for first in firsts], axis=0)
        result = plain_dot(left, at.dffn[...])
        for target in range(nb):
            at.part_down[(slot, *bits_of(target, m))] = result[target * down_rows:(target + 1) * down_rows].astype(low)

    def compute_small():
        total = at.small_before[...]
        total = total + jnp.concatenate([at.gain_row[...], jnp.zeros((7, width), jnp.float32)], axis=0)
        at.part_small[...] = jnp.zeros_like(at.part_small)
        for target in range(nb):
            at.part_small[(0, *bits_of(target, m), slice(0, 8), slice(0, rows))] = total[:, target * rows:(target + 1) * rows]

    def compute(piece_of):
        if piece_of.family is wide:
            compute_wide(piece_of.kept_at, piece_of.slot)
        elif piece_of.family is down:
            compute_down(piece_of.kept_at, piece_of.slot)
        else:
            compute_small()
        piece_of.start(0)

    def moves(tick):
        for stage in range(m + n - 1, -1, -1):
            if 0 <= tick - stage < len(pairs):
                for piece_of in pairs[tick - stage]:
                    piece_of.finish(stage)
                    piece_of.start(stage + 1)

    work = AttentionBackward(at, m, piece, 0, 1)
    for pair in pairs[:2]:
        for piece_of in pair:
            compute(piece_of)
    ready(loads.metas)
    work.begin()
    ready(loads.heads)
    for group in range(KEY_VALUE_HEADS):
        moves(group)
        for piece_of in pairs[group + 2]:
            compute(piece_of)
        work.group(group)
        work.follow(group)
    cosine, sine = at.cosines[...], at.sines[...]
    moves(5)
    compute(pairs[7][0])
    ready(loads.w_query)
    for virtual in range(KEY_VALUE_HEADS, KEY_VALUE_HEADS + m - 1):
        work.follow(virtual)
        if virtual == KEY_VALUE_HEADS:
            work.queries(cosine, sine)
    moves(6)
    ready(loads.rest)
    ready(loads.kv_weight)
    work.keys(cosine, sine)
    compute(pairs[7][1])
    moves(7)
    for piece_of in pairs[8] + pairs[9][:2]:
        compute(piece_of)
    dhidden, gain_share = norm_gradient(at.dnorm[...], at.hid[...], at.norms[0:1, :].astype(jnp.float32))
    at.gain_row[...] = gain_share
    at.grad_out[...] = (at.grad[...] + dhidden).T
    compute(pairs[9][2])
    for tick in range(8, len(pairs) + m + n - 1):
        moves(tick)
    for pair in pairs:
        for piece_of in pair:
            piece_of.finish(m + n)
    for pair in pairs:
        for piece_of in pair:
            piece_of.drained(range(1, m + n + 1))
    work.drained()


def unpack_kernel(sizes, wide_hbm, down_hbm, little_hbm, hidden_in, gradient_in, *refs):
    rows, padded = sizes
    norm_attn, norm_ffn, query, key, value, out, gate, up, down_out, router, hidden, gradient = refs[:12]
    wide, down, little, rest, sems = refs[12:]
    carried = [
        pltpu.make_async_copy(source, target, sems.at[at])
        for at, (source, target) in enumerate(((hidden_in, hidden), (gradient_in, gradient)))
    ]
    loads = [
        pltpu.make_async_copy(source, target, sems.at[2 + at])
        for at, (source, target) in enumerate(((wide_hbm, wide), (down_hbm, down), (little_hbm, little)))
    ]
    for copy in loads + carried:
        copy.start()
    for load in loads:
        load.wait()
    norm_attn[...] = little[0, 0:1, :rows]
    norm_ffn[...] = little[0, 1:2, :rows]
    router[...] = little[0, 2:4, :rows]
    for unit in range(5):
        for first, target in ((0, gate), (5, up), (10, rest)):
            tile = wide[first + unit].astype(jnp.float32)
            for side in range(2):
                column = side * 1280 + unit * UNIT_COLUMNS
                target[:, column:column + UNIT_COLUMNS] = tile[side * padded:side * padded + rows]
        down_rows = down.shape[1]
        down_out[unit * down_rows:(unit + 1) * down_rows, :] = down[unit].astype(jnp.float32)
    width = query.shape[1]
    both = rest[:, :2 * KEYS_WIDTH].T
    for group in range(KEY_VALUE_HEADS):
        here, first = slice(group * HEAD_DIMENSION, (group + 1) * HEAD_DIMENSION), group * PAIR
        key[here, :] = both[first:first + HEAD_DIMENSION]
        value[here, :] = both[first + HEAD_DIMENSION:first + PAIR]
    query[...] = rest[:, 2 * KEYS_WIDTH:2 * KEYS_WIDTH + width]
    out[...] = rest[:, 2 * KEYS_WIDTH + width:]
    for copy in carried:
        copy.wait()


def final(small, saved, top, bottom, weights, mesh_sizes):
    nb, nd = mesh_sizes
    m, n = nb.bit_length() - 1, nd.bit_length() - 1
    grad = bottom["grad_hidden"]
    piece, width = grad.shape
    hidden_units = weights["w_gate_hbm"].shape[1]
    rows = width // nb
    padded = -(-rows // 8) * 8
    down_rows = hidden_units // nb // 5
    tokens = RECUR * piece

    def spread(array):
        if padded == rows:
            return array
        split = array.reshape(RECUR, nb, rows, piece)
        return jnp.pad(split, ((0, 0), (0, 0), (0, padded - rows), (0, 0))).reshape(RECUR, nb * padded, piece)

    inputs = small | dict(small_before=bottom["small"])
    operands = dict(
        metas_hbm=saved["metas"], turned_hbm=saved["turned"], dat_hbm=bottom["dat"], att_hbm=saved["att"],
        lse_hbm=saved["lse"], kv_hbm=saved["kv"], w_query_hbm=weights["w_query_hbm"],
        key_weight_hbm=weights["key_weight_hbm"], value_weight_hbm=weights["value_weight_hbm"], hid_hbm=saved["hid"],
        grad_hbm=grad, inner_hbm=saved["inner"], nffn_hbm=spread(saved["nffn"]), normed_hbm=spread(saved["normed"]),
        attended_hbm=spread(saved["att"]), dffn_0_hbm=bottom["dffn"], dffn_1_hbm=top["dffn"],
        dgate_0_hbm=bottom["dgate_out"], dgate_1_hbm=top["dgate"], dup_0_hbm=bottom["dup_out"], dup_1_hbm=top["dup"],
        far_0_hbm=bottom["far"], far_1_hbm=top["far"], near_1_hbm=bottom["near_out"],
    )
    near_width = bottom["near_out"].shape[1]
    families = (
        ("wide", 15, (2 * padded, UNIT_COLUMNS), low, WIDE_SLOTS, 1), ("down", 5, (down_rows, width), low, DOWN_SLOTS, 0),
        ("small", 1, (16, 128), jnp.float32, 1, 0),
    )
    outs = dict(grad_out=((width, piece), jnp.float32))
    buffers = attention_buffers(nb, piece, width, low) | dict(
        grad=((piece, width), jnp.float32), gate_side=((tokens, hidden_units), low), up_side=((tokens, hidden_units), low),
        inner=((hidden_units, tokens), low), left=((nb * padded, tokens), low), left_attended=((nb * padded, tokens), low),
        dffn=((tokens, width), low), gain_row=((1, width), jnp.float32),
    )
    for name, count, shape, dtype, slots, split in families:
        outs["out_" + name] = ((count, *shape), dtype)
        buffers["part_" + name] = ((slots, *(2,) * m, *shape), dtype)
        for stage in range(m):
            buffers["blk_%s_%d" % (name, stage)] = ((count, *(2,) * (m - 1 - stage), *shape), dtype)
        for stage in range(n):
            buffers["dp_%s_%d" % (name, stage)] = ((count, *shape), dtype)
    sums, hops = (2 * KEY_VALUE_HEADS, m + nb // 2), (21, m + n + nb // 2)
    semaphores = dict(load_sems=(32,), weight_sems=(2 * KEY_VALUE_HEADS,), kv_send=sums, kv_recv=sums, send_sems=hops, recv_sems=hops)
    names = (*inputs, *operands, *outs, *buffers, *semaphores)
    gradient, wide, down, little = pl.pallas_call(
        functools.partial(final_kernel, (nb, m, n, piece, rows, padded, near_width), names),
        out_shape=[shaped(entry) for entry in outs.values()],
        in_specs=[spec(pltpu.VMEM)] * len(inputs) + [spec(pl.ANY)] * len(operands),
        out_specs=[spec(pltpu.VMEM)] * len(outs),
        scratch_shapes=spaces(buffers.values()) + dma_semaphores(*semaphores.values()),
        compiler_params=pltpu.CompilerParams(
            collective_id=0, has_side_effects=True, vmem_limit_bytes=VMEM_LIMIT
        ),
        cost_estimate=pl.CostEstimate(
            flops=2 * tokens * width * 14000, bytes_accessed=30 * 1024 * 1024, transcendentals=0
        ),
        name="weight_grads",
    )(*inputs.values(), *operands.values())
    shapes = (
        (1, rows), (1, rows), (rows, width), (KEYS_WIDTH, rows), (KEYS_WIDTH, rows), (rows, width),
        (rows, hidden_units), (rows, hidden_units), (5 * down_rows, width), (2, rows), (width, piece), (width, piece),
    )
    outs = pl.pallas_call(
        functools.partial(unpack_kernel, (rows, padded)),
        out_shape=[jax.ShapeDtypeStruct(shape, jnp.float32) for shape in shapes],
        in_specs=[spec(pl.ANY)] * 5,
        out_specs=[spec(pltpu.VMEM)] * 12,
        scratch_shapes=[pltpu.VMEM(array.shape, array.dtype) for array in (wide, down, little)]
        + spaces([((rows, 2560), jnp.float32)]) + dma_semaphores((5,)),
        compiler_params=pltpu.CompilerParams(vmem_limit_bytes=VMEM_LIMIT),
        name="unpack",
    )(wide, down, little, saved["hidden_out"], gradient)
    norm_a, norm_f, query, key, value, out, gate, up, down, router, hidden, gradient = outs
    return (
        hidden.T[None], gradient.T[None], norm_a[0], norm_f[0], query, key.T, value.T, out, gate, up, down, router.T,
    )


def local(
    tokens,
    depths,
    segments,
    norm_attn,
    norm_ffn,
    w_query,
    key_weight,
    value_weight,
    w_out,
    w_gate,
    w_up,
    w_down,
    w_router,
    cotangent,
    mesh_sizes,
):
    piece = tokens.shape[1]
    positions = lax.axis_index("blk") * piece + jnp.arange(piece, dtype=jnp.int32)
    angles = frequencies(HEAD_DIMENSION)[:, None] * positions.astype(jnp.float32)[None, :]
    tables = dict(cosines=jnp.cos(angles), sines=jnp.sin(angles), norms=jnp.stack([norm_attn, norm_ffn]))
    routing = dict(router=w_router.T, depths=depths)
    heads = dict(w_query_hbm=w_query, key_weight_hbm=key_weight.T, value_weight_hbm=value_weight.T)
    weights = heads | dict(w_out_hbm=w_out, w_gate_hbm=w_gate, w_up_hbm=w_up, w_down_hbm=w_down.T)
    nb = mesh_sizes[0]
    saved = forward(
        tables | routing | dict(tokens=tokens[0].T, cotangent=cotangent[0].T, segments=segments), weights, nb
    )
    operands = dict(
        metas_hbm=saved["metas"], turned_hbm=saved["turned"], dat_hbm=saved["dat"], att_hbm=saved["att"],
        lse_hbm=saved["lse"], kv_hbm=saved["kv"], grad_hbm=saved["grad_hidden"], hid_1_hbm=saved["hid_1"],
        hid_0_hbm=saved["hid"], branch_hbm=saved["branch"], slope_hbm=saved["slope"], silu_hbm=saved["silu"],
        middle_hbm=saved["middle"],
    )
    bottom = backward(1, tables | routing | dict(small_before=saved["small"]), weights | operands, nb)
    return final(tables, saved, saved, bottom, weights, mesh_sizes)


def solution(mesh):
    sizes = (mesh.shape["blk"], mesh.shape["dp"])
    return jax.shard_map(
        functools.partial(local, mesh_sizes=sizes),
        mesh=mesh,
        in_specs=(
            P("dp", "blk", None),
            P("dp", "blk"),
            P("dp", "blk"),
            P(),
            P(),
            P(),
            P(),
            P(),
            P(),
            P(),
            P(),
            P(),
            P(),
            P("dp", "blk", None),
        ),
        out_specs=(
            P("dp", "blk", None),
            P("dp", "blk", None),
            P("blk"),
            P("blk"),
            P("blk", None),
            P("blk", None),
            P("blk", None),
            P("blk", None),
            P("blk", None),
            P("blk", None),
            P("blk", None),
            P("blk", None),
        ),
        check_vma=False,
    )
```

```python
import functools
import itertools
import math
import types

import jax
import jax.numpy as jnp
from jax import lax
from jax.experimental import pallas as pl
from jax.experimental.pallas import tpu as pltpu
from jax.sharding import PartitionSpec as P

QUERY_HEADS = 15
KEY_VALUE_HEADS = 5
HEAD_DIMENSION = 64
RECUR = 2
HEAD_SHARE = QUERY_HEADS // KEY_VALUE_HEADS
KEYS_WIDTH = KEY_VALUE_HEADS * HEAD_DIMENSION
PAIR = 2 * HEAD_DIMENSION
UNIT_COLUMNS = 256
SPAN = 2
VMEM_LIMIT = 63 * 1024 * 1024

epsilon = 1e-05
masked_score = -1e30
low = jnp.bfloat16


def frequencies(head_size):
    return jnp.exp(
        jnp.arange(head_size // 2, dtype=jnp.float32) * (-2.0 * math.log(10000.0) / head_size)
    )


def rms_scale(values):
    return lax.rsqrt(jnp.mean(values * values, axis=-1, keepdims=True) + epsilon)


def norm_gradient(grad_norm, values, gain):
    scale = rms_scale(values)
    weighted = grad_norm * gain
    grad_values = scale * weighted - values * (scale * scale * scale) * jnp.mean(
        weighted * values, axis=-1, keepdims=True
    )
    return grad_values, jnp.sum(grad_norm * values * scale, axis=0, keepdims=True)


def dot_last(left, right):
    return lax.dot_general(left, right, (((1,), (1,)), ((), ())), preferred_element_type=jnp.float32)


def plain_dot(left, right):
    return jnp.dot(left, right, preferred_element_type=jnp.float32)


def bits_of(number, count):
    return tuple((number >> (count - 1 - at)) & 1 for at in range(count))


def bit_of(position, bit):
    return lax.rem(position // (1 << bit), 2)


def block_bits(block, m):
    return tuple(bit_of(block, bit) for bit in range(m - 1, -1, -1))


def flipped(position, bit):
    return position + (1 << bit) * (1 - 2 * bit_of(position, bit))


def remote(source, target, sems, at, device):
    return pltpu.make_async_remote_copy(
        src_ref=source,
        dst_ref=target,
        send_sem=sems[0].at[at],
        recv_sem=sems[1].at[at],
        device_id=device,
        device_id_type=pl.DeviceIdType.MESH,
    )


def greet(partners):
    barrier = pltpu.get_barrier_semaphore()
    for partner in partners:
        pl.semaphore_signal(barrier, inc=1, device_id=partner, device_id_type=pl.DeviceIdType.MESH)
    pl.semaphore_wait(barrier, len(partners))


def turn_heads(turned, cosine, sine, heads):
    split = turned.reshape(heads, 2, HEAD_DIMENSION // 2, turned.shape[1])
    first, second = split[:, 0], split[:, 1]
    both = jnp.stack([first * cosine - second * sine, second * cosine + first * sine], axis=1)
    return both.reshape(turned.shape)


def turn_back(turned, cosine, sine, heads):
    return turn_heads(turned, cosine, -sine, heads)


def head_rows(group, member):
    head = group * HEAD_SHARE + member
    return pl.ds(pl.multiple_of(head * HEAD_DIMENSION, HEAD_DIMENSION), HEAD_DIMENSION)


def as_column(row):
    wide = jnp.broadcast_to(row.astype(jnp.float32), (8, row.shape[1]))
    return wide.T[:, 0:1]


def key_steps(blk, span):
    return blk // (1 << span) + 1


def fill_bias(bias, metas, query_segments, level, blk, m, piece, span):
    many = 1 << span
    key_at = lax.broadcasted_iota(jnp.int32, (many * piece, piece), 0)
    query_at = lax.broadcasted_iota(jnp.int32, (many * piece, piece), 1)

    @pl.loop(0, key_steps(blk, span))
    def _(step):
        rows = metas[block_bits(step, m - span)].reshape(many, 8, piece)
        columns = jnp.concatenate([rows[block].T for block in range(many)], axis=0)
        live = jnp.where(columns[:, 1:2] > level, columns[:, 0:1], -1.0)
        shift = (blk - many * step) * piece
        allowed = (live == query_segments) & (key_at <= query_at + shift) | (key_at == query_at + shift)
        masked = jnp.where(allowed, 0.0, masked_score).astype(bias.dtype)
        bias[pl.ds(many * step, many)] = masked.reshape(many, piece, piece)


def step_bias(bias, step, piece, span):
    many = 1 << span
    here = bias[pl.ds(many * step, many)].reshape(many * piece, piece).astype(jnp.float32)
    return jnp.concatenate([here] * HEAD_SHARE, axis=1)


def kv_weight_loads(key_hbm, value_hbm, target, sems):
    copies = []
    for group in range(KEY_VALUE_HEADS):
        for side, source in enumerate((key_hbm, value_hbm)):
            rows = pl.ds(group * HEAD_DIMENSION, HEAD_DIMENSION)
            place = pl.ds(group * PAIR + side * HEAD_DIMENSION, HEAD_DIMENSION)
            copies.append(pltpu.make_async_copy(source.at[rows], target.at[place], sems.at[2 * group + side]))
    return copies


def turn_keys(both, cosine, sine):
    half = HEAD_DIMENSION // 2
    split = both.reshape(KEY_VALUE_HEADS, 4, half, both.shape[1])
    first, second = split[:, 0], split[:, 1]
    turned = [first * cosine - second * sine, second * cosine + first * sine, split[:, 2], split[:, 3]]
    return jnp.stack(turned, axis=1).reshape(both.shape)


def spec(memory):
    return pl.BlockSpec(memory_space=memory)


def shaped(entry):
    return jax.ShapeDtypeStruct(*entry)


def spaces(entries):
    return [pltpu.VMEM(*entry) for entry in entries]


def dma_semaphores(*shapes):
    return [pltpu.SemaphoreType.DMA(shape) for shape in shapes]


class Piece:
    def __init__(self, at, kept_at, slot, flavour, family, sems, bits, middle=False):
        self.at, self.kept_at, self.slot, self.family, self.sems = at, kept_at, slot, family, sems
        self.m, self.n = bits
        rising = list(range(1, self.m))
        bits_in_turn = ([0] + rising, [0] + rising[::-1], [1, 0] + rising[1:], [self.m - 1, 0] + rising[-2::-1])[flavour]
        left = list(range(self.m - 1, -1, -1))
        self.order = []
        for bit in bits_in_turn:
            place = left.index(bit)
            left.pop(place)
            self.order.append((bit, place, len(left)))
        self.last = self.m + self.n
        self.blk = lax.axis_index("blk")
        self.dp = lax.axis_index("dp") if self.n else None
        self.middle, self.stages = middle, self.last + 1
        if middle:
            inner = bit_of(self.dp, 0) != bit_of(self.dp, 1)
            outer = jnp.logical_not(inner)
            self.sends, self.receives = (outer, inner, inner), (inner, inner, outer)

    def half(self, ref, side):
        size = self.family.shape[self.family.split] // 2
        here = pl.ds(0 if isinstance(side, int) else pl.multiple_of(side * size, size), size)
        return ref.at[here, :] if self.family.split == 0 else ref.at[:, here]

    def held(self, stage):
        if stage == 0:
            return self.family.part, self.slot
        return self.family.blk[stage - 1], self.kept_at

    def copy(self, stage):
        m, family = self.m, self.family
        if stage < m:
            bit, place, others = self.order[stage]
            ref, index = self.held(stage)
            chosen = [slice(None)] * (others + 1)
            chosen[place] = 1 - bit_of(self.blk, bit)
            source = ref.at[(index, *chosen)]
            target = family.blk[stage].at[self.kept_at]
            device = {"blk": flipped(self.blk, bit)}
        elif self.middle:
            source, target, device = (
                (family.blk[m - 1], family.dp[0], {"dp": flipped(self.dp, 0)}),
                (family.dp[0], family.dp[1], {"dp": 3 - self.dp}),
                (family.out, family.out, {"dp": flipped(self.dp, 0)}),
            )[stage - m]
            source, target = source.at[self.kept_at], target.at[self.kept_at]
        elif stage < self.last:
            bit = stage - m
            if bit == 0:
                source = self.half(family.blk[m - 1].at[self.kept_at], 1 - bit_of(self.dp, 0))
            else:
                source = self.half(family.dp[bit - 1].at[self.kept_at], 0)
            target = self.half(family.dp[bit].at[self.kept_at], 0)
            device = {"dp": flipped(self.dp, bit)}
        else:
            source = self.half(family.out.at[self.kept_at], bit_of(self.dp, 0))
            target = source
            device = {"dp": flipped(self.dp, 0)}
        return remote(source, target, self.sems, (self.at, stage), device)

    def where(self, roles, stage, body):
        if self.middle and stage >= self.m:
            pl.when(roles[stage - self.m])(body)
        else:
            body()

    def start(self, stage):
        self.where(self.sends if self.middle else None, stage, lambda: self.copy(stage).start())

    def finish(self, stage):
        self.where(self.receives if self.middle else None, stage, lambda: self.receive(stage))

    def receive(self, stage):
        m, family = self.m, self.family
        self.copy(stage).wait_recv()
        if stage < m:
            bit, place, others = self.order[stage]
            ref, index = self.held(stage)
            for combo in itertools.product(range(2), repeat=others):
                chosen = list(combo)
                chosen.insert(place, bit_of(self.blk, bit))
                into = family.blk[stage].at[(self.kept_at, *combo)]
                self.add(into, into, ref.at[(index, *chosen)])
            if stage == 0:
                self.copy(0).wait_send()
        elif stage < self.last and self.middle:
            kept, sums = self.kept_at, family.dp
            if stage == m:
                self.add(sums[0].at[kept], sums[0].at[kept], family.blk[m - 1].at[kept])
            else:
                self.add(family.out.at[kept], sums[0].at[kept], sums[1].at[kept])
        elif stage < self.last:
            bit = stage - m
            got = self.half(family.dp[bit].at[self.kept_at], 0)
            if bit == 0:
                own = self.half(family.blk[m - 1].at[self.kept_at], bit_of(self.dp, 0))
            else:
                own = self.half(family.dp[bit - 1].at[self.kept_at], 0)
            into = got
            if stage == self.last - 1:
                into = self.half(family.out.at[self.kept_at], bit_of(self.dp, 0))
            self.add(into, got, own)

    def add(self, into, left, right):
        into[...] = left[...] + right[...]

    def drained(self, stages):
        for stage in stages:
            self.where(self.sends if self.middle else None, stage, lambda: self.copy(stage).wait_send())


class EarlyPiece(Piece):
    def __init__(self, *parts):
        super().__init__(*parts)
        self.stages = 7

    def quarter(self, ref, bit, side):
        size = self.family.shape[0] // (2 << bit)
        here = pl.ds(pl.multiple_of(side * size, size), size)
        return ref.at[(slice(None),) * (len(ref.shape) - 2) + (here,)]

    def before(self, stage):
        return self.family.part.at[self.slot] if stage == 0 else self.family.early[stage - 1].at[self.kept_at]

    def copy(self, stage):
        if stage < 2:
            source = self.quarter(self.before(stage), stage, 1 - bit_of(self.dp, stage))
            target, device = self.family.early[stage].at[self.kept_at], {"dp": flipped(self.dp, stage)}
        elif stage < 5:
            bit, place, others = self.order[stage - 2]
            chosen = [slice(None)] * (others + 1)
            chosen[place] = 1 - bit_of(self.blk, bit)
            source = self.family.early[stage - 1].at[(self.kept_at, *chosen)]
            target, device = self.family.early[stage].at[self.kept_at], {"blk": flipped(self.blk, bit)}
        else:
            source = self.quarter(self.family.out.at[self.kept_at], 0, bit_of(self.dp, 0))
            if stage == 5:
                source = self.quarter(source, 1, bit_of(self.dp, 1))
            target, device = source, {"dp": flipped(self.dp, 6 - stage)}
        return remote(source, target, self.sems, (self.at, stage), device)

    def receive(self, stage):
        kept = self.kept_at
        self.copy(stage).wait_recv()
        if stage < 2:
            got = self.family.early[stage].at[kept]
            self.add(got, got, self.quarter(self.before(stage), stage, bit_of(self.dp, stage)))
            if stage == 0:
                self.copy(0).wait_send()
        elif stage < 5:
            bit, place, others = self.order[stage - 2]
            for combo in itertools.product(range(2), repeat=others):
                chosen = list(combo)
                chosen.insert(place, bit_of(self.blk, bit))
                got = self.family.early[stage].at[(kept, *combo)]
                into = got
                if stage == 4:
                    into = self.quarter(self.family.out.at[kept], 0, bit_of(self.dp, 0))
                    into = self.quarter(into, 1, bit_of(self.dp, 1))
                self.add(into, got, self.family.early[stage - 1].at[(kept, *chosen)])


def feed_forward_backward(at, level, gradient, ready, done):
    column = at.router[level:level + 1, :].astype(jnp.float32)
    active = as_column(at.depths[...]) > float(level)
    hidden = at.hid_level[...]
    chosen = jax.nn.sigmoid(jnp.sum(hidden * column, axis=1, keepdims=True))
    at.dbranch[...] = jnp.where(active, chosen, 0.0) * gradient
    dchosen = jnp.where(active, jnp.sum(gradient * at.branch_level[...], axis=1, keepdims=True), 0.0)
    dlogit = dchosen * chosen * (1.0 - chosen)
    at.small[2 + level:3 + level, :] = jnp.sum(hidden * dlogit, axis=0, keepdims=True)
    at.grad_hidden[...] = gradient + dlogit * column
    at.dffn[...] = at.dbranch[...].astype(low)

    ready(0)
    dinner = plain_dot(at.dffn[...], at.w_down[...])
    at.dgate[...] = (dinner * at.slope_level[...].astype(jnp.float32)).astype(low)
    at.dup[...] = (dinner * at.silu_level[...].astype(jnp.float32)).astype(low)
    done()
    at.dnorm_turned[...] = plain_dot(at.w_gate[...], at.dgate[...].T) + plain_dot(at.w_up[...], at.dup[...].T)
    ready(1)
    dnorm = at.dnorm_turned[...].T
    dmiddle, gain_share = norm_gradient(dnorm, at.middle_level[...], at.norms[1:2, :].astype(jnp.float32))
    at.small[1:2, :] += gain_share
    at.grad_hidden[...] += dmiddle
    dattn = (at.dbranch[...] + dmiddle).astype(low)
    lead = at.far.shape[1] - dattn.shape[1]
    at.far[:, :lead] = jnp.zeros((dattn.shape[0], lead), low)
    at.far[:, lead:] = dattn
    at.dat[...] = plain_dot(at.w_out[...], dattn.T).astype(low)


def forward_kernel(sizes, names, *refs):
    m, piece = sizes
    at = types.SimpleNamespace(**dict(zip(names, refs)))
    blk = lax.axis_index("blk")
    mine = block_bits(blk, m)
    kv, metas = at.kv, at.metas
    weights = (
        (at.w_query_hbm, at.w_query), (at.w_out_hbm, at.w_out), (at.w_gate_hbm, at.w_gate), (at.w_up_hbm, at.w_up), (at.w_down_hbm, at.w_down),
    )
    loads = [pltpu.make_async_copy(*pair, at.load_sems.at[index]) for index, pair in enumerate(weights)]
    kv_loads = kv_weight_loads(at.key_weight_hbm, at.value_weight_hbm, at.kv_weight, at.weight_sems)
    for load in kv_loads + loads:
        load.start()
    saved = (
        (at.normed, at.normed_out), (at.turned, at.turned_out), (kv, at.kv_out), (at.lse, at.lse_out),
        (at.att, at.att_out), (at.nffn, at.nffn_out), (at.inner, at.inner_out),
    )

    def save(index, level):
        return pltpu.make_async_copy(
            saved[index][0].at[level] if index == 2 else saved[index][0], saved[index][1].at[level], at.save_sems.at[index, level]
        )

    first = (
        (at.hid.at[0], at.hid_out), (at.middle, at.middle_out), (at.silu, at.silu_out),
        (at.slope, at.slope_out), (at.branch, at.branch_out), (metas, at.metas_out),
        (at.far, at.far_out), (at.dat, at.dat_out), (at.dffn, at.dffn_out), (at.dgate, at.dgate_out), (at.dup, at.dup_out),
        (at.hid.at[1], at.hid_1_out),
    )
    late = [pltpu.make_async_copy(*pair, at.late_sems.at[index]) for index, pair in enumerate(first)]
    segment_row = at.segments[...].astype(jnp.float32)
    depth_column = as_column(at.depths[...])
    metas[mine] = jnp.concatenate(
        [segment_row, at.depths[...].astype(jnp.float32), jnp.zeros((6, piece), jnp.float32)], axis=0
    )
    greet([{"blk": flipped(blk, bit)} for bit in range(m)])

    def place(known):
        return tuple(slice(None) if bit in known else mine[m - 1 - bit] for bit in range(m - 1, -1, -1))

    orders = (list(range(1, m)), list(range(m - 1, 0, -1)))
    kv_sems = (at.kv_send, at.kv_recv)

    def kv_copies(level, group, stage):
        if stage == m - 1:
            ref = kv.at[(level, group, *place(range(1, m)))]
            return [remote(ref, ref, kv_sems, (level, group, 2 * stage), {"blk": flipped(blk, 0)})]
        copies = []
        for side, order in enumerate(orders):
            rows = pl.ds(side * (piece // 2), piece // 2)
            ref = kv.at[(level, group, *place(order[:stage]), rows)]
            copies.append(remote(ref, ref, kv_sems, (level, group, 2 * stage + side), {"blk": flipped(blk, order[stage])}))
        return copies

    def kv_advance(level, group, stage):
        if stage > 0:
            for copy in kv_copies(level, group, stage - 1):
                copy.wait_recv()
        if stage < m:
            for copy in kv_copies(level, group, stage):
                copy.start()

    def meta_copy(stage):
        bits = list(range(1, m)) + [0]
        ref = metas.at[place(bits[:stage])]
        return remote(ref, ref, (at.meta_send, at.meta_recv), stage, {"blk": flipped(blk, bits[stage])})

    meta_copy(0).start()
    cosine, sine = at.cosines[...], at.sines[...]
    gain_attn, gain_ffn = at.norms[0:1, :].astype(jnp.float32), at.norms[1:2, :].astype(jnp.float32)
    routers = at.router[...].astype(jnp.float32)
    at.hid[0] = at.tokens[...].T.astype(jnp.float32)
    late[0].start()
    at.query_pad[HEAD_DIMENSION:, :] = jnp.zeros_like(at.query_pad[HEAD_DIMENSION:, :])

    @pl.loop(0, RECUR)
    def _(level):
        @pl.when(level > 0)
        def _():
            for index in range(5):
                save(index, 0).wait()

        hidden = at.hid[level]
        at.flat[...] = (hidden * rms_scale(hidden) * gain_attn).astype(low)
        at.normed[...] = at.flat[...].T

        @pl.when(level == 0)
        def _():
            for load in kv_loads:
                load.wait()

        both = turn_keys(plain_dot(at.kv_weight[...], at.normed[...]), cosine, sine).T.astype(low)
        for group in range(KEY_VALUE_HEADS):
            kv[(level, group, *mine)] = both[:, group * PAIR:(group + 1) * PAIR]
            kv_advance(level, group, 0)

        @pl.when(level == 0)
        def _():
            loads[0].wait()
            for stage in range(1, m - 1):
                meta_copy(stage - 1).wait_recv()
                meta_copy(stage).start()

        queries = turn_heads(plain_dot(at.flat[...], at.w_query[...]).T, cosine, sine, QUERY_HEADS)
        at.turned[...] = (queries * HEAD_DIMENSION ** (-0.5)).astype(low)

        @pl.when(level == 0)
        def _():
            for stage in range(max(1, m - 1), m):
                meta_copy(stage - 1).wait_recv()
                meta_copy(stage).start()

        for stage in range(1, m - 1):
            for group in range(KEY_VALUE_HEADS):
                kv_advance(level, group, stage)
        kv_advance(level, 0, m - 1)

        @pl.when(level == 0)
        def _():
            meta_copy(m - 1).wait_recv()
            late[5].start()

        fill_bias(at.bias, metas, segment_row, level.astype(jnp.float32), blk, m, piece, SPAN)

        @pl.loop(0, KEY_VALUE_HEADS)
        def _(group):
            @pl.when(group + 1 < KEY_VALUE_HEADS)
            def _():
                kv_advance(level, group + 1, m - 1)

            kv_advance(level, group, m)
            for member in range(HEAD_SHARE):
                at.query_pad[:HEAD_DIMENSION, member * piece:(member + 1) * piece] = at.turned[head_rows(group, member), :]
            at.top[...] = jnp.full_like(at.top, masked_score)
            at.total[...] = jnp.zeros_like(at.total)

            @pl.loop(0, key_steps(blk, SPAN))
            def _(index):
                step = key_steps(blk, SPAN) - 1 - index
                rows = kv[(level, group, *block_bits(step, m - SPAN))].reshape((1 << SPAN) * piece, PAIR)
                scores = plain_dot(rows, at.query_pad[...]) + step_bias(at.bias, step, piece, SPAN)
                before = at.top[0:1, :]
                after = jnp.maximum(before, jnp.max(scores, axis=0, keepdims=True))
                raised = jnp.exp(scores - after)
                shrink = jnp.exp(before - after)
                at.top[0:1, :] = after
                ones = jnp.ones((16, rows.shape[0]), low)
                left = jnp.concatenate([rows.T[HEAD_DIMENSION:], ones], axis=0)
                at.total[...] = at.total[...] * shrink + plain_dot(left, raised.astype(low))

            sums = at.total[HEAD_DIMENSION:HEAD_DIMENSION + 1, :]
            at.lse[pl.ds(group, 1), :] = at.top[0:1, :] + jnp.log(sums)
            out = at.total[:HEAD_DIMENSION, :] / sums
            for member in range(HEAD_SHARE):
                at.att[head_rows(group, member), :] = out[:, member * piece:(member + 1) * piece].astype(low)

        for index in range(5):
            save(index, level).start()

        @pl.when(level == 0)
        def _():
            loads[1].wait()

        @pl.when(level > 0)
        def _():
            save(5, 0).wait()
            save(6, 0).wait()
            for copy in late[1:5]:
                copy.wait()

        attn = plain_dot(at.att[...].T, at.w_out[...])
        mid = at.hid[level] + attn
        at.middle[...] = mid
        at.branch[...] = attn
        at.flat[...] = (mid * rms_scale(mid) * gain_ffn).astype(low)
        at.nffn[...] = at.flat[...].T
        save(5, level).start()

        @pl.when(level == 0)
        def _():
            loads[2].wait()
            loads[3].wait()

        gate_pre = plain_dot(at.flat[...], at.w_gate[...])
        up_pre = plain_dot(at.flat[...], at.w_up[...])
        opened = jax.nn.sigmoid(gate_pre)
        passed = gate_pre * opened
        at.silu[...] = passed.astype(low)
        at.slope[...] = (up_pre * (opened + passed - passed * opened)).astype(low)
        at.inner[...] = (passed * up_pre).astype(low).T
        save(6, level).start()

        @pl.when(level == 0)
        def _():
            loads[4].wait()

        at.branch[...] += plain_dot(at.w_down[...], at.inner[...]).T
        column = jnp.where(level == 0, routers[0:1, :], routers[1:2, :])
        logit = jnp.sum(at.hid[level] * column, axis=1, keepdims=True)
        weight = jnp.where(depth_column > level.astype(jnp.float32), jax.nn.sigmoid(logit), 0.0)
        at.hid[level + 1] = at.hid[level] + weight * at.branch[...]

        @pl.when(level == 0)
        def _():
            for copy in late[1:5]:
                copy.start()

    at.hidden_out[...] = at.hid[RECUR].T
    top = RECUR - 1
    at.hid_level, at.branch_level, at.middle_level = at.hid.at[top], at.branch, at.middle
    at.silu_level, at.slope_level = at.silu, at.slope
    at.small[...] = jnp.zeros_like(at.small)
    feed_forward_backward(at, top, at.cotangent[...].T.astype(jnp.float32), lambda part: None, lambda: None)
    for copy in late[6:]:
        copy.start()
    for stage in range(m):
        meta_copy(stage).wait_send()
    for level in range(RECUR):
        for group in range(KEY_VALUE_HEADS):
            for stage in range(m):
                for copy in kv_copies(level, group, stage):
                    copy.wait_send()
    for index in range(len(saved)):
        save(index, RECUR - 1).wait()
    for copy in late[:1] + late[5:]:
        copy.wait()


def far_width(width):
    return 2 * width + 2 * KEYS_WIDTH - 1536


def forward(small, weights, nb):
    m = nb.bit_length() - 1
    width, piece = small["tokens"].shape
    hidden_units = weights["w_gate_hbm"].shape[1]
    blocks, wide = (2,) * m, HEAD_SHARE * piece
    rows, turned = ((piece, width), jnp.float32), ((RECUR, width, piece), low)
    hidden = ((piece, hidden_units), low)
    saved = dict(
        normed=turned, turned=turned, kv=((RECUR, KEY_VALUE_HEADS, *blocks, piece, PAIR), low),
        lse=((RECUR, 8, wide), jnp.float32), att=turned, nffn=turned, inner=((RECUR, hidden_units, piece), low),
        metas=((*blocks, 8, piece), jnp.float32), far=((piece, far_width(width)), low), dat=((width, piece), low),
        dffn=((piece, width), low), dgate=hidden, dup=hidden,
    )
    first = dict(hid=rows, middle=rows, silu=hidden, slope=hidden, branch=rows)
    outs = dict(hidden_out=((width, piece), jnp.float32), grad_hidden=rows, small=((8, width), jnp.float32))
    anywhere = {name + "_out": entry for name, entry in (saved | first | dict(hid_1=rows)).items()}
    single = {name: (shape[1:], dtype) for name, (shape, dtype) in saved.items() if shape[0] == RECUR and name not in ("kv", "metas")}
    buffers = {name[:-4]: (array.shape, array.dtype) for name, array in weights.items()} | saved | single | first | dict(
        kv_weight=((2 * KEYS_WIDTH, width), low),
        hid=((RECUR + 1, piece, width), jnp.float32), flat=((piece, width), low),
        bias=((nb, piece, piece), jnp.float32), query_pad=((PAIR, wide), low), top=((8, wide), jnp.float32),
        total=((HEAD_DIMENSION + 16, wide), jnp.float32), dbranch=rows, dnorm_turned=((width, piece), jnp.float32),
    )
    semaphores = dict(
        load_sems=(5,), weight_sems=(2 * KEY_VALUE_HEADS,), save_sems=(7, RECUR), late_sems=(12,), kv_send=(RECUR, KEY_VALUE_HEADS, 2 * m),
        kv_recv=(RECUR, KEY_VALUE_HEADS, 2 * m), meta_send=(m,), meta_recv=(m,),
    )
    results = pl.pallas_call(
        functools.partial(forward_kernel, (m, piece), (*small, *weights, *outs, *anywhere, *buffers, *semaphores)),
        out_shape=[shaped(entry) for entry in (outs | anywhere).values()],
        in_specs=[spec(pltpu.VMEM)] * len(small) + [spec(pl.ANY)] * len(weights),
        out_specs=[spec(pltpu.VMEM)] * len(outs) + [spec(pl.ANY)] * len(anywhere),
        scratch_shapes=spaces(buffers.values()) + dma_semaphores(*semaphores.values()),
        compiler_params=pltpu.CompilerParams(
            collective_id=1, has_side_effects=True, vmem_limit_bytes=VMEM_LIMIT
        ),
        cost_estimate=pl.CostEstimate(
            flops=3 * RECUR * piece * width * 10240, bytes_accessed=48 * 1024 * 1024, transcendentals=0
        ),
        name="forward_levels",
    )(*small.values(), *weights.values())
    return dict(zip((*outs, *(name[:-4] for name in anywhere)), results))


class AttentionBackward:
    def __init__(self, at, m, piece, level, span):
        self.at, self.m, self.piece, self.level, self.span = at, m, piece, level, span
        self.blk = lax.axis_index("blk")
        self.family = types.SimpleNamespace(part=at.part, blk=at.halves, dp=(), out=None, shape=(piece // 2, PAIR), split=0)

    def pieces(self, group):
        sems = (self.at.kv_send, self.at.kv_recv)
        return [
            Piece(2 * group + side, 2 * group + side, 2 * group + side, side, self.family, sems, (self.m, 0))
            for side in range(2)
        ]

    def move(self, group, stage):
        for piece_of in self.pieces(group):
            piece_of.finish(stage)
            if stage + 1 < self.m:
                piece_of.start(stage + 1)

    def begin(self):
        at = self.at
        query_segments = at.metas[block_bits(self.blk, self.m)][0:1, :]
        fill_bias(at.bias, at.metas, query_segments, float(self.level), self.blk, self.m, self.piece, self.span)
        at.query_pad[HEAD_DIMENSION:, :] = jnp.zeros_like(at.query_pad[HEAD_DIMENSION:, :])
        at.dat_pad[:HEAD_DIMENSION, :] = jnp.zeros_like(at.dat_pad[:HEAD_DIMENSION, :])

    def group(self, group):
        at, m, piece, blk = self.at, self.m, self.piece, self.blk
        half = piece // 2
        carried = []
        for member in range(HEAD_SHARE):
            rows, lanes = head_rows(group, member), slice(member * piece, (member + 1) * piece)
            at.query_pad[:HEAD_DIMENSION, lanes] = at.turned[rows, :]
            at.dat_pad[HEAD_DIMENSION:, lanes] = at.dat_turned[rows, :]
            product = at.dat_turned[rows, :].astype(jnp.float32) * at.att_turned[rows, :].astype(jnp.float32)
            carried.append(jnp.sum(product, axis=0, keepdims=True))
        carried = jnp.concatenate(carried, axis=1)
        at.query_rows[...] = at.query_pad[...].T
        at.dat_rows[...] = at.dat_pad[...].T
        log_total = at.lse[pl.ds(group, 1), :]
        at.dq_sum[...] = jnp.zeros_like(at.dq_sum)

        span, lead = self.span, m - self.span

        @pl.loop(0, key_steps(blk, span))
        def _(step):
            rows = at.kv[(group, *block_bits(step, lead))].reshape((1 << span) * piece, PAIR)
            probability = jnp.exp(plain_dot(rows, at.query_pad[...]) + step_bias(at.bias, step, piece, span) - log_total)
            dprob = plain_dot(rows, at.dat_pad[...])
            dscores = (probability * (dprob - carried)).astype(low)
            share = plain_dot(dscores, at.query_rows[...]) + plain_dot(probability.astype(low), at.dat_rows[...])
            share = share.astype(low)
            for block in range(1 << span):
                for side in range(2):
                    first = block * piece + side * half
                    place = (2 * group + side, *block_bits(step, lead), *bits_of(block, span))
                    at.part[place] = share[first:first + half]
            at.dq_sum[...] += plain_dot(rows.T[:HEAD_DIMENSION], dscores)

        @pl.loop(key_steps(blk, span), 1 << lead)
        def _(step):
            for block in range(1 << span):
                for side in range(2):
                    place = (2 * group + side, *block_bits(step, lead), *bits_of(block, span))
                    at.part[place] = jnp.zeros((half, PAIR), low)

        for piece_of in self.pieces(group):
            piece_of.start(0)
        for member in range(HEAD_SHARE):
            at.dq_turned[head_rows(group, member), :] = at.dq_sum[:, member * piece:(member + 1) * piece]

    def follow(self, group):
        for stage in range(self.m - 1):
            earlier = group - 1 - stage
            if isinstance(group, int):
                if 0 <= earlier < KEY_VALUE_HEADS:
                    self.move(earlier, stage)
            else:
                @pl.when(earlier >= 0)
                def _():
                    self.move(earlier, stage)

    def queries(self, cosine, sine):
        at = self.at
        dqueries = turn_back(at.dq_turned[...] * HEAD_DIMENSION ** (-0.5), cosine, sine, QUERY_HEADS).astype(low)
        self.put(2 * KEYS_WIDTH, dqueries.T)
        at.dnorm[...] = plain_dot(at.w_query[...], dqueries).T

    def put(self, column, values):
        self.at.near[:, column:column + values.shape[1]] = values

    def keys(self, cosine, sine):
        at, m = self.at, self.m
        filled = 2 * KEYS_WIDTH + QUERY_HEADS * HEAD_DIMENSION
        self.put(filled, jnp.zeros((self.piece, at.near.shape[1] - filled), low))
        sums = []
        for group in range(KEY_VALUE_HEADS):
            self.move(group, m - 1)
            sums.append(jnp.concatenate([at.halves[m - 1][2 * group], at.halves[m - 1][2 * group + 1]], axis=0))
        both = jnp.concatenate(sums, axis=1).astype(jnp.float32).T
        both = turn_keys(both, cosine, -sine).astype(low).T
        self.put(0, both)
        at.dnorm[...] += plain_dot(both, at.kv_weight[...])

    def drained(self):
        for group in range(KEY_VALUE_HEADS):
            for piece_of in self.pieces(group):
                piece_of.drained(range(1, self.m))


def attention_buffers(nb, piece, width, bias_type):
    m, wide, heads = nb.bit_length() - 1, HEAD_SHARE * piece, 2 * KEY_VALUE_HEADS
    turned = ((width, piece), low)
    pad, pad_rows = ((PAIR, wide), low), ((wide, PAIR), low)
    buffers = dict(
        turned=turned, dat_turned=turned, att_turned=turned, kv=((KEY_VALUE_HEADS, *(2,) * m, piece, PAIR), low),
        lse=((8, wide), jnp.float32), metas=((*(2,) * m, 8, piece), jnp.float32), w_query=((width, width), low),
        kv_weight=((2 * KEYS_WIDTH, width), low), dq_turned=((width, piece), jnp.float32),
        bias=((nb, piece, piece), bias_type), query_pad=pad, dat_pad=pad, query_rows=pad_rows, dat_rows=pad_rows,
        dq_sum=((HEAD_DIMENSION, wide), jnp.float32), part=((heads, *(2,) * m, piece // 2, PAIR), low),
        dnorm=((piece, width), jnp.float32), hid=((piece, width), jnp.float32),
    )
    for stage in range(m):
        buffers["half_%d" % stage] = ((heads, *(2,) * (m - 1 - stage), piece // 2, PAIR), low)
    return buffers


def backward_kernel(sizes, names, *refs):
    m, piece, level = sizes
    at = types.SimpleNamespace(**dict(zip(names, refs)))
    at.halves = [getattr(at, "half_%d" % stage) for stage in range(m)]
    at.near = at.near_out
    blk = lax.axis_index("blk")
    pairs = (
        (at.metas_hbm, at.metas), (at.turned_hbm.at[level], at.turned), (at.dat_hbm, at.dat_turned),
        (at.att_hbm.at[level], at.att_turned), (at.lse_hbm.at[level], at.lse), (at.kv_hbm.at[level], at.kv),
        (at.w_query_hbm, at.w_query),
        (at.grad_hbm, at.grad_hidden), (at.hid_1_hbm, at.hid),
        (at.hid_0_hbm, at.hid_level), (at.branch_hbm, at.branch_level), (at.w_down_hbm, at.w_down),
        (at.slope_hbm, at.slope_level), (at.silu_hbm, at.silu_level), (at.w_gate_hbm, at.w_gate), (at.w_up_hbm, at.w_up),
        (at.middle_hbm, at.middle_level), (at.w_out_hbm, at.w_out),
    )
    loads = [pltpu.make_async_copy(*pair, at.load_sems.at[index]) for index, pair in enumerate(pairs)]
    loads += kv_weight_loads(at.key_weight_hbm, at.value_weight_hbm, at.kv_weight, at.weight_sems)
    for load in loads:
        load.start()
    saves = [
        pltpu.make_async_copy(*pair, at.save_sems.at[index])
        for index, pair in enumerate(((at.dgate, at.dgate_out), (at.dup, at.dup_out)))
    ]
    greet([{"blk": flipped(blk, bit)} for bit in range(m)])
    work = AttentionBackward(at, m, piece, level, SPAN)
    loads[0].wait()
    work.begin()
    for load in loads[1:6]:
        load.wait()

    @pl.loop(0, KEY_VALUE_HEADS)
    def _(group):
        work.group(group)
        work.follow(group)

    cosine, sine = at.cosines[...], at.sines[...]
    for virtual in range(KEY_VALUE_HEADS, KEY_VALUE_HEADS + m - 1):
        work.follow(virtual)
        if virtual == KEY_VALUE_HEADS:
            loads[6].wait()
            work.queries(cosine, sine)
    for load in loads[7:]:
        load.wait()
    work.keys(cosine, sine)
    dhidden, gain_share = norm_gradient(at.dnorm[...], at.hid[...], at.norms[0:1, :].astype(jnp.float32))
    at.small[...] = at.small_before[...]
    at.small[0:1, :] = gain_share
    gradient = at.grad_hidden[...] + dhidden
    at.dnorm[...] = gradient
    feed_forward_backward(at, level - 1, at.dnorm[...], lambda part: None, lambda: [save.start() for save in saves])
    work.drained()
    for save in saves:
        save.wait()


def backward(level, small, operands, nb):
    m = nb.bit_length() - 1
    piece, width = operands["grad_hbm"].shape
    hidden_units = operands["w_gate_hbm"].shape[1]
    rows, flat, hidden = ((piece, width), jnp.float32), ((piece, width), low), ((piece, hidden_units), low)
    outs = dict(
        grad_hidden=rows, small=((8, width), jnp.float32), near_out=((piece, 1792), low), dffn=flat,
        dat=((width, piece), low), far=((piece, far_width(width)), low),
    )
    anywhere = dict(dgate_out=hidden, dup_out=hidden)
    buffers = attention_buffers(nb, piece, width, jnp.float32) | dict(
        hid_level=rows, branch_level=rows, middle_level=rows, w_down=((width, hidden_units), low), slope_level=hidden,
        silu_level=hidden, w_gate=((width, hidden_units), low), w_up=((width, hidden_units), low),
        w_out=((width, width), low), dbranch=rows, dnorm_turned=((width, piece), jnp.float32), dgate=hidden, dup=hidden,
    )
    sums = (2 * KEY_VALUE_HEADS, m)
    semaphores = dict(load_sems=(18,), weight_sems=(2 * KEY_VALUE_HEADS,), save_sems=(2,), kv_send=sums, kv_recv=sums)
    results = pl.pallas_call(
        functools.partial(
            backward_kernel, (m, piece, level), (*small, *operands, *outs, *anywhere, *buffers, *semaphores)
        ),
        out_shape=[shaped(entry) for entry in (outs | anywhere).values()],
        in_specs=[spec(pltpu.VMEM)] * len(small) + [spec(pl.ANY)] * len(operands),
        out_specs=[spec(pltpu.VMEM)] * len(outs) + [spec(pl.ANY)] * len(anywhere),
        scratch_shapes=spaces(buffers.values()) + dma_semaphores(*semaphores.values()),
        compiler_params=pltpu.CompilerParams(
            collective_id=2, has_side_effects=True, vmem_limit_bytes=VMEM_LIMIT
        ),
        cost_estimate=pl.CostEstimate(
            flops=2 * piece * width * 20000, bytes_accessed=32 * 1024 * 1024, transcendentals=0
        ),
        name="backward_level",
    )(*small.values(), *operands.values())
    return dict(zip((*outs, *anywhere), results))


WIDE_SLOTS, DOWN_SLOTS, EARLY = 4, 2, 2


def final_kernel(sizes, names, *refs):
    nb, m, n, piece, rows, padded, near_width = sizes
    at = types.SimpleNamespace(**dict(zip(names, refs)))
    at.halves = [getattr(at, "half_%d" % stage) for stage in range(m)]
    blk, dp = lax.axis_index("blk"), lax.axis_index("dp")
    at.near = at.gate_side.at[pl.ds(0, piece), pl.ds(0, near_width)]
    counter = itertools.count()

    def load(source, target):
        return pltpu.make_async_copy(source, target, at.load_sems.at[next(counter)])

    def both_lanes(ref, target):
        return [load(ref.at[level], target.at[:, pl.ds(level * piece, piece)]) for level in range(RECUR)]

    def both_rows(low_ref, deep_ref, target, width):
        pairs = ((low_ref, 0), (deep_ref, piece))
        return [load(ref, target.at[pl.ds(first, piece), pl.ds(0, width)]) for ref, first in pairs]

    hidden_units, width = at.gate_side.shape[1], at.dffn.shape[1]
    far_lanes = at.far_0_hbm.shape[1]
    loads = types.SimpleNamespace(
        nffn=both_lanes(at.nffn_hbm, at.left),
        dgate=both_rows(at.dgate_0_hbm, at.dgate_1_hbm, at.gate_side, hidden_units),
        inner=both_lanes(at.inner_hbm, at.inner),
        dffn=both_rows(at.dffn_0_hbm, at.dffn_1_hbm, at.dffn, width),
        metas=[load(at.metas_hbm, at.metas)],
        heads=[
            load(at.turned_hbm.at[0], at.turned), load(at.dat_hbm, at.dat_turned), load(at.att_hbm.at[0], at.att_turned),
            load(at.lse_hbm.at[0], at.lse), load(at.kv_hbm.at[0], at.kv),
        ],
        dup=both_rows(at.dup_0_hbm, at.dup_1_hbm, at.up_side, hidden_units),
        w_query=[load(at.w_query_hbm, at.w_query)],
        rest=[
            load(at.hid_hbm, at.hid), load(at.grad_hbm, at.grad),
        ],
        attended=both_lanes(at.attended_hbm, at.left_attended),
        kv_weight=kv_weight_loads(at.key_weight_hbm, at.value_weight_hbm, at.kv_weight, at.weight_sems),
    )
    late = types.SimpleNamespace(
        near=[load(at.near_1_hbm, at.gate_side.at[pl.ds(piece, piece), pl.ds(0, near_width)])],
        far=both_rows(at.far_0_hbm, at.far_1_hbm, at.up_side, far_lanes),
        normed=both_lanes(at.normed_hbm, at.left),
    )

    def begin(copies):
        for copy in copies:
            copy.start()

    def ready(copies):
        for copy in copies:
            copy.wait()

    for copies in vars(loads).values():
        begin(copies)
    greet([{"blk": flipped(blk, bit)} for bit in range(m)] + [{"dp": flipped(dp, bit)} for bit in range(n)])

    down_rows = at.part_down.shape[-2]

    def family(name, shape, split):
        return types.SimpleNamespace(
            part=getattr(at, "part_" + name), out=getattr(at, "out_" + name), shape=shape, split=split,
            blk=[getattr(at, "blk_%s_%d" % (name, stage)) for stage in range(m)],
            dp=[getattr(at, "dp_%s_%d" % (name, stage)) for stage in range(n)],
        )

    wide = family("wide", (2 * padded, UNIT_COLUMNS), 1)
    down = family("down", (down_rows, width), 0)
    little = family("small", (16, 128), 0)
    many = 5 - at.out_down.shape[0]
    if many:
        deep = types.SimpleNamespace(
            part=at.part_down, out=at.out_deep, shape=(down_rows, width),
            early=[at.early_0, at.early_1, at.early_2, at.early_3, at.early_4],
        )
    sems = (at.send_sems, at.recv_sems)
    units = itertools.count()

    def unit(holder, index, flavour, halves=n != 2):
        return Piece(next(units), index, index % holder.part.shape[0], flavour, holder, sems, (m, n), not halves)

    def down_unit(index):
        if index < many:
            return EarlyPiece(next(units), index, index % DOWN_SLOTS, 1, deep, sems, (m, n))
        return Piece(next(units), index - many, index % DOWN_SLOTS, 1, down, sems, (m, n), n == 2)

    pairs = [[unit(wide, index, 0), down_unit(index)] for index in range(5)]
    pairs += [[unit(wide, index, first), unit(wide, index + 1, first + 1)] for index, first in ((5, 2), (7, 0), (9, 2))]
    pairs += [[unit(wide, 11, 0, True), unit(wide, 12, 1, True)]]
    pairs += [[unit(wide, 13, 0, True), unit(wide, 14, 1, True), unit(little, 0, 0, True)]]

    def compute_wide(index, slot):
        if index == 0:
            ready(loads.nffn)
            ready(loads.dgate)
        if index == 5:
            begin(late.near)
            ready(loads.dup)
        if index == 10:
            begin(late.far)
            begin(late.normed)
            ready(late.near)
            ready(late.normed)
            ready(loads.attended)
            ready(late.far)
        block, column = index // 5, (index % 5) * UNIT_COLUMNS
        second = 1280 + column
        upper_columns, lower_columns = slice(column, column + UNIT_COLUMNS), slice(second, second + UNIT_COLUMNS)
        if block < 2:
            right = at.gate_side if block == 0 else at.up_side
            upper = plain_dot(at.left[...], right[:, upper_columns])
            lower = plain_dot(at.left[...], right[:, lower_columns])
        else:
            upper = plain_dot(at.left[...], at.gate_side[:, upper_columns])
            lower = None
            if second < 1600:
                lower = plain_dot(at.left[...], at.gate_side[:, lower_columns])
            if second >= 1536:
                more = plain_dot(at.left_attended[...], at.up_side[:, second - 1536:second - 1536 + UNIT_COLUMNS])
                lower = more if lower is None else lower + more
        for target in range(nb):
            here = slice(target * padded, (target + 1) * padded)
            both = jnp.concatenate([upper[here], lower[here]], axis=0)
            at.part_wide[(slot, *bits_of(target, m))] = both.astype(low)

    def compute_down(index, slot):
        if index == 0:
            ready(loads.inner)
            ready(loads.dffn)
        firsts = [(target * 5 + index) * down_rows for target in range(nb)]
        left = jnp.concatenate([at.inner[first:first + down_rows, :] for first in firsts], axis=0)
        result = plain_dot(left, at.dffn[...])
        for target in range(nb):
            at.part_down[(slot, *bits_of(target, m))] = result[target * down_rows:(target + 1) * down_rows].astype(low)

    def compute_small():
        total = at.small_before[...]
        total = total + jnp.concatenate([at.gain_row[...], jnp.zeros((7, width), jnp.float32)], axis=0)
        at.part_small[...] = jnp.zeros_like(at.part_small)
        for target in range(nb):
            at.part_small[(0, *bits_of(target, m), slice(0, 8), slice(0, rows))] = total[:, target * rows:(target + 1) * rows]

    def compute(piece_of):
        if piece_of.family is wide:
            compute_wide(piece_of.kept_at, piece_of.slot)
        elif piece_of.family is little:
            compute_small()
        elif piece_of.family is down:
            compute_down(piece_of.kept_at + many, piece_of.slot)
        else:
            compute_down(piece_of.kept_at, piece_of.slot)
        piece_of.start(0)

    def moves(tick):
        for stage in range(m + n, -1, -1):
            if 0 <= tick - stage < len(pairs):
                for piece_of in pairs[tick - stage]:
                    if stage + 1 < piece_of.stages:
                        piece_of.finish(stage)
                        piece_of.start(stage + 1)

    work = AttentionBackward(at, m, piece, 0, 1)
    for pair in pairs[:2]:
        for piece_of in pair:
            compute(piece_of)
    ready(loads.metas)
    work.begin()
    ready(loads.heads)
    for group in range(KEY_VALUE_HEADS):
        moves(group)
        for piece_of in pairs[group + 2]:
            compute(piece_of)
        work.group(group)
        work.follow(group)
    cosine, sine = at.cosines[...], at.sines[...]
    moves(5)
    compute(pairs[7][0])
    ready(loads.w_query)
    for virtual in range(KEY_VALUE_HEADS, KEY_VALUE_HEADS + m - 1):
        work.follow(virtual)
        if virtual == KEY_VALUE_HEADS:
            work.queries(cosine, sine)
    moves(6)
    ready(loads.rest)
    ready(loads.kv_weight)
    work.keys(cosine, sine)
    compute(pairs[7][1])
    moves(7)
    for piece_of in pairs[8] + pairs[9][:2]:
        compute(piece_of)
    dhidden, gain_share = norm_gradient(at.dnorm[...], at.hid[...], at.norms[0:1, :].astype(jnp.float32))
    at.gain_row[...] = gain_share
    at.grad_out[...] = (at.grad[...] + dhidden).T
    compute(pairs[9][2])
    for tick in range(8, len(pairs) + m + n - 1):
        moves(tick)
    for pair in pairs:
        for piece_of in pair:
            piece_of.finish(piece_of.stages - 1)
    for pair in pairs:
        for piece_of in pair:
            piece_of.drained(range(1, piece_of.stages))
    work.drained()


def unpack_kernel(sizes, hidden_in, gradient_in, wide_hbm, little_hbm, *refs):
    rows, padded, counts = sizes
    down_hbm, refs = refs[:len(counts)], refs[len(counts):]
    norm_attn, norm_ffn, query, key, value, out, gate, up, down_out, router, hidden, gradient = refs[:12]
    wide, little, down, rest, sems = refs[12:]
    carried = [
        pltpu.make_async_copy(source, target, sems.at[at])
        for at, (source, target) in enumerate(((hidden_in, hidden), (gradient_in, gradient)))
    ]
    pairs, first = [(wide_hbm, wide), (little_hbm, little)], 0
    for source, count in zip(down_hbm, counts):
        pairs.append((source, down.at[pl.ds(first, count)]))
        first += count
    loads = [pltpu.make_async_copy(*pair, sems.at[2 + at]) for at, pair in enumerate(pairs)]
    for copy in loads + carried:
        copy.start()
    for load in loads:
        load.wait()
    norm_attn[...] = little[0, 0:1, :rows]
    norm_ffn[...] = little[0, 1:2, :rows]
    router[...] = little[0, 2:4, :rows]
    for unit in range(5):
        for first, target in ((0, gate), (5, up), (10, rest)):
            tile = wide[first + unit].astype(jnp.float32)
            for side in range(2):
                column = side * 1280 + unit * UNIT_COLUMNS
                target[:, column:column + UNIT_COLUMNS] = tile[side * padded:side * padded + rows]
        down_rows = down.shape[1]
        down_out[unit * down_rows:(unit + 1) * down_rows, :] = down[unit].astype(jnp.float32)
    width = query.shape[1]
    both = rest[:, :2 * KEYS_WIDTH].T
    for group in range(KEY_VALUE_HEADS):
        here, first = slice(group * HEAD_DIMENSION, (group + 1) * HEAD_DIMENSION), group * PAIR
        key[here, :] = both[first:first + HEAD_DIMENSION]
        value[here, :] = both[first + HEAD_DIMENSION:first + PAIR]
    query[...] = rest[:, 2 * KEYS_WIDTH:2 * KEYS_WIDTH + width]
    out[...] = rest[:, 2 * KEYS_WIDTH + width:]
    for copy in carried:
        copy.wait()


def final(small, saved, top, bottom, weights, mesh_sizes):
    nb, nd = mesh_sizes
    m, n = nb.bit_length() - 1, nd.bit_length() - 1
    grad = bottom["grad_hidden"]
    piece, width = grad.shape
    hidden_units = weights["w_gate_hbm"].shape[1]
    rows = width // nb
    padded = -(-rows // 8) * 8
    down_rows = hidden_units // nb // 5
    tokens = RECUR * piece

    def spread(array):
        if padded == rows:
            return array
        split = array.reshape(RECUR, nb, rows, piece)
        return jnp.pad(split, ((0, 0), (0, 0), (0, padded - rows), (0, 0))).reshape(RECUR, nb * padded, piece)

    inputs = small | dict(small_before=bottom["small"])
    operands = dict(
        metas_hbm=saved["metas"], turned_hbm=saved["turned"], dat_hbm=bottom["dat"], att_hbm=saved["att"],
        lse_hbm=saved["lse"], kv_hbm=saved["kv"], w_query_hbm=weights["w_query_hbm"],
        key_weight_hbm=weights["key_weight_hbm"], value_weight_hbm=weights["value_weight_hbm"], hid_hbm=saved["hid"],
        grad_hbm=grad, inner_hbm=saved["inner"], nffn_hbm=spread(saved["nffn"]), normed_hbm=spread(saved["normed"]),
        attended_hbm=spread(saved["att"]), dffn_0_hbm=bottom["dffn"], dffn_1_hbm=top["dffn"],
        dgate_0_hbm=bottom["dgate_out"], dgate_1_hbm=top["dgate"], dup_0_hbm=bottom["dup_out"], dup_1_hbm=top["dup"],
        far_0_hbm=bottom["far"], far_1_hbm=top["far"], near_1_hbm=bottom["near_out"],
    )
    near_width = bottom["near_out"].shape[1]
    many = EARLY if (m, n) == (3, 2) else 0
    families = (
        ("wide", 15, (2 * padded, UNIT_COLUMNS), low, WIDE_SLOTS, 1),
        ("down", 5 - many, (down_rows, width), low, DOWN_SLOTS, 0),
        ("small", 1, (16, 128), jnp.float32, 1, 0),
    )
    outs = dict(grad_out=((width, piece), jnp.float32))
    buffers = attention_buffers(nb, piece, width, low) | dict(
        grad=((piece, width), jnp.float32), gate_side=((tokens, hidden_units), low), up_side=((tokens, hidden_units), low),
        inner=((hidden_units, tokens), low), left=((nb * padded, tokens), low), left_attended=((nb * padded, tokens), low),
        dffn=((tokens, width), low), gain_row=((1, width), jnp.float32),
    )
    for name, count, shape, dtype, slots, split in families:
        outs["out_" + name] = ((count, *shape), dtype)
        buffers["part_" + name] = ((slots, *(2,) * m, *shape), dtype)
        for stage in range(m):
            buffers["blk_%s_%d" % (name, stage)] = ((count, *(2,) * (m - 1 - stage), *shape), dtype)
        for stage in range(n):
            buffers["dp_%s_%d" % (name, stage)] = ((count, *shape), dtype)
    if many:
        outs["out_deep"] = ((many, down_rows, width), low)
        for stage, (lead, share) in enumerate((((2, 2, 2), 2), ((2, 2, 2), 4), ((2, 2), 4), ((2,), 4), ((), 4))):
            buffers["early_%d" % stage] = ((many, *lead, down_rows // share, width), low)
    sums, hops = (2 * KEY_VALUE_HEADS, m), (21, m + n + 2)
    semaphores = dict(load_sems=(32,), weight_sems=(2 * KEY_VALUE_HEADS,), kv_send=sums, kv_recv=sums, send_sems=hops, recv_sems=hops)
    names = (*inputs, *operands, *outs, *buffers, *semaphores)
    gradient, wide, down, little, *deep = pl.pallas_call(
        functools.partial(final_kernel, (nb, m, n, piece, rows, padded, near_width), names),
        out_shape=[shaped(entry) for entry in outs.values()],
        in_specs=[spec(pltpu.VMEM)] * len(inputs) + [spec(pl.ANY)] * len(operands),
        out_specs=[spec(pltpu.VMEM)] * len(outs),
        scratch_shapes=spaces(buffers.values()) + dma_semaphores(*semaphores.values()),
        compiler_params=pltpu.CompilerParams(
            collective_id=0, has_side_effects=True, vmem_limit_bytes=VMEM_LIMIT
        ),
        cost_estimate=pl.CostEstimate(
            flops=2 * tokens * width * 14000, bytes_accessed=30 * 1024 * 1024, transcendentals=0
        ),
        name="weight_grads",
    )(*inputs.values(), *operands.values())
    shapes = (
        (1, rows), (1, rows), (rows, width), (KEYS_WIDTH, rows), (KEYS_WIDTH, rows), (rows, width),
        (rows, hidden_units), (rows, hidden_units), (5 * down_rows, width), (2, rows), (width, piece), (width, piece),
    )
    outs = pl.pallas_call(
        functools.partial(unpack_kernel, (rows, padded, [array.shape[0] for array in (*deep, down)])),
        out_shape=[jax.ShapeDtypeStruct(shape, jnp.float32) for shape in shapes],
        in_specs=[spec(pl.ANY)] * (5 + len(deep)),
        out_specs=[spec(pltpu.VMEM)] * 12,
        scratch_shapes=[pltpu.VMEM(array.shape, array.dtype) for array in (wide, little)]
        + spaces([((5, down_rows, width), low), ((rows, 2560), jnp.float32)]) + dma_semaphores((6,)),
        compiler_params=pltpu.CompilerParams(vmem_limit_bytes=VMEM_LIMIT),
        name="unpack",
    )(saved["hidden_out"], gradient, wide, little, *deep, down)
    norm_a, norm_f, query, key, value, out, gate, up, down, router, hidden, gradient = outs
    return (
        hidden.T[None], gradient.T[None], norm_a[0], norm_f[0], query, key.T, value.T, out, gate, up, down, router.T,
    )


def local(
    tokens,
    depths,
    segments,
    norm_attn,
    norm_ffn,
    w_query,
    key_weight,
    value_weight,
    w_out,
    w_gate,
    w_up,
    w_down,
    w_router,
    cotangent,
    mesh_sizes,
):
    piece = tokens.shape[1]
    positions = lax.axis_index("blk") * piece + jnp.arange(piece, dtype=jnp.int32)
    angles = frequencies(HEAD_DIMENSION)[:, None] * positions.astype(jnp.float32)[None, :]
    tables = dict(cosines=jnp.cos(angles), sines=jnp.sin(angles), norms=jnp.stack([norm_attn, norm_ffn]))
    routing = dict(router=w_router.T, depths=depths)
    heads = dict(w_query_hbm=w_query, key_weight_hbm=key_weight.T, value_weight_hbm=value_weight.T)
    weights = heads | dict(w_out_hbm=w_out, w_gate_hbm=w_gate, w_up_hbm=w_up, w_down_hbm=w_down.T)
    nb = mesh_sizes[0]
    saved = forward(
        tables | routing | dict(tokens=tokens[0].T, cotangent=cotangent[0].T, segments=segments), weights, nb
    )
    operands = dict(
        metas_hbm=saved["metas"], turned_hbm=saved["turned"], dat_hbm=saved["dat"], att_hbm=saved["att"],
        lse_hbm=saved["lse"], kv_hbm=saved["kv"], grad_hbm=saved["grad_hidden"], hid_1_hbm=saved["hid_1"],
        hid_0_hbm=saved["hid"], branch_hbm=saved["branch"], slope_hbm=saved["slope"], silu_hbm=saved["silu"],
        middle_hbm=saved["middle"],
    )
    bottom = backward(1, tables | routing | dict(small_before=saved["small"]), weights | operands, nb)
    return final(tables, saved, saved, bottom, weights, mesh_sizes)


def solution(mesh):
    sizes = (mesh.shape["blk"], mesh.shape["dp"])
    return jax.shard_map(
        functools.partial(local, mesh_sizes=sizes),
        mesh=mesh,
        in_specs=(
            P("dp", "blk", None),
            P("dp", "blk"),
            P("dp", "blk"),
            P(),
            P(),
            P(),
            P(),
            P(),
            P(),
            P(),
            P(),
            P(),
            P(),
            P("dp", "blk", None),
        ),
        out_specs=(
            P("dp", "blk", None),
            P("dp", "blk", None),
            P("blk"),
            P("blk"),
            P("blk", None),
            P("blk", None),
            P("blk", None),
            P("blk", None),
            P("blk", None),
            P("blk", None),
            P("blk", None),
            P("blk", None),
        ),
        check_vma=False,
    )
```

```python
import functools
import itertools
import math
import types

import jax
import jax.numpy as jnp
from jax import lax
from jax.experimental import pallas as pl
from jax.experimental.pallas import tpu as pltpu
from jax.sharding import PartitionSpec as P

QUERY_HEADS = 15
KEY_VALUE_HEADS = 5
HEAD_DIMENSION = 64
RECUR = 2
HEAD_SHARE = QUERY_HEADS // KEY_VALUE_HEADS
KEYS_WIDTH = KEY_VALUE_HEADS * HEAD_DIMENSION
PAIR = 2 * HEAD_DIMENSION
UNIT_COLUMNS = 256
SPAN = 2
VMEM_LIMIT = 63 * 1024 * 1024

epsilon = 1e-05
masked_score = -1e30
low = jnp.bfloat16


def frequencies(head_size):
    return jnp.exp(
        jnp.arange(head_size // 2, dtype=jnp.float32) * (-2.0 * math.log(10000.0) / head_size)
    )


def rms_scale(values):
    return lax.rsqrt(jnp.mean(values * values, axis=-1, keepdims=True) + epsilon)


def norm_gradient(grad_norm, values, gain):
    scale = rms_scale(values)
    weighted = grad_norm * gain
    grad_values = scale * weighted - values * (scale * scale * scale) * jnp.mean(
        weighted * values, axis=-1, keepdims=True
    )
    return grad_values, jnp.sum(grad_norm * values * scale, axis=0, keepdims=True)


def dot_last(left, right):
    return lax.dot_general(left, right, (((1,), (1,)), ((), ())), preferred_element_type=jnp.float32)


def plain_dot(left, right):
    return jnp.dot(left, right, preferred_element_type=jnp.float32)


def bits_of(number, count):
    return tuple((number >> (count - 1 - at)) & 1 for at in range(count))


def bit_of(position, bit):
    return lax.rem(position // (1 << bit), 2)


def block_bits(block, m):
    return tuple(bit_of(block, bit) for bit in range(m - 1, -1, -1))


def flipped(position, bit):
    return position + (1 << bit) * (1 - 2 * bit_of(position, bit))


def remote(source, target, sems, at, device):
    return pltpu.make_async_remote_copy(
        src_ref=source,
        dst_ref=target,
        send_sem=sems[0].at[at],
        recv_sem=sems[1].at[at],
        device_id=device,
        device_id_type=pl.DeviceIdType.MESH,
    )


def greet(partners):
    barrier = pltpu.get_barrier_semaphore()
    for partner in partners:
        pl.semaphore_signal(barrier, inc=1, device_id=partner, device_id_type=pl.DeviceIdType.MESH)
    pl.semaphore_wait(barrier, len(partners))


def turn_heads(turned, cosine, sine, heads):
    split = turned.reshape(heads, 2, HEAD_DIMENSION // 2, turned.shape[1])
    first, second = split[:, 0], split[:, 1]
    both = jnp.stack([first * cosine - second * sine, second * cosine + first * sine], axis=1)
    return both.reshape(turned.shape)


def turn_back(turned, cosine, sine, heads):
    return turn_heads(turned, cosine, -sine, heads)


def head_rows(group, member):
    head = group * HEAD_SHARE + member
    return pl.ds(pl.multiple_of(head * HEAD_DIMENSION, HEAD_DIMENSION), HEAD_DIMENSION)


def as_column(row):
    wide = jnp.broadcast_to(row.astype(jnp.float32), (8, row.shape[1]))
    return wide.T[:, 0:1]


def key_steps(blk, span):
    return blk // (1 << span) + 1


def fill_bias(bias, metas, query_segments, level, blk, m, piece, span):
    many = 1 << span
    key_at = lax.broadcasted_iota(jnp.int32, (many * piece, piece), 0)
    query_at = lax.broadcasted_iota(jnp.int32, (many * piece, piece), 1)

    @pl.loop(0, key_steps(blk, span))
    def _(step):
        rows = metas[block_bits(step, m - span)].reshape(many, 8, piece)
        columns = jnp.concatenate([rows[block].T for block in range(many)], axis=0)
        live = jnp.where(columns[:, 1:2] > level, columns[:, 0:1], -1.0)
        shift = (blk - many * step) * piece
        allowed = (live == query_segments) & (key_at <= query_at + shift) | (key_at == query_at + shift)
        masked = jnp.where(allowed, 0.0, masked_score).astype(bias.dtype)
        bias[pl.ds(many * step, many)] = masked.reshape(many, piece, piece)


def step_bias(bias, step, piece, span):
    many = 1 << span
    here = bias[pl.ds(many * step, many)].reshape(many * piece, piece).astype(jnp.float32)
    return jnp.concatenate([here] * HEAD_SHARE, axis=1)


def kv_weight_loads(key_hbm, value_hbm, target, sems):
    copies = []
    for group in range(KEY_VALUE_HEADS):
        for side, source in enumerate((key_hbm, value_hbm)):
            rows = pl.ds(group * HEAD_DIMENSION, HEAD_DIMENSION)
            place = pl.ds(group * PAIR + side * HEAD_DIMENSION, HEAD_DIMENSION)
            copies.append(pltpu.make_async_copy(source.at[rows], target.at[place], sems.at[2 * group + side]))
    return copies


def turn_keys(both, cosine, sine):
    half = HEAD_DIMENSION // 2
    split = both.reshape(KEY_VALUE_HEADS, 4, half, both.shape[1])
    first, second = split[:, 0], split[:, 1]
    turned = [first * cosine - second * sine, second * cosine + first * sine, split[:, 2], split[:, 3]]
    return jnp.stack(turned, axis=1).reshape(both.shape)


def spec(memory):
    return pl.BlockSpec(memory_space=memory)


def shaped(entry):
    return jax.ShapeDtypeStruct(*entry)


def spaces(entries):
    return [pltpu.VMEM(*entry) for entry in entries]


def dma_semaphores(*shapes):
    return [pltpu.SemaphoreType.DMA(shape) for shape in shapes]


class Piece:
    def __init__(self, at, kept_at, slot, flavour, family, sems, bits, middle=False):
        self.at, self.kept_at, self.slot, self.family, self.sems = at, kept_at, slot, family, sems
        self.m, self.n = bits
        left = list(range(self.m - 1, -1, -1))
        self.order = []
        for stage in range(self.m):
            place = len(left) - 1 if stage == 0 or flavour == 0 else 0
            self.order.append((left.pop(place), place, len(left)))
        self.last = self.m + self.n
        self.blk = lax.axis_index("blk")
        self.dp = lax.axis_index("dp") if self.n else None
        self.middle = middle
        if middle:
            inner = bit_of(self.dp, 0) != bit_of(self.dp, 1)
            outer = jnp.logical_not(inner)
            self.sends, self.receives = (outer, inner, inner), (inner, inner, outer)

    def half(self, ref, side):
        size = self.family.shape[self.family.split] // 2
        here = pl.ds(0 if isinstance(side, int) else pl.multiple_of(side * size, size), size)
        return ref.at[here, :] if self.family.split == 0 else ref.at[:, here]

    def held(self, stage):
        if stage == 0:
            return self.family.part, self.slot
        return self.family.blk[stage - 1], self.kept_at

    def copy(self, stage):
        m, family = self.m, self.family
        if stage < m:
            bit, place, others = self.order[stage]
            ref, index = self.held(stage)
            chosen = [slice(None)] * (others + 1)
            chosen[place] = 1 - bit_of(self.blk, bit)
            source = ref.at[(index, *chosen)]
            target = family.blk[stage].at[self.kept_at]
            device = {"blk": flipped(self.blk, bit)}
        elif self.middle:
            source, target, device = (
                (family.blk[m - 1], family.dp[0], {"dp": flipped(self.dp, 0)}),
                (family.dp[0], family.dp[1], {"dp": 3 - self.dp}),
                (family.out, family.out, {"dp": flipped(self.dp, 0)}),
            )[stage - m]
            source, target = source.at[self.kept_at], target.at[self.kept_at]
        elif stage < self.last:
            bit = stage - m
            if bit == 0:
                source = self.half(family.blk[m - 1].at[self.kept_at], 1 - bit_of(self.dp, 0))
            else:
                source = self.half(family.dp[bit - 1].at[self.kept_at], 0)
            target = self.half(family.dp[bit].at[self.kept_at], 0)
            device = {"dp": flipped(self.dp, bit)}
        else:
            source = self.half(family.out.at[self.kept_at], bit_of(self.dp, 0))
            target = source
            device = {"dp": flipped(self.dp, 0)}
        return remote(source, target, self.sems, (self.at, stage), device)

    def where(self, roles, stage, body):
        if self.middle and stage >= self.m:
            pl.when(roles[stage - self.m])(body)
        else:
            body()

    def start(self, stage):
        self.where(self.sends if self.middle else None, stage, lambda: self.copy(stage).start())

    def finish(self, stage):
        self.where(self.receives if self.middle else None, stage, lambda: self.receive(stage))

    def receive(self, stage):
        m, family = self.m, self.family
        self.copy(stage).wait_recv()
        if stage < m:
            bit, place, others = self.order[stage]
            ref, index = self.held(stage)
            for combo in itertools.product(range(2), repeat=others):
                chosen = list(combo)
                chosen.insert(place, bit_of(self.blk, bit))
                into = family.blk[stage].at[(self.kept_at, *combo)]
                self.add(into, into, ref.at[(index, *chosen)])
            if stage == 0:
                self.copy(0).wait_send()
        elif stage < self.last and self.middle:
            kept, sums = self.kept_at, family.dp
            if stage == m:
                self.add(sums[0].at[kept], sums[0].at[kept], family.blk[m - 1].at[kept])
            else:
                self.add(family.out.at[kept], sums[0].at[kept], sums[1].at[kept])
        elif stage < self.last:
            bit = stage - m
            got = self.half(family.dp[bit].at[self.kept_at], 0)
            if bit == 0:
                own = self.half(family.blk[m - 1].at[self.kept_at], bit_of(self.dp, 0))
            else:
                own = self.half(family.dp[bit - 1].at[self.kept_at], 0)
            into = got
            if stage == self.last - 1:
                into = self.half(family.out.at[self.kept_at], bit_of(self.dp, 0))
            self.add(into, got, own)

    def add(self, into, left, right):
        into[...] = left[...] + right[...]

    def drained(self, stages):
        for stage in stages:
            self.where(self.sends if self.middle else None, stage, lambda: self.copy(stage).wait_send())


def spread_heads(target, first, rows):
    piece = rows.shape[1]
    for head in range(QUERY_HEADS):
        group, member = divmod(head, HEAD_SHARE)
        here = slice(member * piece, (member + 1) * piece)
        target[group, first:first + HEAD_DIMENSION, here] = rows[head * HEAD_DIMENSION:(head + 1) * HEAD_DIMENSION]


def joined_heads(source, piece):
    return jnp.concatenate([
        source[group, :, member * piece:(member + 1) * piece]
        for group in range(KEY_VALUE_HEADS) for member in range(HEAD_SHARE)
    ], axis=0)


def feed_forward_backward(at, level, gradient, ready, done):
    column = at.router[level:level + 1, :].astype(jnp.float32)
    active = as_column(at.depths[...]) > float(level)
    hidden = at.hid_level[...]
    chosen = jax.nn.sigmoid(jnp.sum(hidden * column, axis=1, keepdims=True))
    at.dbranch[...] = jnp.where(active, chosen, 0.0) * gradient
    dchosen = jnp.where(active, jnp.sum(gradient * at.branch_level[...], axis=1, keepdims=True), 0.0)
    dlogit = dchosen * chosen * (1.0 - chosen)
    at.small[2 + level:3 + level, :] = jnp.sum(hidden * dlogit, axis=0, keepdims=True)
    at.grad_hidden[...] = gradient + dlogit * column
    at.dffn[...] = at.dbranch[...].astype(low)

    ready(0)
    dinner = plain_dot(at.dffn[...], at.w_down[...])
    at.dgate[...] = (dinner * at.slope_level[...].astype(jnp.float32)).astype(low)
    at.dup[...] = (dinner * at.silu_level[...].astype(jnp.float32)).astype(low)
    done()
    at.dnorm_turned[...] = plain_dot(at.w_gate[...], at.dgate[...].T) + plain_dot(at.w_up[...], at.dup[...].T)
    ready(1)
    dnorm = at.dnorm_turned[...].T
    dmiddle, gain_share = norm_gradient(dnorm, at.middle_level[...], at.norms[1:2, :].astype(jnp.float32))
    at.small[1:2, :] += gain_share
    at.grad_hidden[...] += dmiddle
    dattn = (at.dbranch[...] + dmiddle).astype(low)
    lead = at.far.shape[1] - dattn.shape[1]
    at.far[:, :lead] = jnp.zeros((dattn.shape[0], lead), low)
    at.far[:, lead:] = dattn
    dat = plain_dot(at.w_out[...], dattn.T).astype(low)
    at.dat[:, :HEAD_DIMENSION, :] = jnp.zeros((KEY_VALUE_HEADS, HEAD_DIMENSION, at.dat.shape[2]), low)
    spread_heads(at.dat, HEAD_DIMENSION, dat)


def forward_kernel(sizes, names, *refs):
    m, piece = sizes
    at = types.SimpleNamespace(**dict(zip(names, refs)))
    blk = lax.axis_index("blk")
    mine = block_bits(blk, m)
    kv, metas = at.kv, at.metas
    weights = (
        (at.w_query_hbm, at.w_query), (at.w_out_hbm, at.w_out), (at.w_gate_hbm, at.w_gate), (at.w_up_hbm, at.w_up), (at.w_down_hbm, at.w_down),
    )
    loads = [pltpu.make_async_copy(*pair, at.load_sems.at[index]) for index, pair in enumerate(weights)]
    kv_loads = kv_weight_loads(at.key_weight_hbm, at.value_weight_hbm, at.kv_weight, at.weight_sems)
    for load in kv_loads + loads:
        load.start()
    saved = (
        (at.normed, at.normed_out), (at.turned, at.turned_out), (kv, at.kv_out), (at.lse, at.lse_out),
        (at.att, at.att_out), (at.nffn, at.nffn_out), (at.inner, at.inner_out), (at.heads, at.heads_out),
    )

    def save(index, level):
        return pltpu.make_async_copy(
            saved[index][0].at[level] if index == 2 else saved[index][0], saved[index][1].at[level], at.save_sems.at[index, level]
        )

    first = (
        (at.hid.at[0], at.hid_out), (at.middle, at.middle_out), (at.silu, at.silu_out),
        (at.slope, at.slope_out), (at.branch, at.branch_out), (metas, at.metas_out),
        (at.far, at.far_out), (at.dat, at.dat_out), (at.dffn, at.dffn_out), (at.dgate, at.dgate_out), (at.dup, at.dup_out),
        (at.hid.at[1], at.hid_1_out),
    )
    late = [pltpu.make_async_copy(*pair, at.late_sems.at[index]) for index, pair in enumerate(first)]
    segment_row = at.segments[...].astype(jnp.float32)
    depth_column = as_column(at.depths[...])
    metas[mine] = jnp.concatenate(
        [segment_row, at.depths[...].astype(jnp.float32), jnp.zeros((6, piece), jnp.float32)], axis=0
    )
    greet([{"blk": flipped(blk, bit)} for bit in range(m)])

    def place(known):
        return tuple(slice(None) if bit in known else mine[m - 1 - bit] for bit in range(m - 1, -1, -1))

    orders = (list(range(1, m)), list(range(m - 1, 0, -1)))
    kv_sems = (at.kv_send, at.kv_recv)

    def kv_copies(level, group, stage):
        if stage == m - 1:
            ref = kv.at[(level, group, *place(range(1, m)))]
            return [remote(ref, ref, kv_sems, (level, group, 2 * stage), {"blk": flipped(blk, 0)})]
        copies = []
        for side, order in enumerate(orders):
            rows = pl.ds(side * (piece // 2), piece // 2)
            ref = kv.at[(level, group, *place(order[:stage]), rows)]
            copies.append(remote(ref, ref, kv_sems, (level, group, 2 * stage + side), {"blk": flipped(blk, order[stage])}))
        return copies

    def kv_advance(level, group, stage):
        if stage > 0:
            for copy in kv_copies(level, group, stage - 1):
                copy.wait_recv()
        if stage < m:
            for copy in kv_copies(level, group, stage):
                copy.start()

    def meta_copy(stage):
        bits = list(range(1, m)) + [0]
        ref = metas.at[place(bits[:stage])]
        return remote(ref, ref, (at.meta_send, at.meta_recv), stage, {"blk": flipped(blk, bits[stage])})

    meta_copy(0).start()
    cosine, sine = at.cosines[...], at.sines[...]
    gain_attn, gain_ffn = at.norms[0:1, :].astype(jnp.float32), at.norms[1:2, :].astype(jnp.float32)
    routers = at.router[...].astype(jnp.float32)
    at.hid[0] = at.tokens[...].T.astype(jnp.float32)
    late[0].start()
    at.turned[:, HEAD_DIMENSION:, :] = jnp.zeros((KEY_VALUE_HEADS, HEAD_DIMENSION, at.turned.shape[2]), low)

    @pl.loop(0, RECUR)
    def _(level):
        @pl.when(level > 0)
        def _():
            for index in (0, 1, 2, 3, 4, 7):
                save(index, 0).wait()

        hidden = at.hid[level]
        at.flat[...] = (hidden * rms_scale(hidden) * gain_attn).astype(low)
        at.normed[...] = at.flat[...].T

        @pl.when(level == 0)
        def _():
            for load in kv_loads:
                load.wait()

        both = turn_keys(plain_dot(at.kv_weight[...], at.normed[...]), cosine, sine).T.astype(low)
        for group in range(KEY_VALUE_HEADS):
            kv[(level, group, *mine)] = both[:, group * PAIR:(group + 1) * PAIR]
            kv_advance(level, group, 0)

        @pl.when(level == 0)
        def _():
            loads[0].wait()
            for stage in range(1, m - 1):
                meta_copy(stage - 1).wait_recv()
                meta_copy(stage).start()

        queries = turn_heads(plain_dot(at.flat[...], at.w_query[...]).T, cosine, sine, QUERY_HEADS)
        spread_heads(at.turned, 0, (queries * HEAD_DIMENSION ** (-0.5)).astype(low))

        @pl.when(level == 0)
        def _():
            for stage in range(max(1, m - 1), m):
                meta_copy(stage - 1).wait_recv()
                meta_copy(stage).start()

        for stage in range(1, m - 1):
            for group in range(KEY_VALUE_HEADS):
                kv_advance(level, group, stage)
        kv_advance(level, 0, m - 1)

        @pl.when(level == 0)
        def _():
            meta_copy(m - 1).wait_recv()
            late[5].start()

        fill_bias(at.bias, metas, segment_row, level.astype(jnp.float32), blk, m, piece, SPAN)

        @pl.loop(0, KEY_VALUE_HEADS)
        def _(group):
            @pl.when(group + 1 < KEY_VALUE_HEADS)
            def _():
                kv_advance(level, group + 1, m - 1)

            kv_advance(level, group, m)
            def scores_of(step):
                rows = kv[(level, group, *block_bits(step, m - SPAN))].reshape((1 << SPAN) * piece, PAIR)
                left = jnp.concatenate([rows.T[HEAD_DIMENSION:], jnp.ones((16, rows.shape[0]), low)], axis=0)
                return plain_dot(rows, at.turned[group]) + step_bias(at.bias, step, piece, SPAN), left

            at.top[...] = jnp.full_like(at.top, masked_score)
            at.total[...] = jnp.zeros_like(at.total)

            @pl.loop(0, key_steps(blk, SPAN))
            def _(index):
                scores, left = scores_of(key_steps(blk, SPAN) - 1 - index)
                before = at.top[0:1, :]
                after = jnp.maximum(before, jnp.max(scores, axis=0, keepdims=True))
                at.top[0:1, :] = after
                raised = jnp.exp(scores - after).astype(low)
                at.total[...] = at.total[...] * jnp.exp(before - after) + plain_dot(left, raised)

            sums = at.total[HEAD_DIMENSION:HEAD_DIMENSION + 1, :]
            at.lse[pl.ds(group, 1), :] = at.top[0:1, :] + jnp.log(sums)
            at.heads[group] = (at.total[:HEAD_DIMENSION, :] / sums).astype(low)

        at.att[...] = joined_heads(at.heads, piece)
        for index in (0, 1, 2, 3, 4, 7):
            save(index, level).start()

        @pl.when(level == 0)
        def _():
            loads[1].wait()

        @pl.when(level > 0)
        def _():
            save(5, 0).wait()
            save(6, 0).wait()
            for copy in late[1:5]:
                copy.wait()

        attn = plain_dot(at.att[...].T, at.w_out[...])
        mid = at.hid[level] + attn
        at.middle[...] = mid
        at.branch[...] = attn
        at.flat[...] = (mid * rms_scale(mid) * gain_ffn).astype(low)
        at.nffn[...] = at.flat[...].T
        save(5, level).start()

        @pl.when(level == 0)
        def _():
            loads[2].wait()
            loads[3].wait()

        gate_pre = plain_dot(at.flat[...], at.w_gate[...])
        up_pre = plain_dot(at.flat[...], at.w_up[...])
        opened = jax.nn.sigmoid(gate_pre)
        passed = gate_pre * opened
        at.silu[...] = passed.astype(low)
        at.slope[...] = (up_pre * (opened + passed - passed * opened)).astype(low)
        at.inner[...] = (passed * up_pre).astype(low).T
        save(6, level).start()

        @pl.when(level == 0)
        def _():
            loads[4].wait()

        at.branch[...] += plain_dot(at.w_down[...], at.inner[...]).T
        column = jnp.where(level == 0, routers[0:1, :], routers[1:2, :])
        logit = jnp.sum(at.hid[level] * column, axis=1, keepdims=True)
        weight = jnp.where(depth_column > level.astype(jnp.float32), jax.nn.sigmoid(logit), 0.0)
        at.hid[level + 1] = at.hid[level] + weight * at.branch[...]

        @pl.when(level == 0)
        def _():
            for copy in late[1:5]:
                copy.start()

    at.hidden_out[...] = at.hid[RECUR].T
    top = RECUR - 1
    at.hid_level, at.branch_level, at.middle_level = at.hid.at[top], at.branch, at.middle
    at.silu_level, at.slope_level = at.silu, at.slope
    at.small[...] = jnp.zeros_like(at.small)
    feed_forward_backward(at, top, at.cotangent[...].T.astype(jnp.float32), lambda part: None, lambda: None)
    for copy in late[6:]:
        copy.start()
    for stage in range(m):
        meta_copy(stage).wait_send()
    for level in range(RECUR):
        for group in range(KEY_VALUE_HEADS):
            for stage in range(m):
                for copy in kv_copies(level, group, stage):
                    copy.wait_send()
    for index in range(len(saved)):
        save(index, RECUR - 1).wait()
    for copy in late[:1] + late[5:]:
        copy.wait()


def far_width(width):
    return 2 * width + 2 * KEYS_WIDTH - 1536


def forward(small, weights, nb):
    m = nb.bit_length() - 1
    width, piece = small["tokens"].shape
    hidden_units = weights["w_gate_hbm"].shape[1]
    blocks, wide = (2,) * m, HEAD_SHARE * piece
    rows, turned = ((piece, width), jnp.float32), ((RECUR, width, piece), low)
    hidden = ((piece, hidden_units), low)
    saved = dict(
        normed=turned, turned=((RECUR, KEY_VALUE_HEADS, PAIR, wide), low), kv=((RECUR, KEY_VALUE_HEADS, *blocks, piece, PAIR), low),
        lse=((RECUR, 8, wide), jnp.float32), att=turned, nffn=turned, inner=((RECUR, hidden_units, piece), low),
        metas=((*blocks, 8, piece), jnp.float32), far=((piece, far_width(width)), low), dat=((KEY_VALUE_HEADS, PAIR, wide), low),
        heads=((RECUR, KEY_VALUE_HEADS, HEAD_DIMENSION, wide), low),
        dffn=((piece, width), low), dgate=hidden, dup=hidden,
    )
    first = dict(hid=rows, middle=rows, silu=hidden, slope=hidden, branch=rows)
    outs = dict(hidden_out=((width, piece), jnp.float32), grad_hidden=rows, small=((8, width), jnp.float32))
    anywhere = {name + "_out": entry for name, entry in (saved | first | dict(hid_1=rows)).items()}
    single = {name: (shape[1:], dtype) for name, (shape, dtype) in saved.items() if shape[0] == RECUR and name not in ("kv", "metas")}
    buffers = {name[:-4]: (array.shape, array.dtype) for name, array in weights.items()} | saved | single | first | dict(
        kv_weight=((2 * KEYS_WIDTH, width), low),
        hid=((RECUR + 1, piece, width), jnp.float32), flat=((piece, width), low),
        bias=((nb, piece, piece), jnp.float32), top=((8, wide), jnp.float32),
        total=((HEAD_DIMENSION + 16, wide), jnp.float32), dbranch=rows, dnorm_turned=((width, piece), jnp.float32),
    )
    semaphores = dict(
        load_sems=(5,), weight_sems=(2 * KEY_VALUE_HEADS,), save_sems=(8, RECUR), late_sems=(12,), kv_send=(RECUR, KEY_VALUE_HEADS, 2 * m),
        kv_recv=(RECUR, KEY_VALUE_HEADS, 2 * m), meta_send=(m,), meta_recv=(m,),
    )
    results = pl.pallas_call(
        functools.partial(forward_kernel, (m, piece), (*small, *weights, *outs, *anywhere, *buffers, *semaphores)),
        out_shape=[shaped(entry) for entry in (outs | anywhere).values()],
        in_specs=[spec(pltpu.VMEM)] * len(small) + [spec(pl.ANY)] * len(weights),
        out_specs=[spec(pltpu.VMEM)] * len(outs) + [spec(pl.ANY)] * len(anywhere),
        scratch_shapes=spaces(buffers.values()) + dma_semaphores(*semaphores.values()),
        compiler_params=pltpu.CompilerParams(
            collective_id=1, has_side_effects=True, vmem_limit_bytes=VMEM_LIMIT
        ),
        cost_estimate=pl.CostEstimate(
            flops=3 * RECUR * piece * width * 10240, bytes_accessed=48 * 1024 * 1024, transcendentals=0
        ),
        name="forward_levels",
    )(*small.values(), *weights.values())
    return dict(zip((*outs, *(name[:-4] for name in anywhere)), results))


class AttentionBackward:
    def __init__(self, at, m, piece, level, span):
        self.at, self.m, self.piece, self.level, self.span = at, m, piece, level, span
        self.blk = lax.axis_index("blk")
        self.family = types.SimpleNamespace(part=at.part, blk=at.halves, dp=(), out=None, shape=(piece // 2, PAIR), split=0)

    def pieces(self, group):
        sems = (self.at.kv_send, self.at.kv_recv)
        return [
            Piece(2 * group + side, 2 * group + side, 2 * group + side, side, self.family, sems, (self.m, 0))
            for side in range(2)
        ]

    def move(self, group, stage):
        for piece_of in self.pieces(group):
            piece_of.finish(stage)
            if stage + 1 < self.m:
                piece_of.start(stage + 1)

    def begin(self):
        at = self.at
        query_segments = at.metas[block_bits(self.blk, self.m)][0:1, :]
        fill_bias(at.bias, at.metas, query_segments, float(self.level), self.blk, self.m, self.piece, self.span)

    def group(self, group):
        at, m, piece, blk = self.at, self.m, self.piece, self.blk
        half = piece // 2
        queries, dat = at.turned[group], at.dat_turned[group]
        at.query_rows[...] = queries.T
        at.dat_rows[...] = dat.T
        product = dat[HEAD_DIMENSION:].astype(jnp.float32) * at.heads[group].astype(jnp.float32)
        carried = jnp.sum(product, axis=0, keepdims=True)
        log_total = at.lse[pl.ds(group, 1), :]
        span, lead = self.span, m - self.span

        def share_of(step):
            rows = at.kv[(group, *block_bits(step, lead))].reshape((1 << span) * piece, PAIR)
            probability = jnp.exp(plain_dot(rows, at.turned[group]) + step_bias(at.bias, step, piece, span) - log_total)
            dprob = plain_dot(rows, at.dat_turned[group])
            dscores = (probability * (dprob - carried)).astype(low)
            share = plain_dot(dscores, at.query_rows[...]) + plain_dot(probability.astype(low), at.dat_rows[...])
            share = share.astype(low)
            for block in range(1 << span):
                for side in range(2):
                    first = block * piece + side * half
                    place = (2 * group + side, *block_bits(step, lead), *bits_of(block, span))
                    at.part[place] = share[first:first + half]
            return plain_dot(rows.T[:HEAD_DIMENSION], dscores)

        at.dq_heads[group] = jnp.zeros(at.dq_heads.shape[1:], jnp.float32)

        @pl.loop(0, key_steps(blk, span))
        def _(step):
            at.dq_heads[group] += share_of(step)

        @pl.loop(key_steps(blk, span), 1 << lead)
        def _(step):
            for block in range(1 << span):
                for side in range(2):
                    place = (2 * group + side, *block_bits(step, lead), *bits_of(block, span))
                    at.part[place] = jnp.zeros((half, PAIR), low)

        for piece_of in self.pieces(group):
            piece_of.start(0)

    def follow(self, group):
        for stage in range(self.m - 1):
            earlier = group - 1 - stage
            if isinstance(group, int):
                if 0 <= earlier < KEY_VALUE_HEADS:
                    self.move(earlier, stage)
            else:
                @pl.when(earlier >= 0)
                def _():
                    self.move(earlier, stage)

    def queries(self, cosine, sine):
        at = self.at
        dqueries = turn_back(joined_heads(at.dq_heads, self.piece) * HEAD_DIMENSION ** (-0.5), cosine, sine, QUERY_HEADS).astype(low)
        self.put(2 * KEYS_WIDTH, dqueries.T)
        at.dnorm[...] = plain_dot(at.w_query[...], dqueries).T

    def put(self, column, values):
        self.at.near[:, column:column + values.shape[1]] = values

    def keys(self, cosine, sine):
        at, m = self.at, self.m
        filled = 2 * KEYS_WIDTH + QUERY_HEADS * HEAD_DIMENSION
        self.put(filled, jnp.zeros((self.piece, at.near.shape[1] - filled), low))
        sums = []
        for group in range(KEY_VALUE_HEADS):
            self.move(group, m - 1)
            sums.append(jnp.concatenate([at.halves[m - 1][2 * group], at.halves[m - 1][2 * group + 1]], axis=0))
        both = jnp.concatenate(sums, axis=1).astype(jnp.float32).T
        both = turn_keys(both, cosine, -sine).astype(low).T
        self.put(0, both)
        at.dnorm[...] += plain_dot(both, at.kv_weight[...])

    def drained(self):
        for group in range(KEY_VALUE_HEADS):
            for piece_of in self.pieces(group):
                piece_of.drained(range(1, self.m))


def attention_buffers(nb, piece, width, bias_type):
    m, wide, heads = nb.bit_length() - 1, HEAD_SHARE * piece, 2 * KEY_VALUE_HEADS
    padded, pad_rows = ((KEY_VALUE_HEADS, PAIR, wide), low), ((wide, PAIR), low)
    buffers = dict(
        turned=padded, dat_turned=padded, heads=((KEY_VALUE_HEADS, HEAD_DIMENSION, wide), low), kv=((KEY_VALUE_HEADS, *(2,) * m, piece, PAIR), low),
        lse=((8, wide), jnp.float32), metas=((*(2,) * m, 8, piece), jnp.float32), w_query=((width, width), low),
        kv_weight=((2 * KEYS_WIDTH, width), low), dq_heads=((KEY_VALUE_HEADS, HEAD_DIMENSION, wide), jnp.float32),
        bias=((nb, piece, piece), bias_type), query_rows=pad_rows, dat_rows=pad_rows,
        part=((heads, *(2,) * m, piece // 2, PAIR), low),
        dnorm=((piece, width), jnp.float32), hid=((piece, width), jnp.float32),
    )
    for stage in range(m):
        buffers["half_%d" % stage] = ((heads, *(2,) * (m - 1 - stage), piece // 2, PAIR), low)
    return buffers


def backward_kernel(sizes, names, *refs):
    m, piece, level = sizes
    at = types.SimpleNamespace(**dict(zip(names, refs)))
    at.halves = [getattr(at, "half_%d" % stage) for stage in range(m)]
    at.near = at.near_out
    blk = lax.axis_index("blk")
    pairs = (
        (at.metas_hbm, at.metas), (at.turned_hbm.at[level], at.turned), (at.dat_hbm, at.dat_turned),
        (at.heads_hbm.at[level], at.heads), (at.lse_hbm.at[level], at.lse), (at.kv_hbm.at[level], at.kv),
        (at.w_query_hbm, at.w_query),
        (at.grad_hbm, at.grad_hidden), (at.hid_1_hbm, at.hid),
        (at.hid_0_hbm, at.hid_level), (at.branch_hbm, at.branch_level), (at.w_down_hbm, at.w_down),
        (at.slope_hbm, at.slope_level), (at.silu_hbm, at.silu_level), (at.w_gate_hbm, at.w_gate), (at.w_up_hbm, at.w_up),
        (at.middle_hbm, at.middle_level), (at.w_out_hbm, at.w_out),
    )
    loads = [pltpu.make_async_copy(*pair, at.load_sems.at[index]) for index, pair in enumerate(pairs)]
    loads += kv_weight_loads(at.key_weight_hbm, at.value_weight_hbm, at.kv_weight, at.weight_sems)
    for load in loads:
        load.start()
    saves = [
        pltpu.make_async_copy(*pair, at.save_sems.at[index])
        for index, pair in enumerate(((at.dgate, at.dgate_out), (at.dup, at.dup_out)))
    ]
    greet([{"blk": flipped(blk, bit)} for bit in range(m)])
    work = AttentionBackward(at, m, piece, level, SPAN)
    loads[0].wait()
    work.begin()
    for load in loads[1:6]:
        load.wait()

    @pl.loop(0, KEY_VALUE_HEADS)
    def _(group):
        work.group(group)
        work.follow(group)

    cosine, sine = at.cosines[...], at.sines[...]
    for virtual in range(KEY_VALUE_HEADS, KEY_VALUE_HEADS + m - 1):
        work.follow(virtual)
        if virtual == KEY_VALUE_HEADS:
            loads[6].wait()
            work.queries(cosine, sine)
    for load in loads[7:]:
        load.wait()
    work.keys(cosine, sine)
    dhidden, gain_share = norm_gradient(at.dnorm[...], at.hid[...], at.norms[0:1, :].astype(jnp.float32))
    at.small[...] = at.small_before[...]
    at.small[0:1, :] = gain_share
    gradient = at.grad_hidden[...] + dhidden
    at.dnorm[...] = gradient
    feed_forward_backward(at, level - 1, at.dnorm[...], lambda part: None, lambda: [save.start() for save in saves])
    work.drained()
    for save in saves:
        save.wait()


def backward(level, small, operands, nb):
    m = nb.bit_length() - 1
    piece, width = operands["grad_hbm"].shape
    hidden_units = operands["w_gate_hbm"].shape[1]
    rows, flat, hidden = ((piece, width), jnp.float32), ((piece, width), low), ((piece, hidden_units), low)
    outs = dict(
        grad_hidden=rows, small=((8, width), jnp.float32), near_out=((piece, 1792), low), dffn=flat,
        dat=((KEY_VALUE_HEADS, PAIR, HEAD_SHARE * piece), low), far=((piece, far_width(width)), low),
    )
    anywhere = dict(dgate_out=hidden, dup_out=hidden)
    buffers = attention_buffers(nb, piece, width, jnp.float32) | dict(
        hid_level=rows, branch_level=rows, middle_level=rows, w_down=((width, hidden_units), low), slope_level=hidden,
        silu_level=hidden, w_gate=((width, hidden_units), low), w_up=((width, hidden_units), low),
        w_out=((width, width), low), dbranch=rows, dnorm_turned=((width, piece), jnp.float32), dgate=hidden, dup=hidden,
    )
    sums = (2 * KEY_VALUE_HEADS, m)
    semaphores = dict(load_sems=(18,), weight_sems=(2 * KEY_VALUE_HEADS,), save_sems=(2,), kv_send=sums, kv_recv=sums)
    results = pl.pallas_call(
        functools.partial(
            backward_kernel, (m, piece, level), (*small, *operands, *outs, *anywhere, *buffers, *semaphores)
        ),
        out_shape=[shaped(entry) for entry in (outs | anywhere).values()],
        in_specs=[spec(pltpu.VMEM)] * len(small) + [spec(pl.ANY)] * len(operands),
        out_specs=[spec(pltpu.VMEM)] * len(outs) + [spec(pl.ANY)] * len(anywhere),
        scratch_shapes=spaces(buffers.values()) + dma_semaphores(*semaphores.values()),
        compiler_params=pltpu.CompilerParams(
            collective_id=2, has_side_effects=True, vmem_limit_bytes=VMEM_LIMIT
        ),
        cost_estimate=pl.CostEstimate(
            flops=2 * piece * width * 20000, bytes_accessed=32 * 1024 * 1024, transcendentals=0
        ),
        name="backward_level",
    )(*small.values(), *operands.values())
    return dict(zip((*outs, *anywhere), results))


WIDE_SLOTS, DOWN_SLOTS = 4, 2


def final_kernel(sizes, names, *refs):
    nb, m, n, piece, rows, padded, near_width = sizes
    at = types.SimpleNamespace(**dict(zip(names, refs)))
    at.halves = [getattr(at, "half_%d" % stage) for stage in range(m)]
    blk, dp = lax.axis_index("blk"), lax.axis_index("dp")
    at.near = at.gate_side.at[pl.ds(0, piece), pl.ds(0, near_width)]
    counter = itertools.count()

    def load(source, target):
        return pltpu.make_async_copy(source, target, at.load_sems.at[next(counter)])

    def both_lanes(ref, target):
        return [load(ref.at[level], target.at[:, pl.ds(level * piece, piece)]) for level in range(RECUR)]

    def both_rows(low_ref, deep_ref, target, width):
        pairs = ((low_ref, 0), (deep_ref, piece))
        return [load(ref, target.at[pl.ds(first, piece), pl.ds(0, width)]) for ref, first in pairs]

    hidden_units, width = at.gate_side.shape[1], at.dffn.shape[1]
    far_lanes = at.far_0_hbm.shape[1]
    loads = types.SimpleNamespace(
        nffn=both_lanes(at.nffn_hbm, at.left),
        dgate=both_rows(at.dgate_0_hbm, at.dgate_1_hbm, at.gate_side, hidden_units),
        inner=both_lanes(at.inner_hbm, at.inner),
        dffn=both_rows(at.dffn_0_hbm, at.dffn_1_hbm, at.dffn, width),
        metas=[load(at.metas_hbm, at.metas)],
        heads=[
            load(at.turned_hbm.at[0], at.turned), load(at.dat_hbm, at.dat_turned), load(at.heads_hbm.at[0], at.heads),
            load(at.lse_hbm.at[0], at.lse), load(at.kv_hbm.at[0], at.kv),
        ],
        dup=both_rows(at.dup_0_hbm, at.dup_1_hbm, at.up_side, hidden_units),
        w_query=[load(at.w_query_hbm, at.w_query)],
        rest=[
            load(at.hid_hbm, at.hid), load(at.grad_hbm, at.grad),
        ],
        attended=both_lanes(at.attended_hbm, at.left_attended),
        kv_weight=kv_weight_loads(at.key_weight_hbm, at.value_weight_hbm, at.kv_weight, at.weight_sems),
    )
    late = types.SimpleNamespace(
        near=[load(at.near_1_hbm, at.gate_side.at[pl.ds(piece, piece), pl.ds(0, near_width)])],
        far=both_rows(at.far_0_hbm, at.far_1_hbm, at.up_side, far_lanes),
        normed=both_lanes(at.normed_hbm, at.left),
    )

    def begin(copies):
        for copy in copies:
            copy.start()

    def ready(copies):
        for copy in copies:
            copy.wait()

    for copies in vars(loads).values():
        begin(copies)
    greet([{"blk": flipped(blk, bit)} for bit in range(m)] + [{"dp": flipped(dp, bit)} for bit in range(n)])

    down_rows = at.part_down.shape[-2]

    def family(name, shape, split):
        return types.SimpleNamespace(
            part=getattr(at, "part_" + name), out=getattr(at, "out_" + name), shape=shape, split=split,
            blk=[getattr(at, "blk_%s_%d" % (name, stage)) for stage in range(m)],
            dp=[getattr(at, "dp_%s_%d" % (name, stage)) for stage in range(n)],
        )

    wide = family("wide", (2 * padded, UNIT_COLUMNS), 1)
    down = family("down", (down_rows, width), 0)
    little = family("small", (16, 128), 0)
    sems = (at.send_sems, at.recv_sems)
    units = itertools.count()

    def unit(holder, index, flavour, halves=n != 2):
        return Piece(next(units), index, index % holder.part.shape[0], flavour, holder, sems, (m, n), not halves)

    pairs = [[unit(wide, index, 0), unit(down, index, 1)] for index in range(5)]
    pairs += [[unit(wide, index, 0), unit(wide, index + 1, 1)] for index in (5, 7, 9)]
    pairs += [[unit(wide, 11, 0, True), unit(wide, 12, 1, True)]]
    pairs += [[unit(wide, 13, 0, True), unit(wide, 14, 1, True), unit(little, 0, 0, True)]]

    def compute_wide(index, slot):
        if index == 0:
            ready(loads.nffn)
            ready(loads.dgate)
        if index == 5:
            begin(late.near)
            ready(loads.dup)
        if index == 10:
            begin(late.far)
            begin(late.normed)
            ready(late.near)
            ready(late.normed)
            ready(loads.attended)
            ready(late.far)
        block, column = index // 5, (index % 5) * UNIT_COLUMNS
        second = 1280 + column
        upper_columns, lower_columns = slice(column, column + UNIT_COLUMNS), slice(second, second + UNIT_COLUMNS)
        if block < 2:
            right = at.gate_side if block == 0 else at.up_side
            upper = plain_dot(at.left[...], right[:, upper_columns])
            lower = plain_dot(at.left[...], right[:, lower_columns])
        else:
            upper = plain_dot(at.left[...], at.gate_side[:, upper_columns])
            lower = None
            if second < 1600:
                lower = plain_dot(at.left[...], at.gate_side[:, lower_columns])
            if second >= 1536:
                more = plain_dot(at.left_attended[...], at.up_side[:, second - 1536:second - 1536 + UNIT_COLUMNS])
                lower = more if lower is None else lower + more
        for target in range(nb):
            here = slice(target * padded, (target + 1) * padded)
            both = jnp.concatenate([upper[here], lower[here]], axis=0)
            at.part_wide[(slot, *bits_of(target, m))] = both.astype(low)

    def compute_down(index, slot):
        if index == 0:
            ready(loads.inner)
            ready(loads.dffn)
        firsts = [(target * 5 + index) * down_rows for target in range(nb)]
        left = jnp.concatenate([at.inner[first:first + down_rows, :] for first in firsts], axis=0)
        result = plain_dot(left, at.dffn[...])
        for target in range(nb):
            at.part_down[(slot, *bits_of(target, m))] = result[target * down_rows:(target + 1) * down_rows].astype(low)

    def compute_small():
        total = at.small_before[...]
        total = total + jnp.concatenate([at.gain_row[...], jnp.zeros((7, width), jnp.float32)], axis=0)
        at.part_small[...] = jnp.zeros_like(at.part_small)
        for target in range(nb):
            at.part_small[(0, *bits_of(target, m), slice(0, 8), slice(0, rows))] = total[:, target * rows:(target + 1) * rows]

    def compute(piece_of):
        if piece_of.family is wide:
            compute_wide(piece_of.kept_at, piece_of.slot)
        elif piece_of.family is down:
            compute_down(piece_of.kept_at, piece_of.slot)
        else:
            compute_small()
        piece_of.start(0)

    def moves(tick):
        for stage in range(m + n - 1, -1, -1):
            if 0 <= tick - stage < len(pairs):
                for piece_of in pairs[tick - stage]:
                    piece_of.finish(stage)
                    piece_of.start(stage + 1)

    work = AttentionBackward(at, m, piece, 0, 1)
    for pair in pairs[:2]:
        for piece_of in pair:
            compute(piece_of)
    ready(loads.metas)
    work.begin()
    ready(loads.heads)
    for group in range(KEY_VALUE_HEADS):
        moves(group)
        for piece_of in pairs[group + 2]:
            compute(piece_of)
        work.group(group)
        work.follow(group)
    cosine, sine = at.cosines[...], at.sines[...]
    moves(5)
    compute(pairs[7][0])
    ready(loads.w_query)
    for virtual in range(KEY_VALUE_HEADS, KEY_VALUE_HEADS + m - 1):
        work.follow(virtual)
        if virtual == KEY_VALUE_HEADS:
            work.queries(cosine, sine)
    moves(6)
    ready(loads.rest)
    ready(loads.kv_weight)
    work.keys(cosine, sine)
    compute(pairs[7][1])
    moves(7)
    for piece_of in pairs[8] + pairs[9][:2]:
        compute(piece_of)
    dhidden, gain_share = norm_gradient(at.dnorm[...], at.hid[...], at.norms[0:1, :].astype(jnp.float32))
    at.gain_row[...] = gain_share
    at.grad_out[...] = (at.grad[...] + dhidden).T
    compute(pairs[9][2])
    for tick in range(8, len(pairs) + m + n - 1):
        moves(tick)
    for pair in pairs:
        for piece_of in pair:
            piece_of.finish(m + n)
    for pair in pairs:
        for piece_of in pair:
            piece_of.drained(range(1, m + n + 1))
    work.drained()


def unpack_kernel(sizes, wide_hbm, down_hbm, little_hbm, hidden_in, gradient_in, *refs):
    rows, padded = sizes
    norm_attn, norm_ffn, query, key, value, out, gate, up, down_out, router, hidden, gradient = refs[:12]
    wide, down, little, rest, sems = refs[12:]
    carried = [
        pltpu.make_async_copy(source, target, sems.at[at])
        for at, (source, target) in enumerate(((hidden_in, hidden), (gradient_in, gradient)))
    ]
    loads = [
        pltpu.make_async_copy(source, target, sems.at[2 + at])
        for at, (source, target) in enumerate(((wide_hbm, wide), (down_hbm, down), (little_hbm, little)))
    ]
    for copy in loads + carried:
        copy.start()
    for load in loads:
        load.wait()
    norm_attn[...] = little[0, 0:1, :rows]
    norm_ffn[...] = little[0, 1:2, :rows]
    router[...] = little[0, 2:4, :rows]
    for unit in range(5):
        for first, target in ((0, gate), (5, up), (10, rest)):
            tile = wide[first + unit].astype(jnp.float32)
            for side in range(2):
                column = side * 1280 + unit * UNIT_COLUMNS
                target[:, column:column + UNIT_COLUMNS] = tile[side * padded:side * padded + rows]
        down_rows = down.shape[1]
        down_out[unit * down_rows:(unit + 1) * down_rows, :] = down[unit].astype(jnp.float32)
    width = query.shape[1]
    both = rest[:, :2 * KEYS_WIDTH].T
    for group in range(KEY_VALUE_HEADS):
        here, first = slice(group * HEAD_DIMENSION, (group + 1) * HEAD_DIMENSION), group * PAIR
        key[here, :] = both[first:first + HEAD_DIMENSION]
        value[here, :] = both[first + HEAD_DIMENSION:first + PAIR]
    query[...] = rest[:, 2 * KEYS_WIDTH:2 * KEYS_WIDTH + width]
    out[...] = rest[:, 2 * KEYS_WIDTH + width:]
    for copy in carried:
        copy.wait()


def final(small, saved, top, bottom, weights, mesh_sizes):
    nb, nd = mesh_sizes
    m, n = nb.bit_length() - 1, nd.bit_length() - 1
    grad = bottom["grad_hidden"]
    piece, width = grad.shape
    hidden_units = weights["w_gate_hbm"].shape[1]
    rows = width // nb
    padded = -(-rows // 8) * 8
    down_rows = hidden_units // nb // 5
    tokens = RECUR * piece

    def spread(array):
        if padded == rows:
            return array
        split = array.reshape(RECUR, nb, rows, piece)
        return jnp.pad(split, ((0, 0), (0, 0), (0, padded - rows), (0, 0))).reshape(RECUR, nb * padded, piece)

    inputs = small | dict(small_before=bottom["small"])
    operands = dict(
        metas_hbm=saved["metas"], turned_hbm=saved["turned"], dat_hbm=bottom["dat"], heads_hbm=saved["heads"],
        lse_hbm=saved["lse"], kv_hbm=saved["kv"], w_query_hbm=weights["w_query_hbm"],
        key_weight_hbm=weights["key_weight_hbm"], value_weight_hbm=weights["value_weight_hbm"], hid_hbm=saved["hid"],
        grad_hbm=grad, inner_hbm=saved["inner"], nffn_hbm=spread(saved["nffn"]), normed_hbm=spread(saved["normed"]),
        attended_hbm=spread(saved["att"]), dffn_0_hbm=bottom["dffn"], dffn_1_hbm=top["dffn"],
        dgate_0_hbm=bottom["dgate_out"], dgate_1_hbm=top["dgate"], dup_0_hbm=bottom["dup_out"], dup_1_hbm=top["dup"],
        far_0_hbm=bottom["far"], far_1_hbm=top["far"], near_1_hbm=bottom["near_out"],
    )
    near_width = bottom["near_out"].shape[1]
    families = (
        ("wide", 15, (2 * padded, UNIT_COLUMNS), low, WIDE_SLOTS, 1), ("down", 5, (down_rows, width), low, DOWN_SLOTS, 0),
        ("small", 1, (16, 128), jnp.float32, 1, 0),
    )
    outs = dict(grad_out=((width, piece), jnp.float32))
    buffers = attention_buffers(nb, piece, width, low) | dict(
        grad=((piece, width), jnp.float32), gate_side=((tokens, hidden_units), low), up_side=((tokens, hidden_units), low),
        inner=((hidden_units, tokens), low), left=((nb * padded, tokens), low), left_attended=((nb * padded, tokens), low),
        dffn=((tokens, width), low), gain_row=((1, width), jnp.float32),
    )
    for name, count, shape, dtype, slots, split in families:
        outs["out_" + name] = ((count, *shape), dtype)
        buffers["part_" + name] = ((slots, *(2,) * m, *shape), dtype)
        for stage in range(m):
            buffers["blk_%s_%d" % (name, stage)] = ((count, *(2,) * (m - 1 - stage), *shape), dtype)
        for stage in range(n):
            buffers["dp_%s_%d" % (name, stage)] = ((count, *shape), dtype)
    sums, hops = (2 * KEY_VALUE_HEADS, m), (21, m + n + 1)
    semaphores = dict(load_sems=(32,), weight_sems=(2 * KEY_VALUE_HEADS,), kv_send=sums, kv_recv=sums, send_sems=hops, recv_sems=hops)
    names = (*inputs, *operands, *outs, *buffers, *semaphores)
    gradient, wide, down, little = pl.pallas_call(
        functools.partial(final_kernel, (nb, m, n, piece, rows, padded, near_width), names),
        out_shape=[shaped(entry) for entry in outs.values()],
        in_specs=[spec(pltpu.VMEM)] * len(inputs) + [spec(pl.ANY)] * len(operands),
        out_specs=[spec(pltpu.VMEM)] * len(outs),
        scratch_shapes=spaces(buffers.values()) + dma_semaphores(*semaphores.values()),
        compiler_params=pltpu.CompilerParams(
            collective_id=0, has_side_effects=True, vmem_limit_bytes=VMEM_LIMIT
        ),
        cost_estimate=pl.CostEstimate(
            flops=2 * tokens * width * 14000, bytes_accessed=30 * 1024 * 1024, transcendentals=0
        ),
        name="weight_grads",
    )(*inputs.values(), *operands.values())
    shapes = (
        (1, rows), (1, rows), (rows, width), (KEYS_WIDTH, rows), (KEYS_WIDTH, rows), (rows, width),
        (rows, hidden_units), (rows, hidden_units), (5 * down_rows, width), (2, rows), (width, piece), (width, piece),
    )
    outs = pl.pallas_call(
        functools.partial(unpack_kernel, (rows, padded)),
        out_shape=[jax.ShapeDtypeStruct(shape, jnp.float32) for shape in shapes],
        in_specs=[spec(pl.ANY)] * 5,
        out_specs=[spec(pltpu.VMEM)] * 12,
        scratch_shapes=[pltpu.VMEM(array.shape, array.dtype) for array in (wide, down, little)]
        + spaces([((rows, 2560), jnp.float32)]) + dma_semaphores((5,)),
        compiler_params=pltpu.CompilerParams(vmem_limit_bytes=VMEM_LIMIT),
        name="unpack",
    )(wide, down, little, saved["hidden_out"], gradient)
    norm_a, norm_f, query, key, value, out, gate, up, down, router, hidden, gradient = outs
    return (
        hidden.T[None], gradient.T[None], norm_a[0], norm_f[0], query, key.T, value.T, out, gate, up, down, router.T,
    )


def local(
    tokens,
    depths,
    segments,
    norm_attn,
    norm_ffn,
    w_query,
    key_weight,
    value_weight,
    w_out,
    w_gate,
    w_up,
    w_down,
    w_router,
    cotangent,
    mesh_sizes,
):
    piece = tokens.shape[1]
    positions = lax.axis_index("blk") * piece + jnp.arange(piece, dtype=jnp.int32)
    angles = frequencies(HEAD_DIMENSION)[:, None] * positions.astype(jnp.float32)[None, :]
    tables = dict(cosines=jnp.cos(angles), sines=jnp.sin(angles), norms=jnp.stack([norm_attn, norm_ffn]))
    routing = dict(router=w_router.T, depths=depths)
    heads = dict(w_query_hbm=w_query, key_weight_hbm=key_weight.T, value_weight_hbm=value_weight.T)
    weights = heads | dict(w_out_hbm=w_out, w_gate_hbm=w_gate, w_up_hbm=w_up, w_down_hbm=w_down.T)
    nb = mesh_sizes[0]
    saved = forward(
        tables | routing | dict(tokens=tokens[0].T, cotangent=cotangent[0].T, segments=segments), weights, nb
    )
    operands = dict(
        metas_hbm=saved["metas"], turned_hbm=saved["turned"], dat_hbm=saved["dat"], heads_hbm=saved["heads"],
        lse_hbm=saved["lse"], kv_hbm=saved["kv"], grad_hbm=saved["grad_hidden"], hid_1_hbm=saved["hid_1"],
        hid_0_hbm=saved["hid"], branch_hbm=saved["branch"], slope_hbm=saved["slope"], silu_hbm=saved["silu"],
        middle_hbm=saved["middle"],
    )
    bottom = backward(1, tables | routing | dict(small_before=saved["small"]), weights | operands, nb)
    return final(tables, saved, saved, bottom, weights, mesh_sizes)


def solution(mesh):
    sizes = (mesh.shape["blk"], mesh.shape["dp"])
    return jax.shard_map(
        functools.partial(local, mesh_sizes=sizes),
        mesh=mesh,
        in_specs=(
            P("dp", "blk", None),
            P("dp", "blk"),
            P("dp", "blk"),
            P(),
            P(),
            P(),
            P(),
            P(),
            P(),
            P(),
            P(),
            P(),
            P(),
            P("dp", "blk", None),
        ),
        out_specs=(
            P("dp", "blk", None),
            P("dp", "blk", None),
            P("blk"),
            P("blk"),
            P("blk", None),
            P("blk", None),
            P("blk", None),
            P("blk", None),
            P("blk", None),
            P("blk", None),
            P("blk", None),
            P("blk", None),
        ),
        check_vma=False,
    )
```

```python
import functools
import itertools
import math
import types

import jax
import jax.numpy as jnp
from jax import lax
from jax.experimental import pallas as pl
from jax.experimental.pallas import tpu as pltpu
from jax.sharding import PartitionSpec as P

QUERY_HEADS = 15
KEY_VALUE_HEADS = 5
HEAD_DIMENSION = 64
RECUR = 2
HEAD_SHARE = QUERY_HEADS // KEY_VALUE_HEADS
KEYS_WIDTH = KEY_VALUE_HEADS * HEAD_DIMENSION
PAIR = 2 * HEAD_DIMENSION
UNIT_COLUMNS = 256
SPAN = 2
VMEM_LIMIT = 63 * 1024 * 1024

epsilon = 1e-05
masked_score = -1e30
low = jnp.bfloat16


def frequencies(head_size):
    return jnp.exp(
        jnp.arange(head_size // 2, dtype=jnp.float32) * (-2.0 * math.log(10000.0) / head_size)
    )


def rms_scale(values):
    return lax.rsqrt(jnp.mean(values * values, axis=-1, keepdims=True) + epsilon)


def norm_gradient(grad_norm, values, gain):
    scale = rms_scale(values)
    weighted = grad_norm * gain
    grad_values = scale * weighted - values * (scale * scale * scale) * jnp.mean(
        weighted * values, axis=-1, keepdims=True
    )
    return grad_values, jnp.sum(grad_norm * values * scale, axis=0, keepdims=True)


def dot_last(left, right):
    return lax.dot_general(left, right, (((1,), (1,)), ((), ())), preferred_element_type=jnp.float32)


def plain_dot(left, right):
    return jnp.dot(left, right, preferred_element_type=jnp.float32)


def bits_of(number, count):
    return tuple((number >> (count - 1 - at)) & 1 for at in range(count))


def bit_of(position, bit):
    return lax.rem(position // (1 << bit), 2)


def block_bits(block, m):
    return tuple(bit_of(block, bit) for bit in range(m - 1, -1, -1))


def flipped(position, bit):
    return position + (1 << bit) * (1 - 2 * bit_of(position, bit))


def remote(source, target, sems, at, device):
    return pltpu.make_async_remote_copy(
        src_ref=source,
        dst_ref=target,
        send_sem=sems[0].at[at],
        recv_sem=sems[1].at[at],
        device_id=device,
        device_id_type=pl.DeviceIdType.MESH,
    )


def greet(partners):
    barrier = pltpu.get_barrier_semaphore()
    for partner in partners:
        pl.semaphore_signal(barrier, inc=1, device_id=partner, device_id_type=pl.DeviceIdType.MESH)
    pl.semaphore_wait(barrier, len(partners))


def turn_heads(turned, cosine, sine, heads):
    split = turned.reshape(heads, 2, HEAD_DIMENSION // 2, turned.shape[1])
    first, second = split[:, 0], split[:, 1]
    both = jnp.stack([first * cosine - second * sine, second * cosine + first * sine], axis=1)
    return both.reshape(turned.shape)


def turn_back(turned, cosine, sine, heads):
    return turn_heads(turned, cosine, -sine, heads)


def head_rows(group, member):
    head = group * HEAD_SHARE + member
    return pl.ds(pl.multiple_of(head * HEAD_DIMENSION, HEAD_DIMENSION), HEAD_DIMENSION)


def as_column(row):
    wide = jnp.broadcast_to(row.astype(jnp.float32), (8, row.shape[1]))
    return wide.T[:, 0:1]


def key_steps(blk, span):
    return blk // (1 << span) + 1


def fill_bias(bias, metas, query_segments, level, blk, m, piece, span):
    many = 1 << span
    key_at = lax.broadcasted_iota(jnp.int32, (many * piece, piece), 0)
    query_at = lax.broadcasted_iota(jnp.int32, (many * piece, piece), 1)

    @pl.loop(0, key_steps(blk, span))
    def _(step):
        rows = metas[block_bits(step, m - span)].reshape(many, 8, piece)
        columns = jnp.concatenate([rows[block].T for block in range(many)], axis=0)
        live = jnp.where(columns[:, 1:2] > level, columns[:, 0:1], -1.0)
        shift = (blk - many * step) * piece
        allowed = (live == query_segments) & (key_at <= query_at + shift) | (key_at == query_at + shift)
        masked = jnp.where(allowed, 0.0, masked_score).astype(bias.dtype)
        bias[pl.ds(many * step, many)] = masked.reshape(many, piece, piece)


def step_bias(bias, step, piece, span):
    many = 1 << span
    here = bias[pl.ds(many * step, many)].reshape(many * piece, piece).astype(jnp.float32)
    return jnp.concatenate([here] * HEAD_SHARE, axis=1)


def kv_weight_loads(key_hbm, value_hbm, target, sems):
    copies = []
    for group in range(KEY_VALUE_HEADS):
        for side, source in enumerate((key_hbm, value_hbm)):
            rows = pl.ds(group * HEAD_DIMENSION, HEAD_DIMENSION)
            place = pl.ds(group * PAIR + side * HEAD_DIMENSION, HEAD_DIMENSION)
            copies.append(pltpu.make_async_copy(source.at[rows], target.at[place], sems.at[2 * group + side]))
    return copies


def turn_keys(both, cosine, sine):
    half = HEAD_DIMENSION // 2
    split = both.reshape(KEY_VALUE_HEADS, 4, half, both.shape[1])
    first, second = split[:, 0], split[:, 1]
    turned = [first * cosine - second * sine, second * cosine + first * sine, split[:, 2], split[:, 3]]
    return jnp.stack(turned, axis=1).reshape(both.shape)


def spec(memory):
    return pl.BlockSpec(memory_space=memory)


def shaped(entry):
    return jax.ShapeDtypeStruct(*entry)


def spaces(entries):
    return [pltpu.VMEM(*entry) for entry in entries]


def dma_semaphores(*shapes):
    return [pltpu.SemaphoreType.DMA(shape) for shape in shapes]


class Piece:
    def __init__(self, at, kept_at, slot, flavour, family, sems, bits, middle=False):
        self.at, self.kept_at, self.slot, self.family, self.sems = at, kept_at, slot, family, sems
        self.m, self.n = bits
        left = list(range(self.m - 1, -1, -1))
        self.order = []
        for stage in range(self.m):
            place = len(left) - 1 if stage == 0 or flavour == 0 else 0
            self.order.append((left.pop(place), place, len(left)))
        self.last = self.m + self.n
        self.blk = lax.axis_index("blk")
        self.dp = lax.axis_index("dp") if self.n else None
        self.middle = middle
        if middle:
            inner = bit_of(self.dp, 0) != bit_of(self.dp, 1)
            outer = jnp.logical_not(inner)
            self.sends, self.receives = (outer, inner, inner), (inner, inner, outer)

    def half(self, ref, side):
        size = self.family.shape[self.family.split] // 2
        here = pl.ds(0 if isinstance(side, int) else pl.multiple_of(side * size, size), size)
        return ref.at[here, :] if self.family.split == 0 else ref.at[:, here]

    def held(self, stage):
        if stage == 0:
            return self.family.part, self.slot
        return self.family.blk[stage - 1], self.kept_at

    def copy(self, stage):
        m, family = self.m, self.family
        if stage < m:
            bit, place, others = self.order[stage]
            ref, index = self.held(stage)
            chosen = [slice(None)] * (others + 1)
            chosen[place] = 1 - bit_of(self.blk, bit)
            source = ref.at[(index, *chosen)]
            target = family.blk[stage].at[self.kept_at]
            device = {"blk": flipped(self.blk, bit)}
        elif self.middle:
            source, target, device = (
                (family.blk[m - 1], family.dp[0], {"dp": flipped(self.dp, 0)}),
                (family.dp[0], family.dp[1], {"dp": 3 - self.dp}),
                (family.out, family.out, {"dp": flipped(self.dp, 0)}),
            )[stage - m]
            source, target = source.at[self.kept_at], target.at[self.kept_at]
        elif stage < self.last:
            bit = stage - m
            if bit == 0:
                source = self.half(family.blk[m - 1].at[self.kept_at], 1 - bit_of(self.dp, 0))
            else:
                source = self.half(family.dp[bit - 1].at[self.kept_at], 0)
            target = self.half(family.dp[bit].at[self.kept_at], 0)
            device = {"dp": flipped(self.dp, bit)}
        else:
            source = self.half(family.out.at[self.kept_at], bit_of(self.dp, 0))
            target = source
            device = {"dp": flipped(self.dp, 0)}
        return remote(source, target, self.sems, (self.at, stage), device)

    def where(self, roles, stage, body):
        if self.middle and stage >= self.m:
            pl.when(roles[stage - self.m])(body)
        else:
            body()

    def start(self, stage):
        self.where(self.sends if self.middle else None, stage, lambda: self.copy(stage).start())

    def finish(self, stage):
        self.where(self.receives if self.middle else None, stage, lambda: self.receive(stage))

    def receive(self, stage):
        m, family = self.m, self.family
        self.copy(stage).wait_recv()
        if stage < m:
            bit, place, others = self.order[stage]
            ref, index = self.held(stage)
            for combo in itertools.product(range(2), repeat=others):
                chosen = list(combo)
                chosen.insert(place, bit_of(self.blk, bit))
                into = family.blk[stage].at[(self.kept_at, *combo)]
                self.add(into, into, ref.at[(index, *chosen)])
            if stage == 0:
                self.copy(0).wait_send()
        elif stage < self.last and self.middle:
            kept, sums = self.kept_at, family.dp
            if stage == m:
                self.add(sums[0].at[kept], sums[0].at[kept], family.blk[m - 1].at[kept])
            else:
                self.add(family.out.at[kept], sums[0].at[kept], sums[1].at[kept])
        elif stage < self.last:
            bit = stage - m
            got = self.half(family.dp[bit].at[self.kept_at], 0)
            if bit == 0:
                own = self.half(family.blk[m - 1].at[self.kept_at], bit_of(self.dp, 0))
            else:
                own = self.half(family.dp[bit - 1].at[self.kept_at], 0)
            into = got
            if stage == self.last - 1:
                into = self.half(family.out.at[self.kept_at], bit_of(self.dp, 0))
            self.add(into, got, own)

    def add(self, into, left, right):
        into[...] = left[...] + right[...]

    def drained(self, stages):
        for stage in stages:
            self.where(self.sends if self.middle else None, stage, lambda: self.copy(stage).wait_send())


def feed_forward_backward(at, level, gradient, ready, done):
    column = at.router[level:level + 1, :].astype(jnp.float32)
    active = as_column(at.depths[...]) > float(level)
    hidden = at.hid_level[...]
    chosen = jax.nn.sigmoid(jnp.sum(hidden * column, axis=1, keepdims=True))
    at.dbranch[...] = jnp.where(active, chosen, 0.0) * gradient
    dchosen = jnp.where(active, jnp.sum(gradient * at.branch_level[...], axis=1, keepdims=True), 0.0)
    dlogit = dchosen * chosen * (1.0 - chosen)
    at.small[2 + level:3 + level, :] = jnp.sum(hidden * dlogit, axis=0, keepdims=True)
    at.grad_hidden[...] = gradient + dlogit * column
    at.dffn[...] = at.dbranch[...].astype(low)

    ready(0)
    dinner = plain_dot(at.dffn[...], at.w_down[...])
    at.dgate[...] = (dinner * at.slope_level[...].astype(jnp.float32)).astype(low)
    at.dup[...] = (dinner * at.silu_level[...].astype(jnp.float32)).astype(low)
    done()
    at.dnorm_turned[...] = plain_dot(at.w_gate[...], at.dgate[...].T) + plain_dot(at.w_up[...], at.dup[...].T)
    ready(1)
    dnorm = at.dnorm_turned[...].T
    dmiddle, gain_share = norm_gradient(dnorm, at.middle_level[...], at.norms[1:2, :].astype(jnp.float32))
    at.small[1:2, :] += gain_share
    at.grad_hidden[...] += dmiddle
    dattn = (at.dbranch[...] + dmiddle).astype(low)
    lead = at.far.shape[1] - dattn.shape[1]
    at.far[:, :lead] = jnp.zeros((dattn.shape[0], lead), low)
    at.far[:, lead:] = dattn
    at.dat[...] = plain_dot(at.w_out[...], dattn.T).astype(low)


def forward_kernel(sizes, names, *refs):
    m, piece = sizes
    at = types.SimpleNamespace(**dict(zip(names, refs)))
    blk = lax.axis_index("blk")
    mine = block_bits(blk, m)
    kv, metas = at.kv, at.metas
    weights = (
        (at.w_query_hbm, at.w_query), (at.w_out_hbm, at.w_out), (at.w_gate_hbm, at.w_gate), (at.w_up_hbm, at.w_up), (at.w_down_hbm, at.w_down),
    )
    loads = [pltpu.make_async_copy(*pair, at.load_sems.at[index]) for index, pair in enumerate(weights)]
    kv_loads = kv_weight_loads(at.key_weight_hbm, at.value_weight_hbm, at.kv_weight, at.weight_sems)
    for load in kv_loads + loads:
        load.start()
    saved = (
        (at.normed, at.normed_out), (at.turned, at.turned_out), (kv, at.kv_out), (at.lse, at.lse_out),
        (at.att, at.att_out), (at.nffn, at.nffn_out), (at.inner, at.inner_out),
    )

    def save(index, level):
        return pltpu.make_async_copy(
            saved[index][0].at[level] if index == 2 else saved[index][0], saved[index][1].at[level], at.save_sems.at[index, level]
        )

    first = (
        (at.hid.at[0], at.hid_out), (at.middle, at.middle_out), (at.silu, at.silu_out),
        (at.slope, at.slope_out), (at.branch, at.branch_out), (metas, at.metas_out),
        (at.far, at.far_out), (at.dat, at.dat_out), (at.dffn, at.dffn_out), (at.dgate, at.dgate_out), (at.dup, at.dup_out),
        (at.hid.at[1], at.hid_1_out),
    )
    late = [pltpu.make_async_copy(*pair, at.late_sems.at[index]) for index, pair in enumerate(first)]
    segment_row = at.segments[...].astype(jnp.float32)
    depth_column = as_column(at.depths[...])
    metas[mine] = jnp.concatenate(
        [segment_row, at.depths[...].astype(jnp.float32), jnp.zeros((6, piece), jnp.float32)], axis=0
    )
    greet([{"blk": flipped(blk, bit)} for bit in range(m)])

    def place(known):
        return tuple(slice(None) if bit in known else mine[m - 1 - bit] for bit in range(m - 1, -1, -1))

    orders = (list(range(1, m)), list(range(m - 1, 0, -1)))
    kv_sems = (at.kv_send, at.kv_recv)

    def kv_copies(level, group, stage):
        if stage == m - 1:
            ref = kv.at[(level, group, *place(range(1, m)))]
            return [remote(ref, ref, kv_sems, (level, group, 2 * stage), {"blk": flipped(blk, 0)})]
        copies = []
        for side, order in enumerate(orders):
            rows = pl.ds(side * (piece // 2), piece // 2)
            ref = kv.at[(level, group, *place(order[:stage]), rows)]
            copies.append(remote(ref, ref, kv_sems, (level, group, 2 * stage + side), {"blk": flipped(blk, order[stage])}))
        return copies

    def kv_advance(level, group, stage):
        if stage > 0:
            for copy in kv_copies(level, group, stage - 1):
                copy.wait_recv()
        if stage < m:
            for copy in kv_copies(level, group, stage):
                copy.start()

    def meta_copy(stage):
        bits = list(range(1, m)) + [0]
        ref = metas.at[place(bits[:stage])]
        return remote(ref, ref, (at.meta_send, at.meta_recv), stage, {"blk": flipped(blk, bits[stage])})

    meta_copy(0).start()
    cosine, sine = at.cosines[...], at.sines[...]
    gain_attn, gain_ffn = at.norms[0:1, :].astype(jnp.float32), at.norms[1:2, :].astype(jnp.float32)
    routers = at.router[...].astype(jnp.float32)
    at.hid[0] = at.tokens[...].T.astype(jnp.float32)
    late[0].start()
    at.query_pad[HEAD_DIMENSION:, :] = jnp.zeros_like(at.query_pad[HEAD_DIMENSION:, :])

    @pl.loop(0, RECUR)
    def _(level):
        @pl.when(level > 0)
        def _():
            for index in range(5):
                save(index, 0).wait()

        hidden = at.hid[level]
        at.flat[...] = (hidden * rms_scale(hidden) * gain_attn).astype(low)
        at.normed[...] = at.flat[...].T

        @pl.when(level == 0)
        def _():
            for load in kv_loads:
                load.wait()

        both = turn_keys(plain_dot(at.kv_weight[...], at.normed[...]), cosine, sine).T.astype(low)
        for group in range(KEY_VALUE_HEADS):
            kv[(level, group, *mine)] = both[:, group * PAIR:(group + 1) * PAIR]
            kv_advance(level, group, 0)

        @pl.when(level == 0)
        def _():
            loads[0].wait()
            for stage in range(1, m - 1):
                meta_copy(stage - 1).wait_recv()
                meta_copy(stage).start()

        queries = turn_heads(plain_dot(at.flat[...], at.w_query[...]).T, cosine, sine, QUERY_HEADS)
        at.turned[...] = (queries * HEAD_DIMENSION ** (-0.5)).astype(low)

        @pl.when(level == 0)
        def _():
            for stage in range(max(1, m - 1), m):
                meta_copy(stage - 1).wait_recv()
                meta_copy(stage).start()

        for stage in range(1, m - 1):
            for upper in range(2):
                @pl.when(bit_of(blk, 1) == upper)
                def _():
                    for side in (0, 1) if upper else (1, 0):
                        for group in range(KEY_VALUE_HEADS):
                            kv_copies(level, group, stage - 1)[side].wait_recv()
                            kv_copies(level, group, stage)[side].start()

        kv_advance(level, 0, m - 1)

        @pl.when(level == 0)
        def _():
            meta_copy(m - 1).wait_recv()
            late[5].start()

        fill_bias(at.bias, metas, segment_row, level.astype(jnp.float32), blk, m, piece, SPAN)

        @pl.loop(0, KEY_VALUE_HEADS)
        def _(group):
            @pl.when(group + 1 < KEY_VALUE_HEADS)
            def _():
                kv_advance(level, group + 1, m - 1)

            kv_advance(level, group, m)
            for member in range(HEAD_SHARE):
                at.query_pad[:HEAD_DIMENSION, member * piece:(member + 1) * piece] = at.turned[head_rows(group, member), :]
            at.top[...] = jnp.full_like(at.top, masked_score)
            at.total[...] = jnp.zeros_like(at.total)

            @pl.loop(0, key_steps(blk, SPAN))
            def _(index):
                step = key_steps(blk, SPAN) - 1 - index
                rows = kv[(level, group, *block_bits(step, m - SPAN))].reshape((1 << SPAN) * piece, PAIR)
                scores = plain_dot(rows, at.query_pad[...]) + step_bias(at.bias, step, piece, SPAN)
                before = at.top[0:1, :]
                after = jnp.maximum(before, jnp.max(scores, axis=0, keepdims=True))
                raised = jnp.exp(scores - after)
                shrink = jnp.exp(before - after)
                at.top[0:1, :] = after
                ones = jnp.ones((16, rows.shape[0]), low)
                left = jnp.concatenate([rows.T[HEAD_DIMENSION:], ones], axis=0)
                at.total[...] = at.total[...] * shrink + plain_dot(left, raised.astype(low))

            sums = at.total[HEAD_DIMENSION:HEAD_DIMENSION + 1, :]
            at.lse[pl.ds(group, 1), :] = at.top[0:1, :] + jnp.log(sums)
            out = at.total[:HEAD_DIMENSION, :] / sums
            for member in range(HEAD_SHARE):
                at.att[head_rows(group, member), :] = out[:, member * piece:(member + 1) * piece].astype(low)

        for index in range(5):
            save(index, level).start()

        @pl.when(level == 0)
        def _():
            loads[1].wait()

        @pl.when(level > 0)
        def _():
            save(5, 0).wait()
            save(6, 0).wait()
            for copy in late[1:5]:
                copy.wait()

        attn = plain_dot(at.att[...].T, at.w_out[...])
        mid = at.hid[level] + attn
        at.middle[...] = mid
        at.branch[...] = attn
        at.flat[...] = (mid * rms_scale(mid) * gain_ffn).astype(low)
        at.nffn[...] = at.flat[...].T
        save(5, level).start()

        @pl.when(level == 0)
        def _():
            loads[2].wait()
            loads[3].wait()

        gate_pre = plain_dot(at.flat[...], at.w_gate[...])
        up_pre = plain_dot(at.flat[...], at.w_up[...])
        opened = jax.nn.sigmoid(gate_pre)
        passed = gate_pre * opened
        at.silu[...] = passed.astype(low)
        at.slope[...] = (up_pre * (opened + passed - passed * opened)).astype(low)
        at.inner[...] = (passed * up_pre).astype(low).T
        save(6, level).start()

        @pl.when(level == 0)
        def _():
            loads[4].wait()

        at.branch[...] += plain_dot(at.w_down[...], at.inner[...]).T
        column = jnp.where(level == 0, routers[0:1, :], routers[1:2, :])
        logit = jnp.sum(at.hid[level] * column, axis=1, keepdims=True)
        weight = jnp.where(depth_column > level.astype(jnp.float32), jax.nn.sigmoid(logit), 0.0)
        at.hid[level + 1] = at.hid[level] + weight * at.branch[...]

        @pl.when(level == 0)
        def _():
            for copy in late[1:5]:
                copy.start()

    at.hidden_out[...] = at.hid[RECUR].T
    top = RECUR - 1
    at.hid_level, at.branch_level, at.middle_level = at.hid.at[top], at.branch, at.middle
    at.silu_level, at.slope_level = at.silu, at.slope
    at.small[...] = jnp.zeros_like(at.small)
    feed_forward_backward(at, top, at.cotangent[...].T.astype(jnp.float32), lambda part: None, lambda: None)
    for copy in late[6:]:
        copy.start()
    for stage in range(m):
        meta_copy(stage).wait_send()
    for level in range(RECUR):
        for group in range(KEY_VALUE_HEADS):
            for stage in range(m):
                for copy in kv_copies(level, group, stage):
                    copy.wait_send()
    for index in range(len(saved)):
        save(index, RECUR - 1).wait()
    for copy in late[:1] + late[5:]:
        copy.wait()


def far_width(width):
    return 2 * width + 2 * KEYS_WIDTH - 1536


def forward(small, weights, nb):
    m = nb.bit_length() - 1
    width, piece = small["tokens"].shape
    hidden_units = weights["w_gate_hbm"].shape[1]
    blocks, wide = (2,) * m, HEAD_SHARE * piece
    rows, turned = ((piece, width), jnp.float32), ((RECUR, width, piece), low)
    hidden = ((piece, hidden_units), low)
    saved = dict(
        normed=turned, turned=turned, kv=((RECUR, KEY_VALUE_HEADS, *blocks, piece, PAIR), low),
        lse=((RECUR, 8, wide), jnp.float32), att=turned, nffn=turned, inner=((RECUR, hidden_units, piece), low),
        metas=((*blocks, 8, piece), jnp.float32), far=((piece, far_width(width)), low), dat=((width, piece), low),
        dffn=((piece, width), low), dgate=hidden, dup=hidden,
    )
    first = dict(hid=rows, middle=rows, silu=hidden, slope=hidden, branch=rows)
    outs = dict(hidden_out=((width, piece), jnp.float32), grad_hidden=rows, small=((8, width), jnp.float32))
    anywhere = {name + "_out": entry for name, entry in (saved | first | dict(hid_1=rows)).items()}
    single = {name: (shape[1:], dtype) for name, (shape, dtype) in saved.items() if shape[0] == RECUR and name not in ("kv", "metas")}
    buffers = {name[:-4]: (array.shape, array.dtype) for name, array in weights.items()} | saved | single | first | dict(
        kv_weight=((2 * KEYS_WIDTH, width), low),
        hid=((RECUR + 1, piece, width), jnp.float32), flat=((piece, width), low),
        bias=((nb, piece, piece), jnp.float32), query_pad=((PAIR, wide), low), top=((8, wide), jnp.float32),
        total=((HEAD_DIMENSION + 16, wide), jnp.float32), dbranch=rows, dnorm_turned=((width, piece), jnp.float32),
    )
    semaphores = dict(
        load_sems=(5,), weight_sems=(2 * KEY_VALUE_HEADS,), save_sems=(7, RECUR), late_sems=(12,), kv_send=(RECUR, KEY_VALUE_HEADS, 2 * m),
        kv_recv=(RECUR, KEY_VALUE_HEADS, 2 * m), meta_send=(m,), meta_recv=(m,),
    )
    results = pl.pallas_call(
        functools.partial(forward_kernel, (m, piece), (*small, *weights, *outs, *anywhere, *buffers, *semaphores)),
        out_shape=[shaped(entry) for entry in (outs | anywhere).values()],
        in_specs=[spec(pltpu.VMEM)] * len(small) + [spec(pl.ANY)] * len(weights),
        out_specs=[spec(pltpu.VMEM)] * len(outs) + [spec(pl.ANY)] * len(anywhere),
        scratch_shapes=spaces(buffers.values()) + dma_semaphores(*semaphores.values()),
        compiler_params=pltpu.CompilerParams(
            collective_id=1, has_side_effects=True, vmem_limit_bytes=VMEM_LIMIT
        ),
        cost_estimate=pl.CostEstimate(
            flops=3 * RECUR * piece * width * 10240, bytes_accessed=48 * 1024 * 1024, transcendentals=0
        ),
        name="forward_levels",
    )(*small.values(), *weights.values())
    return dict(zip((*outs, *(name[:-4] for name in anywhere)), results))


class AttentionBackward:
    def __init__(self, at, m, piece, level, span):
        self.at, self.m, self.piece, self.level, self.span = at, m, piece, level, span
        self.blk = lax.axis_index("blk")
        self.family = types.SimpleNamespace(part=at.part, blk=at.halves, dp=(), out=None, shape=(piece // 2, PAIR), split=0)

    def pieces(self, group):
        sems = (self.at.kv_send, self.at.kv_recv)
        return [
            Piece(2 * group + side, 2 * group + side, 2 * group + side, side, self.family, sems, (self.m, 0))
            for side in range(2)
        ]

    def move(self, group, stage):
        for piece_of in self.pieces(group):
            piece_of.finish(stage)
            if stage + 1 < self.m:
                piece_of.start(stage + 1)

    def begin(self):
        at = self.at
        query_segments = at.metas[block_bits(self.blk, self.m)][0:1, :]
        fill_bias(at.bias, at.metas, query_segments, float(self.level), self.blk, self.m, self.piece, self.span)
        at.query_pad[HEAD_DIMENSION:, :] = jnp.zeros_like(at.query_pad[HEAD_DIMENSION:, :])
        at.dat_pad[:HEAD_DIMENSION, :] = jnp.zeros_like(at.dat_pad[:HEAD_DIMENSION, :])

    def group(self, group):
        at, m, piece, blk = self.at, self.m, self.piece, self.blk
        half = piece // 2
        carried = []
        for member in range(HEAD_SHARE):
            rows, lanes = head_rows(group, member), slice(member * piece, (member + 1) * piece)
            at.query_pad[:HEAD_DIMENSION, lanes] = at.turned[rows, :]
            at.dat_pad[HEAD_DIMENSION:, lanes] = at.dat_turned[rows, :]
            product = at.dat_turned[rows, :].astype(jnp.float32) * at.att_turned[rows, :].astype(jnp.float32)
            carried.append(jnp.sum(product, axis=0, keepdims=True))
        carried = jnp.concatenate(carried, axis=1)
        at.query_rows[...] = at.query_pad[...].T
        at.dat_rows[...] = at.dat_pad[...].T
        log_total = at.lse[pl.ds(group, 1), :]
        at.dq_sum[...] = jnp.zeros_like(at.dq_sum)

        span, lead = self.span, m - self.span

        @pl.loop(0, key_steps(blk, span))
        def _(step):
            rows = at.kv[(group, *block_bits(step, lead))].reshape((1 << span) * piece, PAIR)
            probability = jnp.exp(plain_dot(rows, at.query_pad[...]) + step_bias(at.bias, step, piece, span) - log_total)
            dprob = plain_dot(rows, at.dat_pad[...])
            dscores = (probability * (dprob - carried)).astype(low)
            share = plain_dot(dscores, at.query_rows[...]) + plain_dot(probability.astype(low), at.dat_rows[...])
            share = share.astype(low)
            for block in range(1 << span):
                for side in range(2):
                    first = block * piece + side * half
                    place = (2 * group + side, *block_bits(step, lead), *bits_of(block, span))
                    at.part[place] = share[first:first + half]
            at.dq_sum[...] += plain_dot(rows.T[:HEAD_DIMENSION], dscores)

        @pl.loop(key_steps(blk, span), 1 << lead)
        def _(step):
            for block in range(1 << span):
                for side in range(2):
                    place = (2 * group + side, *block_bits(step, lead), *bits_of(block, span))
                    at.part[place] = jnp.zeros((half, PAIR), low)

        for piece_of in self.pieces(group):
            piece_of.start(0)
        for member in range(HEAD_SHARE):
            at.dq_turned[head_rows(group, member), :] = at.dq_sum[:, member * piece:(member + 1) * piece]

    def follow(self, group):
        for stage in range(self.m - 1):
            earlier = group - 1 - stage
            if isinstance(group, int):
                if 0 <= earlier < KEY_VALUE_HEADS:
                    self.move(earlier, stage)
            else:
                @pl.when(earlier >= 0)
                def _():
                    self.move(earlier, stage)

    def queries(self, cosine, sine):
        at = self.at
        dqueries = turn_back(at.dq_turned[...] * HEAD_DIMENSION ** (-0.5), cosine, sine, QUERY_HEADS).astype(low)
        self.put(2 * KEYS_WIDTH, dqueries.T)
        at.dnorm[...] = plain_dot(at.w_query[...], dqueries).T

    def put(self, column, values):
        self.at.near[:, column:column + values.shape[1]] = values

    def keys(self, cosine, sine):
        at, m = self.at, self.m
        filled = 2 * KEYS_WIDTH + QUERY_HEADS * HEAD_DIMENSION
        self.put(filled, jnp.zeros((self.piece, at.near.shape[1] - filled), low))
        sums = []
        for group in range(KEY_VALUE_HEADS):
            self.move(group, m - 1)
            sums.append(jnp.concatenate([at.halves[m - 1][2 * group], at.halves[m - 1][2 * group + 1]], axis=0))
        both = jnp.concatenate(sums, axis=1).astype(jnp.float32).T
        both = turn_keys(both, cosine, -sine).astype(low).T
        self.put(0, both)
        at.dnorm[...] += plain_dot(both, at.kv_weight[...])

    def drained(self):
        for group in range(KEY_VALUE_HEADS):
            for piece_of in self.pieces(group):
                piece_of.drained(range(1, self.m))


def attention_buffers(nb, piece, width, bias_type):
    m, wide, heads = nb.bit_length() - 1, HEAD_SHARE * piece, 2 * KEY_VALUE_HEADS
    turned = ((width, piece), low)
    pad, pad_rows = ((PAIR, wide), low), ((wide, PAIR), low)
    buffers = dict(
        turned=turned, dat_turned=turned, att_turned=turned, kv=((KEY_VALUE_HEADS, *(2,) * m, piece, PAIR), low),
        lse=((8, wide), jnp.float32), metas=((*(2,) * m, 8, piece), jnp.float32), w_query=((width, width), low),
        kv_weight=((2 * KEYS_WIDTH, width), low), dq_turned=((width, piece), jnp.float32),
        bias=((nb, piece, piece), bias_type), query_pad=pad, dat_pad=pad, query_rows=pad_rows, dat_rows=pad_rows,
        dq_sum=((HEAD_DIMENSION, wide), jnp.float32), part=((heads, *(2,) * m, piece // 2, PAIR), low),
        dnorm=((piece, width), jnp.float32), hid=((piece, width), jnp.float32),
    )
    for stage in range(m):
        buffers["half_%d" % stage] = ((heads, *(2,) * (m - 1 - stage), piece // 2, PAIR), low)
    return buffers


def backward_kernel(sizes, names, *refs):
    m, piece, level = sizes
    at = types.SimpleNamespace(**dict(zip(names, refs)))
    at.halves = [getattr(at, "half_%d" % stage) for stage in range(m)]
    at.near = at.near_out
    blk = lax.axis_index("blk")
    pairs = (
        (at.metas_hbm, at.metas), (at.turned_hbm.at[level], at.turned), (at.dat_hbm, at.dat_turned),
        (at.att_hbm.at[level], at.att_turned), (at.lse_hbm.at[level], at.lse), (at.kv_hbm.at[level], at.kv),
        (at.w_query_hbm, at.w_query),
        (at.grad_hbm, at.grad_hidden), (at.hid_1_hbm, at.hid),
        (at.hid_0_hbm, at.hid_level), (at.branch_hbm, at.branch_level), (at.w_down_hbm, at.w_down),
        (at.slope_hbm, at.slope_level), (at.silu_hbm, at.silu_level), (at.w_gate_hbm, at.w_gate), (at.w_up_hbm, at.w_up),
        (at.middle_hbm, at.middle_level), (at.w_out_hbm, at.w_out),
    )
    loads = [pltpu.make_async_copy(*pair, at.load_sems.at[index]) for index, pair in enumerate(pairs)]
    loads += kv_weight_loads(at.key_weight_hbm, at.value_weight_hbm, at.kv_weight, at.weight_sems)
    for load in loads:
        load.start()
    saves = [
        pltpu.make_async_copy(*pair, at.save_sems.at[index])
        for index, pair in enumerate(((at.dgate, at.dgate_out), (at.dup, at.dup_out)))
    ]
    greet([{"blk": flipped(blk, bit)} for bit in range(m)])
    work = AttentionBackward(at, m, piece, level, SPAN)
    loads[0].wait()
    work.begin()
    for load in loads[1:6]:
        load.wait()

    @pl.loop(0, KEY_VALUE_HEADS)
    def _(group):
        work.group(group)
        work.follow(group)

    cosine, sine = at.cosines[...], at.sines[...]
    for virtual in range(KEY_VALUE_HEADS, KEY_VALUE_HEADS + m - 1):
        work.follow(virtual)
        if virtual == KEY_VALUE_HEADS:
            loads[6].wait()
            work.queries(cosine, sine)
    for load in loads[7:]:
        load.wait()
    work.keys(cosine, sine)
    dhidden, gain_share = norm_gradient(at.dnorm[...], at.hid[...], at.norms[0:1, :].astype(jnp.float32))
    at.small[...] = at.small_before[...]
    at.small[0:1, :] = gain_share
    gradient = at.grad_hidden[...] + dhidden
    at.dnorm[...] = gradient
    feed_forward_backward(at, level - 1, at.dnorm[...], lambda part: None, lambda: [save.start() for save in saves])
    work.drained()
    for save in saves:
        save.wait()


def backward(level, small, operands, nb):
    m = nb.bit_length() - 1
    piece, width = operands["grad_hbm"].shape
    hidden_units = operands["w_gate_hbm"].shape[1]
    rows, flat, hidden = ((piece, width), jnp.float32), ((piece, width), low), ((piece, hidden_units), low)
    outs = dict(
        grad_hidden=rows, small=((8, width), jnp.float32), near_out=((piece, 1792), low), dffn=flat,
        dat=((width, piece), low), far=((piece, far_width(width)), low),
    )
    anywhere = dict(dgate_out=hidden, dup_out=hidden)
    buffers = attention_buffers(nb, piece, width, jnp.float32) | dict(
        hid_level=rows, branch_level=rows, middle_level=rows, w_down=((width, hidden_units), low), slope_level=hidden,
        silu_level=hidden, w_gate=((width, hidden_units), low), w_up=((width, hidden_units), low),
        w_out=((width, width), low), dbranch=rows, dnorm_turned=((width, piece), jnp.float32), dgate=hidden, dup=hidden,
    )
    sums = (2 * KEY_VALUE_HEADS, m)
    semaphores = dict(load_sems=(18,), weight_sems=(2 * KEY_VALUE_HEADS,), save_sems=(2,), kv_send=sums, kv_recv=sums)
    results = pl.pallas_call(
        functools.partial(
            backward_kernel, (m, piece, level), (*small, *operands, *outs, *anywhere, *buffers, *semaphores)
        ),
        out_shape=[shaped(entry) for entry in (outs | anywhere).values()],
        in_specs=[spec(pltpu.VMEM)] * len(small) + [spec(pl.ANY)] * len(operands),
        out_specs=[spec(pltpu.VMEM)] * len(outs) + [spec(pl.ANY)] * len(anywhere),
        scratch_shapes=spaces(buffers.values()) + dma_semaphores(*semaphores.values()),
        compiler_params=pltpu.CompilerParams(
            collective_id=2, has_side_effects=True, vmem_limit_bytes=VMEM_LIMIT
        ),
        cost_estimate=pl.CostEstimate(
            flops=2 * piece * width * 20000, bytes_accessed=32 * 1024 * 1024, transcendentals=0
        ),
        name="backward_level",
    )(*small.values(), *operands.values())
    return dict(zip((*outs, *anywhere), results))


WIDE_SLOTS, DOWN_SLOTS = 4, 2


def final_kernel(sizes, names, *refs):
    nb, m, n, piece, rows, padded, near_width = sizes
    at = types.SimpleNamespace(**dict(zip(names, refs)))
    at.halves = [getattr(at, "half_%d" % stage) for stage in range(m)]
    blk, dp = lax.axis_index("blk"), lax.axis_index("dp")
    at.near = at.gate_side.at[pl.ds(0, piece), pl.ds(0, near_width)]
    counter = itertools.count()

    def load(source, target):
        return pltpu.make_async_copy(source, target, at.load_sems.at[next(counter)])

    def both_lanes(ref, target):
        return [load(ref.at[level], target.at[:, pl.ds(level * piece, piece)]) for level in range(RECUR)]

    def both_rows(low_ref, deep_ref, target, width):
        pairs = ((low_ref, 0), (deep_ref, piece))
        return [load(ref, target.at[pl.ds(first, piece), pl.ds(0, width)]) for ref, first in pairs]

    hidden_units, width = at.gate_side.shape[1], at.dffn.shape[1]
    far_lanes = at.far_0_hbm.shape[1]
    loads = types.SimpleNamespace(
        nffn=both_lanes(at.nffn_hbm, at.left),
        dgate=both_rows(at.dgate_0_hbm, at.dgate_1_hbm, at.gate_side, hidden_units),
        inner=both_lanes(at.inner_hbm, at.inner),
        dffn=both_rows(at.dffn_0_hbm, at.dffn_1_hbm, at.dffn, width),
        metas=[load(at.metas_hbm, at.metas)],
        heads=[
            load(at.turned_hbm.at[0], at.turned), load(at.dat_hbm, at.dat_turned), load(at.att_hbm.at[0], at.att_turned),
            load(at.lse_hbm.at[0], at.lse), load(at.kv_hbm.at[0], at.kv),
        ],
        dup=both_rows(at.dup_0_hbm, at.dup_1_hbm, at.up_side, hidden_units),
        w_query=[load(at.w_query_hbm, at.w_query)],
        rest=[
            load(at.hid_hbm, at.hid), load(at.grad_hbm, at.grad),
        ],
        attended=both_lanes(at.attended_hbm, at.left_attended),
        kv_weight=kv_weight_loads(at.key_weight_hbm, at.value_weight_hbm, at.kv_weight, at.weight_sems),
    )
    late = types.SimpleNamespace(
        near=[load(at.near_1_hbm, at.gate_side.at[pl.ds(piece, piece), pl.ds(0, near_width)])],
        far=both_rows(at.far_0_hbm, at.far_1_hbm, at.up_side, far_lanes),
        normed=both_lanes(at.normed_hbm, at.left),
    )

    def begin(copies):
        for copy in copies:
            copy.start()

    def ready(copies):
        for copy in copies:
            copy.wait()

    for copies in vars(loads).values():
        begin(copies)
    greet([{"blk": flipped(blk, bit)} for bit in range(m)] + [{"dp": flipped(dp, bit)} for bit in range(n)])

    down_rows = at.part_down.shape[-2]

    def family(name, shape, split):
        return types.SimpleNamespace(
            part=getattr(at, "part_" + name), out=getattr(at, "out_" + name), shape=shape, split=split,
            blk=[getattr(at, "blk_%s_%d" % (name, stage)) for stage in range(m)],
            dp=[getattr(at, "dp_%s_%d" % (name, stage)) for stage in range(n)],
        )

    wide = family("wide", (2 * padded, UNIT_COLUMNS), 1)
    down = family("down", (down_rows, width), 0)
    little = family("small", (16, 128), 0)
    sems = (at.send_sems, at.recv_sems)
    units = itertools.count()

    def unit(holder, index, flavour, halves=n != 2):
        return Piece(next(units), index, index % holder.part.shape[0], flavour, holder, sems, (m, n), not halves)

    pairs = [[unit(wide, index, 0), unit(down, index, 1)] for index in range(5)]
    pairs += [[unit(wide, index, 0), unit(wide, index + 1, 1)] for index in (5, 7, 9)]
    pairs += [[unit(wide, 11, 0, True), unit(wide, 12, 1, True)]]
    pairs += [[unit(wide, 13, 0, True), unit(wide, 14, 1, True), unit(little, 0, 0, True)]]

    def compute_wide(index, slot):
        if index == 0:
            ready(loads.nffn)
            ready(loads.dgate)
        if index == 5:
            begin(late.near)
            ready(loads.dup)
        if index == 10:
            begin(late.far)
            begin(late.normed)
            ready(late.near)
            ready(late.normed)
            ready(loads.attended)
            ready(late.far)
        block, column = index // 5, (index % 5) * UNIT_COLUMNS
        second = 1280 + column
        upper_columns, lower_columns = slice(column, column + UNIT_COLUMNS), slice(second, second + UNIT_COLUMNS)
        if block < 2:
            right = at.gate_side if block == 0 else at.up_side
            upper = plain_dot(at.left[...], right[:, upper_columns])
            lower = plain_dot(at.left[...], right[:, lower_columns])
        else:
            upper = plain_dot(at.left[...], at.gate_side[:, upper_columns])
            lower = None
            if second < 1600:
                lower = plain_dot(at.left[...], at.gate_side[:, lower_columns])
            if second >= 1536:
                more = plain_dot(at.left_attended[...], at.up_side[:, second - 1536:second - 1536 + UNIT_COLUMNS])
                lower = more if lower is None else lower + more
        for target in range(nb):
            here = slice(target * padded, (target + 1) * padded)
            both = jnp.concatenate([upper[here], lower[here]], axis=0)
            at.part_wide[(slot, *bits_of(target, m))] = both.astype(low)

    def compute_down(index, slot):
        if index == 0:
            ready(loads.inner)
            ready(loads.dffn)
        firsts = [(target * 5 + index) * down_rows for target in range(nb)]
        left = jnp.concatenate([at.inner[first:first + down_rows, :] for first in firsts], axis=0)
        result = plain_dot(left, at.dffn[...])
        for target in range(nb):
            at.part_down[(slot, *bits_of(target, m))] = result[target * down_rows:(target + 1) * down_rows].astype(low)

    def compute_small():
        total = at.small_before[...]
        total = total + jnp.concatenate([at.gain_row[...], jnp.zeros((7, width), jnp.float32)], axis=0)
        at.part_small[...] = jnp.zeros_like(at.part_small)
        for target in range(nb):
            at.part_small[(0, *bits_of(target, m), slice(0, 8), slice(0, rows))] = total[:, target * rows:(target + 1) * rows]

    def compute(piece_of):
        if piece_of.family is wide:
            compute_wide(piece_of.kept_at, piece_of.slot)
        elif piece_of.family is down:
            compute_down(piece_of.kept_at, piece_of.slot)
        else:
            compute_small()
        piece_of.start(0)

    def moves(tick):
        for stage in range(m + n - 1, -1, -1):
            if 0 <= tick - stage < len(pairs):
                for piece_of in pairs[tick - stage]:
                    piece_of.finish(stage)
                    piece_of.start(stage + 1)

    work = AttentionBackward(at, m, piece, 0, 1)
    for pair in pairs[:2]:
        for piece_of in pair:
            compute(piece_of)
    ready(loads.metas)
    work.begin()
    ready(loads.heads)
    for group in range(KEY_VALUE_HEADS):
        moves(group)
        for piece_of in pairs[group + 2]:
            compute(piece_of)
        work.group(group)
        work.follow(group)
    cosine, sine = at.cosines[...], at.sines[...]
    moves(5)
    compute(pairs[7][0])
    ready(loads.w_query)
    for virtual in range(KEY_VALUE_HEADS, KEY_VALUE_HEADS + m - 1):
        work.follow(virtual)
        if virtual == KEY_VALUE_HEADS:
            work.queries(cosine, sine)
    moves(6)
    ready(loads.rest)
    ready(loads.kv_weight)
    work.keys(cosine, sine)
    compute(pairs[7][1])
    moves(7)
    for piece_of in pairs[8] + pairs[9][:2]:
        compute(piece_of)
    dhidden, gain_share = norm_gradient(at.dnorm[...], at.hid[...], at.norms[0:1, :].astype(jnp.float32))
    at.gain_row[...] = gain_share
    at.grad_out[...] = (at.grad[...] + dhidden).T
    compute(pairs[9][2])
    for tick in range(8, len(pairs) + m + n - 1):
        moves(tick)
    for pair in pairs:
        for piece_of in pair:
            piece_of.finish(m + n)
    for pair in pairs:
        for piece_of in pair:
            piece_of.drained(range(1, m + n + 1))
    work.drained()


def unpack_kernel(sizes, names, *refs):
    rows, padded = sizes
    at = types.SimpleNamespace(**dict(zip(names, refs)))
    counter = itertools.count()

    def moved(source, target):
        return pltpu.make_async_copy(source, target, at.sems.at[next(counter)])

    loads = [moved(at.wide_in.at[pl.ds(first, 5)], at.wide.at[pl.ds(first, 5)]) for first in (10, 0, 5)]
    loads += [moved(at.down_in, at.down), moved(at.little_in, at.little)]
    loads += [moved(at.hidden_in, at.hidden), moved(at.gradient_in, at.gradient)]
    for load in loads:
        load.start()
    stores = []

    def send(source, target):
        stores.append(moved(source, target))
        stores[-1].start()

    def columns(first, target):
        for unit in range(5):
            tile = at.wide[first + unit].astype(jnp.float32)
            for side in range(2):
                column = side * 1280 + unit * UNIT_COLUMNS
                target[:, column:column + UNIT_COLUMNS] = tile[side * padded:side * padded + rows]

    loads[0].wait()
    columns(10, at.rest)
    width = at.query.shape[1]
    both = at.rest[:, :2 * KEYS_WIDTH].T
    for group in range(KEY_VALUE_HEADS):
        here, first = slice(group * HEAD_DIMENSION, (group + 1) * HEAD_DIMENSION), group * PAIR
        at.key[here, :] = both[first:first + HEAD_DIMENSION]
        at.value[here, :] = both[first + HEAD_DIMENSION:first + PAIR]
    at.query[...] = at.rest[:, 2 * KEYS_WIDTH:2 * KEYS_WIDTH + width]
    at.attended[...] = at.rest[:, 2 * KEYS_WIDTH + width:]
    for source, target in (
        (at.key, at.key_out), (at.value, at.value_out), (at.query, at.query_out), (at.attended, at.attended_out),
    ):
        send(source, target)
    for load, first, target, place in ((loads[1], 0, at.gate, at.gate_out), (loads[2], 5, at.up, at.up_out)):
        load.wait()
        columns(first, target)
        send(target, place)
    loads[3].wait()
    down_rows = at.down.shape[1]
    for unit in range(5):
        at.down_float[unit * down_rows:(unit + 1) * down_rows, :] = at.down[unit].astype(jnp.float32)
    send(at.down_float, at.down_out)
    loads[4].wait()
    at.norm_attn[...] = at.little[0, 0:1, :rows]
    at.norm_ffn[...] = at.little[0, 1:2, :rows]
    at.router[...] = at.little[0, 2:4, :rows]
    loads[5].wait()
    send(at.hidden, at.hidden_out)
    loads[6].wait()
    send(at.gradient, at.gradient_out)
    for store in stores:
        store.wait()


def final(small, saved, top, bottom, weights, mesh_sizes):
    nb, nd = mesh_sizes
    m, n = nb.bit_length() - 1, nd.bit_length() - 1
    grad = bottom["grad_hidden"]
    piece, width = grad.shape
    hidden_units = weights["w_gate_hbm"].shape[1]
    rows = width // nb
    padded = -(-rows // 8) * 8
    down_rows = hidden_units // nb // 5
    tokens = RECUR * piece

    def spread(array):
        if padded == rows:
            return array
        split = array.reshape(RECUR, nb, rows, piece)
        return jnp.pad(split, ((0, 0), (0, 0), (0, padded - rows), (0, 0))).reshape(RECUR, nb * padded, piece)

    inputs = small | dict(small_before=bottom["small"])
    operands = dict(
        metas_hbm=saved["metas"], turned_hbm=saved["turned"], dat_hbm=bottom["dat"], att_hbm=saved["att"],
        lse_hbm=saved["lse"], kv_hbm=saved["kv"], w_query_hbm=weights["w_query_hbm"],
        key_weight_hbm=weights["key_weight_hbm"], value_weight_hbm=weights["value_weight_hbm"], hid_hbm=saved["hid"],
        grad_hbm=grad, inner_hbm=saved["inner"], nffn_hbm=spread(saved["nffn"]), normed_hbm=spread(saved["normed"]),
        attended_hbm=spread(saved["att"]), dffn_0_hbm=bottom["dffn"], dffn_1_hbm=top["dffn"],
        dgate_0_hbm=bottom["dgate_out"], dgate_1_hbm=top["dgate"], dup_0_hbm=bottom["dup_out"], dup_1_hbm=top["dup"],
        far_0_hbm=bottom["far"], far_1_hbm=top["far"], near_1_hbm=bottom["near_out"],
    )
    near_width = bottom["near_out"].shape[1]
    families = (
        ("wide", 15, (2 * padded, UNIT_COLUMNS), low, WIDE_SLOTS, 1), ("down", 5, (down_rows, width), low, DOWN_SLOTS, 0),
        ("small", 1, (16, 128), jnp.float32, 1, 0),
    )
    outs = dict(grad_out=((width, piece), jnp.float32))
    buffers = attention_buffers(nb, piece, width, low) | dict(
        grad=((piece, width), jnp.float32), gate_side=((tokens, hidden_units), low), up_side=((tokens, hidden_units), low),
        inner=((hidden_units, tokens), low), left=((nb * padded, tokens), low), left_attended=((nb * padded, tokens), low),
        dffn=((tokens, width), low), gain_row=((1, width), jnp.float32),
    )
    for name, count, shape, dtype, slots, split in families:
        outs["out_" + name] = ((count, *shape), dtype)
        buffers["part_" + name] = ((slots, *(2,) * m, *shape), dtype)
        for stage in range(m):
            buffers["blk_%s_%d" % (name, stage)] = ((count, *(2,) * (m - 1 - stage), *shape), dtype)
        for stage in range(n):
            buffers["dp_%s_%d" % (name, stage)] = ((count, *shape), dtype)
    sums, hops = (2 * KEY_VALUE_HEADS, m), (21, m + n + 1)
    semaphores = dict(load_sems=(32,), weight_sems=(2 * KEY_VALUE_HEADS,), kv_send=sums, kv_recv=sums, send_sems=hops, recv_sems=hops)
    names = (*inputs, *operands, *outs, *buffers, *semaphores)
    gradient, wide, down, little = pl.pallas_call(
        functools.partial(final_kernel, (nb, m, n, piece, rows, padded, near_width), names),
        out_shape=[shaped(entry) for entry in outs.values()],
        in_specs=[spec(pltpu.VMEM)] * len(inputs) + [spec(pl.ANY)] * len(operands),
        out_specs=[spec(pltpu.VMEM)] * len(outs),
        scratch_shapes=spaces(buffers.values()) + dma_semaphores(*semaphores.values()),
        compiler_params=pltpu.CompilerParams(
            collective_id=0, has_side_effects=True, vmem_limit_bytes=VMEM_LIMIT
        ),
        cost_estimate=pl.CostEstimate(
            flops=2 * tokens * width * 14000, bytes_accessed=30 * 1024 * 1024, transcendentals=0
        ),
        name="weight_grads",
    )(*inputs.values(), *operands.values())
    heads, square, tall, turned = (KEYS_WIDTH, rows), (rows, width), (rows, hidden_units), (width, piece)
    operands = dict(wide_in=wide, down_in=down, little_in=little, hidden_in=saved["hidden_out"], gradient_in=gradient)
    near_outs = dict(norm_attn=(1, rows), norm_ffn=(1, rows), router=(2, rows))
    far_outs = dict(
        key_out=heads, value_out=heads, query_out=square, attended_out=square, gate_out=tall, up_out=tall,
        down_out=(5 * down_rows, width), hidden_out=turned, gradient_out=turned,
    )
    buffers = dict(
        wide=(wide.shape, low), down=(down.shape, low), little=(little.shape, jnp.float32), rest=((rows, 2560), jnp.float32),
        key=(heads, jnp.float32), value=(heads, jnp.float32), query=(square, jnp.float32), attended=(square, jnp.float32),
        gate=(tall, jnp.float32), up=(tall, jnp.float32), down_float=((5 * down_rows, width), jnp.float32),
        hidden=(turned, jnp.float32), gradient=(turned, jnp.float32),
    )
    outs = pl.pallas_call(
        functools.partial(unpack_kernel, (rows, padded), (*operands, *near_outs, *far_outs, *buffers, *dict(sems=0))),
        out_shape=[jax.ShapeDtypeStruct(shape, jnp.float32) for shape in (near_outs | far_outs).values()],
        in_specs=[spec(pl.ANY)] * len(operands),
        out_specs=[spec(pltpu.VMEM)] * len(near_outs) + [spec(pl.ANY)] * len(far_outs),
        scratch_shapes=spaces(buffers.values()) + dma_semaphores((16,)),
        compiler_params=pltpu.CompilerParams(vmem_limit_bytes=VMEM_LIMIT),
        name="unpack",
    )(*operands.values())
    norm_a, norm_f, router, key, value, query, out, gate, up, down, hidden, gradient = outs
    return (
        hidden.T[None], gradient.T[None], norm_a[0], norm_f[0], query, key.T, value.T, out, gate, up, down, router.T,
    )


def local(
    tokens,
    depths,
    segments,
    norm_attn,
    norm_ffn,
    w_query,
    key_weight,
    value_weight,
    w_out,
    w_gate,
    w_up,
    w_down,
    w_router,
    cotangent,
    mesh_sizes,
):
    piece = tokens.shape[1]
    positions = lax.axis_index("blk") * piece + jnp.arange(piece, dtype=jnp.int32)
    angles = frequencies(HEAD_DIMENSION)[:, None] * positions.astype(jnp.float32)[None, :]
    tables = dict(cosines=jnp.cos(angles), sines=jnp.sin(angles), norms=jnp.stack([norm_attn, norm_ffn]))
    routing = dict(router=w_router.T, depths=depths)
    heads = dict(w_query_hbm=w_query, key_weight_hbm=key_weight.T, value_weight_hbm=value_weight.T)
    weights = heads | dict(w_out_hbm=w_out, w_gate_hbm=w_gate, w_up_hbm=w_up, w_down_hbm=w_down.T)
    nb = mesh_sizes[0]
    saved = forward(
        tables | routing | dict(tokens=tokens[0].T, cotangent=cotangent[0].T, segments=segments), weights, nb
    )
    operands = dict(
        metas_hbm=saved["metas"], turned_hbm=saved["turned"], dat_hbm=saved["dat"], att_hbm=saved["att"],
        lse_hbm=saved["lse"], kv_hbm=saved["kv"], grad_hbm=saved["grad_hidden"], hid_1_hbm=saved["hid_1"],
        hid_0_hbm=saved["hid"], branch_hbm=saved["branch"], slope_hbm=saved["slope"], silu_hbm=saved["silu"],
        middle_hbm=saved["middle"],
    )
    bottom = backward(1, tables | routing | dict(small_before=saved["small"]), weights | operands, nb)
    return final(tables, saved, saved, bottom, weights, mesh_sizes)


def solution(mesh):
    sizes = (mesh.shape["blk"], mesh.shape["dp"])
    return jax.shard_map(
        functools.partial(local, mesh_sizes=sizes),
        mesh=mesh,
        in_specs=(
            P("dp", "blk", None),
            P("dp", "blk"),
            P("dp", "blk"),
            P(),
            P(),
            P(),
            P(),
            P(),
            P(),
            P(),
            P(),
            P(),
            P(),
            P("dp", "blk", None),
        ),
        out_specs=(
            P("dp", "blk", None),
            P("dp", "blk", None),
            P("blk"),
            P("blk"),
            P("blk", None),
            P("blk", None),
            P("blk", None),
            P("blk", None),
            P("blk", None),
            P("blk", None),
            P("blk", None),
            P("blk", None),
        ),
        check_vma=False,
    )
```

```python
import functools
import itertools
import math
import types

import jax
import jax.numpy as jnp
from jax import lax
from jax.experimental import pallas as pl
from jax.experimental.pallas import tpu as pltpu
from jax.sharding import PartitionSpec as P

QUERY_HEADS = 15
KEY_VALUE_HEADS = 5
HEAD_DIMENSION = 64
RECUR = 2
HEAD_SHARE = QUERY_HEADS // KEY_VALUE_HEADS
KEYS_WIDTH = KEY_VALUE_HEADS * HEAD_DIMENSION
PAIR = 2 * HEAD_DIMENSION
UNIT_COLUMNS = 256
SPAN = 2
VMEM_LIMIT = 63 * 1024 * 1024

epsilon = 1e-05
masked_score = -1e30
low = jnp.bfloat16


def frequencies(head_size):
    return jnp.exp(
        jnp.arange(head_size // 2, dtype=jnp.float32) * (-2.0 * math.log(10000.0) / head_size)
    )


def rms_scale(values):
    return lax.rsqrt(jnp.mean(values * values, axis=-1, keepdims=True) + epsilon)


def norm_gradient(grad_norm, values, gain):
    scale = rms_scale(values)
    weighted = grad_norm * gain
    grad_values = scale * weighted - values * (scale * scale * scale) * jnp.mean(
        weighted * values, axis=-1, keepdims=True
    )
    return grad_values, jnp.sum(grad_norm * values * scale, axis=0, keepdims=True)


def dot_last(left, right):
    return lax.dot_general(left, right, (((1,), (1,)), ((), ())), preferred_element_type=jnp.float32)


def plain_dot(left, right):
    return jnp.dot(left, right, preferred_element_type=jnp.float32)


def bits_of(number, count):
    return tuple((number >> (count - 1 - at)) & 1 for at in range(count))


def bit_of(position, bit):
    return lax.rem(position // (1 << bit), 2)


def block_bits(block, m):
    return tuple(bit_of(block, bit) for bit in range(m - 1, -1, -1))


def flipped(position, bit):
    return position + (1 << bit) * (1 - 2 * bit_of(position, bit))


def remote(source, target, sems, at, device):
    return pltpu.make_async_remote_copy(
        src_ref=source,
        dst_ref=target,
        send_sem=sems[0].at[at],
        recv_sem=sems[1].at[at],
        device_id=device,
        device_id_type=pl.DeviceIdType.MESH,
    )


def greet(partners):
    barrier = pltpu.get_barrier_semaphore()
    for partner in partners:
        pl.semaphore_signal(barrier, inc=1, device_id=partner, device_id_type=pl.DeviceIdType.MESH)
    pl.semaphore_wait(barrier, len(partners))


def turn_heads(turned, cosine, sine, heads):
    split = turned.reshape(heads, 2, HEAD_DIMENSION // 2, turned.shape[1])
    first, second = split[:, 0], split[:, 1]
    both = jnp.stack([first * cosine - second * sine, second * cosine + first * sine], axis=1)
    return both.reshape(turned.shape)


def turn_back(turned, cosine, sine, heads):
    return turn_heads(turned, cosine, -sine, heads)


def head_rows(group, member):
    head = group * HEAD_SHARE + member
    return pl.ds(pl.multiple_of(head * HEAD_DIMENSION, HEAD_DIMENSION), HEAD_DIMENSION)


def as_column(row):
    wide = jnp.broadcast_to(row.astype(jnp.float32), (8, row.shape[1]))
    return wide.T[:, 0:1]


def key_steps(blk, span):
    return blk // (1 << span) + 1


def fill_bias(bias, metas, query_segments, level, blk, m, piece, span):
    many = 1 << span
    key_at = lax.broadcasted_iota(jnp.int32, (many * piece, piece), 0)
    query_at = lax.broadcasted_iota(jnp.int32, (many * piece, piece), 1)

    @pl.loop(0, key_steps(blk, span))
    def _(step):
        rows = metas[block_bits(step, m - span)].reshape(many, 8, piece)
        columns = jnp.concatenate([rows[block].T for block in range(many)], axis=0)
        live = jnp.where(columns[:, 1:2] > level, columns[:, 0:1], -1.0)
        shift = (blk - many * step) * piece
        allowed = (live == query_segments) & (key_at <= query_at + shift) | (key_at == query_at + shift)
        masked = jnp.where(allowed, 0.0, masked_score).astype(bias.dtype)
        bias[pl.ds(many * step, many)] = masked.reshape(many, piece, piece)


def step_bias(bias, step, piece, span):
    many = 1 << span
    here = bias[pl.ds(many * step, many)].reshape(many * piece, piece).astype(jnp.float32)
    return jnp.concatenate([here] * HEAD_SHARE, axis=1)


def kv_weight_loads(key_hbm, value_hbm, target, sems):
    copies = []
    for group in range(KEY_VALUE_HEADS):
        for side, source in enumerate((key_hbm, value_hbm)):
            rows = pl.ds(group * HEAD_DIMENSION, HEAD_DIMENSION)
            place = pl.ds(group * PAIR + side * HEAD_DIMENSION, HEAD_DIMENSION)
            copies.append(pltpu.make_async_copy(source.at[rows], target.at[place], sems.at[2 * group + side]))
    return copies


def turn_keys(both, cosine, sine):
    half = HEAD_DIMENSION // 2
    split = both.reshape(KEY_VALUE_HEADS, 4, half, both.shape[1])
    first, second = split[:, 0], split[:, 1]
    turned = [first * cosine - second * sine, second * cosine + first * sine, split[:, 2], split[:, 3]]
    return jnp.stack(turned, axis=1).reshape(both.shape)


def gain_rows(at):
    rows = [ref[...].astype(jnp.float32).reshape(1, ref.shape[0]) for ref in (at.norm_attn, at.norm_ffn)]
    return jnp.concatenate(rows, axis=0)


def spec(memory):
    return pl.BlockSpec(memory_space=memory)


def shaped(entry):
    return jax.ShapeDtypeStruct(*entry)


def spaces(entries):
    return [pltpu.VMEM(*entry) for entry in entries]


def dma_semaphores(*shapes):
    return [pltpu.SemaphoreType.DMA(shape) for shape in shapes]


class Piece:
    def __init__(self, at, kept_at, slot, flavour, family, sems, bits, middle=False):
        self.at, self.kept_at, self.slot, self.family, self.sems = at, kept_at, slot, family, sems
        self.m, self.n = bits
        left = list(range(self.m - 1, -1, -1))
        self.order = []
        for stage in range(self.m):
            place = len(left) - 1 if stage == 0 or flavour == 0 else 0
            self.order.append((left.pop(place), place, len(left)))
        self.last = self.m + self.n
        self.blk = lax.axis_index("blk")
        self.dp = lax.axis_index("dp") if self.n else None
        self.middle = middle
        if middle:
            inner = bit_of(self.dp, 0) != bit_of(self.dp, 1)
            outer = jnp.logical_not(inner)
            self.sends, self.receives = (outer, inner, inner), (inner, inner, outer)

    def half(self, ref, side):
        size = self.family.shape[self.family.split] // 2
        here = pl.ds(0 if isinstance(side, int) else pl.multiple_of(side * size, size), size)
        return ref.at[here, :] if self.family.split == 0 else ref.at[:, here]

    def held(self, stage):
        if stage == 0:
            return self.family.part, self.slot
        return self.family.blk[stage - 1], self.kept_at

    def copy(self, stage):
        m, family = self.m, self.family
        if stage < m:
            bit, place, others = self.order[stage]
            ref, index = self.held(stage)
            chosen = [slice(None)] * (others + 1)
            chosen[place] = 1 - bit_of(self.blk, bit)
            source = ref.at[(index, *chosen)]
            target = family.blk[stage].at[self.kept_at]
            device = {"blk": flipped(self.blk, bit)}
        elif self.middle:
            source, target, device = (
                (family.blk[m - 1], family.dp[0], {"dp": flipped(self.dp, 0)}),
                (family.dp[0], family.dp[1], {"dp": 3 - self.dp}),
                (family.out, family.out, {"dp": flipped(self.dp, 0)}),
            )[stage - m]
            source, target = source.at[self.kept_at], target.at[self.kept_at]
        elif stage < self.last:
            bit = stage - m
            if bit == 0:
                source = self.half(family.blk[m - 1].at[self.kept_at], 1 - bit_of(self.dp, 0))
            else:
                source = self.half(family.dp[bit - 1].at[self.kept_at], 0)
            target = self.half(family.dp[bit].at[self.kept_at], 0)
            device = {"dp": flipped(self.dp, bit)}
        else:
            source = self.half(family.out.at[self.kept_at], bit_of(self.dp, 0))
            target = source
            device = {"dp": flipped(self.dp, 0)}
        return remote(source, target, self.sems, (self.at, stage), device)

    def where(self, roles, stage, body):
        if self.middle and stage >= self.m:
            pl.when(roles[stage - self.m])(body)
        else:
            body()

    def start(self, stage):
        self.where(self.sends if self.middle else None, stage, lambda: self.copy(stage).start())

    def finish(self, stage):
        self.where(self.receives if self.middle else None, stage, lambda: self.receive(stage))

    def receive(self, stage):
        m, family = self.m, self.family
        self.copy(stage).wait_recv()
        if stage < m:
            bit, place, others = self.order[stage]
            ref, index = self.held(stage)
            for combo in itertools.product(range(2), repeat=others):
                chosen = list(combo)
                chosen.insert(place, bit_of(self.blk, bit))
                into = family.blk[stage].at[(self.kept_at, *combo)]
                self.add(into, into, ref.at[(index, *chosen)])
            if stage == 0:
                self.copy(0).wait_send()
        elif stage < self.last and self.middle:
            kept, sums = self.kept_at, family.dp
            if stage == m:
                self.add(sums[0].at[kept], sums[0].at[kept], family.blk[m - 1].at[kept])
            else:
                self.add(family.out.at[kept], sums[0].at[kept], sums[1].at[kept])
        elif stage < self.last:
            bit = stage - m
            got = self.half(family.dp[bit].at[self.kept_at], 0)
            if bit == 0:
                own = self.half(family.blk[m - 1].at[self.kept_at], bit_of(self.dp, 0))
            else:
                own = self.half(family.dp[bit - 1].at[self.kept_at], 0)
            into = got
            if stage == self.last - 1:
                into = self.half(family.out.at[self.kept_at], bit_of(self.dp, 0))
            self.add(into, got, own)

    def add(self, into, left, right):
        into[...] = left[...] + right[...]

    def drained(self, stages):
        for stage in stages:
            self.where(self.sends if self.middle else None, stage, lambda: self.copy(stage).wait_send())


def feed_forward_backward(at, level, gradient, ready, done):
    column = at.router[level:level + 1, :].astype(jnp.float32)
    active = as_column(at.depths[...]) > float(level)
    hidden = at.hid_level[...]
    chosen = jax.nn.sigmoid(jnp.sum(hidden * column, axis=1, keepdims=True))
    at.dbranch[...] = jnp.where(active, chosen, 0.0) * gradient
    dchosen = jnp.where(active, jnp.sum(gradient * at.branch_level[...], axis=1, keepdims=True), 0.0)
    dlogit = dchosen * chosen * (1.0 - chosen)
    at.small[2 + level:3 + level, :] = jnp.sum(hidden * dlogit, axis=0, keepdims=True)
    at.grad_hidden[...] = gradient + dlogit * column
    at.dffn[...] = at.dbranch[...].astype(low)

    ready(0)
    dinner = plain_dot(at.dffn[...], at.w_down[...])
    at.dgate[...] = (dinner * at.slope_level[...].astype(jnp.float32)).astype(low)
    at.dup[...] = (dinner * at.silu_level[...].astype(jnp.float32)).astype(low)
    done()
    at.dnorm_turned[...] = plain_dot(at.w_gate[...], at.dgate[...].T) + plain_dot(at.w_up[...], at.dup[...].T)
    ready(1)
    dnorm = at.dnorm_turned[...].T
    dmiddle, gain_share = norm_gradient(dnorm, at.middle_level[...], at.norms[1:2, :].astype(jnp.float32))
    at.small[1:2, :] += gain_share
    at.grad_hidden[...] += dmiddle
    dattn = (at.dbranch[...] + dmiddle).astype(low)
    lead = at.far.shape[1] - dattn.shape[1]
    at.far[:, :lead] = jnp.zeros((dattn.shape[0], lead), low)
    at.far[:, lead:] = dattn
    at.dat[...] = plain_dot(at.w_out[...], dattn.T).astype(low)


def forward_kernel(sizes, names, *refs):
    m, piece = sizes
    at = types.SimpleNamespace(**dict(zip(names, refs)))
    at.norms = gain_rows(at)
    blk = lax.axis_index("blk")
    mine = block_bits(blk, m)
    kv, metas = at.kv, at.metas
    weights = (
        (at.w_query_hbm, at.w_query), (at.w_out_hbm, at.w_out), (at.w_gate_hbm, at.w_gate), (at.w_up_hbm, at.w_up), (at.w_down_hbm, at.w_down),
    )
    loads = [pltpu.make_async_copy(*pair, at.load_sems.at[index]) for index, pair in enumerate(weights)]
    kv_loads = kv_weight_loads(at.key_weight_hbm, at.value_weight_hbm, at.kv_weight, at.weight_sems)
    for load in kv_loads + loads:
        load.start()
    saved = (
        (at.normed, at.normed_out), (at.turned, at.turned_out), (kv, at.kv_out), (at.lse, at.lse_out),
        (at.att, at.att_out), (at.nffn, at.nffn_out), (at.inner, at.inner_out),
    )

    def save(index, level):
        return pltpu.make_async_copy(
            saved[index][0].at[level] if index == 2 else saved[index][0], saved[index][1].at[level], at.save_sems.at[index, level]
        )

    first = (
        (at.hid.at[0], at.hid_out), (at.middle, at.middle_out), (at.silu, at.silu_out),
        (at.slope, at.slope_out), (at.branch, at.branch_out), (metas, at.metas_out),
        (at.far, at.far_out), (at.dat, at.dat_out), (at.dffn, at.dffn_out), (at.dgate, at.dgate_out), (at.dup, at.dup_out),
        (at.hid.at[1], at.hid_1_out),
    )
    late = [pltpu.make_async_copy(*pair, at.late_sems.at[index]) for index, pair in enumerate(first)]
    segment_row = at.segments[...].astype(jnp.float32)
    depth_column = as_column(at.depths[...])
    metas[mine] = jnp.concatenate(
        [segment_row, at.depths[...].astype(jnp.float32), jnp.zeros((6, piece), jnp.float32)], axis=0
    )
    greet([{"blk": flipped(blk, bit)} for bit in range(m)])

    def place(known):
        return tuple(slice(None) if bit in known else mine[m - 1 - bit] for bit in range(m - 1, -1, -1))

    orders = (list(range(1, m)), list(range(m - 1, 0, -1)))
    kv_sems = (at.kv_send, at.kv_recv)

    def kv_copies(level, group, stage):
        if stage == m - 1:
            ref = kv.at[(level, group, *place(range(1, m)))]
            return [remote(ref, ref, kv_sems, (level, group, 2 * stage), {"blk": flipped(blk, 0)})]
        copies = []
        for side, order in enumerate(orders):
            rows = pl.ds(side * (piece // 2), piece // 2)
            ref = kv.at[(level, group, *place(order[:stage]), rows)]
            copies.append(remote(ref, ref, kv_sems, (level, group, 2 * stage + side), {"blk": flipped(blk, order[stage])}))
        return copies

    def kv_advance(level, group, stage):
        if stage > 0:
            for copy in kv_copies(level, group, stage - 1):
                copy.wait_recv()
        if stage < m:
            for copy in kv_copies(level, group, stage):
                copy.start()

    def meta_copy(stage):
        bits = list(range(1, m)) + [0]
        ref = metas.at[place(bits[:stage])]
        return remote(ref, ref, (at.meta_send, at.meta_recv), stage, {"blk": flipped(blk, bits[stage])})

    meta_copy(0).start()
    cosine, sine = at.cosines[...], at.sines[...]
    gain_attn, gain_ffn = at.norms[0:1, :].astype(jnp.float32), at.norms[1:2, :].astype(jnp.float32)
    routers = at.router[...].astype(jnp.float32)
    at.hid[0] = at.tokens[...].T.astype(jnp.float32)
    late[0].start()
    at.query_pad[HEAD_DIMENSION:, :] = jnp.zeros_like(at.query_pad[HEAD_DIMENSION:, :])

    @pl.loop(0, RECUR)
    def _(level):
        @pl.when(level > 0)
        def _():
            for index in range(5):
                save(index, 0).wait()

        hidden = at.hid[level]
        at.flat[...] = (hidden * rms_scale(hidden) * gain_attn).astype(low)
        at.normed[...] = at.flat[...].T

        @pl.when(level == 0)
        def _():
            for load in kv_loads:
                load.wait()

        both = turn_keys(plain_dot(at.kv_weight[...], at.normed[...]), cosine, sine).T.astype(low)
        for group in range(KEY_VALUE_HEADS):
            kv[(level, group, *mine)] = both[:, group * PAIR:(group + 1) * PAIR]
            kv_advance(level, group, 0)

        @pl.when(level == 0)
        def _():
            loads[0].wait()
            for stage in range(1, m - 1):
                meta_copy(stage - 1).wait_recv()
                meta_copy(stage).start()

        queries = turn_heads(plain_dot(at.flat[...], at.w_query[...]).T, cosine, sine, QUERY_HEADS)
        at.turned[...] = (queries * HEAD_DIMENSION ** (-0.5)).astype(low)

        @pl.when(level == 0)
        def _():
            for stage in range(max(1, m - 1), m):
                meta_copy(stage - 1).wait_recv()
                meta_copy(stage).start()

        for stage in range(1, m - 1):
            for group in range(KEY_VALUE_HEADS):
                kv_advance(level, group, stage)
        kv_advance(level, 0, m - 1)

        @pl.when(level == 0)
        def _():
            meta_copy(m - 1).wait_recv()
            late[5].start()

        fill_bias(at.bias, metas, segment_row, level.astype(jnp.float32), blk, m, piece, SPAN)

        @pl.loop(0, KEY_VALUE_HEADS)
        def _(group):
            @pl.when(group + 1 < KEY_VALUE_HEADS)
            def _():
                kv_advance(level, group + 1, m - 1)

            kv_advance(level, group, m)
            for member in range(HEAD_SHARE):
                at.query_pad[:HEAD_DIMENSION, member * piece:(member + 1) * piece] = at.turned[head_rows(group, member), :]
            at.top[...] = jnp.full_like(at.top, masked_score)
            at.total[...] = jnp.zeros_like(at.total)

            @pl.loop(0, key_steps(blk, SPAN))
            def _(index):
                step = key_steps(blk, SPAN) - 1 - index
                rows = kv[(level, group, *block_bits(step, m - SPAN))].reshape((1 << SPAN) * piece, PAIR)
                scores = plain_dot(rows, at.query_pad[...]) + step_bias(at.bias, step, piece, SPAN)
                before = at.top[0:1, :]
                after = jnp.maximum(before, jnp.max(scores, axis=0, keepdims=True))
                raised = jnp.exp(scores - after)
                shrink = jnp.exp(before - after)
                at.top[0:1, :] = after
                ones = jnp.ones((16, rows.shape[0]), low)
                left = jnp.concatenate([rows.T[HEAD_DIMENSION:], ones], axis=0)
                at.total[...] = at.total[...] * shrink + plain_dot(left, raised.astype(low))

            sums = at.total[HEAD_DIMENSION:HEAD_DIMENSION + 1, :]
            at.lse[pl.ds(group, 1), :] = at.top[0:1, :] + jnp.log(sums)
            out = at.total[:HEAD_DIMENSION, :] / sums
            for member in range(HEAD_SHARE):
                at.att[head_rows(group, member), :] = out[:, member * piece:(member + 1) * piece].astype(low)

        for index in range(5):
            save(index, level).start()

        @pl.when(level == 0)
        def _():
            loads[1].wait()

        @pl.when(level > 0)
        def _():
            save(5, 0).wait()
            save(6, 0).wait()
            for copy in late[1:5]:
                copy.wait()

        attn = plain_dot(at.att[...].T, at.w_out[...])
        mid = at.hid[level] + attn
        at.middle[...] = mid
        at.branch[...] = attn
        at.flat[...] = (mid * rms_scale(mid) * gain_ffn).astype(low)
        at.nffn[...] = at.flat[...].T
        save(5, level).start()

        @pl.when(level == 0)
        def _():
            loads[2].wait()
            loads[3].wait()

        gate_pre = plain_dot(at.flat[...], at.w_gate[...])
        up_pre = plain_dot(at.flat[...], at.w_up[...])
        opened = jax.nn.sigmoid(gate_pre)
        passed = gate_pre * opened
        at.silu[...] = passed.astype(low)
        at.slope[...] = (up_pre * (opened + passed - passed * opened)).astype(low)
        at.inner[...] = (passed * up_pre).astype(low).T
        save(6, level).start()

        @pl.when(level == 0)
        def _():
            loads[4].wait()

        at.branch[...] += plain_dot(at.w_down[...], at.inner[...]).T
        column = jnp.where(level == 0, routers[0:1, :], routers[1:2, :])
        logit = jnp.sum(at.hid[level] * column, axis=1, keepdims=True)
        weight = jnp.where(depth_column > level.astype(jnp.float32), jax.nn.sigmoid(logit), 0.0)
        at.hid[level + 1] = at.hid[level] + weight * at.branch[...]

        @pl.when(level == 0)
        def _():
            for copy in late[1:5]:
                copy.start()

    at.hidden_out[...] = at.hid[RECUR].T
    top = RECUR - 1
    at.hid_level, at.branch_level, at.middle_level = at.hid.at[top], at.branch, at.middle
    at.silu_level, at.slope_level = at.silu, at.slope
    at.small[...] = jnp.zeros_like(at.small)
    feed_forward_backward(at, top, at.cotangent[...].T.astype(jnp.float32), lambda part: None, lambda: None)
    for copy in late[6:]:
        copy.start()
    for stage in range(m):
        meta_copy(stage).wait_send()
    for level in range(RECUR):
        for group in range(KEY_VALUE_HEADS):
            for stage in range(m):
                for copy in kv_copies(level, group, stage):
                    copy.wait_send()
    for index in range(len(saved)):
        save(index, RECUR - 1).wait()
    for copy in late[:1] + late[5:]:
        copy.wait()


def far_width(width):
    return 2 * width + 2 * KEYS_WIDTH - 1536


def forward(small, weights, nb):
    m = nb.bit_length() - 1
    width, piece = small["tokens"].shape
    hidden_units = weights["w_gate_hbm"].shape[1]
    blocks, wide = (2,) * m, HEAD_SHARE * piece
    rows, turned = ((piece, width), jnp.float32), ((RECUR, width, piece), low)
    hidden = ((piece, hidden_units), low)
    saved = dict(
        normed=turned, turned=turned, kv=((RECUR, KEY_VALUE_HEADS, *blocks, piece, PAIR), low),
        lse=((RECUR, 8, wide), jnp.float32), att=turned, nffn=turned, inner=((RECUR, hidden_units, piece), low),
        metas=((*blocks, 8, piece), jnp.float32), far=((piece, far_width(width)), low), dat=((width, piece), low),
        dffn=((piece, width), low), dgate=hidden, dup=hidden,
    )
    first = dict(hid=rows, middle=rows, silu=hidden, slope=hidden, branch=rows)
    outs = dict(hidden_out=((width, piece), jnp.float32), grad_hidden=rows, small=((8, width), jnp.float32))
    anywhere = {name + "_out": entry for name, entry in (saved | first | dict(hid_1=rows)).items()}
    single = {name: (shape[1:], dtype) for name, (shape, dtype) in saved.items() if shape[0] == RECUR and name not in ("kv", "metas")}
    buffers = {name[:-4]: (array.shape, array.dtype) for name, array in weights.items()} | saved | single | first | dict(
        kv_weight=((2 * KEYS_WIDTH, width), low),
        hid=((RECUR + 1, piece, width), jnp.float32), flat=((piece, width), low),
        bias=((nb, piece, piece), jnp.float32), query_pad=((PAIR, wide), low), top=((8, wide), jnp.float32),
        total=((HEAD_DIMENSION + 16, wide), jnp.float32), dbranch=rows, dnorm_turned=((width, piece), jnp.float32),
    )
    semaphores = dict(
        load_sems=(5,), weight_sems=(2 * KEY_VALUE_HEADS,), save_sems=(7, RECUR), late_sems=(12,), kv_send=(RECUR, KEY_VALUE_HEADS, 2 * m),
        kv_recv=(RECUR, KEY_VALUE_HEADS, 2 * m), meta_send=(m,), meta_recv=(m,),
    )
    results = pl.pallas_call(
        functools.partial(forward_kernel, (m, piece), (*small, *weights, *outs, *anywhere, *buffers, *semaphores)),
        out_shape=[shaped(entry) for entry in (outs | anywhere).values()],
        in_specs=[spec(pltpu.VMEM)] * len(small) + [spec(pl.ANY)] * len(weights),
        out_specs=[spec(pltpu.VMEM)] * len(outs) + [spec(pl.ANY)] * len(anywhere),
        scratch_shapes=spaces(buffers.values()) + dma_semaphores(*semaphores.values()),
        compiler_params=pltpu.CompilerParams(
            collective_id=1, has_side_effects=True, vmem_limit_bytes=VMEM_LIMIT
        ),
        cost_estimate=pl.CostEstimate(
            flops=3 * RECUR * piece * width * 10240, bytes_accessed=48 * 1024 * 1024, transcendentals=0
        ),
        name="forward_levels",
    )(*small.values(), *weights.values())
    return dict(zip((*outs, *(name[:-4] for name in anywhere)), results))


class AttentionBackward:
    def __init__(self, at, m, piece, level, span):
        self.at, self.m, self.piece, self.level, self.span = at, m, piece, level, span
        self.blk = lax.axis_index("blk")
        self.family = types.SimpleNamespace(part=at.part, blk=at.halves, dp=(), out=None, shape=(piece // 2, PAIR), split=0)

    def pieces(self, group):
        sems = (self.at.kv_send, self.at.kv_recv)
        return [
            Piece(2 * group + side, 2 * group + side, 2 * group + side, side, self.family, sems, (self.m, 0))
            for side in range(2)
        ]

    def move(self, group, stage):
        for piece_of in self.pieces(group):
            piece_of.finish(stage)
            if stage + 1 < self.m:
                piece_of.start(stage + 1)

    def begin(self):
        at = self.at
        query_segments = at.metas[block_bits(self.blk, self.m)][0:1, :]
        fill_bias(at.bias, at.metas, query_segments, float(self.level), self.blk, self.m, self.piece, self.span)
        at.query_pad[HEAD_DIMENSION:, :] = jnp.zeros_like(at.query_pad[HEAD_DIMENSION:, :])
        at.dat_pad[:HEAD_DIMENSION, :] = jnp.zeros_like(at.dat_pad[:HEAD_DIMENSION, :])

    def group(self, group):
        at, m, piece, blk = self.at, self.m, self.piece, self.blk
        half = piece // 2
        carried = []
        for member in range(HEAD_SHARE):
            rows, lanes = head_rows(group, member), slice(member * piece, (member + 1) * piece)
            at.query_pad[:HEAD_DIMENSION, lanes] = at.turned[rows, :]
            at.dat_pad[HEAD_DIMENSION:, lanes] = at.dat_turned[rows, :]
            product = at.dat_turned[rows, :].astype(jnp.float32) * at.att_turned[rows, :].astype(jnp.float32)
            carried.append(jnp.sum(product, axis=0, keepdims=True))
        carried = jnp.concatenate(carried, axis=1)
        at.query_rows[...] = at.query_pad[...].T
        at.dat_rows[...] = at.dat_pad[...].T
        log_total = at.lse[pl.ds(group, 1), :]
        at.dq_sum[...] = jnp.zeros_like(at.dq_sum)

        span, lead = self.span, m - self.span

        @pl.loop(0, key_steps(blk, span))
        def _(step):
            rows = at.kv[(group, *block_bits(step, lead))].reshape((1 << span) * piece, PAIR)
            probability = jnp.exp(plain_dot(rows, at.query_pad[...]) + step_bias(at.bias, step, piece, span) - log_total)
            dprob = plain_dot(rows, at.dat_pad[...])
            dscores = (probability * (dprob - carried)).astype(low)
            share = plain_dot(dscores, at.query_rows[...]) + plain_dot(probability.astype(low), at.dat_rows[...])
            share = share.astype(low)
            for block in range(1 << span):
                for side in range(2):
                    first = block * piece + side * half
                    place = (2 * group + side, *block_bits(step, lead), *bits_of(block, span))
                    at.part[place] = share[first:first + half]
            at.dq_sum[...] += plain_dot(rows.T[:HEAD_DIMENSION], dscores)

        @pl.loop(key_steps(blk, span), 1 << lead)
        def _(step):
            for block in range(1 << span):
                for side in range(2):
                    place = (2 * group + side, *block_bits(step, lead), *bits_of(block, span))
                    at.part[place] = jnp.zeros((half, PAIR), low)

        for piece_of in self.pieces(group):
            piece_of.start(0)
        for member in range(HEAD_SHARE):
            at.dq_turned[head_rows(group, member), :] = at.dq_sum[:, member * piece:(member + 1) * piece]

    def follow(self, group):
        for stage in range(self.m - 1):
            earlier = group - 1 - stage
            if isinstance(group, int):
                if 0 <= earlier < KEY_VALUE_HEADS:
                    self.move(earlier, stage)
            else:
                @pl.when(earlier >= 0)
                def _():
                    self.move(earlier, stage)

    def queries(self, cosine, sine):
        at = self.at
        dqueries = turn_back(at.dq_turned[...] * HEAD_DIMENSION ** (-0.5), cosine, sine, QUERY_HEADS).astype(low)
        self.put(2 * KEYS_WIDTH, dqueries.T)
        at.dnorm[...] = plain_dot(at.w_query[...], dqueries).T

    def put(self, column, values):
        self.at.near[:, column:column + values.shape[1]] = values

    def keys(self, cosine, sine):
        at, m = self.at, self.m
        filled = 2 * KEYS_WIDTH + QUERY_HEADS * HEAD_DIMENSION
        self.put(filled, jnp.zeros((self.piece, at.near.shape[1] - filled), low))
        sums = []
        for group in range(KEY_VALUE_HEADS):
            self.move(group, m - 1)
            sums.append(jnp.concatenate([at.halves[m - 1][2 * group], at.halves[m - 1][2 * group + 1]], axis=0))
        both = jnp.concatenate(sums, axis=1).astype(jnp.float32).T
        both = turn_keys(both, cosine, -sine).astype(low).T
        self.put(0, both)
        at.dnorm[...] += plain_dot(both, at.kv_weight[...])

    def drained(self):
        for group in range(KEY_VALUE_HEADS):
            for piece_of in self.pieces(group):
                piece_of.drained(range(1, self.m))


def attention_buffers(nb, piece, width, bias_type):
    m, wide, heads = nb.bit_length() - 1, HEAD_SHARE * piece, 2 * KEY_VALUE_HEADS
    turned = ((width, piece), low)
    pad, pad_rows = ((PAIR, wide), low), ((wide, PAIR), low)
    buffers = dict(
        turned=turned, dat_turned=turned, att_turned=turned, kv=((KEY_VALUE_HEADS, *(2,) * m, piece, PAIR), low),
        lse=((8, wide), jnp.float32), metas=((*(2,) * m, 8, piece), jnp.float32), w_query=((width, width), low),
        kv_weight=((2 * KEYS_WIDTH, width), low), dq_turned=((width, piece), jnp.float32),
        bias=((nb, piece, piece), bias_type), query_pad=pad, dat_pad=pad, query_rows=pad_rows, dat_rows=pad_rows,
        dq_sum=((HEAD_DIMENSION, wide), jnp.float32), part=((heads, *(2,) * m, piece // 2, PAIR), low),
        dnorm=((piece, width), jnp.float32), hid=((piece, width), jnp.float32),
    )
    for stage in range(m):
        buffers["half_%d" % stage] = ((heads, *(2,) * (m - 1 - stage), piece // 2, PAIR), low)
    return buffers


def backward_kernel(sizes, names, *refs):
    m, piece, level = sizes
    at = types.SimpleNamespace(**dict(zip(names, refs)))
    at.norms = gain_rows(at)
    at.halves = [getattr(at, "half_%d" % stage) for stage in range(m)]
    at.near = at.near_out
    blk = lax.axis_index("blk")
    pairs = (
        (at.metas_hbm, at.metas), (at.turned_hbm.at[level], at.turned), (at.dat_hbm, at.dat_turned),
        (at.att_hbm.at[level], at.att_turned), (at.lse_hbm.at[level], at.lse), (at.kv_hbm.at[level], at.kv),
        (at.w_query_hbm, at.w_query),
        (at.grad_hbm, at.grad_hidden), (at.hid_1_hbm, at.hid),
        (at.hid_0_hbm, at.hid_level), (at.branch_hbm, at.branch_level), (at.w_down_hbm, at.w_down),
        (at.slope_hbm, at.slope_level), (at.silu_hbm, at.silu_level), (at.w_gate_hbm, at.w_gate), (at.w_up_hbm, at.w_up),
        (at.middle_hbm, at.middle_level), (at.w_out_hbm, at.w_out),
    )
    loads = [pltpu.make_async_copy(*pair, at.load_sems.at[index]) for index, pair in enumerate(pairs)]
    loads += kv_weight_loads(at.key_weight_hbm, at.value_weight_hbm, at.kv_weight, at.weight_sems)
    for load in loads:
        load.start()
    saves = [
        pltpu.make_async_copy(*pair, at.save_sems.at[index])
        for index, pair in enumerate(((at.dgate, at.dgate_out), (at.dup, at.dup_out)))
    ]
    greet([{"blk": flipped(blk, bit)} for bit in range(m)])
    work = AttentionBackward(at, m, piece, level, SPAN)
    loads[0].wait()
    work.begin()
    for load in loads[1:6]:
        load.wait()

    @pl.loop(0, KEY_VALUE_HEADS)
    def _(group):
        work.group(group)
        work.follow(group)

    cosine, sine = at.cosines[...], at.sines[...]
    for virtual in range(KEY_VALUE_HEADS, KEY_VALUE_HEADS + m - 1):
        work.follow(virtual)
        if virtual == KEY_VALUE_HEADS:
            loads[6].wait()
            work.queries(cosine, sine)
    for load in loads[7:]:
        load.wait()
    work.keys(cosine, sine)
    dhidden, gain_share = norm_gradient(at.dnorm[...], at.hid[...], at.norms[0:1, :].astype(jnp.float32))
    at.small[...] = at.small_before[...]
    at.small[0:1, :] = gain_share
    gradient = at.grad_hidden[...] + dhidden
    at.dnorm[...] = gradient
    feed_forward_backward(at, level - 1, at.dnorm[...], lambda part: None, lambda: [save.start() for save in saves])
    work.drained()
    for save in saves:
        save.wait()


def backward(level, small, operands, nb):
    m = nb.bit_length() - 1
    piece, width = operands["grad_hbm"].shape
    hidden_units = operands["w_gate_hbm"].shape[1]
    rows, flat, hidden = ((piece, width), jnp.float32), ((piece, width), low), ((piece, hidden_units), low)
    outs = dict(
        grad_hidden=rows, small=((8, width), jnp.float32), near_out=((piece, 1792), low), dffn=flat,
        dat=((width, piece), low), far=((piece, far_width(width)), low),
    )
    anywhere = dict(dgate_out=hidden, dup_out=hidden)
    buffers = attention_buffers(nb, piece, width, jnp.float32) | dict(
        hid_level=rows, branch_level=rows, middle_level=rows, w_down=((width, hidden_units), low), slope_level=hidden,
        silu_level=hidden, w_gate=((width, hidden_units), low), w_up=((width, hidden_units), low),
        w_out=((width, width), low), dbranch=rows, dnorm_turned=((width, piece), jnp.float32), dgate=hidden, dup=hidden,
    )
    sums = (2 * KEY_VALUE_HEADS, m)
    semaphores = dict(load_sems=(18,), weight_sems=(2 * KEY_VALUE_HEADS,), save_sems=(2,), kv_send=sums, kv_recv=sums)
    results = pl.pallas_call(
        functools.partial(
            backward_kernel, (m, piece, level), (*small, *operands, *outs, *anywhere, *buffers, *semaphores)
        ),
        out_shape=[shaped(entry) for entry in (outs | anywhere).values()],
        in_specs=[spec(pltpu.VMEM)] * len(small) + [spec(pl.ANY)] * len(operands),
        out_specs=[spec(pltpu.VMEM)] * len(outs) + [spec(pl.ANY)] * len(anywhere),
        scratch_shapes=spaces(buffers.values()) + dma_semaphores(*semaphores.values()),
        compiler_params=pltpu.CompilerParams(
            collective_id=2, has_side_effects=True, vmem_limit_bytes=VMEM_LIMIT
        ),
        cost_estimate=pl.CostEstimate(
            flops=2 * piece * width * 20000, bytes_accessed=32 * 1024 * 1024, transcendentals=0
        ),
        name="backward_level",
    )(*small.values(), *operands.values())
    return dict(zip((*outs, *anywhere), results))


WIDE_SLOTS, DOWN_SLOTS = 4, 2


def final_kernel(sizes, names, *refs):
    nb, m, n, piece, rows, padded, near_width = sizes
    at = types.SimpleNamespace(**dict(zip(names, refs)))
    at.norms = gain_rows(at)
    at.halves = [getattr(at, "half_%d" % stage) for stage in range(m)]
    blk, dp = lax.axis_index("blk"), lax.axis_index("dp")
    at.near = at.gate_side.at[pl.ds(0, piece), pl.ds(0, near_width)]
    counter = itertools.count()

    def load(source, target):
        return pltpu.make_async_copy(source, target, at.load_sems.at[next(counter)])

    def both_lanes(ref, target):
        return [load(ref.at[level], target.at[:, pl.ds(level * piece, piece)]) for level in range(RECUR)]

    def both_rows(low_ref, deep_ref, target, width):
        pairs = ((low_ref, 0), (deep_ref, piece))
        return [load(ref, target.at[pl.ds(first, piece), pl.ds(0, width)]) for ref, first in pairs]

    hidden_units, width = at.gate_side.shape[1], at.dffn.shape[1]
    far_lanes = at.far_0_hbm.shape[1]
    loads = types.SimpleNamespace(
        nffn=both_lanes(at.nffn_hbm, at.left),
        dgate=both_rows(at.dgate_0_hbm, at.dgate_1_hbm, at.gate_side, hidden_units),
        inner=both_lanes(at.inner_hbm, at.inner),
        dffn=both_rows(at.dffn_0_hbm, at.dffn_1_hbm, at.dffn, width),
        metas=[load(at.metas_hbm, at.metas)],
        heads=[
            load(at.turned_hbm.at[0], at.turned), load(at.dat_hbm, at.dat_turned), load(at.att_hbm.at[0], at.att_turned),
            load(at.lse_hbm.at[0], at.lse), load(at.kv_hbm.at[0], at.kv),
        ],
        dup=both_rows(at.dup_0_hbm, at.dup_1_hbm, at.up_side, hidden_units),
        w_query=[load(at.w_query_hbm, at.w_query)],
        rest=[
            load(at.hid_hbm, at.hid), load(at.grad_hbm, at.grad),
        ],
        attended=both_lanes(at.attended_hbm, at.left_attended),
        kv_weight=kv_weight_loads(at.key_weight_hbm, at.value_weight_hbm, at.kv_weight, at.weight_sems),
    )
    late = types.SimpleNamespace(
        near=[load(at.near_1_hbm, at.gate_side.at[pl.ds(piece, piece), pl.ds(0, near_width)])],
        far=both_rows(at.far_0_hbm, at.far_1_hbm, at.up_side, far_lanes),
        normed=both_lanes(at.normed_hbm, at.left),
    )

    def begin(copies):
        for copy in copies:
            copy.start()

    def ready(copies):
        for copy in copies:
            copy.wait()

    for copies in vars(loads).values():
        begin(copies)
    greet([{"blk": flipped(blk, bit)} for bit in range(m)] + [{"dp": flipped(dp, bit)} for bit in range(n)])

    down_rows = at.part_down.shape[-2]

    def family(name, shape, split):
        return types.SimpleNamespace(
            part=getattr(at, "part_" + name), out=getattr(at, "out_" + name), shape=shape, split=split,
            blk=[getattr(at, "blk_%s_%d" % (name, stage)) for stage in range(m)],
            dp=[getattr(at, "dp_%s_%d" % (name, stage)) for stage in range(n)],
        )

    wide = family("wide", (2 * padded, UNIT_COLUMNS), 1)
    down = family("down", (down_rows, width), 0)
    little = family("small", (16, 128), 0)
    sems = (at.send_sems, at.recv_sems)
    units = itertools.count()

    def unit(holder, index, flavour, halves=n != 2):
        return Piece(next(units), index, index % holder.part.shape[0], flavour, holder, sems, (m, n), not halves)

    pairs = [[unit(wide, index, 0), unit(down, index, 1)] for index in range(5)]
    pairs += [[unit(wide, index, 0), unit(wide, index + 1, 1)] for index in (5, 7, 9)]
    pairs += [[unit(wide, 11, 0, True), unit(wide, 12, 1, True)]]
    pairs += [[unit(wide, 13, 0, True), unit(wide, 14, 1, True), unit(little, 0, 0, True)]]

    def compute_wide(index, slot):
        if index == 0:
            ready(loads.nffn)
            ready(loads.dgate)
        if index == 5:
            begin(late.near)
            ready(loads.dup)
        if index == 10:
            begin(late.far)
            begin(late.normed)
            ready(late.near)
            ready(late.normed)
            ready(loads.attended)
            ready(late.far)
        block, column = index // 5, (index % 5) * UNIT_COLUMNS
        second = 1280 + column
        upper_columns, lower_columns = slice(column, column + UNIT_COLUMNS), slice(second, second + UNIT_COLUMNS)
        if block < 2:
            right = at.gate_side if block == 0 else at.up_side
            upper = plain_dot(at.left[...], right[:, upper_columns])
            lower = plain_dot(at.left[...], right[:, lower_columns])
        else:
            upper = plain_dot(at.left[...], at.gate_side[:, upper_columns])
            lower = None
            if second < 1600:
                lower = plain_dot(at.left[...], at.gate_side[:, lower_columns])
            if second >= 1536:
                more = plain_dot(at.left_attended[...], at.up_side[:, second - 1536:second - 1536 + UNIT_COLUMNS])
                lower = more if lower is None else lower + more
        for target in range(nb):
            here = slice(target * padded, (target + 1) * padded)
            both = jnp.concatenate([upper[here], lower[here]], axis=0)
            at.part_wide[(slot, *bits_of(target, m))] = both.astype(low)

    def compute_down(index, slot):
        if index == 0:
            ready(loads.inner)
            ready(loads.dffn)
        firsts = [(target * 5 + index) * down_rows for target in range(nb)]
        left = jnp.concatenate([at.inner[first:first + down_rows, :] for first in firsts], axis=0)
        result = plain_dot(left, at.dffn[...])
        for target in range(nb):
            at.part_down[(slot, *bits_of(target, m))] = result[target * down_rows:(target + 1) * down_rows].astype(low)

    def compute_small():
        total = at.small_before[...]
        total = total + jnp.concatenate([at.gain_row[...], jnp.zeros((7, width), jnp.float32)], axis=0)
        at.part_small[...] = jnp.zeros_like(at.part_small)
        for target in range(nb):
            at.part_small[(0, *bits_of(target, m), slice(0, 8), slice(0, rows))] = total[:, target * rows:(target + 1) * rows]

    def compute(piece_of):
        if piece_of.family is wide:
            compute_wide(piece_of.kept_at, piece_of.slot)
        elif piece_of.family is down:
            compute_down(piece_of.kept_at, piece_of.slot)
        else:
            compute_small()
        piece_of.start(0)

    def moves(tick):
        for stage in range(m + n - 1, -1, -1):
            if 0 <= tick - stage < len(pairs):
                for piece_of in pairs[tick - stage]:
                    piece_of.finish(stage)
                    piece_of.start(stage + 1)

    work = AttentionBackward(at, m, piece, 0, 1)
    for pair in pairs[:2]:
        for piece_of in pair:
            compute(piece_of)
    ready(loads.metas)
    work.begin()
    ready(loads.heads)
    for group in range(KEY_VALUE_HEADS):
        moves(group)
        for piece_of in pairs[group + 2]:
            compute(piece_of)
        work.group(group)
        work.follow(group)
    cosine, sine = at.cosines[...], at.sines[...]
    moves(5)
    compute(pairs[7][0])
    ready(loads.w_query)
    for virtual in range(KEY_VALUE_HEADS, KEY_VALUE_HEADS + m - 1):
        work.follow(virtual)
        if virtual == KEY_VALUE_HEADS:
            work.queries(cosine, sine)
    moves(6)
    ready(loads.rest)
    ready(loads.kv_weight)
    work.keys(cosine, sine)
    compute(pairs[7][1])
    moves(7)
    for piece_of in pairs[8] + pairs[9][:2]:
        compute(piece_of)
    dhidden, gain_share = norm_gradient(at.dnorm[...], at.hid[...], at.norms[0:1, :].astype(jnp.float32))
    at.gain_row[...] = gain_share
    at.grad_out[...] = (at.grad[...] + dhidden).T
    compute(pairs[9][2])
    for tick in range(8, len(pairs) + m + n - 1):
        moves(tick)
    for pair in pairs:
        for piece_of in pair:
            piece_of.finish(m + n)
    for pair in pairs:
        for piece_of in pair:
            piece_of.drained(range(1, m + n + 1))
    work.drained()


def unpack_kernel(sizes, names, *refs):
    rows, padded = sizes
    at = types.SimpleNamespace(**dict(zip(names, refs)))
    counter = itertools.count()

    def moved(source, target):
        return pltpu.make_async_copy(source, target, at.sems.at[next(counter)])

    loads = [moved(at.wide_in.at[pl.ds(first, 5)], at.wide.at[pl.ds(first, 5)]) for first in (10, 0, 5)]
    loads += [moved(at.down_in, at.down), moved(at.little_in, at.little)]
    loads += [moved(at.hidden_in, at.hidden), moved(at.gradient_in, at.gradient)]
    for load in loads:
        load.start()
    stores = []

    def send(source, target):
        stores.append(moved(source, target))
        stores[-1].start()

    def columns(first, target):
        for unit in range(5):
            tile = at.wide[first + unit].astype(jnp.float32)
            for side in range(2):
                column = side * 1280 + unit * UNIT_COLUMNS
                target[:, column:column + UNIT_COLUMNS] = tile[side * padded:side * padded + rows]

    loads[0].wait()
    columns(10, at.rest)
    width = at.query.shape[1]
    both = at.rest[:, :2 * KEYS_WIDTH].T
    for group in range(KEY_VALUE_HEADS):
        here, first = slice(group * HEAD_DIMENSION, (group + 1) * HEAD_DIMENSION), group * PAIR
        at.key[here, :] = both[first:first + HEAD_DIMENSION]
        at.value[here, :] = both[first + HEAD_DIMENSION:first + PAIR]
    at.query[...] = at.rest[:, 2 * KEYS_WIDTH:2 * KEYS_WIDTH + width]
    at.attended[...] = at.rest[:, 2 * KEYS_WIDTH + width:]
    for source, target in (
        (at.key, at.key_out), (at.value, at.value_out), (at.query, at.query_out), (at.attended, at.attended_out),
    ):
        send(source, target)
    for load, first, target, place in ((loads[1], 0, at.gate, at.gate_out), (loads[2], 5, at.up, at.up_out)):
        load.wait()
        columns(first, target)
        send(target, place)
    loads[3].wait()
    down_rows = at.down.shape[1]
    for unit in range(5):
        at.down_float[unit * down_rows:(unit + 1) * down_rows, :] = at.down[unit].astype(jnp.float32)
    send(at.down_float, at.down_out)
    loads[4].wait()
    at.norm_attn[...] = at.little[0, 0:1, :rows]
    at.norm_ffn[...] = at.little[0, 1:2, :rows]
    at.router[...] = at.little[0, 2:4, :rows]
    loads[5].wait()
    send(at.hidden, at.hidden_out)
    loads[6].wait()
    send(at.gradient, at.gradient_out)
    for store in stores:
        store.wait()


def final(small, saved, top, bottom, weights, mesh_sizes):
    nb, nd = mesh_sizes
    m, n = nb.bit_length() - 1, nd.bit_length() - 1
    grad = bottom["grad_hidden"]
    piece, width = grad.shape
    hidden_units = weights["w_gate_hbm"].shape[1]
    rows = width // nb
    padded = -(-rows // 8) * 8
    down_rows = hidden_units // nb // 5
    tokens = RECUR * piece

    def spread(array):
        if padded == rows:
            return array
        split = array.reshape(RECUR, nb, rows, piece)
        return jnp.pad(split, ((0, 0), (0, 0), (0, padded - rows), (0, 0))).reshape(RECUR, nb * padded, piece)

    inputs = small | dict(small_before=bottom["small"])
    operands = dict(
        metas_hbm=saved["metas"], turned_hbm=saved["turned"], dat_hbm=bottom["dat"], att_hbm=saved["att"],
        lse_hbm=saved["lse"], kv_hbm=saved["kv"], w_query_hbm=weights["w_query_hbm"],
        key_weight_hbm=weights["key_weight_hbm"], value_weight_hbm=weights["value_weight_hbm"], hid_hbm=saved["hid"],
        grad_hbm=grad, inner_hbm=saved["inner"], nffn_hbm=spread(saved["nffn"]), normed_hbm=spread(saved["normed"]),
        attended_hbm=spread(saved["att"]), dffn_0_hbm=bottom["dffn"], dffn_1_hbm=top["dffn"],
        dgate_0_hbm=bottom["dgate_out"], dgate_1_hbm=top["dgate"], dup_0_hbm=bottom["dup_out"], dup_1_hbm=top["dup"],
        far_0_hbm=bottom["far"], far_1_hbm=top["far"], near_1_hbm=bottom["near_out"],
    )
    near_width = bottom["near_out"].shape[1]
    families = (
        ("wide", 15, (2 * padded, UNIT_COLUMNS), low, WIDE_SLOTS, 1), ("down", 5, (down_rows, width), low, DOWN_SLOTS, 0),
        ("small", 1, (16, 128), jnp.float32, 1, 0),
    )
    outs = dict(grad_out=((width, piece), jnp.float32))
    buffers = attention_buffers(nb, piece, width, low) | dict(
        grad=((piece, width), jnp.float32), gate_side=((tokens, hidden_units), low), up_side=((tokens, hidden_units), low),
        inner=((hidden_units, tokens), low), left=((nb * padded, tokens), low), left_attended=((nb * padded, tokens), low),
        dffn=((tokens, width), low), gain_row=((1, width), jnp.float32),
    )
    for name, count, shape, dtype, slots, split in families:
        outs["out_" + name] = ((count, *shape), dtype)
        buffers["part_" + name] = ((slots, *(2,) * m, *shape), dtype)
        for stage in range(m):
            buffers["blk_%s_%d" % (name, stage)] = ((count, *(2,) * (m - 1 - stage), *shape), dtype)
        for stage in range(n):
            buffers["dp_%s_%d" % (name, stage)] = ((count, *shape), dtype)
    sums, hops = (2 * KEY_VALUE_HEADS, m), (21, m + n + 1)
    semaphores = dict(load_sems=(32,), weight_sems=(2 * KEY_VALUE_HEADS,), kv_send=sums, kv_recv=sums, send_sems=hops, recv_sems=hops)
    names = (*inputs, *operands, *outs, *buffers, *semaphores)
    gradient, wide, down, little = pl.pallas_call(
        functools.partial(final_kernel, (nb, m, n, piece, rows, padded, near_width), names),
        out_shape=[shaped(entry) for entry in outs.values()],
        in_specs=[spec(pltpu.VMEM)] * len(inputs) + [spec(pl.ANY)] * len(operands),
        out_specs=[spec(pltpu.VMEM)] * len(outs),
        scratch_shapes=spaces(buffers.values()) + dma_semaphores(*semaphores.values()),
        compiler_params=pltpu.CompilerParams(
            collective_id=0, has_side_effects=True, vmem_limit_bytes=VMEM_LIMIT
        ),
        cost_estimate=pl.CostEstimate(
            flops=2 * tokens * width * 14000, bytes_accessed=30 * 1024 * 1024, transcendentals=0
        ),
        name="weight_grads",
    )(*inputs.values(), *operands.values())
    heads, square, tall, turned = (KEYS_WIDTH, rows), (rows, width), (rows, hidden_units), (width, piece)
    operands = dict(wide_in=wide, down_in=down, little_in=little, hidden_in=saved["hidden_out"], gradient_in=gradient)
    near_outs = dict(norm_attn=(1, rows), norm_ffn=(1, rows), router=(2, rows))
    far_outs = dict(
        key_out=heads, value_out=heads, query_out=square, attended_out=square, gate_out=tall, up_out=tall,
        down_out=(5 * down_rows, width), hidden_out=turned, gradient_out=turned,
    )
    buffers = dict(
        wide=(wide.shape, low), down=(down.shape, low), little=(little.shape, jnp.float32), rest=((rows, 2560), jnp.float32),
        key=(heads, jnp.float32), value=(heads, jnp.float32), query=(square, jnp.float32), attended=(square, jnp.float32),
        gate=(tall, jnp.float32), up=(tall, jnp.float32), down_float=((5 * down_rows, width), jnp.float32),
        hidden=(turned, jnp.float32), gradient=(turned, jnp.float32),
    )
    outs = pl.pallas_call(
        functools.partial(unpack_kernel, (rows, padded), (*operands, *near_outs, *far_outs, *buffers, *dict(sems=0))),
        out_shape=[jax.ShapeDtypeStruct(shape, jnp.float32) for shape in (near_outs | far_outs).values()],
        in_specs=[spec(pl.ANY)] * len(operands),
        out_specs=[spec(pltpu.VMEM)] * len(near_outs) + [spec(pl.ANY)] * len(far_outs),
        scratch_shapes=spaces(buffers.values()) + dma_semaphores((16,)),
        compiler_params=pltpu.CompilerParams(vmem_limit_bytes=VMEM_LIMIT),
        name="unpack",
    )(*operands.values())
    norm_a, norm_f, router, key, value, query, out, gate, up, down, hidden, gradient = outs
    return (
        hidden.T[None], gradient.T[None], norm_a[0], norm_f[0], query, key.T, value.T, out, gate, up, down, router.T,
    )


def local(
    tokens,
    depths,
    segments,
    norm_attn,
    norm_ffn,
    w_query,
    key_weight,
    value_weight,
    w_out,
    w_gate,
    w_up,
    w_down,
    w_router,
    cotangent,
    mesh_sizes,
):
    piece = tokens.shape[1]
    positions = lax.axis_index("blk") * piece + jnp.arange(piece, dtype=jnp.int32)
    angles = frequencies(HEAD_DIMENSION)[:, None] * positions.astype(jnp.float32)[None, :]
    tables = dict(cosines=jnp.cos(angles), sines=jnp.sin(angles), norm_attn=norm_attn, norm_ffn=norm_ffn)
    routing = dict(router=w_router.T, depths=depths)
    heads = dict(w_query_hbm=w_query, key_weight_hbm=key_weight.T, value_weight_hbm=value_weight.T)
    weights = heads | dict(w_out_hbm=w_out, w_gate_hbm=w_gate, w_up_hbm=w_up, w_down_hbm=w_down.T)
    nb = mesh_sizes[0]
    saved = forward(
        tables | routing | dict(tokens=tokens[0].T, cotangent=cotangent[0].T, segments=segments), weights, nb
    )
    operands = dict(
        metas_hbm=saved["metas"], turned_hbm=saved["turned"], dat_hbm=saved["dat"], att_hbm=saved["att"],
        lse_hbm=saved["lse"], kv_hbm=saved["kv"], grad_hbm=saved["grad_hidden"], hid_1_hbm=saved["hid_1"],
        hid_0_hbm=saved["hid"], branch_hbm=saved["branch"], slope_hbm=saved["slope"], silu_hbm=saved["silu"],
        middle_hbm=saved["middle"],
    )
    bottom = backward(1, tables | routing | dict(small_before=saved["small"]), weights | operands, nb)
    return final(tables, saved, saved, bottom, weights, mesh_sizes)


def solution(mesh):
    sizes = (mesh.shape["blk"], mesh.shape["dp"])
    return jax.shard_map(
        functools.partial(local, mesh_sizes=sizes),
        mesh=mesh,
        in_specs=(
            P("dp", "blk", None),
            P("dp", "blk"),
            P("dp", "blk"),
            P(),
            P(),
            P(),
            P(),
            P(),
            P(),
            P(),
            P(),
            P(),
            P(),
            P("dp", "blk", None),
        ),
        out_specs=(
            P("dp", "blk", None),
            P("dp", "blk", None),
            P("blk"),
            P("blk"),
            P("blk", None),
            P("blk", None),
            P("blk", None),
            P("blk", None),
            P("blk", None),
            P("blk", None),
            P("blk", None),
            P("blk", None),
        ),
        check_vma=False,
    )
```
